32 devices in a mesh: gx: 2 (over core), gy: 16 (over z, y, x).
Axes of the slice: x: 2, y: 2, z: 4, core: 2. Of those that a mesh axis runs over, the one named last changes fastest.
Arguments:
- hidden_in: bfloat16 [2, 8192, 768], P(None, ('gx', 'gy')), may hold values from -6 to 6
- rand_table: int32 [2, 128, 3], P(None, ('gx', 'gy')), may hold values from 0 to 63
- norm1_gain: bfloat16 [768], P(('gx', 'gy')), may hold values from 0.5 to 1.5
- norm1_bias: bfloat16 [768], P(('gx', 'gy')), may hold values from -3 to 3
- w_qkv: bfloat16 [768, 2304], P(('gx', 'gy')), may hold values from -0.21875 to 0.21875
- query_bias: bfloat16 [768], P(('gx', 'gy')), may hold values from -3 to 3
- value_bias: bfloat16 [768], P(('gx', 'gy')), may hold values from -0.59765625 to 0.59765625
- w_out: bfloat16 [768, 768], P(('gx', 'gy')), may hold values from -1.25 to 1.25
- out_bias: bfloat16 [768], P(('gx', 'gy')), may hold values from -2 to 2
- norm2_gain: bfloat16 [768], P(('gx', 'gy')), may hold values from 0.5 to 1.5
- norm2_bias: bfloat16 [768], P(('gx', 'gy')), may hold values from -2 to 2
- w_up: bfloat16 [768, 3072], P(('gx', 'gy')), may hold values from -0.21875 to 0.21875
- up_bias: bfloat16 [3072], P(('gx', 'gy')), may hold values from -3 to 3
- w_down: bfloat16 [3072, 768], P(('gx', 'gy')), may hold values from -0.109375 to 0.109375
- down_bias: bfloat16 [768], P(('gx', 'gy')), may hold values from -2 to 2
- cotangent: bfloat16 [2, 8192, 768], P(None, ('gx', 'gy')), may hold values from -6 to 6
Outputs:
- hidden_out: bfloat16 [2, 8192, 768], P(None, ('gx', 'gy'))
- grad_hidden: float32 [2, 8192, 768], P(None, ('gx', 'gy'))
- grad_norm1_gain: float32 [768], P(('gx', 'gy'))
- grad_norm1_bias: float32 [768], P(('gx', 'gy'))
- grad_w_qkv: float32 [768, 2304], P(('gx', 'gy'))
- grad_query_bias: float32 [768], P(('gx', 'gy'))
- grad_value_bias: float32 [768], P(('gx', 'gy'))
- grad_w_out: float32 [768, 768], P(('gx', 'gy'))
- grad_out_bias: float32 [768], P(('gx', 'gy'))
- grad_norm2_gain: float32 [768], P(('gx', 'gy'))
- grad_norm2_bias: float32 [768], P(('gx', 'gy'))
- grad_w_up: float32 [768, 3072], P(('gx', 'gy'))
- grad_up_bias: float32 [3072], P(('gx', 'gy'))
- grad_w_down: float32 [3072, 768], P(('gx', 'gy'))
- grad_down_bias: float32 [768], P(('gx', 'gy'))
The draws below stay inside these ranges and needn't reach their ends.
All inputs are finite; a program needn't handle non-finite values.
Results may differ from the reference program's by a relative error of at most 0.012.
Values may be sent and summed in bfloat16 or wider, within the bound.
A program may use at most 320 MiB of HBM per device.

```python
import jax
import jax.numpy as jnp
from jax import lax

HEADS = 12
HEAD_DIM = 64
D = 768
FF = 3072
BLOCK = 64
RANDOM = 3
SEQ = 4096
MICRO = 2
TOKENS = 8192
N_GX = 2


def set_ends(drawn, stream_key, smallest, top_value):
    longest = drawn.shape.index(max(drawn.shape))
    spots = []
    for shift in (0, 1):
        where = [jax.random.randint(jax.random.fold_in(stream_key, axis), (), 0, length) for axis, length in enumerate(drawn.shape)]
        where[longest] = (where[longest] + shift) % drawn.shape[longest]
        spots.append(tuple(where))
    return drawn.at[spots[0]].set(smallest).at[spots[1]].set(top_value)


def block_scale(own_key, dims, split, least, top_value):
    def one(dim, shards_of):
        heights = jax.random.uniform(jax.random.fold_in(jax.random.fold_in(own_key, 6), dim), (shards_of,), jnp.float32, least / len(split), top_value / len(split))
        return jnp.repeat(jnp.exp(heights), dims[dim] // shards_of).reshape((-1,) + (1,) * (len(dims) - dim - 1))

    loudness = one(*split[0])
    for cut in split[1:]:
        loudness = loudness * one(*cut)
    return loudness


def gaussian(key, extent, width, reach, cuts=(), kind=jnp.bfloat16):
    loudness = block_scale(key, extent, cuts, -0.22, 0.18) if cuts else 1.0
    values = jax.random.normal(key, extent, jnp.float32) * width * loudness
    return jnp.minimum(jnp.maximum(values, -reach), reach).astype(kind)


def setup_inputs(seed: int = 0) -> dict:
    splits = jax.random.split(jax.random.key(seed), 17)
    hidden_in = gaussian(splits[0], (MICRO, TOKENS, D), 1.0, 6.0, ((1, 32),))
    rand_table = set_ends(jax.random.randint(splits[1], (MICRO, TOKENS // BLOCK, RANDOM), 0, SEQ // BLOCK), jax.random.fold_in(splits[1], 1), 0, (SEQ // BLOCK) - 1).astype(jnp.int32)
    norm1_gain = jnp.clip(1.0 + 0.1 * jax.random.normal(splits[2], (D,), jnp.float32), 0.5, 1.5).astype(jnp.bfloat16)
    norm1_bias = gaussian(splits[3], (D,), 0.5, 3.0, ((0, 32),))
    w_qkv = gaussian(splits[4], (D, 3 * D), D ** -0.5, 0.21875, ((0, 32),))
    query_bias = gaussian(splits[5], (D,), 0.5, 3.0, ((0, 32),))
    value_bias = gaussian(splits[6], (D,), 0.1, 0.59765625, ((0, 32),))
    w_out = gaussian(splits[7], (D, D), (D // 32) ** -0.5, 1.25, ((0, 32),))
    out_bias = gaussian(splits[8], (D,), 0.3, 2.0, ((0, 32),))
    norm2_gain = jnp.clip(1.0 + 0.1 * jax.random.normal(splits[9], (D,), jnp.float32), 0.5, 1.5).astype(jnp.bfloat16)
    norm2_bias = gaussian(splits[10], (D,), 0.3, 2.0, ((0, 32),))
    w_up = gaussian(splits[11], (D, FF), D ** -0.5, 0.21875, ((0, 32),))
    up_bias = gaussian(splits[12], (FF,), 0.5, 3.0, ((0, 32),))
    w_down = gaussian(splits[13], (FF, D), FF ** -0.5, 0.109375, ((0, 32),))
    down_bias = gaussian(splits[14], (D,), 0.3, 2.0, ((0, 32),))
    cotangent = gaussian(splits[15], (MICRO, TOKENS, D), 1.0, 6.0, ((1, 32),))
    return {"hidden_in": hidden_in, "rand_table": rand_table, "norm1_gain": norm1_gain, "norm1_bias": norm1_bias, "w_qkv": w_qkv, "query_bias": query_bias, "value_bias": value_bias, "w_out": w_out, "out_bias": out_bias, "norm2_gain": norm2_gain, "norm2_bias": norm2_bias, "w_up": w_up, "up_bias": up_bias, "w_down": w_down, "down_bias": down_bias, "cotangent": cotangent}


@jax.custom_vjp
def low(v):
    return lax.optimization_barrier(v.astype(jnp.bfloat16)).astype(jnp.float32)

@jax.custom_vjp
def low_back(v):
    return v

def low_keep(v):
    return (low(v), None)

def low_pass(kept, grad):
    return (grad,)

def back_keep(v):
    return (v, None)

def back_low(kept, grad):
    return (low(grad),)
low.defvjp(low_keep, low_pass)
low_back.defvjp(back_keep, back_low)
EPSILON = 1e-05
HIGHEST = lax.Precision.HIGHEST

def layer_norm(values_in, norm_gain, norm_shift):
    centre = values_in - lax.optimization_barrier(jnp.mean(values_in, axis=-1, keepdims=True))
    spread = lax.optimization_barrier(jnp.mean(centre * centre, axis=-1, keepdims=True))
    return centre * lax.rsqrt(spread + EPSILON) * norm_gain + norm_shift

def gelu_tanh(values_in):
    return jax.nn.gelu(values_in, approximate=True)

def block_allowed(query_ids, random_rows, key_ids, block_total):
    nearby = jnp.abs(query_ids[:, None] - key_ids[None, :]) <= 1
    global_keys = (key_ids == 0) | (key_ids == block_total - 1)
    global_rows = (query_ids == 0) | (query_ids == block_total - 1)
    picked = jnp.any(random_rows[:, :, None] == key_ids[None, None, :], axis=1)
    return nearby | global_keys[None, :] | global_rows[:, None] | picked

def window_layer(params, tokens_in, table_rows):
    gain_one, shift_one, qkv_full, query_shift, value_shift, out_full, out_shift, gain_two, shift_two, up_full, up_shift, down_full, down_shift = params
    seq_len = tokens_in.shape[0]
    block_total = seq_len // BLOCK
    normed = low(layer_norm(tokens_in, gain_one, shift_one))
    packed = jnp.dot(normed, qkv_full, precision=HIGHEST)
    query_heads = low(low_back(packed[:, :D] + query_shift)).reshape(seq_len, HEADS, HEAD_DIM)
    key_heads = low(low_back(packed[:, D:2 * D])).reshape(seq_len, HEADS, HEAD_DIM)
    value_heads = low(low_back(packed[:, 2 * D:] + value_shift)).reshape(seq_len, HEADS, HEAD_DIM)
    block_rows = min(512, seq_len)
    key_ids = jnp.arange(seq_len, dtype=jnp.int32) // BLOCK
    score_scale = HEAD_DIM ** (-0.5)

    def attend(position):
        first_row = position * block_rows
        query_part = lax.dynamic_slice_in_dim(query_heads, first_row, block_rows, 0)
        table_part = lax.dynamic_slice_in_dim(table_rows, first_row // BLOCK, block_rows // BLOCK, 0)
        query_ids = (first_row + jnp.arange(block_rows, dtype=jnp.int32)) // BLOCK
        allowed = block_allowed(query_ids, jnp.repeat(table_part, BLOCK, axis=0), key_ids, block_total)[None]
        scores = low_back(jnp.einsum('qhd,khd->hqk', query_part, key_heads, precision=HIGHEST) * score_scale)
        masked = jnp.where(allowed, scores, -1e+30)
        row_top = lax.optimization_barrier(jnp.max(masked, axis=-1, keepdims=True))
        powered = jnp.where(allowed, jnp.exp(masked - row_top), 0.0)
        weights_now = low(powered / lax.optimization_barrier(jnp.sum(powered, axis=-1, keepdims=True)))
        return jnp.einsum('hqk,khd->qhd', weights_now, value_heads, precision=HIGHEST)
    pieces = lax.map(jax.checkpoint(attend), jnp.arange(seq_len // block_rows, dtype=jnp.int32))
    mixed = low(low_back(pieces.reshape(seq_len, D)))
    branch = low_back(jnp.dot(mixed, out_full, precision=HIGHEST) + out_shift)
    residual = tokens_in + branch
    second = low(layer_norm(residual, gain_two, shift_two))
    upper = low_back(jnp.dot(second, up_full, precision=HIGHEST) + up_shift)
    active = low(gelu_tanh(upper))
    return residual + low_back(jnp.dot(active, down_full, precision=HIGHEST) + down_shift)

def reference(hidden_in, rand_table, norm1_gain, norm1_bias, w_qkv, query_bias, value_bias, w_out, out_bias, norm2_gain, norm2_bias, w_up, up_bias, w_down, down_bias, cotangent):
    params = tuple((item.astype(jnp.float32) for item in (norm1_gain, norm1_bias, w_qkv, query_bias, value_bias, w_out, out_bias, norm2_gain, norm2_bias, w_up, up_bias, w_down, down_bias)))
    window_count = MICRO * N_GX
    tokens_all = hidden_in.astype(jnp.float32).reshape(window_count, SEQ, D)
    tables = rand_table.reshape(window_count, SEQ // BLOCK, RANDOM)
    window_step = jax.checkpoint(window_layer)

    def forward(params_now, tokens_now):

        def advance(carry_now, pair_now):
            return (carry_now, window_step(params_now, pair_now[0], pair_now[1]))
        _, outputs = lax.scan(advance, jnp.zeros((), jnp.float32), (tokens_now, tables))
        return outputs
    outputs, pullback = jax.vjp(forward, params, tokens_all)
    grad_params, grad_tokens = pullback(cotangent.astype(jnp.float32).reshape(window_count, SEQ, D))
    return (outputs.reshape(MICRO, TOKENS, D).astype(jnp.bfloat16), grad_tokens.reshape(MICRO, TOKENS, D), grad_params[0], grad_params[1], grad_params[2], grad_params[3], grad_params[4], grad_params[5], grad_params[6], grad_params[7], grad_params[8], grad_params[9], grad_params[10], grad_params[11], grad_params[12])
```

```python
import functools

import jax
import jax.numpy as jnp
from jax import lax
from jax.experimental import pallas as pl
from jax.experimental.pallas import tpu as pltpu
from jax.sharding import PartitionSpec as P

HEADS = 12
HEAD_DIM = 64
D = 768
FF = 3072
BLOCK = 64
RANDOM = 3
LANES = 2 * HEAD_DIM
EPSILON = 1e-05
NEGATIVE = -1e30
SCALE = HEAD_DIM**-0.5
CHUNK = 256
SPAN = 8

F32 = jnp.float32
BF16 = jnp.bfloat16
VMEM = pltpu.VMEM


def whole(space=VMEM):
    return pl.BlockSpec(memory_space=space)


def params_of(megabytes):
    return pltpu.CompilerParams(vmem_limit_bytes=megabytes * 1024 * 1024)


def head_place(head):
    return (head // 3) * 4 + head % 3


def dot(left, right):
    return lax.dot_general(left, right, (((1,), (0,)), ((), ())), preferred_element_type=F32)


def dot_rt(left, right):
    return lax.dot_general(left, right, (((1,), (1,)), ((), ())), preferred_element_type=F32)


def dot_lt(left, right):
    return lax.dot_general(left, right, (((0,), (0,)), ((), ())), preferred_element_type=F32)


def swap_halves(tile):
    return pltpu.roll(tile, HEAD_DIM, axis=tile.ndim - 1)


def low_lanes(rows):
    return lax.broadcasted_iota(jnp.int32, (rows, LANES), 1) < HEAD_DIM


def norm_parts(values):
    centre = values - jnp.mean(values, axis=-1, keepdims=True)
    spread = jnp.mean(centre * centre, axis=-1, keepdims=True)
    inverse = lax.rsqrt(spread + EPSILON)
    return centre * inverse, inverse


def norm_pull(grad, normal, inverse, gain):
    scaled = grad * gain
    return inverse * (
        scaled
        - jnp.mean(scaled, axis=-1, keepdims=True)
        - normal * jnp.mean(scaled * normal, axis=-1, keepdims=True)
    )


def qkv_kernel(x_ref, gain_ref, shift_ref, w_ref, bias_ref, normed_ref, send_ref):
    micro, rows, _ = x_ref.shape
    values = x_ref[...].reshape(micro * rows, D).astype(F32)
    normal, _ = norm_parts(values)
    normed_ref[...] = (normal * gain_ref[...] + shift_ref[...]).astype(BF16)
    low = low_lanes(rows)
    for chunk in range(3 * D // CHUNK):
        columns = slice(chunk * CHUNK, (chunk + 1) * CHUNK)
        packed = dot(normed_ref[...], w_ref[:, columns]) + bias_ref[:, columns]
        if chunk < D // CHUNK:
            packed = packed.astype(BF16).astype(F32) * SCALE
        for tile in range(CHUNK // LANES):
            part = packed[:, tile * LANES : (tile + 1) * LANES]
            first, second = part[:rows], part[rows:]
            if chunk < D // CHUNK:
                head = (chunk * CHUNK // LANES + tile) * 2
                even = jnp.where(low, first, swap_halves(second))
                odd = jnp.where(low, swap_halves(first), second)
                send_ref[head_place(head), 0] = even.astype(BF16)
                send_ref[head_place(head + 1), 0] = odd.astype(BF16)
            else:
                head = (chunk * CHUNK - D) // LANES + tile
                send_ref[head_place(head), 1] = first.astype(BF16)
                send_ref[head_place(head), 2] = swap_halves(second).astype(BF16)


def qkv_forward(x, gain, shift, w, bias, groups):
    micro, rows, _ = x.shape
    return pl.pallas_call(
        qkv_kernel,
        out_shape=(
            jax.ShapeDtypeStruct((micro * rows, D), BF16),
            jax.ShapeDtypeStruct((groups, 3, rows, LANES), BF16),
        ),
        in_specs=[whole()] * 5,
        out_specs=(whole(), whole()),
        compiler_params=params_of(48),
        name="qkv_forward",
    )(x, gain, shift, w, bias)


def half_mask(low_half):
    lane = lax.broadcasted_iota(jnp.int32, (1, LANES), 1)
    keep = (lane < HEAD_DIM) if low_half else (lane >= HEAD_DIM)
    return jnp.where(keep, 1.0, 0.0).astype(BF16)


def slots_of(table_ref, micro, block, blocks):
    picks = [table_ref[micro, block * RANDOM + number] for number in range(RANDOM)]
    last = blocks - 1
    ids = [block - 1, block, block + 1, 0, last] + picks
    dropped = [None, None, None, block == 1, block == last - 1]
    for number in range(RANDOM):
        pick = picks[number]
        bad = (jnp.abs(pick - block) <= 1) | (pick == 0) | (pick == last)
        for earlier in range(number):
            bad = bad | (pick == picks[earlier])
        dropped.append(bad)
    lane = lax.broadcasted_iota(jnp.int32, (1, LANES), 1)
    tiles = []
    for pair in range(len(ids) // 2):
        level = [
            0.0 if bad is None else jnp.where(bad, NEGATIVE, 0.0).astype(F32)
            for bad in dropped[2 * pair : 2 * pair + 2]
        ]
        tiles.append(jnp.where(lane < HEAD_DIM, level[0], level[1]))
    return ids, jnp.concatenate(tiles, axis=1)


def attend_kernel(table_ref, qkv_ref, out_ref, lse_ref, s_ref):
    groups, _, local, _, _ = qkv_ref.shape
    blocks = groups * local
    low = low_lanes(BLOCK)
    masks = [half_mask(True), half_mask(False)]

    def load(component, block):
        return qkv_ref[block // local, component, block % local]

    def sparse(block, carry):
        mixed, logs = [], []
        for micro in range(2):
            ids, bias = slots_of(table_ref, micro, block, blocks)
            keys = jnp.concatenate([load(1 + micro, spot) for spot in ids], axis=0)
            query = load(0, block) * masks[micro]
            scores = dot_rt(query, keys) + bias
            top = jnp.max(scores, axis=1, keepdims=True)
            powered = jnp.exp(scores - top)
            total = jnp.sum(powered, axis=1, keepdims=True)
            mixed.append(dot(powered.astype(BF16), keys) * (1.0 / total))
            logs.append(top + jnp.log(total))
        out_ref[block // local, block % local] = jnp.where(low, mixed[1], mixed[0]).astype(BF16)
        lse_ref[block] = jnp.where(low, logs[0], logs[1])
        return carry

    lax.fori_loop(1, blocks - 1, sparse, 0)

    spans = blocks // SPAN
    ends = (0, blocks - 1)
    results = []
    for micro in range(2):
        query = jnp.concatenate([load(0, end) for end in ends], axis=0) * masks[micro]

        def keys_at(span, micro=micro):
            return jnp.concatenate(
                [load(1 + micro, span * SPAN + spot) for spot in range(SPAN)], axis=0
            )

        def first_pass(span, top, query=query, keys_at=keys_at):
            scores = dot_rt(query, keys_at(span))
            s_ref[span] = scores
            return jnp.maximum(top, jnp.max(scores, axis=1, keepdims=True))

        top = lax.fori_loop(0, spans, first_pass, jnp.full((2 * BLOCK, 1), NEGATIVE, F32))

        def second_pass(span, carry, top=top, keys_at=keys_at):
            total, mixed = carry
            powered = jnp.exp(s_ref[span] - top)
            return (
                total + jnp.sum(powered, axis=1, keepdims=True),
                mixed + dot(powered.astype(BF16), keys_at(span)),
            )

        total, mixed = lax.fori_loop(
            0,
            spans,
            second_pass,
            (jnp.zeros((2 * BLOCK, 1), F32), jnp.zeros((2 * BLOCK, LANES), F32)),
        )
        results.append((mixed * (1.0 / total), top + jnp.log(total)))
    for place, end in enumerate(ends):
        rows = slice(place * BLOCK, (place + 1) * BLOCK)
        out_ref[end // local, end % local] = jnp.where(
            low, results[1][0][rows], results[0][0][rows]
        ).astype(BF16)
        lse_ref[end] = jnp.where(low, results[0][1][rows], results[1][1][rows])


def attention_forward(table, qkv):
    groups, _, local, _, _ = qkv.shape
    blocks = groups * local
    return pl.pallas_call(
        attend_kernel,
        out_shape=(
            jax.ShapeDtypeStruct((groups, local, BLOCK, LANES), BF16),
            jax.ShapeDtypeStruct((blocks, BLOCK, LANES), F32),
        ),
        in_specs=[whole(pltpu.SMEM), whole()],
        out_specs=(whole(), whole()),
        scratch_shapes=[VMEM((blocks // SPAN, 2 * BLOCK, SPAN * BLOCK), F32)],
        compiler_params=params_of(48),
        name="attention_forward",
    )(table, qkv)


def attend_back_kernel(table_ref, qkv_ref, grad_ref, lse_ref, out_ref, sums_ref, p_ref, dp_ref):
    groups, _, local, _, _ = qkv_ref.shape
    blocks = groups * local
    low = low_lanes(BLOCK)
    masks = [half_mask(True), half_mask(False)]

    def load(component, block):
        return qkv_ref[block // local, component, block % local]

    def load_grad(block):
        return grad_ref[block // local, block % local]

    def clear(block, carry):
        for micro in range(2):
            sums_ref[micro, block] = jnp.zeros((BLOCK, LANES), F32)
        return carry

    lax.fori_loop(0, blocks, clear, 0)

    def sparse(block, carry):
        grads = []
        for micro in range(2):
            ids, bias = slots_of(table_ref, micro, block, blocks)
            keys = jnp.concatenate([load(1 + micro, spot) for spot in ids], axis=0)
            both = jnp.concatenate(
                [load(0, block) * masks[micro], load_grad(block) * masks[1 - micro]], axis=0
            )
            products = dot_rt(both, keys)
            logs = lse_ref[block][:, micro * HEAD_DIM : micro * HEAD_DIM + 1]
            weights = jnp.exp(products[:BLOCK] + bias - logs)
            grad_weights = products[BLOCK:]
            delta = jnp.sum(weights * grad_weights, axis=1, keepdims=True)
            grad_scores = weights * (grad_weights - delta)
            stacked = jnp.concatenate([grad_scores, weights], axis=0).astype(BF16)
            grads.append(dot(stacked[:BLOCK], keys))
            shares = dot_lt(stacked, both)
            for place, spot in enumerate(ids):
                sums_ref[micro, spot] += shares[place * BLOCK : (place + 1) * BLOCK]
        out_ref[block // local, 0, block % local] = (
            jnp.where(low, grads[0], grads[1]) * SCALE
        ).astype(BF16)
        return carry

    lax.fori_loop(1, blocks - 1, sparse, 0)

    spans = blocks // SPAN
    ends = (0, blocks - 1)
    results = []
    for micro in range(2):
        query = jnp.concatenate([load(0, end) for end in ends], axis=0) * masks[micro]
        grad = jnp.concatenate([load_grad(end) for end in ends], axis=0) * masks[1 - micro]
        both = jnp.concatenate([query, grad], axis=0)
        logs = jnp.concatenate(
            [lse_ref[end][:, micro * HEAD_DIM : micro * HEAD_DIM + 1] for end in ends], axis=0
        )

        def keys_at(span, micro=micro):
            return jnp.concatenate(
                [load(1 + micro, span * SPAN + spot) for spot in range(SPAN)], axis=0
            )

        def first_pass(span, delta, both=both, logs=logs, keys_at=keys_at):
            products = dot_rt(both, keys_at(span))
            weights = jnp.exp(products[: 2 * BLOCK] - logs)
            grad_weights = products[2 * BLOCK :]
            p_ref[span] = weights
            dp_ref[span] = grad_weights
            return delta + jnp.sum(weights * grad_weights, axis=1, keepdims=True)

        delta = lax.fori_loop(0, spans, first_pass, jnp.zeros((2 * BLOCK, 1), F32))

        def second_pass(span, carry, delta=delta, both=both, keys_at=keys_at, micro=micro):
            weights = p_ref[span]
            grad_scores = weights * (dp_ref[span] - delta)
            stacked = jnp.concatenate([grad_scores, weights], axis=0).astype(BF16)
            shares = dot_lt(stacked, both)
            for spot in range(SPAN):
                sums_ref[micro, span * SPAN + spot] += shares[spot * BLOCK : (spot + 1) * BLOCK]
            return carry + dot(stacked[: 2 * BLOCK], keys_at(span))

        results.append(
            lax.fori_loop(0, spans, second_pass, jnp.zeros((2 * BLOCK, LANES), F32))
        )
    for place, end in enumerate(ends):
        rows = slice(place * BLOCK, (place + 1) * BLOCK)
        out_ref[end // local, 0, end % local] = (
            jnp.where(low, results[0][rows], results[1][rows]) * SCALE
        ).astype(BF16)

    def finish(block, carry):
        for micro in range(2):
            out_ref[block // local, 1 + micro, block % local] = sums_ref[micro, block].astype(BF16)
        return carry

    lax.fori_loop(0, blocks, finish, 0)


def attention_backward(table, qkv, grad, lse):
    groups, _, local, _, _ = qkv.shape
    blocks = groups * local
    spans = VMEM((blocks // SPAN, 2 * BLOCK, SPAN * BLOCK), F32)
    return pl.pallas_call(
        attend_back_kernel,
        out_shape=jax.ShapeDtypeStruct(qkv.shape, BF16),
        in_specs=[whole(pltpu.SMEM), whole(), whole(), whole()],
        out_specs=whole(),
        scratch_shapes=[VMEM((2, blocks, BLOCK, LANES), F32), spans, spans],
        compiler_params=params_of(48),
        name="attention_backward",
    )(table, qkv, grad, lse)


def middle_kernel(
    mixed_in_ref,
    x_ref,
    dy_ref,
    w_out_ref,
    out_shift_ref,
    gain_ref,
    shift_ref,
    up_shift_ref,
    down_shift_ref,
    w_up_ref,
    w_down_ref,
    hidden_ref,
    send_ref,
    dres_ref,
    g_out_ref,
    g_up_ref,
    g_down_ref,
    g_up_bias_ref,
    g_small_ref,
    mixed_ref,
    residual_ref,
    second_ref,
    second_t_ref,
    total_ref,
    dsecond_ref,
):
    micro, rows, _ = x_ref.shape
    step = pl.program_id(0)
    low = low_lanes(rows)

    @pl.when(step == 0)
    def _():
        for pair in range(HEADS // 2):
            even = mixed_in_ref[head_place(2 * pair)].astype(F32)
            odd = mixed_in_ref[head_place(2 * pair + 1)].astype(F32)
            columns = slice(pair * LANES, (pair + 1) * LANES)
            mixed_ref[:rows, columns] = jnp.where(low, swap_halves(even), odd).astype(BF16)
            mixed_ref[rows:, columns] = jnp.where(low, even, swap_halves(odd)).astype(BF16)
        residual = x_ref[...].reshape(micro * rows, D).astype(F32) + (
            dot(mixed_ref[...], w_out_ref[...]) + out_shift_ref[...]
        )
        residual_ref[...] = residual
        normal, _ = norm_parts(residual)
        second = normal * gain_ref[...] + shift_ref[...]
        second_ref[...] = second.astype(BF16)
        second_t_ref[...] = second.T.astype(BF16)
        total_ref[...] = jnp.zeros_like(total_ref)
        dsecond_ref[...] = jnp.zeros_like(dsecond_ref)

    upper = dot(second_ref[...], w_up_ref[...]) + up_shift_ref[...]
    factor = 0.7978845608028654
    square = upper * upper
    bent = jnp.tanh(factor * (upper + 0.044715 * (upper * square)))
    half = 0.5 * (1.0 + bent)
    active = (upper * half).astype(BF16)
    slope = half + 0.5 * upper * (1.0 - bent * bent) * (
        factor + (3.0 * 0.044715 * factor) * square
    )
    dy = dy_ref[...]
    total_ref[...] += dot(active, w_down_ref[...])
    g_down_ref[...] = dot_lt(active, dy).astype(g_down_ref.dtype)
    dupper = (dot_rt(dy, w_down_ref[...]) * slope).astype(BF16)
    g_up_bias_ref[...] = jnp.sum(dupper.astype(F32), axis=0, keepdims=True)
    g_up_ref[...] = dot(second_t_ref[...], dupper).astype(g_up_ref.dtype)
    dsecond_ref[...] += dot_rt(dupper, w_up_ref[...])

    @pl.when(step == pl.num_programs(0) - 1)
    def _():
        residual = residual_ref[...]
        hidden_ref[...] = (
            (residual + (total_ref[...] + down_shift_ref[...])).astype(BF16).reshape(x_ref.shape)
        )
        normal, inverse = norm_parts(residual)
        dsecond = dsecond_ref[...]
        grad_out = dy_ref[...].astype(F32)
        g_small_ref[0:1] = jnp.sum(dsecond * normal, axis=0, keepdims=True)
        g_small_ref[1:2] = jnp.sum(dsecond, axis=0, keepdims=True)
        g_small_ref[2:3] = jnp.sum(grad_out, axis=0, keepdims=True)
        dres = grad_out + norm_pull(dsecond, normal, inverse, gain_ref[...])
        dres_ref[...] = dres
        branch = dres.astype(BF16)
        g_small_ref[3:4] = jnp.sum(branch.astype(F32), axis=0, keepdims=True)
        g_out_ref[...] = dot_lt(mixed_ref[...], branch).astype(g_out_ref.dtype)
        dmixed = dot_rt(branch, w_out_ref[...])
        for pair in range(HEADS // 2):
            part = dmixed[:, pair * LANES : (pair + 1) * LANES]
            first, last = part[:rows], part[rows:]
            even = jnp.where(low, last, swap_halves(first))
            odd = jnp.where(low, swap_halves(last), first)
            send_ref[head_place(2 * pair)] = even.astype(BF16)
            send_ref[head_place(2 * pair + 1)] = odd.astype(BF16)


def middle(mixed_in, x, dy, w_out, out_shift, gain, shift, up_shift, down_shift, w_up, w_down, kind):
    micro, rows, _ = x.shape
    tokens = micro * rows
    groups = mixed_in.shape[0]

    def fixed(shape):
        return pl.BlockSpec(shape, lambda step: (0,) * len(shape))

    vector = fixed((1, D))
    steps = FF // CHUNK
    return pl.pallas_call(
        middle_kernel,
        grid=(steps,),
        out_shape=(
            jax.ShapeDtypeStruct(x.shape, BF16),
            jax.ShapeDtypeStruct((groups, rows, LANES), BF16),
            jax.ShapeDtypeStruct((tokens, D), F32),
            jax.ShapeDtypeStruct((D, D), kind),
            jax.ShapeDtypeStruct((D, FF), kind),
            jax.ShapeDtypeStruct((FF, D), kind),
            jax.ShapeDtypeStruct((1, FF), F32),
            jax.ShapeDtypeStruct((4, D), F32),
        ),
        in_specs=[
            fixed(mixed_in.shape),
            fixed(x.shape),
            fixed((tokens, D)),
            fixed((D, D)),
            vector,
            vector,
            vector,
            pl.BlockSpec((1, CHUNK), lambda step: (0, step)),
            vector,
            pl.BlockSpec((D, CHUNK), lambda step: (0, step)),
            pl.BlockSpec((CHUNK, D), lambda step: (step, 0)),
        ],
        out_specs=(
            fixed(x.shape),
            fixed((groups, rows, LANES)),
            fixed((tokens, D)),
            fixed((D, D)),
            pl.BlockSpec((D, CHUNK), lambda step: (0, step)),
            pl.BlockSpec((CHUNK, D), lambda step: (step, 0)),
            pl.BlockSpec((1, CHUNK), lambda step: (0, step)),
            fixed((4, D)),
        ),
        scratch_shapes=[
            VMEM((tokens, D), BF16),
            VMEM((tokens, D), F32),
            VMEM((tokens, D), BF16),
            VMEM((D, tokens), BF16),
            VMEM((tokens, D), F32),
            VMEM((tokens, D), F32),
        ],
        compiler_params=params_of(56),
        name="middle",
    )(mixed_in, x, dy, w_out, out_shift, gain, shift, up_shift, down_shift, w_up, w_down)


def qkv_back_kernel(
    recv_ref,
    normed_ref,
    x_ref,
    dres_ref,
    gain_ref,
    w_ref,
    grad_ref,
    g_qkv_ref,
    g_bias_ref,
    g_small_ref,
    packed_ref,
    normed_t_ref,
    dnormed_ref,
):
    micro, rows, _ = x_ref.shape
    step = pl.program_id(0)
    low = low_lanes(rows)

    @pl.when(step == 0)
    def _():
        for pair in range(HEADS // 2):
            even = recv_ref[head_place(2 * pair), 0].astype(F32)
            odd = recv_ref[head_place(2 * pair + 1), 0].astype(F32)
            spot, columns = pair // 2, slice((pair % 2) * LANES, (pair % 2 + 1) * LANES)
            packed_ref[spot, :rows, columns] = jnp.where(low, even, swap_halves(odd)).astype(BF16)
            packed_ref[spot, rows:, columns] = jnp.where(low, swap_halves(even), odd).astype(BF16)
        for head in range(HEADS):
            spot = D // CHUNK + head // 2
            columns = slice((head % 2) * LANES, (head % 2 + 1) * LANES)
            packed_ref[spot, :rows, columns] = recv_ref[head_place(head), 1]
            packed_ref[spot, rows:, columns] = swap_halves(
                recv_ref[head_place(head), 2].astype(F32)
            ).astype(BF16)
        normed_t_ref[...] = normed_ref[...].astype(F32).T.astype(BF16)
        dnormed_ref[...] = jnp.zeros_like(dnormed_ref)

    packed = packed_ref[step]
    g_bias_ref[...] = jnp.sum(packed.astype(F32), axis=0, keepdims=True)
    g_qkv_ref[...] = dot(normed_t_ref[...], packed).astype(g_qkv_ref.dtype)
    dnormed_ref[...] += dot_rt(packed, w_ref[...])

    @pl.when(step == pl.num_programs(0) - 1)
    def _():
        normal, inverse = norm_parts(x_ref[...].reshape(micro * rows, D).astype(F32))
        dnormed = dnormed_ref[...]
        g_small_ref[0:1] = jnp.sum(dnormed * normal, axis=0, keepdims=True)
        g_small_ref[1:2] = jnp.sum(dnormed, axis=0, keepdims=True)
        grad = dres_ref[...] + norm_pull(dnormed, normal, inverse, gain_ref[...])
        grad_ref[...] = grad.reshape(x_ref.shape)


def qkv_backward(recv, normed, x, dres, gain, w, kind):
    micro, rows, _ = x.shape
    tokens = micro * rows

    def fixed(shape):
        return pl.BlockSpec(shape, lambda step: (0,) * len(shape))

    steps = 3 * D // CHUNK
    return pl.pallas_call(
        qkv_back_kernel,
        grid=(steps,),
        out_shape=(
            jax.ShapeDtypeStruct(x.shape, F32),
            jax.ShapeDtypeStruct((D, 3 * D), kind),
            jax.ShapeDtypeStruct((1, 3 * D), F32),
            jax.ShapeDtypeStruct((2, D), F32),
        ),
        in_specs=[
            fixed(recv.shape),
            fixed((tokens, D)),
            fixed(x.shape),
            fixed((tokens, D)),
            fixed((1, D)),
            pl.BlockSpec((D, CHUNK), lambda step: (0, step)),
        ],
        out_specs=(
            fixed(x.shape),
            pl.BlockSpec((D, CHUNK), lambda step: (0, step)),
            pl.BlockSpec((1, CHUNK), lambda step: (0, step)),
            fixed((2, D)),
        ),
        scratch_shapes=[
            VMEM((steps, tokens, CHUNK), BF16),
            VMEM((D, tokens), BF16),
            VMEM((tokens, D), F32),
        ],
        compiler_params=params_of(56),
        name="qkv_backward",
    )(recv, normed, x, dres, gain, w)


AXES = ("gx", "gy")


def gather(array):
    return lax.all_gather(array, AXES, axis=0, tiled=True)


def scatter(array):
    return lax.psum_scatter(array, AXES, scatter_dimension=0, tiled=True)


def exchange(array):
    return lax.all_to_all(array, "gy", 0, 0, tiled=True)


def by_heads(w_qkv):
    rows = w_qkv.shape[0]
    sides = w_qkv[:, D:].reshape(rows, 2, HEADS, HEAD_DIM)
    return jnp.concatenate([w_qkv[:, :D], jnp.swapaxes(sides, 1, 2).reshape(rows, 2 * D)], axis=1)


def by_parts(w_qkv):
    rows = w_qkv.shape[0]
    sides = w_qkv[:, D:].reshape(rows, HEADS, 2, HEAD_DIM)
    return jnp.concatenate([w_qkv[:, :D], jnp.swapaxes(sides, 1, 2).reshape(rows, 2 * D)], axis=1)


def shards(
    hidden_in,
    rand_table,
    norm1_gain,
    norm1_bias,
    w_qkv,
    query_bias,
    value_bias,
    w_out,
    out_bias,
    norm2_gain,
    norm2_bias,
    w_up,
    up_bias,
    w_down,
    down_bias,
    cotangent,
):
    micro, rows, _ = hidden_in.shape
    groups = lax.axis_size("gy")
    local = rows // BLOCK
    own = norm1_gain.shape[0]

    vectors = jnp.concatenate(
        [
            norm1_gain,
            norm1_bias,
            query_bias,
            value_bias,
            out_bias,
            norm2_gain,
            norm2_bias,
            down_bias,
            up_bias,
        ]
    )
    table = lax.all_gather(rand_table, "gy", axis=1, tiled=True)
    table = table.reshape(micro, groups * local * RANDOM)
    vectors = gather(vectors[None]).astype(F32)
    gain_one, shift_one, query_shift, value_shift, out_shift, gain_two, shift_two, down_shift = (
        vectors[:, number * own : (number + 1) * own].reshape(1, D) for number in range(8)
    )
    up_shift = vectors[:, 8 * own :].reshape(1, FF)
    w_qkv_full = gather(by_heads(w_qkv))
    w_out_full, w_up_full, w_down_full = gather(w_out), gather(w_up), gather(w_down)
    packed_bias = by_heads(
        jnp.concatenate([query_shift, jnp.zeros_like(query_shift), value_shift], axis=1)
    )

    normed, send = qkv_forward(hidden_in, gain_one, shift_one, w_qkv_full, packed_bias, groups)
    qkv = exchange(send).reshape(groups, 3, local, BLOCK, LANES)
    mixed, lse = attention_forward(table, qkv)
    mixed_back = exchange(mixed.reshape(groups, rows, LANES))
    hidden_out, grad_send, dres, g_out, g_up, g_down, g_up_bias, g_mid = middle(
        mixed_back,
        hidden_in,
        cotangent.reshape(micro * rows, D),
        w_out_full,
        out_shift,
        gain_two,
        shift_two,
        up_shift,
        down_shift,
        w_up_full,
        w_down_full,
        F32,
    )
    grad_mixed = exchange(grad_send).reshape(groups, local, BLOCK, LANES)
    dqkv = attention_backward(table, qkv, grad_mixed, lse)
    dqkv_back = exchange(dqkv.reshape(groups, 3, rows, LANES))
    grad_hidden, g_qkv, g_packed, g_first = qkv_backward(
        dqkv_back, normed, hidden_in, dres, gain_one, w_qkv_full, F32
    )

    g_packed = by_parts(g_packed)
    small = [
        g_first[0],
        g_first[1],
        g_packed[0, :D],
        g_packed[0, 2 * D :],
        g_mid[3],
        g_mid[0],
        g_mid[1],
        g_mid[2],
    ]
    ranks = D // own
    small = jnp.concatenate(
        [item.reshape(ranks, own) for item in small] + [g_up_bias.reshape(ranks, 4 * own)], axis=1
    )
    small = scatter(small)[0]
    parts = [small[number * own : (number + 1) * own] for number in range(8)]
    return (
        hidden_out,
        grad_hidden,
        parts[0],
        parts[1],
        by_parts(scatter(g_qkv)),
        parts[2],
        parts[3],
        scatter(g_out),
        parts[4],
        parts[5],
        parts[6],
        scatter(g_up),
        small[8 * own :],
        scatter(g_down),
        parts[7],
    )


def solution(mesh):
    tokens = P(None, AXES, None)
    vector = P(AXES)
    matrix = P(AXES, None)
    placed = (
        tokens,
        tokens,
        vector,
        vector,
        matrix,
        vector,
        vector,
        matrix,
        vector,
        vector,
        vector,
        matrix,
        vector,
        matrix,
        vector,
        tokens,
    )
    returned = (
        tokens,
        tokens,
        vector,
        vector,
        matrix,
        vector,
        vector,
        matrix,
        vector,
        vector,
        vector,
        matrix,
        vector,
        matrix,
        vector,
    )
    return jax.shard_map(
        shards, mesh=mesh, in_specs=placed, out_specs=returned, check_vma=False
    )
```

```python
import functools

import jax
import jax.numpy as jnp
from jax import lax
from jax.experimental import pallas as pl
from jax.experimental.pallas import tpu as pltpu
from jax.sharding import PartitionSpec as P

HEADS = 12
HEAD_DIM = 64
D = 768
FF = 3072
BLOCK = 64
RANDOM = 3
LANES = 2 * HEAD_DIM
EPSILON = 1e-05
NEGATIVE = -1e30
SCALE = HEAD_DIM**-0.5
CHUNK = 256
SPAN = 8

F32 = jnp.float32
BF16 = jnp.bfloat16
VMEM = pltpu.VMEM


def whole(space=VMEM):
    return pl.BlockSpec(memory_space=space)


def params_of(megabytes):
    return pltpu.CompilerParams(vmem_limit_bytes=megabytes * 1024 * 1024)


def head_place(head):
    return (head // 3) * 4 + head % 3


def dot(left, right):
    return lax.dot_general(left, right, (((1,), (0,)), ((), ())), preferred_element_type=F32)


def dot_rt(left, right):
    return lax.dot_general(left, right, (((1,), (1,)), ((), ())), preferred_element_type=F32)


def dot_lt(left, right):
    return lax.dot_general(left, right, (((0,), (0,)), ((), ())), preferred_element_type=F32)


def swap_halves(tile):
    return pltpu.roll(tile, HEAD_DIM, axis=tile.ndim - 1)


def low_lanes(rows):
    return lax.broadcasted_iota(jnp.int32, (rows, LANES), 1) < HEAD_DIM


def norm_parts(values):
    centre = values - jnp.mean(values, axis=-1, keepdims=True)
    spread = jnp.mean(centre * centre, axis=-1, keepdims=True)
    inverse = lax.rsqrt(spread + EPSILON)
    return centre * inverse, inverse


def norm_pull(grad, normal, inverse, gain):
    scaled = grad * gain
    return inverse * (
        scaled
        - jnp.mean(scaled, axis=-1, keepdims=True)
        - normal * jnp.mean(scaled * normal, axis=-1, keepdims=True)
    )


def qkv_kernel(x_ref, gain_ref, shift_ref, w_ref, bias_ref, normed_ref, send_ref):
    micro, rows, _ = x_ref.shape
    values = x_ref[...].reshape(micro * rows, D).astype(F32)
    normal, _ = norm_parts(values)
    normed_ref[...] = (normal * gain_ref[...] + shift_ref[...]).astype(BF16)
    low = low_lanes(rows)
    for chunk in range(3 * D // CHUNK):
        columns = slice(chunk * CHUNK, (chunk + 1) * CHUNK)
        packed = dot(normed_ref[...], w_ref[:, columns]) + bias_ref[:, columns]
        if chunk < D // CHUNK:
            packed = packed.astype(BF16).astype(F32) * SCALE
        for tile in range(CHUNK // LANES):
            part = packed[:, tile * LANES : (tile + 1) * LANES]
            first, second = part[:rows], part[rows:]
            if chunk < D // CHUNK:
                head = (chunk * CHUNK // LANES + tile) * 2
                even = jnp.where(low, first, swap_halves(second))
                odd = jnp.where(low, swap_halves(first), second)
                send_ref[head_place(head), 0] = even.astype(BF16)
                send_ref[head_place(head + 1), 0] = odd.astype(BF16)
            else:
                head = (chunk * CHUNK - D) // LANES + tile
                send_ref[head_place(head), 1] = first.astype(BF16)
                send_ref[head_place(head), 2] = swap_halves(second).astype(BF16)


def qkv_forward(x, gain, shift, w, bias, groups):
    micro, rows, _ = x.shape
    return pl.pallas_call(
        qkv_kernel,
        out_shape=(
            jax.ShapeDtypeStruct((micro * rows, D), BF16),
            jax.ShapeDtypeStruct((groups, 3, rows, LANES), BF16),
        ),
        in_specs=[whole()] * 5,
        out_specs=(whole(), whole()),
        compiler_params=params_of(48),
        name="qkv_forward",
    )(x, gain, shift, w, bias)


def half_mask(low_half):
    lane = lax.broadcasted_iota(jnp.int32, (1, LANES), 1)
    keep = (lane < HEAD_DIM) if low_half else (lane >= HEAD_DIM)
    return jnp.where(keep, 1.0, 0.0).astype(BF16)


def slots_of(table_ref, micro, block, blocks):
    picks = [table_ref[micro, block * RANDOM + number] for number in range(RANDOM)]
    last = blocks - 1
    ids = [block - 1, block, block + 1, 0, last] + picks
    dropped = [None, None, None, block == 1, block == last - 1]
    for number in range(RANDOM):
        pick = picks[number]
        bad = (jnp.abs(pick - block) <= 1) | (pick == 0) | (pick == last)
        for earlier in range(number):
            bad = bad | (pick == picks[earlier])
        dropped.append(bad)
    lane = lax.broadcasted_iota(jnp.int32, (1, LANES), 1)
    tiles = []
    for pair in range(len(ids) // 2):
        level = [
            0.0 if bad is None else jnp.where(bad, NEGATIVE, 0.0).astype(F32)
            for bad in dropped[2 * pair : 2 * pair + 2]
        ]
        tiles.append(jnp.where(lane < HEAD_DIM, level[0], level[1]))
    return ids, jnp.concatenate(tiles, axis=1)


def attend_kernel(table_ref, qkv_ref, out_ref, lse_ref, s_ref):
    groups, _, local, _, _ = qkv_ref.shape
    blocks = groups * local
    low = low_lanes(BLOCK)
    masks = [half_mask(True), half_mask(False)]

    def load(component, block):
        return qkv_ref[block // local, component, block % local]

    def sparse(block, carry):
        mixed, logs = [], []
        for micro in range(2):
            ids, bias = slots_of(table_ref, micro, block, blocks)
            keys = jnp.concatenate([load(1 + micro, spot) for spot in ids], axis=0)
            query = load(0, block) * masks[micro]
            scores = dot_rt(query, keys) + bias
            top = jnp.max(scores, axis=1, keepdims=True)
            powered = jnp.exp(scores - top)
            total = jnp.sum(powered, axis=1, keepdims=True)
            mixed.append(dot(powered.astype(BF16), keys) * (1.0 / total))
            logs.append(top + jnp.log(total))
        out_ref[block // local, block % local] = jnp.where(low, mixed[1], mixed[0]).astype(BF16)
        lse_ref[block] = jnp.where(low, logs[0], logs[1])
        return carry

    lax.fori_loop(1, blocks - 1, sparse, 0)

    spans = blocks // SPAN
    ends = (0, blocks - 1)
    results = []
    for micro in range(2):
        query = jnp.concatenate([load(0, end) for end in ends], axis=0) * masks[micro]

        def keys_at(span, micro=micro):
            return jnp.concatenate(
                [load(1 + micro, span * SPAN + spot) for spot in range(SPAN)], axis=0
            )

        def first_pass(span, top, query=query, keys_at=keys_at):
            scores = dot_rt(query, keys_at(span))
            s_ref[span] = scores
            return jnp.maximum(top, jnp.max(scores, axis=1, keepdims=True))

        top = lax.fori_loop(0, spans, first_pass, jnp.full((2 * BLOCK, 1), NEGATIVE, F32))

        def second_pass(span, carry, top=top, keys_at=keys_at):
            total, mixed = carry
            powered = jnp.exp(s_ref[span] - top)
            return (
                total + jnp.sum(powered, axis=1, keepdims=True),
                mixed + dot(powered.astype(BF16), keys_at(span)),
            )

        total, mixed = lax.fori_loop(
            0,
            spans,
            second_pass,
            (jnp.zeros((2 * BLOCK, 1), F32), jnp.zeros((2 * BLOCK, LANES), F32)),
        )
        results.append((mixed * (1.0 / total), top + jnp.log(total)))
    for place, end in enumerate(ends):
        rows = slice(place * BLOCK, (place + 1) * BLOCK)
        out_ref[end // local, end % local] = jnp.where(
            low, results[1][0][rows], results[0][0][rows]
        ).astype(BF16)
        lse_ref[end] = jnp.where(low, results[0][1][rows], results[1][1][rows])


def attention_forward(table, qkv):
    groups, _, local, _, _ = qkv.shape
    blocks = groups * local
    return pl.pallas_call(
        attend_kernel,
        out_shape=(
            jax.ShapeDtypeStruct((groups, local, BLOCK, LANES), BF16),
            jax.ShapeDtypeStruct((blocks, BLOCK, LANES), F32),
        ),
        in_specs=[whole(pltpu.SMEM), whole()],
        out_specs=(whole(), whole()),
        scratch_shapes=[VMEM((blocks // SPAN, 2 * BLOCK, SPAN * BLOCK), F32)],
        compiler_params=params_of(48),
        name="attention_forward",
    )(table, qkv)


def attend_back_kernel(table_ref, qkv_ref, grad_ref, lse_ref, out_ref, sums_ref, p_ref, dp_ref):
    groups, _, local, _, _ = qkv_ref.shape
    blocks = groups * local
    low = low_lanes(BLOCK)
    masks = [half_mask(True), half_mask(False)]

    def load(component, block):
        return qkv_ref[block // local, component, block % local]

    def load_grad(block):
        return grad_ref[block // local, block % local]

    def clear(block, carry):
        for micro in range(2):
            sums_ref[micro, block] = jnp.zeros((BLOCK, LANES), F32)
        return carry

    lax.fori_loop(0, blocks, clear, 0)

    def sparse(block, carry):
        grads = []
        for micro in range(2):
            ids, bias = slots_of(table_ref, micro, block, blocks)
            keys = jnp.concatenate([load(1 + micro, spot) for spot in ids], axis=0)
            both = jnp.concatenate(
                [load(0, block) * masks[micro], load_grad(block) * masks[1 - micro]], axis=0
            )
            products = dot_rt(both, keys)
            logs = lse_ref[block][:, micro * HEAD_DIM : micro * HEAD_DIM + 1]
            weights = jnp.exp(products[:BLOCK] + bias - logs)
            grad_weights = products[BLOCK:]
            delta = jnp.sum(weights * grad_weights, axis=1, keepdims=True)
            grad_scores = weights * (grad_weights - delta)
            stacked = jnp.concatenate([grad_scores, weights], axis=0).astype(BF16)
            grads.append(dot(stacked[:BLOCK], keys))
            shares = dot_lt(stacked, both)
            for place, spot in enumerate(ids):
                sums_ref[micro, spot] += shares[place * BLOCK : (place + 1) * BLOCK]
        out_ref[block // local, 0, block % local] = (
            jnp.where(low, grads[0], grads[1]) * SCALE
        ).astype(BF16)
        return carry

    lax.fori_loop(1, blocks - 1, sparse, 0)

    spans = blocks // SPAN
    ends = (0, blocks - 1)
    results = []
    for micro in range(2):
        query = jnp.concatenate([load(0, end) for end in ends], axis=0) * masks[micro]
        grad = jnp.concatenate([load_grad(end) for end in ends], axis=0) * masks[1 - micro]
        both = jnp.concatenate([query, grad], axis=0)
        logs = jnp.concatenate(
            [lse_ref[end][:, micro * HEAD_DIM : micro * HEAD_DIM + 1] for end in ends], axis=0
        )

        def keys_at(span, micro=micro):
            return jnp.concatenate(
                [load(1 + micro, span * SPAN + spot) for spot in range(SPAN)], axis=0
            )

        def first_pass(span, delta, both=both, logs=logs, keys_at=keys_at):
            products = dot_rt(both, keys_at(span))
            weights = jnp.exp(products[: 2 * BLOCK] - logs)
            grad_weights = products[2 * BLOCK :]
            p_ref[span] = weights
            dp_ref[span] = grad_weights
            return delta + jnp.sum(weights * grad_weights, axis=1, keepdims=True)

        delta = lax.fori_loop(0, spans, first_pass, jnp.zeros((2 * BLOCK, 1), F32))

        def second_pass(span, carry, delta=delta, both=both, keys_at=keys_at, micro=micro):
            weights = p_ref[span]
            grad_scores = weights * (dp_ref[span] - delta)
            stacked = jnp.concatenate([grad_scores, weights], axis=0).astype(BF16)
            shares = dot_lt(stacked, both)
            for spot in range(SPAN):
                sums_ref[micro, span * SPAN + spot] += shares[spot * BLOCK : (spot + 1) * BLOCK]
            return carry + dot(stacked[: 2 * BLOCK], keys_at(span))

        results.append(
            lax.fori_loop(0, spans, second_pass, jnp.zeros((2 * BLOCK, LANES), F32))
        )
    for place, end in enumerate(ends):
        rows = slice(place * BLOCK, (place + 1) * BLOCK)
        out_ref[end // local, 0, end % local] = (
            jnp.where(low, results[0][rows], results[1][rows]) * SCALE
        ).astype(BF16)

    def finish(block, carry):
        for micro in range(2):
            out_ref[block // local, 1 + micro, block % local] = sums_ref[micro, block].astype(BF16)
        return carry

    lax.fori_loop(0, blocks, finish, 0)


def attention_backward(table, qkv, grad, lse):
    groups, _, local, _, _ = qkv.shape
    blocks = groups * local
    spans = VMEM((blocks // SPAN, 2 * BLOCK, SPAN * BLOCK), F32)
    return pl.pallas_call(
        attend_back_kernel,
        out_shape=jax.ShapeDtypeStruct(qkv.shape, BF16),
        in_specs=[whole(pltpu.SMEM), whole(), whole(), whole()],
        out_specs=whole(),
        scratch_shapes=[VMEM((2, blocks, BLOCK, LANES), F32), spans, spans],
        compiler_params=params_of(48),
        name="attention_backward",
    )(table, qkv, grad, lse)


def middle_kernel(
    mixed_in_ref,
    x_ref,
    dy_ref,
    w_out_ref,
    out_shift_ref,
    gain_ref,
    shift_ref,
    up_shift_ref,
    down_shift_ref,
    w_up_ref,
    w_down_ref,
    hidden_ref,
    send_ref,
    dres_ref,
    g_out_ref,
    g_up_ref,
    g_down_ref,
    g_up_bias_ref,
    g_small_ref,
    mixed_ref,
    residual_ref,
    second_ref,
    second_t_ref,
    total_ref,
    dsecond_ref,
):
    micro, rows, _ = x_ref.shape
    step = pl.program_id(0)
    low = low_lanes(rows)

    @pl.when(step == 0)
    def _():
        for pair in range(HEADS // 2):
            even = mixed_in_ref[head_place(2 * pair)].astype(F32)
            odd = mixed_in_ref[head_place(2 * pair + 1)].astype(F32)
            columns = slice(pair * LANES, (pair + 1) * LANES)
            mixed_ref[:rows, columns] = jnp.where(low, swap_halves(even), odd).astype(BF16)
            mixed_ref[rows:, columns] = jnp.where(low, even, swap_halves(odd)).astype(BF16)
        residual = x_ref[...].reshape(micro * rows, D).astype(F32) + (
            dot(mixed_ref[...], w_out_ref[...]) + out_shift_ref[...]
        )
        residual_ref[...] = residual
        normal, _ = norm_parts(residual)
        second = normal * gain_ref[...] + shift_ref[...]
        second_ref[...] = second.astype(BF16)
        second_t_ref[...] = second.T.astype(BF16)
        total_ref[...] = jnp.zeros_like(total_ref)
        dsecond_ref[...] = jnp.zeros_like(dsecond_ref)

    upper = dot(second_ref[...], w_up_ref[...]) + up_shift_ref[...]
    factor = 0.7978845608028654
    square = upper * upper
    bent = jnp.tanh(factor * (upper + 0.044715 * (upper * square)))
    half = 0.5 * (1.0 + bent)
    active = (upper * half).astype(BF16)
    slope = half + 0.5 * upper * (1.0 - bent * bent) * (
        factor + (3.0 * 0.044715 * factor) * square
    )
    dy = dy_ref[...]
    total_ref[...] += dot(active, w_down_ref[...])
    g_down_ref[...] = dot_lt(active, dy).astype(g_down_ref.dtype)
    dupper = (dot_rt(dy, w_down_ref[...]) * slope).astype(BF16)
    g_up_bias_ref[...] = jnp.sum(dupper.astype(F32), axis=0, keepdims=True)
    g_up_ref[...] = dot(second_t_ref[...], dupper).astype(g_up_ref.dtype)
    dsecond_ref[...] += dot_rt(dupper, w_up_ref[...])

    @pl.when(step == pl.num_programs(0) - 1)
    def _():
        residual = residual_ref[...]
        hidden_ref[...] = (
            (residual + (total_ref[...] + down_shift_ref[...])).astype(BF16).reshape(x_ref.shape)
        )
        normal, inverse = norm_parts(residual)
        dsecond = dsecond_ref[...]
        grad_out = dy_ref[...].astype(F32)
        g_small_ref[0:1] = jnp.sum(dsecond * normal, axis=0, keepdims=True)
        g_small_ref[1:2] = jnp.sum(dsecond, axis=0, keepdims=True)
        g_small_ref[2:3] = jnp.sum(grad_out, axis=0, keepdims=True)
        dres = grad_out + norm_pull(dsecond, normal, inverse, gain_ref[...])
        dres_ref[...] = dres
        branch = dres.astype(BF16)
        g_small_ref[3:4] = jnp.sum(branch.astype(F32), axis=0, keepdims=True)
        g_out_ref[...] = dot_lt(mixed_ref[...], branch).astype(g_out_ref.dtype)
        dmixed = dot_rt(branch, w_out_ref[...])
        for pair in range(HEADS // 2):
            part = dmixed[:, pair * LANES : (pair + 1) * LANES]
            first, last = part[:rows], part[rows:]
            even = jnp.where(low, last, swap_halves(first))
            odd = jnp.where(low, swap_halves(last), first)
            send_ref[head_place(2 * pair)] = even.astype(BF16)
            send_ref[head_place(2 * pair + 1)] = odd.astype(BF16)


def middle(mixed_in, x, dy, w_out, out_shift, gain, shift, up_shift, down_shift, w_up, w_down, kind):
    micro, rows, _ = x.shape
    tokens = micro * rows
    groups = mixed_in.shape[0]

    def fixed(shape):
        return pl.BlockSpec(shape, lambda step: (0,) * len(shape))

    vector = fixed((1, D))
    steps = FF // CHUNK
    return pl.pallas_call(
        middle_kernel,
        grid=(steps,),
        out_shape=(
            jax.ShapeDtypeStruct(x.shape, BF16),
            jax.ShapeDtypeStruct((groups, rows, LANES), BF16),
            jax.ShapeDtypeStruct((tokens, D), F32),
            jax.ShapeDtypeStruct((D, D), kind),
            jax.ShapeDtypeStruct((D, FF), kind),
            jax.ShapeDtypeStruct((FF, D), kind),
            jax.ShapeDtypeStruct((1, FF), F32),
            jax.ShapeDtypeStruct((4, D), F32),
        ),
        in_specs=[
            fixed(mixed_in.shape),
            fixed(x.shape),
            fixed((tokens, D)),
            fixed((D, D)),
            vector,
            vector,
            vector,
            pl.BlockSpec((1, CHUNK), lambda step: (0, step)),
            vector,
            pl.BlockSpec((D, CHUNK), lambda step: (0, step)),
            pl.BlockSpec((CHUNK, D), lambda step: (step, 0)),
        ],
        out_specs=(
            fixed(x.shape),
            fixed((groups, rows, LANES)),
            fixed((tokens, D)),
            fixed((D, D)),
            pl.BlockSpec((D, CHUNK), lambda step: (0, step)),
            pl.BlockSpec((CHUNK, D), lambda step: (step, 0)),
            pl.BlockSpec((1, CHUNK), lambda step: (0, step)),
            fixed((4, D)),
        ),
        scratch_shapes=[
            VMEM((tokens, D), BF16),
            VMEM((tokens, D), F32),
            VMEM((tokens, D), BF16),
            VMEM((D, tokens), BF16),
            VMEM((tokens, D), F32),
            VMEM((tokens, D), F32),
        ],
        compiler_params=params_of(56),
        name="middle",
    )(mixed_in, x, dy, w_out, out_shift, gain, shift, up_shift, down_shift, w_up, w_down)


def qkv_back_kernel(
    recv_ref,
    normed_ref,
    x_ref,
    dres_ref,
    gain_ref,
    w_ref,
    grad_ref,
    g_qkv_ref,
    g_bias_ref,
    g_small_ref,
    packed_ref,
    normed_t_ref,
    dnormed_ref,
):
    micro, rows, _ = x_ref.shape
    step = pl.program_id(0)
    low = low_lanes(rows)

    @pl.when(step == 0)
    def _():
        for pair in range(HEADS // 2):
            even = recv_ref[head_place(2 * pair), 0].astype(F32)
            odd = recv_ref[head_place(2 * pair + 1), 0].astype(F32)
            spot, columns = pair // 2, slice((pair % 2) * LANES, (pair % 2 + 1) * LANES)
            packed_ref[spot, :rows, columns] = jnp.where(low, even, swap_halves(odd)).astype(BF16)
            packed_ref[spot, rows:, columns] = jnp.where(low, swap_halves(even), odd).astype(BF16)
        for head in range(HEADS):
            spot = D // CHUNK + head // 2
            columns = slice((head % 2) * LANES, (head % 2 + 1) * LANES)
            packed_ref[spot, :rows, columns] = recv_ref[head_place(head), 1]
            packed_ref[spot, rows:, columns] = swap_halves(
                recv_ref[head_place(head), 2].astype(F32)
            ).astype(BF16)
        normed_t_ref[...] = normed_ref[...].astype(F32).T.astype(BF16)
        dnormed_ref[...] = jnp.zeros_like(dnormed_ref)

    packed = packed_ref[step]
    g_bias_ref[...] = jnp.sum(packed.astype(F32), axis=0, keepdims=True)
    g_qkv_ref[...] = dot(normed_t_ref[...], packed).astype(g_qkv_ref.dtype)
    dnormed_ref[...] += dot_rt(packed, w_ref[...])

    @pl.when(step == pl.num_programs(0) - 1)
    def _():
        normal, inverse = norm_parts(x_ref[...].reshape(micro * rows, D).astype(F32))
        dnormed = dnormed_ref[...]
        g_small_ref[0:1] = jnp.sum(dnormed * normal, axis=0, keepdims=True)
        g_small_ref[1:2] = jnp.sum(dnormed, axis=0, keepdims=True)
        grad = dres_ref[...] + norm_pull(dnormed, normal, inverse, gain_ref[...])
        grad_ref[...] = grad.reshape(x_ref.shape)


def qkv_backward(recv, normed, x, dres, gain, w, kind):
    micro, rows, _ = x.shape
    tokens = micro * rows

    def fixed(shape):
        return pl.BlockSpec(shape, lambda step: (0,) * len(shape))

    steps = 3 * D // CHUNK
    return pl.pallas_call(
        qkv_back_kernel,
        grid=(steps,),
        out_shape=(
            jax.ShapeDtypeStruct(x.shape, F32),
            jax.ShapeDtypeStruct((D, 3 * D), kind),
            jax.ShapeDtypeStruct((1, 3 * D), F32),
            jax.ShapeDtypeStruct((2, D), F32),
        ),
        in_specs=[
            fixed(recv.shape),
            fixed((tokens, D)),
            fixed(x.shape),
            fixed((tokens, D)),
            fixed((1, D)),
            pl.BlockSpec((D, CHUNK), lambda step: (0, step)),
        ],
        out_specs=(
            fixed(x.shape),
            pl.BlockSpec((D, CHUNK), lambda step: (0, step)),
            pl.BlockSpec((1, CHUNK), lambda step: (0, step)),
            fixed((2, D)),
        ),
        scratch_shapes=[
            VMEM((steps, tokens, CHUNK), BF16),
            VMEM((D, tokens), BF16),
            VMEM((tokens, D), F32),
        ],
        compiler_params=params_of(56),
        name="qkv_backward",
    )(recv, normed, x, dres, gain, w)


AXES = ("gx", "gy")


def gather(array):
    return lax.all_gather(array, AXES, axis=0, tiled=True)


def scatter(array):
    return lax.psum_scatter(array, AXES, scatter_dimension=0, tiled=True)


def exchange(array):
    return lax.all_to_all(array, "gy", 0, 0, tiled=True)


def by_heads(w_qkv):
    rows = w_qkv.shape[0]
    sides = w_qkv[:, D:].reshape(rows, 2, HEADS, HEAD_DIM)
    return jnp.concatenate([w_qkv[:, :D], jnp.swapaxes(sides, 1, 2).reshape(rows, 2 * D)], axis=1)


def by_parts(w_qkv):
    rows = w_qkv.shape[0]
    sides = w_qkv[:, D:].reshape(rows, HEADS, 2, HEAD_DIM)
    return jnp.concatenate([w_qkv[:, :D], jnp.swapaxes(sides, 1, 2).reshape(rows, 2 * D)], axis=1)


def general_shards(
    hidden_in,
    rand_table,
    norm1_gain,
    norm1_bias,
    w_qkv,
    query_bias,
    value_bias,
    w_out,
    out_bias,
    norm2_gain,
    norm2_bias,
    w_up,
    up_bias,
    w_down,
    down_bias,
    cotangent,
):
    micro, rows, _ = hidden_in.shape
    groups = lax.axis_size("gy")
    local = rows // BLOCK
    own = norm1_gain.shape[0]

    vectors = jnp.concatenate(
        [
            norm1_gain,
            norm1_bias,
            query_bias,
            value_bias,
            out_bias,
            norm2_gain,
            norm2_bias,
            down_bias,
            up_bias,
        ]
    )
    table = lax.all_gather(rand_table, "gy", axis=1, tiled=True)
    table = table.reshape(micro, groups * local * RANDOM)
    vectors = gather(vectors[None]).astype(F32)
    gain_one, shift_one, query_shift, value_shift, out_shift, gain_two, shift_two, down_shift = (
        vectors[:, number * own : (number + 1) * own].reshape(1, D) for number in range(8)
    )
    up_shift = vectors[:, 8 * own :].reshape(1, FF)
    w_qkv_full = gather(by_heads(w_qkv))
    w_out_full, w_up_full, w_down_full = gather(w_out), gather(w_up), gather(w_down)
    packed_bias = by_heads(
        jnp.concatenate([query_shift, jnp.zeros_like(query_shift), value_shift], axis=1)
    )

    normed, send = qkv_forward(hidden_in, gain_one, shift_one, w_qkv_full, packed_bias, groups)
    qkv = exchange(send).reshape(groups, 3, local, BLOCK, LANES)
    mixed, lse = attention_forward(table, qkv)
    mixed_back = exchange(mixed.reshape(groups, rows, LANES))
    hidden_out, grad_send, dres, g_out, g_up, g_down, g_up_bias, g_mid = middle(
        mixed_back,
        hidden_in,
        cotangent.reshape(micro * rows, D),
        w_out_full,
        out_shift,
        gain_two,
        shift_two,
        up_shift,
        down_shift,
        w_up_full,
        w_down_full,
        F32,
    )
    grad_mixed = exchange(grad_send).reshape(groups, local, BLOCK, LANES)
    dqkv = attention_backward(table, qkv, grad_mixed, lse)
    dqkv_back = exchange(dqkv.reshape(groups, 3, rows, LANES))
    grad_hidden, g_qkv, g_packed, g_first = qkv_backward(
        dqkv_back, normed, hidden_in, dres, gain_one, w_qkv_full, F32
    )

    g_packed = by_parts(g_packed)
    small = [
        g_first[0],
        g_first[1],
        g_packed[0, :D],
        g_packed[0, 2 * D :],
        g_mid[3],
        g_mid[0],
        g_mid[1],
        g_mid[2],
    ]
    ranks = D // own
    small = jnp.concatenate(
        [item.reshape(ranks, own) for item in small] + [g_up_bias.reshape(ranks, 4 * own)], axis=1
    )
    small = scatter(small)[0]
    parts = [small[number * own : (number + 1) * own] for number in range(8)]
    return (
        hidden_out,
        grad_hidden,
        parts[0],
        parts[1],
        by_parts(scatter(g_qkv)),
        parts[2],
        parts[3],
        scatter(g_out),
        parts[4],
        parts[5],
        parts[6],
        scatter(g_up),
        small[8 * own :],
        scatter(g_down),
        parts[7],
    )


MESH = pl.DeviceIdType.MESH
ANY = pl.ANY
PLANES = 4
SPOTS = 4
PIECES = 2
RANKS = 2 * PLANES * SPOTS
TILES = 3 * D // LANES
HALF_TILES = TILES // 2
QUERY_ORDER = (0, 2, 3, 5, 6, 8, 9, 11, 1, 4, 7, 10)


def column_order():
    order = [("q", head) for head in QUERY_ORDER]
    for spot in range(SPOTS):
        for place in (2 * 3 * spot, 2 * 3 * spot + 2):
            order += [("k", place // 2), ("v", place // 2)]
        order += [("v", 3 * spot + 2), ("k", 3 * spot + 2)]
    return order


def natural_block(entry):
    return "qkv".index(entry[0]) * HEADS + entry[1]


def take_blocks(array, order):
    parts = []
    start = 0
    while start < len(order):
        stop = start + 1
        while stop < len(order) and order[stop] == order[stop - 1] + 1:
            stop += 1
        parts.append(array[..., order[start] * HEAD_DIM : (order[start] + stop - start) * HEAD_DIM])
        start = stop
    return jnp.concatenate(parts, axis=-1)


def flip(value, bits):
    if bits == 0:
        return value
    if bits == 1:
        return value + 1 - 2 * lax.rem(value, 2)
    if bits == 2:
        return value + 2 - 4 * lax.div(value, 2)
    return 3 - value


def place_here():
    core, rank = lax.axis_index("gx"), lax.axis_index("gy")
    return core, lax.div(rank, SPOTS), lax.rem(rank, SPOTS)


def rank_of(plane, spot):
    return plane * SPOTS + spot


def greet(partners):
    barrier = pltpu.get_barrier_semaphore()
    for partner in partners:
        pl.semaphore_signal(barrier, inc=1, device_id=partner, device_id_type=MESH)
    pl.semaphore_wait(barrier, len(partners))


def remote(source, target, send_sem, recv_sem, device):
    return pltpu.make_async_remote_copy(
        src_ref=source,
        dst_ref=target,
        send_sem=send_sem,
        recv_sem=recv_sem,
        device_id=device,
        device_id_type=MESH,
    )


def column_partners(core, plane, spot):
    partners = [(1 - core, rank_of(plane, spot))]
    for bits in range(1, PLANES):
        for other in (core, 1 - core):
            partners.append((other, rank_of(flip(plane, bits), spot)))
    return partners


def all_partners(core, plane, spot):
    return column_partners(core, plane, spot) + [
        (core, rank_of(plane, flip(spot, 1))),
        (core, rank_of(plane, flip(spot, 2))),
    ]


def to_planes(source, target, send_sem, recv_sem, local_sem):
    core, plane, spot = place_here()
    half, odd = lax.div(plane, 2), lax.rem(plane, 2)
    sends, keeps = [], []
    for micro in range(2):
        goal = 2 * micro + core
        here = (goal == plane) & (half == core)
        send = remote(
            source.at[micro],
            target.at[odd],
            send_sem.at[micro],
            recv_sem.at[odd],
            (half, rank_of(goal, spot)),
        )
        keep = pltpu.make_async_copy(source.at[micro], target.at[odd], local_sem.at[micro])

        @pl.when(jnp.logical_not(here))
        def _(send=send):
            send.start()

        @pl.when(here)
        def _(keep=keep):
            keep.start()

        sends.append((here, send))
        keeps.append((here, keep))

    def finish():
        for piece in range(PIECES):
            mine = (odd == core) & (plane == 2 * core + piece)
            arrival = remote(
                source.at[0],
                target.at[piece],
                send_sem.at[0],
                recv_sem.at[piece],
                (core, rank_of(plane, spot)),
            )

            @pl.when(jnp.logical_not(mine))
            def _(arrival=arrival):
                arrival.wait_recv()

        for (here, send), (_, keep) in zip(sends, keeps):

            @pl.when(jnp.logical_not(here))
            def _(send=send):
                send.wait_send()

            @pl.when(here)
            def _(keep=keep):
                keep.wait()

    return finish


def from_planes(source, target, send_sem, recv_sem, local_sem):
    core, plane, spot = place_here()
    micro, odd = lax.div(plane, 2), lax.rem(plane, 2)
    sends, keeps = [], []
    for piece in range(PIECES):
        goal = 2 * core + piece
        here = (goal == plane) & (odd == core)
        send = remote(
            source.at[piece],
            target.at[micro],
            send_sem.at[piece],
            recv_sem.at[micro],
            (odd, rank_of(goal, spot)),
        )
        keep = pltpu.make_async_copy(source.at[piece], target.at[micro], local_sem.at[piece])

        @pl.when(jnp.logical_not(here))
        def _(send=send):
            send.start()

        @pl.when(here)
        def _(keep=keep):
            keep.start()

        sends.append((here, send))
        keeps.append((here, keep))

    def finish():
        for number in range(2):
            mine = (2 * number + core == plane) & (micro == core)
            arrival = remote(
                source.at[0],
                target.at[number],
                send_sem.at[0],
                recv_sem.at[number],
                (core, rank_of(plane, spot)),
            )

            @pl.when(jnp.logical_not(mine))
            def _(arrival=arrival):
                arrival.wait_recv()

        for (here, send), (_, keep) in zip(sends, keeps):

            @pl.when(jnp.logical_not(here))
            def _(send=send):
                send.wait_send()

            @pl.when(here)
            def _(keep=keep):
                keep.wait()

    return finish


class Gather:
    SENDS = 31

    def __init__(self, source, target, send_sem, recv_sem, local_sem):
        self.source, self.target = source, target
        self.send_sem, self.recv_sem = send_sem, recv_sem
        self.core, self.plane, self.spot = place_here()
        self.sends = []
        self.own = pltpu.make_async_copy(
            source, target.at[self.core, self.plane, self.spot], local_sem
        )
        self.own.start()

    def send(self, source, plane, spot, device):
        copy = remote(
            source,
            self.target.at[self.core, plane, spot],
            self.send_sem.at[len(self.sends)],
            self.recv_sem.at[self.core, plane, spot],
            device,
        )
        copy.start()
        self.sends.append(copy)

    def arrive(self, core, plane, spot):
        shard = self.target.at[core, plane, spot]
        remote(
            shard,
            shard,
            self.send_sem.at[0],
            self.recv_sem.at[core, plane, spot],
            (self.core, rank_of(self.plane, self.spot)),
        ).wait_recv()

    def neighbour(self, bits):
        return (self.core, rank_of(self.plane, flip(self.spot, bits)))

    def sibling(self):
        return (1 - self.core, rank_of(self.plane, self.spot))

    def start(self):
        for bits in range(1, PLANES):
            goal = (self.core, rank_of(flip(self.plane, bits), self.spot))
            self.send(self.source, self.plane, self.spot, goal)
        for goal in (self.neighbour(1), self.neighbour(2), self.sibling()):
            self.send(self.source, self.plane, self.spot, goal)

    def column(self):
        for bits in range(1, PLANES):
            plane = flip(self.plane, bits)
            self.arrive(self.core, plane, self.spot)
            shard = self.target.at[self.core, plane, self.spot]
            for goal in (self.neighbour(1), self.neighbour(2), self.sibling()):
                self.send(shard, plane, self.spot, goal)

    def across(self):
        for bits in range(PLANES):
            plane = flip(self.plane, bits)
            for side in (1, 2):
                spot = flip(self.spot, side)
                self.arrive(self.core, plane, spot)
                shard = self.target.at[self.core, plane, spot]
                if (side == 1) == (bits < 2):
                    self.send(shard, plane, spot, self.neighbour(3 - side))
                self.send(shard, plane, spot, self.sibling())

    def corner(self):
        spot = flip(self.spot, 3)
        for bits in range(PLANES):
            plane = flip(self.plane, bits)
            self.arrive(self.core, plane, spot)
            self.send(self.target.at[self.core, plane, spot], plane, spot, self.sibling())

    def finish(self):
        for bits in range(PLANES):
            for side in range(SPOTS):
                self.arrive(1 - self.core, flip(self.plane, bits), flip(self.spot, side))
        self.own.wait()
        for copy in self.sends:
            copy.wait_send()


def settle(shards_ref, out_ref, tiles_of):
    rows = shards_ref.shape[3] // 2
    width = shards_ref.shape[4]

    def pair(number, carry):
        core, plane, side = (
            lax.div(number, 2 * PLANES),
            lax.rem(lax.div(number, 2), PLANES),
            lax.rem(number, 2),
        )
        goal = pl.ds(pl.multiple_of(number * 2 * rows, 16), 2 * rows)
        for tile in range(width // LANES):
            columns = slice(tile * LANES, (tile + 1) * LANES)
            first = shards_ref[core, plane, 2 * side, :, columns].astype(F32)
            second = shards_ref[core, plane, 2 * side + 1, :, columns].astype(F32)
            left, right = tiles_of(tile)
            out_ref[goal, left * LANES : (left + 1) * LANES] = jnp.concatenate(
                [first[:rows], second[:rows]], axis=0
            ).astype(BF16)
            out_ref[goal, right * LANES : (right + 1) * LANES] = jnp.concatenate(
                [first[rows:], second[rows:]], axis=0
            ).astype(BF16)
        return carry

    lax.fori_loop(0, RANKS // 2, pair, 0)


def alternate(tile):
    return 2 * tile, 2 * tile + 1


def in_order(tile):
    return tile, D // LANES // 2 + tile


def collect_kernel(
    x_ref,
    dy_ref,
    vec_ref,
    s_qkv_ref,
    s_out_ref,
    s_up_ref,
    s_down_ref,
    xs_ref,
    dys_ref,
    vecs_ref,
    w_qkv_ref,
    w_out_ref,
    w_up_ref,
    w_down_ref,
    g_qkv_ref,
    g_out_ref,
    g_up_ref,
    send_sem,
    recv_sem,
    local_sem,
    move_send,
    move_recv,
    move_local,
):
    core, plane, spot = place_here()
    greet(all_partners(core, plane, spot))
    pairs = (
        (vec_ref, vecs_ref),
        (s_qkv_ref, g_qkv_ref),
        (s_out_ref, g_out_ref),
        (s_up_ref, g_up_ref),
        (s_down_ref, w_down_ref),
    )
    finish_x = to_planes(x_ref, xs_ref, move_send.at[0], move_recv.at[0], move_local.at[0])
    gathers = []
    for number, (source, target) in enumerate(pairs):
        one = Gather(
            source, target, send_sem.at[number], recv_sem.at[number], local_sem.at[number]
        )
        one.start()
        gathers.append(one)
    finish_dy = to_planes(dy_ref, dys_ref, move_send.at[1], move_recv.at[1], move_local.at[1])
    for one in gathers:
        one.column()
    for one in gathers:
        one.across()
    for one in gathers:
        one.corner()
    for one in gathers:
        one.finish()
    settle(g_qkv_ref, w_qkv_ref, alternate)
    settle(g_out_ref, w_out_ref, in_order)
    settle(g_up_ref, w_up_ref, alternate)
    finish_x()
    finish_dy()


def collect(x, dy, vec, s_qkv, s_out, s_up, s_down):
    grid = (2, PLANES, SPOTS)
    count = 5
    return pl.pallas_call(
        collect_kernel,
        out_shape=(
            jax.ShapeDtypeStruct(x.shape, BF16),
            jax.ShapeDtypeStruct(dy.shape, BF16),
            jax.ShapeDtypeStruct(grid + vec.shape, BF16),
            jax.ShapeDtypeStruct((D, 3 * D), BF16),
            jax.ShapeDtypeStruct((D, D), BF16),
            jax.ShapeDtypeStruct((D, FF), BF16),
            jax.ShapeDtypeStruct(grid + s_down.shape, BF16),
        ),
        in_specs=[whole(ANY)] * 7,
        out_specs=(whole(ANY), whole(ANY), whole(ANY), whole(), whole(), whole(), whole(ANY)),
        scratch_shapes=[
            VMEM(grid + s_qkv.shape, BF16),
            VMEM(grid + s_out.shape, BF16),
            VMEM(grid + s_up.shape, BF16),
            pltpu.SemaphoreType.DMA((count, Gather.SENDS)),
            pltpu.SemaphoreType.DMA((count,) + grid),
            pltpu.SemaphoreType.DMA((count,)),
            pltpu.SemaphoreType.DMA((2, 2)),
            pltpu.SemaphoreType.DMA((2, 2)),
            pltpu.SemaphoreType.DMA((2, 2)),
        ],
        compiler_params=pltpu.CompilerParams(
            vmem_limit_bytes=56 * 1024 * 1024, collective_id=1, has_side_effects=True
        ),
        name="collect",
    )(x, dy, vec, s_qkv, s_out, s_up, s_down)


def plane_partners(core, plane, spot):
    partners = []
    for other in (core, 1 - core):
        for side in range(SPOTS):
            if other is core and side == 0:
                continue
            partners.append((other, rank_of(plane, flip(spot, side))))
    return partners


def outward_kernel(source_ref, target_ref, send_sem, recv_sem, local_sem):
    core, plane, spot = place_here()
    greet(plane_partners(core, plane, spot))
    sends, keeps = [], []
    for side in (3, 1, 2, 0):
        for other in (core, 1 - core):
            goal = flip(spot, side)
            for piece in range(PIECES):
                source = source_ref.at[other, goal, piece]
                target = target_ref.at[2 * core + piece, spot]
                if side == 0 and other is core:
                    copy = pltpu.make_async_copy(source, target, local_sem.at[piece])
                    keeps.append(copy)
                else:
                    copy = remote(
                        source,
                        target,
                        send_sem.at[len(sends)],
                        recv_sem.at[2 * core + piece, spot],
                        (other, rank_of(plane, goal)),
                    )
                    sends.append(copy)
                copy.start()
    for side in range(SPOTS):
        for other in (core, 1 - core):
            if side == 0 and other is core:
                continue
            for piece in range(PIECES):
                target = target_ref.at[2 * other + piece, flip(spot, side)]
                remote(
                    target,
                    target,
                    send_sem.at[0],
                    recv_sem.at[2 * other + piece, flip(spot, side)],
                    (core, rank_of(plane, spot)),
                ).wait_recv()
    for copy in sends:
        copy.wait_send()
    for copy in keeps:
        copy.wait()


def inward_kernel(source_ref, target_ref, send_sem, recv_sem, local_sem):
    core, plane, spot = place_here()
    greet(plane_partners(core, plane, spot))
    sends, keeps = [], []
    for side in (3, 1, 2, 0):
        for other in (core, 1 - core):
            goal = flip(spot, side)
            for piece in range(PIECES):
                source = source_ref.at[2 * other + piece, goal]
                target = target_ref.at[core, spot, piece]
                if side == 0 and other is core:
                    copy = pltpu.make_async_copy(source, target, local_sem.at[piece])
                    keeps.append(copy)
                else:
                    copy = remote(
                        source,
                        target,
                        send_sem.at[len(sends)],
                        recv_sem.at[core, spot, piece],
                        (other, rank_of(plane, goal)),
                    )
                    sends.append(copy)
                copy.start()
    for side in range(SPOTS):
        for other in (core, 1 - core):
            if side == 0 and other is core:
                continue
            for piece in range(PIECES):
                target = target_ref.at[other, flip(spot, side), piece]
                remote(
                    target,
                    target,
                    send_sem.at[0],
                    recv_sem.at[other, flip(spot, side), piece],
                    (core, rank_of(plane, spot)),
                ).wait_recv()
    for copy in sends:
        copy.wait_send()
    for copy in keeps:
        copy.wait()


def plane_exchange(kernel, source, shape, recv_shape, collective, name):
    return pl.pallas_call(
        kernel,
        out_shape=jax.ShapeDtypeStruct(shape, source.dtype),
        in_specs=[whole(ANY)],
        out_specs=whole(ANY),
        scratch_shapes=[
            pltpu.SemaphoreType.DMA((14,)),
            pltpu.SemaphoreType.DMA(recv_shape),
            pltpu.SemaphoreType.DMA((PIECES,)),
        ],
        compiler_params=pltpu.CompilerParams(
            vmem_limit_bytes=16 * 1024 * 1024, collective_id=collective, has_side_effects=True
        ),
        name=name,
    )(source)


def outward(source, collective, name):
    shape = (PLANES, SPOTS) + source.shape[3:]
    return plane_exchange(outward_kernel, source, shape, (PLANES, SPOTS), collective, name)


def inward(source, collective, name):
    shape = (2, SPOTS, PIECES) + source.shape[2:]
    return plane_exchange(
        inward_kernel, source, shape, (2, SPOTS, PIECES), collective, name
    )


def plane_qkv_kernel(x_ref, vec_ref, w_ref, bias_ref, normed_ref, send_ref):
    pieces, rows, _ = x_ref.shape
    values = x_ref[...].reshape(pieces * rows, D).astype(F32)
    normal, _ = norm_parts(values)
    normed_ref[...] = (normal * vec_ref[0:1] + vec_ref[1:2]).astype(BF16)
    low = low_lanes(rows)
    queries = D // LANES
    for chunk in range(HALF_TILES):
        columns = slice(chunk * CHUNK, (chunk + 1) * CHUNK)
        packed = dot(normed_ref[...], w_ref[:, columns]) + bias_ref[:, columns]
        for side in range(2):
            tile = chunk + side * HALF_TILES
            whole_tile = packed[:, side * LANES : (side + 1) * LANES]
            if tile < queries:
                whole_tile = whole_tile.astype(BF16).astype(F32) * SCALE
            for piece in range(pieces):
                part = whole_tile[piece * rows : (piece + 1) * rows]
                if tile < SPOTS:
                    send_ref[0, tile, piece, 0] = part.astype(BF16)
                elif tile < queries:
                    first = 2 * (tile - SPOTS)
                    shared = send_ref[0, first, piece, 0].astype(F32)
                    send_ref[1, first, piece, 0] = jnp.where(low, part, shared).astype(BF16)
                    shared = send_ref[0, first + 1, piece, 0].astype(F32)
                    send_ref[1, first + 1, piece, 0] = jnp.where(
                        low, swap_halves(part), shared
                    ).astype(BF16)
                else:
                    spot, role = (tile - queries) // 3, (tile - queries) % 3
                    if role < 2:
                        send_ref[role, spot, piece, 1] = part.astype(BF16)
                    else:
                        send_ref[0, spot, piece, 2] = part.astype(BF16)
                        send_ref[1, spot, piece, 2] = part.astype(BF16)


def plane_qkv(x, vec, w, bias):
    pieces, rows, _ = x.shape
    return pl.pallas_call(
        plane_qkv_kernel,
        out_shape=(
            jax.ShapeDtypeStruct((pieces * rows, D), BF16),
            jax.ShapeDtypeStruct((2, SPOTS, PIECES, 3, rows, LANES), BF16),
        ),
        in_specs=[whole()] * 4,
        out_specs=(whole(), whole()),
        compiler_params=params_of(48),
        name="plane_qkv",
    )(x, vec, w, bias)


def plane_attend_kernel(table_ref, qkv_ref, out_ref, lse_ref, s_ref, t_ref):
    groups, _, local, _, _ = qkv_ref.shape
    blocks = groups * local
    half = blocks // 2
    core = lax.axis_index("gx")
    low = low_lanes(BLOCK)
    masks = [half_mask(True), half_mask(False)]

    def load(component, block):
        return qkv_ref[lax.div(block, local), component, lax.rem(block, local)]

    def store(block, value):
        out_ref[lax.div(block, local), lax.rem(block, local)] = value.astype(BF16)

    def one(block, slot, ids, bias):
        keys = jnp.concatenate([load(1 + slot, spot) for spot in ids], axis=0)
        scores = dot_rt(load(0, block) * masks[slot], keys) + bias
        top = jnp.max(scores, axis=1, keepdims=True)
        powered = jnp.exp(scores - top)
        total = jnp.sum(powered, axis=1, keepdims=True)
        mixed = dot(powered.astype(BF16), keys) * (1.0 / total)
        return mixed, top + jnp.log(total)

    def sparse(step, carry):
        mine = 1 + step + core * (half - 1)
        other = 1 + step + (1 - core) * (half - 1)
        ids, bias = slots_of(table_ref, 0, mine, blocks)
        far_ids, far_bias = slots_of(table_ref, 0, other, blocks)
        mixed_a, log_a = one(mine, 0, ids, bias)
        mixed_b, log_b = one(mine, 1, ids, bias)
        mixed_c, log_c = one(other, 0, far_ids, far_bias)
        store(mine, jnp.where(low, mixed_b, mixed_a))
        store(other, mixed_c)
        lse_ref[mine] = jnp.where(low, log_a, log_b)
        lse_ref[other] = jnp.where(low, log_c, 0.0)
        return carry

    lax.fori_loop(0, half - 1, sparse, 0)

    spans = blocks // SPAN
    ends = (0, blocks - 1)
    end = core * (blocks - 1)
    query_a = jnp.concatenate([load(0, number) for number in ends], axis=0) * masks[0]
    query_b = load(0, end) * masks[1]

    def keys_at(span, slot):
        return jnp.concatenate(
            [load(1 + slot, span * SPAN + number) for number in range(SPAN)], axis=0
        )

    def first_pass(span, carry):
        top_a, top_b = carry
        scores_a = dot_rt(query_a, keys_at(span, 0))
        scores_b = dot_rt(query_b, keys_at(span, 1))
        s_ref[span] = scores_a
        t_ref[span] = scores_b
        return (
            jnp.maximum(top_a, jnp.max(scores_a, axis=1, keepdims=True)),
            jnp.maximum(top_b, jnp.max(scores_b, axis=1, keepdims=True)),
        )

    top_a, top_b = lax.fori_loop(
        0,
        spans,
        first_pass,
        (jnp.full((2 * BLOCK, 1), NEGATIVE, F32), jnp.full((BLOCK, 1), NEGATIVE, F32)),
    )

    def second_pass(span, carry):
        total_a, mixed_a, total_b, mixed_b = carry
        powered_a = jnp.exp(s_ref[span] - top_a)
        powered_b = jnp.exp(t_ref[span] - top_b)
        return (
            total_a + jnp.sum(powered_a, axis=1, keepdims=True),
            mixed_a + dot(powered_a.astype(BF16), keys_at(span, 0)),
            total_b + jnp.sum(powered_b, axis=1, keepdims=True),
            mixed_b + dot(powered_b.astype(BF16), keys_at(span, 1)),
        )

    total_a, mixed_a, total_b, mixed_b = lax.fori_loop(
        0,
        spans,
        second_pass,
        (
            jnp.zeros((2 * BLOCK, 1), F32),
            jnp.zeros((2 * BLOCK, LANES), F32),
            jnp.zeros((BLOCK, 1), F32),
            jnp.zeros((BLOCK, LANES), F32),
        ),
    )
    mixed_a = mixed_a * (1.0 / total_a)
    mixed_b = mixed_b * (1.0 / total_b)
    log_a = top_a + jnp.log(total_a)
    log_b = top_b + jnp.log(total_b)
    for place, number in enumerate(ends):
        rows = slice(place * BLOCK, (place + 1) * BLOCK)
        store(number, jnp.where(low, mixed_b, mixed_a[rows]))
        lse_ref[number] = jnp.where(low, log_a[rows], log_b)


def plane_attention(table, qkv):
    groups, _, local, _, _ = qkv.shape
    blocks = groups * local
    spans = blocks // SPAN
    return pl.pallas_call(
        plane_attend_kernel,
        out_shape=(
            jax.ShapeDtypeStruct((groups, local, BLOCK, LANES), BF16),
            jax.ShapeDtypeStruct((blocks, BLOCK, LANES), F32),
        ),
        in_specs=[whole(pltpu.SMEM), whole()],
        out_specs=(whole(), whole()),
        scratch_shapes=[
            VMEM((spans, 2 * BLOCK, SPAN * BLOCK), F32),
            VMEM((spans, BLOCK, SPAN * BLOCK), F32),
        ],
        compiler_params=params_of(48),
        name="plane_attention",
    )(table, qkv)


def plane_attend_back_kernel(
    table_ref, qkv_ref, grad_ref, lse_ref, out_ref, sums_ref, pa_ref, da_ref, pb_ref, db_ref
):
    groups, _, local, _, _ = qkv_ref.shape
    blocks = groups * local
    half = blocks // 2
    core = lax.axis_index("gx")
    low = low_lanes(BLOCK)
    masks = [half_mask(True), half_mask(False)]

    def load(component, block):
        return qkv_ref[lax.div(block, local), component, lax.rem(block, local)]

    def load_grad(block):
        return grad_ref[lax.div(block, local), lax.rem(block, local)]

    def store(component, block, value):
        out_ref[lax.div(block, local), component, lax.rem(block, local)] = value.astype(BF16)

    def clear(block, carry):
        for slot in range(2):
            sums_ref[slot, block] = jnp.zeros((BLOCK, LANES), F32)
        return carry

    lax.fori_loop(0, blocks, clear, 0)

    def one(block, slot, ids, bias):
        keys = jnp.concatenate([load(1 + slot, spot) for spot in ids], axis=0)
        both = jnp.concatenate(
            [load(0, block) * masks[slot], load_grad(block) * masks[1 - slot]], axis=0
        )
        products = dot_rt(both, keys)
        logs = lse_ref[block][:, slot * HEAD_DIM : slot * HEAD_DIM + 1]
        weights = jnp.exp(products[:BLOCK] + bias - logs)
        grad_weights = products[BLOCK:]
        delta = jnp.sum(weights * grad_weights, axis=1, keepdims=True)
        grad_scores = weights * (grad_weights - delta)
        stacked = jnp.concatenate([grad_scores, weights], axis=0).astype(BF16)
        return dot(stacked[:BLOCK], keys), dot_lt(stacked, both)

    def add(slot, ids, shares):
        for place, spot in enumerate(ids):
            sums_ref[slot, spot] += shares[place * BLOCK : (place + 1) * BLOCK]

    def sparse(step, carry):
        mine = 1 + step + core * (half - 1)
        other = 1 + step + (1 - core) * (half - 1)
        ids, bias = slots_of(table_ref, 0, mine, blocks)
        far_ids, far_bias = slots_of(table_ref, 0, other, blocks)
        query_a, shares_a = one(mine, 0, ids, bias)
        query_b, shares_b = one(mine, 1, ids, bias)
        query_c, shares_c = one(other, 0, far_ids, far_bias)
        store(0, mine, jnp.where(low, query_a, query_b) * SCALE)
        store(0, other, query_c * SCALE)
        add(0, ids, shares_a)
        add(1, ids, shares_b)
        add(0, far_ids, shares_c)
        return carry

    lax.fori_loop(0, half - 1, sparse, 0)

    spans = blocks // SPAN
    ends = (0, blocks - 1)
    end = core * (blocks - 1)
    both_a = jnp.concatenate(
        [load(0, number) * masks[0] for number in ends]
        + [load_grad(number) * masks[1] for number in ends],
        axis=0,
    )
    both_b = jnp.concatenate([load(0, end) * masks[1], load_grad(end) * masks[0]], axis=0)
    logs_a = jnp.concatenate([lse_ref[number][:, 0:1] for number in ends], axis=0)
    logs_b = lse_ref[end][:, HEAD_DIM : HEAD_DIM + 1]

    def keys_at(span, slot):
        return jnp.concatenate(
            [load(1 + slot, span * SPAN + number) for number in range(SPAN)], axis=0
        )

    def first_pass(span, carry):
        deltas = []
        for slot, both, logs, p_ref, d_ref in (
            (0, both_a, logs_a, pa_ref, da_ref),
            (1, both_b, logs_b, pb_ref, db_ref),
        ):
            rows = both.shape[0] // 2
            products = dot_rt(both, keys_at(span, slot))
            weights = jnp.exp(products[:rows] - logs)
            grad_weights = products[rows:]
            p_ref[span] = weights
            d_ref[span] = grad_weights
            deltas.append(carry[slot] + jnp.sum(weights * grad_weights, axis=1, keepdims=True))
        return tuple(deltas)

    deltas = lax.fori_loop(
        0, spans, first_pass, (jnp.zeros((2 * BLOCK, 1), F32), jnp.zeros((BLOCK, 1), F32))
    )

    def second_pass(span, carry):
        totals = []
        for slot, both, p_ref, d_ref in (
            (0, both_a, pa_ref, da_ref),
            (1, both_b, pb_ref, db_ref),
        ):
            rows = both.shape[0] // 2
            weights = p_ref[span]
            grad_scores = weights * (d_ref[span] - deltas[slot])
            stacked = jnp.concatenate([grad_scores, weights], axis=0).astype(BF16)
            add(slot, [span * SPAN + number for number in range(SPAN)], dot_lt(stacked, both))
            totals.append(carry[slot] + dot(stacked[:rows], keys_at(span, slot)))
        return tuple(totals)

    query_a, query_b = lax.fori_loop(
        0,
        spans,
        second_pass,
        (jnp.zeros((2 * BLOCK, LANES), F32), jnp.zeros((BLOCK, LANES), F32)),
    )
    for place, number in enumerate(ends):
        rows = slice(place * BLOCK, (place + 1) * BLOCK)
        store(0, number, jnp.where(low, query_a[rows], query_b) * SCALE)

    def finish(block, carry):
        for slot in range(2):
            store(1 + slot, block, sums_ref[slot, block])
        return carry

    lax.fori_loop(0, blocks, finish, 0)


def plane_attention_back(table, qkv, grad, lse):
    groups, _, local, _, _ = qkv.shape
    blocks = groups * local
    spans = blocks // SPAN
    wide = VMEM((spans, 2 * BLOCK, SPAN * BLOCK), F32)
    thin = VMEM((spans, BLOCK, SPAN * BLOCK), F32)
    return pl.pallas_call(
        plane_attend_back_kernel,
        out_shape=jax.ShapeDtypeStruct(qkv.shape, BF16),
        in_specs=[whole(pltpu.SMEM), whole(), whole(), whole()],
        out_specs=whole(),
        scratch_shapes=[VMEM((2, blocks, BLOCK, LANES), F32), wide, wide, thin, thin],
        compiler_params=params_of(48),
        name="plane_attention_back",
    )(table, qkv, grad, lse)


def by_owner(out_ref, values):
    rows = D // RANKS
    width = values.shape[1] // 2
    for owner in range(RANKS):
        part = values[owner * rows : (owner + 1) * rows]
        out_ref[owner] = jnp.concatenate([part[:, :width], part[:, width:]], axis=0).astype(BF16)


def plane_middle_kernel(
    mixed_in_ref,
    x_ref,
    dy_ref,
    vec_ref,
    w_out_ref,
    up_shift_ref,
    w_up_ref,
    w_down_ref,
    hidden_ref,
    send_ref,
    dres_ref,
    g_out_ref,
    g_up_ref,
    g_down_ref,
    g_up_bias_ref,
    g_small_ref,
    mixed_ref,
    residual_ref,
    second_ref,
    second_t_ref,
    total_ref,
    dsecond_ref,
):
    pieces, rows, _ = x_ref.shape
    tokens = pieces * rows
    step = pl.program_id(0)
    low = low_lanes(rows)
    out_shift, gain, shift, down_shift = (vec_ref[number : number + 1] for number in (4, 5, 6, 7))

    @pl.when(step == 0)
    def _():
        core = lax.axis_index("gx")
        for piece in range(pieces):
            span = slice(piece * rows, (piece + 1) * rows)
            for spot in (0, 2):
                first = [mixed_in_ref[side, spot, piece].astype(F32) for side in range(2)]
                last = [mixed_in_ref[side, spot + 1, piece].astype(F32) for side in range(2)]
                own_first = jnp.where(core == 0, first[0], first[1])
                own_last = jnp.where(core == 0, last[0], last[1])
                tiles = (
                    jnp.where(low, swap_halves(first[0]), first[1]),
                    jnp.where(low, own_first, last[0]),
                    swap_halves(jnp.where(low, own_last, last[1])),
                )
                for number, tile in enumerate(tiles):
                    spread = 3 * (spot // 2) + number
                    mixed_ref[span, spread * LANES : (spread + 1) * LANES] = tile.astype(BF16)
        residual = x_ref[...].reshape(tokens, D).astype(F32) + (
            dot(mixed_ref[...], w_out_ref[...]) + out_shift
        )
        residual_ref[...] = residual
        normal, _ = norm_parts(residual)
        second = normal * gain + shift
        second_ref[...] = second.astype(BF16)
        second_t_ref[...] = second.T.astype(BF16)
        total_ref[...] = jnp.zeros_like(total_ref)
        dsecond_ref[...] = jnp.zeros_like(dsecond_ref)

    w_down = w_down_ref[...].reshape(CHUNK, D)
    upper = dot(second_ref[...], w_up_ref[...]) + up_shift_ref[0]
    factor = 0.7978845608028654
    square = upper * upper
    bent = jnp.tanh(factor * (upper + 0.044715 * (upper * square)))
    middle_half = 0.5 * (1.0 + bent)
    active = (upper * middle_half).astype(BF16)
    slope = middle_half + 0.5 * upper * (1.0 - bent * bent) * (
        factor + (3.0 * 0.044715 * factor) * square
    )
    dy = dy_ref[...]
    total_ref[...] += dot(active, w_down)
    g_down_ref[...] = dot_lt(active, dy).astype(BF16).reshape(g_down_ref.shape)
    dupper = (dot_rt(dy, w_down) * slope).astype(BF16)
    g_up_bias_ref[0] = jnp.sum(dupper.astype(F32), axis=0, keepdims=True)
    by_owner(g_up_ref, dot(second_t_ref[...], dupper))
    dsecond_ref[...] += dot_rt(dupper, w_up_ref[...])

    @pl.when(step == pl.num_programs(0) - 1)
    def _():
        residual = residual_ref[...]
        hidden_ref[...] = (
            (residual + (total_ref[...] + down_shift)).astype(BF16).reshape(x_ref.shape)
        )
        normal, inverse = norm_parts(residual)
        dsecond = dsecond_ref[...]
        grad_out = dy_ref[...].astype(F32)
        g_small_ref[0:1] = jnp.sum(dsecond * normal, axis=0, keepdims=True)
        g_small_ref[1:2] = jnp.sum(dsecond, axis=0, keepdims=True)
        g_small_ref[2:3] = jnp.sum(grad_out, axis=0, keepdims=True)
        dres = grad_out + norm_pull(dsecond, normal, inverse, gain)
        dres_ref[...] = dres
        branch = dres.astype(BF16)
        g_small_ref[3:4] = jnp.sum(branch.astype(F32), axis=0, keepdims=True)
        by_owner(g_out_ref, dot_lt(mixed_ref[...], branch))
        dmixed = dot_rt(branch, w_out_ref[...])
        for piece in range(pieces):
            span = slice(piece * rows, (piece + 1) * rows)
            for spot in (0, 2):
                tiles = [
                    dmixed[span, number * LANES : (number + 1) * LANES]
                    for number in range(3 * (spot // 2), 3 * (spot // 2) + 3)
                ]
                flipped = [swap_halves(tile) for tile in tiles]
                send_ref[0, spot, piece] = jnp.where(low, tiles[1], flipped[0]).astype(BF16)
                send_ref[1, spot, piece] = jnp.where(low, tiles[1], tiles[0]).astype(BF16)
                send_ref[0, spot + 1, piece] = jnp.where(low, flipped[2], tiles[1]).astype(BF16)
                send_ref[1, spot + 1, piece] = flipped[2].astype(BF16)


def plane_middle(mixed_in, x, dy, vec, w_out, up_shift, w_up, w_down):
    pieces, rows, _ = x.shape
    tokens = pieces * rows
    shard = D // RANKS

    def fixed(shape):
        return pl.BlockSpec(shape, lambda step: (0,) * len(shape))

    steps = FF // CHUNK
    down = pl.BlockSpec((2, LANES, D), lambda step: (0, step, 0))
    return pl.pallas_call(
        plane_middle_kernel,
        grid=(steps,),
        out_shape=(
            jax.ShapeDtypeStruct(x.shape, BF16),
            jax.ShapeDtypeStruct(mixed_in.shape, BF16),
            jax.ShapeDtypeStruct((tokens, D), F32),
            jax.ShapeDtypeStruct((RANKS, 2 * shard, D // 2), BF16),
            jax.ShapeDtypeStruct((RANKS, 2 * shard, FF // 2), BF16),
            jax.ShapeDtypeStruct((2, FF // 2, D), BF16),
            jax.ShapeDtypeStruct((steps, 1, CHUNK), F32),
            jax.ShapeDtypeStruct((4, D), F32),
        ),
        in_specs=[
            fixed(mixed_in.shape),
            fixed(x.shape),
            fixed((tokens, D)),
            fixed(vec.shape),
            fixed((D, D)),
            pl.BlockSpec((1, 1, CHUNK), lambda step: (step, 0, 0)),
            pl.BlockSpec((D, CHUNK), lambda step: (0, step)),
            down,
        ],
        out_specs=(
            fixed(x.shape),
            fixed(mixed_in.shape),
            fixed((tokens, D)),
            fixed((RANKS, 2 * shard, D // 2)),
            pl.BlockSpec((RANKS, 2 * shard, LANES), lambda step: (0, 0, step)),
            down,
            pl.BlockSpec((1, 1, CHUNK), lambda step: (step, 0, 0)),
            fixed((4, D)),
        ),
        scratch_shapes=[
            VMEM((tokens, D), BF16),
            VMEM((tokens, D), F32),
            VMEM((tokens, D), BF16),
            VMEM((D, tokens), BF16),
            VMEM((tokens, D), F32),
            VMEM((tokens, D), F32),
        ],
        compiler_params=params_of(56),
        name="plane_middle",
    )(mixed_in, x, dy, vec, w_out, up_shift, w_up, w_down)


def plane_qkv_back_kernel(
    recv_ref,
    normed_ref,
    x_ref,
    dres_ref,
    vec_ref,
    w_ref,
    grad_ref,
    g_qkv_ref,
    g_bias_ref,
    g_small_ref,
    packed_ref,
    normed_t_ref,
    dnormed_ref,
):
    pieces, rows, _ = x_ref.shape
    step = pl.program_id(0)
    low = low_lanes(rows)

    @pl.when(step == 0)
    def _():
        core = lax.axis_index("gx")

        def put(tile, piece, value):
            side, chunk = tile // HALF_TILES, tile % HALF_TILES
            packed_ref[
                chunk, piece * rows : (piece + 1) * rows, side * LANES : (side + 1) * LANES
            ] = value.astype(BF16)

        for piece in range(pieces):
            seconds = []
            for spot in range(SPOTS):
                first = recv_ref[0, spot, piece, 0].astype(F32)
                second = recv_ref[1, spot, piece, 0].astype(F32)
                put(spot, piece, jnp.where(low, first, jnp.where(core == 0, first, second)))
                seconds.append(second)
                base = D // LANES + 3 * spot
                put(base, piece, recv_ref[0, spot, piece, 1])
                put(base + 1, piece, recv_ref[1, spot, piece, 1])
                shared = recv_ref[0, spot, piece, 2].astype(F32) + recv_ref[
                    1, spot, piece, 2
                ].astype(F32)
                put(base + 2, piece, shared)
            for number in range(2):
                put(
                    SPOTS + number,
                    piece,
                    jnp.where(low, seconds[2 * number], swap_halves(seconds[2 * number + 1])),
                )
        normed_t_ref[...] = normed_ref[...].astype(F32).T.astype(BF16)
        dnormed_ref[...] = jnp.zeros_like(dnormed_ref)

    packed = packed_ref[step]
    g_bias_ref[0] = jnp.sum(packed.astype(F32), axis=0, keepdims=True)
    by_owner(g_qkv_ref, dot(normed_t_ref[...], packed))
    dnormed_ref[...] += dot_rt(packed, w_ref[...])

    @pl.when(step == pl.num_programs(0) - 1)
    def _():
        normal, inverse = norm_parts(x_ref[...].reshape(pieces * rows, D).astype(F32))
        dnormed = dnormed_ref[...]
        g_small_ref[0:1] = jnp.sum(dnormed * normal, axis=0, keepdims=True)
        g_small_ref[1:2] = jnp.sum(dnormed, axis=0, keepdims=True)
        grad = dres_ref[...] + norm_pull(dnormed, normal, inverse, vec_ref[0:1])
        grad_ref[...] = grad.astype(BF16).reshape(x_ref.shape)


def plane_qkv_back(recv, normed, x, dres, vec, w):
    pieces, rows, _ = x.shape
    tokens = pieces * rows
    shard = D // RANKS

    def fixed(shape):
        return pl.BlockSpec(shape, lambda step: (0,) * len(shape))

    return pl.pallas_call(
        plane_qkv_back_kernel,
        grid=(HALF_TILES,),
        out_shape=(
            jax.ShapeDtypeStruct(x.shape, BF16),
            jax.ShapeDtypeStruct((RANKS, 2 * shard, 3 * D // 2), BF16),
            jax.ShapeDtypeStruct((HALF_TILES, 1, CHUNK), F32),
            jax.ShapeDtypeStruct((2, D), F32),
        ),
        in_specs=[
            fixed(recv.shape),
            fixed((tokens, D)),
            fixed(x.shape),
            fixed((tokens, D)),
            fixed(vec.shape),
            pl.BlockSpec((D, CHUNK), lambda step: (0, step)),
        ],
        out_specs=(
            fixed(x.shape),
            pl.BlockSpec((RANKS, 2 * shard, LANES), lambda step: (0, 0, step)),
            pl.BlockSpec((1, 1, CHUNK), lambda step: (step, 0, 0)),
            fixed((2, D)),
        ),
        scratch_shapes=[
            VMEM((HALF_TILES, tokens, CHUNK), BF16),
            VMEM((D, tokens), BF16),
            VMEM((tokens, D), F32),
        ],
        compiler_params=params_of(56),
        name="plane_qkv_back",
    )(recv, normed, x, dres, vec, w)


class Reduce:
    SENDS = 4 + 2 + 2 + 3
    RECVS = SENDS

    def __init__(self, source, total, near, corner_x, corner_y, side_x, side_y, far, out, sems):
        self.source, self.total, self.near = source, total, near
        self.corner = {1: corner_x, 2: corner_y}
        self.side = {1: side_x, 2: side_y}
        self.far, self.out = far, out
        self.send_sem, self.recv_sem, self.local_sem = sems
        self.core, self.plane, self.spot = place_here()
        self.copies = []
        self.locals = []

    def start(self):
        sibling = (1 - self.core, rank_of(self.plane, self.spot))
        for number, side in enumerate((3, 1, 2, 0)):
            spot = flip(self.spot, side)
            copy = remote(
                self.source.at[1 - self.core, :, spot],
                self.near.at[:, spot],
                self.send_sem.at[number],
                self.recv_sem.at[number],
                sibling,
            )
            copy.start()
            self.copies.append(copy)
            keep = pltpu.make_async_copy(
                self.source.at[self.core, :, spot],
                self.total.at[:, spot],
                self.local_sem.at[number],
            )
            keep.start()
            self.locals.append(keep)

    def take(self, number, side):
        self.copies[number].wait_recv()
        self.locals[number].wait()
        spot = flip(self.spot, side)

        def add(plane, carry):
            self.total[plane, spot] = (
                self.total[plane, spot].astype(F32) + self.near[plane, spot].astype(F32)
            ).astype(self.total.dtype)
            return carry

        lax.fori_loop(0, PLANES, add, 0)

    def corners(self):
        self.take(0, 3)
        spot = flip(self.spot, 3)
        index = 4
        self.corner_copies = []
        for bits in range(PLANES):
            side = 2 if bits < 2 else 1
            self.corner_copies.append(None)
            plane = flip(self.plane, bits)
            copy = remote(
                self.total.at[plane, spot],
                self.corner[side].at[bits % 2],
                self.send_sem.at[index + bits],
                self.recv_sem.at[index + bits],
                (self.core, rank_of(self.plane, flip(self.spot, side))),
            )
            copy.start()
            self.corner_copies[bits] = copy

    def sides(self):
        self.take(1, 1)
        self.take(2, 2)
        self.side_copies = {}
        for side in (1, 2):
            spot = flip(self.spot, side)
            came = 3 - side
            for bits in (0, 1) if came == 2 else (2, 3):
                self.corner_copies[bits].wait_recv()
                plane = flip(self.plane, bits)
                self.total[plane, spot] = (
                    self.total[plane, spot].astype(F32)
                    + self.corner[came][bits % 2].astype(F32)
                ).astype(self.total.dtype)
            copy = remote(
                self.total.at[:, spot],
                self.side[side],
                self.send_sem.at[7 + side],
                self.recv_sem.at[7 + side],
                (self.core, rank_of(self.plane, spot)),
            )
            copy.start()
            self.side_copies[side] = copy

    def columns(self):
        self.take(3, 0)
        for side in (1, 2):
            self.side_copies[side].wait_recv()

        def add(plane, carry):
            self.total[plane, self.spot] = (
                self.total[plane, self.spot].astype(F32)
                + self.side[1][plane].astype(F32)
                + self.side[2][plane].astype(F32)
            ).astype(self.total.dtype)
            return carry

        lax.fori_loop(0, PLANES, add, 0)
        self.far_copies = []
        for bits in range(1, PLANES):
            plane = flip(self.plane, bits)
            copy = remote(
                self.total.at[plane, self.spot],
                self.far.at[bits - 1],
                self.send_sem.at[9 + bits],
                self.recv_sem.at[9 + bits],
                (self.core, rank_of(plane, self.spot)),
            )
            copy.start()
            self.far_copies.append(copy)

    def finish(self):
        value = self.total[self.plane, self.spot].astype(F32)
        for bits in range(1, PLANES):
            self.far_copies[bits - 1].wait_recv()
            value = value + self.far[bits - 1].astype(F32)
        self.out[...] = value
        for copy in self.copies + self.corner_copies + self.far_copies:
            copy.wait_send()
        for side in (1, 2):
            self.side_copies[side].wait_send()


REDUCE_SEMS = 13


def reduce_scratch(shape, kind):
    tail = shape[3:]
    return [
        VMEM((PLANES, SPOTS) + tail, kind),
        VMEM((PLANES, SPOTS) + tail, kind),
        VMEM((2,) + tail, kind),
        VMEM((2,) + tail, kind),
        VMEM((PLANES,) + tail, kind),
        VMEM((PLANES,) + tail, kind),
        VMEM((PLANES - 1,) + tail, kind),
    ]


def spread_kernel(count, *refs):
    hidden_ref, grad_ref = refs[:2]
    sources = refs[2 : 2 + count]
    hidden_out_ref, grad_out_ref = refs[2 + count : 4 + count]
    outs = refs[4 + count : 4 + 2 * count]
    scratch = refs[4 + 2 * count :]
    buffers = scratch[: 7 * count]
    send_sem, recv_sem, local_sem, move_send, move_recv, move_local = scratch[7 * count :]
    core, plane, spot = place_here()
    greet(all_partners(core, plane, spot))
    sums = [
        Reduce(
            source,
            *buffers[7 * number : 7 * number + 7],
            out,
            (send_sem.at[number], recv_sem.at[number], local_sem.at[number]),
        )
        for number, (source, out) in enumerate(zip(sources, outs))
    ]
    for one in sums:
        one.start()
    finish_grad = from_planes(grad_ref, grad_out_ref, move_send.at[0], move_recv.at[0], move_local.at[0])
    finish_hidden = from_planes(
        hidden_ref, hidden_out_ref, move_send.at[1], move_recv.at[1], move_local.at[1]
    )
    for one in sums:
        one.corners()
    for one in sums:
        one.sides()
    for one in sums:
        one.columns()
    for one in sums:
        one.finish()
    finish_grad()
    finish_hidden()


def spread(hidden, grad, sources):
    count = len(sources)
    buffers = []
    for source in sources:
        buffers += reduce_scratch(source.shape, source.dtype)
    return pl.pallas_call(
        functools.partial(spread_kernel, count),
        out_shape=(
            jax.ShapeDtypeStruct(hidden.shape, BF16),
            jax.ShapeDtypeStruct(grad.shape, BF16),
        )
        + tuple(jax.ShapeDtypeStruct(source.shape[3:], F32) for source in sources),
        in_specs=[whole(ANY)] * (2 + count),
        out_specs=(whole(ANY), whole(ANY)) + (whole(),) * count,
        scratch_shapes=buffers
        + [
            pltpu.SemaphoreType.DMA((count, REDUCE_SEMS)),
            pltpu.SemaphoreType.DMA((count, REDUCE_SEMS)),
            pltpu.SemaphoreType.DMA((count, 4)),
            pltpu.SemaphoreType.DMA((2, 2)),
            pltpu.SemaphoreType.DMA((2, 2)),
            pltpu.SemaphoreType.DMA((2, 2)),
        ],
        compiler_params=pltpu.CompilerParams(
            vmem_limit_bytes=56 * 1024 * 1024, collective_id=2, has_side_effects=True
        ),
        name="spread",
    )(hidden, grad, *sources)


def fold_columns(array):
    half = array.shape[1] // 2
    return jnp.concatenate([array[:, :half], array[:, half:]], axis=0)


def unfold_columns(array):
    half = array.shape[0] // 2
    return jnp.concatenate([array[:half], array[half:]], axis=1)


def plane_shards(
    hidden_in,
    rand_table,
    norm1_gain,
    norm1_bias,
    w_qkv,
    query_bias,
    value_bias,
    w_out,
    out_bias,
    norm2_gain,
    norm2_bias,
    w_up,
    up_bias,
    w_down,
    down_bias,
    cotangent,
):
    micro, rows, _ = hidden_in.shape
    local = rows // BLOCK
    own = norm1_gain.shape[0]
    order = [natural_block(entry) for entry in column_order()]
    inverse = [order.index(number) for number in range(len(order))]
    small = (8 + FF // D) * own
    entries = rand_table.size

    vec = jnp.concatenate(
        [
            norm1_gain,
            norm1_bias,
            query_bias,
            value_bias,
            out_bias,
            norm2_gain,
            norm2_bias,
            down_bias,
            up_bias,
            rand_table.reshape(entries).astype(BF16),
            jnp.zeros((16 * LANES - small - entries,), BF16),
        ]
    ).reshape(16, LANES)
    x, dy, vecs, w_qkv_all, w_out_all, w_up_all, w_down_all = collect(
        hidden_in,
        cotangent,
        vec,
        fold_columns(take_blocks(w_qkv, order)),
        fold_columns(w_out),
        fold_columns(w_up),
        w_down,
    )
    vecs = vecs.reshape(RANKS, 16 * LANES)
    vectors = vecs[:, : 8 * own].reshape(RANKS, 8, own).swapaxes(0, 1).reshape(8, D).astype(F32)
    up_shift = vecs[:, 8 * own : small].astype(F32).reshape(2, FF // CHUNK, LANES)
    up_shift = up_shift.swapaxes(0, 1).reshape(FF // CHUNK, 1, CHUNK)
    bias = jnp.concatenate([vectors[2:3], jnp.zeros((1, D), F32), vectors[3:4]], axis=1)
    bias = take_blocks(bias, order).reshape(2, HALF_TILES, LANES)
    bias = bias.swapaxes(0, 1).reshape(1, 3 * D)
    plane = lax.div(lax.axis_index("gy"), SPOTS)
    tables = vecs[:, small : small + entries].reshape(2, PLANES * SPOTS, 2, local * RANDOM)
    tables = tables.astype(jnp.int32).transpose(2, 0, 1, 3).reshape(PLANES, 1, -1)
    table = lax.dynamic_index_in_dim(tables, plane, 0, keepdims=False)

    normed, send = plane_qkv(x, vectors, w_qkv_all, bias)
    qkv = outward(send, 3, "exchange_qkv")
    qkv = qkv.reshape(PLANES * SPOTS, 3, local, BLOCK, LANES)
    mixed, lse = plane_attention(table, qkv)
    mixed = inward(mixed.reshape(PLANES, SPOTS, rows, LANES), 4, "exchange_mixed")
    hidden, grad_send, dres, g_out, g_up, g_down, g_up_bias, g_mid = plane_middle(
        mixed,
        x,
        dy.reshape(micro * rows, D),
        vectors,
        w_out_all,
        up_shift,
        w_up_all,
        w_down_all.reshape(2, FF // 2, D),
    )
    grad_mixed = outward(grad_send, 5, "exchange_dmixed")
    grad_mixed = grad_mixed.reshape(PLANES * SPOTS, local, BLOCK, LANES)
    dqkv = plane_attention_back(table, qkv, grad_mixed, lse)
    dqkv = inward(dqkv.reshape(PLANES, SPOTS, 3, rows, LANES), 6, "exchange_dqkv")
    grad, g_qkv, g_bias, g_first = plane_qkv_back(dqkv, normed, x, dres, vectors, w_qkv_all)

    g_bias = g_bias.reshape(HALF_TILES, 2, LANES).swapaxes(0, 1).reshape(1, 3 * D)
    g_bias = take_blocks(g_bias, inverse)
    singles = jnp.concatenate(
        [g_first, g_bias[:, :D], g_bias[:, 2 * D :], g_mid[3:4], g_mid[0:3]], axis=0
    )
    singles = singles.reshape(8, RANKS, own).swapaxes(0, 1).reshape(RANKS, 8 * own)
    g_up_bias = g_up_bias.reshape(FF // CHUNK, 2, LANES).swapaxes(0, 1).reshape(RANKS, FF // RANKS)
    singles = jnp.concatenate(
        [singles, g_up_bias, jnp.zeros((RANKS, 8 * LANES - small), F32)], axis=1
    )
    grid = (2, PLANES, SPOTS)
    hidden_out, grad_hidden, singles, t_qkv, t_out, t_up, t_down = spread(
        hidden,
        grad,
        [
            singles.reshape(grid + (8, LANES)),
            g_qkv.reshape(grid + g_qkv.shape[1:]),
            g_out.reshape(grid + g_out.shape[1:]),
            g_up.reshape(grid + g_up.shape[1:]),
            g_down.reshape(grid + (FF // RANKS, D)),
        ],
    )
    singles = singles.reshape(8 * LANES)
    parts = [singles[number * own : (number + 1) * own] for number in range(8)]
    return (
        hidden_out,
        grad_hidden.astype(F32),
        parts[0],
        parts[1],
        take_blocks(unfold_columns(t_qkv), inverse),
        parts[2],
        parts[3],
        unfold_columns(t_out),
        parts[4],
        parts[5],
        parts[6],
        unfold_columns(t_up),
        singles[8 * own : small],
        t_down,
        parts[7],
    )


def shards(*arrays):
    micro, rows, _ = arrays[0].shape
    fits = lax.axis_size("gx") == 2 and lax.axis_size("gy") == PLANES * SPOTS
    fits = fits and micro == 2 and rows % BLOCK == 0
    return (plane_shards if fits else general_shards)(*arrays)


def solution(mesh):
    tokens = P(None, AXES, None)
    vector = P(AXES)
    matrix = P(AXES, None)
    placed = (
        tokens,
        tokens,
        vector,
        vector,
        matrix,
        vector,
        vector,
        matrix,
        vector,
        vector,
        vector,
        matrix,
        vector,
        matrix,
        vector,
        tokens,
    )
    returned = (
        tokens,
        tokens,
        vector,
        vector,
        matrix,
        vector,
        vector,
        matrix,
        vector,
        vector,
        vector,
        matrix,
        vector,
        matrix,
        vector,
    )
    return jax.shard_map(
        shards, mesh=mesh, in_specs=placed, out_specs=returned, check_vma=False
    )
```

```python
import functools

import jax
import jax.numpy as jnp
from jax import lax
from jax.experimental import pallas as pl
from jax.experimental.pallas import tpu as pltpu
from jax.sharding import PartitionSpec as P

HEADS = 12
HEAD_DIM = 64
D = 768
FF = 3072
BLOCK = 64
RANDOM = 3
LANES = 2 * HEAD_DIM
EPSILON = 1e-05
NEGATIVE = -1e30
SCALE = HEAD_DIM**-0.5
CHUNK = 256
SPAN = 8

F32 = jnp.float32
BF16 = jnp.bfloat16
VMEM = pltpu.VMEM


def whole(space=VMEM):
    return pl.BlockSpec(memory_space=space)


def params_of(megabytes):
    return pltpu.CompilerParams(vmem_limit_bytes=megabytes * 1024 * 1024)


def head_place(head):
    return (head // 3) * 4 + head % 3


def dot(left, right):
    return lax.dot_general(left, right, (((1,), (0,)), ((), ())), preferred_element_type=F32)


def dot_rt(left, right):
    return lax.dot_general(left, right, (((1,), (1,)), ((), ())), preferred_element_type=F32)


def dot_lt(left, right):
    return lax.dot_general(left, right, (((0,), (0,)), ((), ())), preferred_element_type=F32)


def swap_halves(tile):
    return pltpu.roll(tile, HEAD_DIM, axis=tile.ndim - 1)


def low_lanes(rows):
    return lax.broadcasted_iota(jnp.int32, (rows, LANES), 1) < HEAD_DIM


def norm_parts(values):
    centre = values - jnp.mean(values, axis=-1, keepdims=True)
    spread = jnp.mean(centre * centre, axis=-1, keepdims=True)
    inverse = lax.rsqrt(spread + EPSILON)
    return centre * inverse, inverse


def norm_pull(grad, normal, inverse, gain):
    scaled = grad * gain
    return inverse * (
        scaled
        - jnp.mean(scaled, axis=-1, keepdims=True)
        - normal * jnp.mean(scaled * normal, axis=-1, keepdims=True)
    )


def qkv_kernel(x_ref, gain_ref, shift_ref, w_ref, bias_ref, normed_ref, send_ref):
    micro, rows, _ = x_ref.shape
    values = x_ref[...].reshape(micro * rows, D).astype(F32)
    normal, _ = norm_parts(values)
    normed_ref[...] = (normal * gain_ref[...] + shift_ref[...]).astype(BF16)
    low = low_lanes(rows)
    for chunk in range(3 * D // CHUNK):
        columns = slice(chunk * CHUNK, (chunk + 1) * CHUNK)
        packed = dot(normed_ref[...], w_ref[:, columns]) + bias_ref[:, columns]
        if chunk < D // CHUNK:
            packed = packed.astype(BF16).astype(F32) * SCALE
        for tile in range(CHUNK // LANES):
            part = packed[:, tile * LANES : (tile + 1) * LANES]
            first, second = part[:rows], part[rows:]
            if chunk < D // CHUNK:
                head = (chunk * CHUNK // LANES + tile) * 2
                even = jnp.where(low, first, swap_halves(second))
                odd = jnp.where(low, swap_halves(first), second)
                send_ref[head_place(head), 0] = even.astype(BF16)
                send_ref[head_place(head + 1), 0] = odd.astype(BF16)
            else:
                head = (chunk * CHUNK - D) // LANES + tile
                send_ref[head_place(head), 1] = first.astype(BF16)
                send_ref[head_place(head), 2] = swap_halves(second).astype(BF16)


def qkv_forward(x, gain, shift, w, bias, groups):
    micro, rows, _ = x.shape
    return pl.pallas_call(
        qkv_kernel,
        out_shape=(
            jax.ShapeDtypeStruct((micro * rows, D), BF16),
            jax.ShapeDtypeStruct((groups, 3, rows, LANES), BF16),
        ),
        in_specs=[whole()] * 5,
        out_specs=(whole(), whole()),
        compiler_params=params_of(48),
        name="qkv_forward",
    )(x, gain, shift, w, bias)


def half_mask(low_half):
    lane = lax.broadcasted_iota(jnp.int32, (1, LANES), 1)
    keep = (lane < HEAD_DIM) if low_half else (lane >= HEAD_DIM)
    return jnp.where(keep, 1.0, 0.0).astype(BF16)


def slots_of(table_ref, micro, block, blocks):
    picks = [table_ref[micro, block * RANDOM + number] for number in range(RANDOM)]
    last = blocks - 1
    ids = [block - 1, block, block + 1, 0, last] + picks
    dropped = [None, None, None, block == 1, block == last - 1]
    for number in range(RANDOM):
        pick = picks[number]
        bad = (jnp.abs(pick - block) <= 1) | (pick == 0) | (pick == last)
        for earlier in range(number):
            bad = bad | (pick == picks[earlier])
        dropped.append(bad)
    lane = lax.broadcasted_iota(jnp.int32, (1, LANES), 1)
    tiles = []
    for pair in range(len(ids) // 2):
        level = [
            0.0 if bad is None else jnp.where(bad, NEGATIVE, 0.0).astype(F32)
            for bad in dropped[2 * pair : 2 * pair + 2]
        ]
        tiles.append(jnp.where(lane < HEAD_DIM, level[0], level[1]))
    return ids, jnp.concatenate(tiles, axis=1)


def attend_kernel(table_ref, qkv_ref, out_ref, lse_ref, s_ref):
    groups, _, local, _, _ = qkv_ref.shape
    blocks = groups * local
    low = low_lanes(BLOCK)
    masks = [half_mask(True), half_mask(False)]

    def load(component, block):
        return qkv_ref[block // local, component, block % local]

    def sparse(block, carry):
        mixed, logs = [], []
        for micro in range(2):
            ids, bias = slots_of(table_ref, micro, block, blocks)
            keys = jnp.concatenate([load(1 + micro, spot) for spot in ids], axis=0)
            query = load(0, block) * masks[micro]
            scores = dot_rt(query, keys) + bias
            top = jnp.max(scores, axis=1, keepdims=True)
            powered = jnp.exp(scores - top)
            total = jnp.sum(powered, axis=1, keepdims=True)
            mixed.append(dot(powered.astype(BF16), keys) * (1.0 / total))
            logs.append(top + jnp.log(total))
        out_ref[block // local, block % local] = jnp.where(low, mixed[1], mixed[0]).astype(BF16)
        lse_ref[block] = jnp.where(low, logs[0], logs[1])
        return carry

    lax.fori_loop(1, blocks - 1, sparse, 0)

    spans = blocks // SPAN
    ends = (0, blocks - 1)
    results = []
    for micro in range(2):
        query = jnp.concatenate([load(0, end) for end in ends], axis=0) * masks[micro]

        def keys_at(span, micro=micro):
            return jnp.concatenate(
                [load(1 + micro, span * SPAN + spot) for spot in range(SPAN)], axis=0
            )

        def first_pass(span, top, query=query, keys_at=keys_at):
            scores = dot_rt(query, keys_at(span))
            s_ref[span] = scores
            return jnp.maximum(top, jnp.max(scores, axis=1, keepdims=True))

        top = lax.fori_loop(0, spans, first_pass, jnp.full((2 * BLOCK, 1), NEGATIVE, F32))

        def second_pass(span, carry, top=top, keys_at=keys_at):
            total, mixed = carry
            powered = jnp.exp(s_ref[span] - top)
            return (
                total + jnp.sum(powered, axis=1, keepdims=True),
                mixed + dot(powered.astype(BF16), keys_at(span)),
            )

        total, mixed = lax.fori_loop(
            0,
            spans,
            second_pass,
            (jnp.zeros((2 * BLOCK, 1), F32), jnp.zeros((2 * BLOCK, LANES), F32)),
        )
        results.append((mixed * (1.0 / total), top + jnp.log(total)))
    for place, end in enumerate(ends):
        rows = slice(place * BLOCK, (place + 1) * BLOCK)
        out_ref[end // local, end % local] = jnp.where(
            low, results[1][0][rows], results[0][0][rows]
        ).astype(BF16)
        lse_ref[end] = jnp.where(low, results[0][1][rows], results[1][1][rows])


def attention_forward(table, qkv):
    groups, _, local, _, _ = qkv.shape
    blocks = groups * local
    return pl.pallas_call(
        attend_kernel,
        out_shape=(
            jax.ShapeDtypeStruct((groups, local, BLOCK, LANES), BF16),
            jax.ShapeDtypeStruct((blocks, BLOCK, LANES), F32),
        ),
        in_specs=[whole(pltpu.SMEM), whole()],
        out_specs=(whole(), whole()),
        scratch_shapes=[VMEM((blocks // SPAN, 2 * BLOCK, SPAN * BLOCK), F32)],
        compiler_params=params_of(48),
        name="attention_forward",
    )(table, qkv)


def attend_back_kernel(table_ref, qkv_ref, grad_ref, lse_ref, out_ref, sums_ref, p_ref, dp_ref):
    groups, _, local, _, _ = qkv_ref.shape
    blocks = groups * local
    low = low_lanes(BLOCK)
    masks = [half_mask(True), half_mask(False)]

    def load(component, block):
        return qkv_ref[block // local, component, block % local]

    def load_grad(block):
        return grad_ref[block // local, block % local]

    def clear(block, carry):
        for micro in range(2):
            sums_ref[micro, block] = jnp.zeros((BLOCK, LANES), F32)
        return carry

    lax.fori_loop(0, blocks, clear, 0)

    def sparse(block, carry):
        grads = []
        for micro in range(2):
            ids, bias = slots_of(table_ref, micro, block, blocks)
            keys = jnp.concatenate([load(1 + micro, spot) for spot in ids], axis=0)
            both = jnp.concatenate(
                [load(0, block) * masks[micro], load_grad(block) * masks[1 - micro]], axis=0
            )
            products = dot_rt(both, keys)
            logs = lse_ref[block][:, micro * HEAD_DIM : micro * HEAD_DIM + 1]
            weights = jnp.exp(products[:BLOCK] + bias - logs)
            grad_weights = products[BLOCK:]
            delta = jnp.sum(weights * grad_weights, axis=1, keepdims=True)
            grad_scores = weights * (grad_weights - delta)
            stacked = jnp.concatenate([grad_scores, weights], axis=0).astype(BF16)
            grads.append(dot(stacked[:BLOCK], keys))
            shares = dot_lt(stacked, both)
            for place, spot in enumerate(ids):
                sums_ref[micro, spot] += shares[place * BLOCK : (place + 1) * BLOCK]
        out_ref[block // local, 0, block % local] = (
            jnp.where(low, grads[0], grads[1]) * SCALE
        ).astype(BF16)
        return carry

    lax.fori_loop(1, blocks - 1, sparse, 0)

    spans = blocks // SPAN
    ends = (0, blocks - 1)
    results = []
    for micro in range(2):
        query = jnp.concatenate([load(0, end) for end in ends], axis=0) * masks[micro]
        grad = jnp.concatenate([load_grad(end) for end in ends], axis=0) * masks[1 - micro]
        both = jnp.concatenate([query, grad], axis=0)
        logs = jnp.concatenate(
            [lse_ref[end][:, micro * HEAD_DIM : micro * HEAD_DIM + 1] for end in ends], axis=0
        )

        def keys_at(span, micro=micro):
            return jnp.concatenate(
                [load(1 + micro, span * SPAN + spot) for spot in range(SPAN)], axis=0
            )

        def first_pass(span, delta, both=both, logs=logs, keys_at=keys_at):
            products = dot_rt(both, keys_at(span))
            weights = jnp.exp(products[: 2 * BLOCK] - logs)
            grad_weights = products[2 * BLOCK :]
            p_ref[span] = weights
            dp_ref[span] = grad_weights
            return delta + jnp.sum(weights * grad_weights, axis=1, keepdims=True)

        delta = lax.fori_loop(0, spans, first_pass, jnp.zeros((2 * BLOCK, 1), F32))

        def second_pass(span, carry, delta=delta, both=both, keys_at=keys_at, micro=micro):
            weights = p_ref[span]
            grad_scores = weights * (dp_ref[span] - delta)
            stacked = jnp.concatenate([grad_scores, weights], axis=0).astype(BF16)
            shares = dot_lt(stacked, both)
            for spot in range(SPAN):
                sums_ref[micro, span * SPAN + spot] += shares[spot * BLOCK : (spot + 1) * BLOCK]
            return carry + dot(stacked[: 2 * BLOCK], keys_at(span))

        results.append(
            lax.fori_loop(0, spans, second_pass, jnp.zeros((2 * BLOCK, LANES), F32))
        )
    for place, end in enumerate(ends):
        rows = slice(place * BLOCK, (place + 1) * BLOCK)
        out_ref[end // local, 0, end % local] = (
            jnp.where(low, results[0][rows], results[1][rows]) * SCALE
        ).astype(BF16)

    def finish(block, carry):
        for micro in range(2):
            out_ref[block // local, 1 + micro, block % local] = sums_ref[micro, block].astype(BF16)
        return carry

    lax.fori_loop(0, blocks, finish, 0)


def attention_backward(table, qkv, grad, lse):
    groups, _, local, _, _ = qkv.shape
    blocks = groups * local
    spans = VMEM((blocks // SPAN, 2 * BLOCK, SPAN * BLOCK), F32)
    return pl.pallas_call(
        attend_back_kernel,
        out_shape=jax.ShapeDtypeStruct(qkv.shape, BF16),
        in_specs=[whole(pltpu.SMEM), whole(), whole(), whole()],
        out_specs=whole(),
        scratch_shapes=[VMEM((2, blocks, BLOCK, LANES), F32), spans, spans],
        compiler_params=params_of(48),
        name="attention_backward",
    )(table, qkv, grad, lse)


def middle_kernel(
    mixed_in_ref,
    x_ref,
    dy_ref,
    w_out_ref,
    out_shift_ref,
    gain_ref,
    shift_ref,
    up_shift_ref,
    down_shift_ref,
    w_up_ref,
    w_down_ref,
    hidden_ref,
    send_ref,
    dres_ref,
    g_out_ref,
    g_up_ref,
    g_down_ref,
    g_up_bias_ref,
    g_small_ref,
    mixed_ref,
    residual_ref,
    second_ref,
    second_t_ref,
    total_ref,
    dsecond_ref,
):
    micro, rows, _ = x_ref.shape
    step = pl.program_id(0)
    low = low_lanes(rows)

    @pl.when(step == 0)
    def _():
        for pair in range(HEADS // 2):
            even = mixed_in_ref[head_place(2 * pair)].astype(F32)
            odd = mixed_in_ref[head_place(2 * pair + 1)].astype(F32)
            columns = slice(pair * LANES, (pair + 1) * LANES)
            mixed_ref[:rows, columns] = jnp.where(low, swap_halves(even), odd).astype(BF16)
            mixed_ref[rows:, columns] = jnp.where(low, even, swap_halves(odd)).astype(BF16)
        residual = x_ref[...].reshape(micro * rows, D).astype(F32) + (
            dot(mixed_ref[...], w_out_ref[...]) + out_shift_ref[...]
        )
        residual_ref[...] = residual
        normal, _ = norm_parts(residual)
        second = normal * gain_ref[...] + shift_ref[...]
        second_ref[...] = second.astype(BF16)
        second_t_ref[...] = second.T.astype(BF16)
        total_ref[...] = jnp.zeros_like(total_ref)
        dsecond_ref[...] = jnp.zeros_like(dsecond_ref)

    upper = dot(second_ref[...], w_up_ref[...]) + up_shift_ref[...]
    factor = 0.7978845608028654
    square = upper * upper
    bent = jnp.tanh(factor * (upper + 0.044715 * (upper * square)))
    half = 0.5 * (1.0 + bent)
    active = (upper * half).astype(BF16)
    slope = half + 0.5 * upper * (1.0 - bent * bent) * (
        factor + (3.0 * 0.044715 * factor) * square
    )
    dy = dy_ref[...]
    total_ref[...] += dot(active, w_down_ref[...])
    g_down_ref[...] = dot_lt(active, dy).astype(g_down_ref.dtype)
    dupper = (dot_rt(dy, w_down_ref[...]) * slope).astype(BF16)
    g_up_bias_ref[...] = jnp.sum(dupper.astype(F32), axis=0, keepdims=True)
    g_up_ref[...] = dot(second_t_ref[...], dupper).astype(g_up_ref.dtype)
    dsecond_ref[...] += dot_rt(dupper, w_up_ref[...])

    @pl.when(step == pl.num_programs(0) - 1)
    def _():
        residual = residual_ref[...]
        hidden_ref[...] = (
            (residual + (total_ref[...] + down_shift_ref[...])).astype(BF16).reshape(x_ref.shape)
        )
        normal, inverse = norm_parts(residual)
        dsecond = dsecond_ref[...]
        grad_out = dy_ref[...].astype(F32)
        g_small_ref[0:1] = jnp.sum(dsecond * normal, axis=0, keepdims=True)
        g_small_ref[1:2] = jnp.sum(dsecond, axis=0, keepdims=True)
        g_small_ref[2:3] = jnp.sum(grad_out, axis=0, keepdims=True)
        dres = grad_out + norm_pull(dsecond, normal, inverse, gain_ref[...])
        dres_ref[...] = dres
        branch = dres.astype(BF16)
        g_small_ref[3:4] = jnp.sum(branch.astype(F32), axis=0, keepdims=True)
        g_out_ref[...] = dot_lt(mixed_ref[...], branch).astype(g_out_ref.dtype)
        dmixed = dot_rt(branch, w_out_ref[...])
        for pair in range(HEADS // 2):
            part = dmixed[:, pair * LANES : (pair + 1) * LANES]
            first, last = part[:rows], part[rows:]
            even = jnp.where(low, last, swap_halves(first))
            odd = jnp.where(low, swap_halves(last), first)
            send_ref[head_place(2 * pair)] = even.astype(BF16)
            send_ref[head_place(2 * pair + 1)] = odd.astype(BF16)


def middle(mixed_in, x, dy, w_out, out_shift, gain, shift, up_shift, down_shift, w_up, w_down, kind):
    micro, rows, _ = x.shape
    tokens = micro * rows
    groups = mixed_in.shape[0]

    def fixed(shape):
        return pl.BlockSpec(shape, lambda step: (0,) * len(shape))

    vector = fixed((1, D))
    steps = FF // CHUNK
    return pl.pallas_call(
        middle_kernel,
        grid=(steps,),
        out_shape=(
            jax.ShapeDtypeStruct(x.shape, BF16),
            jax.ShapeDtypeStruct((groups, rows, LANES), BF16),
            jax.ShapeDtypeStruct((tokens, D), F32),
            jax.ShapeDtypeStruct((D, D), kind),
            jax.ShapeDtypeStruct((D, FF), kind),
            jax.ShapeDtypeStruct((FF, D), kind),
            jax.ShapeDtypeStruct((1, FF), F32),
            jax.ShapeDtypeStruct((4, D), F32),
        ),
        in_specs=[
            fixed(mixed_in.shape),
            fixed(x.shape),
            fixed((tokens, D)),
            fixed((D, D)),
            vector,
            vector,
            vector,
            pl.BlockSpec((1, CHUNK), lambda step: (0, step)),
            vector,
            pl.BlockSpec((D, CHUNK), lambda step: (0, step)),
            pl.BlockSpec((CHUNK, D), lambda step: (step, 0)),
        ],
        out_specs=(
            fixed(x.shape),
            fixed((groups, rows, LANES)),
            fixed((tokens, D)),
            fixed((D, D)),
            pl.BlockSpec((D, CHUNK), lambda step: (0, step)),
            pl.BlockSpec((CHUNK, D), lambda step: (step, 0)),
            pl.BlockSpec((1, CHUNK), lambda step: (0, step)),
            fixed((4, D)),
        ),
        scratch_shapes=[
            VMEM((tokens, D), BF16),
            VMEM((tokens, D), F32),
            VMEM((tokens, D), BF16),
            VMEM((D, tokens), BF16),
            VMEM((tokens, D), F32),
            VMEM((tokens, D), F32),
        ],
        compiler_params=params_of(56),
        name="middle",
    )(mixed_in, x, dy, w_out, out_shift, gain, shift, up_shift, down_shift, w_up, w_down)


def qkv_back_kernel(
    recv_ref,
    normed_ref,
    x_ref,
    dres_ref,
    gain_ref,
    w_ref,
    grad_ref,
    g_qkv_ref,
    g_bias_ref,
    g_small_ref,
    packed_ref,
    normed_t_ref,
    dnormed_ref,
):
    micro, rows, _ = x_ref.shape
    step = pl.program_id(0)
    low = low_lanes(rows)

    @pl.when(step == 0)
    def _():
        for pair in range(HEADS // 2):
            even = recv_ref[head_place(2 * pair), 0].astype(F32)
            odd = recv_ref[head_place(2 * pair + 1), 0].astype(F32)
            spot, columns = pair // 2, slice((pair % 2) * LANES, (pair % 2 + 1) * LANES)
            packed_ref[spot, :rows, columns] = jnp.where(low, even, swap_halves(odd)).astype(BF16)
            packed_ref[spot, rows:, columns] = jnp.where(low, swap_halves(even), odd).astype(BF16)
        for head in range(HEADS):
            spot = D // CHUNK + head // 2
            columns = slice((head % 2) * LANES, (head % 2 + 1) * LANES)
            packed_ref[spot, :rows, columns] = recv_ref[head_place(head), 1]
            packed_ref[spot, rows:, columns] = swap_halves(
                recv_ref[head_place(head), 2].astype(F32)
            ).astype(BF16)
        normed_t_ref[...] = normed_ref[...].astype(F32).T.astype(BF16)
        dnormed_ref[...] = jnp.zeros_like(dnormed_ref)

    packed = packed_ref[step]
    g_bias_ref[...] = jnp.sum(packed.astype(F32), axis=0, keepdims=True)
    g_qkv_ref[...] = dot(normed_t_ref[...], packed).astype(g_qkv_ref.dtype)
    dnormed_ref[...] += dot_rt(packed, w_ref[...])

    @pl.when(step == pl.num_programs(0) - 1)
    def _():
        normal, inverse = norm_parts(x_ref[...].reshape(micro * rows, D).astype(F32))
        dnormed = dnormed_ref[...]
        g_small_ref[0:1] = jnp.sum(dnormed * normal, axis=0, keepdims=True)
        g_small_ref[1:2] = jnp.sum(dnormed, axis=0, keepdims=True)
        grad = dres_ref[...] + norm_pull(dnormed, normal, inverse, gain_ref[...])
        grad_ref[...] = grad.reshape(x_ref.shape)


def qkv_backward(recv, normed, x, dres, gain, w, kind):
    micro, rows, _ = x.shape
    tokens = micro * rows

    def fixed(shape):
        return pl.BlockSpec(shape, lambda step: (0,) * len(shape))

    steps = 3 * D // CHUNK
    return pl.pallas_call(
        qkv_back_kernel,
        grid=(steps,),
        out_shape=(
            jax.ShapeDtypeStruct(x.shape, F32),
            jax.ShapeDtypeStruct((D, 3 * D), kind),
            jax.ShapeDtypeStruct((1, 3 * D), F32),
            jax.ShapeDtypeStruct((2, D), F32),
        ),
        in_specs=[
            fixed(recv.shape),
            fixed((tokens, D)),
            fixed(x.shape),
            fixed((tokens, D)),
            fixed((1, D)),
            pl.BlockSpec((D, CHUNK), lambda step: (0, step)),
        ],
        out_specs=(
            fixed(x.shape),
            pl.BlockSpec((D, CHUNK), lambda step: (0, step)),
            pl.BlockSpec((1, CHUNK), lambda step: (0, step)),
            fixed((2, D)),
        ),
        scratch_shapes=[
            VMEM((steps, tokens, CHUNK), BF16),
            VMEM((D, tokens), BF16),
            VMEM((tokens, D), F32),
        ],
        compiler_params=params_of(56),
        name="qkv_backward",
    )(recv, normed, x, dres, gain, w)


AXES = ("gx", "gy")


def gather(array):
    return lax.all_gather(array, AXES, axis=0, tiled=True)


def scatter(array):
    return lax.psum_scatter(array, AXES, scatter_dimension=0, tiled=True)


def exchange(array):
    return lax.all_to_all(array, "gy", 0, 0, tiled=True)


def by_heads(w_qkv):
    rows = w_qkv.shape[0]
    sides = w_qkv[:, D:].reshape(rows, 2, HEADS, HEAD_DIM)
    return jnp.concatenate([w_qkv[:, :D], jnp.swapaxes(sides, 1, 2).reshape(rows, 2 * D)], axis=1)


def by_parts(w_qkv):
    rows = w_qkv.shape[0]
    sides = w_qkv[:, D:].reshape(rows, HEADS, 2, HEAD_DIM)
    return jnp.concatenate([w_qkv[:, :D], jnp.swapaxes(sides, 1, 2).reshape(rows, 2 * D)], axis=1)


def general_shards(
    hidden_in,
    rand_table,
    norm1_gain,
    norm1_bias,
    w_qkv,
    query_bias,
    value_bias,
    w_out,
    out_bias,
    norm2_gain,
    norm2_bias,
    w_up,
    up_bias,
    w_down,
    down_bias,
    cotangent,
):
    micro, rows, _ = hidden_in.shape
    groups = lax.axis_size("gy")
    local = rows // BLOCK
    own = norm1_gain.shape[0]

    vectors = jnp.concatenate(
        [
            norm1_gain,
            norm1_bias,
            query_bias,
            value_bias,
            out_bias,
            norm2_gain,
            norm2_bias,
            down_bias,
            up_bias,
        ]
    )
    table = lax.all_gather(rand_table, "gy", axis=1, tiled=True)
    table = table.reshape(micro, groups * local * RANDOM)
    vectors = gather(vectors[None]).astype(F32)
    gain_one, shift_one, query_shift, value_shift, out_shift, gain_two, shift_two, down_shift = (
        vectors[:, number * own : (number + 1) * own].reshape(1, D) for number in range(8)
    )
    up_shift = vectors[:, 8 * own :].reshape(1, FF)
    w_qkv_full = gather(by_heads(w_qkv))
    w_out_full, w_up_full, w_down_full = gather(w_out), gather(w_up), gather(w_down)
    packed_bias = by_heads(
        jnp.concatenate([query_shift, jnp.zeros_like(query_shift), value_shift], axis=1)
    )

    normed, send = qkv_forward(hidden_in, gain_one, shift_one, w_qkv_full, packed_bias, groups)
    qkv = exchange(send).reshape(groups, 3, local, BLOCK, LANES)
    mixed, lse = attention_forward(table, qkv)
    mixed_back = exchange(mixed.reshape(groups, rows, LANES))
    hidden_out, grad_send, dres, g_out, g_up, g_down, g_up_bias, g_mid = middle(
        mixed_back,
        hidden_in,
        cotangent.reshape(micro * rows, D),
        w_out_full,
        out_shift,
        gain_two,
        shift_two,
        up_shift,
        down_shift,
        w_up_full,
        w_down_full,
        F32,
    )
    grad_mixed = exchange(grad_send).reshape(groups, local, BLOCK, LANES)
    dqkv = attention_backward(table, qkv, grad_mixed, lse)
    dqkv_back = exchange(dqkv.reshape(groups, 3, rows, LANES))
    grad_hidden, g_qkv, g_packed, g_first = qkv_backward(
        dqkv_back, normed, hidden_in, dres, gain_one, w_qkv_full, F32
    )

    g_packed = by_parts(g_packed)
    small = [
        g_first[0],
        g_first[1],
        g_packed[0, :D],
        g_packed[0, 2 * D :],
        g_mid[3],
        g_mid[0],
        g_mid[1],
        g_mid[2],
    ]
    ranks = D // own
    small = jnp.concatenate(
        [item.reshape(ranks, own) for item in small] + [g_up_bias.reshape(ranks, 4 * own)], axis=1
    )
    small = scatter(small)[0]
    parts = [small[number * own : (number + 1) * own] for number in range(8)]
    return (
        hidden_out,
        grad_hidden,
        parts[0],
        parts[1],
        by_parts(scatter(g_qkv)),
        parts[2],
        parts[3],
        scatter(g_out),
        parts[4],
        parts[5],
        parts[6],
        scatter(g_up),
        small[8 * own :],
        scatter(g_down),
        parts[7],
    )


MESH = pl.DeviceIdType.MESH
ANY = pl.ANY
PLANES = 4
SPOTS = 4
PIECES = 2
RANKS = 2 * PLANES * SPOTS
TILES = 3 * D // LANES
HALF_TILES = TILES // 2
QUERY_ORDER = (0, 2, 3, 5, 6, 8, 9, 11, 1, 4, 7, 10)


def column_order():
    order = [("q", head) for head in QUERY_ORDER]
    for spot in range(SPOTS):
        for place in (2 * 3 * spot, 2 * 3 * spot + 2):
            order += [("k", place // 2), ("v", place // 2)]
        order += [("v", 3 * spot + 2), ("k", 3 * spot + 2)]
    return order


def natural_block(entry):
    return "qkv".index(entry[0]) * HEADS + entry[1]


def take_blocks(array, order):
    parts = []
    start = 0
    while start < len(order):
        stop = start + 1
        while stop < len(order) and order[stop] == order[stop - 1] + 1:
            stop += 1
        parts.append(array[..., order[start] * HEAD_DIM : (order[start] + stop - start) * HEAD_DIM])
        start = stop
    return jnp.concatenate(parts, axis=-1)


def flip(value, bits):
    if bits == 0:
        return value
    if bits == 1:
        return value + 1 - 2 * lax.rem(value, 2)
    if bits == 2:
        return value + 2 - 4 * lax.div(value, 2)
    return 3 - value


def place_here():
    core, rank = lax.axis_index("gx"), lax.axis_index("gy")
    return core, lax.div(rank, SPOTS), lax.rem(rank, SPOTS)


def rank_of(plane, spot):
    return plane * SPOTS + spot


def greet(partners):
    barrier = pltpu.get_barrier_semaphore()
    for partner in partners:
        pl.semaphore_signal(barrier, inc=1, device_id=partner, device_id_type=MESH)
    pl.semaphore_wait(barrier, len(partners))


def remote(source, target, send_sem, recv_sem, device):
    return pltpu.make_async_remote_copy(
        src_ref=source,
        dst_ref=target,
        send_sem=send_sem,
        recv_sem=recv_sem,
        device_id=device,
        device_id_type=MESH,
    )


def column_partners(core, plane, spot):
    partners = [(1 - core, rank_of(plane, spot))]
    for bits in range(1, PLANES):
        for other in (core, 1 - core):
            partners.append((other, rank_of(flip(plane, bits), spot)))
    return partners


def all_partners(core, plane, spot):
    return column_partners(core, plane, spot) + [
        (core, rank_of(plane, flip(spot, 1))),
        (core, rank_of(plane, flip(spot, 2))),
    ]


def to_planes(source, target, send_sem, recv_sem, local_sem):
    core, plane, spot = place_here()
    half, odd = lax.div(plane, 2), lax.rem(plane, 2)
    sends, keeps = [], []
    for micro in range(2):
        goal = 2 * micro + core
        here = (goal == plane) & (half == core)
        send = remote(
            source.at[micro],
            target.at[odd],
            send_sem.at[micro],
            recv_sem.at[odd],
            (half, rank_of(goal, spot)),
        )
        keep = pltpu.make_async_copy(source.at[micro], target.at[odd], local_sem.at[micro])

        @pl.when(jnp.logical_not(here))
        def _(send=send):
            send.start()

        @pl.when(here)
        def _(keep=keep):
            keep.start()

        sends.append((here, send))
        keeps.append((here, keep))

    def finish():
        for piece in range(PIECES):
            mine = (odd == core) & (plane == 2 * core + piece)
            arrival = remote(
                source.at[0],
                target.at[piece],
                send_sem.at[0],
                recv_sem.at[piece],
                (core, rank_of(plane, spot)),
            )

            @pl.when(jnp.logical_not(mine))
            def _(arrival=arrival):
                arrival.wait_recv()

        for (here, send), (_, keep) in zip(sends, keeps):

            @pl.when(jnp.logical_not(here))
            def _(send=send):
                send.wait_send()

            @pl.when(here)
            def _(keep=keep):
                keep.wait()

    return finish


def from_planes(source, target, send_sem, recv_sem, local_sem):
    core, plane, spot = place_here()
    micro, odd = lax.div(plane, 2), lax.rem(plane, 2)
    sends, keeps = [], []
    for piece in range(PIECES):
        goal = 2 * core + piece
        here = (goal == plane) & (odd == core)
        send = remote(
            source.at[piece],
            target.at[micro],
            send_sem.at[piece],
            recv_sem.at[micro],
            (odd, rank_of(goal, spot)),
        )
        keep = pltpu.make_async_copy(source.at[piece], target.at[micro], local_sem.at[piece])

        @pl.when(jnp.logical_not(here))
        def _(send=send):
            send.start()

        @pl.when(here)
        def _(keep=keep):
            keep.start()

        sends.append((here, send))
        keeps.append((here, keep))

    def finish():
        for number in range(2):
            mine = (2 * number + core == plane) & (micro == core)
            arrival = remote(
                source.at[0],
                target.at[number],
                send_sem.at[0],
                recv_sem.at[number],
                (core, rank_of(plane, spot)),
            )

            @pl.when(jnp.logical_not(mine))
            def _(arrival=arrival):
                arrival.wait_recv()

        for (here, send), (_, keep) in zip(sends, keeps):

            @pl.when(jnp.logical_not(here))
            def _(send=send):
                send.wait_send()

            @pl.when(here)
            def _(keep=keep):
                keep.wait()

    return finish


class Gather:
    SENDS = 31

    def __init__(self, source, target, send_sem, recv_sem, local_sem):
        self.source, self.target = source, target
        self.send_sem, self.recv_sem = send_sem, recv_sem
        self.core, self.plane, self.spot = place_here()
        self.sends = []
        self.own = pltpu.make_async_copy(
            source, target.at[self.core, self.plane, self.spot], local_sem
        )
        self.own.start()

    def send(self, source, plane, spot, device):
        copy = remote(
            source,
            self.target.at[self.core, plane, spot],
            self.send_sem.at[len(self.sends)],
            self.recv_sem.at[self.core, plane, spot],
            device,
        )
        copy.start()
        self.sends.append(copy)

    def arrive(self, core, plane, spot):
        shard = self.target.at[core, plane, spot]
        remote(
            shard,
            shard,
            self.send_sem.at[0],
            self.recv_sem.at[core, plane, spot],
            (self.core, rank_of(self.plane, self.spot)),
        ).wait_recv()

    def neighbour(self, bits):
        return (self.core, rank_of(self.plane, flip(self.spot, bits)))

    def sibling(self):
        return (1 - self.core, rank_of(self.plane, self.spot))

    def start(self):
        for bits in range(1, PLANES):
            goal = (self.core, rank_of(flip(self.plane, bits), self.spot))
            self.send(self.source, self.plane, self.spot, goal)
        for goal in (self.neighbour(1), self.neighbour(2), self.sibling()):
            self.send(self.source, self.plane, self.spot, goal)

    def column(self):
        for bits in range(1, PLANES):
            plane = flip(self.plane, bits)
            self.arrive(self.core, plane, self.spot)
            shard = self.target.at[self.core, plane, self.spot]
            for goal in (self.neighbour(1), self.neighbour(2), self.sibling()):
                self.send(shard, plane, self.spot, goal)

    def across(self):
        for bits in range(PLANES):
            plane = flip(self.plane, bits)
            for side in (1, 2):
                spot = flip(self.spot, side)
                self.arrive(self.core, plane, spot)
                shard = self.target.at[self.core, plane, spot]
                if (side == 1) == (bits < 2):
                    self.send(shard, plane, spot, self.neighbour(3 - side))
                self.send(shard, plane, spot, self.sibling())

    def corner(self):
        spot = flip(self.spot, 3)
        for bits in range(PLANES):
            plane = flip(self.plane, bits)
            self.arrive(self.core, plane, spot)
            self.send(self.target.at[self.core, plane, spot], plane, spot, self.sibling())

    def finish(self):
        for bits in range(PLANES):
            for side in range(SPOTS):
                self.arrive(1 - self.core, flip(self.plane, bits), flip(self.spot, side))
        self.own.wait()
        for copy in self.sends:
            copy.wait_send()


def settle(shards_ref, plan):
    rows = shards_ref.shape[3] // 2

    def pair(number, carry):
        core, plane, side = (
            lax.div(number, 2 * PLANES),
            lax.rem(lax.div(number, 2), PLANES),
            lax.rem(number, 2),
        )
        goal = pl.ds(pl.multiple_of(number * 2 * rows, 16), 2 * rows)
        for tile, out_ref, (left, right) in plan:
            columns = slice(tile * LANES, (tile + 1) * LANES)
            first = shards_ref[core, plane, 2 * side, :, columns].astype(F32)
            second = shards_ref[core, plane, 2 * side + 1, :, columns].astype(F32)
            out_ref[goal, left * LANES : (left + 1) * LANES] = jnp.concatenate(
                [first[:rows], second[:rows]], axis=0
            ).astype(BF16)
            out_ref[goal, right * LANES : (right + 1) * LANES] = jnp.concatenate(
                [first[rows:], second[rows:]], axis=0
            ).astype(BF16)
        return carry

    lax.fori_loop(0, RANKS // 2, pair, 0)


def alternate(tile):
    return 2 * tile, 2 * tile + 1


def collect_kernel(
    x_ref,
    vec_ref,
    s_qkv_ref,
    xs_ref,
    vecs_ref,
    w_qkv_ref,
    g_qkv_ref,
    send_sem,
    recv_sem,
    local_sem,
    move_send,
    move_recv,
    move_local,
):
    core, plane, spot = place_here()
    greet(all_partners(core, plane, spot))
    gathers = []
    for number, (source, target) in enumerate(((vec_ref, vecs_ref), (s_qkv_ref, g_qkv_ref))):
        one = Gather(
            source, target, send_sem.at[number], recv_sem.at[number], local_sem.at[number]
        )
        one.start()
        gathers.append(one)
    finish_x = to_planes(x_ref, xs_ref, move_send, move_recv, move_local)
    for one in gathers:
        one.column()
    for one in gathers:
        one.across()
    for one in gathers:
        one.corner()
    for one in gathers:
        one.finish()
    settle(g_qkv_ref, [(tile, w_qkv_ref, alternate(tile)) for tile in range(HALF_TILES)])
    finish_x()


def collect(x, vec, s_qkv):
    grid = (2, PLANES, SPOTS)
    return pl.pallas_call(
        collect_kernel,
        out_shape=(
            jax.ShapeDtypeStruct(x.shape, BF16),
            jax.ShapeDtypeStruct(grid + vec.shape, BF16),
            jax.ShapeDtypeStruct((D, 3 * D), BF16),
        ),
        in_specs=[whole(ANY)] * 3,
        out_specs=(whole(ANY), whole(ANY), whole()),
        scratch_shapes=[
            VMEM(grid + s_qkv.shape, BF16),
            pltpu.SemaphoreType.DMA((2, Gather.SENDS)),
            pltpu.SemaphoreType.DMA((2,) + grid),
            pltpu.SemaphoreType.DMA((2,)),
            pltpu.SemaphoreType.DMA((2,)),
            pltpu.SemaphoreType.DMA((2,)),
            pltpu.SemaphoreType.DMA((2,)),
        ],
        compiler_params=pltpu.CompilerParams(
            vmem_limit_bytes=48 * 1024 * 1024, collective_id=1, has_side_effects=True
        ),
        name="collect",
    )(x, vec, s_qkv)


def plane_partners(core, plane, spot):
    partners = []
    for other in (core, 1 - core):
        for side in range(SPOTS):
            if other is core and side == 0:
                continue
            partners.append((other, rank_of(plane, flip(spot, side))))
    return partners


def both_partners(core, plane, spot):
    return plane_partners(core, plane, spot) + column_partners(core, plane, spot)[1:]


def outward_send(source_ref, target_ref, send_sem, recv_sem, local_sem):
    core, plane, spot = place_here()
    sends, keeps = [], []
    for side in (3, 1, 2, 0):
        for other in (core, 1 - core):
            goal = flip(spot, side)
            for piece in range(PIECES):
                source = source_ref.at[other, goal, piece]
                target = target_ref.at[2 * core + piece, spot]
                if side == 0 and other is core:
                    copy = pltpu.make_async_copy(source, target, local_sem.at[piece])
                    keeps.append(copy)
                else:
                    copy = remote(
                        source,
                        target,
                        send_sem.at[len(sends)],
                        recv_sem.at[2 * core + piece, spot],
                        (other, rank_of(plane, goal)),
                    )
                    sends.append(copy)
                copy.start()

    def finish():
        for side in range(SPOTS):
            for other in (core, 1 - core):
                if side == 0 and other is core:
                    continue
                for piece in range(PIECES):
                    target = target_ref.at[2 * other + piece, flip(spot, side)]
                    remote(
                        target,
                        target,
                        send_sem.at[0],
                        recv_sem.at[2 * other + piece, flip(spot, side)],
                        (core, rank_of(plane, spot)),
                    ).wait_recv()
        for copy in sends:
            copy.wait_send()
        for copy in keeps:
            copy.wait()

    return finish


def inward_send(source_ref, target_ref, send_sem, recv_sem, local_sem):
    core, plane, spot = place_here()
    sends, keeps = [], []
    for side in (3, 1, 2, 0):
        for other in (core, 1 - core):
            goal = flip(spot, side)
            for piece in range(PIECES):
                source = source_ref.at[2 * other + piece, goal]
                target = target_ref.at[core, spot, piece]
                if side == 0 and other is core:
                    copy = pltpu.make_async_copy(source, target, local_sem.at[piece])
                    keeps.append(copy)
                else:
                    copy = remote(
                        source,
                        target,
                        send_sem.at[len(sends)],
                        recv_sem.at[core, spot, piece],
                        (other, rank_of(plane, goal)),
                    )
                    sends.append(copy)
                copy.start()

    def finish():
        for side in range(SPOTS):
            for other in (core, 1 - core):
                if side == 0 and other is core:
                    continue
                for piece in range(PIECES):
                    target = target_ref.at[other, flip(spot, side), piece]
                    remote(
                        target,
                        target,
                        send_sem.at[0],
                        recv_sem.at[other, flip(spot, side), piece],
                        (core, rank_of(plane, spot)),
                    ).wait_recv()
        for copy in sends:
            copy.wait_send()
        for copy in keeps:
            copy.wait()

    return finish


def exchange_sems(recv_shape):
    return [
        pltpu.SemaphoreType.DMA((14,)),
        pltpu.SemaphoreType.DMA(recv_shape),
        pltpu.SemaphoreType.DMA((PIECES,)),
    ]


def outward_kernel(source_ref, target_ref, send_sem, recv_sem, local_sem):
    greet(plane_partners(*place_here()))
    outward_send(source_ref, target_ref, send_sem, recv_sem, local_sem)()


def inward_kernel(source_ref, target_ref, send_sem, recv_sem, local_sem):
    greet(plane_partners(*place_here()))
    inward_send(source_ref, target_ref, send_sem, recv_sem, local_sem)()


def plane_exchange(kernel, source, shape, recv_shape, collective, name):
    return pl.pallas_call(
        kernel,
        out_shape=jax.ShapeDtypeStruct(shape, source.dtype),
        in_specs=[whole(ANY)],
        out_specs=whole(ANY),
        scratch_shapes=exchange_sems(recv_shape),
        compiler_params=pltpu.CompilerParams(
            vmem_limit_bytes=16 * 1024 * 1024, collective_id=collective, has_side_effects=True
        ),
        name=name,
    )(source)


def outward(source, collective, name):
    shape = (PLANES, SPOTS) + source.shape[3:]
    return plane_exchange(outward_kernel, source, shape, (PLANES, SPOTS), collective, name)


def inward(source, collective, name):
    shape = (2, SPOTS, PIECES) + source.shape[2:]
    return plane_exchange(
        inward_kernel, source, shape, (2, SPOTS, PIECES), collective, name
    )


def column_send(source, target, send_sem, recv_sem, local_sem):
    core, plane, spot = place_here()
    keep = pltpu.make_async_copy(source, target.at[plane], local_sem)
    keep.start()
    copies = []
    for bits in range(1, PLANES):
        copy = remote(
            source,
            target.at[plane],
            send_sem.at[bits - 1],
            recv_sem.at[plane],
            (core, rank_of(flip(plane, bits), spot)),
        )
        copy.start()
        copies.append(copy)

    def finish():
        for bits in range(1, PLANES):
            other = flip(plane, bits)
            remote(
                source,
                target.at[other],
                send_sem.at[0],
                recv_sem.at[other],
                (core, rank_of(plane, spot)),
            ).wait_recv()
        for copy in copies:
            copy.wait_send()
        keep.wait()

    return finish


def exchange_qkv_kernel(
    source_ref,
    s_ou_ref,
    s_down_ref,
    target_ref,
    c_ou_ref,
    c_down_ref,
    send_sem,
    recv_sem,
    local_sem,
    column_send_sem,
    column_recv_sem,
    column_local_sem,
):
    greet(both_partners(*place_here()))
    finish = outward_send(source_ref, target_ref, send_sem, recv_sem, local_sem)
    finishes = [
        column_send(
            source,
            target,
            column_send_sem.at[number],
            column_recv_sem.at[number],
            column_local_sem.at[number],
        )
        for number, (source, target) in enumerate(
            ((s_ou_ref, c_ou_ref), (s_down_ref, c_down_ref))
        )
    ]
    finish()
    for one in finishes:
        one()


def exchange_qkv(source, s_ou, s_down):
    return pl.pallas_call(
        exchange_qkv_kernel,
        out_shape=(
            jax.ShapeDtypeStruct((PLANES, SPOTS) + source.shape[3:], BF16),
            jax.ShapeDtypeStruct((PLANES,) + s_ou.shape, BF16),
            jax.ShapeDtypeStruct((PLANES,) + s_down.shape, BF16),
        ),
        in_specs=[whole(ANY)] * 3,
        out_specs=(whole(ANY),) * 3,
        scratch_shapes=exchange_sems((PLANES, SPOTS))
        + [
            pltpu.SemaphoreType.DMA((2, PLANES - 1)),
            pltpu.SemaphoreType.DMA((2, PLANES)),
            pltpu.SemaphoreType.DMA((2,)),
        ],
        compiler_params=pltpu.CompilerParams(
            vmem_limit_bytes=16 * 1024 * 1024, collective_id=3, has_side_effects=True
        ),
        name="exchange_qkv",
    )(source, s_ou, s_down)


class PlaneGather:
    SENDS = 3 + 4 + 2

    def __init__(self, column, target, send_sem, recv_sem, local_sem):
        self.column, self.target = column, target
        self.send_sem, self.recv_sem = send_sem, recv_sem
        self.core, self.plane, self.spot = place_here()
        self.sends = []
        self.own = pltpu.make_async_copy(column, target.at[self.core, :, self.spot], local_sem)
        self.own.start()
        for goal in (self.neighbour(1), self.neighbour(2), self.sibling()):
            self.send(column, slice(0, PLANES), self.spot, 0, goal)

    def neighbour(self, bits):
        return (self.core, rank_of(self.plane, flip(self.spot, bits)))

    def sibling(self):
        return (1 - self.core, rank_of(self.plane, self.spot))

    def piece(self, core, planes, spot):
        return self.target.at[core, planes, spot]

    def send(self, source, planes, spot, part, goal):
        copy = remote(
            source,
            self.piece(self.core, planes, spot),
            self.send_sem.at[len(self.sends)],
            self.recv_sem.at[self.core, spot, part],
            goal,
        )
        copy.start()
        self.sends.append(copy)

    def arrive(self, core, planes, spot, part):
        piece = self.piece(core, planes, spot)
        remote(
            piece,
            piece,
            self.send_sem.at[0],
            self.recv_sem.at[core, spot, part],
            (self.core, rank_of(self.plane, self.spot)),
        ).wait_recv()

    def forward(self):
        for side in (1, 2):
            spot = flip(self.spot, side)
            everything = slice(0, PLANES)
            self.arrive(self.core, everything, spot, 0)
            half = slice(0, 2) if side == 1 else slice(2, 4)
            self.send(
                self.piece(self.core, half, spot), half, spot, side - 1, self.neighbour(3 - side)
            )
            self.send(self.piece(self.core, everything, spot), everything, spot, 0, self.sibling())

    def corner(self):
        spot = flip(self.spot, 3)
        for part, half in enumerate((slice(0, 2), slice(2, 4))):
            self.arrive(self.core, half, spot, part)
            self.send(self.piece(self.core, half, spot), half, spot, part, self.sibling())

    def finish(self):
        for side in range(3):
            self.arrive(1 - self.core, slice(0, PLANES), flip(self.spot, side), 0)
        for part, half in enumerate((slice(0, 2), slice(2, 4))):
            self.arrive(1 - self.core, half, flip(self.spot, 3), part)
        self.own.wait()
        for copy in self.sends:
            copy.wait_send()


def plane_qkv_kernel(x_ref, vec_ref, w_ref, bias_ref, normed_ref, send_ref):
    pieces, rows, _ = x_ref.shape
    values = x_ref[...].reshape(pieces * rows, D).astype(F32)
    normal, _ = norm_parts(values)
    normed_ref[...] = (normal * vec_ref[0:1] + vec_ref[1:2]).astype(BF16)
    low = low_lanes(rows)
    queries = D // LANES
    for chunk in range(HALF_TILES):
        columns = slice(chunk * CHUNK, (chunk + 1) * CHUNK)
        packed = dot(normed_ref[...], w_ref[:, columns]) + bias_ref[:, columns]
        for side in range(2):
            tile = chunk + side * HALF_TILES
            whole_tile = packed[:, side * LANES : (side + 1) * LANES]
            if tile < queries:
                whole_tile = whole_tile.astype(BF16).astype(F32) * SCALE
            for piece in range(pieces):
                part = whole_tile[piece * rows : (piece + 1) * rows]
                if tile < SPOTS:
                    send_ref[0, tile, piece, 0] = part.astype(BF16)
                elif tile < queries:
                    first = 2 * (tile - SPOTS)
                    shared = send_ref[0, first, piece, 0].astype(F32)
                    send_ref[1, first, piece, 0] = jnp.where(low, part, shared).astype(BF16)
                    shared = send_ref[0, first + 1, piece, 0].astype(F32)
                    send_ref[1, first + 1, piece, 0] = jnp.where(
                        low, swap_halves(part), shared
                    ).astype(BF16)
                else:
                    spot, role = (tile - queries) // 3, (tile - queries) % 3
                    if role < 2:
                        send_ref[role, spot, piece, 1] = part.astype(BF16)
                    else:
                        send_ref[0, spot, piece, 2] = part.astype(BF16)
                        send_ref[1, spot, piece, 2] = part.astype(BF16)


def plane_qkv(x, vec, w, bias):
    pieces, rows, _ = x.shape
    return pl.pallas_call(
        plane_qkv_kernel,
        out_shape=(
            jax.ShapeDtypeStruct((pieces * rows, D), BF16),
            jax.ShapeDtypeStruct((2, SPOTS, PIECES, 3, rows, LANES), BF16),
        ),
        in_specs=[whole()] * 4,
        out_specs=(whole(), whole()),
        compiler_params=params_of(48),
        name="plane_qkv",
    )(x, vec, w, bias)


def plane_attend_kernel(
    table_ref,
    qkv_ref,
    dy_ref,
    c_ou_ref,
    c_down_ref,
    back_ref,
    lse_ref,
    dys_ref,
    w_out_ref,
    w_up_ref,
    w_down_ref,
    g_ou_ref,
    out_ref,
    s_ref,
    t_ref,
    send_sem,
    recv_sem,
    local_sem,
    gather_send,
    gather_recv,
    gather_local,
    move_send,
    move_recv,
    move_local,
):
    greet(both_partners(*place_here()))
    gathers = [
        PlaneGather(
            column,
            target,
            gather_send.at[number],
            gather_recv.at[number],
            gather_local.at[number],
        )
        for number, (column, target) in enumerate(
            ((c_ou_ref, g_ou_ref), (c_down_ref, w_down_ref))
        )
    ]
    finish_dy = to_planes(dy_ref, dys_ref, move_send, move_recv, move_local)
    groups, _, local, _, _ = qkv_ref.shape
    blocks = groups * local
    half = blocks // 2
    core = lax.axis_index("gx")
    low = low_lanes(BLOCK)
    masks = [half_mask(True), half_mask(False)]

    def load(component, block):
        return qkv_ref[lax.div(block, local), component, lax.rem(block, local)]

    def store(block, value):
        rank = lax.div(block, local)
        out_ref[lax.div(rank, SPOTS), lax.rem(rank, SPOTS), lax.rem(block, local)] = value.astype(BF16)

    def one(block, slot, ids, bias):
        keys = jnp.concatenate([load(1 + slot, spot) for spot in ids], axis=0)
        scores = dot_rt(load(0, block) * masks[slot], keys) + bias
        top = jnp.max(scores, axis=1, keepdims=True)
        powered = jnp.exp(scores - top)
        total = jnp.sum(powered, axis=1, keepdims=True)
        mixed = dot(powered.astype(BF16), keys) * (1.0 / total)
        return mixed, top + jnp.log(total)

    def sparse(step, carry):
        mine = 1 + step + core * (half - 1)
        other = 1 + step + (1 - core) * (half - 1)
        ids, bias = slots_of(table_ref, 0, mine, blocks)
        far_ids, far_bias = slots_of(table_ref, 0, other, blocks)
        mixed_a, log_a = one(mine, 0, ids, bias)
        mixed_b, log_b = one(mine, 1, ids, bias)
        mixed_c, log_c = one(other, 0, far_ids, far_bias)
        store(mine, jnp.where(low, mixed_b, mixed_a))
        store(other, mixed_c)
        lse_ref[mine] = jnp.where(low, log_a, log_b)
        lse_ref[other] = jnp.where(low, log_c, 0.0)
        return carry

    lax.fori_loop(0, half // 2, sparse, 0)
    gathers[0].forward()
    lax.fori_loop(half // 2, half - 1, sparse, 0)

    spans = blocks // SPAN
    ends = (0, blocks - 1)
    end = core * (blocks - 1)
    query_a = jnp.concatenate([load(0, number) for number in ends], axis=0) * masks[0]
    query_b = load(0, end) * masks[1]

    def keys_at(span, slot):
        return jnp.concatenate(
            [load(1 + slot, span * SPAN + number) for number in range(SPAN)], axis=0
        )

    def first_pass(span, carry):
        top_a, top_b = carry
        scores_a = dot_rt(query_a, keys_at(span, 0))
        scores_b = dot_rt(query_b, keys_at(span, 1))
        s_ref[span] = scores_a
        t_ref[span] = scores_b
        return (
            jnp.maximum(top_a, jnp.max(scores_a, axis=1, keepdims=True)),
            jnp.maximum(top_b, jnp.max(scores_b, axis=1, keepdims=True)),
        )

    top_a, top_b = lax.fori_loop(
        0,
        spans,
        first_pass,
        (jnp.full((2 * BLOCK, 1), NEGATIVE, F32), jnp.full((BLOCK, 1), NEGATIVE, F32)),
    )

    def second_pass(span, carry):
        total_a, mixed_a, total_b, mixed_b = carry
        powered_a = jnp.exp(s_ref[span] - top_a)
        powered_b = jnp.exp(t_ref[span] - top_b)
        return (
            total_a + jnp.sum(powered_a, axis=1, keepdims=True),
            mixed_a + dot(powered_a.astype(BF16), keys_at(span, 0)),
            total_b + jnp.sum(powered_b, axis=1, keepdims=True),
            mixed_b + dot(powered_b.astype(BF16), keys_at(span, 1)),
        )

    total_a, mixed_a, total_b, mixed_b = lax.fori_loop(
        0,
        spans,
        second_pass,
        (
            jnp.zeros((2 * BLOCK, 1), F32),
            jnp.zeros((2 * BLOCK, LANES), F32),
            jnp.zeros((BLOCK, 1), F32),
            jnp.zeros((BLOCK, LANES), F32),
        ),
    )
    mixed_a = mixed_a * (1.0 / total_a)
    mixed_b = mixed_b * (1.0 / total_b)
    log_a = top_a + jnp.log(total_a)
    log_b = top_b + jnp.log(total_b)
    for place, number in enumerate(ends):
        rows = slice(place * BLOCK, (place + 1) * BLOCK)
        store(number, jnp.where(low, mixed_b, mixed_a[rows]))
        lse_ref[number] = jnp.where(low, log_a[rows], log_b)

    gathers[1].forward()
    finish_mixed = inward_send(out_ref, back_ref, send_sem, recv_sem, local_sem)
    gathers[0].corner()
    gathers[0].finish()
    outs = D // LANES // 2
    settle(
        g_ou_ref,
        [(tile, w_out_ref, (tile, outs + tile)) for tile in range(outs)]
        + [(outs + tile, w_up_ref, alternate(tile)) for tile in range(FF // CHUNK)],
    )
    gathers[1].corner()
    gathers[1].finish()
    finish_dy()
    finish_mixed()


def plane_attention(table, qkv, dy, c_ou, c_down):
    groups, _, local, _, _ = qkv.shape
    blocks = groups * local
    spans = blocks // SPAN
    grid = (2, PLANES, SPOTS)
    tile = (local, BLOCK, LANES)
    return pl.pallas_call(
        plane_attend_kernel,
        out_shape=(
            jax.ShapeDtypeStruct((2, SPOTS, PIECES) + tile, BF16),
            jax.ShapeDtypeStruct((blocks, BLOCK, LANES), F32),
            jax.ShapeDtypeStruct(dy.shape, BF16),
            jax.ShapeDtypeStruct((D, D), BF16),
            jax.ShapeDtypeStruct((D, FF), BF16),
            jax.ShapeDtypeStruct(grid + c_down.shape[1:], BF16),
        ),
        in_specs=[whole(pltpu.SMEM), whole(), whole(ANY), whole(ANY), whole(ANY)],
        out_specs=(whole(ANY), whole(), whole(ANY), whole(), whole(), whole(ANY)),
        scratch_shapes=[
            VMEM(grid + c_ou.shape[1:], BF16),
            VMEM((PLANES, SPOTS) + tile, BF16),
            VMEM((spans, 2 * BLOCK, SPAN * BLOCK), F32),
            VMEM((spans, BLOCK, SPAN * BLOCK), F32),
        ]
        + exchange_sems((2, SPOTS, PIECES))
        + [
            pltpu.SemaphoreType.DMA((2, PlaneGather.SENDS)),
            pltpu.SemaphoreType.DMA((2, 2, SPOTS, 2)),
            pltpu.SemaphoreType.DMA((2,)),
            pltpu.SemaphoreType.DMA((2,)),
            pltpu.SemaphoreType.DMA((2,)),
            pltpu.SemaphoreType.DMA((2,)),
        ],
        compiler_params=pltpu.CompilerParams(
            vmem_limit_bytes=56 * 1024 * 1024, collective_id=4, has_side_effects=True
        ),
        name="plane_attention",
    )(table, qkv, dy, c_ou, c_down)


def plane_attend_back_kernel(
    table_ref, qkv_ref, grad_ref, lse_ref, out_ref, sums_ref, pa_ref, da_ref, pb_ref, db_ref
):
    groups, _, local, _, _ = qkv_ref.shape
    blocks = groups * local
    half = blocks // 2
    core = lax.axis_index("gx")
    low = low_lanes(BLOCK)
    masks = [half_mask(True), half_mask(False)]

    def load(component, block):
        return qkv_ref[lax.div(block, local), component, lax.rem(block, local)]

    def load_grad(block):
        return grad_ref[lax.div(block, local), lax.rem(block, local)]

    def store(component, block, value):
        out_ref[lax.div(block, local), component, lax.rem(block, local)] = value.astype(BF16)

    def clear(block, carry):
        for slot in range(2):
            sums_ref[slot, block] = jnp.zeros((BLOCK, LANES), F32)
        return carry

    lax.fori_loop(0, blocks, clear, 0)

    def one(block, slot, ids, bias):
        keys = jnp.concatenate([load(1 + slot, spot) for spot in ids], axis=0)
        both = jnp.concatenate(
            [load(0, block) * masks[slot], load_grad(block) * masks[1 - slot]], axis=0
        )
        products = dot_rt(both, keys)
        logs = lse_ref[block][:, slot * HEAD_DIM : slot * HEAD_DIM + 1]
        weights = jnp.exp(products[:BLOCK] + bias - logs)
        grad_weights = products[BLOCK:]
        delta = jnp.sum(weights * grad_weights, axis=1, keepdims=True)
        grad_scores = weights * (grad_weights - delta)
        stacked = jnp.concatenate([grad_scores, weights], axis=0).astype(BF16)
        return dot(stacked[:BLOCK], keys), dot_lt(stacked, both)

    def add(slot, ids, shares):
        for place, spot in enumerate(ids):
            sums_ref[slot, spot] += shares[place * BLOCK : (place + 1) * BLOCK]

    def sparse(step, carry):
        mine = 1 + step + core * (half - 1)
        other = 1 + step + (1 - core) * (half - 1)
        ids, bias = slots_of(table_ref, 0, mine, blocks)
        far_ids, far_bias = slots_of(table_ref, 0, other, blocks)
        query_a, shares_a = one(mine, 0, ids, bias)
        query_b, shares_b = one(mine, 1, ids, bias)
        query_c, shares_c = one(other, 0, far_ids, far_bias)
        store(0, mine, jnp.where(low, query_a, query_b) * SCALE)
        store(0, other, query_c * SCALE)
        add(0, ids, shares_a)
        add(1, ids, shares_b)
        add(0, far_ids, shares_c)
        return carry

    lax.fori_loop(0, half - 1, sparse, 0)

    spans = blocks // SPAN
    ends = (0, blocks - 1)
    end = core * (blocks - 1)
    both_a = jnp.concatenate(
        [load(0, number) * masks[0] for number in ends]
        + [load_grad(number) * masks[1] for number in ends],
        axis=0,
    )
    both_b = jnp.concatenate([load(0, end) * masks[1], load_grad(end) * masks[0]], axis=0)
    logs_a = jnp.concatenate([lse_ref[number][:, 0:1] for number in ends], axis=0)
    logs_b = lse_ref[end][:, HEAD_DIM : HEAD_DIM + 1]

    def keys_at(span, slot):
        return jnp.concatenate(
            [load(1 + slot, span * SPAN + number) for number in range(SPAN)], axis=0
        )

    def first_pass(span, carry):
        deltas = []
        for slot, both, logs, p_ref, d_ref in (
            (0, both_a, logs_a, pa_ref, da_ref),
            (1, both_b, logs_b, pb_ref, db_ref),
        ):
            rows = both.shape[0] // 2
            products = dot_rt(both, keys_at(span, slot))
            weights = jnp.exp(products[:rows] - logs)
            grad_weights = products[rows:]
            p_ref[span] = weights
            d_ref[span] = grad_weights
            deltas.append(carry[slot] + jnp.sum(weights * grad_weights, axis=1, keepdims=True))
        return tuple(deltas)

    deltas = lax.fori_loop(
        0, spans, first_pass, (jnp.zeros((2 * BLOCK, 1), F32), jnp.zeros((BLOCK, 1), F32))
    )

    def second_pass(span, carry):
        totals = []
        for slot, both, p_ref, d_ref in (
            (0, both_a, pa_ref, da_ref),
            (1, both_b, pb_ref, db_ref),
        ):
            rows = both.shape[0] // 2
            weights = p_ref[span]
            grad_scores = weights * (d_ref[span] - deltas[slot])
            stacked = jnp.concatenate([grad_scores, weights], axis=0).astype(BF16)
            add(slot, [span * SPAN + number for number in range(SPAN)], dot_lt(stacked, both))
            totals.append(carry[slot] + dot(stacked[:rows], keys_at(span, slot)))
        return tuple(totals)

    query_a, query_b = lax.fori_loop(
        0,
        spans,
        second_pass,
        (jnp.zeros((2 * BLOCK, LANES), F32), jnp.zeros((BLOCK, LANES), F32)),
    )
    for place, number in enumerate(ends):
        rows = slice(place * BLOCK, (place + 1) * BLOCK)
        store(0, number, jnp.where(low, query_a[rows], query_b) * SCALE)

    def finish(block, carry):
        for slot in range(2):
            store(1 + slot, block, sums_ref[slot, block])
        return carry

    lax.fori_loop(0, blocks, finish, 0)


def plane_attention_back(table, qkv, grad, lse):
    groups, _, local, _, _ = qkv.shape
    blocks = groups * local
    spans = blocks // SPAN
    wide = VMEM((spans, 2 * BLOCK, SPAN * BLOCK), F32)
    thin = VMEM((spans, BLOCK, SPAN * BLOCK), F32)
    return pl.pallas_call(
        plane_attend_back_kernel,
        out_shape=jax.ShapeDtypeStruct(qkv.shape, BF16),
        in_specs=[whole(pltpu.SMEM), whole(), whole(), whole()],
        out_specs=whole(),
        scratch_shapes=[VMEM((2, blocks, BLOCK, LANES), F32), wide, wide, thin, thin],
        compiler_params=params_of(48),
        name="plane_attention_back",
    )(table, qkv, grad, lse)


def by_owner(out_ref, values):
    rows = D // RANKS
    width = values.shape[1] // 2
    for owner in range(RANKS):
        part = values[owner * rows : (owner + 1) * rows]
        out_ref[owner] = jnp.concatenate([part[:, :width], part[:, width:]], axis=0).astype(BF16)


def plane_middle_kernel(
    mixed_in_ref,
    x_ref,
    dy_ref,
    vec_ref,
    w_out_ref,
    up_shift_ref,
    w_up_ref,
    w_down_ref,
    hidden_ref,
    send_ref,
    dres_ref,
    g_out_ref,
    g_up_ref,
    g_down_ref,
    g_up_bias_ref,
    g_small_ref,
    mixed_ref,
    residual_ref,
    second_ref,
    second_t_ref,
    total_ref,
    dsecond_ref,
):
    pieces, rows, _ = x_ref.shape
    tokens = pieces * rows
    step = pl.program_id(0)
    low = low_lanes(rows)
    out_shift, gain, shift, down_shift = (vec_ref[number : number + 1] for number in (4, 5, 6, 7))

    @pl.when(step == 0)
    def _():
        core = lax.axis_index("gx")
        for piece in range(pieces):
            span = slice(piece * rows, (piece + 1) * rows)
            for spot in (0, 2):
                first = [mixed_in_ref[side, spot, piece].astype(F32) for side in range(2)]
                last = [mixed_in_ref[side, spot + 1, piece].astype(F32) for side in range(2)]
                own_first = jnp.where(core == 0, first[0], first[1])
                own_last = jnp.where(core == 0, last[0], last[1])
                tiles = (
                    jnp.where(low, swap_halves(first[0]), first[1]),
                    jnp.where(low, own_first, last[0]),
                    swap_halves(jnp.where(low, own_last, last[1])),
                )
                for number, tile in enumerate(tiles):
                    spread = 3 * (spot // 2) + number
                    mixed_ref[span, spread * LANES : (spread + 1) * LANES] = tile.astype(BF16)
        residual = x_ref[...].reshape(tokens, D).astype(F32) + (
            dot(mixed_ref[...], w_out_ref[...]) + out_shift
        )
        residual_ref[...] = residual
        normal, _ = norm_parts(residual)
        second = normal * gain + shift
        second_ref[...] = second.astype(BF16)
        second_t_ref[...] = second.T.astype(BF16)
        total_ref[...] = jnp.zeros_like(total_ref)
        dsecond_ref[...] = jnp.zeros_like(dsecond_ref)

    w_down = w_down_ref[...].reshape(CHUNK, D)
    upper = dot(second_ref[...], w_up_ref[...]) + up_shift_ref[0]
    factor = 0.7978845608028654
    square = upper * upper
    bent = jnp.tanh(factor * (upper + 0.044715 * (upper * square)))
    middle_half = 0.5 * (1.0 + bent)
    active = (upper * middle_half).astype(BF16)
    slope = middle_half + 0.5 * upper * (1.0 - bent * bent) * (
        factor + (3.0 * 0.044715 * factor) * square
    )
    dy = dy_ref[...]
    total_ref[...] += dot(active, w_down)
    g_down_ref[...] = dot_lt(active, dy).astype(BF16).reshape(g_down_ref.shape)
    dupper = (dot_rt(dy, w_down) * slope).astype(BF16)
    g_up_bias_ref[0] = jnp.sum(dupper.astype(F32), axis=0, keepdims=True)
    by_owner(g_up_ref, dot(second_t_ref[...], dupper))
    dsecond_ref[...] += dot_rt(dupper, w_up_ref[...])

    @pl.when(step == pl.num_programs(0) - 1)
    def _():
        residual = residual_ref[...]
        hidden_ref[...] = (
            (residual + (total_ref[...] + down_shift)).astype(BF16).reshape(x_ref.shape)
        )
        normal, inverse = norm_parts(residual)
        dsecond = dsecond_ref[...]
        grad_out = dy_ref[...].astype(F32)
        g_small_ref[0:1] = jnp.sum(dsecond * normal, axis=0, keepdims=True)
        g_small_ref[1:2] = jnp.sum(dsecond, axis=0, keepdims=True)
        g_small_ref[2:3] = jnp.sum(grad_out, axis=0, keepdims=True)
        dres = grad_out + norm_pull(dsecond, normal, inverse, gain)
        dres_ref[...] = dres
        branch = dres.astype(BF16)
        g_small_ref[3:4] = jnp.sum(branch.astype(F32), axis=0, keepdims=True)
        by_owner(g_out_ref, dot_lt(mixed_ref[...], branch))
        dmixed = dot_rt(branch, w_out_ref[...])
        for piece in range(pieces):
            span = slice(piece * rows, (piece + 1) * rows)
            for spot in (0, 2):
                tiles = [
                    dmixed[span, number * LANES : (number + 1) * LANES]
                    for number in range(3 * (spot // 2), 3 * (spot // 2) + 3)
                ]
                flipped = [swap_halves(tile) for tile in tiles]
                send_ref[0, spot, piece] = jnp.where(low, tiles[1], flipped[0]).astype(BF16)
                send_ref[1, spot, piece] = jnp.where(low, tiles[1], tiles[0]).astype(BF16)
                send_ref[0, spot + 1, piece] = jnp.where(low, flipped[2], tiles[1]).astype(BF16)
                send_ref[1, spot + 1, piece] = flipped[2].astype(BF16)


def plane_middle(mixed_in, x, dy, vec, w_out, up_shift, w_up, w_down):
    pieces, rows, _ = x.shape
    tokens = pieces * rows
    shard = D // RANKS

    def fixed(shape):
        return pl.BlockSpec(shape, lambda step: (0,) * len(shape))

    steps = FF // CHUNK
    down = pl.BlockSpec((2, LANES, D), lambda step: (0, step, 0))
    return pl.pallas_call(
        plane_middle_kernel,
        grid=(steps,),
        out_shape=(
            jax.ShapeDtypeStruct(x.shape, BF16),
            jax.ShapeDtypeStruct(mixed_in.shape, BF16),
            jax.ShapeDtypeStruct((tokens, D), F32),
            jax.ShapeDtypeStruct((RANKS, 2 * shard, D // 2), BF16),
            jax.ShapeDtypeStruct((RANKS, 2 * shard, FF // 2), BF16),
            jax.ShapeDtypeStruct((2, FF // 2, D), BF16),
            jax.ShapeDtypeStruct((steps, 1, CHUNK), F32),
            jax.ShapeDtypeStruct((4, D), F32),
        ),
        in_specs=[
            fixed(mixed_in.shape),
            fixed(x.shape),
            fixed((tokens, D)),
            fixed(vec.shape),
            fixed((D, D)),
            pl.BlockSpec((1, 1, CHUNK), lambda step: (step, 0, 0)),
            pl.BlockSpec((D, CHUNK), lambda step: (0, step)),
            down,
        ],
        out_specs=(
            fixed(x.shape),
            fixed(mixed_in.shape),
            fixed((tokens, D)),
            fixed((RANKS, 2 * shard, D // 2)),
            pl.BlockSpec((RANKS, 2 * shard, LANES), lambda step: (0, 0, step)),
            down,
            pl.BlockSpec((1, 1, CHUNK), lambda step: (step, 0, 0)),
            fixed((4, D)),
        ),
        scratch_shapes=[
            VMEM((tokens, D), BF16),
            VMEM((tokens, D), F32),
            VMEM((tokens, D), BF16),
            VMEM((D, tokens), BF16),
            VMEM((tokens, D), F32),
            VMEM((tokens, D), F32),
        ],
        compiler_params=params_of(56),
        name="plane_middle",
    )(mixed_in, x, dy, vec, w_out, up_shift, w_up, w_down)


def plane_qkv_back_kernel(
    recv_ref,
    normed_ref,
    x_ref,
    dres_ref,
    vec_ref,
    w_ref,
    grad_ref,
    g_qkv_ref,
    g_bias_ref,
    g_small_ref,
    packed_ref,
    normed_t_ref,
    dnormed_ref,
):
    pieces, rows, _ = x_ref.shape
    step = pl.program_id(0)
    low = low_lanes(rows)

    @pl.when(step == 0)
    def _():
        core = lax.axis_index("gx")

        def put(tile, piece, value):
            side, chunk = tile // HALF_TILES, tile % HALF_TILES
            packed_ref[
                chunk, piece * rows : (piece + 1) * rows, side * LANES : (side + 1) * LANES
            ] = value.astype(BF16)

        for piece in range(pieces):
            seconds = []
            for spot in range(SPOTS):
                first = recv_ref[0, spot, piece, 0].astype(F32)
                second = recv_ref[1, spot, piece, 0].astype(F32)
                put(spot, piece, jnp.where(low, first, jnp.where(core == 0, first, second)))
                seconds.append(second)
                base = D // LANES + 3 * spot
                put(base, piece, recv_ref[0, spot, piece, 1])
                put(base + 1, piece, recv_ref[1, spot, piece, 1])
                shared = recv_ref[0, spot, piece, 2].astype(F32) + recv_ref[
                    1, spot, piece, 2
                ].astype(F32)
                put(base + 2, piece, shared)
            for number in range(2):
                put(
                    SPOTS + number,
                    piece,
                    jnp.where(low, seconds[2 * number], swap_halves(seconds[2 * number + 1])),
                )
        normed_t_ref[...] = normed_ref[...].astype(F32).T.astype(BF16)
        dnormed_ref[...] = jnp.zeros_like(dnormed_ref)

    packed = packed_ref[step]
    g_bias_ref[0] = jnp.sum(packed.astype(F32), axis=0, keepdims=True)
    by_owner(g_qkv_ref, dot(normed_t_ref[...], packed))
    dnormed_ref[...] += dot_rt(packed, w_ref[...])

    @pl.when(step == pl.num_programs(0) - 1)
    def _():
        normal, inverse = norm_parts(x_ref[...].reshape(pieces * rows, D).astype(F32))
        dnormed = dnormed_ref[...]
        g_small_ref[0:1] = jnp.sum(dnormed * normal, axis=0, keepdims=True)
        g_small_ref[1:2] = jnp.sum(dnormed, axis=0, keepdims=True)
        grad = dres_ref[...] + norm_pull(dnormed, normal, inverse, vec_ref[0:1])
        grad_ref[...] = grad.astype(BF16).reshape(x_ref.shape)


def plane_qkv_back(recv, normed, x, dres, vec, w):
    pieces, rows, _ = x.shape
    tokens = pieces * rows
    shard = D // RANKS

    def fixed(shape):
        return pl.BlockSpec(shape, lambda step: (0,) * len(shape))

    return pl.pallas_call(
        plane_qkv_back_kernel,
        grid=(HALF_TILES,),
        out_shape=(
            jax.ShapeDtypeStruct(x.shape, BF16),
            jax.ShapeDtypeStruct((RANKS, 2 * shard, 3 * D // 2), BF16),
            jax.ShapeDtypeStruct((HALF_TILES, 1, CHUNK), F32),
            jax.ShapeDtypeStruct((2, D), F32),
        ),
        in_specs=[
            fixed(recv.shape),
            fixed((tokens, D)),
            fixed(x.shape),
            fixed((tokens, D)),
            fixed(vec.shape),
            pl.BlockSpec((D, CHUNK), lambda step: (0, step)),
        ],
        out_specs=(
            fixed(x.shape),
            pl.BlockSpec((RANKS, 2 * shard, LANES), lambda step: (0, 0, step)),
            pl.BlockSpec((1, 1, CHUNK), lambda step: (step, 0, 0)),
            fixed((2, D)),
        ),
        scratch_shapes=[
            VMEM((HALF_TILES, tokens, CHUNK), BF16),
            VMEM((D, tokens), BF16),
            VMEM((tokens, D), F32),
        ],
        compiler_params=params_of(56),
        name="plane_qkv_back",
    )(recv, normed, x, dres, vec, w)


class Reduce:
    SENDS = 4 + 2 + 2 + 3
    RECVS = SENDS

    def __init__(self, source, total, near, corner_x, corner_y, side_x, side_y, far, out, sems):
        self.source, self.total, self.near = source, total, near
        self.corner = {1: corner_x, 2: corner_y}
        self.side = {1: side_x, 2: side_y}
        self.far, self.out = far, out
        self.send_sem, self.recv_sem, self.local_sem = sems
        self.core, self.plane, self.spot = place_here()
        self.copies = []
        self.locals = []

    def start(self):
        sibling = (1 - self.core, rank_of(self.plane, self.spot))
        for number, side in enumerate((3, 1, 2, 0)):
            spot = flip(self.spot, side)
            copy = remote(
                self.source.at[1 - self.core, :, spot],
                self.near.at[:, spot],
                self.send_sem.at[number],
                self.recv_sem.at[number],
                sibling,
            )
            copy.start()
            self.copies.append(copy)
            keep = pltpu.make_async_copy(
                self.source.at[self.core, :, spot],
                self.total.at[:, spot],
                self.local_sem.at[number],
            )
            keep.start()
            self.locals.append(keep)

    def take(self, number, side):
        self.copies[number].wait_recv()
        self.locals[number].wait()
        spot = flip(self.spot, side)

        def add(plane, carry):
            self.total[plane, spot] = (
                self.total[plane, spot].astype(F32) + self.near[plane, spot].astype(F32)
            ).astype(self.total.dtype)
            return carry

        lax.fori_loop(0, PLANES, add, 0)

    def corners(self):
        self.take(0, 3)
        spot = flip(self.spot, 3)
        index = 4
        self.corner_copies = []
        for bits in range(PLANES):
            side = 2 if bits < 2 else 1
            self.corner_copies.append(None)
            plane = flip(self.plane, bits)
            copy = remote(
                self.total.at[plane, spot],
                self.corner[side].at[bits % 2],
                self.send_sem.at[index + bits],
                self.recv_sem.at[index + bits],
                (self.core, rank_of(self.plane, flip(self.spot, side))),
            )
            copy.start()
            self.corner_copies[bits] = copy

    def sides(self):
        self.take(1, 1)
        self.take(2, 2)
        self.side_copies = {}
        for side in (1, 2):
            spot = flip(self.spot, side)
            came = 3 - side
            for bits in (0, 1) if came == 2 else (2, 3):
                self.corner_copies[bits].wait_recv()
                plane = flip(self.plane, bits)
                self.total[plane, spot] = (
                    self.total[plane, spot].astype(F32)
                    + self.corner[came][bits % 2].astype(F32)
                ).astype(self.total.dtype)
            copy = remote(
                self.total.at[:, spot],
                self.side[side],
                self.send_sem.at[7 + side],
                self.recv_sem.at[7 + side],
                (self.core, rank_of(self.plane, spot)),
            )
            copy.start()
            self.side_copies[side] = copy

    def columns(self):
        self.take(3, 0)
        for side in (1, 2):
            self.side_copies[side].wait_recv()

        def add(plane, carry):
            self.total[plane, self.spot] = (
                self.total[plane, self.spot].astype(F32)
                + self.side[1][plane].astype(F32)
                + self.side[2][plane].astype(F32)
            ).astype(self.total.dtype)
            return carry

        lax.fori_loop(0, PLANES, add, 0)
        self.far_copies = []
        for bits in range(1, PLANES):
            plane = flip(self.plane, bits)
            copy = remote(
                self.total.at[plane, self.spot],
                self.far.at[bits - 1],
                self.send_sem.at[9 + bits],
                self.recv_sem.at[9 + bits],
                (self.core, rank_of(plane, self.spot)),
            )
            copy.start()
            self.far_copies.append(copy)

    def finish(self):
        value = self.total[self.plane, self.spot].astype(F32)
        for bits in range(1, PLANES):
            self.far_copies[bits - 1].wait_recv()
            value = value + self.far[bits - 1].astype(F32)
        self.out[...] = value
        for copy in self.copies + self.corner_copies + self.far_copies:
            copy.wait_send()
        for side in (1, 2):
            self.side_copies[side].wait_send()


REDUCE_SEMS = 13


def reduce_scratch(shape, kind):
    tail = shape[3:]
    return [
        VMEM((PLANES, SPOTS) + tail, kind),
        VMEM((PLANES, SPOTS) + tail, kind),
        VMEM((2,) + tail, kind),
        VMEM((2,) + tail, kind),
        VMEM((PLANES,) + tail, kind),
        VMEM((PLANES,) + tail, kind),
        VMEM((PLANES - 1,) + tail, kind),
    ]


def spread_kernel(count, *refs):
    hidden_ref, grad_ref = refs[:2]
    sources = refs[2 : 2 + count]
    hidden_out_ref, grad_out_ref = refs[2 + count : 4 + count]
    outs = refs[4 + count : 4 + 2 * count]
    scratch = refs[4 + 2 * count :]
    buffers = scratch[: 7 * count]
    send_sem, recv_sem, local_sem, move_send, move_recv, move_local = scratch[7 * count :]
    core, plane, spot = place_here()
    greet(all_partners(core, plane, spot))
    sums = [
        Reduce(
            source,
            *buffers[7 * number : 7 * number + 7],
            out,
            (send_sem.at[number], recv_sem.at[number], local_sem.at[number]),
        )
        for number, (source, out) in enumerate(zip(sources, outs))
    ]
    for one in sums:
        one.start()
    finish_grad = from_planes(grad_ref, grad_out_ref, move_send.at[0], move_recv.at[0], move_local.at[0])
    finish_hidden = from_planes(
        hidden_ref, hidden_out_ref, move_send.at[1], move_recv.at[1], move_local.at[1]
    )
    for one in sums:
        one.corners()
    for one in sums:
        one.sides()
    for one in sums:
        one.columns()
    for one in sums:
        one.finish()
    finish_grad()
    finish_hidden()


def spread(hidden, grad, sources):
    count = len(sources)
    buffers = []
    for source in sources:
        buffers += reduce_scratch(source.shape, source.dtype)
    return pl.pallas_call(
        functools.partial(spread_kernel, count),
        out_shape=(
            jax.ShapeDtypeStruct(hidden.shape, BF16),
            jax.ShapeDtypeStruct(grad.shape, BF16),
        )
        + tuple(jax.ShapeDtypeStruct(source.shape[3:], F32) for source in sources),
        in_specs=[whole(ANY)] * (2 + count),
        out_specs=(whole(ANY), whole(ANY)) + (whole(),) * count,
        scratch_shapes=buffers
        + [
            pltpu.SemaphoreType.DMA((count, REDUCE_SEMS)),
            pltpu.SemaphoreType.DMA((count, REDUCE_SEMS)),
            pltpu.SemaphoreType.DMA((count, 4)),
            pltpu.SemaphoreType.DMA((2, 2)),
            pltpu.SemaphoreType.DMA((2, 2)),
            pltpu.SemaphoreType.DMA((2, 2)),
        ],
        compiler_params=pltpu.CompilerParams(
            vmem_limit_bytes=56 * 1024 * 1024, collective_id=2, has_side_effects=True
        ),
        name="spread",
    )(hidden, grad, *sources)


def fold_columns(array):
    half = array.shape[1] // 2
    return jnp.concatenate([array[:, :half], array[:, half:]], axis=0)


def unfold_columns(array):
    half = array.shape[0] // 2
    return jnp.concatenate([array[:half], array[half:]], axis=1)


def plane_shards(
    hidden_in,
    rand_table,
    norm1_gain,
    norm1_bias,
    w_qkv,
    query_bias,
    value_bias,
    w_out,
    out_bias,
    norm2_gain,
    norm2_bias,
    w_up,
    up_bias,
    w_down,
    down_bias,
    cotangent,
):
    micro, rows, _ = hidden_in.shape
    local = rows // BLOCK
    own = norm1_gain.shape[0]
    order = [natural_block(entry) for entry in column_order()]
    inverse = [order.index(number) for number in range(len(order))]
    small = (8 + FF // D) * own
    entries = rand_table.size

    vec = jnp.concatenate(
        [
            norm1_gain,
            norm1_bias,
            query_bias,
            value_bias,
            out_bias,
            norm2_gain,
            norm2_bias,
            down_bias,
            up_bias,
            rand_table.reshape(entries).astype(BF16),
            jnp.zeros((16 * LANES - small - entries,), BF16),
        ]
    ).reshape(16, LANES)
    x, vecs, w_qkv_all = collect(hidden_in, vec, fold_columns(take_blocks(w_qkv, order)))
    vecs = vecs.reshape(RANKS, 16 * LANES)
    vectors = vecs[:, : 8 * own].reshape(RANKS, 8, own).swapaxes(0, 1).reshape(8, D).astype(F32)
    up_shift = vecs[:, 8 * own : small].astype(F32).reshape(2, FF // CHUNK, LANES)
    up_shift = up_shift.swapaxes(0, 1).reshape(FF // CHUNK, 1, CHUNK)
    bias = jnp.concatenate([vectors[2:3], jnp.zeros((1, D), F32), vectors[3:4]], axis=1)
    bias = take_blocks(bias, order).reshape(2, HALF_TILES, LANES)
    bias = bias.swapaxes(0, 1).reshape(1, 3 * D)
    plane = lax.div(lax.axis_index("gy"), SPOTS)
    tables = vecs[:, small : small + entries].reshape(2, PLANES * SPOTS, 2, local * RANDOM)
    tables = tables.astype(jnp.int32).transpose(2, 0, 1, 3).reshape(PLANES, 1, -1)
    table = lax.dynamic_index_in_dim(tables, plane, 0, keepdims=False)

    normed, send = plane_qkv(x, vectors, w_qkv_all, bias)
    s_ou = jnp.concatenate([fold_columns(w_out), fold_columns(w_up)], axis=1)
    qkv, c_ou, c_down = exchange_qkv(send, s_ou, w_down)
    qkv = qkv.reshape(PLANES * SPOTS, 3, local, BLOCK, LANES)
    mixed, lse, dy, w_out_all, w_up_all, w_down_all = plane_attention(
        table, qkv, cotangent, c_ou, c_down
    )
    mixed = mixed.reshape(2, SPOTS, PIECES, rows, LANES)
    hidden, grad_send, dres, g_out, g_up, g_down, g_up_bias, g_mid = plane_middle(
        mixed,
        x,
        dy.reshape(micro * rows, D),
        vectors,
        w_out_all,
        up_shift,
        w_up_all,
        w_down_all.reshape(2, FF // 2, D),
    )
    grad_mixed = outward(grad_send, 5, "exchange_dmixed")
    grad_mixed = grad_mixed.reshape(PLANES * SPOTS, local, BLOCK, LANES)
    dqkv = plane_attention_back(table, qkv, grad_mixed, lse)
    dqkv = inward(dqkv.reshape(PLANES, SPOTS, 3, rows, LANES), 6, "exchange_dqkv")
    grad, g_qkv, g_bias, g_first = plane_qkv_back(dqkv, normed, x, dres, vectors, w_qkv_all)

    g_bias = g_bias.reshape(HALF_TILES, 2, LANES).swapaxes(0, 1).reshape(1, 3 * D)
    g_bias = take_blocks(g_bias, inverse)
    singles = jnp.concatenate(
        [g_first, g_bias[:, :D], g_bias[:, 2 * D :], g_mid[3:4], g_mid[0:3]], axis=0
    )
    singles = singles.reshape(8, RANKS, own).swapaxes(0, 1).reshape(RANKS, 8 * own)
    g_up_bias = g_up_bias.reshape(FF // CHUNK, 2, LANES).swapaxes(0, 1).reshape(RANKS, FF // RANKS)
    singles = jnp.concatenate(
        [singles, g_up_bias, jnp.zeros((RANKS, 8 * LANES - small), F32)], axis=1
    )
    grid = (2, PLANES, SPOTS)
    hidden_out, grad_hidden, singles, t_qkv, t_out, t_up, t_down = spread(
        hidden,
        grad,
        [
            singles.reshape(grid + (8, LANES)),
            g_qkv.reshape(grid + g_qkv.shape[1:]),
            g_out.reshape(grid + g_out.shape[1:]),
            g_up.reshape(grid + g_up.shape[1:]),
            g_down.reshape(grid + (FF // RANKS, D)),
        ],
    )
    singles = singles.reshape(8 * LANES)
    parts = [singles[number * own : (number + 1) * own] for number in range(8)]
    return (
        hidden_out,
        grad_hidden.astype(F32),
        parts[0],
        parts[1],
        take_blocks(unfold_columns(t_qkv), inverse),
        parts[2],
        parts[3],
        unfold_columns(t_out),
        parts[4],
        parts[5],
        parts[6],
        unfold_columns(t_up),
        singles[8 * own : small],
        t_down,
        parts[7],
    )


def shards(*arrays):
    micro, rows, _ = arrays[0].shape
    fits = lax.axis_size("gx") == 2 and lax.axis_size("gy") == PLANES * SPOTS
    fits = fits and micro == 2 and rows % BLOCK == 0
    return (plane_shards if fits else general_shards)(*arrays)


def solution(mesh):
    tokens = P(None, AXES, None)
    vector = P(AXES)
    matrix = P(AXES, None)
    placed = (
        tokens,
        tokens,
        vector,
        vector,
        matrix,
        vector,
        vector,
        matrix,
        vector,
        vector,
        vector,
        matrix,
        vector,
        matrix,
        vector,
        tokens,
    )
    returned = (
        tokens,
        tokens,
        vector,
        vector,
        matrix,
        vector,
        vector,
        matrix,
        vector,
        vector,
        vector,
        matrix,
        vector,
        matrix,
        vector,
    )
    return jax.shard_map(
        shards, mesh=mesh, in_specs=placed, out_specs=returned, check_vma=False
    )
```

```python
import functools

import jax
import jax.numpy as jnp
from jax import lax
from jax.experimental import pallas as pl
from jax.experimental.pallas import tpu as pltpu
from jax.sharding import PartitionSpec as P

HEADS = 12
HEAD_DIM = 64
D = 768
FF = 3072
BLOCK = 64
RANDOM = 3
LANES = 2 * HEAD_DIM
EPSILON = 1e-05
NEGATIVE = -1e30
SCALE = HEAD_DIM**-0.5
CHUNK = 256
SPAN = 8

F32 = jnp.float32
BF16 = jnp.bfloat16
VMEM = pltpu.VMEM


def whole(space=VMEM):
    return pl.BlockSpec(memory_space=space)


def params_of(megabytes):
    return pltpu.CompilerParams(vmem_limit_bytes=megabytes * 1024 * 1024)


def head_place(head):
    return (head // 3) * 4 + head % 3


def dot(left, right):
    return lax.dot_general(left, right, (((1,), (0,)), ((), ())), preferred_element_type=F32)


def dot_rt(left, right):
    return lax.dot_general(left, right, (((1,), (1,)), ((), ())), preferred_element_type=F32)


def dot_lt(left, right):
    return lax.dot_general(left, right, (((0,), (0,)), ((), ())), preferred_element_type=F32)


def swap_halves(tile):
    return pltpu.roll(tile, HEAD_DIM, axis=tile.ndim - 1)


def low_lanes(rows):
    return lax.broadcasted_iota(jnp.int32, (rows, LANES), 1) < HEAD_DIM


def norm_parts(values):
    centre = values - jnp.mean(values, axis=-1, keepdims=True)
    spread = jnp.mean(centre * centre, axis=-1, keepdims=True)
    inverse = lax.rsqrt(spread + EPSILON)
    return centre * inverse, inverse


def norm_pull(grad, normal, inverse, gain):
    scaled = grad * gain
    return inverse * (
        scaled
        - jnp.mean(scaled, axis=-1, keepdims=True)
        - normal * jnp.mean(scaled * normal, axis=-1, keepdims=True)
    )


def qkv_kernel(x_ref, gain_ref, shift_ref, w_ref, bias_ref, normed_ref, send_ref):
    micro, rows, _ = x_ref.shape
    values = x_ref[...].reshape(micro * rows, D).astype(F32)
    normal, _ = norm_parts(values)
    normed_ref[...] = (normal * gain_ref[...] + shift_ref[...]).astype(BF16)
    low = low_lanes(rows)
    for chunk in range(3 * D // CHUNK):
        columns = slice(chunk * CHUNK, (chunk + 1) * CHUNK)
        packed = dot(normed_ref[...], w_ref[:, columns]) + bias_ref[:, columns]
        if chunk < D // CHUNK:
            packed = packed.astype(BF16).astype(F32) * SCALE
        for tile in range(CHUNK // LANES):
            part = packed[:, tile * LANES : (tile + 1) * LANES]
            first, second = part[:rows], part[rows:]
            if chunk < D // CHUNK:
                head = (chunk * CHUNK // LANES + tile) * 2
                even = jnp.where(low, first, swap_halves(second))
                odd = jnp.where(low, swap_halves(first), second)
                send_ref[head_place(head), 0] = even.astype(BF16)
                send_ref[head_place(head + 1), 0] = odd.astype(BF16)
            else:
                head = (chunk * CHUNK - D) // LANES + tile
                send_ref[head_place(head), 1] = first.astype(BF16)
                send_ref[head_place(head), 2] = swap_halves(second).astype(BF16)


def qkv_forward(x, gain, shift, w, bias, groups):
    micro, rows, _ = x.shape
    return pl.pallas_call(
        qkv_kernel,
        out_shape=(
            jax.ShapeDtypeStruct((micro * rows, D), BF16),
            jax.ShapeDtypeStruct((groups, 3, rows, LANES), BF16),
        ),
        in_specs=[whole()] * 5,
        out_specs=(whole(), whole()),
        compiler_params=params_of(48),
        name="qkv_forward",
    )(x, gain, shift, w, bias)


def half_mask(low_half):
    lane = lax.broadcasted_iota(jnp.int32, (1, LANES), 1)
    keep = (lane < HEAD_DIM) if low_half else (lane >= HEAD_DIM)
    return jnp.where(keep, 1.0, 0.0).astype(BF16)


def slots_of(table_ref, micro, block, blocks):
    picks = [table_ref[micro, block * RANDOM + number] for number in range(RANDOM)]
    last = blocks - 1
    ids = [block - 1, block, block + 1, 0, last] + picks
    dropped = [None, None, None, block == 1, block == last - 1]
    for number in range(RANDOM):
        pick = picks[number]
        bad = (jnp.abs(pick - block) <= 1) | (pick == 0) | (pick == last)
        for earlier in range(number):
            bad = bad | (pick == picks[earlier])
        dropped.append(bad)
    lane = lax.broadcasted_iota(jnp.int32, (1, LANES), 1)
    tiles = []
    for pair in range(len(ids) // 2):
        level = [
            0.0 if bad is None else jnp.where(bad, NEGATIVE, 0.0).astype(F32)
            for bad in dropped[2 * pair : 2 * pair + 2]
        ]
        tiles.append(jnp.where(lane < HEAD_DIM, level[0], level[1]))
    return ids, jnp.concatenate(tiles, axis=1)


def attend_kernel(table_ref, qkv_ref, out_ref, lse_ref, s_ref):
    groups, _, local, _, _ = qkv_ref.shape
    blocks = groups * local
    low = low_lanes(BLOCK)
    masks = [half_mask(True), half_mask(False)]

    def load(component, block):
        return qkv_ref[block // local, component, block % local]

    def sparse(block, carry):
        mixed, logs = [], []
        for micro in range(2):
            ids, bias = slots_of(table_ref, micro, block, blocks)
            keys = jnp.concatenate([load(1 + micro, spot) for spot in ids], axis=0)
            query = load(0, block) * masks[micro]
            scores = dot_rt(query, keys) + bias
            top = jnp.max(scores, axis=1, keepdims=True)
            powered = jnp.exp(scores - top)
            total = jnp.sum(powered, axis=1, keepdims=True)
            mixed.append(dot(powered.astype(BF16), keys) * (1.0 / total))
            logs.append(top + jnp.log(total))
        out_ref[block // local, block % local] = jnp.where(low, mixed[1], mixed[0]).astype(BF16)
        lse_ref[block] = jnp.where(low, logs[0], logs[1])
        return carry

    lax.fori_loop(1, blocks - 1, sparse, 0)

    spans = blocks // SPAN
    ends = (0, blocks - 1)
    results = []
    for micro in range(2):
        query = jnp.concatenate([load(0, end) for end in ends], axis=0) * masks[micro]

        def keys_at(span, micro=micro):
            return jnp.concatenate(
                [load(1 + micro, span * SPAN + spot) for spot in range(SPAN)], axis=0
            )

        def first_pass(span, top, query=query, keys_at=keys_at):
            scores = dot_rt(query, keys_at(span))
            s_ref[span] = scores
            return jnp.maximum(top, jnp.max(scores, axis=1, keepdims=True))

        top = lax.fori_loop(0, spans, first_pass, jnp.full((2 * BLOCK, 1), NEGATIVE, F32))

        def second_pass(span, carry, top=top, keys_at=keys_at):
            total, mixed = carry
            powered = jnp.exp(s_ref[span] - top)
            return (
                total + jnp.sum(powered, axis=1, keepdims=True),
                mixed + dot(powered.astype(BF16), keys_at(span)),
            )

        total, mixed = lax.fori_loop(
            0,
            spans,
            second_pass,
            (jnp.zeros((2 * BLOCK, 1), F32), jnp.zeros((2 * BLOCK, LANES), F32)),
        )
        results.append((mixed * (1.0 / total), top + jnp.log(total)))
    for place, end in enumerate(ends):
        rows = slice(place * BLOCK, (place + 1) * BLOCK)
        out_ref[end // local, end % local] = jnp.where(
            low, results[1][0][rows], results[0][0][rows]
        ).astype(BF16)
        lse_ref[end] = jnp.where(low, results[0][1][rows], results[1][1][rows])


def attention_forward(table, qkv):
    groups, _, local, _, _ = qkv.shape
    blocks = groups * local
    return pl.pallas_call(
        attend_kernel,
        out_shape=(
            jax.ShapeDtypeStruct((groups, local, BLOCK, LANES), BF16),
            jax.ShapeDtypeStruct((blocks, BLOCK, LANES), F32),
        ),
        in_specs=[whole(pltpu.SMEM), whole()],
        out_specs=(whole(), whole()),
        scratch_shapes=[VMEM((blocks // SPAN, 2 * BLOCK, SPAN * BLOCK), F32)],
        compiler_params=params_of(48),
        name="attention_forward",
    )(table, qkv)


def attend_back_kernel(table_ref, qkv_ref, grad_ref, lse_ref, out_ref, sums_ref, p_ref, dp_ref):
    groups, _, local, _, _ = qkv_ref.shape
    blocks = groups * local
    low = low_lanes(BLOCK)
    masks = [half_mask(True), half_mask(False)]

    def load(component, block):
        return qkv_ref[block // local, component, block % local]

    def load_grad(block):
        return grad_ref[block // local, block % local]

    def clear(block, carry):
        for micro in range(2):
            sums_ref[micro, block] = jnp.zeros((BLOCK, LANES), F32)
        return carry

    lax.fori_loop(0, blocks, clear, 0)

    def sparse(block, carry):
        grads = []
        for micro in range(2):
            ids, bias = slots_of(table_ref, micro, block, blocks)
            keys = jnp.concatenate([load(1 + micro, spot) for spot in ids], axis=0)
            both = jnp.concatenate(
                [load(0, block) * masks[micro], load_grad(block) * masks[1 - micro]], axis=0
            )
            products = dot_rt(both, keys)
            logs = lse_ref[block][:, micro * HEAD_DIM : micro * HEAD_DIM + 1]
            weights = jnp.exp(products[:BLOCK] + bias - logs)
            grad_weights = products[BLOCK:]
            delta = jnp.sum(weights * grad_weights, axis=1, keepdims=True)
            grad_scores = weights * (grad_weights - delta)
            stacked = jnp.concatenate([grad_scores, weights], axis=0).astype(BF16)
            grads.append(dot(stacked[:BLOCK], keys))
            shares = dot_lt(stacked, both)
            for place, spot in enumerate(ids):
                sums_ref[micro, spot] += shares[place * BLOCK : (place + 1) * BLOCK]
        out_ref[block // local, 0, block % local] = (
            jnp.where(low, grads[0], grads[1]) * SCALE
        ).astype(BF16)
        return carry

    lax.fori_loop(1, blocks - 1, sparse, 0)

    spans = blocks // SPAN
    ends = (0, blocks - 1)
    results = []
    for micro in range(2):
        query = jnp.concatenate([load(0, end) for end in ends], axis=0) * masks[micro]
        grad = jnp.concatenate([load_grad(end) for end in ends], axis=0) * masks[1 - micro]
        both = jnp.concatenate([query, grad], axis=0)
        logs = jnp.concatenate(
            [lse_ref[end][:, micro * HEAD_DIM : micro * HEAD_DIM + 1] for end in ends], axis=0
        )

        def keys_at(span, micro=micro):
            return jnp.concatenate(
                [load(1 + micro, span * SPAN + spot) for spot in range(SPAN)], axis=0
            )

        def first_pass(span, delta, both=both, logs=logs, keys_at=keys_at):
            products = dot_rt(both, keys_at(span))
            weights = jnp.exp(products[: 2 * BLOCK] - logs)
            grad_weights = products[2 * BLOCK :]
            p_ref[span] = weights
            dp_ref[span] = grad_weights
            return delta + jnp.sum(weights * grad_weights, axis=1, keepdims=True)

        delta = lax.fori_loop(0, spans, first_pass, jnp.zeros((2 * BLOCK, 1), F32))

        def second_pass(span, carry, delta=delta, both=both, keys_at=keys_at, micro=micro):
            weights = p_ref[span]
            grad_scores = weights * (dp_ref[span] - delta)
            stacked = jnp.concatenate([grad_scores, weights], axis=0).astype(BF16)
            shares = dot_lt(stacked, both)
            for spot in range(SPAN):
                sums_ref[micro, span * SPAN + spot] += shares[spot * BLOCK : (spot + 1) * BLOCK]
            return carry + dot(stacked[: 2 * BLOCK], keys_at(span))

        results.append(
            lax.fori_loop(0, spans, second_pass, jnp.zeros((2 * BLOCK, LANES), F32))
        )
    for place, end in enumerate(ends):
        rows = slice(place * BLOCK, (place + 1) * BLOCK)
        out_ref[end // local, 0, end % local] = (
            jnp.where(low, results[0][rows], results[1][rows]) * SCALE
        ).astype(BF16)

    def finish(block, carry):
        for micro in range(2):
            out_ref[block // local, 1 + micro, block % local] = sums_ref[micro, block].astype(BF16)
        return carry

    lax.fori_loop(0, blocks, finish, 0)


def attention_backward(table, qkv, grad, lse):
    groups, _, local, _, _ = qkv.shape
    blocks = groups * local
    spans = VMEM((blocks // SPAN, 2 * BLOCK, SPAN * BLOCK), F32)
    return pl.pallas_call(
        attend_back_kernel,
        out_shape=jax.ShapeDtypeStruct(qkv.shape, BF16),
        in_specs=[whole(pltpu.SMEM), whole(), whole(), whole()],
        out_specs=whole(),
        scratch_shapes=[VMEM((2, blocks, BLOCK, LANES), F32), spans, spans],
        compiler_params=params_of(48),
        name="attention_backward",
    )(table, qkv, grad, lse)


def middle_kernel(
    mixed_in_ref,
    x_ref,
    dy_ref,
    w_out_ref,
    out_shift_ref,
    gain_ref,
    shift_ref,
    up_shift_ref,
    down_shift_ref,
    w_up_ref,
    w_down_ref,
    hidden_ref,
    send_ref,
    dres_ref,
    g_out_ref,
    g_up_ref,
    g_down_ref,
    g_up_bias_ref,
    g_small_ref,
    mixed_ref,
    residual_ref,
    second_ref,
    second_t_ref,
    total_ref,
    dsecond_ref,
):
    micro, rows, _ = x_ref.shape
    step = pl.program_id(0)
    low = low_lanes(rows)

    @pl.when(step == 0)
    def _():
        for pair in range(HEADS // 2):
            even = mixed_in_ref[head_place(2 * pair)].astype(F32)
            odd = mixed_in_ref[head_place(2 * pair + 1)].astype(F32)
            columns = slice(pair * LANES, (pair + 1) * LANES)
            mixed_ref[:rows, columns] = jnp.where(low, swap_halves(even), odd).astype(BF16)
            mixed_ref[rows:, columns] = jnp.where(low, even, swap_halves(odd)).astype(BF16)
        residual = x_ref[...].reshape(micro * rows, D).astype(F32) + (
            dot(mixed_ref[...], w_out_ref[...]) + out_shift_ref[...]
        )
        residual_ref[...] = residual
        normal, _ = norm_parts(residual)
        second = normal * gain_ref[...] + shift_ref[...]
        second_ref[...] = second.astype(BF16)
        second_t_ref[...] = second.T.astype(BF16)
        total_ref[...] = jnp.zeros_like(total_ref)
        dsecond_ref[...] = jnp.zeros_like(dsecond_ref)

    upper = dot(second_ref[...], w_up_ref[...]) + up_shift_ref[...]
    factor = 0.7978845608028654
    square = upper * upper
    bent = jnp.tanh(factor * (upper + 0.044715 * (upper * square)))
    half = 0.5 * (1.0 + bent)
    active = (upper * half).astype(BF16)
    slope = half + 0.5 * upper * (1.0 - bent * bent) * (
        factor + (3.0 * 0.044715 * factor) * square
    )
    dy = dy_ref[...]
    total_ref[...] += dot(active, w_down_ref[...])
    g_down_ref[...] = dot_lt(active, dy).astype(g_down_ref.dtype)
    dupper = (dot_rt(dy, w_down_ref[...]) * slope).astype(BF16)
    g_up_bias_ref[...] = jnp.sum(dupper.astype(F32), axis=0, keepdims=True)
    g_up_ref[...] = dot(second_t_ref[...], dupper).astype(g_up_ref.dtype)
    dsecond_ref[...] += dot_rt(dupper, w_up_ref[...])

    @pl.when(step == pl.num_programs(0) - 1)
    def _():
        residual = residual_ref[...]
        hidden_ref[...] = (
            (residual + (total_ref[...] + down_shift_ref[...])).astype(BF16).reshape(x_ref.shape)
        )
        normal, inverse = norm_parts(residual)
        dsecond = dsecond_ref[...]
        grad_out = dy_ref[...].astype(F32)
        g_small_ref[0:1] = jnp.sum(dsecond * normal, axis=0, keepdims=True)
        g_small_ref[1:2] = jnp.sum(dsecond, axis=0, keepdims=True)
        g_small_ref[2:3] = jnp.sum(grad_out, axis=0, keepdims=True)
        dres = grad_out + norm_pull(dsecond, normal, inverse, gain_ref[...])
        dres_ref[...] = dres
        branch = dres.astype(BF16)
        g_small_ref[3:4] = jnp.sum(branch.astype(F32), axis=0, keepdims=True)
        g_out_ref[...] = dot_lt(mixed_ref[...], branch).astype(g_out_ref.dtype)
        dmixed = dot_rt(branch, w_out_ref[...])
        for pair in range(HEADS // 2):
            part = dmixed[:, pair * LANES : (pair + 1) * LANES]
            first, last = part[:rows], part[rows:]
            even = jnp.where(low, last, swap_halves(first))
            odd = jnp.where(low, swap_halves(last), first)
            send_ref[head_place(2 * pair)] = even.astype(BF16)
            send_ref[head_place(2 * pair + 1)] = odd.astype(BF16)


def middle(mixed_in, x, dy, w_out, out_shift, gain, shift, up_shift, down_shift, w_up, w_down, kind):
    micro, rows, _ = x.shape
    tokens = micro * rows
    groups = mixed_in.shape[0]

    def fixed(shape):
        return pl.BlockSpec(shape, lambda step: (0,) * len(shape))

    vector = fixed((1, D))
    steps = FF // CHUNK
    return pl.pallas_call(
        middle_kernel,
        grid=(steps,),
        out_shape=(
            jax.ShapeDtypeStruct(x.shape, BF16),
            jax.ShapeDtypeStruct((groups, rows, LANES), BF16),
            jax.ShapeDtypeStruct((tokens, D), F32),
            jax.ShapeDtypeStruct((D, D), kind),
            jax.ShapeDtypeStruct((D, FF), kind),
            jax.ShapeDtypeStruct((FF, D), kind),
            jax.ShapeDtypeStruct((1, FF), F32),
            jax.ShapeDtypeStruct((4, D), F32),
        ),
        in_specs=[
            fixed(mixed_in.shape),
            fixed(x.shape),
            fixed((tokens, D)),
            fixed((D, D)),
            vector,
            vector,
            vector,
            pl.BlockSpec((1, CHUNK), lambda step: (0, step)),
            vector,
            pl.BlockSpec((D, CHUNK), lambda step: (0, step)),
            pl.BlockSpec((CHUNK, D), lambda step: (step, 0)),
        ],
        out_specs=(
            fixed(x.shape),
            fixed((groups, rows, LANES)),
            fixed((tokens, D)),
            fixed((D, D)),
            pl.BlockSpec((D, CHUNK), lambda step: (0, step)),
            pl.BlockSpec((CHUNK, D), lambda step: (step, 0)),
            pl.BlockSpec((1, CHUNK), lambda step: (0, step)),
            fixed((4, D)),
        ),
        scratch_shapes=[
            VMEM((tokens, D), BF16),
            VMEM((tokens, D), F32),
            VMEM((tokens, D), BF16),
            VMEM((D, tokens), BF16),
            VMEM((tokens, D), F32),
            VMEM((tokens, D), F32),
        ],
        compiler_params=params_of(56),
        name="middle",
    )(mixed_in, x, dy, w_out, out_shift, gain, shift, up_shift, down_shift, w_up, w_down)


def qkv_back_kernel(
    recv_ref,
    normed_ref,
    x_ref,
    dres_ref,
    gain_ref,
    w_ref,
    grad_ref,
    g_qkv_ref,
    g_bias_ref,
    g_small_ref,
    packed_ref,
    normed_t_ref,
    dnormed_ref,
):
    micro, rows, _ = x_ref.shape
    step = pl.program_id(0)
    low = low_lanes(rows)

    @pl.when(step == 0)
    def _():
        for pair in range(HEADS // 2):
            even = recv_ref[head_place(2 * pair), 0].astype(F32)
            odd = recv_ref[head_place(2 * pair + 1), 0].astype(F32)
            spot, columns = pair // 2, slice((pair % 2) * LANES, (pair % 2 + 1) * LANES)
            packed_ref[spot, :rows, columns] = jnp.where(low, even, swap_halves(odd)).astype(BF16)
            packed_ref[spot, rows:, columns] = jnp.where(low, swap_halves(even), odd).astype(BF16)
        for head in range(HEADS):
            spot = D // CHUNK + head // 2
            columns = slice((head % 2) * LANES, (head % 2 + 1) * LANES)
            packed_ref[spot, :rows, columns] = recv_ref[head_place(head), 1]
            packed_ref[spot, rows:, columns] = swap_halves(
                recv_ref[head_place(head), 2].astype(F32)
            ).astype(BF16)
        normed_t_ref[...] = normed_ref[...].astype(F32).T.astype(BF16)
        dnormed_ref[...] = jnp.zeros_like(dnormed_ref)

    packed = packed_ref[step]
    g_bias_ref[...] = jnp.sum(packed.astype(F32), axis=0, keepdims=True)
    g_qkv_ref[...] = dot(normed_t_ref[...], packed).astype(g_qkv_ref.dtype)
    dnormed_ref[...] += dot_rt(packed, w_ref[...])

    @pl.when(step == pl.num_programs(0) - 1)
    def _():
        normal, inverse = norm_parts(x_ref[...].reshape(micro * rows, D).astype(F32))
        dnormed = dnormed_ref[...]
        g_small_ref[0:1] = jnp.sum(dnormed * normal, axis=0, keepdims=True)
        g_small_ref[1:2] = jnp.sum(dnormed, axis=0, keepdims=True)
        grad = dres_ref[...] + norm_pull(dnormed, normal, inverse, gain_ref[...])
        grad_ref[...] = grad.reshape(x_ref.shape)


def qkv_backward(recv, normed, x, dres, gain, w, kind):
    micro, rows, _ = x.shape
    tokens = micro * rows

    def fixed(shape):
        return pl.BlockSpec(shape, lambda step: (0,) * len(shape))

    steps = 3 * D // CHUNK
    return pl.pallas_call(
        qkv_back_kernel,
        grid=(steps,),
        out_shape=(
            jax.ShapeDtypeStruct(x.shape, F32),
            jax.ShapeDtypeStruct((D, 3 * D), kind),
            jax.ShapeDtypeStruct((1, 3 * D), F32),
            jax.ShapeDtypeStruct((2, D), F32),
        ),
        in_specs=[
            fixed(recv.shape),
            fixed((tokens, D)),
            fixed(x.shape),
            fixed((tokens, D)),
            fixed((1, D)),
            pl.BlockSpec((D, CHUNK), lambda step: (0, step)),
        ],
        out_specs=(
            fixed(x.shape),
            pl.BlockSpec((D, CHUNK), lambda step: (0, step)),
            pl.BlockSpec((1, CHUNK), lambda step: (0, step)),
            fixed((2, D)),
        ),
        scratch_shapes=[
            VMEM((steps, tokens, CHUNK), BF16),
            VMEM((D, tokens), BF16),
            VMEM((tokens, D), F32),
        ],
        compiler_params=params_of(56),
        name="qkv_backward",
    )(recv, normed, x, dres, gain, w)


AXES = ("gx", "gy")


def gather(array):
    return lax.all_gather(array, AXES, axis=0, tiled=True)


def scatter(array):
    return lax.psum_scatter(array, AXES, scatter_dimension=0, tiled=True)


def exchange(array):
    return lax.all_to_all(array, "gy", 0, 0, tiled=True)


def by_heads(w_qkv):
    rows = w_qkv.shape[0]
    sides = w_qkv[:, D:].reshape(rows, 2, HEADS, HEAD_DIM)
    return jnp.concatenate([w_qkv[:, :D], jnp.swapaxes(sides, 1, 2).reshape(rows, 2 * D)], axis=1)


def by_parts(w_qkv):
    rows = w_qkv.shape[0]
    sides = w_qkv[:, D:].reshape(rows, HEADS, 2, HEAD_DIM)
    return jnp.concatenate([w_qkv[:, :D], jnp.swapaxes(sides, 1, 2).reshape(rows, 2 * D)], axis=1)


def general_shards(
    hidden_in,
    rand_table,
    norm1_gain,
    norm1_bias,
    w_qkv,
    query_bias,
    value_bias,
    w_out,
    out_bias,
    norm2_gain,
    norm2_bias,
    w_up,
    up_bias,
    w_down,
    down_bias,
    cotangent,
):
    micro, rows, _ = hidden_in.shape
    groups = lax.axis_size("gy")
    local = rows // BLOCK
    own = norm1_gain.shape[0]

    vectors = jnp.concatenate(
        [
            norm1_gain,
            norm1_bias,
            query_bias,
            value_bias,
            out_bias,
            norm2_gain,
            norm2_bias,
            down_bias,
            up_bias,
        ]
    )
    table = lax.all_gather(rand_table, "gy", axis=1, tiled=True)
    table = table.reshape(micro, groups * local * RANDOM)
    vectors = gather(vectors[None]).astype(F32)
    gain_one, shift_one, query_shift, value_shift, out_shift, gain_two, shift_two, down_shift = (
        vectors[:, number * own : (number + 1) * own].reshape(1, D) for number in range(8)
    )
    up_shift = vectors[:, 8 * own :].reshape(1, FF)
    w_qkv_full = gather(by_heads(w_qkv))
    w_out_full, w_up_full, w_down_full = gather(w_out), gather(w_up), gather(w_down)
    packed_bias = by_heads(
        jnp.concatenate([query_shift, jnp.zeros_like(query_shift), value_shift], axis=1)
    )

    normed, send = qkv_forward(hidden_in, gain_one, shift_one, w_qkv_full, packed_bias, groups)
    qkv = exchange(send).reshape(groups, 3, local, BLOCK, LANES)
    mixed, lse = attention_forward(table, qkv)
    mixed_back = exchange(mixed.reshape(groups, rows, LANES))
    hidden_out, grad_send, dres, g_out, g_up, g_down, g_up_bias, g_mid = middle(
        mixed_back,
        hidden_in,
        cotangent.reshape(micro * rows, D),
        w_out_full,
        out_shift,
        gain_two,
        shift_two,
        up_shift,
        down_shift,
        w_up_full,
        w_down_full,
        F32,
    )
    grad_mixed = exchange(grad_send).reshape(groups, local, BLOCK, LANES)
    dqkv = attention_backward(table, qkv, grad_mixed, lse)
    dqkv_back = exchange(dqkv.reshape(groups, 3, rows, LANES))
    grad_hidden, g_qkv, g_packed, g_first = qkv_backward(
        dqkv_back, normed, hidden_in, dres, gain_one, w_qkv_full, F32
    )

    g_packed = by_parts(g_packed)
    small = [
        g_first[0],
        g_first[1],
        g_packed[0, :D],
        g_packed[0, 2 * D :],
        g_mid[3],
        g_mid[0],
        g_mid[1],
        g_mid[2],
    ]
    ranks = D // own
    small = jnp.concatenate(
        [item.reshape(ranks, own) for item in small] + [g_up_bias.reshape(ranks, 4 * own)], axis=1
    )
    small = scatter(small)[0]
    parts = [small[number * own : (number + 1) * own] for number in range(8)]
    return (
        hidden_out,
        grad_hidden,
        parts[0],
        parts[1],
        by_parts(scatter(g_qkv)),
        parts[2],
        parts[3],
        scatter(g_out),
        parts[4],
        parts[5],
        parts[6],
        scatter(g_up),
        small[8 * own :],
        scatter(g_down),
        parts[7],
    )


MESH = pl.DeviceIdType.MESH
ANY = pl.ANY
PLANES = 4
SPOTS = 4
PIECES = 2
RANKS = 2 * PLANES * SPOTS
TILES = 3 * D // LANES
HALF_TILES = TILES // 2
QUERY_ORDER = (0, 2, 3, 5, 6, 8, 9, 11, 1, 4, 7, 10)


def column_order():
    order = [("q", head) for head in QUERY_ORDER]
    for spot in range(SPOTS):
        for place in (2 * 3 * spot, 2 * 3 * spot + 2):
            order += [("k", place // 2), ("v", place // 2)]
        order += [("v", 3 * spot + 2), ("k", 3 * spot + 2)]
    return order


def natural_block(entry):
    return "qkv".index(entry[0]) * HEADS + entry[1]


def take_blocks(array, order):
    parts = []
    start = 0
    while start < len(order):
        stop = start + 1
        while stop < len(order) and order[stop] == order[stop - 1] + 1:
            stop += 1
        parts.append(array[..., order[start] * HEAD_DIM : (order[start] + stop - start) * HEAD_DIM])
        start = stop
    return jnp.concatenate(parts, axis=-1)


def flip(value, bits):
    if bits == 0:
        return value
    if bits == 1:
        return value + 1 - 2 * lax.rem(value, 2)
    if bits == 2:
        return value + 2 - 4 * lax.div(value, 2)
    return 3 - value


def place_here():
    core, rank = lax.axis_index("gx"), lax.axis_index("gy")
    return core, lax.div(rank, SPOTS), lax.rem(rank, SPOTS)


def rank_of(plane, spot):
    return plane * SPOTS + spot


def greet(partners):
    barrier = pltpu.get_barrier_semaphore()
    for partner in partners:
        pl.semaphore_signal(barrier, inc=1, device_id=partner, device_id_type=MESH)
    pl.semaphore_wait(barrier, len(partners))


def remote(source, target, send_sem, recv_sem, device):
    return pltpu.make_async_remote_copy(
        src_ref=source,
        dst_ref=target,
        send_sem=send_sem,
        recv_sem=recv_sem,
        device_id=device,
        device_id_type=MESH,
    )


def column_partners(core, plane, spot):
    partners = [(1 - core, rank_of(plane, spot))]
    for bits in range(1, PLANES):
        for other in (core, 1 - core):
            partners.append((other, rank_of(flip(plane, bits), spot)))
    return partners


def all_partners(core, plane, spot):
    return column_partners(core, plane, spot) + [
        (core, rank_of(plane, flip(spot, 1))),
        (core, rank_of(plane, flip(spot, 2))),
    ]


def to_planes(source, target, send_sem, recv_sem, local_sem):
    core, plane, spot = place_here()
    half, odd = lax.div(plane, 2), lax.rem(plane, 2)
    sends, keeps = [], []
    for micro in range(2):
        goal = 2 * micro + core
        here = (goal == plane) & (half == core)
        send = remote(
            source.at[micro],
            target.at[odd],
            send_sem.at[micro],
            recv_sem.at[odd],
            (half, rank_of(goal, spot)),
        )
        keep = pltpu.make_async_copy(source.at[micro], target.at[odd], local_sem.at[micro])

        @pl.when(jnp.logical_not(here))
        def _(send=send):
            send.start()

        @pl.when(here)
        def _(keep=keep):
            keep.start()

        sends.append((here, send))
        keeps.append((here, keep))

    def finish():
        for piece in range(PIECES):
            mine = (odd == core) & (plane == 2 * core + piece)
            arrival = remote(
                source.at[0],
                target.at[piece],
                send_sem.at[0],
                recv_sem.at[piece],
                (core, rank_of(plane, spot)),
            )

            @pl.when(jnp.logical_not(mine))
            def _(arrival=arrival):
                arrival.wait_recv()

        for (here, send), (_, keep) in zip(sends, keeps):

            @pl.when(jnp.logical_not(here))
            def _(send=send):
                send.wait_send()

            @pl.when(here)
            def _(keep=keep):
                keep.wait()

    return finish


def from_planes(source, target, send_sem, recv_sem, local_sem):
    core, plane, spot = place_here()
    micro, odd = lax.div(plane, 2), lax.rem(plane, 2)
    sends, keeps = [], []
    for piece in range(PIECES):
        goal = 2 * core + piece
        here = (goal == plane) & (odd == core)
        send = remote(
            source.at[piece],
            target.at[micro],
            send_sem.at[piece],
            recv_sem.at[micro],
            (odd, rank_of(goal, spot)),
        )
        keep = pltpu.make_async_copy(source.at[piece], target.at[micro], local_sem.at[piece])

        @pl.when(jnp.logical_not(here))
        def _(send=send):
            send.start()

        @pl.when(here)
        def _(keep=keep):
            keep.start()

        sends.append((here, send))
        keeps.append((here, keep))

    def finish():
        for number in range(2):
            mine = (2 * number + core == plane) & (micro == core)
            arrival = remote(
                source.at[0],
                target.at[number],
                send_sem.at[0],
                recv_sem.at[number],
                (core, rank_of(plane, spot)),
            )

            @pl.when(jnp.logical_not(mine))
            def _(arrival=arrival):
                arrival.wait_recv()

        for (here, send), (_, keep) in zip(sends, keeps):

            @pl.when(jnp.logical_not(here))
            def _(send=send):
                send.wait_send()

            @pl.when(here)
            def _(keep=keep):
                keep.wait()

    return finish


class Gather:
    SENDS = 31

    def __init__(self, source, target, send_sem, recv_sem, local_sem):
        self.source, self.target = source, target
        self.send_sem, self.recv_sem = send_sem, recv_sem
        self.core, self.plane, self.spot = place_here()
        self.sends = []
        self.own = pltpu.make_async_copy(
            source, target.at[self.core, self.plane, self.spot], local_sem
        )
        self.own.start()

    def send(self, source, plane, spot, device):
        copy = remote(
            source,
            self.target.at[self.core, plane, spot],
            self.send_sem.at[len(self.sends)],
            self.recv_sem.at[self.core, plane, spot],
            device,
        )
        copy.start()
        self.sends.append(copy)

    def arrive(self, core, plane, spot):
        shard = self.target.at[core, plane, spot]
        remote(
            shard,
            shard,
            self.send_sem.at[0],
            self.recv_sem.at[core, plane, spot],
            (self.core, rank_of(self.plane, self.spot)),
        ).wait_recv()

    def neighbour(self, bits):
        return (self.core, rank_of(self.plane, flip(self.spot, bits)))

    def sibling(self):
        return (1 - self.core, rank_of(self.plane, self.spot))

    def start(self):
        for bits in range(1, PLANES):
            goal = (self.core, rank_of(flip(self.plane, bits), self.spot))
            self.send(self.source, self.plane, self.spot, goal)
        for goal in (self.neighbour(1), self.neighbour(2), self.sibling()):
            self.send(self.source, self.plane, self.spot, goal)

    def column(self):
        for bits in range(1, PLANES):
            plane = flip(self.plane, bits)
            self.arrive(self.core, plane, self.spot)
            shard = self.target.at[self.core, plane, self.spot]
            for goal in (self.neighbour(1), self.neighbour(2), self.sibling()):
                self.send(shard, plane, self.spot, goal)

    def across(self):
        for bits in range(PLANES):
            plane = flip(self.plane, bits)
            for side in (1, 2):
                spot = flip(self.spot, side)
                self.arrive(self.core, plane, spot)
                shard = self.target.at[self.core, plane, spot]
                if (side == 1) == (bits < 2):
                    self.send(shard, plane, spot, self.neighbour(3 - side))
                self.send(shard, plane, spot, self.sibling())

    def corner(self):
        spot = flip(self.spot, 3)
        for bits in range(PLANES):
            plane = flip(self.plane, bits)
            self.arrive(self.core, plane, spot)
            self.send(self.target.at[self.core, plane, spot], plane, spot, self.sibling())

    def finish(self):
        for bits in range(PLANES):
            for side in range(SPOTS):
                self.arrive(1 - self.core, flip(self.plane, bits), flip(self.spot, side))
        self.own.wait()
        for copy in self.sends:
            copy.wait_send()


def settle(shards_ref, plan):
    rows = shards_ref.shape[3] // 2

    def pair(number, carry):
        core, plane, side = (
            lax.div(number, 2 * PLANES),
            lax.rem(lax.div(number, 2), PLANES),
            lax.rem(number, 2),
        )
        goal = pl.ds(pl.multiple_of(number * 2 * rows, 16), 2 * rows)
        for tile, out_ref, (left, right) in plan:
            columns = slice(tile * LANES, (tile + 1) * LANES)
            first = shards_ref[core, plane, 2 * side, :, columns].astype(F32)
            second = shards_ref[core, plane, 2 * side + 1, :, columns].astype(F32)
            out_ref[goal, left * LANES : (left + 1) * LANES] = jnp.concatenate(
                [first[:rows], second[:rows]], axis=0
            ).astype(BF16)
            out_ref[goal, right * LANES : (right + 1) * LANES] = jnp.concatenate(
                [first[rows:], second[rows:]], axis=0
            ).astype(BF16)
        return carry

    lax.fori_loop(0, RANKS // 2, pair, 0)


def alternate(tile):
    return 2 * tile, 2 * tile + 1


def collect_kernel(
    x_ref,
    vec_ref,
    s_qkv_ref,
    xs_ref,
    vecs_ref,
    w_qkv_ref,
    g_qkv_ref,
    send_sem,
    recv_sem,
    local_sem,
    move_send,
    move_recv,
    move_local,
):
    core, plane, spot = place_here()
    greet(all_partners(core, plane, spot))
    gathers = []
    for number, (source, target) in enumerate(((vec_ref, vecs_ref), (s_qkv_ref, g_qkv_ref))):
        one = Gather(
            source, target, send_sem.at[number], recv_sem.at[number], local_sem.at[number]
        )
        one.start()
        gathers.append(one)
    finish_x = to_planes(x_ref, xs_ref, move_send, move_recv, move_local)
    for one in gathers:
        one.column()
    for one in gathers:
        one.across()
    for one in gathers:
        one.corner()
    for one in gathers:
        one.finish()
    settle(g_qkv_ref, [(tile, w_qkv_ref, alternate(tile)) for tile in range(HALF_TILES)])
    finish_x()


def collect(x, vec, s_qkv):
    grid = (2, PLANES, SPOTS)
    return pl.pallas_call(
        collect_kernel,
        out_shape=(
            jax.ShapeDtypeStruct(x.shape, BF16),
            jax.ShapeDtypeStruct(grid + vec.shape, BF16),
            jax.ShapeDtypeStruct((D, 3 * D), BF16),
        ),
        in_specs=[whole(ANY)] * 3,
        out_specs=(whole(ANY), whole(ANY), whole()),
        scratch_shapes=[
            VMEM(grid + s_qkv.shape, BF16),
            pltpu.SemaphoreType.DMA((2, Gather.SENDS)),
            pltpu.SemaphoreType.DMA((2,) + grid),
            pltpu.SemaphoreType.DMA((2,)),
            pltpu.SemaphoreType.DMA((2,)),
            pltpu.SemaphoreType.DMA((2,)),
            pltpu.SemaphoreType.DMA((2,)),
        ],
        compiler_params=pltpu.CompilerParams(
            vmem_limit_bytes=48 * 1024 * 1024, collective_id=1, has_side_effects=True
        ),
        name="collect",
    )(x, vec, s_qkv)


def plane_partners(core, plane, spot):
    partners = []
    for other in (core, 1 - core):
        for side in range(SPOTS):
            if other is core and side == 0:
                continue
            partners.append((other, rank_of(plane, flip(spot, side))))
    return partners


def both_partners(core, plane, spot):
    return plane_partners(core, plane, spot) + column_partners(core, plane, spot)[1:]


def outward_send(source_ref, target_ref, send_sem, recv_sem, local_sem):
    core, plane, spot = place_here()
    sends, keeps = [], []
    for side in (3, 1, 2, 0):
        for other in (core, 1 - core):
            goal = flip(spot, side)
            for piece in range(PIECES):
                source = source_ref.at[other, goal, piece]
                target = target_ref.at[2 * core + piece, spot]
                if side == 0 and other is core:
                    copy = pltpu.make_async_copy(source, target, local_sem.at[piece])
                    keeps.append(copy)
                else:
                    copy = remote(
                        source,
                        target,
                        send_sem.at[len(sends)],
                        recv_sem.at[2 * core + piece, spot],
                        (other, rank_of(plane, goal)),
                    )
                    sends.append(copy)
                copy.start()

    def finish():
        for side in range(SPOTS):
            for other in (core, 1 - core):
                if side == 0 and other is core:
                    continue
                for piece in range(PIECES):
                    target = target_ref.at[2 * other + piece, flip(spot, side)]
                    remote(
                        target,
                        target,
                        send_sem.at[0],
                        recv_sem.at[2 * other + piece, flip(spot, side)],
                        (core, rank_of(plane, spot)),
                    ).wait_recv()
        for copy in sends:
            copy.wait_send()
        for copy in keeps:
            copy.wait()

    return finish


def inward_send(source_ref, target_ref, send_sem, recv_sem, local_sem):
    core, plane, spot = place_here()
    sends, keeps = [], []
    for side in (3, 1, 2, 0):
        for other in (core, 1 - core):
            goal = flip(spot, side)
            for piece in range(PIECES):
                source = source_ref.at[2 * other + piece, goal]
                target = target_ref.at[core, spot, piece]
                if side == 0 and other is core:
                    copy = pltpu.make_async_copy(source, target, local_sem.at[piece])
                    keeps.append(copy)
                else:
                    copy = remote(
                        source,
                        target,
                        send_sem.at[len(sends)],
                        recv_sem.at[core, spot, piece],
                        (other, rank_of(plane, goal)),
                    )
                    sends.append(copy)
                copy.start()

    def finish():
        for side in range(SPOTS):
            for other in (core, 1 - core):
                if side == 0 and other is core:
                    continue
                for piece in range(PIECES):
                    target = target_ref.at[other, flip(spot, side), piece]
                    remote(
                        target,
                        target,
                        send_sem.at[0],
                        recv_sem.at[other, flip(spot, side), piece],
                        (core, rank_of(plane, spot)),
                    ).wait_recv()
        for copy in sends:
            copy.wait_send()
        for copy in keeps:
            copy.wait()

    return finish


def exchange_sems(recv_shape):
    return [
        pltpu.SemaphoreType.DMA((14,)),
        pltpu.SemaphoreType.DMA(recv_shape),
        pltpu.SemaphoreType.DMA((PIECES,)),
    ]


def outward_kernel(source_ref, target_ref, send_sem, recv_sem, local_sem):
    greet(plane_partners(*place_here()))
    outward_send(source_ref, target_ref, send_sem, recv_sem, local_sem)()


def inward_kernel(source_ref, target_ref, send_sem, recv_sem, local_sem):
    greet(plane_partners(*place_here()))
    inward_send(source_ref, target_ref, send_sem, recv_sem, local_sem)()


def plane_exchange(kernel, source, shape, recv_shape, collective, name):
    return pl.pallas_call(
        kernel,
        out_shape=jax.ShapeDtypeStruct(shape, source.dtype),
        in_specs=[whole(ANY)],
        out_specs=whole(ANY),
        scratch_shapes=exchange_sems(recv_shape),
        compiler_params=pltpu.CompilerParams(
            vmem_limit_bytes=16 * 1024 * 1024, collective_id=collective, has_side_effects=True
        ),
        name=name,
    )(source)


def outward(source, collective, name):
    shape = (PLANES, SPOTS) + source.shape[3:]
    return plane_exchange(outward_kernel, source, shape, (PLANES, SPOTS), collective, name)


def inward(source, collective, name):
    shape = (2, SPOTS, PIECES) + source.shape[2:]
    return plane_exchange(
        inward_kernel, source, shape, (2, SPOTS, PIECES), collective, name
    )


def column_send(source, target, send_sem, recv_sem, local_sem):
    core, plane, spot = place_here()
    keep = pltpu.make_async_copy(source, target.at[plane], local_sem)
    keep.start()
    copies = []
    for bits in range(1, PLANES):
        copy = remote(
            source,
            target.at[plane],
            send_sem.at[bits - 1],
            recv_sem.at[plane],
            (core, rank_of(flip(plane, bits), spot)),
        )
        copy.start()
        copies.append(copy)

    def finish():
        for bits in range(1, PLANES):
            other = flip(plane, bits)
            remote(
                source,
                target.at[other],
                send_sem.at[0],
                recv_sem.at[other],
                (core, rank_of(plane, spot)),
            ).wait_recv()
        for copy in copies:
            copy.wait_send()
        keep.wait()

    return finish


def exchange_qkv_kernel(
    source_ref,
    s_ou_ref,
    s_down_ref,
    target_ref,
    c_ou_ref,
    c_down_ref,
    send_sem,
    recv_sem,
    local_sem,
    column_send_sem,
    column_recv_sem,
    column_local_sem,
):
    greet(both_partners(*place_here()))
    finish = outward_send(source_ref, target_ref, send_sem, recv_sem, local_sem)
    finishes = [
        column_send(
            source,
            target,
            column_send_sem.at[number],
            column_recv_sem.at[number],
            column_local_sem.at[number],
        )
        for number, (source, target) in enumerate(
            ((s_ou_ref, c_ou_ref), (s_down_ref, c_down_ref))
        )
    ]
    finish()
    for one in finishes:
        one()


def exchange_qkv(source, s_ou, s_down):
    return pl.pallas_call(
        exchange_qkv_kernel,
        out_shape=(
            jax.ShapeDtypeStruct((PLANES, SPOTS) + source.shape[3:], BF16),
            jax.ShapeDtypeStruct((PLANES,) + s_ou.shape, BF16),
            jax.ShapeDtypeStruct((PLANES,) + s_down.shape, BF16),
        ),
        in_specs=[whole(ANY)] * 3,
        out_specs=(whole(ANY),) * 3,
        scratch_shapes=exchange_sems((PLANES, SPOTS))
        + [
            pltpu.SemaphoreType.DMA((2, PLANES - 1)),
            pltpu.SemaphoreType.DMA((2, PLANES)),
            pltpu.SemaphoreType.DMA((2,)),
        ],
        compiler_params=pltpu.CompilerParams(
            vmem_limit_bytes=16 * 1024 * 1024, collective_id=3, has_side_effects=True
        ),
        name="exchange_qkv",
    )(source, s_ou, s_down)


class PlaneGather:
    SENDS = 3 + 4 + 2

    def __init__(self, column, target, send_sem, recv_sem, local_sem):
        self.column, self.target = column, target
        self.send_sem, self.recv_sem = send_sem, recv_sem
        self.core, self.plane, self.spot = place_here()
        self.sends = []
        self.own = pltpu.make_async_copy(column, target.at[self.core, :, self.spot], local_sem)
        self.own.start()
        for goal in (self.neighbour(1), self.neighbour(2), self.sibling()):
            self.send(column, slice(0, PLANES), self.spot, 0, goal)

    def neighbour(self, bits):
        return (self.core, rank_of(self.plane, flip(self.spot, bits)))

    def sibling(self):
        return (1 - self.core, rank_of(self.plane, self.spot))

    def piece(self, core, planes, spot):
        return self.target.at[core, planes, spot]

    def send(self, source, planes, spot, part, goal):
        copy = remote(
            source,
            self.piece(self.core, planes, spot),
            self.send_sem.at[len(self.sends)],
            self.recv_sem.at[self.core, spot, part],
            goal,
        )
        copy.start()
        self.sends.append(copy)

    def arrive(self, core, planes, spot, part):
        piece = self.piece(core, planes, spot)
        remote(
            piece,
            piece,
            self.send_sem.at[0],
            self.recv_sem.at[core, spot, part],
            (self.core, rank_of(self.plane, self.spot)),
        ).wait_recv()

    def forward(self):
        for side in (1, 2):
            spot = flip(self.spot, side)
            everything = slice(0, PLANES)
            self.arrive(self.core, everything, spot, 0)
            half = slice(0, 2) if side == 1 else slice(2, 4)
            self.send(
                self.piece(self.core, half, spot), half, spot, side - 1, self.neighbour(3 - side)
            )
            self.send(self.piece(self.core, everything, spot), everything, spot, 0, self.sibling())

    def corner(self):
        spot = flip(self.spot, 3)
        for part, half in enumerate((slice(0, 2), slice(2, 4))):
            self.arrive(self.core, half, spot, part)
            self.send(self.piece(self.core, half, spot), half, spot, part, self.sibling())

    def finish(self):
        for side in range(3):
            self.arrive(1 - self.core, slice(0, PLANES), flip(self.spot, side), 0)
        for part, half in enumerate((slice(0, 2), slice(2, 4))):
            self.arrive(1 - self.core, half, flip(self.spot, 3), part)
        self.own.wait()
        for copy in self.sends:
            copy.wait_send()


def sort_entries(table_ref, sorted_ref):
    count = table_ref.shape[1]
    along = jnp.broadcast_to(table_ref[...].astype(F32), (count, count))
    down = along.T
    lane = lax.broadcasted_iota(jnp.int32, (count, count), 1).astype(F32)
    row = lax.broadcasted_iota(jnp.int32, (count, count), 0).astype(F32)
    before = (along < down) | ((along == down) & (lane < row))
    rank = jnp.sum(jnp.where(before, 1.0, 0.0), axis=1, keepdims=True)
    sorted_ref[0:1] = jnp.sum(jnp.where(rank == lane, row, 0.0), axis=0, keepdims=True).astype(
        jnp.int32
    )
    sorted_ref[1:2] = jnp.sum(jnp.where(down <= lane, 1.0, 0.0), axis=0, keepdims=True).astype(
        jnp.int32
    )


def plane_qkv_kernel(
    x_ref, vec_ref, w_ref, bias_ref, table_ref, normed_ref, send_ref, sorted_ref
):
    sort_entries(table_ref, sorted_ref)
    pieces, rows, _ = x_ref.shape
    values = x_ref[...].reshape(pieces * rows, D).astype(F32)
    normal, _ = norm_parts(values)
    normed_ref[...] = (normal * vec_ref[0:1] + vec_ref[1:2]).astype(BF16)
    low = low_lanes(rows)
    queries = D // LANES
    for chunk in range(HALF_TILES):
        columns = slice(chunk * CHUNK, (chunk + 1) * CHUNK)
        packed = dot(normed_ref[...], w_ref[:, columns]) + bias_ref[:, columns]
        for side in range(2):
            tile = chunk + side * HALF_TILES
            whole_tile = packed[:, side * LANES : (side + 1) * LANES]
            if tile < queries:
                whole_tile = whole_tile.astype(BF16).astype(F32) * SCALE
            for piece in range(pieces):
                part = whole_tile[piece * rows : (piece + 1) * rows]
                if tile < SPOTS:
                    send_ref[0, tile, piece, 0] = part.astype(BF16)
                elif tile < queries:
                    first = 2 * (tile - SPOTS)
                    shared = send_ref[0, first, piece, 0].astype(F32)
                    send_ref[1, first, piece, 0] = jnp.where(low, part, shared).astype(BF16)
                    shared = send_ref[0, first + 1, piece, 0].astype(F32)
                    send_ref[1, first + 1, piece, 0] = jnp.where(
                        low, swap_halves(part), shared
                    ).astype(BF16)
                else:
                    spot, role = (tile - queries) // 3, (tile - queries) % 3
                    if role < 2:
                        send_ref[role, spot, piece, 1] = part.astype(BF16)
                    else:
                        send_ref[0, spot, piece, 2] = part.astype(BF16)
                        send_ref[1, spot, piece, 2] = part.astype(BF16)


def plane_qkv(x, vec, w, bias, table):
    pieces, rows, _ = x.shape
    return pl.pallas_call(
        plane_qkv_kernel,
        out_shape=(
            jax.ShapeDtypeStruct((pieces * rows, D), BF16),
            jax.ShapeDtypeStruct((2, SPOTS, PIECES, 3, rows, LANES), BF16),
            jax.ShapeDtypeStruct((2, table.shape[1]), jnp.int32),
        ),
        in_specs=[whole()] * 5,
        out_specs=(whole(), whole(), whole()),
        compiler_params=params_of(48),
        name="plane_qkv",
    )(x, vec, w, bias, table)


def plane_attend_kernel(
    table_ref,
    qkv_ref,
    dy_ref,
    c_ou_ref,
    c_down_ref,
    back_ref,
    lse_ref,
    dys_ref,
    w_out_ref,
    w_up_ref,
    w_down_ref,
    g_ou_ref,
    out_ref,
    s_ref,
    t_ref,
    send_sem,
    recv_sem,
    local_sem,
    gather_send,
    gather_recv,
    gather_local,
    move_send,
    move_recv,
    move_local,
):
    greet(both_partners(*place_here()))
    gathers = [
        PlaneGather(
            column,
            target,
            gather_send.at[number],
            gather_recv.at[number],
            gather_local.at[number],
        )
        for number, (column, target) in enumerate(
            ((c_ou_ref, g_ou_ref), (c_down_ref, w_down_ref))
        )
    ]
    finish_dy = to_planes(dy_ref, dys_ref, move_send, move_recv, move_local)
    groups, _, local, _, _ = qkv_ref.shape
    blocks = groups * local
    half = blocks // 2
    core = lax.axis_index("gx")
    low = low_lanes(BLOCK)
    masks = [half_mask(True), half_mask(False)]

    def load(component, block):
        return qkv_ref[lax.div(block, local), component, lax.rem(block, local)]

    def store(block, value):
        rank = lax.div(block, local)
        out_ref[lax.div(rank, SPOTS), lax.rem(rank, SPOTS), lax.rem(block, local)] = value.astype(BF16)

    def one(block, slot, ids, bias):
        keys = jnp.concatenate([load(1 + slot, spot) for spot in ids], axis=0)
        scores = dot_rt(load(0, block) * masks[slot], keys) + bias
        top = jnp.max(scores, axis=1, keepdims=True)
        powered = jnp.exp(scores - top)
        total = jnp.sum(powered, axis=1, keepdims=True)
        mixed = dot(powered.astype(BF16), keys) * (1.0 / total)
        return mixed, top + jnp.log(total)

    def sparse(step, carry):
        mine = 1 + step + core * (half - 1)
        other = 1 + step + (1 - core) * (half - 1)
        ids, bias = slots_of(table_ref, 0, mine, blocks)
        far_ids, far_bias = slots_of(table_ref, 0, other, blocks)
        mixed_a, log_a = one(mine, 0, ids, bias)
        mixed_b, log_b = one(mine, 1, ids, bias)
        mixed_c, log_c = one(other, 0, far_ids, far_bias)
        store(mine, jnp.where(low, mixed_b, mixed_a))
        store(other, mixed_c)
        lse_ref[mine] = jnp.where(low, log_a, log_b)
        lse_ref[other] = jnp.where(low, log_c, 0.0)
        return carry

    lax.fori_loop(0, half // 2, sparse, 0)
    gathers[0].forward()
    lax.fori_loop(half // 2, half - 1, sparse, 0)

    spans = blocks // SPAN
    ends = (0, blocks - 1)
    end = core * (blocks - 1)
    query_a = jnp.concatenate([load(0, number) for number in ends], axis=0) * masks[0]
    query_b = load(0, end) * masks[1]

    def keys_at(span, slot):
        return jnp.concatenate(
            [load(1 + slot, span * SPAN + number) for number in range(SPAN)], axis=0
        )

    def first_pass(span, carry):
        top_a, top_b = carry
        scores_a = dot_rt(query_a, keys_at(span, 0))
        scores_b = dot_rt(query_b, keys_at(span, 1))
        s_ref[span] = scores_a
        t_ref[span] = scores_b
        return (
            jnp.maximum(top_a, jnp.max(scores_a, axis=1, keepdims=True)),
            jnp.maximum(top_b, jnp.max(scores_b, axis=1, keepdims=True)),
        )

    top_a, top_b = lax.fori_loop(
        0,
        spans,
        first_pass,
        (jnp.full((2 * BLOCK, 1), NEGATIVE, F32), jnp.full((BLOCK, 1), NEGATIVE, F32)),
    )

    def second_pass(span, carry):
        total_a, mixed_a, total_b, mixed_b = carry
        powered_a = jnp.exp(s_ref[span] - top_a)
        powered_b = jnp.exp(t_ref[span] - top_b)
        return (
            total_a + jnp.sum(powered_a, axis=1, keepdims=True),
            mixed_a + dot(powered_a.astype(BF16), keys_at(span, 0)),
            total_b + jnp.sum(powered_b, axis=1, keepdims=True),
            mixed_b + dot(powered_b.astype(BF16), keys_at(span, 1)),
        )

    total_a, mixed_a, total_b, mixed_b = lax.fori_loop(
        0,
        spans,
        second_pass,
        (
            jnp.zeros((2 * BLOCK, 1), F32),
            jnp.zeros((2 * BLOCK, LANES), F32),
            jnp.zeros((BLOCK, 1), F32),
            jnp.zeros((BLOCK, LANES), F32),
        ),
    )
    mixed_a = mixed_a * (1.0 / total_a)
    mixed_b = mixed_b * (1.0 / total_b)
    log_a = top_a + jnp.log(total_a)
    log_b = top_b + jnp.log(total_b)
    for place, number in enumerate(ends):
        rows = slice(place * BLOCK, (place + 1) * BLOCK)
        store(number, jnp.where(low, mixed_b, mixed_a[rows]))
        lse_ref[number] = jnp.where(low, log_a[rows], log_b)

    gathers[1].forward()
    finish_mixed = inward_send(out_ref, back_ref, send_sem, recv_sem, local_sem)
    gathers[0].corner()
    gathers[0].finish()
    outs = D // LANES // 2
    settle(
        g_ou_ref,
        [(tile, w_out_ref, (tile, outs + tile)) for tile in range(outs)]
        + [(outs + tile, w_up_ref, alternate(tile)) for tile in range(FF // CHUNK)],
    )
    gathers[1].corner()
    gathers[1].finish()
    finish_dy()
    finish_mixed()


def plane_attention(table, qkv, dy, c_ou, c_down):
    groups, _, local, _, _ = qkv.shape
    blocks = groups * local
    spans = blocks // SPAN
    grid = (2, PLANES, SPOTS)
    tile = (local, BLOCK, LANES)
    return pl.pallas_call(
        plane_attend_kernel,
        out_shape=(
            jax.ShapeDtypeStruct((2, SPOTS, PIECES) + tile, BF16),
            jax.ShapeDtypeStruct((blocks, BLOCK, LANES), F32),
            jax.ShapeDtypeStruct(dy.shape, BF16),
            jax.ShapeDtypeStruct((D, D), BF16),
            jax.ShapeDtypeStruct((D, FF), BF16),
            jax.ShapeDtypeStruct(grid + c_down.shape[1:], BF16),
        ),
        in_specs=[whole(pltpu.SMEM), whole(), whole(ANY), whole(ANY), whole(ANY)],
        out_specs=(whole(ANY), whole(), whole(ANY), whole(), whole(), whole(ANY)),
        scratch_shapes=[
            VMEM(grid + c_ou.shape[1:], BF16),
            VMEM((PLANES, SPOTS) + tile, BF16),
            VMEM((spans, 2 * BLOCK, SPAN * BLOCK), F32),
            VMEM((spans, BLOCK, SPAN * BLOCK), F32),
        ]
        + exchange_sems((2, SPOTS, PIECES))
        + [
            pltpu.SemaphoreType.DMA((2, PlaneGather.SENDS)),
            pltpu.SemaphoreType.DMA((2, 2, SPOTS, 2)),
            pltpu.SemaphoreType.DMA((2,)),
            pltpu.SemaphoreType.DMA((2,)),
            pltpu.SemaphoreType.DMA((2,)),
            pltpu.SemaphoreType.DMA((2,)),
        ],
        compiler_params=pltpu.CompilerParams(
            vmem_limit_bytes=56 * 1024 * 1024, collective_id=4, has_side_effects=True
        ),
        name="plane_attention",
    )(table, qkv, dy, c_ou, c_down)


def inward_targets(core, spot):
    for side in (3, 1, 2, 0):
        for other in (core, 1 - core):
            yield side, other, flip(spot, side), side == 0 and other is core


class Inward:
    def __init__(self, source, target, send_sem, recv_sem, local_sem):
        self.source, self.target = source, target
        self.send_sem, self.recv_sem, self.local_sem = send_sem, recv_sem, local_sem
        self.core, self.plane, self.spot = place_here()
        self.sends, self.keeps = [], []

    def send(self, other, goal, stays, piece, part, parts):
        source = self.source.at[2 * other + piece, goal, parts]
        target = self.target.at[self.core, self.spot, piece, parts]
        if stays:
            copy = pltpu.make_async_copy(source, target, self.local_sem.at[part, piece])
            self.keeps.append(copy)
        else:
            copy = remote(
                source,
                target,
                self.send_sem.at[len(self.sends)],
                self.recv_sem.at[self.core, self.spot, piece, part],
                (other, rank_of(self.plane, goal)),
            )
            self.sends.append(copy)
        copy.start()

    def finish(self, widths):
        for side, other, goal, stays in inward_targets(self.core, self.spot):
            if stays:
                continue
            for piece in range(PIECES):
                for part, parts in enumerate(widths):
                    target = self.target.at[other, goal, piece, parts]
                    remote(
                        target,
                        target,
                        self.send_sem.at[0],
                        self.recv_sem.at[other, goal, piece, part],
                        (self.core, rank_of(self.plane, self.spot)),
                    ).wait_recv()
        for copy in self.sends:
            copy.wait_send()
        for copy in self.keeps:
            copy.wait()


def plane_attend_back_kernel(count, *refs):
    table_ref, sorted_ref, qkv_ref, grad_source_ref, lse_ref, hidden_ref = refs[:6]
    sources, refs = refs[6 : 6 + count], refs[6 + count :]
    back_ref, hidden_out_ref = refs[:2]
    outs, refs = refs[2 : 2 + count], refs[2 + count :]
    buffers, refs = refs[: 7 * count], refs[7 * count :]
    grad_ref, out_ref, sums_ref, shares_ref, walked_ref = refs[:5]
    reduce_send, reduce_recv, reduce_local = refs[5:8]
    grad_sems, back_sems, move_sems = refs[8:11], refs[11:14], refs[14:17]

    groups, _, local, _, _ = qkv_ref.shape
    blocks = groups * local
    half = blocks // 2
    core, plane, spot = place_here()
    low = low_lanes(BLOCK)
    masks = [half_mask(True), half_mask(False)]

    greet(both_partners(core, plane, spot))
    finish_grad = outward_send(grad_source_ref, grad_ref, *grad_sems)
    reduces = [
        Reduce(
            source,
            *buffers[7 * number : 7 * number + 7],
            out,
            (reduce_send.at[number], reduce_recv.at[number], reduce_local.at[number]),
        )
        for number, (source, out) in enumerate(zip(sources, outs))
    ]
    for one in reduces:
        one.start()
    finish_hidden = from_planes(hidden_ref, hidden_out_ref, *move_sems)

    def load(component, block):
        return qkv_ref[lax.div(block, local), component, lax.rem(block, local)]

    def load_grad(block):
        rank = lax.div(block, local)
        return grad_ref[lax.div(rank, SPOTS), lax.rem(rank, SPOTS), lax.rem(block, local)]

    def store(component, block, value):
        rank = lax.div(block, local)
        out_ref[
            lax.div(rank, SPOTS), lax.rem(rank, SPOTS), component, lax.rem(block, local)
        ] = value.astype(BF16)

    nothing = jnp.zeros((BLOCK, LANES), F32)

    def clear(block, carry):
        for slot in range(2):
            sums_ref[slot, block] = nothing
        return carry

    lax.fori_loop(0, blocks, clear, 0)
    finish_grad()

    spans = blocks // SPAN
    ends = (0, blocks - 1)
    end = core * (blocks - 1)
    both_a = jnp.concatenate(
        [load(0, number) * masks[0] for number in ends]
        + [load_grad(number) * masks[1] for number in ends],
        axis=0,
    )
    both_b = jnp.concatenate([load(0, end) * masks[1], load_grad(end) * masks[0]], axis=0)
    logs_a = jnp.concatenate([lse_ref[number][:, 0:1] for number in ends], axis=0)
    logs_b = lse_ref[end][:, HEAD_DIM : HEAD_DIM + 1]
    wide = SPAN * BLOCK // LANES
    sides = ((0, both_a, logs_a), (1, both_b, logs_b))

    def keys_at(span, slot):
        return jnp.concatenate(
            [load(1 + slot, span * SPAN + number) for number in range(SPAN)], axis=0
        )

    def put(slot, first, value):
        for piece in range(value.shape[0] // BLOCK):
            for column in range(wide):
                shares_ref[slot, first + piece * wide + column] = value[
                    piece * BLOCK : (piece + 1) * BLOCK, column * LANES : (column + 1) * LANES
                ]

    def get(slot, first, pieces):
        return jnp.concatenate(
            [
                jnp.concatenate(
                    [shares_ref[slot, first + piece * wide + column] for column in range(wide)],
                    axis=1,
                )
                for piece in range(pieces)
            ],
            axis=0,
        )

    def first_pass(span, carry):
        deltas = []
        for slot, both, logs in sides:
            rows = both.shape[0] // 2
            size = rows // BLOCK * wide
            products = dot_rt(both, keys_at(span, slot))
            weights = jnp.exp(products[:rows] - logs)
            grad_weights = products[rows:]
            put(slot, span * size, weights)
            put(slot, (spans + span) * size, grad_weights)
            deltas.append(carry[slot] + jnp.sum(weights * grad_weights, axis=1, keepdims=True))
        return tuple(deltas)

    deltas = lax.fori_loop(
        0, spans, first_pass, (jnp.zeros((2 * BLOCK, 1), F32), jnp.zeros((BLOCK, 1), F32))
    )

    def second_pass(span, carry):
        totals = []
        for slot, both, logs in sides:
            rows = both.shape[0] // 2
            size = rows // BLOCK * wide
            weights = get(slot, span * size, rows // BLOCK)
            grad_scores = weights * (
                get(slot, (spans + span) * size, rows // BLOCK) - deltas[slot]
            )
            stacked = jnp.concatenate([grad_scores, weights], axis=0).astype(BF16)
            shares = dot_lt(stacked, both)
            for number in range(SPAN):
                sums_ref[slot, span * SPAN + number] += shares[
                    number * BLOCK : (number + 1) * BLOCK
                ]
            totals.append(carry[slot] + dot(stacked[:rows], keys_at(span, slot)))
        return tuple(totals)

    query_a, query_b = lax.fori_loop(
        0,
        spans,
        second_pass,
        (jnp.zeros((2 * BLOCK, LANES), F32), nothing),
    )
    for place, number in enumerate(ends):
        rows = slice(place * BLOCK, (place + 1) * BLOCK)
        store(0, number, jnp.where(low, query_a[rows], query_b) * SCALE)
        for slot in range(2):
            for pick in range(RANDOM):
                shares_ref[slot, number * RANDOM + pick] = nothing

    for one in reduces:
        one.corners()

    def one_block(block, slot, ids, bias):
        keys = jnp.concatenate([load(1 + slot, number) for number in ids], axis=0)
        both = jnp.concatenate(
            [load(0, block) * masks[slot], load_grad(block) * masks[1 - slot]], axis=0
        )
        products = dot_rt(both, keys)
        logs = lse_ref[block][:, slot * HEAD_DIM : slot * HEAD_DIM + 1]
        weights = jnp.exp(products[:BLOCK] + bias - logs)
        grad_weights = products[BLOCK:]
        delta = jnp.sum(weights * grad_weights, axis=1, keepdims=True)
        grad_scores = weights * (grad_weights - delta)
        stacked = jnp.concatenate([grad_scores, weights], axis=0).astype(BF16)
        return dot(stacked[:BLOCK], keys), dot_lt(stacked, both)

    def add(block, slot, shares):
        fixed = (block - 1, block, block + 1, 0, blocks - 1)
        for place, number in enumerate(fixed):
            sums_ref[slot, number] += shares[place * BLOCK : (place + 1) * BLOCK]
        for pick in range(RANDOM):
            place = len(fixed) + pick
            shares_ref[slot, block * RANDOM + pick] = shares[
                place * BLOCK : (place + 1) * BLOCK
            ]

    def sparse(step, carry):
        mine = 1 + step + core * (half - 1)
        other = 1 + step + (1 - core) * (half - 1)
        ids, bias = slots_of(table_ref, 0, mine, blocks)
        far_ids, far_bias = slots_of(table_ref, 0, other, blocks)
        query_a, shares_a = one_block(mine, 0, ids, bias)
        query_b, shares_b = one_block(mine, 1, ids, bias)
        query_c, shares_c = one_block(other, 0, far_ids, far_bias)
        store(0, mine, jnp.where(low, query_a, query_b) * SCALE)
        store(0, other, query_c * SCALE)
        add(mine, 0, shares_a)
        add(mine, 1, shares_b)
        add(other, 0, shares_c)
        for pick in range(RANDOM):
            shares_ref[1, other * RANDOM + pick] = nothing
        return carry

    back = Inward(out_ref, back_ref, *back_sems)
    widths = (slice(0, 1), slice(1, 3))

    def send_queries(piece):
        for side, other, goal, stays in inward_targets(core, spot):
            back.send(other, goal, stays, piece, 0, widths[0])

    lax.fori_loop(0, half // 2, sparse, 0)
    for one in reduces:
        one.sides()
    send_queries(0)
    lax.fori_loop(half // 2, half - 1, sparse, 0)
    send_queries(1)
    for one in reduces:
        one.columns()

    def walk(number, carry):
        entry = sorted_ref[0, number]
        earlier = sorted_ref[0, jnp.maximum(number - 1, 0)]
        keep = jnp.where(table_ref[0, entry] == table_ref[0, earlier], 1.0, 0.0).astype(F32)
        totals = []
        for slot in range(2):
            total = carry[slot] * keep + shares_ref[slot, entry]
            walked_ref[slot, number] = total.astype(BF16)
            totals.append(total)
        return tuple(totals)

    lax.fori_loop(0, blocks * RANDOM, walk, (nothing, nothing))

    for side, other, goal, stays in inward_targets(core, spot):
        for piece in range(PIECES):
            first = ((2 * other + piece) * SPOTS + goal) * local

            def close(number, carry, first=first):
                block = first + number
                stop = sorted_ref[1, block]
                start = jnp.where(block == 0, 0, sorted_ref[1, jnp.maximum(block - 1, 0)])
                some = jnp.where(stop > start, 1.0, 0.0).astype(F32)
                for slot in range(2):
                    share = walked_ref[slot, jnp.maximum(stop - 1, 0)].astype(F32)
                    store(1 + slot, block, sums_ref[slot, block] + share * some)
                return carry

            lax.fori_loop(0, local, close, 0)
            back.send(other, goal, stays, piece, 1, widths[1])

    for one in reduces:
        one.finish()
    finish_hidden()
    back.finish(widths)


def plane_attention_back(table, sorted_table, qkv, grad_source, lse, hidden, sources):
    groups, _, local, _, _ = qkv.shape
    blocks = groups * local
    count = len(sources)
    buffers = []
    for source in sources:
        buffers += reduce_scratch(source.shape, source.dtype)
    tile = (local, BLOCK, LANES)
    dma = pltpu.SemaphoreType.DMA
    return pl.pallas_call(
        functools.partial(plane_attend_back_kernel, count),
        out_shape=(
            jax.ShapeDtypeStruct((2, SPOTS, PIECES, 3) + tile, BF16),
            jax.ShapeDtypeStruct(hidden.shape, BF16),
        )
        + tuple(jax.ShapeDtypeStruct(source.shape[3:], F32) for source in sources),
        in_specs=[
            whole(pltpu.SMEM),
            whole(pltpu.SMEM),
            whole(),
            whole(ANY),
            whole(),
            whole(ANY),
        ]
        + [whole(ANY)] * count,
        out_specs=(whole(ANY), whole(ANY)) + (whole(),) * count,
        scratch_shapes=buffers
        + [
            VMEM((PLANES, SPOTS) + tile, BF16),
            VMEM((PLANES, SPOTS, 3) + tile, BF16),
            VMEM((2, blocks, BLOCK, LANES), F32),
            VMEM((2, blocks * RANDOM, BLOCK, LANES), F32),
            VMEM((2, blocks * RANDOM, BLOCK, LANES), BF16),
            dma((count, REDUCE_SEMS)),
            dma((count, REDUCE_SEMS)),
            dma((count, 4)),
        ]
        + exchange_sems((PLANES, SPOTS))
        + [
            dma((28,)),
            dma((2, SPOTS, PIECES, 2)),
            dma((2, PIECES)),
            dma((2,)),
            dma((2,)),
            dma((2,)),
        ],
        compiler_params=pltpu.CompilerParams(
            vmem_limit_bytes=60 * 1024 * 1024, collective_id=5, has_side_effects=True
        ),
        name="plane_attention_back",
    )(table, sorted_table, qkv, grad_source, lse, hidden, *sources)


def by_owner(out_ref, values):
    rows = D // RANKS
    width = values.shape[1] // 2
    for owner in range(RANKS):
        part = values[owner * rows : (owner + 1) * rows]
        out_ref[owner] = jnp.concatenate([part[:, :width], part[:, width:]], axis=0).astype(BF16)


def plane_middle_kernel(
    mixed_in_ref,
    x_ref,
    dy_ref,
    vec_ref,
    w_out_ref,
    up_shift_ref,
    w_up_ref,
    w_down_ref,
    hidden_ref,
    send_ref,
    dres_ref,
    g_out_ref,
    g_up_ref,
    g_down_ref,
    g_up_bias_ref,
    g_small_ref,
    mixed_ref,
    residual_ref,
    second_ref,
    second_t_ref,
    total_ref,
    dsecond_ref,
):
    pieces, rows, _ = x_ref.shape
    tokens = pieces * rows
    step = pl.program_id(0)
    low = low_lanes(rows)
    out_shift, gain, shift, down_shift = (vec_ref[number : number + 1] for number in (4, 5, 6, 7))

    @pl.when(step == 0)
    def _():
        core = lax.axis_index("gx")
        for piece in range(pieces):
            span = slice(piece * rows, (piece + 1) * rows)
            for spot in (0, 2):
                first = [mixed_in_ref[side, spot, piece].astype(F32) for side in range(2)]
                last = [mixed_in_ref[side, spot + 1, piece].astype(F32) for side in range(2)]
                own_first = jnp.where(core == 0, first[0], first[1])
                own_last = jnp.where(core == 0, last[0], last[1])
                tiles = (
                    jnp.where(low, swap_halves(first[0]), first[1]),
                    jnp.where(low, own_first, last[0]),
                    swap_halves(jnp.where(low, own_last, last[1])),
                )
                for number, tile in enumerate(tiles):
                    spread = 3 * (spot // 2) + number
                    mixed_ref[span, spread * LANES : (spread + 1) * LANES] = tile.astype(BF16)
        residual = x_ref[...].reshape(tokens, D).astype(F32) + (
            dot(mixed_ref[...], w_out_ref[...]) + out_shift
        )
        residual_ref[...] = residual
        normal, _ = norm_parts(residual)
        second = normal * gain + shift
        second_ref[...] = second.astype(BF16)
        second_t_ref[...] = second.T.astype(BF16)
        total_ref[...] = jnp.zeros_like(total_ref)
        dsecond_ref[...] = jnp.zeros_like(dsecond_ref)

    w_down = w_down_ref[...].reshape(CHUNK, D)
    upper = dot(second_ref[...], w_up_ref[...]) + up_shift_ref[0]
    factor = 0.7978845608028654
    square = upper * upper
    bent = jnp.tanh(factor * (upper + 0.044715 * (upper * square)))
    middle_half = 0.5 * (1.0 + bent)
    active = (upper * middle_half).astype(BF16)
    slope = middle_half + 0.5 * upper * (1.0 - bent * bent) * (
        factor + (3.0 * 0.044715 * factor) * square
    )
    dy = dy_ref[...]
    total_ref[...] += dot(active, w_down)
    g_down_ref[...] = dot_lt(active, dy).astype(BF16).reshape(g_down_ref.shape)
    dupper = (dot_rt(dy, w_down) * slope).astype(BF16)
    g_up_bias_ref[0] = jnp.sum(dupper.astype(F32), axis=0, keepdims=True)
    by_owner(g_up_ref, dot(second_t_ref[...], dupper))
    dsecond_ref[...] += dot_rt(dupper, w_up_ref[...])

    @pl.when(step == pl.num_programs(0) - 1)
    def _():
        residual = residual_ref[...]
        hidden_ref[...] = (
            (residual + (total_ref[...] + down_shift)).astype(BF16).reshape(x_ref.shape)
        )
        normal, inverse = norm_parts(residual)
        dsecond = dsecond_ref[...]
        grad_out = dy_ref[...].astype(F32)
        g_small_ref[0:1] = jnp.sum(dsecond * normal, axis=0, keepdims=True)
        g_small_ref[1:2] = jnp.sum(dsecond, axis=0, keepdims=True)
        g_small_ref[2:3] = jnp.sum(grad_out, axis=0, keepdims=True)
        dres = grad_out + norm_pull(dsecond, normal, inverse, gain)
        dres_ref[...] = dres
        branch = dres.astype(BF16)
        g_small_ref[3:4] = jnp.sum(branch.astype(F32), axis=0, keepdims=True)
        by_owner(g_out_ref, dot_lt(mixed_ref[...], branch))
        dmixed = dot_rt(branch, w_out_ref[...])
        for piece in range(pieces):
            span = slice(piece * rows, (piece + 1) * rows)
            for spot in (0, 2):
                tiles = [
                    dmixed[span, number * LANES : (number + 1) * LANES]
                    for number in range(3 * (spot // 2), 3 * (spot // 2) + 3)
                ]
                flipped = [swap_halves(tile) for tile in tiles]
                send_ref[0, spot, piece] = jnp.where(low, tiles[1], flipped[0]).astype(BF16)
                send_ref[1, spot, piece] = jnp.where(low, tiles[1], tiles[0]).astype(BF16)
                send_ref[0, spot + 1, piece] = jnp.where(low, flipped[2], tiles[1]).astype(BF16)
                send_ref[1, spot + 1, piece] = flipped[2].astype(BF16)


def plane_middle(mixed_in, x, dy, vec, w_out, up_shift, w_up, w_down):
    pieces, rows, _ = x.shape
    tokens = pieces * rows
    shard = D // RANKS

    def fixed(shape):
        return pl.BlockSpec(shape, lambda step: (0,) * len(shape))

    steps = FF // CHUNK
    down = pl.BlockSpec((2, LANES, D), lambda step: (0, step, 0))
    return pl.pallas_call(
        plane_middle_kernel,
        grid=(steps,),
        out_shape=(
            jax.ShapeDtypeStruct(x.shape, BF16),
            jax.ShapeDtypeStruct(mixed_in.shape, BF16),
            jax.ShapeDtypeStruct((tokens, D), F32),
            jax.ShapeDtypeStruct((RANKS, 2 * shard, D // 2), BF16),
            jax.ShapeDtypeStruct((RANKS, 2 * shard, FF // 2), BF16),
            jax.ShapeDtypeStruct((2, FF // 2, D), BF16),
            jax.ShapeDtypeStruct((steps, 1, CHUNK), F32),
            jax.ShapeDtypeStruct((4, D), F32),
        ),
        in_specs=[
            fixed(mixed_in.shape),
            fixed(x.shape),
            fixed((tokens, D)),
            fixed(vec.shape),
            fixed((D, D)),
            pl.BlockSpec((1, 1, CHUNK), lambda step: (step, 0, 0)),
            pl.BlockSpec((D, CHUNK), lambda step: (0, step)),
            down,
        ],
        out_specs=(
            fixed(x.shape),
            fixed(mixed_in.shape),
            fixed((tokens, D)),
            fixed((RANKS, 2 * shard, D // 2)),
            pl.BlockSpec((RANKS, 2 * shard, LANES), lambda step: (0, 0, step)),
            down,
            pl.BlockSpec((1, 1, CHUNK), lambda step: (step, 0, 0)),
            fixed((4, D)),
        ),
        scratch_shapes=[
            VMEM((tokens, D), BF16),
            VMEM((tokens, D), F32),
            VMEM((tokens, D), BF16),
            VMEM((D, tokens), BF16),
            VMEM((tokens, D), F32),
            VMEM((tokens, D), F32),
        ],
        compiler_params=params_of(56),
        name="plane_middle",
    )(mixed_in, x, dy, vec, w_out, up_shift, w_up, w_down)


def plane_qkv_back_kernel(
    recv_ref,
    normed_ref,
    x_ref,
    dres_ref,
    vec_ref,
    w_ref,
    grad_ref,
    g_qkv_ref,
    g_bias_ref,
    g_small_ref,
    packed_ref,
    normed_t_ref,
    dnormed_ref,
):
    pieces, rows, _ = x_ref.shape
    step = pl.program_id(0)
    low = low_lanes(rows)

    @pl.when(step == 0)
    def _():
        core = lax.axis_index("gx")

        def put(tile, piece, value):
            side, chunk = tile // HALF_TILES, tile % HALF_TILES
            packed_ref[
                chunk, piece * rows : (piece + 1) * rows, side * LANES : (side + 1) * LANES
            ] = value.astype(BF16)

        for piece in range(pieces):
            seconds = []
            for spot in range(SPOTS):
                first = recv_ref[0, spot, piece, 0].astype(F32)
                second = recv_ref[1, spot, piece, 0].astype(F32)
                put(spot, piece, jnp.where(low, first, jnp.where(core == 0, first, second)))
                seconds.append(second)
                base = D // LANES + 3 * spot
                put(base, piece, recv_ref[0, spot, piece, 1])
                put(base + 1, piece, recv_ref[1, spot, piece, 1])
                shared = recv_ref[0, spot, piece, 2].astype(F32) + recv_ref[
                    1, spot, piece, 2
                ].astype(F32)
                put(base + 2, piece, shared)
            for number in range(2):
                put(
                    SPOTS + number,
                    piece,
                    jnp.where(low, seconds[2 * number], swap_halves(seconds[2 * number + 1])),
                )
        normed_t_ref[...] = normed_ref[...].astype(F32).T.astype(BF16)
        dnormed_ref[...] = jnp.zeros_like(dnormed_ref)

    packed = packed_ref[step]
    g_bias_ref[0] = jnp.sum(packed.astype(F32), axis=0, keepdims=True)
    by_owner(g_qkv_ref, dot(normed_t_ref[...], packed))
    dnormed_ref[...] += dot_rt(packed, w_ref[...])

    @pl.when(step == pl.num_programs(0) - 1)
    def _():
        normal, inverse = norm_parts(x_ref[...].reshape(pieces * rows, D).astype(F32))
        dnormed = dnormed_ref[...]
        g_small_ref[0:1] = jnp.sum(dnormed * normal, axis=0, keepdims=True)
        g_small_ref[1:2] = jnp.sum(dnormed, axis=0, keepdims=True)
        grad = dres_ref[...] + norm_pull(dnormed, normal, inverse, vec_ref[0:1])
        grad_ref[...] = grad.astype(BF16).reshape(x_ref.shape)


def plane_qkv_back(recv, normed, x, dres, vec, w):
    pieces, rows, _ = x.shape
    tokens = pieces * rows
    shard = D // RANKS

    def fixed(shape):
        return pl.BlockSpec(shape, lambda step: (0,) * len(shape))

    return pl.pallas_call(
        plane_qkv_back_kernel,
        grid=(HALF_TILES,),
        out_shape=(
            jax.ShapeDtypeStruct(x.shape, BF16),
            jax.ShapeDtypeStruct((RANKS, 2 * shard, 3 * D // 2), BF16),
            jax.ShapeDtypeStruct((HALF_TILES, 1, CHUNK), F32),
            jax.ShapeDtypeStruct((2, D), F32),
        ),
        in_specs=[
            fixed(recv.shape),
            fixed((tokens, D)),
            fixed(x.shape),
            fixed((tokens, D)),
            fixed(vec.shape),
            pl.BlockSpec((D, CHUNK), lambda step: (0, step)),
        ],
        out_specs=(
            fixed(x.shape),
            pl.BlockSpec((RANKS, 2 * shard, LANES), lambda step: (0, 0, step)),
            pl.BlockSpec((1, 1, CHUNK), lambda step: (step, 0, 0)),
            fixed((2, D)),
        ),
        scratch_shapes=[
            VMEM((HALF_TILES, tokens, CHUNK), BF16),
            VMEM((D, tokens), BF16),
            VMEM((tokens, D), F32),
        ],
        compiler_params=params_of(56),
        name="plane_qkv_back",
    )(recv, normed, x, dres, vec, w)


class Reduce:
    SENDS = 4 + 2 + 2 + 3
    RECVS = SENDS

    def __init__(self, source, total, near, corner_x, corner_y, side_x, side_y, far, out, sems):
        self.source, self.total, self.near = source, total, near
        self.corner = {1: corner_x, 2: corner_y}
        self.side = {1: side_x, 2: side_y}
        self.far, self.out = far, out
        self.send_sem, self.recv_sem, self.local_sem = sems
        self.core, self.plane, self.spot = place_here()
        self.copies = []
        self.locals = []

    def start(self):
        sibling = (1 - self.core, rank_of(self.plane, self.spot))
        for number, side in enumerate((3, 1, 2, 0)):
            spot = flip(self.spot, side)
            copy = remote(
                self.source.at[1 - self.core, :, spot],
                self.near.at[:, spot],
                self.send_sem.at[number],
                self.recv_sem.at[number],
                sibling,
            )
            copy.start()
            self.copies.append(copy)
            keep = pltpu.make_async_copy(
                self.source.at[self.core, :, spot],
                self.total.at[:, spot],
                self.local_sem.at[number],
            )
            keep.start()
            self.locals.append(keep)

    def take(self, number, side):
        self.copies[number].wait_recv()
        self.locals[number].wait()
        spot = flip(self.spot, side)

        def add(plane, carry):
            self.total[plane, spot] = (
                self.total[plane, spot].astype(F32) + self.near[plane, spot].astype(F32)
            ).astype(self.total.dtype)
            return carry

        lax.fori_loop(0, PLANES, add, 0)

    def corners(self):
        self.take(0, 3)
        spot = flip(self.spot, 3)
        index = 4
        self.corner_copies = []
        for bits in range(PLANES):
            side = 2 if bits < 2 else 1
            self.corner_copies.append(None)
            plane = flip(self.plane, bits)
            copy = remote(
                self.total.at[plane, spot],
                self.corner[side].at[bits % 2],
                self.send_sem.at[index + bits],
                self.recv_sem.at[index + bits],
                (self.core, rank_of(self.plane, flip(self.spot, side))),
            )
            copy.start()
            self.corner_copies[bits] = copy

    def sides(self):
        self.take(1, 1)
        self.take(2, 2)
        self.side_copies = {}
        for side in (1, 2):
            spot = flip(self.spot, side)
            came = 3 - side
            for bits in (0, 1) if came == 2 else (2, 3):
                self.corner_copies[bits].wait_recv()
                plane = flip(self.plane, bits)
                self.total[plane, spot] = (
                    self.total[plane, spot].astype(F32)
                    + self.corner[came][bits % 2].astype(F32)
                ).astype(self.total.dtype)
            copy = remote(
                self.total.at[:, spot],
                self.side[side],
                self.send_sem.at[7 + side],
                self.recv_sem.at[7 + side],
                (self.core, rank_of(self.plane, spot)),
            )
            copy.start()
            self.side_copies[side] = copy

    def columns(self):
        self.take(3, 0)
        for side in (1, 2):
            self.side_copies[side].wait_recv()

        def add(plane, carry):
            self.total[plane, self.spot] = (
                self.total[plane, self.spot].astype(F32)
                + self.side[1][plane].astype(F32)
                + self.side[2][plane].astype(F32)
            ).astype(self.total.dtype)
            return carry

        lax.fori_loop(0, PLANES, add, 0)
        self.far_copies = []
        for bits in range(1, PLANES):
            plane = flip(self.plane, bits)
            copy = remote(
                self.total.at[plane, self.spot],
                self.far.at[bits - 1],
                self.send_sem.at[9 + bits],
                self.recv_sem.at[9 + bits],
                (self.core, rank_of(plane, self.spot)),
            )
            copy.start()
            self.far_copies.append(copy)

    def finish(self):
        value = self.total[self.plane, self.spot].astype(F32)
        for bits in range(1, PLANES):
            self.far_copies[bits - 1].wait_recv()
            value = value + self.far[bits - 1].astype(F32)
        self.out[...] = value
        for copy in self.copies + self.corner_copies + self.far_copies:
            copy.wait_send()
        for side in (1, 2):
            self.side_copies[side].wait_send()


REDUCE_SEMS = 13


def reduce_scratch(shape, kind):
    tail = shape[3:]
    return [
        VMEM((PLANES, SPOTS) + tail, kind),
        VMEM((PLANES, SPOTS) + tail, kind),
        VMEM((2,) + tail, kind),
        VMEM((2,) + tail, kind),
        VMEM((PLANES,) + tail, kind),
        VMEM((PLANES,) + tail, kind),
        VMEM((PLANES - 1,) + tail, kind),
    ]


def spread_kernel(count, *refs):
    grad_ref = refs[0]
    sources = refs[1 : 1 + count]
    grad_out_ref = refs[1 + count]
    outs = refs[2 + count : 2 + 2 * count]
    scratch = refs[2 + 2 * count :]
    buffers = scratch[: 7 * count]
    send_sem, recv_sem, local_sem, move_send, move_recv, move_local = scratch[7 * count :]
    core, plane, spot = place_here()
    greet(all_partners(core, plane, spot))
    sums = [
        Reduce(
            source,
            *buffers[7 * number : 7 * number + 7],
            out,
            (send_sem.at[number], recv_sem.at[number], local_sem.at[number]),
        )
        for number, (source, out) in enumerate(zip(sources, outs))
    ]
    for one in sums:
        one.start()
    finish_grad = from_planes(grad_ref, grad_out_ref, move_send, move_recv, move_local)
    for one in sums:
        one.corners()
    for one in sums:
        one.sides()
    for one in sums:
        one.columns()
    for one in sums:
        one.finish()
    finish_grad()


def spread(grad, sources):
    count = len(sources)
    buffers = []
    for source in sources:
        buffers += reduce_scratch(source.shape, source.dtype)
    return pl.pallas_call(
        functools.partial(spread_kernel, count),
        out_shape=(jax.ShapeDtypeStruct(grad.shape, BF16),)
        + tuple(jax.ShapeDtypeStruct(source.shape[3:], F32) for source in sources),
        in_specs=[whole(ANY)] * (1 + count),
        out_specs=(whole(ANY),) + (whole(),) * count,
        scratch_shapes=buffers
        + [
            pltpu.SemaphoreType.DMA((count, REDUCE_SEMS)),
            pltpu.SemaphoreType.DMA((count, REDUCE_SEMS)),
            pltpu.SemaphoreType.DMA((count, 4)),
            pltpu.SemaphoreType.DMA((2,)),
            pltpu.SemaphoreType.DMA((2,)),
            pltpu.SemaphoreType.DMA((2,)),
        ],
        compiler_params=pltpu.CompilerParams(
            vmem_limit_bytes=56 * 1024 * 1024, collective_id=2, has_side_effects=True
        ),
        name="spread",
    )(grad, *sources)


def fold_columns(array):
    half = array.shape[1] // 2
    return jnp.concatenate([array[:, :half], array[:, half:]], axis=0)


def unfold_columns(array):
    half = array.shape[0] // 2
    return jnp.concatenate([array[:half], array[half:]], axis=1)


def plane_shards(
    hidden_in,
    rand_table,
    norm1_gain,
    norm1_bias,
    w_qkv,
    query_bias,
    value_bias,
    w_out,
    out_bias,
    norm2_gain,
    norm2_bias,
    w_up,
    up_bias,
    w_down,
    down_bias,
    cotangent,
):
    micro, rows, _ = hidden_in.shape
    local = rows // BLOCK
    own = norm1_gain.shape[0]
    order = [natural_block(entry) for entry in column_order()]
    inverse = [order.index(number) for number in range(len(order))]
    small = (8 + FF // D) * own
    entries = rand_table.size

    vec = jnp.concatenate(
        [
            norm1_gain,
            norm1_bias,
            query_bias,
            value_bias,
            out_bias,
            norm2_gain,
            norm2_bias,
            down_bias,
            up_bias,
            rand_table.reshape(entries).astype(BF16),
            jnp.zeros((16 * LANES - small - entries,), BF16),
        ]
    ).reshape(16, LANES)
    x, vecs, w_qkv_all = collect(hidden_in, vec, fold_columns(take_blocks(w_qkv, order)))
    vecs = vecs.reshape(RANKS, 16 * LANES)
    vectors = vecs[:, : 8 * own].reshape(RANKS, 8, own).swapaxes(0, 1).reshape(8, D).astype(F32)
    up_shift = vecs[:, 8 * own : small].astype(F32).reshape(2, FF // CHUNK, LANES)
    up_shift = up_shift.swapaxes(0, 1).reshape(FF // CHUNK, 1, CHUNK)
    bias = jnp.concatenate([vectors[2:3], jnp.zeros((1, D), F32), vectors[3:4]], axis=1)
    bias = take_blocks(bias, order).reshape(2, HALF_TILES, LANES)
    bias = bias.swapaxes(0, 1).reshape(1, 3 * D)
    plane = lax.div(lax.axis_index("gy"), SPOTS)
    tables = vecs[:, small : small + entries].reshape(2, PLANES * SPOTS, 2, local * RANDOM)
    tables = tables.astype(jnp.int32).transpose(2, 0, 1, 3).reshape(PLANES, 1, -1)
    table = lax.dynamic_index_in_dim(tables, plane, 0, keepdims=False)
    spare = -table.shape[1] % LANES
    table = jnp.pad(table, ((0, 0), (0, spare)), constant_values=2 * LANES)

    normed, send, sorted_table = plane_qkv(x, vectors, w_qkv_all, bias, table)
    s_ou = jnp.concatenate([fold_columns(w_out), fold_columns(w_up)], axis=1)
    qkv, c_ou, c_down = exchange_qkv(send, s_ou, w_down)
    qkv = qkv.reshape(PLANES * SPOTS, 3, local, BLOCK, LANES)
    mixed, lse, dy, w_out_all, w_up_all, w_down_all = plane_attention(
        table, qkv, cotangent, c_ou, c_down
    )
    mixed = mixed.reshape(2, SPOTS, PIECES, rows, LANES)
    hidden, grad_send, dres, g_out, g_up, g_down, g_up_bias, g_mid = plane_middle(
        mixed,
        x,
        dy.reshape(micro * rows, D),
        vectors,
        w_out_all,
        up_shift,
        w_up_all,
        w_down_all.reshape(2, FF // 2, D),
    )
    grid = (2, PLANES, SPOTS)
    dqkv, hidden_out, t_out, t_up, t_down = plane_attention_back(
        table,
        sorted_table,
        qkv,
        grad_send.reshape(2, SPOTS, PIECES, local, BLOCK, LANES),
        lse,
        hidden,
        [
            g_out.reshape(grid + g_out.shape[1:]),
            g_up.reshape(grid + g_up.shape[1:]),
            g_down.reshape(grid + (FF // RANKS, D)),
        ],
    )
    dqkv = dqkv.reshape(2, SPOTS, PIECES, 3, rows, LANES)
    grad, g_qkv, g_bias, g_first = plane_qkv_back(dqkv, normed, x, dres, vectors, w_qkv_all)

    g_bias = g_bias.reshape(HALF_TILES, 2, LANES).swapaxes(0, 1).reshape(1, 3 * D)
    g_bias = take_blocks(g_bias, inverse)
    singles = jnp.concatenate(
        [g_first, g_bias[:, :D], g_bias[:, 2 * D :], g_mid[3:4], g_mid[0:3]], axis=0
    )
    singles = singles.reshape(8, RANKS, own).swapaxes(0, 1).reshape(RANKS, 8 * own)
    g_up_bias = g_up_bias.reshape(FF // CHUNK, 2, LANES).swapaxes(0, 1).reshape(RANKS, FF // RANKS)
    singles = jnp.concatenate(
        [singles, g_up_bias, jnp.zeros((RANKS, 8 * LANES - small), F32)], axis=1
    )
    grad_hidden, singles, t_qkv = spread(
        grad,
        [singles.reshape(grid + (8, LANES)), g_qkv.reshape(grid + g_qkv.shape[1:])],
    )
    singles = singles.reshape(8 * LANES)
    parts = [singles[number * own : (number + 1) * own] for number in range(8)]
    return (
        hidden_out,
        grad_hidden.astype(F32),
        parts[0],
        parts[1],
        take_blocks(unfold_columns(t_qkv), inverse),
        parts[2],
        parts[3],
        unfold_columns(t_out),
        parts[4],
        parts[5],
        parts[6],
        unfold_columns(t_up),
        singles[8 * own : small],
        t_down,
        parts[7],
    )


def shards(*arrays):
    micro, rows, _ = arrays[0].shape
    fits = lax.axis_size("gx") == 2 and lax.axis_size("gy") == PLANES * SPOTS
    fits = fits and micro == 2 and rows % BLOCK == 0
    return (plane_shards if fits else general_shards)(*arrays)


def solution(mesh):
    tokens = P(None, AXES, None)
    vector = P(AXES)
    matrix = P(AXES, None)
    placed = (
        tokens,
        tokens,
        vector,
        vector,
        matrix,
        vector,
        vector,
        matrix,
        vector,
        vector,
        vector,
        matrix,
        vector,
        matrix,
        vector,
        tokens,
    )
    returned = (
        tokens,
        tokens,
        vector,
        vector,
        matrix,
        vector,
        vector,
        matrix,
        vector,
        vector,
        vector,
        matrix,
        vector,
        matrix,
        vector,
    )
    return jax.shard_map(
        shards, mesh=mesh, in_specs=placed, out_specs=returned, check_vma=False
    )
```

```python
import functools

import jax
import jax.numpy as jnp
from jax import lax
from jax.experimental import pallas as pl
from jax.experimental.pallas import tpu as pltpu
from jax.sharding import PartitionSpec as P

HEADS = 12
HEAD_DIM = 64
D = 768
FF = 3072
BLOCK = 64
RANDOM = 3
LANES = 2 * HEAD_DIM
EPSILON = 1e-05
NEGATIVE = -1e30
SCALE = HEAD_DIM**-0.5
CHUNK = 256
SPAN = 8

F32 = jnp.float32
BF16 = jnp.bfloat16
VMEM = pltpu.VMEM


def whole(space=VMEM):
    return pl.BlockSpec(memory_space=space)


def params_of(megabytes):
    return pltpu.CompilerParams(vmem_limit_bytes=megabytes * 1024 * 1024)


def head_place(head):
    return (head // 3) * 4 + head % 3


def dot(left, right):
    return lax.dot_general(left, right, (((1,), (0,)), ((), ())), preferred_element_type=F32)


def dot_rt(left, right):
    return lax.dot_general(left, right, (((1,), (1,)), ((), ())), preferred_element_type=F32)


def dot_lt(left, right):
    return lax.dot_general(left, right, (((0,), (0,)), ((), ())), preferred_element_type=F32)


def swap_halves(tile):
    return pltpu.roll(tile, HEAD_DIM, axis=tile.ndim - 1)


def low_lanes(rows):
    return lax.broadcasted_iota(jnp.int32, (rows, LANES), 1) < HEAD_DIM


def norm_parts(values):
    centre = values - jnp.mean(values, axis=-1, keepdims=True)
    spread = jnp.mean(centre * centre, axis=-1, keepdims=True)
    inverse = lax.rsqrt(spread + EPSILON)
    return centre * inverse, inverse


def norm_pull(grad, normal, inverse, gain):
    scaled = grad * gain
    return inverse * (
        scaled
        - jnp.mean(scaled, axis=-1, keepdims=True)
        - normal * jnp.mean(scaled * normal, axis=-1, keepdims=True)
    )


def qkv_kernel(x_ref, gain_ref, shift_ref, w_ref, bias_ref, normed_ref, send_ref):
    micro, rows, _ = x_ref.shape
    values = x_ref[...].reshape(micro * rows, D).astype(F32)
    normal, _ = norm_parts(values)
    normed_ref[...] = (normal * gain_ref[...] + shift_ref[...]).astype(BF16)
    low = low_lanes(rows)
    for chunk in range(3 * D // CHUNK):
        columns = slice(chunk * CHUNK, (chunk + 1) * CHUNK)
        packed = dot(normed_ref[...], w_ref[:, columns]) + bias_ref[:, columns]
        if chunk < D // CHUNK:
            packed = packed.astype(BF16).astype(F32) * SCALE
        for tile in range(CHUNK // LANES):
            part = packed[:, tile * LANES : (tile + 1) * LANES]
            first, second = part[:rows], part[rows:]
            if chunk < D // CHUNK:
                head = (chunk * CHUNK // LANES + tile) * 2
                even = jnp.where(low, first, swap_halves(second))
                odd = jnp.where(low, swap_halves(first), second)
                send_ref[head_place(head), 0] = even.astype(BF16)
                send_ref[head_place(head + 1), 0] = odd.astype(BF16)
            else:
                head = (chunk * CHUNK - D) // LANES + tile
                send_ref[head_place(head), 1] = first.astype(BF16)
                send_ref[head_place(head), 2] = swap_halves(second).astype(BF16)


def qkv_forward(x, gain, shift, w, bias, groups):
    micro, rows, _ = x.shape
    return pl.pallas_call(
        qkv_kernel,
        out_shape=(
            jax.ShapeDtypeStruct((micro * rows, D), BF16),
            jax.ShapeDtypeStruct((groups, 3, rows, LANES), BF16),
        ),
        in_specs=[whole()] * 5,
        out_specs=(whole(), whole()),
        compiler_params=params_of(48),
        name="qkv_forward",
    )(x, gain, shift, w, bias)


def half_mask(low_half):
    lane = lax.broadcasted_iota(jnp.int32, (1, LANES), 1)
    keep = (lane < HEAD_DIM) if low_half else (lane >= HEAD_DIM)
    return jnp.where(keep, 1.0, 0.0).astype(BF16)


def inner_slots(table_ref, block, blocks):
    ids, bias = slots_of(table_ref, 0, block, blocks)
    edge = (block == 0) | (block == blocks - 1)
    ids[0] = jnp.maximum(ids[0], 0)
    ids[2] = jnp.minimum(ids[2], blocks - 1)
    return ids, bias + jnp.where(edge, NEGATIVE, 0.0).astype(F32)


def slots_of(table_ref, micro, block, blocks):
    picks = [table_ref[micro, block * RANDOM + number] for number in range(RANDOM)]
    last = blocks - 1
    ids = [block - 1, block, block + 1, 0, last] + picks
    dropped = [None, None, None, block == 1, block == last - 1]
    for number in range(RANDOM):
        pick = picks[number]
        bad = (jnp.abs(pick - block) <= 1) | (pick == 0) | (pick == last)
        for earlier in range(number):
            bad = bad | (pick == picks[earlier])
        dropped.append(bad)
    lane = lax.broadcasted_iota(jnp.int32, (1, LANES), 1)
    tiles = []
    for pair in range(len(ids) // 2):
        level = [
            0.0 if bad is None else jnp.where(bad, NEGATIVE, 0.0).astype(F32)
            for bad in dropped[2 * pair : 2 * pair + 2]
        ]
        tiles.append(jnp.where(lane < HEAD_DIM, level[0], level[1]))
    return ids, jnp.concatenate(tiles, axis=1)


def attend_kernel(table_ref, qkv_ref, out_ref, lse_ref, s_ref):
    groups, _, local, _, _ = qkv_ref.shape
    blocks = groups * local
    low = low_lanes(BLOCK)
    masks = [half_mask(True), half_mask(False)]

    def load(component, block):
        return qkv_ref[block // local, component, block % local]

    def sparse(block, carry):
        mixed, logs = [], []
        for micro in range(2):
            ids, bias = slots_of(table_ref, micro, block, blocks)
            keys = jnp.concatenate([load(1 + micro, spot) for spot in ids], axis=0)
            query = load(0, block) * masks[micro]
            scores = dot_rt(query, keys) + bias
            top = jnp.max(scores, axis=1, keepdims=True)
            powered = jnp.exp(scores - top)
            total = jnp.sum(powered, axis=1, keepdims=True)
            mixed.append(dot(powered.astype(BF16), keys) * (1.0 / total))
            logs.append(top + jnp.log(total))
        out_ref[block // local, block % local] = jnp.where(low, mixed[1], mixed[0]).astype(BF16)
        lse_ref[block] = jnp.where(low, logs[0], logs[1])
        return carry

    lax.fori_loop(1, blocks - 1, sparse, 0)

    spans = blocks // SPAN
    ends = (0, blocks - 1)
    results = []
    for micro in range(2):
        query = jnp.concatenate([load(0, end) for end in ends], axis=0) * masks[micro]

        def keys_at(span, micro=micro):
            return jnp.concatenate(
                [load(1 + micro, span * SPAN + spot) for spot in range(SPAN)], axis=0
            )

        def first_pass(span, top, query=query, keys_at=keys_at):
            scores = dot_rt(query, keys_at(span))
            s_ref[span] = scores
            return jnp.maximum(top, jnp.max(scores, axis=1, keepdims=True))

        top = lax.fori_loop(0, spans, first_pass, jnp.full((2 * BLOCK, 1), NEGATIVE, F32))

        def second_pass(span, carry, top=top, keys_at=keys_at):
            total, mixed = carry
            powered = jnp.exp(s_ref[span] - top)
            return (
                total + jnp.sum(powered, axis=1, keepdims=True),
                mixed + dot(powered.astype(BF16), keys_at(span)),
            )

        total, mixed = lax.fori_loop(
            0,
            spans,
            second_pass,
            (jnp.zeros((2 * BLOCK, 1), F32), jnp.zeros((2 * BLOCK, LANES), F32)),
        )
        results.append((mixed * (1.0 / total), top + jnp.log(total)))
    for place, end in enumerate(ends):
        rows = slice(place * BLOCK, (place + 1) * BLOCK)
        out_ref[end // local, end % local] = jnp.where(
            low, results[1][0][rows], results[0][0][rows]
        ).astype(BF16)
        lse_ref[end] = jnp.where(low, results[0][1][rows], results[1][1][rows])


def attention_forward(table, qkv):
    groups, _, local, _, _ = qkv.shape
    blocks = groups * local
    return pl.pallas_call(
        attend_kernel,
        out_shape=(
            jax.ShapeDtypeStruct((groups, local, BLOCK, LANES), BF16),
            jax.ShapeDtypeStruct((blocks, BLOCK, LANES), F32),
        ),
        in_specs=[whole(pltpu.SMEM), whole()],
        out_specs=(whole(), whole()),
        scratch_shapes=[VMEM((blocks // SPAN, 2 * BLOCK, SPAN * BLOCK), F32)],
        compiler_params=params_of(48),
        name="attention_forward",
    )(table, qkv)


def attend_back_kernel(table_ref, qkv_ref, grad_ref, lse_ref, out_ref, sums_ref, p_ref, dp_ref):
    groups, _, local, _, _ = qkv_ref.shape
    blocks = groups * local
    low = low_lanes(BLOCK)
    masks = [half_mask(True), half_mask(False)]

    def load(component, block):
        return qkv_ref[block // local, component, block % local]

    def load_grad(block):
        return grad_ref[block // local, block % local]

    def clear(block, carry):
        for micro in range(2):
            sums_ref[micro, block] = jnp.zeros((BLOCK, LANES), F32)
        return carry

    lax.fori_loop(0, blocks, clear, 0)

    def sparse(block, carry):
        grads = []
        for micro in range(2):
            ids, bias = slots_of(table_ref, micro, block, blocks)
            keys = jnp.concatenate([load(1 + micro, spot) for spot in ids], axis=0)
            both = jnp.concatenate(
                [load(0, block) * masks[micro], load_grad(block) * masks[1 - micro]], axis=0
            )
            products = dot_rt(both, keys)
            logs = lse_ref[block][:, micro * HEAD_DIM : micro * HEAD_DIM + 1]
            weights = jnp.exp(products[:BLOCK] + bias - logs)
            grad_weights = products[BLOCK:]
            delta = jnp.sum(weights * grad_weights, axis=1, keepdims=True)
            grad_scores = weights * (grad_weights - delta)
            stacked = jnp.concatenate([grad_scores, weights], axis=0).astype(BF16)
            grads.append(dot(stacked[:BLOCK], keys))
            shares = dot_lt(stacked, both)
            for place, spot in enumerate(ids):
                sums_ref[micro, spot] += shares[place * BLOCK : (place + 1) * BLOCK]
        out_ref[block // local, 0, block % local] = (
            jnp.where(low, grads[0], grads[1]) * SCALE
        ).astype(BF16)
        return carry

    lax.fori_loop(1, blocks - 1, sparse, 0)

    spans = blocks // SPAN
    ends = (0, blocks - 1)
    results = []
    for micro in range(2):
        query = jnp.concatenate([load(0, end) for end in ends], axis=0) * masks[micro]
        grad = jnp.concatenate([load_grad(end) for end in ends], axis=0) * masks[1 - micro]
        both = jnp.concatenate([query, grad], axis=0)
        logs = jnp.concatenate(
            [lse_ref[end][:, micro * HEAD_DIM : micro * HEAD_DIM + 1] for end in ends], axis=0
        )

        def keys_at(span, micro=micro):
            return jnp.concatenate(
                [load(1 + micro, span * SPAN + spot) for spot in range(SPAN)], axis=0
            )

        def first_pass(span, delta, both=both, logs=logs, keys_at=keys_at):
            products = dot_rt(both, keys_at(span))
            weights = jnp.exp(products[: 2 * BLOCK] - logs)
            grad_weights = products[2 * BLOCK :]
            p_ref[span] = weights
            dp_ref[span] = grad_weights
            return delta + jnp.sum(weights * grad_weights, axis=1, keepdims=True)

        delta = lax.fori_loop(0, spans, first_pass, jnp.zeros((2 * BLOCK, 1), F32))

        def second_pass(span, carry, delta=delta, both=both, keys_at=keys_at, micro=micro):
            weights = p_ref[span]
            grad_scores = weights * (dp_ref[span] - delta)
            stacked = jnp.concatenate([grad_scores, weights], axis=0).astype(BF16)
            shares = dot_lt(stacked, both)
            for spot in range(SPAN):
                sums_ref[micro, span * SPAN + spot] += shares[spot * BLOCK : (spot + 1) * BLOCK]
            return carry + dot(stacked[: 2 * BLOCK], keys_at(span))

        results.append(
            lax.fori_loop(0, spans, second_pass, jnp.zeros((2 * BLOCK, LANES), F32))
        )
    for place, end in enumerate(ends):
        rows = slice(place * BLOCK, (place + 1) * BLOCK)
        out_ref[end // local, 0, end % local] = (
            jnp.where(low, results[0][rows], results[1][rows]) * SCALE
        ).astype(BF16)

    def finish(block, carry):
        for micro in range(2):
            out_ref[block // local, 1 + micro, block % local] = sums_ref[micro, block].astype(BF16)
        return carry

    lax.fori_loop(0, blocks, finish, 0)


def attention_backward(table, qkv, grad, lse):
    groups, _, local, _, _ = qkv.shape
    blocks = groups * local
    spans = VMEM((blocks // SPAN, 2 * BLOCK, SPAN * BLOCK), F32)
    return pl.pallas_call(
        attend_back_kernel,
        out_shape=jax.ShapeDtypeStruct(qkv.shape, BF16),
        in_specs=[whole(pltpu.SMEM), whole(), whole(), whole()],
        out_specs=whole(),
        scratch_shapes=[VMEM((2, blocks, BLOCK, LANES), F32), spans, spans],
        compiler_params=params_of(48),
        name="attention_backward",
    )(table, qkv, grad, lse)


def middle_kernel(
    mixed_in_ref,
    x_ref,
    dy_ref,
    w_out_ref,
    out_shift_ref,
    gain_ref,
    shift_ref,
    up_shift_ref,
    down_shift_ref,
    w_up_ref,
    w_down_ref,
    hidden_ref,
    send_ref,
    dres_ref,
    g_out_ref,
    g_up_ref,
    g_down_ref,
    g_up_bias_ref,
    g_small_ref,
    mixed_ref,
    residual_ref,
    second_ref,
    second_t_ref,
    total_ref,
    dsecond_ref,
):
    micro, rows, _ = x_ref.shape
    step = pl.program_id(0)
    low = low_lanes(rows)

    @pl.when(step == 0)
    def _():
        for pair in range(HEADS // 2):
            even = mixed_in_ref[head_place(2 * pair)].astype(F32)
            odd = mixed_in_ref[head_place(2 * pair + 1)].astype(F32)
            columns = slice(pair * LANES, (pair + 1) * LANES)
            mixed_ref[:rows, columns] = jnp.where(low, swap_halves(even), odd).astype(BF16)
            mixed_ref[rows:, columns] = jnp.where(low, even, swap_halves(odd)).astype(BF16)
        residual = x_ref[...].reshape(micro * rows, D).astype(F32) + (
            dot(mixed_ref[...], w_out_ref[...]) + out_shift_ref[...]
        )
        residual_ref[...] = residual
        normal, _ = norm_parts(residual)
        second = normal * gain_ref[...] + shift_ref[...]
        second_ref[...] = second.astype(BF16)
        second_t_ref[...] = second.T.astype(BF16)
        total_ref[...] = jnp.zeros_like(total_ref)
        dsecond_ref[...] = jnp.zeros_like(dsecond_ref)

    upper = dot(second_ref[...], w_up_ref[...]) + up_shift_ref[...]
    factor = 0.7978845608028654
    square = upper * upper
    bent = jnp.tanh(factor * (upper + 0.044715 * (upper * square)))
    half = 0.5 * (1.0 + bent)
    active = (upper * half).astype(BF16)
    slope = half + 0.5 * upper * (1.0 - bent * bent) * (
        factor + (3.0 * 0.044715 * factor) * square
    )
    dy = dy_ref[...]
    total_ref[...] += dot(active, w_down_ref[...])
    g_down_ref[...] = dot_lt(active, dy).astype(g_down_ref.dtype)
    dupper = (dot_rt(dy, w_down_ref[...]) * slope).astype(BF16)
    g_up_bias_ref[...] = jnp.sum(dupper.astype(F32), axis=0, keepdims=True)
    g_up_ref[...] = dot(second_t_ref[...], dupper).astype(g_up_ref.dtype)
    dsecond_ref[...] += dot_rt(dupper, w_up_ref[...])

    @pl.when(step == pl.num_programs(0) - 1)
    def _():
        residual = residual_ref[...]
        hidden_ref[...] = (
            (residual + (total_ref[...] + down_shift_ref[...])).astype(BF16).reshape(x_ref.shape)
        )
        normal, inverse = norm_parts(residual)
        dsecond = dsecond_ref[...]
        grad_out = dy_ref[...].astype(F32)
        g_small_ref[0:1] = jnp.sum(dsecond * normal, axis=0, keepdims=True)
        g_small_ref[1:2] = jnp.sum(dsecond, axis=0, keepdims=True)
        g_small_ref[2:3] = jnp.sum(grad_out, axis=0, keepdims=True)
        dres = grad_out + norm_pull(dsecond, normal, inverse, gain_ref[...])
        dres_ref[...] = dres
        branch = dres.astype(BF16)
        g_small_ref[3:4] = jnp.sum(branch.astype(F32), axis=0, keepdims=True)
        g_out_ref[...] = dot_lt(mixed_ref[...], branch).astype(g_out_ref.dtype)
        dmixed = dot_rt(branch, w_out_ref[...])
        for pair in range(HEADS // 2):
            part = dmixed[:, pair * LANES : (pair + 1) * LANES]
            first, last = part[:rows], part[rows:]
            even = jnp.where(low, last, swap_halves(first))
            odd = jnp.where(low, swap_halves(last), first)
            send_ref[head_place(2 * pair)] = even.astype(BF16)
            send_ref[head_place(2 * pair + 1)] = odd.astype(BF16)


def middle(mixed_in, x, dy, w_out, out_shift, gain, shift, up_shift, down_shift, w_up, w_down, kind):
    micro, rows, _ = x.shape
    tokens = micro * rows
    groups = mixed_in.shape[0]

    def fixed(shape):
        return pl.BlockSpec(shape, lambda step: (0,) * len(shape))

    vector = fixed((1, D))
    steps = FF // CHUNK
    return pl.pallas_call(
        middle_kernel,
        grid=(steps,),
        out_shape=(
            jax.ShapeDtypeStruct(x.shape, BF16),
            jax.ShapeDtypeStruct((groups, rows, LANES), BF16),
            jax.ShapeDtypeStruct((tokens, D), F32),
            jax.ShapeDtypeStruct((D, D), kind),
            jax.ShapeDtypeStruct((D, FF), kind),
            jax.ShapeDtypeStruct((FF, D), kind),
            jax.ShapeDtypeStruct((1, FF), F32),
            jax.ShapeDtypeStruct((4, D), F32),
        ),
        in_specs=[
            fixed(mixed_in.shape),
            fixed(x.shape),
            fixed((tokens, D)),
            fixed((D, D)),
            vector,
            vector,
            vector,
            pl.BlockSpec((1, CHUNK), lambda step: (0, step)),
            vector,
            pl.BlockSpec((D, CHUNK), lambda step: (0, step)),
            pl.BlockSpec((CHUNK, D), lambda step: (step, 0)),
        ],
        out_specs=(
            fixed(x.shape),
            fixed((groups, rows, LANES)),
            fixed((tokens, D)),
            fixed((D, D)),
            pl.BlockSpec((D, CHUNK), lambda step: (0, step)),
            pl.BlockSpec((CHUNK, D), lambda step: (step, 0)),
            pl.BlockSpec((1, CHUNK), lambda step: (0, step)),
            fixed((4, D)),
        ),
        scratch_shapes=[
            VMEM((tokens, D), BF16),
            VMEM((tokens, D), F32),
            VMEM((tokens, D), BF16),
            VMEM((D, tokens), BF16),
            VMEM((tokens, D), F32),
            VMEM((tokens, D), F32),
        ],
        compiler_params=params_of(56),
        name="middle",
    )(mixed_in, x, dy, w_out, out_shift, gain, shift, up_shift, down_shift, w_up, w_down)


def qkv_back_kernel(
    recv_ref,
    normed_ref,
    x_ref,
    dres_ref,
    gain_ref,
    w_ref,
    grad_ref,
    g_qkv_ref,
    g_bias_ref,
    g_small_ref,
    packed_ref,
    normed_t_ref,
    dnormed_ref,
):
    micro, rows, _ = x_ref.shape
    step = pl.program_id(0)
    low = low_lanes(rows)

    @pl.when(step == 0)
    def _():
        for pair in range(HEADS // 2):
            even = recv_ref[head_place(2 * pair), 0].astype(F32)
            odd = recv_ref[head_place(2 * pair + 1), 0].astype(F32)
            spot, columns = pair // 2, slice((pair % 2) * LANES, (pair % 2 + 1) * LANES)
            packed_ref[spot, :rows, columns] = jnp.where(low, even, swap_halves(odd)).astype(BF16)
            packed_ref[spot, rows:, columns] = jnp.where(low, swap_halves(even), odd).astype(BF16)
        for head in range(HEADS):
            spot = D // CHUNK + head // 2
            columns = slice((head % 2) * LANES, (head % 2 + 1) * LANES)
            packed_ref[spot, :rows, columns] = recv_ref[head_place(head), 1]
            packed_ref[spot, rows:, columns] = swap_halves(
                recv_ref[head_place(head), 2].astype(F32)
            ).astype(BF16)
        normed_t_ref[...] = normed_ref[...].astype(F32).T.astype(BF16)
        dnormed_ref[...] = jnp.zeros_like(dnormed_ref)

    packed = packed_ref[step]
    g_bias_ref[...] = jnp.sum(packed.astype(F32), axis=0, keepdims=True)
    g_qkv_ref[...] = dot(normed_t_ref[...], packed).astype(g_qkv_ref.dtype)
    dnormed_ref[...] += dot_rt(packed, w_ref[...])

    @pl.when(step == pl.num_programs(0) - 1)
    def _():
        normal, inverse = norm_parts(x_ref[...].reshape(micro * rows, D).astype(F32))
        dnormed = dnormed_ref[...]
        g_small_ref[0:1] = jnp.sum(dnormed * normal, axis=0, keepdims=True)
        g_small_ref[1:2] = jnp.sum(dnormed, axis=0, keepdims=True)
        grad = dres_ref[...] + norm_pull(dnormed, normal, inverse, gain_ref[...])
        grad_ref[...] = grad.reshape(x_ref.shape)


def qkv_backward(recv, normed, x, dres, gain, w, kind):
    micro, rows, _ = x.shape
    tokens = micro * rows

    def fixed(shape):
        return pl.BlockSpec(shape, lambda step: (0,) * len(shape))

    steps = 3 * D // CHUNK
    return pl.pallas_call(
        qkv_back_kernel,
        grid=(steps,),
        out_shape=(
            jax.ShapeDtypeStruct(x.shape, F32),
            jax.ShapeDtypeStruct((D, 3 * D), kind),
            jax.ShapeDtypeStruct((1, 3 * D), F32),
            jax.ShapeDtypeStruct((2, D), F32),
        ),
        in_specs=[
            fixed(recv.shape),
            fixed((tokens, D)),
            fixed(x.shape),
            fixed((tokens, D)),
            fixed((1, D)),
            pl.BlockSpec((D, CHUNK), lambda step: (0, step)),
        ],
        out_specs=(
            fixed(x.shape),
            pl.BlockSpec((D, CHUNK), lambda step: (0, step)),
            pl.BlockSpec((1, CHUNK), lambda step: (0, step)),
            fixed((2, D)),
        ),
        scratch_shapes=[
            VMEM((steps, tokens, CHUNK), BF16),
            VMEM((D, tokens), BF16),
            VMEM((tokens, D), F32),
        ],
        compiler_params=params_of(56),
        name="qkv_backward",
    )(recv, normed, x, dres, gain, w)


AXES = ("gx", "gy")


def gather(array):
    return lax.all_gather(array, AXES, axis=0, tiled=True)


def scatter(array):
    return lax.psum_scatter(array, AXES, scatter_dimension=0, tiled=True)


def exchange(array):
    return lax.all_to_all(array, "gy", 0, 0, tiled=True)


def by_heads(w_qkv):
    rows = w_qkv.shape[0]
    sides = w_qkv[:, D:].reshape(rows, 2, HEADS, HEAD_DIM)
    return jnp.concatenate([w_qkv[:, :D], jnp.swapaxes(sides, 1, 2).reshape(rows, 2 * D)], axis=1)


def by_parts(w_qkv):
    rows = w_qkv.shape[0]
    sides = w_qkv[:, D:].reshape(rows, HEADS, 2, HEAD_DIM)
    return jnp.concatenate([w_qkv[:, :D], jnp.swapaxes(sides, 1, 2).reshape(rows, 2 * D)], axis=1)


def general_shards(
    hidden_in,
    rand_table,
    norm1_gain,
    norm1_bias,
    w_qkv,
    query_bias,
    value_bias,
    w_out,
    out_bias,
    norm2_gain,
    norm2_bias,
    w_up,
    up_bias,
    w_down,
    down_bias,
    cotangent,
):
    micro, rows, _ = hidden_in.shape
    groups = lax.axis_size("gy")
    local = rows // BLOCK
    own = norm1_gain.shape[0]

    vectors = jnp.concatenate(
        [
            norm1_gain,
            norm1_bias,
            query_bias,
            value_bias,
            out_bias,
            norm2_gain,
            norm2_bias,
            down_bias,
            up_bias,
        ]
    )
    table = lax.all_gather(rand_table, "gy", axis=1, tiled=True)
    table = table.reshape(micro, groups * local * RANDOM)
    vectors = gather(vectors[None]).astype(F32)
    gain_one, shift_one, query_shift, value_shift, out_shift, gain_two, shift_two, down_shift = (
        vectors[:, number * own : (number + 1) * own].reshape(1, D) for number in range(8)
    )
    up_shift = vectors[:, 8 * own :].reshape(1, FF)
    w_qkv_full = gather(by_heads(w_qkv))
    w_out_full, w_up_full, w_down_full = gather(w_out), gather(w_up), gather(w_down)
    packed_bias = by_heads(
        jnp.concatenate([query_shift, jnp.zeros_like(query_shift), value_shift], axis=1)
    )

    normed, send = qkv_forward(hidden_in, gain_one, shift_one, w_qkv_full, packed_bias, groups)
    qkv = exchange(send).reshape(groups, 3, local, BLOCK, LANES)
    mixed, lse = attention_forward(table, qkv)
    mixed_back = exchange(mixed.reshape(groups, rows, LANES))
    hidden_out, grad_send, dres, g_out, g_up, g_down, g_up_bias, g_mid = middle(
        mixed_back,
        hidden_in,
        cotangent.reshape(micro * rows, D),
        w_out_full,
        out_shift,
        gain_two,
        shift_two,
        up_shift,
        down_shift,
        w_up_full,
        w_down_full,
        F32,
    )
    grad_mixed = exchange(grad_send).reshape(groups, local, BLOCK, LANES)
    dqkv = attention_backward(table, qkv, grad_mixed, lse)
    dqkv_back = exchange(dqkv.reshape(groups, 3, rows, LANES))
    grad_hidden, g_qkv, g_packed, g_first = qkv_backward(
        dqkv_back, normed, hidden_in, dres, gain_one, w_qkv_full, F32
    )

    g_packed = by_parts(g_packed)
    small = [
        g_first[0],
        g_first[1],
        g_packed[0, :D],
        g_packed[0, 2 * D :],
        g_mid[3],
        g_mid[0],
        g_mid[1],
        g_mid[2],
    ]
    ranks = D // own
    small = jnp.concatenate(
        [item.reshape(ranks, own) for item in small] + [g_up_bias.reshape(ranks, 4 * own)], axis=1
    )
    small = scatter(small)[0]
    parts = [small[number * own : (number + 1) * own] for number in range(8)]
    return (
        hidden_out,
        grad_hidden,
        parts[0],
        parts[1],
        by_parts(scatter(g_qkv)),
        parts[2],
        parts[3],
        scatter(g_out),
        parts[4],
        parts[5],
        parts[6],
        scatter(g_up),
        small[8 * own :],
        scatter(g_down),
        parts[7],
    )


MESH = pl.DeviceIdType.MESH
ANY = pl.ANY
PLANES = 4
SPOTS = 4
PIECES = 2
RANKS = 2 * PLANES * SPOTS
TILES = 3 * D // LANES
HALF_TILES = TILES // 2
QUERY_ORDER = (0, 2, 3, 5, 6, 8, 9, 11, 1, 4, 7, 10)


def column_order():
    order = [("q", head) for head in QUERY_ORDER]
    for spot in range(SPOTS):
        for place in (2 * 3 * spot, 2 * 3 * spot + 2):
            order += [("k", place // 2), ("v", place // 2)]
        order += [("v", 3 * spot + 2), ("k", 3 * spot + 2)]
    return order


def natural_block(entry):
    return "qkv".index(entry[0]) * HEADS + entry[1]


def take_blocks(array, order):
    parts = []
    start = 0
    while start < len(order):
        stop = start + 1
        while stop < len(order) and order[stop] == order[stop - 1] + 1:
            stop += 1
        parts.append(array[..., order[start] * HEAD_DIM : (order[start] + stop - start) * HEAD_DIM])
        start = stop
    return jnp.concatenate(parts, axis=-1)


def flip(value, bits):
    if bits == 0:
        return value
    if bits == 1:
        return value + 1 - 2 * lax.rem(value, 2)
    if bits == 2:
        return value + 2 - 4 * lax.div(value, 2)
    return 3 - value


def place_here():
    core, rank = lax.axis_index("gx"), lax.axis_index("gy")
    return core, lax.div(rank, SPOTS), lax.rem(rank, SPOTS)


def rank_of(plane, spot):
    return plane * SPOTS + spot


def greet(partners):
    barrier = pltpu.get_barrier_semaphore()
    for partner in partners:
        pl.semaphore_signal(barrier, inc=1, device_id=partner, device_id_type=MESH)
    pl.semaphore_wait(barrier, len(partners))


def remote(source, target, send_sem, recv_sem, device):
    return pltpu.make_async_remote_copy(
        src_ref=source,
        dst_ref=target,
        send_sem=send_sem,
        recv_sem=recv_sem,
        device_id=device,
        device_id_type=MESH,
    )


def column_partners(core, plane, spot):
    partners = [(1 - core, rank_of(plane, spot))]
    for bits in range(1, PLANES):
        for other in (core, 1 - core):
            partners.append((other, rank_of(flip(plane, bits), spot)))
    return partners


def all_partners(core, plane, spot):
    return column_partners(core, plane, spot) + [
        (core, rank_of(plane, flip(spot, 1))),
        (core, rank_of(plane, flip(spot, 2))),
    ]


def to_planes(source, target, send_sem, recv_sem, local_sem):
    core, plane, spot = place_here()
    half, odd = lax.div(plane, 2), lax.rem(plane, 2)
    sends, keeps = [], []
    for micro in range(2):
        goal = 2 * micro + core
        here = (goal == plane) & (half == core)
        send = remote(
            source.at[micro],
            target.at[odd],
            send_sem.at[micro],
            recv_sem.at[odd],
            (half, rank_of(goal, spot)),
        )
        keep = pltpu.make_async_copy(source.at[micro], target.at[odd], local_sem.at[micro])

        @pl.when(jnp.logical_not(here))
        def _(send=send):
            send.start()

        @pl.when(here)
        def _(keep=keep):
            keep.start()

        sends.append((here, send))
        keeps.append((here, keep))

    def finish():
        for piece in range(PIECES):
            mine = (odd == core) & (plane == 2 * core + piece)
            arrival = remote(
                source.at[0],
                target.at[piece],
                send_sem.at[0],
                recv_sem.at[piece],
                (core, rank_of(plane, spot)),
            )

            @pl.when(jnp.logical_not(mine))
            def _(arrival=arrival):
                arrival.wait_recv()

        for (here, send), (_, keep) in zip(sends, keeps):

            @pl.when(jnp.logical_not(here))
            def _(send=send):
                send.wait_send()

            @pl.when(here)
            def _(keep=keep):
                keep.wait()

    return finish


def from_planes(source, target, send_sem, recv_sem, local_sem):
    core, plane, spot = place_here()
    micro, odd = lax.div(plane, 2), lax.rem(plane, 2)
    sends, keeps = [], []
    for piece in range(PIECES):
        goal = 2 * core + piece
        here = (goal == plane) & (odd == core)
        send = remote(
            source.at[piece],
            target.at[micro],
            send_sem.at[piece],
            recv_sem.at[micro],
            (odd, rank_of(goal, spot)),
        )
        keep = pltpu.make_async_copy(source.at[piece], target.at[micro], local_sem.at[piece])

        @pl.when(jnp.logical_not(here))
        def _(send=send):
            send.start()

        @pl.when(here)
        def _(keep=keep):
            keep.start()

        sends.append((here, send))
        keeps.append((here, keep))

    def finish():
        for number in range(2):
            mine = (2 * number + core == plane) & (micro == core)
            arrival = remote(
                source.at[0],
                target.at[number],
                send_sem.at[0],
                recv_sem.at[number],
                (core, rank_of(plane, spot)),
            )

            @pl.when(jnp.logical_not(mine))
            def _(arrival=arrival):
                arrival.wait_recv()

        for (here, send), (_, keep) in zip(sends, keeps):

            @pl.when(jnp.logical_not(here))
            def _(send=send):
                send.wait_send()

            @pl.when(here)
            def _(keep=keep):
                keep.wait()

    return finish


class Gather:
    SENDS = 31

    def __init__(self, source, target, send_sem, recv_sem, local_sem):
        self.source, self.target = source, target
        self.send_sem, self.recv_sem = send_sem, recv_sem
        self.core, self.plane, self.spot = place_here()
        self.sends = []
        self.own = pltpu.make_async_copy(
            source, target.at[self.core, self.plane, self.spot], local_sem
        )
        self.own.start()

    def send(self, source, plane, spot, device):
        copy = remote(
            source,
            self.target.at[self.core, plane, spot],
            self.send_sem.at[len(self.sends)],
            self.recv_sem.at[self.core, plane, spot],
            device,
        )
        copy.start()
        self.sends.append(copy)

    def arrive(self, core, plane, spot):
        shard = self.target.at[core, plane, spot]
        remote(
            shard,
            shard,
            self.send_sem.at[0],
            self.recv_sem.at[core, plane, spot],
            (self.core, rank_of(self.plane, self.spot)),
        ).wait_recv()

    def neighbour(self, bits):
        return (self.core, rank_of(self.plane, flip(self.spot, bits)))

    def sibling(self):
        return (1 - self.core, rank_of(self.plane, self.spot))

    def start(self):
        for bits in range(1, PLANES):
            goal = (self.core, rank_of(flip(self.plane, bits), self.spot))
            self.send(self.source, self.plane, self.spot, goal)
        for goal in (self.neighbour(1), self.neighbour(2), self.sibling()):
            self.send(self.source, self.plane, self.spot, goal)

    def column(self):
        for bits in range(1, PLANES):
            plane = flip(self.plane, bits)
            self.arrive(self.core, plane, self.spot)
            shard = self.target.at[self.core, plane, self.spot]
            for goal in (self.neighbour(1), self.neighbour(2), self.sibling()):
                self.send(shard, plane, self.spot, goal)

    def across(self):
        for bits in range(PLANES):
            plane = flip(self.plane, bits)
            for side in (1, 2):
                spot = flip(self.spot, side)
                self.arrive(self.core, plane, spot)
                shard = self.target.at[self.core, plane, spot]
                if (side == 1) == (bits < 2):
                    self.send(shard, plane, spot, self.neighbour(3 - side))
                self.send(shard, plane, spot, self.sibling())

    def corner(self):
        spot = flip(self.spot, 3)
        for bits in range(PLANES):
            plane = flip(self.plane, bits)
            self.arrive(self.core, plane, spot)
            self.send(self.target.at[self.core, plane, spot], plane, spot, self.sibling())

    def finish(self):
        for bits in range(PLANES):
            for side in range(SPOTS):
                self.arrive(1 - self.core, flip(self.plane, bits), flip(self.spot, side))
        self.own.wait()
        for copy in self.sends:
            copy.wait_send()


def settle(shards_ref, plan):
    rows = shards_ref.shape[3] // 2

    def pair(number, carry):
        core, plane, side = (
            lax.div(number, 2 * PLANES),
            lax.rem(lax.div(number, 2), PLANES),
            lax.rem(number, 2),
        )
        goal = pl.ds(pl.multiple_of(number * 2 * rows, 16), 2 * rows)
        for tile, out_ref, (left, right) in plan:
            columns = slice(tile * LANES, (tile + 1) * LANES)
            first = shards_ref[core, plane, 2 * side, :, columns].astype(F32)
            second = shards_ref[core, plane, 2 * side + 1, :, columns].astype(F32)
            out_ref[goal, left * LANES : (left + 1) * LANES] = jnp.concatenate(
                [first[:rows], second[:rows]], axis=0
            ).astype(BF16)
            out_ref[goal, right * LANES : (right + 1) * LANES] = jnp.concatenate(
                [first[rows:], second[rows:]], axis=0
            ).astype(BF16)
        return carry

    lax.fori_loop(0, RANKS // 2, pair, 0)


def alternate(tile):
    return 2 * tile, 2 * tile + 1


def collect_kernel(
    x_ref,
    vec_ref,
    s_qkv_ref,
    xs_ref,
    vecs_ref,
    w_qkv_ref,
    g_qkv_ref,
    send_sem,
    recv_sem,
    local_sem,
    move_send,
    move_recv,
    move_local,
):
    core, plane, spot = place_here()
    greet(all_partners(core, plane, spot))
    gathers = []
    for number, (source, target) in enumerate(((vec_ref, vecs_ref), (s_qkv_ref, g_qkv_ref))):
        one = Gather(
            source, target, send_sem.at[number], recv_sem.at[number], local_sem.at[number]
        )
        one.start()
        gathers.append(one)
    finish_x = to_planes(x_ref, xs_ref, move_send, move_recv, move_local)
    for one in gathers:
        one.column()
    for one in gathers:
        one.across()
    for one in gathers:
        one.corner()
    for one in gathers:
        one.finish()
    settle(g_qkv_ref, [(tile, w_qkv_ref, alternate(tile)) for tile in range(HALF_TILES)])
    finish_x()


def collect(x, vec, s_qkv):
    grid = (2, PLANES, SPOTS)
    return pl.pallas_call(
        collect_kernel,
        out_shape=(
            jax.ShapeDtypeStruct(x.shape, BF16),
            jax.ShapeDtypeStruct(grid + vec.shape, BF16),
            jax.ShapeDtypeStruct((D, 3 * D), BF16),
        ),
        in_specs=[whole(ANY)] * 3,
        out_specs=(whole(ANY), whole(ANY), whole()),
        scratch_shapes=[
            VMEM(grid + s_qkv.shape, BF16),
            pltpu.SemaphoreType.DMA((2, Gather.SENDS)),
            pltpu.SemaphoreType.DMA((2,) + grid),
            pltpu.SemaphoreType.DMA((2,)),
            pltpu.SemaphoreType.DMA((2,)),
            pltpu.SemaphoreType.DMA((2,)),
            pltpu.SemaphoreType.DMA((2,)),
        ],
        compiler_params=pltpu.CompilerParams(
            vmem_limit_bytes=48 * 1024 * 1024, collective_id=1, has_side_effects=True
        ),
        name="collect",
    )(x, vec, s_qkv)


def plane_partners(core, plane, spot):
    partners = []
    for other in (core, 1 - core):
        for side in range(SPOTS):
            if other is core and side == 0:
                continue
            partners.append((other, rank_of(plane, flip(spot, side))))
    return partners


def both_partners(core, plane, spot):
    return plane_partners(core, plane, spot) + column_partners(core, plane, spot)[1:]


def outward_send(source_ref, target_ref, send_sem, recv_sem, local_sem):
    core, plane, spot = place_here()
    sends, keeps = [], []
    for side in (3, 1, 2, 0):
        for other in (core, 1 - core):
            goal = flip(spot, side)
            for piece in range(PIECES):
                source = source_ref.at[other, goal, piece]
                target = target_ref.at[2 * core + piece, spot]
                if side == 0 and other is core:
                    copy = pltpu.make_async_copy(source, target, local_sem.at[piece])
                    keeps.append(copy)
                else:
                    copy = remote(
                        source,
                        target,
                        send_sem.at[len(sends)],
                        recv_sem.at[2 * core + piece, spot],
                        (other, rank_of(plane, goal)),
                    )
                    sends.append(copy)
                copy.start()

    def finish():
        for side in range(SPOTS):
            for other in (core, 1 - core):
                if side == 0 and other is core:
                    continue
                for piece in range(PIECES):
                    target = target_ref.at[2 * other + piece, flip(spot, side)]
                    remote(
                        target,
                        target,
                        send_sem.at[0],
                        recv_sem.at[2 * other + piece, flip(spot, side)],
                        (core, rank_of(plane, spot)),
                    ).wait_recv()
        for copy in sends:
            copy.wait_send()
        for copy in keeps:
            copy.wait()

    return finish


def inward_send(source_ref, target_ref, send_sem, recv_sem, local_sem):
    core, plane, spot = place_here()
    sends, keeps = [], []
    for side in (3, 1, 2, 0):
        for other in (core, 1 - core):
            goal = flip(spot, side)
            for piece in range(PIECES):
                source = source_ref.at[2 * other + piece, goal]
                target = target_ref.at[core, spot, piece]
                if side == 0 and other is core:
                    copy = pltpu.make_async_copy(source, target, local_sem.at[piece])
                    keeps.append(copy)
                else:
                    copy = remote(
                        source,
                        target,
                        send_sem.at[len(sends)],
                        recv_sem.at[core, spot, piece],
                        (other, rank_of(plane, goal)),
                    )
                    sends.append(copy)
                copy.start()

    def finish():
        for side in range(SPOTS):
            for other in (core, 1 - core):
                if side == 0 and other is core:
                    continue
                for piece in range(PIECES):
                    target = target_ref.at[other, flip(spot, side), piece]
                    remote(
                        target,
                        target,
                        send_sem.at[0],
                        recv_sem.at[other, flip(spot, side), piece],
                        (core, rank_of(plane, spot)),
                    ).wait_recv()
        for copy in sends:
            copy.wait_send()
        for copy in keeps:
            copy.wait()

    return finish


def exchange_sems(recv_shape):
    return [
        pltpu.SemaphoreType.DMA((14,)),
        pltpu.SemaphoreType.DMA(recv_shape),
        pltpu.SemaphoreType.DMA((PIECES,)),
    ]


def outward_kernel(source_ref, target_ref, send_sem, recv_sem, local_sem):
    greet(plane_partners(*place_here()))
    outward_send(source_ref, target_ref, send_sem, recv_sem, local_sem)()


def inward_kernel(source_ref, target_ref, send_sem, recv_sem, local_sem):
    greet(plane_partners(*place_here()))
    inward_send(source_ref, target_ref, send_sem, recv_sem, local_sem)()


def plane_exchange(kernel, source, shape, recv_shape, collective, name):
    return pl.pallas_call(
        kernel,
        out_shape=jax.ShapeDtypeStruct(shape, source.dtype),
        in_specs=[whole(ANY)],
        out_specs=whole(ANY),
        scratch_shapes=exchange_sems(recv_shape),
        compiler_params=pltpu.CompilerParams(
            vmem_limit_bytes=16 * 1024 * 1024, collective_id=collective, has_side_effects=True
        ),
        name=name,
    )(source)


def outward(source, collective, name):
    shape = (PLANES, SPOTS) + source.shape[3:]
    return plane_exchange(outward_kernel, source, shape, (PLANES, SPOTS), collective, name)


def inward(source, collective, name):
    shape = (2, SPOTS, PIECES) + source.shape[2:]
    return plane_exchange(
        inward_kernel, source, shape, (2, SPOTS, PIECES), collective, name
    )


def column_send(source, target, send_sem, recv_sem, local_sem):
    core, plane, spot = place_here()
    keep = pltpu.make_async_copy(source, target.at[plane], local_sem)
    keep.start()
    copies = []
    for bits in range(1, PLANES):
        copy = remote(
            source,
            target.at[plane],
            send_sem.at[bits - 1],
            recv_sem.at[plane],
            (core, rank_of(flip(plane, bits), spot)),
        )
        copy.start()
        copies.append(copy)

    def finish():
        for bits in range(1, PLANES):
            other = flip(plane, bits)
            remote(
                source,
                target.at[other],
                send_sem.at[0],
                recv_sem.at[other],
                (core, rank_of(plane, spot)),
            ).wait_recv()
        for copy in copies:
            copy.wait_send()
        keep.wait()

    return finish


def exchange_qkv_kernel(
    source_ref,
    s_ou_ref,
    s_down_ref,
    target_ref,
    c_ou_ref,
    c_down_ref,
    send_sem,
    recv_sem,
    local_sem,
    column_send_sem,
    column_recv_sem,
    column_local_sem,
):
    greet(both_partners(*place_here()))
    finish = outward_send(source_ref, target_ref, send_sem, recv_sem, local_sem)
    finishes = [
        column_send(
            source,
            target,
            column_send_sem.at[number],
            column_recv_sem.at[number],
            column_local_sem.at[number],
        )
        for number, (source, target) in enumerate(
            ((s_ou_ref, c_ou_ref), (s_down_ref, c_down_ref))
        )
    ]
    finish()
    for one in finishes:
        one()


def exchange_qkv(source, s_ou, s_down):
    return pl.pallas_call(
        exchange_qkv_kernel,
        out_shape=(
            jax.ShapeDtypeStruct((PLANES, SPOTS) + source.shape[3:], BF16),
            jax.ShapeDtypeStruct((PLANES,) + s_ou.shape, BF16),
            jax.ShapeDtypeStruct((PLANES,) + s_down.shape, BF16),
        ),
        in_specs=[whole(ANY)] * 3,
        out_specs=(whole(ANY),) * 3,
        scratch_shapes=exchange_sems((PLANES, SPOTS))
        + [
            pltpu.SemaphoreType.DMA((2, PLANES - 1)),
            pltpu.SemaphoreType.DMA((2, PLANES)),
            pltpu.SemaphoreType.DMA((2,)),
        ],
        compiler_params=pltpu.CompilerParams(
            vmem_limit_bytes=16 * 1024 * 1024, collective_id=3, has_side_effects=True
        ),
        name="exchange_qkv",
    )(source, s_ou, s_down)


class PlaneGather:
    SENDS = 3 + 4 + 2

    def __init__(self, column, target, send_sem, recv_sem, local_sem):
        self.column, self.target = column, target
        self.send_sem, self.recv_sem = send_sem, recv_sem
        self.core, self.plane, self.spot = place_here()
        self.sends = []
        self.own = pltpu.make_async_copy(column, target.at[self.core, :, self.spot], local_sem)
        self.own.start()
        for goal in (self.neighbour(1), self.neighbour(2), self.sibling()):
            self.send(column, slice(0, PLANES), self.spot, 0, goal)

    def neighbour(self, bits):
        return (self.core, rank_of(self.plane, flip(self.spot, bits)))

    def sibling(self):
        return (1 - self.core, rank_of(self.plane, self.spot))

    def piece(self, core, planes, spot):
        return self.target.at[core, planes, spot]

    def send(self, source, planes, spot, part, goal):
        copy = remote(
            source,
            self.piece(self.core, planes, spot),
            self.send_sem.at[len(self.sends)],
            self.recv_sem.at[self.core, spot, part],
            goal,
        )
        copy.start()
        self.sends.append(copy)

    def arrive(self, core, planes, spot, part):
        piece = self.piece(core, planes, spot)
        remote(
            piece,
            piece,
            self.send_sem.at[0],
            self.recv_sem.at[core, spot, part],
            (self.core, rank_of(self.plane, self.spot)),
        ).wait_recv()

    def forward(self):
        for side in (1, 2):
            spot = flip(self.spot, side)
            everything = slice(0, PLANES)
            self.arrive(self.core, everything, spot, 0)
            half = slice(0, 2) if side == 1 else slice(2, 4)
            self.send(
                self.piece(self.core, half, spot), half, spot, side - 1, self.neighbour(3 - side)
            )
            self.send(self.piece(self.core, everything, spot), everything, spot, 0, self.sibling())

    def corner(self):
        spot = flip(self.spot, 3)
        for part, half in enumerate((slice(0, 2), slice(2, 4))):
            self.arrive(self.core, half, spot, part)
            self.send(self.piece(self.core, half, spot), half, spot, part, self.sibling())

    def finish(self):
        for side in range(3):
            self.arrive(1 - self.core, slice(0, PLANES), flip(self.spot, side), 0)
        for part, half in enumerate((slice(0, 2), slice(2, 4))):
            self.arrive(1 - self.core, half, flip(self.spot, 3), part)
        self.own.wait()
        for copy in self.sends:
            copy.wait_send()


def sort_entries(table_ref, sorted_ref, entries):
    count = table_ref.shape[1]
    core = lax.axis_index("gx")
    lane = lax.broadcasted_iota(jnp.int32, (count, count), 1)
    row = lax.broadcasted_iota(jnp.int32, (count, count), 0).astype(F32)
    everything = jnp.broadcast_to(table_ref[...].astype(F32), (count, count))
    half = entries // 2
    inside = (lane >= core * half) & (lane < (core + 1) * half)
    lane = lane.astype(F32)
    for number, along in enumerate((everything, jnp.where(inside, everything, 2.0 * LANES))):
        down = along.T
        before = (along < down) | ((along == down) & (lane < row))
        rank = jnp.sum(jnp.where(before, 1.0, 0.0), axis=1, keepdims=True)
        order = jnp.sum(jnp.where(rank == lane, row, 0.0), axis=0, keepdims=True)
        upto = jnp.sum(jnp.where(down <= lane, 1.0, 0.0), axis=0, keepdims=True)
        sorted_ref[2 * number : 2 * number + 1] = order.astype(jnp.int32)
        sorted_ref[2 * number + 1 : 2 * number + 2] = upto.astype(jnp.int32)


def plane_qkv_kernel(
    x_ref, vec_ref, w_ref, bias_ref, table_ref, normed_ref, send_ref, sorted_ref
):
    pieces, rows, _ = x_ref.shape
    sort_entries(table_ref, sorted_ref, PLANES * SPOTS * (rows // BLOCK) * RANDOM)
    values = x_ref[...].reshape(pieces * rows, D).astype(F32)
    normal, _ = norm_parts(values)
    normed_ref[...] = (normal * vec_ref[0:1] + vec_ref[1:2]).astype(BF16)
    low = low_lanes(rows)
    queries = D // LANES
    for chunk in range(HALF_TILES):
        columns = slice(chunk * CHUNK, (chunk + 1) * CHUNK)
        packed = dot(normed_ref[...], w_ref[:, columns]) + bias_ref[:, columns]
        for side in range(2):
            tile = chunk + side * HALF_TILES
            whole_tile = packed[:, side * LANES : (side + 1) * LANES]
            if tile < queries:
                whole_tile = whole_tile.astype(BF16).astype(F32) * SCALE
            for piece in range(pieces):
                part = whole_tile[piece * rows : (piece + 1) * rows]
                if tile < SPOTS:
                    send_ref[0, tile, piece, 0] = part.astype(BF16)
                elif tile < queries:
                    first = 2 * (tile - SPOTS)
                    shared = send_ref[0, first, piece, 0].astype(F32)
                    send_ref[1, first, piece, 0] = jnp.where(low, part, shared).astype(BF16)
                    shared = send_ref[0, first + 1, piece, 0].astype(F32)
                    send_ref[1, first + 1, piece, 0] = jnp.where(
                        low, swap_halves(part), shared
                    ).astype(BF16)
                else:
                    spot, role = (tile - queries) // 3, (tile - queries) % 3
                    if role < 2:
                        send_ref[role, spot, piece, 1] = part.astype(BF16)
                    else:
                        send_ref[0, spot, piece, 2] = part.astype(BF16)
                        send_ref[1, spot, piece, 2] = part.astype(BF16)


def plane_qkv(x, vec, w, bias, table):
    pieces, rows, _ = x.shape
    return pl.pallas_call(
        plane_qkv_kernel,
        out_shape=(
            jax.ShapeDtypeStruct((pieces * rows, D), BF16),
            jax.ShapeDtypeStruct((2, SPOTS, PIECES, 3, rows, LANES), BF16),
            jax.ShapeDtypeStruct((4, table.shape[1]), jnp.int32),
        ),
        in_specs=[whole()] * 5,
        out_specs=(whole(), whole(), whole()),
        compiler_params=params_of(48),
        name="plane_qkv",
    )(x, vec, w, bias, table)


def plane_attend_kernel(
    table_ref,
    qkv_ref,
    dy_ref,
    c_ou_ref,
    c_down_ref,
    back_ref,
    lse_ref,
    dys_ref,
    w_out_ref,
    w_up_ref,
    w_down_ref,
    g_ou_ref,
    out_ref,
    s_ref,
    t_ref,
    send_sem,
    recv_sem,
    local_sem,
    gather_send,
    gather_recv,
    gather_local,
    move_send,
    move_recv,
    move_local,
):
    greet(both_partners(*place_here()))
    gathers = [
        PlaneGather(
            column,
            target,
            gather_send.at[number],
            gather_recv.at[number],
            gather_local.at[number],
        )
        for number, (column, target) in enumerate(
            ((c_ou_ref, g_ou_ref), (c_down_ref, w_down_ref))
        )
    ]
    finish_dy = to_planes(dy_ref, dys_ref, move_send, move_recv, move_local)
    groups, _, local, _, _ = qkv_ref.shape
    blocks = groups * local
    half = blocks // 2
    core = lax.axis_index("gx")
    low = low_lanes(BLOCK)
    masks = [half_mask(True), half_mask(False)]

    def load(component, block):
        return qkv_ref[lax.div(block, local), component, lax.rem(block, local)]

    def store(block, value):
        rank = lax.div(block, local)
        out_ref[lax.div(rank, SPOTS), lax.rem(rank, SPOTS), lax.rem(block, local)] = value.astype(BF16)

    def one(block, slot, ids, bias):
        keys = jnp.concatenate([load(1 + slot, spot) for spot in ids], axis=0)
        scores = dot_rt(load(0, block) * masks[slot], keys) + bias
        top = jnp.max(scores, axis=1, keepdims=True)
        powered = jnp.exp(scores - top)
        total = jnp.sum(powered, axis=1, keepdims=True)
        mixed = dot(powered.astype(BF16), keys) * (1.0 / total)
        return mixed, top + jnp.log(total)

    def sparse(step, carry):
        mine = 1 + step + core * (half - 1)
        other = 1 + step + (1 - core) * (half - 1)
        ids, bias = slots_of(table_ref, 0, mine, blocks)
        far_ids, far_bias = slots_of(table_ref, 0, other, blocks)
        mixed_a, log_a = one(mine, 0, ids, bias)
        mixed_b, log_b = one(mine, 1, ids, bias)
        mixed_c, log_c = one(other, 0, far_ids, far_bias)
        store(mine, jnp.where(low, mixed_b, mixed_a))
        store(other, mixed_c)
        lse_ref[mine] = jnp.where(low, log_a, log_b)
        lse_ref[other] = jnp.where(low, log_c, 0.0)
        return carry

    lax.fori_loop(0, half // 2, sparse, 0)
    gathers[0].forward()
    lax.fori_loop(half // 2, half - 1, sparse, 0)

    spans = blocks // SPAN
    ends = (0, blocks - 1)
    end = core * (blocks - 1)
    query_a = jnp.concatenate([load(0, number) for number in ends], axis=0) * masks[0]
    query_b = load(0, end) * masks[1]

    def keys_at(span, slot):
        return jnp.concatenate(
            [load(1 + slot, span * SPAN + number) for number in range(SPAN)], axis=0
        )

    def first_pass(span, carry):
        top_a, top_b = carry
        scores_a = dot_rt(query_a, keys_at(span, 0))
        scores_b = dot_rt(query_b, keys_at(span, 1))
        s_ref[span] = scores_a
        t_ref[span] = scores_b
        return (
            jnp.maximum(top_a, jnp.max(scores_a, axis=1, keepdims=True)),
            jnp.maximum(top_b, jnp.max(scores_b, axis=1, keepdims=True)),
        )

    top_a, top_b = lax.fori_loop(
        0,
        spans,
        first_pass,
        (jnp.full((2 * BLOCK, 1), NEGATIVE, F32), jnp.full((BLOCK, 1), NEGATIVE, F32)),
    )

    def second_pass(span, carry):
        total_a, mixed_a, total_b, mixed_b = carry
        powered_a = jnp.exp(s_ref[span] - top_a)
        powered_b = jnp.exp(t_ref[span] - top_b)
        return (
            total_a + jnp.sum(powered_a, axis=1, keepdims=True),
            mixed_a + dot(powered_a.astype(BF16), keys_at(span, 0)),
            total_b + jnp.sum(powered_b, axis=1, keepdims=True),
            mixed_b + dot(powered_b.astype(BF16), keys_at(span, 1)),
        )

    total_a, mixed_a, total_b, mixed_b = lax.fori_loop(
        0,
        spans,
        second_pass,
        (
            jnp.zeros((2 * BLOCK, 1), F32),
            jnp.zeros((2 * BLOCK, LANES), F32),
            jnp.zeros((BLOCK, 1), F32),
            jnp.zeros((BLOCK, LANES), F32),
        ),
    )
    mixed_a = mixed_a * (1.0 / total_a)
    mixed_b = mixed_b * (1.0 / total_b)
    log_a = top_a + jnp.log(total_a)
    log_b = top_b + jnp.log(total_b)
    for place, number in enumerate(ends):
        rows = slice(place * BLOCK, (place + 1) * BLOCK)
        store(number, jnp.where(low, mixed_b, mixed_a[rows]))
        lse_ref[number] = jnp.where(low, log_a[rows], log_b)

    gathers[1].forward()
    finish_mixed = inward_send(out_ref, back_ref, send_sem, recv_sem, local_sem)
    gathers[0].corner()
    gathers[0].finish()
    outs = D // LANES // 2
    settle(
        g_ou_ref,
        [(tile, w_out_ref, (tile, outs + tile)) for tile in range(outs)]
        + [(outs + tile, w_up_ref, alternate(tile)) for tile in range(FF // CHUNK)],
    )
    gathers[1].corner()
    gathers[1].finish()
    finish_dy()
    finish_mixed()


def plane_attention(table, qkv, dy, c_ou, c_down):
    groups, _, local, _, _ = qkv.shape
    blocks = groups * local
    spans = blocks // SPAN
    grid = (2, PLANES, SPOTS)
    tile = (local, BLOCK, LANES)
    return pl.pallas_call(
        plane_attend_kernel,
        out_shape=(
            jax.ShapeDtypeStruct((2, SPOTS, PIECES) + tile, BF16),
            jax.ShapeDtypeStruct((blocks, BLOCK, LANES), F32),
            jax.ShapeDtypeStruct(dy.shape, BF16),
            jax.ShapeDtypeStruct((D, D), BF16),
            jax.ShapeDtypeStruct((D, FF), BF16),
            jax.ShapeDtypeStruct(grid + c_down.shape[1:], BF16),
        ),
        in_specs=[whole(pltpu.SMEM), whole(), whole(ANY), whole(ANY), whole(ANY)],
        out_specs=(whole(ANY), whole(), whole(ANY), whole(), whole(), whole(ANY)),
        scratch_shapes=[
            VMEM(grid + c_ou.shape[1:], BF16),
            VMEM((PLANES, SPOTS) + tile, BF16),
            VMEM((spans, 2 * BLOCK, SPAN * BLOCK), F32),
            VMEM((spans, BLOCK, SPAN * BLOCK), F32),
        ]
        + exchange_sems((2, SPOTS, PIECES))
        + [
            pltpu.SemaphoreType.DMA((2, PlaneGather.SENDS)),
            pltpu.SemaphoreType.DMA((2, 2, SPOTS, 2)),
            pltpu.SemaphoreType.DMA((2,)),
            pltpu.SemaphoreType.DMA((2,)),
            pltpu.SemaphoreType.DMA((2,)),
            pltpu.SemaphoreType.DMA((2,)),
        ],
        compiler_params=pltpu.CompilerParams(
            vmem_limit_bytes=56 * 1024 * 1024, collective_id=4, has_side_effects=True
        ),
        name="plane_attention",
    )(table, qkv, dy, c_ou, c_down)


class Outward:
    def __init__(self, source, target, send_sem, recv_sem, local_sem):
        self.target, self.recv_sem, self.send_sem = target, recv_sem, send_sem
        self.core, self.plane, self.spot = place_here()
        self.sends, self.keeps = [], []
        for side in (3, 1, 2, 0):
            for other in (self.core, 1 - self.core):
                goal = flip(self.spot, side)
                for piece in range(PIECES):
                    start = source.at[other, goal, piece]
                    stop = target.at[2 * self.core + piece, self.spot]
                    if side == 0 and other is self.core:
                        copy = pltpu.make_async_copy(start, stop, local_sem.at[piece])
                        self.keeps.append(copy)
                    else:
                        copy = remote(
                            start,
                            stop,
                            send_sem.at[len(self.sends)],
                            recv_sem.at[2 * self.core + piece, self.spot],
                            (other, rank_of(self.plane, goal)),
                        )
                        self.sends.append(copy)
                    copy.start()

    def arrive(self, side):
        for other in (self.core, 1 - self.core):
            if side == 0 and other is self.core:
                for copy in self.keeps:
                    copy.wait()
                continue
            for piece in range(PIECES):
                place = (2 * other + piece, flip(self.spot, side))
                remote(
                    self.target.at[place],
                    self.target.at[place],
                    self.send_sem.at[0],
                    self.recv_sem.at[place],
                    (self.core, rank_of(self.plane, self.spot)),
                ).wait_recv()

    def finish(self):
        for copy in self.sends:
            copy.wait_send()


def inward_targets(core, spot):
    for side in (3, 1, 2, 0):
        for other in (core, 1 - core):
            yield side, other, flip(spot, side), side == 0 and other is core


class Inward:
    def __init__(self, source, target, send_sem, recv_sem, local_sem):
        self.source, self.target = source, target
        self.send_sem, self.recv_sem, self.local_sem = send_sem, recv_sem, local_sem
        self.core, self.plane, self.spot = place_here()
        self.sends, self.keeps = [], []

    def send(self, other, goal, stays, piece, part, parts):
        source = self.source.at[2 * other + piece, goal, parts]
        target = self.target.at[self.core, self.spot, piece, parts]
        if stays:
            copy = pltpu.make_async_copy(source, target, self.local_sem.at[part, piece])
            self.keeps.append(copy)
        else:
            copy = remote(
                source,
                target,
                self.send_sem.at[len(self.sends)],
                self.recv_sem.at[self.core, self.spot, piece, part],
                (other, rank_of(self.plane, goal)),
            )
            self.sends.append(copy)
        copy.start()

    def finish(self, parts_of):
        for side, other, goal, stays in inward_targets(self.core, self.spot):
            if stays:
                continue
            for piece in range(PIECES):
                for part, parts in enumerate(parts_of[0 if other is self.core else 1]):
                    target = self.target.at[other, goal, piece, parts]
                    remote(
                        target,
                        target,
                        self.send_sem.at[0],
                        self.recv_sem.at[other, goal, piece, part],
                        (self.core, rank_of(self.plane, self.spot)),
                    ).wait_recv()
        for copy in self.sends:
            copy.wait_send()
        for copy in self.keeps:
            copy.wait()


KEYS_A, QUERIES, KEYS_B = range(3)


def plane_attend_back_kernel(count, *refs):
    table_ref, sorted_ref, qkv_ref, grad_source_ref, lse_ref, hidden_ref = refs[:6]
    sources, refs = refs[6 : 6 + count], refs[6 + count :]
    back_ref, hidden_out_ref = refs[:2]
    outs, refs = refs[2 : 2 + count], refs[2 + count :]
    buffers, refs = refs[: 7 * count], refs[7 * count :]
    grad_ref, out_ref, sums_ref, shares_ref, walked_ref, sibling_ref = refs[:6]
    scores_refs, refs = refs[6:10], refs[10:]
    reduce_send, reduce_recv, reduce_local = refs[:3]
    grad_sems, back_sems, move_sems, sibling_sems = refs[3:6], refs[6:9], refs[9:12], refs[12:14]

    groups, _, local, _, _ = qkv_ref.shape
    blocks = groups * local
    core, plane, spot = place_here()
    low = low_lanes(BLOCK)
    masks = [half_mask(True), half_mask(False)]

    greet(both_partners(core, plane, spot))
    grads = Outward(grad_source_ref, grad_ref, *grad_sems)
    reduces = [
        Reduce(
            source,
            *buffers[7 * number : 7 * number + 7],
            out,
            (reduce_send.at[number], reduce_recv.at[number], reduce_local.at[number]),
        )
        for number, (source, out) in enumerate(zip(sources, outs))
    ]
    for one in reduces:
        one.start()
    finish_hidden = from_planes(hidden_ref, hidden_out_ref, *move_sems)

    def load(component, block):
        return qkv_ref[lax.div(block, local), component, lax.rem(block, local)]

    def load_grad(block):
        rank = lax.div(block, local)
        return grad_ref[lax.div(rank, SPOTS), lax.rem(rank, SPOTS), lax.rem(block, local)]

    def store(component, block, value):
        rank = lax.div(block, local)
        out_ref[
            lax.div(rank, SPOTS), lax.rem(rank, SPOTS), component, lax.rem(block, local)
        ] = value.astype(BF16)

    def stored(component, block):
        rank = lax.div(block, local)
        return out_ref[
            lax.div(rank, SPOTS), lax.rem(rank, SPOTS), component, lax.rem(block, local)
        ].astype(F32)

    nothing = jnp.zeros((BLOCK, LANES), F32)

    def clear(block, carry):
        for slot in range(2):
            sums_ref[slot, block] = nothing
        return carry

    lax.fori_loop(0, blocks, clear, 0)

    def one_block(block, slot):
        ids, bias = inner_slots(table_ref, block, blocks)
        keys = jnp.concatenate([load(1 + slot, number) for number in ids], axis=0)
        both = jnp.concatenate(
            [load(0, block) * masks[slot], load_grad(block) * masks[1 - slot]], axis=0
        )
        products = dot_rt(both, keys)
        logs = lse_ref[block][:, slot * HEAD_DIM : slot * HEAD_DIM + 1]
        weights = jnp.exp(products[:BLOCK] + bias - logs)
        grad_weights = products[BLOCK:]
        delta = jnp.sum(weights * grad_weights, axis=1, keepdims=True)
        grad_scores = weights * (grad_weights - delta)
        stacked = jnp.concatenate([grad_scores, weights], axis=0).astype(BF16)
        return dot(stacked[:BLOCK], keys), dot_lt(stacked, both)

    fixed = 5

    def rank_blocks(rank, slot):
        first = rank * local
        results = [one_block(first + number, slot) for number in range(local)]

        def share(number, place):
            return results[number][1][place * BLOCK : (place + 1) * BLOCK]

        for shift in range(-1, local + 1):
            parts = [
                share(number, shift - number + 1)
                for number in range(local)
                if 0 <= shift - number + 1 <= 2
            ]
            target = jnp.minimum(jnp.maximum(first + shift, 0), blocks - 1)
            sums_ref[slot, target] += functools.reduce(jnp.add, parts)
        for place, target in ((3, 0), (4, blocks - 1)):
            sums_ref[slot, target] += functools.reduce(
                jnp.add, [share(number, place) for number in range(local)]
            )
        for number in range(local):
            for pick in range(RANDOM):
                shares_ref[slot, (first + number) * RANDOM + pick] = share(number, fixed + pick)
        return [result[0] for result in results]

    def head_a(side):
        def body(number, carry):
            rank = number * SPOTS + flip(spot, side)
            for place, query in enumerate(rank_blocks(rank, 0)):
                store(QUERIES, rank * local + place, query * SCALE)
            return carry

        lax.fori_loop(0, PLANES, body, 0)

    def head_b(number, carry):
        rank = core * (groups // 2) + number
        for place, query in enumerate(rank_blocks(rank, 1)):
            block = rank * local + place
            store(QUERIES, block, jnp.where(low, stored(QUERIES, block), query * SCALE))
        return carry

    spans = blocks // SPAN
    ends = (0, blocks - 1)

    def dense(slot, p_ref, d_ref, numbers):
        both = jnp.concatenate(
            [load(0, number) * masks[slot] for number in numbers]
            + [load_grad(number) * masks[1 - slot] for number in numbers],
            axis=0,
        )
        rows = len(numbers) * BLOCK
        column = slot * HEAD_DIM
        logs = jnp.concatenate(
            [lse_ref[number][:, column : column + 1] for number in numbers], axis=0
        )

        def keys_at(span):
            return jnp.concatenate(
                [load(1 + slot, span * SPAN + number) for number in range(SPAN)], axis=0
            )

        def first_pass(span, delta):
            products = dot_rt(both, keys_at(span))
            weights = jnp.exp(products[:rows] - logs)
            grad_weights = products[rows:]
            p_ref[span] = weights
            d_ref[span] = grad_weights
            return delta + jnp.sum(weights * grad_weights, axis=1, keepdims=True)

        delta = lax.fori_loop(0, spans, first_pass, jnp.zeros((rows, 1), F32), unroll=2)

        def second_pass(span, total):
            weights = p_ref[span]
            grad_scores = weights * (d_ref[span] - delta)
            stacked = jnp.concatenate([grad_scores, weights], axis=0).astype(BF16)
            shares = dot_lt(stacked, both)
            for number in range(SPAN):
                sums_ref[slot, span * SPAN + number] += shares[
                    number * BLOCK : (number + 1) * BLOCK
                ]
            return total + dot(stacked[:rows], keys_at(span))

        total = lax.fori_loop(0, spans, second_pass, jnp.zeros((rows, LANES), F32), unroll=2)
        for place, number in enumerate(numbers):
            query = total[place * BLOCK : (place + 1) * BLOCK] * SCALE
            if slot == 1:
                query = jnp.where(low, stored(QUERIES, number), query)
            store(QUERIES, number, query)

    def walk(slot, length):
        def body(number, total):
            entry = sorted_ref[2 * slot, number]
            earlier = sorted_ref[2 * slot, jnp.maximum(number - 1, 0)]
            keep = jnp.where(table_ref[0, entry] == table_ref[0, earlier], 1.0, 0.0).astype(F32)
            total = total * keep + shares_ref[slot, entry]
            walked_ref[slot, number] = total.astype(BF16)
            return total

        lax.fori_loop(0, length, body, nothing, unroll=4)

    def close(slot, rank, component):
        def body(number, carry):
            block = rank * local + number
            stop = sorted_ref[2 * slot + 1, block]
            start = jnp.where(block == 0, 0, sorted_ref[2 * slot + 1, jnp.maximum(block - 1, 0)])
            some = jnp.where(stop > start, 1.0, 0.0).astype(F32)
            share = walked_ref[slot, jnp.maximum(stop - 1, 0)].astype(F32)
            store(component, block, sums_ref[slot, block] + share * some)
            return carry

        lax.fori_loop(0, local, body, 0, unroll=True)

    back = Inward(out_ref, back_ref, *back_sems)
    own_parts = (slice(0, 1), slice(1, 2), slice(2, 3))
    far_parts = (slice(0, 2),)

    for side in range(SPOTS):
        grads.arrive(side)
        head_a(side)
        if side == 1:
            for one in reduces:
                one.corners()
    dense(0, scores_refs[0], scores_refs[1], ends)
    for one in reduces:
        one.sides()
    walk(0, blocks * RANDOM)
    for side, other, goal, stays in inward_targets(core, spot):
        for piece in range(PIECES):
            close(0, (2 * other + piece) * SPOTS + goal, KEYS_A)
            if other is core:
                back.send(other, goal, stays, piece, 0, own_parts[0])
            else:
                back.send(other, goal, stays, piece, 0, far_parts[0])
    lax.fori_loop(0, groups // 2, head_b, 0)
    dense(1, scores_refs[2], scores_refs[3], (core * (blocks - 1),))
    for side, other, goal, stays in inward_targets(core, spot):
        if other is core:
            for piece in range(PIECES):
                back.send(other, goal, stays, piece, 1, own_parts[1])
    walk(1, blocks * RANDOM // 2)
    for number in range(PIECES):
        for goal in range(SPOTS):
            close(1, (2 * (1 - core) + number) * SPOTS + goal, KEYS_B)
    across = remote(
        out_ref.at[pl.ds(2 * (1 - core), PIECES), :, KEYS_B],
        sibling_ref,
        sibling_sems[0],
        sibling_sems[1],
        (1 - core, rank_of(plane, spot)),
    )
    across.start()
    for number in range(PIECES):
        for goal in range(SPOTS):
            close(1, (2 * core + number) * SPOTS + goal, KEYS_B)
    for one in reduces:
        one.columns()
    across.wait_recv()
    for side, other, goal, stays in inward_targets(core, spot):
        if other is core:
            for piece in range(PIECES):
                place = (2 * core + piece, goal, KEYS_B)
                out_ref[place] = (
                    out_ref[place].astype(F32) + sibling_ref[piece, goal].astype(F32)
                ).astype(BF16)
                back.send(other, goal, stays, piece, 2, own_parts[2])
    for one in reduces:
        one.finish()
    finish_hidden()
    grads.finish()
    across.wait_send()
    back.finish((own_parts, far_parts))


def plane_attention_back(table, sorted_table, qkv, grad_source, lse, hidden, sources):
    groups, _, local, _, _ = qkv.shape
    blocks = groups * local
    spans = blocks // SPAN
    count = len(sources)
    buffers = []
    for source in sources:
        buffers += reduce_scratch(source.shape, source.dtype)
    tile = (local, BLOCK, LANES)
    wide = VMEM((spans, 2 * BLOCK, SPAN * BLOCK), F32)
    thin = VMEM((spans, BLOCK, SPAN * BLOCK), F32)
    dma = pltpu.SemaphoreType.DMA
    return pl.pallas_call(
        functools.partial(plane_attend_back_kernel, count),
        out_shape=(
            jax.ShapeDtypeStruct((2, SPOTS, PIECES, 3) + tile, BF16),
            jax.ShapeDtypeStruct(hidden.shape, BF16),
        )
        + tuple(jax.ShapeDtypeStruct(source.shape[3:], F32) for source in sources),
        in_specs=[
            whole(pltpu.SMEM),
            whole(pltpu.SMEM),
            whole(),
            whole(ANY),
            whole(),
            whole(ANY),
        ]
        + [whole(ANY)] * count,
        out_specs=(whole(ANY), whole(ANY)) + (whole(),) * count,
        scratch_shapes=buffers
        + [
            VMEM((PLANES, SPOTS) + tile, BF16),
            VMEM((PLANES, SPOTS, 3) + tile, BF16),
            VMEM((2, blocks, BLOCK, LANES), F32),
            VMEM((2, blocks * RANDOM, BLOCK, LANES), F32),
            VMEM((2, blocks * RANDOM, BLOCK, LANES), BF16),
            VMEM((PIECES, SPOTS) + tile, BF16),
            wide,
            wide,
            thin,
            thin,
            dma((count, REDUCE_SEMS)),
            dma((count, REDUCE_SEMS)),
            dma((count, 4)),
        ]
        + exchange_sems((PLANES, SPOTS))
        + [
            dma((36,)),
            dma((2, SPOTS, PIECES, 3)),
            dma((3, PIECES)),
            dma((2,)),
            dma((2,)),
            dma((2,)),
            dma,
            dma,
        ],
        compiler_params=pltpu.CompilerParams(
            vmem_limit_bytes=62 * 1024 * 1024, collective_id=5, has_side_effects=True
        ),
        name="plane_attention_back",
    )(table, sorted_table, qkv, grad_source, lse, hidden, *sources)


def by_owner(out_ref, values):
    rows = D // RANKS
    width = values.shape[1] // 2
    for owner in range(RANKS):
        part = values[owner * rows : (owner + 1) * rows]
        out_ref[owner] = jnp.concatenate([part[:, :width], part[:, width:]], axis=0).astype(BF16)


def plane_middle_kernel(
    mixed_in_ref,
    x_ref,
    dy_ref,
    vec_ref,
    w_out_ref,
    up_shift_ref,
    w_up_ref,
    w_down_ref,
    hidden_ref,
    send_ref,
    dres_ref,
    g_out_ref,
    g_up_ref,
    g_down_ref,
    g_up_bias_ref,
    g_small_ref,
    mixed_ref,
    residual_ref,
    second_ref,
    second_t_ref,
    total_ref,
    dsecond_ref,
):
    pieces, rows, _ = x_ref.shape
    tokens = pieces * rows
    step = pl.program_id(0)
    low = low_lanes(rows)
    out_shift, gain, shift, down_shift = (vec_ref[number : number + 1] for number in (4, 5, 6, 7))

    @pl.when(step == 0)
    def _():
        core = lax.axis_index("gx")
        for piece in range(pieces):
            span = slice(piece * rows, (piece + 1) * rows)
            for spot in (0, 2):
                first = [mixed_in_ref[side, spot, piece].astype(F32) for side in range(2)]
                last = [mixed_in_ref[side, spot + 1, piece].astype(F32) for side in range(2)]
                own_first = jnp.where(core == 0, first[0], first[1])
                own_last = jnp.where(core == 0, last[0], last[1])
                tiles = (
                    jnp.where(low, swap_halves(first[0]), first[1]),
                    jnp.where(low, own_first, last[0]),
                    swap_halves(jnp.where(low, own_last, last[1])),
                )
                for number, tile in enumerate(tiles):
                    spread = 3 * (spot // 2) + number
                    mixed_ref[span, spread * LANES : (spread + 1) * LANES] = tile.astype(BF16)
        residual = x_ref[...].reshape(tokens, D).astype(F32) + (
            dot(mixed_ref[...], w_out_ref[...]) + out_shift
        )
        residual_ref[...] = residual
        normal, _ = norm_parts(residual)
        second = normal * gain + shift
        second_ref[...] = second.astype(BF16)
        second_t_ref[...] = second.T.astype(BF16)
        total_ref[...] = jnp.zeros_like(total_ref)
        dsecond_ref[...] = jnp.zeros_like(dsecond_ref)

    w_down = w_down_ref[...].reshape(CHUNK, D)
    upper = dot(second_ref[...], w_up_ref[...]) + up_shift_ref[0]
    factor = 0.7978845608028654
    square = upper * upper
    bent = jnp.tanh(factor * (upper + 0.044715 * (upper * square)))
    middle_half = 0.5 * (1.0 + bent)
    active = (upper * middle_half).astype(BF16)
    slope = middle_half + 0.5 * upper * (1.0 - bent * bent) * (
        factor + (3.0 * 0.044715 * factor) * square
    )
    dy = dy_ref[...]
    total_ref[...] += dot(active, w_down)
    g_down_ref[...] = dot_lt(active, dy).astype(BF16).reshape(g_down_ref.shape)
    dupper = (dot_rt(dy, w_down) * slope).astype(BF16)
    g_up_bias_ref[0] = jnp.sum(dupper.astype(F32), axis=0, keepdims=True)
    by_owner(g_up_ref, dot(second_t_ref[...], dupper))
    dsecond_ref[...] += dot_rt(dupper, w_up_ref[...])

    @pl.when(step == pl.num_programs(0) - 1)
    def _():
        residual = residual_ref[...]
        hidden_ref[...] = (
            (residual + (total_ref[...] + down_shift)).astype(BF16).reshape(x_ref.shape)
        )
        normal, inverse = norm_parts(residual)
        dsecond = dsecond_ref[...]
        grad_out = dy_ref[...].astype(F32)
        g_small_ref[0:1] = jnp.sum(dsecond * normal, axis=0, keepdims=True)
        g_small_ref[1:2] = jnp.sum(dsecond, axis=0, keepdims=True)
        g_small_ref[2:3] = jnp.sum(grad_out, axis=0, keepdims=True)
        dres = grad_out + norm_pull(dsecond, normal, inverse, gain)
        dres_ref[...] = dres
        branch = dres.astype(BF16)
        g_small_ref[3:4] = jnp.sum(branch.astype(F32), axis=0, keepdims=True)
        by_owner(g_out_ref, dot_lt(mixed_ref[...], branch))
        dmixed = dot_rt(branch, w_out_ref[...])
        for piece in range(pieces):
            span = slice(piece * rows, (piece + 1) * rows)
            for spot in (0, 2):
                tiles = [
                    dmixed[span, number * LANES : (number + 1) * LANES]
                    for number in range(3 * (spot // 2), 3 * (spot // 2) + 3)
                ]
                flipped = [swap_halves(tile) for tile in tiles]
                send_ref[0, spot, piece] = jnp.where(low, tiles[1], flipped[0]).astype(BF16)
                send_ref[1, spot, piece] = jnp.where(low, tiles[1], tiles[0]).astype(BF16)
                send_ref[0, spot + 1, piece] = jnp.where(low, flipped[2], tiles[1]).astype(BF16)
                send_ref[1, spot + 1, piece] = flipped[2].astype(BF16)


def plane_middle(mixed_in, x, dy, vec, w_out, up_shift, w_up, w_down):
    pieces, rows, _ = x.shape
    tokens = pieces * rows
    shard = D // RANKS

    def fixed(shape):
        return pl.BlockSpec(shape, lambda step: (0,) * len(shape))

    steps = FF // CHUNK
    down = pl.BlockSpec((2, LANES, D), lambda step: (0, step, 0))
    return pl.pallas_call(
        plane_middle_kernel,
        grid=(steps,),
        out_shape=(
            jax.ShapeDtypeStruct(x.shape, BF16),
            jax.ShapeDtypeStruct(mixed_in.shape, BF16),
            jax.ShapeDtypeStruct((tokens, D), F32),
            jax.ShapeDtypeStruct((RANKS, 2 * shard, D // 2), BF16),
            jax.ShapeDtypeStruct((RANKS, 2 * shard, FF // 2), BF16),
            jax.ShapeDtypeStruct((2, FF // 2, D), BF16),
            jax.ShapeDtypeStruct((steps, 1, CHUNK), F32),
            jax.ShapeDtypeStruct((4, D), F32),
        ),
        in_specs=[
            fixed(mixed_in.shape),
            fixed(x.shape),
            fixed((tokens, D)),
            fixed(vec.shape),
            fixed((D, D)),
            pl.BlockSpec((1, 1, CHUNK), lambda step: (step, 0, 0)),
            pl.BlockSpec((D, CHUNK), lambda step: (0, step)),
            down,
        ],
        out_specs=(
            fixed(x.shape),
            fixed(mixed_in.shape),
            fixed((tokens, D)),
            fixed((RANKS, 2 * shard, D // 2)),
            pl.BlockSpec((RANKS, 2 * shard, LANES), lambda step: (0, 0, step)),
            down,
            pl.BlockSpec((1, 1, CHUNK), lambda step: (step, 0, 0)),
            fixed((4, D)),
        ),
        scratch_shapes=[
            VMEM((tokens, D), BF16),
            VMEM((tokens, D), F32),
            VMEM((tokens, D), BF16),
            VMEM((D, tokens), BF16),
            VMEM((tokens, D), F32),
            VMEM((tokens, D), F32),
        ],
        compiler_params=params_of(56),
        name="plane_middle",
    )(mixed_in, x, dy, vec, w_out, up_shift, w_up, w_down)


class Reduce:
    SENDS = 4 + 2 + 2 + 3
    RECVS = SENDS

    def __init__(self, source, total, near, corner_x, corner_y, side_x, side_y, far, out, sems):
        self.source, self.total, self.near = source, total, near
        self.corner = {1: corner_x, 2: corner_y}
        self.side = {1: side_x, 2: side_y}
        self.far, self.out = far, out
        self.send_sem, self.recv_sem, self.local_sem = sems
        self.core, self.plane, self.spot = place_here()
        self.copies = []
        self.locals = []

    def start(self):
        sibling = (1 - self.core, rank_of(self.plane, self.spot))
        for number, side in enumerate((3, 1, 2, 0)):
            spot = flip(self.spot, side)
            copy = remote(
                self.source.at[1 - self.core, :, spot],
                self.near.at[:, spot],
                self.send_sem.at[number],
                self.recv_sem.at[number],
                sibling,
            )
            copy.start()
            self.copies.append(copy)
            keep = pltpu.make_async_copy(
                self.source.at[self.core, :, spot],
                self.total.at[:, spot],
                self.local_sem.at[number],
            )
            keep.start()
            self.locals.append(keep)

    def take(self, number, side):
        self.copies[number].wait_recv()
        self.locals[number].wait()
        spot = flip(self.spot, side)

        def add(plane, carry):
            self.total[plane, spot] = (
                self.total[plane, spot].astype(F32) + self.near[plane, spot].astype(F32)
            ).astype(self.total.dtype)
            return carry

        lax.fori_loop(0, PLANES, add, 0)

    def corners(self):
        self.take(0, 3)
        spot = flip(self.spot, 3)
        index = 4
        self.corner_copies = []
        for bits in range(PLANES):
            side = 2 if bits < 2 else 1
            self.corner_copies.append(None)
            plane = flip(self.plane, bits)
            copy = remote(
                self.total.at[plane, spot],
                self.corner[side].at[bits % 2],
                self.send_sem.at[index + bits],
                self.recv_sem.at[index + bits],
                (self.core, rank_of(self.plane, flip(self.spot, side))),
            )
            copy.start()
            self.corner_copies[bits] = copy

    def sides(self):
        self.take(1, 1)
        self.take(2, 2)
        self.side_copies = {}
        for side in (1, 2):
            spot = flip(self.spot, side)
            came = 3 - side
            for bits in (0, 1) if came == 2 else (2, 3):
                self.corner_copies[bits].wait_recv()
                plane = flip(self.plane, bits)
                self.total[plane, spot] = (
                    self.total[plane, spot].astype(F32)
                    + self.corner[came][bits % 2].astype(F32)
                ).astype(self.total.dtype)
            copy = remote(
                self.total.at[:, spot],
                self.side[side],
                self.send_sem.at[7 + side],
                self.recv_sem.at[7 + side],
                (self.core, rank_of(self.plane, spot)),
            )
            copy.start()
            self.side_copies[side] = copy

    def columns(self):
        self.take(3, 0)
        for side in (1, 2):
            self.side_copies[side].wait_recv()

        def add(plane, carry):
            self.total[plane, self.spot] = (
                self.total[plane, self.spot].astype(F32)
                + self.side[1][plane].astype(F32)
                + self.side[2][plane].astype(F32)
            ).astype(self.total.dtype)
            return carry

        lax.fori_loop(0, PLANES, add, 0)
        self.far_copies = []
        for bits in range(1, PLANES):
            plane = flip(self.plane, bits)
            copy = remote(
                self.total.at[plane, self.spot],
                self.far.at[bits - 1],
                self.send_sem.at[9 + bits],
                self.recv_sem.at[9 + bits],
                (self.core, rank_of(plane, self.spot)),
            )
            copy.start()
            self.far_copies.append(copy)

    def finish(self):
        value = self.total[self.plane, self.spot].astype(F32)
        for bits in range(1, PLANES):
            self.far_copies[bits - 1].wait_recv()
            value = value + self.far[bits - 1].astype(F32)
        self.out[...] = value
        for copy in self.copies + self.corner_copies + self.far_copies:
            copy.wait_send()
        for side in (1, 2):
            self.side_copies[side].wait_send()


REDUCE_SEMS = 13


def reduce_scratch(shape, kind):
    tail = shape[3:]
    return [
        VMEM((PLANES, SPOTS) + tail, kind),
        VMEM((PLANES, SPOTS) + tail, kind),
        VMEM((2,) + tail, kind),
        VMEM((2,) + tail, kind),
        VMEM((PLANES,) + tail, kind),
        VMEM((PLANES,) + tail, kind),
        VMEM((PLANES - 1,) + tail, kind),
    ]


class Doubling:
    STEPS = 5

    def __init__(self, totals, boxes, send_sem, recv_sem):
        self.totals, self.boxes = totals, boxes
        self.send_sem, self.recv_sem = send_sem, recv_sem
        core, plane, spot = place_here()
        self.partners = (
            (1 - core, rank_of(plane, spot)),
            (core, rank_of(plane, flip(spot, 1))),
            (core, rank_of(plane, flip(spot, 2))),
            (core, rank_of(flip(plane, 1), spot)),
            (core, rank_of(flip(plane, 2), spot)),
        )
        self.copies = []

    def start(self, step):
        self.copies = []
        for number, (total, box) in enumerate(zip(self.totals, self.boxes)):
            copy = remote(
                total,
                box.at[step],
                self.send_sem.at[step, number],
                self.recv_sem.at[step, number],
                self.partners[step],
            )
            copy.start()
            self.copies.append(copy)

    def finish(self, step):
        for copy, total, box in zip(self.copies, self.totals, self.boxes):
            copy.wait()
            total[...] += box[step]


PARTS = 3


def finish_kernel(
    recv_ref,
    normed_ref,
    x_ref,
    dres_hbm,
    vec_ref,
    w_hbm,
    g_mid_ref,
    g_up_bias_ref,
    grad_ref,
    g_qkv_ref,
    rows_out_ref,
    tiles_out_ref,
    *scratch,
):
    sources, scratch = scratch[:PARTS], scratch[PARTS:]
    buffers, scratch = scratch[: 7 * PARTS], scratch[7 * PARTS :]
    packed_ref, dnormed_ref, gradient_ref, dres_ref, w_ref = scratch[:5]
    rows_ref, tiles_ref, rows_box, tiles_box = scratch[5:9]
    send_sem, recv_sem, local_sem, load_sem, sum_send, sum_recv = scratch[9:15]
    move_sems = scratch[15:18]
    pieces, rows, _ = x_ref.shape
    tokens = pieces * rows
    core, plane, spot = place_here()
    low = low_lanes(rows)

    load_w = pltpu.make_async_copy(w_hbm, w_ref, load_sem.at[0])
    load_dres = pltpu.make_async_copy(dres_hbm, dres_ref, load_sem.at[1])
    load_w.start()
    load_dres.start()
    greet(all_partners(core, plane, spot))

    def put(tile, piece, value):
        side, chunk = tile // HALF_TILES, tile % HALF_TILES
        packed_ref[
            piece * rows : (piece + 1) * rows,
            chunk * CHUNK + side * LANES : chunk * CHUNK + (side + 1) * LANES,
        ] = value.astype(BF16)

    for piece in range(pieces):
        seconds = []
        for goal in range(SPOTS):
            first = recv_ref[0, goal, piece, QUERIES].astype(F32)
            second = recv_ref[1, goal, piece, QUERIES].astype(F32)
            put(goal, piece, jnp.where(low, first, jnp.where(core == 0, first, second)))
            seconds.append(second)
            base = D // LANES + 3 * goal
            put(base, piece, recv_ref[0, goal, piece, KEYS_A])
            put(base + 1, piece, recv_ref[1, goal, piece, KEYS_A])
            put(base + 2, piece, recv_ref[core, goal, piece, KEYS_B])
        for number in range(2):
            put(
                SPOTS + number,
                piece,
                jnp.where(low, seconds[2 * number], swap_halves(seconds[2 * number + 1])),
            )

    load_w.wait()
    for chunk in range(HALF_TILES):
        columns = slice(chunk * CHUNK, (chunk + 1) * CHUNK)
        share = dot_rt(packed_ref[:, columns], w_ref[:, columns])
        if chunk == 0:
            dnormed_ref[...] = share
        else:
            dnormed_ref[...] += share
    normal, inverse = norm_parts(x_ref[...].reshape(tokens, D).astype(F32))
    dnormed = dnormed_ref[...]
    load_dres.wait()
    gradient = dres_ref[...] + norm_pull(dnormed, normal, inverse, vec_ref[0:1])
    gradient_ref[...] = gradient.astype(BF16).reshape(x_ref.shape)
    finish_grad = from_planes(gradient_ref, grad_ref, *move_sems)

    rows_ref[0:1] = jnp.sum(dnormed * normal, axis=0, keepdims=True)
    rows_ref[1:2] = jnp.sum(dnormed, axis=0, keepdims=True)
    rows_ref[2:6] = g_mid_ref[...]
    rows_ref[6:8] = jnp.zeros((2, D), F32)
    tiles_ref[...] = jnp.zeros_like(tiles_ref)
    for step in range(FF // CHUNK):
        tiles_ref[step : step + 1] = g_up_bias_ref[step]
    for chunk in range(HALF_TILES):
        number = FF // CHUNK + chunk
        tiles_ref[number : number + 1] = jnp.sum(
            packed_ref[:, chunk * CHUNK : (chunk + 1) * CHUNK].astype(F32), axis=0, keepdims=True
        )
    sums = Doubling((rows_ref, tiles_ref), (rows_box, tiles_box), sum_send, sum_recv)
    sums.start(0)

    width = HALF_TILES // PARTS * LANES
    reduces = [
        Reduce(
            sources[part],
            *buffers[7 * part : 7 * part + 7],
            g_qkv_ref.at[:, part * width : (part + 1) * width],
            (send_sem.at[part], recv_sem.at[part], local_sem.at[part]),
        )
        for part in range(PARTS)
    ]
    shard = D // RANKS
    normed_t = normed_ref[...].astype(F32).T.astype(BF16)
    for part in range(PARTS):
        for number in range(HALF_TILES // PARTS):
            chunk = part * (HALF_TILES // PARTS) + number
            values = dot(normed_t, packed_ref[:, chunk * CHUNK : (chunk + 1) * CHUNK])
            columns = slice(number * LANES, (number + 1) * LANES)
            for owner in range(RANKS):
                mine = values[owner * shard : (owner + 1) * shard]
                sources[part][
                    owner // (PLANES * SPOTS), owner // SPOTS % PLANES, owner % SPOTS, :, columns
                ] = jnp.concatenate([mine[:, :LANES], mine[:, LANES:]], axis=0).astype(BF16)
        reduces[part].start()
        if part > 0:
            reduces[part - 1].corners()
        if part > 1:
            reduces[part - 2].sides()
    sums.finish(0)
    sums.start(1)
    reduces[2].corners()
    reduces[1].sides()
    sums.finish(1)
    sums.start(2)
    reduces[0].columns()
    reduces[2].sides()
    sums.finish(2)
    sums.start(3)
    reduces[1].columns()
    sums.finish(3)
    sums.start(4)
    reduces[2].columns()
    sums.finish(4)
    for one in reduces:
        one.finish()
    rows_out_ref[...] = rows_ref[...]
    tiles_out_ref[...] = tiles_ref[...]
    finish_grad()


def finish_layer(recv, normed, x, dres, vec, w, g_mid, g_up_bias):
    pieces, rows, _ = x.shape
    tokens = pieces * rows
    shard = D // RANKS
    grid = (2, PLANES, SPOTS)
    part = grid + (2 * shard, HALF_TILES // PARTS * LANES)
    buffers = []
    for _ in range(PARTS):
        buffers += reduce_scratch(part, BF16)
    tiles = -(-(FF // CHUNK + HALF_TILES) // 8) * 8
    dma = pltpu.SemaphoreType.DMA
    return pl.pallas_call(
        finish_kernel,
        out_shape=(
            jax.ShapeDtypeStruct(x.shape, BF16),
            jax.ShapeDtypeStruct((2 * shard, 3 * D // 2), F32),
            jax.ShapeDtypeStruct((8, D), F32),
            jax.ShapeDtypeStruct((tiles, CHUNK), F32),
        ),
        in_specs=[
            whole(),
            whole(),
            whole(),
            whole(ANY),
            whole(),
            whole(ANY),
            whole(),
            whole(),
        ],
        out_specs=(whole(ANY), whole(), whole(), whole()),
        scratch_shapes=[VMEM(part, BF16)] * PARTS
        + buffers
        + [
            VMEM((tokens, 3 * D), BF16),
            VMEM((tokens, D), F32),
            VMEM(x.shape, BF16),
            VMEM((tokens, D), F32),
            VMEM(w.shape, BF16),
            VMEM((8, D), F32),
            VMEM((tiles, CHUNK), F32),
            VMEM((Doubling.STEPS, 8, D), F32),
            VMEM((Doubling.STEPS, tiles, CHUNK), F32),
            dma((PARTS, REDUCE_SEMS)),
            dma((PARTS, REDUCE_SEMS)),
            dma((PARTS, 4)),
            dma((2,)),
            dma((Doubling.STEPS, 2)),
            dma((Doubling.STEPS, 2)),
            dma((2,)),
            dma((2,)),
            dma((2,)),
        ],
        compiler_params=pltpu.CompilerParams(
            vmem_limit_bytes=60 * 1024 * 1024, collective_id=2, has_side_effects=True
        ),
        name="finish_layer",
    )(recv, normed, x, dres, vec, w, g_mid, g_up_bias)


def fold_columns(array):
    half = array.shape[1] // 2
    return jnp.concatenate([array[:, :half], array[:, half:]], axis=0)


def unfold_columns(array):
    half = array.shape[0] // 2
    return jnp.concatenate([array[:half], array[half:]], axis=1)


def plane_shards(
    hidden_in,
    rand_table,
    norm1_gain,
    norm1_bias,
    w_qkv,
    query_bias,
    value_bias,
    w_out,
    out_bias,
    norm2_gain,
    norm2_bias,
    w_up,
    up_bias,
    w_down,
    down_bias,
    cotangent,
):
    micro, rows, _ = hidden_in.shape
    local = rows // BLOCK
    own = norm1_gain.shape[0]
    order = [natural_block(entry) for entry in column_order()]
    inverse = [order.index(number) for number in range(len(order))]
    small = (8 + FF // D) * own
    entries = rand_table.size

    vec = jnp.concatenate(
        [
            norm1_gain,
            norm1_bias,
            query_bias,
            value_bias,
            out_bias,
            norm2_gain,
            norm2_bias,
            down_bias,
            up_bias,
            rand_table.reshape(entries).astype(BF16),
            jnp.zeros((16 * LANES - small - entries,), BF16),
        ]
    ).reshape(16, LANES)
    x, vecs, w_qkv_all = collect(hidden_in, vec, fold_columns(take_blocks(w_qkv, order)))
    vecs = vecs.reshape(RANKS, 16 * LANES)
    vectors = vecs[:, : 8 * own].reshape(RANKS, 8, own).swapaxes(0, 1).reshape(8, D).astype(F32)
    up_shift = vecs[:, 8 * own : small].astype(F32).reshape(2, FF // CHUNK, LANES)
    up_shift = up_shift.swapaxes(0, 1).reshape(FF // CHUNK, 1, CHUNK)
    bias = jnp.concatenate([vectors[2:3], jnp.zeros((1, D), F32), vectors[3:4]], axis=1)
    bias = take_blocks(bias, order).reshape(2, HALF_TILES, LANES)
    bias = bias.swapaxes(0, 1).reshape(1, 3 * D)
    plane = lax.div(lax.axis_index("gy"), SPOTS)
    tables = vecs[:, small : small + entries].reshape(2, PLANES * SPOTS, 2, local * RANDOM)
    tables = tables.astype(jnp.int32).transpose(2, 0, 1, 3).reshape(PLANES, 1, -1)
    table = lax.dynamic_index_in_dim(tables, plane, 0, keepdims=False)
    spare = -table.shape[1] % LANES
    table = jnp.pad(table, ((0, 0), (0, spare)), constant_values=2 * LANES)

    normed, send, sorted_table = plane_qkv(x, vectors, w_qkv_all, bias, table)
    s_ou = jnp.concatenate([fold_columns(w_out), fold_columns(w_up)], axis=1)
    qkv, c_ou, c_down = exchange_qkv(send, s_ou, w_down)
    qkv = qkv.reshape(PLANES * SPOTS, 3, local, BLOCK, LANES)
    mixed, lse, dy, w_out_all, w_up_all, w_down_all = plane_attention(
        table, qkv, cotangent, c_ou, c_down
    )
    mixed = mixed.reshape(2, SPOTS, PIECES, rows, LANES)
    hidden, grad_send, dres, g_out, g_up, g_down, g_up_bias, g_mid = plane_middle(
        mixed,
        x,
        dy.reshape(micro * rows, D),
        vectors,
        w_out_all,
        up_shift,
        w_up_all,
        w_down_all.reshape(2, FF // 2, D),
    )
    grid = (2, PLANES, SPOTS)
    dqkv, hidden_out, t_out, t_up, t_down = plane_attention_back(
        table,
        sorted_table,
        qkv,
        grad_send.reshape(2, SPOTS, PIECES, local, BLOCK, LANES),
        lse,
        hidden,
        [
            g_out.reshape(grid + g_out.shape[1:]),
            g_up.reshape(grid + g_up.shape[1:]),
            g_down.reshape(grid + (FF // RANKS, D)),
        ],
    )
    dqkv = dqkv.reshape(2, SPOTS, PIECES, 3, rows, LANES)
    grad_hidden, t_qkv, sum_rows, sum_tiles = finish_layer(
        dqkv, normed, x, dres, vectors, w_qkv_all, g_mid, g_up_bias
    )

    mine = lax.axis_index("gx") * PLANES * SPOTS + lax.axis_index("gy")
    sum_tiles = sum_tiles.reshape(-1, 2, LANES)
    g_bias = sum_tiles[FF // CHUNK : FF // CHUNK + HALF_TILES].swapaxes(0, 1).reshape(1, 3 * D)
    g_bias = take_blocks(g_bias, inverse)
    sum_rows = jnp.concatenate([sum_rows, g_bias[:, :D], g_bias[:, 2 * D :]], axis=0)
    parts = lax.dynamic_slice_in_dim(sum_rows, mine * own, own, 1)
    g_up_bias = sum_tiles[: FF // CHUNK].swapaxes(0, 1).reshape(FF)
    g_up_bias = lax.dynamic_slice_in_dim(g_up_bias, mine * (FF // RANKS), FF // RANKS, 0)
    return (
        hidden_out,
        grad_hidden.astype(F32),
        parts[0],
        parts[1],
        take_blocks(unfold_columns(t_qkv), inverse),
        parts[8],
        parts[9],
        unfold_columns(t_out),
        parts[5],
        parts[2],
        parts[3],
        unfold_columns(t_up),
        g_up_bias,
        t_down,
        parts[4],
    )


def shards(*arrays):
    micro, rows, _ = arrays[0].shape
    fits = lax.axis_size("gx") == 2 and lax.axis_size("gy") == PLANES * SPOTS
    fits = fits and micro == 2 and rows % BLOCK == 0
    return (plane_shards if fits else general_shards)(*arrays)


def solution(mesh):
    tokens = P(None, AXES, None)
    vector = P(AXES)
    matrix = P(AXES, None)
    placed = (
        tokens,
        tokens,
        vector,
        vector,
        matrix,
        vector,
        vector,
        matrix,
        vector,
        vector,
        vector,
        matrix,
        vector,
        matrix,
        vector,
        tokens,
    )
    returned = (
        tokens,
        tokens,
        vector,
        vector,
        matrix,
        vector,
        vector,
        matrix,
        vector,
        vector,
        vector,
        matrix,
        vector,
        matrix,
        vector,
    )
    return jax.shard_map(
        shards, mesh=mesh, in_specs=placed, out_specs=returned, check_vma=False
    )
```

```python
import functools

import jax
import jax.numpy as jnp
from jax import lax
from jax.experimental import pallas as pl
from jax.experimental.pallas import tpu as pltpu
from jax.sharding import PartitionSpec as P

HEADS = 12
HEAD_DIM = 64
D = 768
FF = 3072
BLOCK = 64
RANDOM = 3
LANES = 2 * HEAD_DIM
EPSILON = 1e-05
NEGATIVE = -1e30
SCALE = HEAD_DIM**-0.5
CHUNK = 256
SPAN = 8

F32 = jnp.float32
BF16 = jnp.bfloat16
VMEM = pltpu.VMEM


def whole(space=VMEM):
    return pl.BlockSpec(memory_space=space)


def params_of(megabytes):
    return pltpu.CompilerParams(vmem_limit_bytes=megabytes * 1024 * 1024)


def head_place(head):
    return (head // 3) * 4 + head % 3


def dot(left, right):
    return lax.dot_general(left, right, (((1,), (0,)), ((), ())), preferred_element_type=F32)


def dot_rt(left, right):
    return lax.dot_general(left, right, (((1,), (1,)), ((), ())), preferred_element_type=F32)


def dot_lt(left, right):
    return lax.dot_general(left, right, (((0,), (0,)), ((), ())), preferred_element_type=F32)


def swap_halves(tile):
    return pltpu.roll(tile, HEAD_DIM, axis=tile.ndim - 1)


def low_lanes(rows):
    return lax.broadcasted_iota(jnp.int32, (rows, LANES), 1) < HEAD_DIM


def norm_parts(values):
    centre = values - jnp.mean(values, axis=-1, keepdims=True)
    spread = jnp.mean(centre * centre, axis=-1, keepdims=True)
    inverse = lax.rsqrt(spread + EPSILON)
    return centre * inverse, inverse


def norm_pull(grad, normal, inverse, gain):
    scaled = grad * gain
    return inverse * (
        scaled
        - jnp.mean(scaled, axis=-1, keepdims=True)
        - normal * jnp.mean(scaled * normal, axis=-1, keepdims=True)
    )


def qkv_kernel(x_ref, gain_ref, shift_ref, w_ref, bias_ref, normed_ref, send_ref):
    micro, rows, _ = x_ref.shape
    values = x_ref[...].reshape(micro * rows, D).astype(F32)
    normal, _ = norm_parts(values)
    normed_ref[...] = (normal * gain_ref[...] + shift_ref[...]).astype(BF16)
    low = low_lanes(rows)
    for chunk in range(3 * D // CHUNK):
        columns = slice(chunk * CHUNK, (chunk + 1) * CHUNK)
        packed = dot(normed_ref[...], w_ref[:, columns]) + bias_ref[:, columns]
        if chunk < D // CHUNK:
            packed = packed.astype(BF16).astype(F32) * SCALE
        for tile in range(CHUNK // LANES):
            part = packed[:, tile * LANES : (tile + 1) * LANES]
            first, second = part[:rows], part[rows:]
            if chunk < D // CHUNK:
                head = (chunk * CHUNK // LANES + tile) * 2
                even = jnp.where(low, first, swap_halves(second))
                odd = jnp.where(low, swap_halves(first), second)
                send_ref[head_place(head), 0] = even.astype(BF16)
                send_ref[head_place(head + 1), 0] = odd.astype(BF16)
            else:
                head = (chunk * CHUNK - D) // LANES + tile
                send_ref[head_place(head), 1] = first.astype(BF16)
                send_ref[head_place(head), 2] = swap_halves(second).astype(BF16)


def qkv_forward(x, gain, shift, w, bias, groups):
    micro, rows, _ = x.shape
    return pl.pallas_call(
        qkv_kernel,
        out_shape=(
            jax.ShapeDtypeStruct((micro * rows, D), BF16),
            jax.ShapeDtypeStruct((groups, 3, rows, LANES), BF16),
        ),
        in_specs=[whole()] * 5,
        out_specs=(whole(), whole()),
        compiler_params=params_of(48),
        name="qkv_forward",
    )(x, gain, shift, w, bias)


def half_mask(low_half):
    lane = lax.broadcasted_iota(jnp.int32, (1, LANES), 1)
    keep = (lane < HEAD_DIM) if low_half else (lane >= HEAD_DIM)
    return jnp.where(keep, 1.0, 0.0).astype(BF16)


def inner_slots(pick, block, blocks):
    ids, bias = picked_slots([pick(block, number) for number in range(RANDOM)], block, blocks)
    edge = (block == 0) | (block == blocks - 1)
    ids[0] = jnp.maximum(ids[0], 0)
    ids[2] = jnp.minimum(ids[2], blocks - 1)
    return ids, bias + jnp.where(edge, NEGATIVE, 0.0).astype(F32)


def slots_of(table_ref, micro, block, blocks):
    picks = [table_ref[micro, block * RANDOM + number] for number in range(RANDOM)]
    return picked_slots(picks, block, blocks)


def picked_slots(picks, block, blocks):
    last = blocks - 1
    ids = [block - 1, block, block + 1, 0, last] + picks
    dropped = [None, None, None, block == 1, block == last - 1]
    for number in range(RANDOM):
        pick = picks[number]
        bad = (jnp.abs(pick - block) <= 1) | (pick == 0) | (pick == last)
        for earlier in range(number):
            bad = bad | (pick == picks[earlier])
        dropped.append(bad)
    lane = lax.broadcasted_iota(jnp.int32, (1, LANES), 1)
    tiles = []
    for pair in range(len(ids) // 2):
        level = [
            0.0 if bad is None else jnp.where(bad, NEGATIVE, 0.0).astype(F32)
            for bad in dropped[2 * pair : 2 * pair + 2]
        ]
        tiles.append(jnp.where(lane < HEAD_DIM, level[0], level[1]))
    return ids, jnp.concatenate(tiles, axis=1)


def attend_kernel(table_ref, qkv_ref, out_ref, lse_ref, s_ref):
    groups, _, local, _, _ = qkv_ref.shape
    blocks = groups * local
    low = low_lanes(BLOCK)
    masks = [half_mask(True), half_mask(False)]

    def load(component, block):
        return qkv_ref[block // local, component, block % local]

    def sparse(block, carry):
        mixed, logs = [], []
        for micro in range(2):
            ids, bias = slots_of(table_ref, micro, block, blocks)
            keys = jnp.concatenate([load(1 + micro, spot) for spot in ids], axis=0)
            query = load(0, block) * masks[micro]
            scores = dot_rt(query, keys) + bias
            top = jnp.max(scores, axis=1, keepdims=True)
            powered = jnp.exp(scores - top)
            total = jnp.sum(powered, axis=1, keepdims=True)
            mixed.append(dot(powered.astype(BF16), keys) * (1.0 / total))
            logs.append(top + jnp.log(total))
        out_ref[block // local, block % local] = jnp.where(low, mixed[1], mixed[0]).astype(BF16)
        lse_ref[block] = jnp.where(low, logs[0], logs[1])
        return carry

    lax.fori_loop(1, blocks - 1, sparse, 0)

    spans = blocks // SPAN
    ends = (0, blocks - 1)
    results = []
    for micro in range(2):
        query = jnp.concatenate([load(0, end) for end in ends], axis=0) * masks[micro]

        def keys_at(span, micro=micro):
            return jnp.concatenate(
                [load(1 + micro, span * SPAN + spot) for spot in range(SPAN)], axis=0
            )

        def first_pass(span, top, query=query, keys_at=keys_at):
            scores = dot_rt(query, keys_at(span))
            s_ref[span] = scores
            return jnp.maximum(top, jnp.max(scores, axis=1, keepdims=True))

        top = lax.fori_loop(0, spans, first_pass, jnp.full((2 * BLOCK, 1), NEGATIVE, F32))

        def second_pass(span, carry, top=top, keys_at=keys_at):
            total, mixed = carry
            powered = jnp.exp(s_ref[span] - top)
            return (
                total + jnp.sum(powered, axis=1, keepdims=True),
                mixed + dot(powered.astype(BF16), keys_at(span)),
            )

        total, mixed = lax.fori_loop(
            0,
            spans,
            second_pass,
            (jnp.zeros((2 * BLOCK, 1), F32), jnp.zeros((2 * BLOCK, LANES), F32)),
        )
        results.append((mixed * (1.0 / total), top + jnp.log(total)))
    for place, end in enumerate(ends):
        rows = slice(place * BLOCK, (place + 1) * BLOCK)
        out_ref[end // local, end % local] = jnp.where(
            low, results[1][0][rows], results[0][0][rows]
        ).astype(BF16)
        lse_ref[end] = jnp.where(low, results[0][1][rows], results[1][1][rows])


def attention_forward(table, qkv):
    groups, _, local, _, _ = qkv.shape
    blocks = groups * local
    return pl.pallas_call(
        attend_kernel,
        out_shape=(
            jax.ShapeDtypeStruct((groups, local, BLOCK, LANES), BF16),
            jax.ShapeDtypeStruct((blocks, BLOCK, LANES), F32),
        ),
        in_specs=[whole(pltpu.SMEM), whole()],
        out_specs=(whole(), whole()),
        scratch_shapes=[VMEM((blocks // SPAN, 2 * BLOCK, SPAN * BLOCK), F32)],
        compiler_params=params_of(48),
        name="attention_forward",
    )(table, qkv)


def attend_back_kernel(table_ref, qkv_ref, grad_ref, lse_ref, out_ref, sums_ref, p_ref, dp_ref):
    groups, _, local, _, _ = qkv_ref.shape
    blocks = groups * local
    low = low_lanes(BLOCK)
    masks = [half_mask(True), half_mask(False)]

    def load(component, block):
        return qkv_ref[block // local, component, block % local]

    def load_grad(block):
        return grad_ref[block // local, block % local]

    def clear(block, carry):
        for micro in range(2):
            sums_ref[micro, block] = jnp.zeros((BLOCK, LANES), F32)
        return carry

    lax.fori_loop(0, blocks, clear, 0)

    def sparse(block, carry):
        grads = []
        for micro in range(2):
            ids, bias = slots_of(table_ref, micro, block, blocks)
            keys = jnp.concatenate([load(1 + micro, spot) for spot in ids], axis=0)
            both = jnp.concatenate(
                [load(0, block) * masks[micro], load_grad(block) * masks[1 - micro]], axis=0
            )
            products = dot_rt(both, keys)
            logs = lse_ref[block][:, micro * HEAD_DIM : micro * HEAD_DIM + 1]
            weights = jnp.exp(products[:BLOCK] + bias - logs)
            grad_weights = products[BLOCK:]
            delta = jnp.sum(weights * grad_weights, axis=1, keepdims=True)
            grad_scores = weights * (grad_weights - delta)
            stacked = jnp.concatenate([grad_scores, weights], axis=0).astype(BF16)
            grads.append(dot(stacked[:BLOCK], keys))
            shares = dot_lt(stacked, both)
            for place, spot in enumerate(ids):
                sums_ref[micro, spot] += shares[place * BLOCK : (place + 1) * BLOCK]
        out_ref[block // local, 0, block % local] = (
            jnp.where(low, grads[0], grads[1]) * SCALE
        ).astype(BF16)
        return carry

    lax.fori_loop(1, blocks - 1, sparse, 0)

    spans = blocks // SPAN
    ends = (0, blocks - 1)
    results = []
    for micro in range(2):
        query = jnp.concatenate([load(0, end) for end in ends], axis=0) * masks[micro]
        grad = jnp.concatenate([load_grad(end) for end in ends], axis=0) * masks[1 - micro]
        both = jnp.concatenate([query, grad], axis=0)
        logs = jnp.concatenate(
            [lse_ref[end][:, micro * HEAD_DIM : micro * HEAD_DIM + 1] for end in ends], axis=0
        )

        def keys_at(span, micro=micro):
            return jnp.concatenate(
                [load(1 + micro, span * SPAN + spot) for spot in range(SPAN)], axis=0
            )

        def first_pass(span, delta, both=both, logs=logs, keys_at=keys_at):
            products = dot_rt(both, keys_at(span))
            weights = jnp.exp(products[: 2 * BLOCK] - logs)
            grad_weights = products[2 * BLOCK :]
            p_ref[span] = weights
            dp_ref[span] = grad_weights
            return delta + jnp.sum(weights * grad_weights, axis=1, keepdims=True)

        delta = lax.fori_loop(0, spans, first_pass, jnp.zeros((2 * BLOCK, 1), F32))

        def second_pass(span, carry, delta=delta, both=both, keys_at=keys_at, micro=micro):
            weights = p_ref[span]
            grad_scores = weights * (dp_ref[span] - delta)
            stacked = jnp.concatenate([grad_scores, weights], axis=0).astype(BF16)
            shares = dot_lt(stacked, both)
            for spot in range(SPAN):
                sums_ref[micro, span * SPAN + spot] += shares[spot * BLOCK : (spot + 1) * BLOCK]
            return carry + dot(stacked[: 2 * BLOCK], keys_at(span))

        results.append(
            lax.fori_loop(0, spans, second_pass, jnp.zeros((2 * BLOCK, LANES), F32))
        )
    for place, end in enumerate(ends):
        rows = slice(place * BLOCK, (place + 1) * BLOCK)
        out_ref[end // local, 0, end % local] = (
            jnp.where(low, results[0][rows], results[1][rows]) * SCALE
        ).astype(BF16)

    def finish(block, carry):
        for micro in range(2):
            out_ref[block // local, 1 + micro, block % local] = sums_ref[micro, block].astype(BF16)
        return carry

    lax.fori_loop(0, blocks, finish, 0)


def attention_backward(table, qkv, grad, lse):
    groups, _, local, _, _ = qkv.shape
    blocks = groups * local
    spans = VMEM((blocks // SPAN, 2 * BLOCK, SPAN * BLOCK), F32)
    return pl.pallas_call(
        attend_back_kernel,
        out_shape=jax.ShapeDtypeStruct(qkv.shape, BF16),
        in_specs=[whole(pltpu.SMEM), whole(), whole(), whole()],
        out_specs=whole(),
        scratch_shapes=[VMEM((2, blocks, BLOCK, LANES), F32), spans, spans],
        compiler_params=params_of(48),
        name="attention_backward",
    )(table, qkv, grad, lse)


def middle_kernel(
    mixed_in_ref,
    x_ref,
    dy_ref,
    w_out_ref,
    out_shift_ref,
    gain_ref,
    shift_ref,
    up_shift_ref,
    down_shift_ref,
    w_up_ref,
    w_down_ref,
    hidden_ref,
    send_ref,
    dres_ref,
    g_out_ref,
    g_up_ref,
    g_down_ref,
    g_up_bias_ref,
    g_small_ref,
    mixed_ref,
    residual_ref,
    second_ref,
    second_t_ref,
    total_ref,
    dsecond_ref,
):
    micro, rows, _ = x_ref.shape
    step = pl.program_id(0)
    low = low_lanes(rows)

    @pl.when(step == 0)
    def _():
        for pair in range(HEADS // 2):
            even = mixed_in_ref[head_place(2 * pair)].astype(F32)
            odd = mixed_in_ref[head_place(2 * pair + 1)].astype(F32)
            columns = slice(pair * LANES, (pair + 1) * LANES)
            mixed_ref[:rows, columns] = jnp.where(low, swap_halves(even), odd).astype(BF16)
            mixed_ref[rows:, columns] = jnp.where(low, even, swap_halves(odd)).astype(BF16)
        residual = x_ref[...].reshape(micro * rows, D).astype(F32) + (
            dot(mixed_ref[...], w_out_ref[...]) + out_shift_ref[...]
        )
        residual_ref[...] = residual
        normal, _ = norm_parts(residual)
        second = normal * gain_ref[...] + shift_ref[...]
        second_ref[...] = second.astype(BF16)
        second_t_ref[...] = second.T.astype(BF16)
        total_ref[...] = jnp.zeros_like(total_ref)
        dsecond_ref[...] = jnp.zeros_like(dsecond_ref)

    upper = dot(second_ref[...], w_up_ref[...]) + up_shift_ref[...]
    factor = 0.7978845608028654
    square = upper * upper
    bent = jnp.tanh(factor * (upper + 0.044715 * (upper * square)))
    half = 0.5 * (1.0 + bent)
    active = (upper * half).astype(BF16)
    slope = half + 0.5 * upper * (1.0 - bent * bent) * (
        factor + (3.0 * 0.044715 * factor) * square
    )
    dy = dy_ref[...]
    total_ref[...] += dot(active, w_down_ref[...])
    g_down_ref[...] = dot_lt(active, dy).astype(g_down_ref.dtype)
    dupper = (dot_rt(dy, w_down_ref[...]) * slope).astype(BF16)
    g_up_bias_ref[...] = jnp.sum(dupper.astype(F32), axis=0, keepdims=True)
    g_up_ref[...] = dot(second_t_ref[...], dupper).astype(g_up_ref.dtype)
    dsecond_ref[...] += dot_rt(dupper, w_up_ref[...])

    @pl.when(step == pl.num_programs(0) - 1)
    def _():
        residual = residual_ref[...]
        hidden_ref[...] = (
            (residual + (total_ref[...] + down_shift_ref[...])).astype(BF16).reshape(x_ref.shape)
        )
        normal, inverse = norm_parts(residual)
        dsecond = dsecond_ref[...]
        grad_out = dy_ref[...].astype(F32)
        g_small_ref[0:1] = jnp.sum(dsecond * normal, axis=0, keepdims=True)
        g_small_ref[1:2] = jnp.sum(dsecond, axis=0, keepdims=True)
        g_small_ref[2:3] = jnp.sum(grad_out, axis=0, keepdims=True)
        dres = grad_out + norm_pull(dsecond, normal, inverse, gain_ref[...])
        dres_ref[...] = dres
        branch = dres.astype(BF16)
        g_small_ref[3:4] = jnp.sum(branch.astype(F32), axis=0, keepdims=True)
        g_out_ref[...] = dot_lt(mixed_ref[...], branch).astype(g_out_ref.dtype)
        dmixed = dot_rt(branch, w_out_ref[...])
        for pair in range(HEADS // 2):
            part = dmixed[:, pair * LANES : (pair + 1) * LANES]
            first, last = part[:rows], part[rows:]
            even = jnp.where(low, last, swap_halves(first))
            odd = jnp.where(low, swap_halves(last), first)
            send_ref[head_place(2 * pair)] = even.astype(BF16)
            send_ref[head_place(2 * pair + 1)] = odd.astype(BF16)


def middle(mixed_in, x, dy, w_out, out_shift, gain, shift, up_shift, down_shift, w_up, w_down, kind):
    micro, rows, _ = x.shape
    tokens = micro * rows
    groups = mixed_in.shape[0]

    def fixed(shape):
        return pl.BlockSpec(shape, lambda step: (0,) * len(shape))

    vector = fixed((1, D))
    steps = FF // CHUNK
    return pl.pallas_call(
        middle_kernel,
        grid=(steps,),
        out_shape=(
            jax.ShapeDtypeStruct(x.shape, BF16),
            jax.ShapeDtypeStruct((groups, rows, LANES), BF16),
            jax.ShapeDtypeStruct((tokens, D), F32),
            jax.ShapeDtypeStruct((D, D), kind),
            jax.ShapeDtypeStruct((D, FF), kind),
            jax.ShapeDtypeStruct((FF, D), kind),
            jax.ShapeDtypeStruct((1, FF), F32),
            jax.ShapeDtypeStruct((4, D), F32),
        ),
        in_specs=[
            fixed(mixed_in.shape),
            fixed(x.shape),
            fixed((tokens, D)),
            fixed((D, D)),
            vector,
            vector,
            vector,
            pl.BlockSpec((1, CHUNK), lambda step: (0, step)),
            vector,
            pl.BlockSpec((D, CHUNK), lambda step: (0, step)),
            pl.BlockSpec((CHUNK, D), lambda step: (step, 0)),
        ],
        out_specs=(
            fixed(x.shape),
            fixed((groups, rows, LANES)),
            fixed((tokens, D)),
            fixed((D, D)),
            pl.BlockSpec((D, CHUNK), lambda step: (0, step)),
            pl.BlockSpec((CHUNK, D), lambda step: (step, 0)),
            pl.BlockSpec((1, CHUNK), lambda step: (0, step)),
            fixed((4, D)),
        ),
        scratch_shapes=[
            VMEM((tokens, D), BF16),
            VMEM((tokens, D), F32),
            VMEM((tokens, D), BF16),
            VMEM((D, tokens), BF16),
            VMEM((tokens, D), F32),
            VMEM((tokens, D), F32),
        ],
        compiler_params=params_of(56),
        name="middle",
    )(mixed_in, x, dy, w_out, out_shift, gain, shift, up_shift, down_shift, w_up, w_down)


def qkv_back_kernel(
    recv_ref,
    normed_ref,
    x_ref,
    dres_ref,
    gain_ref,
    w_ref,
    grad_ref,
    g_qkv_ref,
    g_bias_ref,
    g_small_ref,
    packed_ref,
    normed_t_ref,
    dnormed_ref,
):
    micro, rows, _ = x_ref.shape
    step = pl.program_id(0)
    low = low_lanes(rows)

    @pl.when(step == 0)
    def _():
        for pair in range(HEADS // 2):
            even = recv_ref[head_place(2 * pair), 0].astype(F32)
            odd = recv_ref[head_place(2 * pair + 1), 0].astype(F32)
            spot, columns = pair // 2, slice((pair % 2) * LANES, (pair % 2 + 1) * LANES)
            packed_ref[spot, :rows, columns] = jnp.where(low, even, swap_halves(odd)).astype(BF16)
            packed_ref[spot, rows:, columns] = jnp.where(low, swap_halves(even), odd).astype(BF16)
        for head in range(HEADS):
            spot = D // CHUNK + head // 2
            columns = slice((head % 2) * LANES, (head % 2 + 1) * LANES)
            packed_ref[spot, :rows, columns] = recv_ref[head_place(head), 1]
            packed_ref[spot, rows:, columns] = swap_halves(
                recv_ref[head_place(head), 2].astype(F32)
            ).astype(BF16)
        normed_t_ref[...] = normed_ref[...].astype(F32).T.astype(BF16)
        dnormed_ref[...] = jnp.zeros_like(dnormed_ref)

    packed = packed_ref[step]
    g_bias_ref[...] = jnp.sum(packed.astype(F32), axis=0, keepdims=True)
    g_qkv_ref[...] = dot(normed_t_ref[...], packed).astype(g_qkv_ref.dtype)
    dnormed_ref[...] += dot_rt(packed, w_ref[...])

    @pl.when(step == pl.num_programs(0) - 1)
    def _():
        normal, inverse = norm_parts(x_ref[...].reshape(micro * rows, D).astype(F32))
        dnormed = dnormed_ref[...]
        g_small_ref[0:1] = jnp.sum(dnormed * normal, axis=0, keepdims=True)
        g_small_ref[1:2] = jnp.sum(dnormed, axis=0, keepdims=True)
        grad = dres_ref[...] + norm_pull(dnormed, normal, inverse, gain_ref[...])
        grad_ref[...] = grad.reshape(x_ref.shape)


def qkv_backward(recv, normed, x, dres, gain, w, kind):
    micro, rows, _ = x.shape
    tokens = micro * rows

    def fixed(shape):
        return pl.BlockSpec(shape, lambda step: (0,) * len(shape))

    steps = 3 * D // CHUNK
    return pl.pallas_call(
        qkv_back_kernel,
        grid=(steps,),
        out_shape=(
            jax.ShapeDtypeStruct(x.shape, F32),
            jax.ShapeDtypeStruct((D, 3 * D), kind),
            jax.ShapeDtypeStruct((1, 3 * D), F32),
            jax.ShapeDtypeStruct((2, D), F32),
        ),
        in_specs=[
            fixed(recv.shape),
            fixed((tokens, D)),
            fixed(x.shape),
            fixed((tokens, D)),
            fixed((1, D)),
            pl.BlockSpec((D, CHUNK), lambda step: (0, step)),
        ],
        out_specs=(
            fixed(x.shape),
            pl.BlockSpec((D, CHUNK), lambda step: (0, step)),
            pl.BlockSpec((1, CHUNK), lambda step: (0, step)),
            fixed((2, D)),
        ),
        scratch_shapes=[
            VMEM((steps, tokens, CHUNK), BF16),
            VMEM((D, tokens), BF16),
            VMEM((tokens, D), F32),
        ],
        compiler_params=params_of(56),
        name="qkv_backward",
    )(recv, normed, x, dres, gain, w)


AXES = ("gx", "gy")


def gather(array):
    return lax.all_gather(array, AXES, axis=0, tiled=True)


def scatter(array):
    return lax.psum_scatter(array, AXES, scatter_dimension=0, tiled=True)


def exchange(array):
    return lax.all_to_all(array, "gy", 0, 0, tiled=True)


def by_heads(w_qkv):
    rows = w_qkv.shape[0]
    sides = w_qkv[:, D:].reshape(rows, 2, HEADS, HEAD_DIM)
    return jnp.concatenate([w_qkv[:, :D], jnp.swapaxes(sides, 1, 2).reshape(rows, 2 * D)], axis=1)


def by_parts(w_qkv):
    rows = w_qkv.shape[0]
    sides = w_qkv[:, D:].reshape(rows, HEADS, 2, HEAD_DIM)
    return jnp.concatenate([w_qkv[:, :D], jnp.swapaxes(sides, 1, 2).reshape(rows, 2 * D)], axis=1)


def general_shards(
    hidden_in,
    rand_table,
    norm1_gain,
    norm1_bias,
    w_qkv,
    query_bias,
    value_bias,
    w_out,
    out_bias,
    norm2_gain,
    norm2_bias,
    w_up,
    up_bias,
    w_down,
    down_bias,
    cotangent,
):
    micro, rows, _ = hidden_in.shape
    groups = lax.axis_size("gy")
    local = rows // BLOCK
    own = norm1_gain.shape[0]

    vectors = jnp.concatenate(
        [
            norm1_gain,
            norm1_bias,
            query_bias,
            value_bias,
            out_bias,
            norm2_gain,
            norm2_bias,
            down_bias,
            up_bias,
        ]
    )
    table = lax.all_gather(rand_table, "gy", axis=1, tiled=True)
    table = table.reshape(micro, groups * local * RANDOM)
    vectors = gather(vectors[None]).astype(F32)
    gain_one, shift_one, query_shift, value_shift, out_shift, gain_two, shift_two, down_shift = (
        vectors[:, number * own : (number + 1) * own].reshape(1, D) for number in range(8)
    )
    up_shift = vectors[:, 8 * own :].reshape(1, FF)
    w_qkv_full = gather(by_heads(w_qkv))
    w_out_full, w_up_full, w_down_full = gather(w_out), gather(w_up), gather(w_down)
    packed_bias = by_heads(
        jnp.concatenate([query_shift, jnp.zeros_like(query_shift), value_shift], axis=1)
    )

    normed, send = qkv_forward(hidden_in, gain_one, shift_one, w_qkv_full, packed_bias, groups)
    qkv = exchange(send).reshape(groups, 3, local, BLOCK, LANES)
    mixed, lse = attention_forward(table, qkv)
    mixed_back = exchange(mixed.reshape(groups, rows, LANES))
    hidden_out, grad_send, dres, g_out, g_up, g_down, g_up_bias, g_mid = middle(
        mixed_back,
        hidden_in,
        cotangent.reshape(micro * rows, D),
        w_out_full,
        out_shift,
        gain_two,
        shift_two,
        up_shift,
        down_shift,
        w_up_full,
        w_down_full,
        F32,
    )
    grad_mixed = exchange(grad_send).reshape(groups, local, BLOCK, LANES)
    dqkv = attention_backward(table, qkv, grad_mixed, lse)
    dqkv_back = exchange(dqkv.reshape(groups, 3, rows, LANES))
    grad_hidden, g_qkv, g_packed, g_first = qkv_backward(
        dqkv_back, normed, hidden_in, dres, gain_one, w_qkv_full, F32
    )

    g_packed = by_parts(g_packed)
    small = [
        g_first[0],
        g_first[1],
        g_packed[0, :D],
        g_packed[0, 2 * D :],
        g_mid[3],
        g_mid[0],
        g_mid[1],
        g_mid[2],
    ]
    ranks = D // own
    small = jnp.concatenate(
        [item.reshape(ranks, own) for item in small] + [g_up_bias.reshape(ranks, 4 * own)], axis=1
    )
    small = scatter(small)[0]
    parts = [small[number * own : (number + 1) * own] for number in range(8)]
    return (
        hidden_out,
        grad_hidden,
        parts[0],
        parts[1],
        by_parts(scatter(g_qkv)),
        parts[2],
        parts[3],
        scatter(g_out),
        parts[4],
        parts[5],
        parts[6],
        scatter(g_up),
        small[8 * own :],
        scatter(g_down),
        parts[7],
    )


MESH = pl.DeviceIdType.MESH
ANY = pl.ANY
PLANES = 4
SPOTS = 4
PIECES = 2
RANKS = 2 * PLANES * SPOTS
TILES = 3 * D // LANES
HALF_TILES = TILES // 2
QUERY_ORDER = (0, 2, 3, 5, 6, 8, 9, 11, 1, 4, 7, 10)


def column_order():
    order = [("q", head) for head in QUERY_ORDER]
    for spot in range(SPOTS):
        for place in (2 * 3 * spot, 2 * 3 * spot + 2):
            order += [("k", place // 2), ("v", place // 2)]
        order += [("v", 3 * spot + 2), ("k", 3 * spot + 2)]
    return order


def natural_block(entry):
    return "qkv".index(entry[0]) * HEADS + entry[1]


def take_blocks(array, order):
    parts = []
    start = 0
    while start < len(order):
        stop = start + 1
        while stop < len(order) and order[stop] == order[stop - 1] + 1:
            stop += 1
        parts.append(array[..., order[start] * HEAD_DIM : (order[start] + stop - start) * HEAD_DIM])
        start = stop
    return jnp.concatenate(parts, axis=-1)


def flip(value, bits):
    if bits == 0:
        return value
    if bits == 1:
        return value + 1 - 2 * lax.rem(value, 2)
    if bits == 2:
        return value + 2 - 4 * lax.div(value, 2)
    return 3 - value


def place_here():
    core, rank = lax.axis_index("gx"), lax.axis_index("gy")
    return core, lax.div(rank, SPOTS), lax.rem(rank, SPOTS)


def rank_of(plane, spot):
    return plane * SPOTS + spot


def greet(partners):
    barrier = pltpu.get_barrier_semaphore()
    for partner in partners:
        pl.semaphore_signal(barrier, inc=1, device_id=partner, device_id_type=MESH)
    pl.semaphore_wait(barrier, len(partners))


def remote(source, target, send_sem, recv_sem, device):
    return pltpu.make_async_remote_copy(
        src_ref=source,
        dst_ref=target,
        send_sem=send_sem,
        recv_sem=recv_sem,
        device_id=device,
        device_id_type=MESH,
    )


def column_partners(core, plane, spot):
    partners = [(1 - core, rank_of(plane, spot))]
    for bits in range(1, PLANES):
        for other in (core, 1 - core):
            partners.append((other, rank_of(flip(plane, bits), spot)))
    return partners


def all_partners(core, plane, spot):
    return column_partners(core, plane, spot) + [
        (core, rank_of(plane, flip(spot, 1))),
        (core, rank_of(plane, flip(spot, 2))),
    ]


def to_planes(source, target, send_sem, recv_sem, local_sem):
    core, plane, spot = place_here()
    half, odd = lax.div(plane, 2), lax.rem(plane, 2)
    sends, keeps = [], []
    for micro in range(2):
        goal = 2 * micro + core
        here = (goal == plane) & (half == core)
        send = remote(
            source.at[micro],
            target.at[odd],
            send_sem.at[micro],
            recv_sem.at[odd],
            (half, rank_of(goal, spot)),
        )
        keep = pltpu.make_async_copy(source.at[micro], target.at[odd], local_sem.at[micro])

        @pl.when(jnp.logical_not(here))
        def _(send=send):
            send.start()

        @pl.when(here)
        def _(keep=keep):
            keep.start()

        sends.append((here, send))
        keeps.append((here, keep))

    def finish():
        for piece in range(PIECES):
            mine = (odd == core) & (plane == 2 * core + piece)
            arrival = remote(
                source.at[0],
                target.at[piece],
                send_sem.at[0],
                recv_sem.at[piece],
                (core, rank_of(plane, spot)),
            )

            @pl.when(jnp.logical_not(mine))
            def _(arrival=arrival):
                arrival.wait_recv()

        for (here, send), (_, keep) in zip(sends, keeps):

            @pl.when(jnp.logical_not(here))
            def _(send=send):
                send.wait_send()

            @pl.when(here)
            def _(keep=keep):
                keep.wait()

    return finish


def from_planes(source, target, send_sem, recv_sem, local_sem):
    core, plane, spot = place_here()
    micro, odd = lax.div(plane, 2), lax.rem(plane, 2)
    sends, keeps = [], []
    for piece in range(PIECES):
        goal = 2 * core + piece
        here = (goal == plane) & (odd == core)
        send = remote(
            source.at[piece],
            target.at[micro],
            send_sem.at[piece],
            recv_sem.at[micro],
            (odd, rank_of(goal, spot)),
        )
        keep = pltpu.make_async_copy(source.at[piece], target.at[micro], local_sem.at[piece])

        @pl.when(jnp.logical_not(here))
        def _(send=send):
            send.start()

        @pl.when(here)
        def _(keep=keep):
            keep.start()

        sends.append((here, send))
        keeps.append((here, keep))

    def finish():
        for number in range(2):
            mine = (2 * number + core == plane) & (micro == core)
            arrival = remote(
                source.at[0],
                target.at[number],
                send_sem.at[0],
                recv_sem.at[number],
                (core, rank_of(plane, spot)),
            )

            @pl.when(jnp.logical_not(mine))
            def _(arrival=arrival):
                arrival.wait_recv()

        for (here, send), (_, keep) in zip(sends, keeps):

            @pl.when(jnp.logical_not(here))
            def _(send=send):
                send.wait_send()

            @pl.when(here)
            def _(keep=keep):
                keep.wait()

    return finish


class Gather:
    SENDS = 31

    def __init__(self, source, target, send_sem, recv_sem, local_sem):
        self.source, self.target = source, target
        self.send_sem, self.recv_sem = send_sem, recv_sem
        self.core, self.plane, self.spot = place_here()
        self.sends = []
        self.own = pltpu.make_async_copy(
            source, target.at[self.core, self.plane, self.spot], local_sem
        )
        self.own.start()

    def send(self, source, plane, spot, device):
        copy = remote(
            source,
            self.target.at[self.core, plane, spot],
            self.send_sem.at[len(self.sends)],
            self.recv_sem.at[self.core, plane, spot],
            device,
        )
        copy.start()
        self.sends.append(copy)

    def arrive(self, core, plane, spot):
        shard = self.target.at[core, plane, spot]
        remote(
            shard,
            shard,
            self.send_sem.at[0],
            self.recv_sem.at[core, plane, spot],
            (self.core, rank_of(self.plane, self.spot)),
        ).wait_recv()

    def neighbour(self, bits):
        return (self.core, rank_of(self.plane, flip(self.spot, bits)))

    def sibling(self):
        return (1 - self.core, rank_of(self.plane, self.spot))

    def start(self):
        for bits in range(1, PLANES):
            goal = (self.core, rank_of(flip(self.plane, bits), self.spot))
            self.send(self.source, self.plane, self.spot, goal)
        for goal in (self.neighbour(1), self.neighbour(2), self.sibling()):
            self.send(self.source, self.plane, self.spot, goal)

    def column(self):
        for bits in range(1, PLANES):
            plane = flip(self.plane, bits)
            self.arrive(self.core, plane, self.spot)
            shard = self.target.at[self.core, plane, self.spot]
            for goal in (self.neighbour(1), self.neighbour(2), self.sibling()):
                self.send(shard, plane, self.spot, goal)

    def across(self):
        for bits in range(PLANES):
            plane = flip(self.plane, bits)
            for side in (1, 2):
                spot = flip(self.spot, side)
                self.arrive(self.core, plane, spot)
                shard = self.target.at[self.core, plane, spot]
                if (side == 1) == (bits < 2):
                    self.send(shard, plane, spot, self.neighbour(3 - side))
                self.send(shard, plane, spot, self.sibling())

    def corner(self):
        spot = flip(self.spot, 3)
        for bits in range(PLANES):
            plane = flip(self.plane, bits)
            self.arrive(self.core, plane, spot)
            self.send(self.target.at[self.core, plane, spot], plane, spot, self.sibling())

    def finish(self):
        for bits in range(PLANES):
            for side in range(SPOTS):
                self.arrive(1 - self.core, flip(self.plane, bits), flip(self.spot, side))
        self.own.wait()
        for copy in self.sends:
            copy.wait_send()


def settle(shards_ref, plan):
    rows = shards_ref.shape[3] // 2

    def pair(number, carry):
        core, plane, side = (
            lax.div(number, 2 * PLANES),
            lax.rem(lax.div(number, 2), PLANES),
            lax.rem(number, 2),
        )
        goal = pl.ds(pl.multiple_of(number * 2 * rows, 16), 2 * rows)
        for tile, out_ref, (left, right) in plan:
            columns = slice(tile * LANES, (tile + 1) * LANES)
            first = shards_ref[core, plane, 2 * side, :, columns].astype(F32)
            second = shards_ref[core, plane, 2 * side + 1, :, columns].astype(F32)
            out_ref[goal, left * LANES : (left + 1) * LANES] = jnp.concatenate(
                [first[:rows], second[:rows]], axis=0
            ).astype(BF16)
            out_ref[goal, right * LANES : (right + 1) * LANES] = jnp.concatenate(
                [first[rows:], second[rows:]], axis=0
            ).astype(BF16)
        return carry

    lax.fori_loop(0, RANKS // 2, pair, 0)


def alternate(tile):
    return 2 * tile, 2 * tile + 1


def plane_partners(core, plane, spot):
    partners = []
    for other in (core, 1 - core):
        for side in range(SPOTS):
            if other is core and side == 0:
                continue
            partners.append((other, rank_of(plane, flip(spot, side))))
    return partners


def both_partners(core, plane, spot):
    return plane_partners(core, plane, spot) + column_partners(core, plane, spot)[1:]


def exchange_sems(recv_shape):
    return [
        pltpu.SemaphoreType.DMA((14,)),
        pltpu.SemaphoreType.DMA(recv_shape),
        pltpu.SemaphoreType.DMA((PIECES,)),
    ]


def sort_entries(table, sorted_ref, entries):
    count = table.shape[1]
    core = lax.axis_index("gx")
    lane = lax.broadcasted_iota(jnp.int32, (count, count), 1)
    row = lax.broadcasted_iota(jnp.int32, (count, count), 0).astype(F32)
    everything = jnp.broadcast_to(table, (count, count))
    half = entries // 2
    inside = (lane >= core * half) & (lane < (core + 1) * half)
    lane = lane.astype(F32)
    for number, along in enumerate((everything, jnp.where(inside, everything, 2.0 * LANES))):
        down = along.T
        before = (along < down) | ((along == down) & (lane < row))
        rank = jnp.sum(jnp.where(before, 1.0, 0.0), axis=1, keepdims=True)
        order = jnp.sum(jnp.where(rank == lane, row, 0.0), axis=0, keepdims=True)
        upto = jnp.sum(jnp.where(down <= lane, 1.0, 0.0), axis=0, keepdims=True)
        sorted_ref[2 * number : 2 * number + 1] = order.astype(jnp.int32)
        sorted_ref[2 * number + 1 : 2 * number + 2] = upto.astype(jnp.int32)


class Outward:
    def __init__(self, source, target, send_sem, recv_sem, local_sem):
        self.target, self.recv_sem, self.send_sem = target, recv_sem, send_sem
        self.core, self.plane, self.spot = place_here()
        self.sends, self.keeps = [], []
        for side in (3, 1, 2, 0):
            for other in (self.core, 1 - self.core):
                goal = flip(self.spot, side)
                for piece in range(PIECES):
                    start = source.at[other, goal, piece]
                    stop = target.at[2 * self.core + piece, self.spot]
                    if side == 0 and other is self.core:
                        copy = pltpu.make_async_copy(start, stop, local_sem.at[piece])
                        self.keeps.append(copy)
                    else:
                        copy = remote(
                            start,
                            stop,
                            send_sem.at[len(self.sends)],
                            recv_sem.at[2 * self.core + piece, self.spot],
                            (other, rank_of(self.plane, goal)),
                        )
                        self.sends.append(copy)
                    copy.start()

    def arrive(self, side):
        for other in (self.core, 1 - self.core):
            if side == 0 and other is self.core:
                for copy in self.keeps:
                    copy.wait()
                continue
            for piece in range(PIECES):
                place = (2 * other + piece, flip(self.spot, side))
                remote(
                    self.target.at[place],
                    self.target.at[place],
                    self.send_sem.at[0],
                    self.recv_sem.at[place],
                    (self.core, rank_of(self.plane, self.spot)),
                ).wait_recv()

    def finish(self):
        for copy in self.sends:
            copy.wait_send()


def inward_targets(core, spot):
    for side in (3, 1, 2, 0):
        for other in (core, 1 - core):
            yield side, other, flip(spot, side), side == 0 and other is core


class Inward:
    def __init__(self, source, target, send_sem, recv_sem, local_sem):
        self.source, self.target = source, target
        self.send_sem, self.recv_sem, self.local_sem = send_sem, recv_sem, local_sem
        self.core, self.plane, self.spot = place_here()
        self.sends, self.keeps = [], []

    def send(self, other, goal, stays, piece, part, parts):
        source = self.source.at[2 * other + piece, goal, parts]
        target = self.target.at[self.core, self.spot, piece, parts]
        if stays:
            copy = pltpu.make_async_copy(source, target, self.local_sem.at[part, piece])
            self.keeps.append(copy)
        else:
            copy = remote(
                source,
                target,
                self.send_sem.at[len(self.sends)],
                self.recv_sem.at[self.core, self.spot, piece, part],
                (other, rank_of(self.plane, goal)),
            )
            self.sends.append(copy)
        copy.start()

    def finish(self, parts_of):
        for side, other, goal, stays in inward_targets(self.core, self.spot):
            if stays:
                continue
            for piece in range(PIECES):
                for part, parts in enumerate(parts_of[0 if other is self.core else 1]):
                    target = self.target.at[other, goal, piece, parts]
                    remote(
                        target,
                        target,
                        self.send_sem.at[0],
                        self.recv_sem.at[other, goal, piece, part],
                        (self.core, rank_of(self.plane, self.spot)),
                    ).wait_recv()
        for copy in self.sends:
            copy.wait_send()
        for copy in self.keeps:
            copy.wait()


KEYS_A, QUERIES, KEYS_B = range(3)


def plane_attend_back_kernel(count, *refs):
    table_ref, sorted_ref, qk_ref, shared_ref, grad_source_ref, lse_ref, hidden_ref = refs[:7]
    sources, refs = refs[7 : 7 + count], refs[7 + count :]
    back_ref, hidden_out_ref = refs[:2]
    outs, refs = refs[2 : 2 + count], refs[2 + count :]
    buffers, refs = refs[: 7 * count], refs[7 * count :]
    grad_ref, out_ref, sums_ref, shares_ref, walked_ref, sibling_ref = refs[:6]
    scores_refs, refs = refs[6:10], refs[10:]
    reduce_send, reduce_recv, reduce_local = refs[:3]
    grad_sems, back_sems, move_sems, sibling_sems = refs[3:6], refs[6:9], refs[9:12], refs[12:14]

    local = qk_ref.shape[3]
    groups = PLANES * SPOTS
    blocks = groups * local
    core, plane, spot = place_here()
    low = low_lanes(BLOCK)
    masks = [half_mask(True), half_mask(False)]

    greet(both_partners(core, plane, spot))
    grads = Outward(grad_source_ref, grad_ref, *grad_sems)
    reduces = [
        Reduce(
            source,
            *buffers[7 * number : 7 * number + 7],
            out,
            (reduce_send.at[number], reduce_recv.at[number], reduce_local.at[number]),
        )
        for number, (source, out) in enumerate(zip(sources, outs))
    ]
    for one in reduces:
        one.start()
    finish_hidden = from_planes(hidden_ref, hidden_out_ref, *move_sems)

    def load(component, block):
        rank, number = lax.div(block, local), lax.rem(block, local)
        if component == 2:
            return shared_ref[lax.div(rank, SPOTS), lax.rem(rank, SPOTS), number]
        return qk_ref[lax.div(rank, SPOTS), lax.rem(rank, SPOTS), component, number]

    def load_grad(block):
        rank = lax.div(block, local)
        return grad_ref[lax.div(rank, SPOTS), lax.rem(rank, SPOTS), lax.rem(block, local)]

    def store(component, block, value):
        rank = lax.div(block, local)
        out_ref[
            lax.div(rank, SPOTS), lax.rem(rank, SPOTS), component, lax.rem(block, local)
        ] = value.astype(BF16)

    def stored(component, block):
        rank = lax.div(block, local)
        return out_ref[
            lax.div(rank, SPOTS), lax.rem(rank, SPOTS), component, lax.rem(block, local)
        ].astype(F32)

    nothing = jnp.zeros((BLOCK, LANES), F32)

    def clear(block, carry):
        for slot in range(2):
            sums_ref[slot, block] = nothing
        return carry

    lax.fori_loop(0, blocks, clear, 0)

    def picked(block, number):
        return table_ref[0, block * RANDOM + number]

    def one_block(block, slot):
        ids, bias = inner_slots(picked, block, blocks)
        keys = jnp.concatenate([load(1 + slot, number) for number in ids], axis=0)
        both = jnp.concatenate(
            [load(0, block) * masks[slot], load_grad(block) * masks[1 - slot]], axis=0
        )
        products = dot_rt(both, keys)
        logs = lse_ref[block][:, slot * HEAD_DIM : slot * HEAD_DIM + 1]
        weights = jnp.exp(products[:BLOCK] + bias - logs)
        grad_weights = products[BLOCK:]
        delta = jnp.sum(weights * grad_weights, axis=1, keepdims=True)
        grad_scores = weights * (grad_weights - delta)
        stacked = jnp.concatenate([grad_scores, weights], axis=0).astype(BF16)
        return dot(stacked[:BLOCK], keys), dot_lt(stacked, both)

    fixed = 5

    def rank_blocks(rank, slot):
        first = rank * local
        results = [one_block(first + number, slot) for number in range(local)]

        def share(number, place):
            return results[number][1][place * BLOCK : (place + 1) * BLOCK]

        for shift in range(-1, local + 1):
            parts = [
                share(number, shift - number + 1)
                for number in range(local)
                if 0 <= shift - number + 1 <= 2
            ]
            target = jnp.minimum(jnp.maximum(first + shift, 0), blocks - 1)
            sums_ref[slot, target] += functools.reduce(jnp.add, parts)
        for place, target in ((3, 0), (4, blocks - 1)):
            sums_ref[slot, target] += functools.reduce(
                jnp.add, [share(number, place) for number in range(local)]
            )
        for number in range(local):
            for pick in range(RANDOM):
                shares_ref[slot, (first + number) * RANDOM + pick] = share(number, fixed + pick)
        return [result[0] for result in results]

    def head_a(side):
        def body(number, carry):
            rank = number * SPOTS + flip(spot, side)
            for place, query in enumerate(rank_blocks(rank, 0)):
                store(QUERIES, rank * local + place, query * SCALE)
            return carry

        lax.fori_loop(0, PLANES, body, 0)

    def head_b(number, carry):
        rank = core * (groups // 2) + number
        for place, query in enumerate(rank_blocks(rank, 1)):
            block = rank * local + place
            store(QUERIES, block, jnp.where(low, stored(QUERIES, block), query * SCALE))
        return carry

    spans = blocks // SPAN
    ends = (0, blocks - 1)

    def dense(slot, p_ref, d_ref, numbers):
        both = jnp.concatenate(
            [load(0, number) * masks[slot] for number in numbers]
            + [load_grad(number) * masks[1 - slot] for number in numbers],
            axis=0,
        )
        rows = len(numbers) * BLOCK
        column = slot * HEAD_DIM
        logs = jnp.concatenate(
            [lse_ref[number][:, column : column + 1] for number in numbers], axis=0
        )

        def keys_at(span):
            return jnp.concatenate(
                [load(1 + slot, span * SPAN + number) for number in range(SPAN)], axis=0
            )

        def first_pass(span, delta):
            products = dot_rt(both, keys_at(span))
            weights = jnp.exp(products[:rows] - logs)
            grad_weights = products[rows:]
            p_ref[span] = weights
            d_ref[span] = grad_weights
            return delta + jnp.sum(weights * grad_weights, axis=1, keepdims=True)

        delta = lax.fori_loop(0, spans, first_pass, jnp.zeros((rows, 1), F32), unroll=2)

        def second_pass(span, total):
            weights = p_ref[span]
            grad_scores = weights * (d_ref[span] - delta)
            stacked = jnp.concatenate([grad_scores, weights], axis=0).astype(BF16)
            shares = dot_lt(stacked, both)
            for number in range(SPAN):
                sums_ref[slot, span * SPAN + number] += shares[
                    number * BLOCK : (number + 1) * BLOCK
                ]
            return total + dot(stacked[:rows], keys_at(span))

        total = lax.fori_loop(0, spans, second_pass, jnp.zeros((rows, LANES), F32), unroll=2)
        for place, number in enumerate(numbers):
            query = total[place * BLOCK : (place + 1) * BLOCK] * SCALE
            if slot == 1:
                query = jnp.where(low, stored(QUERIES, number), query)
            store(QUERIES, number, query)

    def walk(slot, length):
        def body(number, total):
            entry = sorted_ref[2 * slot, number]
            earlier = sorted_ref[2 * slot, jnp.maximum(number - 1, 0)]
            keep = jnp.where(table_ref[0, entry] == table_ref[0, earlier], 1.0, 0.0).astype(F32)
            total = total * keep + shares_ref[slot, entry]
            walked_ref[slot, number] = total.astype(BF16)
            return total

        lax.fori_loop(0, length, body, nothing, unroll=4)

    def close(slot, rank, component):
        def body(number, carry):
            block = rank * local + number
            stop = sorted_ref[2 * slot + 1, block]
            start = jnp.where(block == 0, 0, sorted_ref[2 * slot + 1, jnp.maximum(block - 1, 0)])
            some = jnp.where(stop > start, 1.0, 0.0).astype(F32)
            share = walked_ref[slot, jnp.maximum(stop - 1, 0)].astype(F32)
            store(component, block, sums_ref[slot, block] + share * some)
            return carry

        lax.fori_loop(0, local, body, 0, unroll=True)

    back = Inward(out_ref, back_ref, *back_sems)
    own_parts = (slice(0, 1), slice(1, 2), slice(2, 3))
    far_parts = (slice(0, 2),)

    for side in range(SPOTS):
        grads.arrive(side)
        head_a(side)
        if side == 1:
            for one in reduces:
                one.corners()
    dense(0, scores_refs[0], scores_refs[1], ends)
    for one in reduces:
        one.sides()
    walk(0, blocks * RANDOM)
    for side, other, goal, stays in inward_targets(core, spot):
        for piece in range(PIECES):
            close(0, (2 * other + piece) * SPOTS + goal, KEYS_A)
            if other is core:
                back.send(other, goal, stays, piece, 0, own_parts[0])
            else:
                back.send(other, goal, stays, piece, 0, far_parts[0])
    lax.fori_loop(0, groups // 2, head_b, 0)
    dense(1, scores_refs[2], scores_refs[3], (core * (blocks - 1),))
    for side, other, goal, stays in inward_targets(core, spot):
        if other is core:
            for piece in range(PIECES):
                back.send(other, goal, stays, piece, 1, own_parts[1])
    walk(1, blocks * RANDOM // 2)
    for number in range(PIECES):
        for goal in range(SPOTS):
            close(1, (2 * (1 - core) + number) * SPOTS + goal, KEYS_B)
    across = remote(
        out_ref.at[pl.ds(2 * (1 - core), PIECES), :, KEYS_B],
        sibling_ref,
        sibling_sems[0],
        sibling_sems[1],
        (1 - core, rank_of(plane, spot)),
    )
    across.start()
    for number in range(PIECES):
        for goal in range(SPOTS):
            close(1, (2 * core + number) * SPOTS + goal, KEYS_B)
    for one in reduces:
        one.columns()
    across.wait_recv()
    for side, other, goal, stays in inward_targets(core, spot):
        if other is core:
            for piece in range(PIECES):
                place = (2 * core + piece, goal, KEYS_B)
                out_ref[place] = (
                    out_ref[place].astype(F32) + sibling_ref[piece, goal].astype(F32)
                ).astype(BF16)
                back.send(other, goal, stays, piece, 2, own_parts[2])
    for one in reduces:
        one.finish()
    finish_hidden()
    grads.finish()
    across.wait_send()
    back.finish((own_parts, far_parts))


def plane_attention_back(table, sorted_table, qk, shared, grad_source, lse, hidden, sources):
    local = qk.shape[3]
    blocks = PLANES * SPOTS * local
    spans = blocks // SPAN
    count = len(sources)
    buffers = []
    for source in sources:
        buffers += reduce_scratch(source.shape, source.dtype)
    tile = (local, BLOCK, LANES)
    wide = VMEM((spans, 2 * BLOCK, SPAN * BLOCK), F32)
    thin = VMEM((spans, BLOCK, SPAN * BLOCK), F32)
    dma = pltpu.SemaphoreType.DMA
    return pl.pallas_call(
        functools.partial(plane_attend_back_kernel, count),
        out_shape=(
            jax.ShapeDtypeStruct((2, SPOTS, PIECES, 3) + tile, BF16),
            jax.ShapeDtypeStruct(hidden.shape, BF16),
        )
        + tuple(jax.ShapeDtypeStruct(source.shape[3:], F32) for source in sources),
        in_specs=[
            whole(pltpu.SMEM),
            whole(pltpu.SMEM),
            whole(),
            whole(),
            whole(ANY),
            whole(),
            whole(ANY),
        ]
        + [whole(ANY)] * count,
        out_specs=(whole(ANY), whole(ANY)) + (whole(),) * count,
        scratch_shapes=buffers
        + [
            VMEM((PLANES, SPOTS) + tile, BF16),
            VMEM((PLANES, SPOTS, 3) + tile, BF16),
            VMEM((2, blocks, BLOCK, LANES), F32),
            VMEM((2, blocks * RANDOM, BLOCK, LANES), F32),
            VMEM((2, blocks * RANDOM, BLOCK, LANES), BF16),
            VMEM((PIECES, SPOTS) + tile, BF16),
            wide,
            wide,
            thin,
            thin,
            dma((count, REDUCE_SEMS)),
            dma((count, REDUCE_SEMS)),
            dma((count, 4)),
        ]
        + exchange_sems((PLANES, SPOTS))
        + [
            dma((36,)),
            dma((2, SPOTS, PIECES, 3)),
            dma((3, PIECES)),
            dma((2,)),
            dma((2,)),
            dma((2,)),
            dma,
            dma,
        ],
        compiler_params=pltpu.CompilerParams(
            vmem_limit_bytes=62 * 1024 * 1024, collective_id=5, has_side_effects=True
        ),
        name="plane_attention_back",
    )(table, sorted_table, qk, shared, grad_source, lse, hidden, *sources)


class PlaneGather:
    SENDS = 3 + 3 + 4 + 2

    def __init__(self, source, target, send_sem, column_sem, recv_sem, local_sem):
        self.source, self.target = source, target
        self.send_sem, self.column_sem, self.recv_sem = send_sem, column_sem, recv_sem
        self.core, self.plane, self.spot = place_here()
        self.sends = []
        self.own = pltpu.make_async_copy(
            source, target.at[self.core, self.plane, self.spot], local_sem
        )
        self.own.start()
        for bits in range(1, PLANES):
            copy = remote(
                source,
                target.at[self.core, self.plane, self.spot],
                send_sem.at[len(self.sends)],
                column_sem.at[self.plane],
                (self.core, rank_of(flip(self.plane, bits), self.spot)),
            )
            copy.start()
            self.sends.append(copy)

    def neighbour(self, bits):
        return (self.core, rank_of(self.plane, flip(self.spot, bits)))

    def sibling(self):
        return (1 - self.core, rank_of(self.plane, self.spot))

    def piece(self, core, planes, spot):
        return self.target.at[core, planes, spot]

    def send(self, planes, spot, part, goal):
        piece = self.piece(self.core, planes, spot)
        copy = remote(
            piece,
            piece,
            self.send_sem.at[len(self.sends)],
            self.recv_sem.at[self.core, spot, part],
            goal,
        )
        copy.start()
        self.sends.append(copy)

    def arrive(self, core, planes, spot, part):
        piece = self.piece(core, planes, spot)
        remote(
            piece,
            piece,
            self.send_sem.at[0],
            self.recv_sem.at[core, spot, part],
            (self.core, rank_of(self.plane, self.spot)),
        ).wait_recv()

    def columns(self):
        self.own.wait()
        for bits in range(1, PLANES):
            other = flip(self.plane, bits)
            shard = self.target.at[self.core, other, self.spot]
            remote(
                shard,
                shard,
                self.send_sem.at[0],
                self.column_sem.at[other],
                (self.core, rank_of(self.plane, self.spot)),
            ).wait_recv()
        for goal in (self.neighbour(1), self.neighbour(2), self.sibling()):
            self.send(slice(0, PLANES), self.spot, 0, goal)

    def forward(self):
        everything = slice(0, PLANES)
        for side in (1, 2):
            spot = flip(self.spot, side)
            self.arrive(self.core, everything, spot, 0)
            half = slice(0, 2) if side == 1 else slice(2, 4)
            self.send(half, spot, side - 1, self.neighbour(3 - side))
            self.send(everything, spot, 0, self.sibling())

    def corner(self):
        spot = flip(self.spot, 3)
        for part, half in enumerate((slice(0, 2), slice(2, 4))):
            self.arrive(self.core, half, spot, part)
            self.send(half, spot, part, self.sibling())

    def finish(self):
        for side in range(3):
            self.arrive(1 - self.core, slice(0, PLANES), flip(self.spot, side), 0)
        for part, half in enumerate((slice(0, 2), slice(2, 4))):
            self.arrive(1 - self.core, half, flip(self.spot, 3), part)
        for copy in self.sends:
            copy.wait_send()


def pair_of_blocks(read, first, second):
    low = low_lanes(1)
    tiles = []
    for block, wanted in ((first, 0), (second, 1)):
        tile = read(block // 2)
        tiles.append(tile if block % 2 == wanted else swap_halves(tile))
    return jnp.where(low, tiles[0], tiles[1])


def fold_tiles(target_ref, start, tiles, read):
    half = len(tiles) // 2
    for number in range(half):
        columns = slice((start + number) * LANES, (start + number + 1) * LANES)
        target_ref[:, columns] = jnp.concatenate(
            [read(tiles[number]), read(tiles[half + number])], axis=0
        ).astype(BF16)


VECTORS = 8


def lay_vectors(vecs_ref, vectors_ref, up_ref):
    rows = vecs_ref.shape[3]
    own, wide = D // RANKS, FF // RANKS
    values = vecs_ref[...].reshape(RANKS, rows, LANES).astype(F32)

    def spread_out(count, width):
        place = lax.broadcasted_iota(jnp.int32, (LANES, count), 1)
        lane = lax.broadcasted_iota(jnp.int32, (LANES, count), 0)
        start = lax.div(place, width) * width
        return jnp.where(place - start == lane, 1.0, 0.0).astype(BF16)

    laid = dot(vecs_ref[...].reshape(RANKS * rows, LANES), spread_out(D, own))
    owner = lax.broadcasted_iota(jnp.int32, (RANKS, 1, D), 0)
    column = lax.broadcasted_iota(jnp.int32, (RANKS, 1, D), 2)
    laid = jnp.where(lax.div(column, own) == owner, laid.reshape(RANKS, rows, D), 0.0)
    vectors_ref[...] = jnp.sum(laid, axis=0)[:VECTORS]
    row = lax.broadcasted_iota(jnp.int32, (1, rows, LANES), 1)
    last = jnp.sum(jnp.where(row == VECTORS, values, 0.0), axis=1)
    laid = dot(last.astype(BF16), spread_out(FF, wide))
    owner = lax.broadcasted_iota(jnp.int32, (RANKS, FF), 0)
    column = lax.broadcasted_iota(jnp.int32, (RANKS, FF), 1)
    laid = jnp.sum(jnp.where(lax.div(column, wide) == owner, laid, 0.0), axis=0, keepdims=True)
    for chunk in range(FF // CHUNK):
        for side in range(2):
            start = side * (FF // 2) + chunk * LANES
            up_ref[chunk, :, side * LANES : (side + 1) * LANES] = laid[:, start : start + LANES]


def lay_table(tables_ref, core, micro, entries):
    count = 2 * LANES
    ranks = PLANES * SPOTS
    values = tables_ref[core].reshape(ranks, tables_ref.shape[3], LANES).astype(F32)
    row = lax.broadcasted_iota(jnp.int32, (1, tables_ref.shape[3], LANES), 1)
    values = jnp.sum(jnp.where(row == micro, values, 0.0), axis=1)
    place = lax.broadcasted_iota(jnp.int32, (LANES, count), 1)
    lane = lax.broadcasted_iota(jnp.int32, (LANES, count), 0)
    start = lax.div(place, entries) * entries
    laid = dot(values.astype(BF16), jnp.where(place - start == lane, 1.0, 0.0).astype(BF16))
    owner = lax.broadcasted_iota(jnp.int32, (ranks, count), 0)
    column = lax.broadcasted_iota(jnp.int32, (ranks, count), 1)
    laid = jnp.sum(jnp.where(lax.div(column, entries) == owner, laid, 0.0), axis=0, keepdims=True)
    column = lax.broadcasted_iota(jnp.int32, (1, count), 1)
    return jnp.where(column < ranks * entries, laid, 2.0 * LANES)


def front_kernel(
    x_in_ref,
    dy_ref,
    vec_ref,
    tab_ref,
    w_qkv_in_ref,
    w_out_in_ref,
    w_up_in_ref,
    w_down_in_ref,
    back_ref,
    x_ref,
    dys_ref,
    w_down_ref,
    w_qkv_hbm,
    w_out_hbm,
    w_up_hbm,
    qk_hbm,
    shared_hbm,
    normed_ref,
    lse_ref,
    vectors_ref,
    up_ref,
    table_ref,
    sorted_ref,
    s_qkv_ref,
    s_ou_ref,
    g_qkv_ref,
    g_ou_ref,
    w_qkv_ref,
    w_out_ref,
    w_up_ref,
    xs_ref,
    vecs_ref,
    tabs_ref,
    bias_ref,
    send_ref,
    qk_ref,
    shared_ref,
    out_ref,
    p_ref,
    q_ref,
    picks_ref,
    *sems,
):
    gather_send, gather_recv, gather_local = sems[:3]
    plane_send, plane_column, plane_recv, plane_local = sems[3:7]
    x_sems, dy_sems = sems[7:10], sems[10:13]
    qkv_send, qkv_recv, qkv_local, shared_send, shared_recv = sems[13:18]
    back_sems, local_sem = sems[18:21], sems[21]
    core, plane, spot = place_here()
    micro, rows, _ = x_in_ref.shape
    tokens = PIECES * rows
    local = rows // BLOCK
    blocks = PLANES * SPOTS * local

    barrier = pltpu.get_barrier_semaphore()
    partners = both_partners(core, plane, spot)
    for partner in partners:
        pl.semaphore_signal(barrier, inc=1, device_id=partner, device_id_type=MESH)

    def natural(ref):
        return lambda tile: ref[:, tile * LANES : (tile + 1) * LANES].astype(F32)

    order = [natural_block(entry) for entry in column_order()]
    read = natural(w_qkv_in_ref)
    fold_tiles(
        s_qkv_ref,
        0,
        list(range(TILES)),
        lambda tile: pair_of_blocks(read, order[2 * tile], order[2 * tile + 1]),
    )
    pl.semaphore_wait(barrier, len(partners))

    finish_x = to_planes(x_in_ref, xs_ref, *x_sems)
    gathers = []
    for number, (source, target) in enumerate(
        ((tab_ref, tabs_ref), (vec_ref, vecs_ref), (s_qkv_ref, g_qkv_ref))
    ):
        one = Gather(
            source, target, gather_send.at[number], gather_recv.at[number], gather_local.at[number]
        )
        one.start()
        gathers.append(one)
    outs = D // LANES // 2
    fold_tiles(s_ou_ref, 0, list(range(D // LANES)), natural(w_out_in_ref))
    fold_tiles(s_ou_ref, outs, list(range(FF // LANES)), natural(w_up_in_ref))
    for one in gathers:
        one.column()
    for one in gathers:
        one.across()
    for one in gathers:
        one.corner()
    finish_x()
    spreads = [
        PlaneGather(
            source,
            target,
            plane_send.at[number],
            plane_column.at[number],
            plane_recv.at[number],
            plane_local.at[number],
        )
        for number, (source, target) in enumerate(
            ((s_ou_ref, g_ou_ref), (w_down_in_ref, w_down_ref))
        )
    ]
    finish_dy = to_planes(dy_ref, dys_ref, *dy_sems)
    keep_x = pltpu.make_async_copy(xs_ref, x_ref, local_sem.at[0])
    keep_x.start()
    normal, _ = norm_parts(xs_ref[...].reshape(tokens, D).astype(F32))
    for one in gathers[:2]:
        one.finish()

    window_core, window_micro = lax.rem(plane, 2), lax.div(plane, 2)
    scalars = pltpu.make_async_copy(tabs_ref.at[window_core], picks_ref, local_sem.at[1])
    scalars.start()
    lay_vectors(vecs_ref, vectors_ref, up_ref)
    normed_ref[...] = (normal * vectors_ref[0:1] + vectors_ref[1:2]).astype(BF16)
    for tile in range(TILES):
        halves = []
        for entry in column_order()[2 * tile : 2 * tile + 2]:
            halves.append(entry)

        def bias_tile(number, halves=halves):
            if number < D // LANES:
                return vectors_ref[2:3, number * LANES : (number + 1) * LANES]
            if number < 2 * D // LANES:
                return jnp.zeros((1, LANES), F32)
            start = (number - 2 * D // LANES) * LANES
            return vectors_ref[3:4, start : start + LANES]

        chunk, side = tile % HALF_TILES, tile // HALF_TILES
        start = chunk * CHUNK + side * LANES
        bias_ref[:, start : start + LANES] = pair_of_blocks(
            bias_tile, order[2 * tile], order[2 * tile + 1]
        )
    gathers[2].finish()
    settle(g_qkv_ref, [(tile, w_qkv_ref, alternate(tile)) for tile in range(HALF_TILES)])
    keep_w = pltpu.make_async_copy(w_qkv_ref, w_qkv_hbm, local_sem.at[2])
    keep_w.start()

    def shaped(value):
        return value.astype(BF16).reshape(local, BLOCK, LANES)

    low = low_lanes(rows)
    queries = D // LANES
    for chunk in range(HALF_TILES):
        columns = slice(chunk * CHUNK, (chunk + 1) * CHUNK)
        packed = dot(normed_ref[...], w_qkv_ref[:, columns]) + bias_ref[:, columns]
        for side in range(2):
            tile = chunk + side * HALF_TILES
            whole_tile = packed[:, side * LANES : (side + 1) * LANES]
            if tile < queries:
                whole_tile = whole_tile.astype(BF16).astype(F32) * SCALE
            for piece in range(PIECES):
                part = whole_tile[piece * rows : (piece + 1) * rows]
                if tile < SPOTS:
                    send_ref[0, tile, piece, 0] = shaped(part)
                elif tile < queries:
                    first = 2 * (tile - SPOTS)
                    shared = send_ref[0, first, piece, 0].reshape(rows, LANES).astype(F32)
                    send_ref[1, first, piece, 0] = shaped(jnp.where(low, part, shared))
                    shared = send_ref[0, first + 1, piece, 0].reshape(rows, LANES).astype(F32)
                    send_ref[1, first + 1, piece, 0] = shaped(
                        jnp.where(low, swap_halves(part), shared)
                    )
                else:
                    goal, role = (tile - queries) // 3, (tile - queries) % 3
                    if role < 2:
                        send_ref[role, goal, piece, 1] = shaped(part)
                    else:
                        send_ref[0, goal, piece, 2] = shaped(part)
    sends, keeps = [], []
    for part, (parts, landing) in enumerate(((slice(0, 2), qk_ref), (2, shared_ref))):
        for side in (3, 1, 2, 0):
            for other in (core, 1 - core) if part == 0 else (core,):
                goal = flip(spot, side)
                for piece in range(PIECES):
                    source = send_ref.at[other if part == 0 else 0, goal, piece, parts]
                    target = landing.at[2 * core + piece, spot]
                    if side == 0 and other is core:
                        copy = pltpu.make_async_copy(source, target, qkv_local.at[part, piece])
                        keeps.append((part, copy))
                    else:
                        copy = remote(
                            source,
                            target,
                            qkv_send.at[len(sends)],
                            qkv_recv.at[2 * core + piece, spot, part],
                            (other, rank_of(plane, goal)),
                        )
                        sends.append(copy)
                    copy.start()
    for one in spreads:
        one.columns()
    table = lay_table(tabs_ref, window_core, window_micro, local * RANDOM)
    table_ref[...] = table.astype(jnp.int32)
    sort_entries(table, sorted_ref, blocks * RANDOM)
    scalars.wait()

    def arrive(part, other, piece, goal):
        target = (qk_ref, shared_ref)[part].at[2 * other + piece, goal]
        remote(
            target,
            target,
            qkv_send.at[0],
            qkv_recv.at[2 * other + piece, goal, part],
            (core, rank_of(plane, spot)),
        ).wait_recv()

    for side in range(SPOTS):
        for other in (core, 1 - core):
            if side > 0 or other is not core:
                for piece in range(PIECES):
                    arrive(0, other, piece, flip(spot, side))
    for part, copy in keeps:
        copy.wait()

    low = low_lanes(BLOCK)
    masks = [half_mask(True), half_mask(False)]

    def tile_of(component, block):
        rank, number = lax.div(block, local), lax.rem(block, local)
        if component == 2:
            return shared_ref[lax.div(rank, SPOTS), lax.rem(rank, SPOTS), number]
        return qk_ref[lax.div(rank, SPOTS), lax.rem(rank, SPOTS), component, number]

    def picked(block, number):
        rank = lax.div(block, local)
        return picks_ref[
            lax.div(rank, SPOTS),
            lax.rem(rank, SPOTS),
            window_micro,
            lax.rem(block, local) * RANDOM + number,
        ]

    def place_of(block):
        rank = lax.div(block, local)
        return lax.div(rank, SPOTS), lax.rem(rank, SPOTS), lax.rem(block, local)

    def put(block, slot, mixed, log):
        place = place_of(block)
        if slot == 0:
            out_ref[place] = mixed.astype(BF16)
            lse_ref[block] = jnp.where(low, log, 0.0)
        else:
            out_ref[place] = jnp.where(low, mixed, out_ref[place].astype(F32)).astype(BF16)
            lse_ref[block] = jnp.where(low, lse_ref[block], log)

    def one_block(block, slot):
        ids, bias = inner_slots(picked, block, blocks)
        keys = jnp.concatenate([tile_of(1 + slot, number) for number in ids], axis=0)
        scores = dot_rt(tile_of(0, block) * masks[slot], keys) + bias
        top = jnp.max(scores, axis=1, keepdims=True)
        powered = jnp.exp(scores - top)
        total = jnp.sum(powered, axis=1, keepdims=True)
        mixed = dot(powered.astype(BF16), keys) * (1.0 / total)
        return mixed, top + jnp.log(total)

    def rank_blocks(rank, slot):
        results = [one_block(rank * local + number, slot) for number in range(local)]
        for number, (mixed, log) in enumerate(results):
            put(rank * local + number, slot, mixed, log)

    spans = blocks // SPAN
    ends = (0, blocks - 1)

    def dense(slot, scores_ref, numbers):
        size = len(numbers) * BLOCK
        query = jnp.concatenate([tile_of(0, number) * masks[slot] for number in numbers], axis=0)

        def keys_at(span):
            return jnp.concatenate(
                [tile_of(1 + slot, span * SPAN + number) for number in range(SPAN)], axis=0
            )

        def first_pass(span, top):
            scores = dot_rt(query, keys_at(span))
            scores_ref[span] = scores
            return jnp.maximum(top, jnp.max(scores, axis=1, keepdims=True))

        top = lax.fori_loop(
            0, spans, first_pass, jnp.full((size, 1), NEGATIVE, F32), unroll=2
        )

        def second_pass(span, carry):
            total, mixed = carry
            powered = jnp.exp(scores_ref[span] - top)
            return (
                total + jnp.sum(powered, axis=1, keepdims=True),
                mixed + dot(powered.astype(BF16), keys_at(span)),
            )

        total, mixed = lax.fori_loop(
            0,
            spans,
            second_pass,
            (jnp.zeros((size, 1), F32), jnp.zeros((size, LANES), F32)),
            unroll=2,
        )
        mixed = mixed * (1.0 / total)
        log = top + jnp.log(total)
        for place, number in enumerate(numbers):
            span = slice(place * BLOCK, (place + 1) * BLOCK)
            put(number, slot, mixed[span], log[span])

    def head_a(number, carry):
        rank_blocks(number, 0)
        return carry

    def head_b(number, carry):
        rank_blocks(core * (PLANES * SPOTS // 2) + number, 1)
        return carry

    shared = []
    half_way = PLANES * SPOTS // 2
    lax.fori_loop(0, half_way, head_a, 0)
    for side in range(SPOTS):
        goal = flip(spot, side)
        for piece in range(PIECES):
            if side > 0:
                arrive(1, core, piece, goal)
            source = shared_ref.at[2 * core + piece, goal]
            copy = remote(
                source,
                source,
                shared_send.at[2 * side + piece],
                shared_recv.at[2 * core + piece, goal],
                (1 - core, rank_of(plane, spot)),
            )
            copy.start()
            shared.append(copy)
    lax.fori_loop(half_way, PLANES * SPOTS, head_a, 0)
    dense(0, p_ref, ends)
    spreads[0].forward()
    back = Inward(out_ref, back_ref, *back_sems)
    everything = slice(0, local)
    for side, other, goal, stays in inward_targets(core, spot):
        if other is not core:
            for piece in range(PIECES):
                back.send(other, goal, stays, piece, 0, everything)
    for side in range(SPOTS):
        for piece in range(PIECES):
            target = shared_ref.at[2 * (1 - core) + piece, flip(spot, side)]
            remote(
                target,
                target,
                shared_send.at[0],
                shared_recv.at[2 * (1 - core) + piece, flip(spot, side)],
                (core, rank_of(plane, spot)),
            ).wait_recv()
    keep_qk = pltpu.make_async_copy(qk_ref, qk_hbm, local_sem.at[3])
    keep_qk.start()
    keep_shared = pltpu.make_async_copy(shared_ref, shared_hbm, local_sem.at[6])
    keep_shared.start()
    lax.fori_loop(0, half_way, head_b, 0)
    dense(1, q_ref, (core * (blocks - 1),))
    spreads[1].forward()
    for side, other, goal, stays in inward_targets(core, spot):
        if other is core:
            for piece in range(PIECES):
                back.send(other, goal, stays, piece, 0, everything)
    spreads[0].corner()
    spreads[0].finish()
    settle(
        g_ou_ref,
        [(tile, w_out_ref, (tile, outs + tile)) for tile in range(outs)]
        + [(outs + tile, w_up_ref, alternate(tile)) for tile in range(FF // CHUNK)],
    )
    keep_out = pltpu.make_async_copy(w_out_ref, w_out_hbm, local_sem.at[4])
    keep_out.start()
    keep_up = pltpu.make_async_copy(w_up_ref, w_up_hbm, local_sem.at[5])
    keep_up.start()
    spreads[1].corner()
    spreads[1].finish()
    finish_dy()
    for copy in sends:
        copy.wait_send()
    for copy in shared:
        copy.wait_send()
    back.finish(((everything,), (everything,)))
    for copy in (keep_x, keep_w, keep_qk, keep_shared, keep_out, keep_up):
        copy.wait()


def front(x, dy, vec, tab, w_qkv, w_out, w_up, w_down):
    micro, rows, _ = x.shape
    tokens = PIECES * rows
    local = rows // BLOCK
    blocks = PLANES * SPOTS * local
    spans = blocks // SPAN
    grid = (2, PLANES, SPOTS)
    shard = D // RANKS
    tile = (local, BLOCK, LANES)
    dma = pltpu.SemaphoreType.DMA
    struct = jax.ShapeDtypeStruct
    ou = (2 * shard, (D + FF) // 2)
    return pl.pallas_call(
        front_kernel,
        out_shape=(
            struct((2, SPOTS, PIECES) + tile, BF16),
            struct(x.shape, BF16),
            struct(dy.shape, BF16),
            struct(grid + w_down.shape, BF16),
            struct((D, 3 * D), BF16),
            struct((D, D), BF16),
            struct((D, FF), BF16),
            struct((PLANES, SPOTS, 2) + tile, BF16),
            struct((PLANES, SPOTS) + tile, BF16),
            struct((tokens, D), BF16),
            struct((blocks, BLOCK, LANES), F32),
            struct((VECTORS, D), F32),
            struct((FF // CHUNK, 1, CHUNK), F32),
            struct((1, 2 * LANES), jnp.int32),
            struct((4, 2 * LANES), jnp.int32),
        ),
        in_specs=[
            whole(ANY),
            whole(ANY),
            whole(ANY),
            whole(ANY),
            whole(),
            whole(),
            whole(),
            whole(ANY),
        ],
        out_specs=(whole(ANY),) * 9 + (whole(),) * 6,
        scratch_shapes=[
            VMEM((2 * shard, 3 * D // 2), BF16),
            VMEM(ou, BF16),
            VMEM(grid + (2 * shard, 3 * D // 2), BF16),
            VMEM(grid + ou, BF16),
            VMEM((D, 3 * D), BF16),
            VMEM((D, D), BF16),
            VMEM((D, FF), BF16),
            VMEM((PIECES, rows, D), BF16),
            VMEM(grid + vec.shape, BF16),
            VMEM(grid + tab.shape, jnp.int32),
            VMEM((1, 3 * D), F32),
            VMEM((2, SPOTS, PIECES, 3) + tile, BF16),
            VMEM((PLANES, SPOTS, 2) + tile, BF16),
            VMEM((PLANES, SPOTS) + tile, BF16),
            VMEM((PLANES, SPOTS) + tile, BF16),
            VMEM((spans, 2 * BLOCK, SPAN * BLOCK), F32),
            VMEM((spans, BLOCK, SPAN * BLOCK), F32),
            pltpu.SMEM((PLANES, SPOTS) + tab.shape, jnp.int32),
            dma((3, Gather.SENDS)),
            dma((3,) + grid),
            dma((3,)),
            dma((2, PlaneGather.SENDS)),
            dma((2, PLANES)),
            dma((2, 2, SPOTS, 2)),
            dma((2,)),
        ]
        + [dma((2,))] * 6
        + [
            dma((20,)),
            dma((PLANES, SPOTS, 2)),
            dma((2, PIECES)),
            dma((2 * SPOTS,)),
            dma((PLANES, SPOTS)),
            dma((14,)),
            dma((2, SPOTS, PIECES, 1)),
            dma((1, PIECES)),
            dma((7,)),
        ],
        compiler_params=pltpu.CompilerParams(
            vmem_limit_bytes=60 * 1024 * 1024, collective_id=1, has_side_effects=True
        ),
        name="front",
    )(x, dy, vec, tab, w_qkv, w_out, w_up, w_down)


def by_owner(out_ref, values):
    rows = D // RANKS
    width = values.shape[1] // 2
    for owner in range(RANKS):
        part = values[owner * rows : (owner + 1) * rows]
        out_ref[owner] = jnp.concatenate([part[:, :width], part[:, width:]], axis=0).astype(BF16)


def plane_middle_kernel(
    mixed_in_ref,
    x_ref,
    dy_ref,
    vec_ref,
    w_out_ref,
    up_shift_ref,
    w_up_ref,
    w_down_ref,
    hidden_ref,
    send_ref,
    dres_ref,
    g_out_ref,
    g_up_ref,
    g_down_ref,
    g_up_bias_ref,
    g_small_ref,
    mixed_ref,
    residual_ref,
    second_ref,
    second_t_ref,
    total_ref,
    dsecond_ref,
):
    pieces, rows, _ = x_ref.shape
    tokens = pieces * rows
    step = pl.program_id(0)
    low = low_lanes(rows)
    out_shift, gain, shift, down_shift = (vec_ref[number : number + 1] for number in (4, 5, 6, 7))

    @pl.when(step == 0)
    def _():
        core = lax.axis_index("gx")
        for piece in range(pieces):
            span = slice(piece * rows, (piece + 1) * rows)
            for spot in (0, 2):
                first = [mixed_in_ref[side, spot, piece].astype(F32) for side in range(2)]
                last = [mixed_in_ref[side, spot + 1, piece].astype(F32) for side in range(2)]
                own_first = jnp.where(core == 0, first[0], first[1])
                own_last = jnp.where(core == 0, last[0], last[1])
                tiles = (
                    jnp.where(low, swap_halves(first[0]), first[1]),
                    jnp.where(low, own_first, last[0]),
                    swap_halves(jnp.where(low, own_last, last[1])),
                )
                for number, tile in enumerate(tiles):
                    spread = 3 * (spot // 2) + number
                    mixed_ref[span, spread * LANES : (spread + 1) * LANES] = tile.astype(BF16)
        residual = x_ref[...].reshape(tokens, D).astype(F32) + (
            dot(mixed_ref[...], w_out_ref[...]) + out_shift
        )
        residual_ref[...] = residual
        normal, _ = norm_parts(residual)
        second = normal * gain + shift
        second_ref[...] = second.astype(BF16)
        second_t_ref[...] = second.T.astype(BF16)
        total_ref[...] = jnp.zeros_like(total_ref)
        dsecond_ref[...] = jnp.zeros_like(dsecond_ref)

    w_down = w_down_ref[...].reshape(CHUNK, D)
    upper = dot(second_ref[...], w_up_ref[...]) + up_shift_ref[0]
    factor = 0.7978845608028654
    square = upper * upper
    bent = jnp.tanh(factor * (upper + 0.044715 * (upper * square)))
    middle_half = 0.5 * (1.0 + bent)
    active = (upper * middle_half).astype(BF16)
    slope = middle_half + 0.5 * upper * (1.0 - bent * bent) * (
        factor + (3.0 * 0.044715 * factor) * square
    )
    dy = dy_ref[...]
    total_ref[...] += dot(active, w_down)
    g_down_ref[...] = dot_lt(active, dy).astype(BF16).reshape(g_down_ref.shape)
    dupper = (dot_rt(dy, w_down) * slope).astype(BF16)
    g_up_bias_ref[0] = jnp.sum(dupper.astype(F32), axis=0, keepdims=True)
    by_owner(g_up_ref, dot(second_t_ref[...], dupper))
    dsecond_ref[...] += dot_rt(dupper, w_up_ref[...])

    @pl.when(step == pl.num_programs(0) - 1)
    def _():
        residual = residual_ref[...]
        hidden_ref[...] = (
            (residual + (total_ref[...] + down_shift)).astype(BF16).reshape(x_ref.shape)
        )
        normal, inverse = norm_parts(residual)
        dsecond = dsecond_ref[...]
        grad_out = dy_ref[...].astype(F32)
        g_small_ref[0:1] = jnp.sum(dsecond * normal, axis=0, keepdims=True)
        g_small_ref[1:2] = jnp.sum(dsecond, axis=0, keepdims=True)
        g_small_ref[2:3] = jnp.sum(grad_out, axis=0, keepdims=True)
        dres = grad_out + norm_pull(dsecond, normal, inverse, gain)
        dres_ref[...] = dres
        branch = dres.astype(BF16)
        g_small_ref[3:4] = jnp.sum(branch.astype(F32), axis=0, keepdims=True)
        by_owner(g_out_ref, dot_lt(mixed_ref[...], branch))
        dmixed = dot_rt(branch, w_out_ref[...])
        for piece in range(pieces):
            span = slice(piece * rows, (piece + 1) * rows)
            for spot in (0, 2):
                tiles = [
                    dmixed[span, number * LANES : (number + 1) * LANES]
                    for number in range(3 * (spot // 2), 3 * (spot // 2) + 3)
                ]
                flipped = [swap_halves(tile) for tile in tiles]
                send_ref[0, spot, piece] = jnp.where(low, tiles[1], flipped[0]).astype(BF16)
                send_ref[1, spot, piece] = jnp.where(low, tiles[1], tiles[0]).astype(BF16)
                send_ref[0, spot + 1, piece] = jnp.where(low, flipped[2], tiles[1]).astype(BF16)
                send_ref[1, spot + 1, piece] = flipped[2].astype(BF16)


def plane_middle(mixed_in, x, dy, vec, w_out, up_shift, w_up, w_down):
    pieces, rows, _ = x.shape
    tokens = pieces * rows
    shard = D // RANKS

    def fixed(shape):
        return pl.BlockSpec(shape, lambda step: (0,) * len(shape))

    steps = FF // CHUNK
    down = pl.BlockSpec((2, LANES, D), lambda step: (0, step, 0))
    return pl.pallas_call(
        plane_middle_kernel,
        grid=(steps,),
        out_shape=(
            jax.ShapeDtypeStruct(x.shape, BF16),
            jax.ShapeDtypeStruct(mixed_in.shape, BF16),
            jax.ShapeDtypeStruct((tokens, D), F32),
            jax.ShapeDtypeStruct((RANKS, 2 * shard, D // 2), BF16),
            jax.ShapeDtypeStruct((RANKS, 2 * shard, FF // 2), BF16),
            jax.ShapeDtypeStruct((2, FF // 2, D), BF16),
            jax.ShapeDtypeStruct((steps, 1, CHUNK), F32),
            jax.ShapeDtypeStruct((4, D), F32),
        ),
        in_specs=[
            fixed(mixed_in.shape),
            fixed(x.shape),
            fixed((tokens, D)),
            fixed(vec.shape),
            fixed((D, D)),
            pl.BlockSpec((1, 1, CHUNK), lambda step: (step, 0, 0)),
            pl.BlockSpec((D, CHUNK), lambda step: (0, step)),
            down,
        ],
        out_specs=(
            fixed(x.shape),
            fixed(mixed_in.shape),
            fixed((tokens, D)),
            fixed((RANKS, 2 * shard, D // 2)),
            pl.BlockSpec((RANKS, 2 * shard, LANES), lambda step: (0, 0, step)),
            down,
            pl.BlockSpec((1, 1, CHUNK), lambda step: (step, 0, 0)),
            fixed((4, D)),
        ),
        scratch_shapes=[
            VMEM((tokens, D), BF16),
            VMEM((tokens, D), F32),
            VMEM((tokens, D), BF16),
            VMEM((D, tokens), BF16),
            VMEM((tokens, D), F32),
            VMEM((tokens, D), F32),
        ],
        compiler_params=params_of(56),
        name="plane_middle",
    )(mixed_in, x, dy, vec, w_out, up_shift, w_up, w_down)


class Reduce:
    SENDS = 4 + 2 + 2 + 3
    RECVS = SENDS

    def __init__(self, source, total, near, corner_x, corner_y, side_x, side_y, far, out, sems):
        self.source, self.total, self.near = source, total, near
        self.corner = {1: corner_x, 2: corner_y}
        self.side = {1: side_x, 2: side_y}
        self.far, self.out = far, out
        self.send_sem, self.recv_sem, self.local_sem = sems
        self.core, self.plane, self.spot = place_here()
        self.copies = []
        self.locals = []

    def start(self):
        sibling = (1 - self.core, rank_of(self.plane, self.spot))
        for number, side in enumerate((3, 1, 2, 0)):
            spot = flip(self.spot, side)
            copy = remote(
                self.source.at[1 - self.core, :, spot],
                self.near.at[:, spot],
                self.send_sem.at[number],
                self.recv_sem.at[number],
                sibling,
            )
            copy.start()
            self.copies.append(copy)
            keep = pltpu.make_async_copy(
                self.source.at[self.core, :, spot],
                self.total.at[:, spot],
                self.local_sem.at[number],
            )
            keep.start()
            self.locals.append(keep)

    def take(self, number, side):
        self.copies[number].wait_recv()
        self.locals[number].wait()
        spot = flip(self.spot, side)

        def add(plane, carry):
            self.total[plane, spot] = (
                self.total[plane, spot].astype(F32) + self.near[plane, spot].astype(F32)
            ).astype(self.total.dtype)
            return carry

        lax.fori_loop(0, PLANES, add, 0)

    def corners(self):
        self.take(0, 3)
        spot = flip(self.spot, 3)
        index = 4
        self.corner_copies = []
        for bits in range(PLANES):
            side = 2 if bits < 2 else 1
            self.corner_copies.append(None)
            plane = flip(self.plane, bits)
            copy = remote(
                self.total.at[plane, spot],
                self.corner[side].at[bits % 2],
                self.send_sem.at[index + bits],
                self.recv_sem.at[index + bits],
                (self.core, rank_of(self.plane, flip(self.spot, side))),
            )
            copy.start()
            self.corner_copies[bits] = copy

    def sides(self):
        self.take(1, 1)
        self.take(2, 2)
        self.side_copies = {}
        for side in (1, 2):
            spot = flip(self.spot, side)
            came = 3 - side
            for bits in (0, 1) if came == 2 else (2, 3):
                self.corner_copies[bits].wait_recv()
                plane = flip(self.plane, bits)
                self.total[plane, spot] = (
                    self.total[plane, spot].astype(F32)
                    + self.corner[came][bits % 2].astype(F32)
                ).astype(self.total.dtype)
            copy = remote(
                self.total.at[:, spot],
                self.side[side],
                self.send_sem.at[7 + side],
                self.recv_sem.at[7 + side],
                (self.core, rank_of(self.plane, spot)),
            )
            copy.start()
            self.side_copies[side] = copy

    def columns(self):
        self.take(3, 0)
        for side in (1, 2):
            self.side_copies[side].wait_recv()

        def add(plane, carry):
            self.total[plane, self.spot] = (
                self.total[plane, self.spot].astype(F32)
                + self.side[1][plane].astype(F32)
                + self.side[2][plane].astype(F32)
            ).astype(self.total.dtype)
            return carry

        lax.fori_loop(0, PLANES, add, 0)
        self.far_copies = []
        for bits in range(1, PLANES):
            plane = flip(self.plane, bits)
            copy = remote(
                self.total.at[plane, self.spot],
                self.far.at[bits - 1],
                self.send_sem.at[9 + bits],
                self.recv_sem.at[9 + bits],
                (self.core, rank_of(plane, self.spot)),
            )
            copy.start()
            self.far_copies.append(copy)

    def finish(self):
        value = self.total[self.plane, self.spot].astype(F32)
        for bits in range(1, PLANES):
            self.far_copies[bits - 1].wait_recv()
            value = value + self.far[bits - 1].astype(F32)
        self.out[...] = value
        for copy in self.copies + self.corner_copies + self.far_copies:
            copy.wait_send()
        for side in (1, 2):
            self.side_copies[side].wait_send()


REDUCE_SEMS = 13


def reduce_scratch(shape, kind):
    tail = shape[3:]
    return [
        VMEM((PLANES, SPOTS) + tail, kind),
        VMEM((PLANES, SPOTS) + tail, kind),
        VMEM((2,) + tail, kind),
        VMEM((2,) + tail, kind),
        VMEM((PLANES,) + tail, kind),
        VMEM((PLANES,) + tail, kind),
        VMEM((PLANES - 1,) + tail, kind),
    ]


class Doubling:
    STEPS = 5

    def __init__(self, totals, boxes, send_sem, recv_sem):
        self.totals, self.boxes = totals, boxes
        self.send_sem, self.recv_sem = send_sem, recv_sem
        core, plane, spot = place_here()
        self.partners = (
            (1 - core, rank_of(plane, spot)),
            (core, rank_of(plane, flip(spot, 1))),
            (core, rank_of(plane, flip(spot, 2))),
            (core, rank_of(flip(plane, 1), spot)),
            (core, rank_of(flip(plane, 2), spot)),
        )
        self.copies = []

    def start(self, step):
        self.copies = []
        for number, (total, box) in enumerate(zip(self.totals, self.boxes)):
            copy = remote(
                total,
                box.at[step],
                self.send_sem.at[step, number],
                self.recv_sem.at[step, number],
                self.partners[step],
            )
            copy.start()
            self.copies.append(copy)

    def finish(self, step):
        for copy, total, box in zip(self.copies, self.totals, self.boxes):
            copy.wait()
            total[...] += box[step]


PARTS = 3


def finish_kernel(
    recv_ref,
    normed_ref,
    x_ref,
    dres_hbm,
    vec_ref,
    w_hbm,
    g_mid_ref,
    g_up_bias_ref,
    grad_ref,
    g_qkv_ref,
    rows_out_ref,
    tiles_out_ref,
    *scratch,
):
    sources, scratch = scratch[:PARTS], scratch[PARTS:]
    buffers, scratch = scratch[: 7 * PARTS], scratch[7 * PARTS :]
    packed_ref, dnormed_ref, gradient_ref, dres_ref, w_ref = scratch[:5]
    rows_ref, tiles_ref, rows_box, tiles_box = scratch[5:9]
    send_sem, recv_sem, local_sem, load_sem, sum_send, sum_recv = scratch[9:15]
    move_sems = scratch[15:18]
    pieces, rows, _ = x_ref.shape
    tokens = pieces * rows
    core, plane, spot = place_here()
    low = low_lanes(rows)

    load_w = pltpu.make_async_copy(w_hbm, w_ref, load_sem.at[0])
    load_dres = pltpu.make_async_copy(dres_hbm, dres_ref, load_sem.at[1])
    load_w.start()
    load_dres.start()
    greet(all_partners(core, plane, spot))

    def put(tile, piece, value):
        side, chunk = tile // HALF_TILES, tile % HALF_TILES
        packed_ref[
            piece * rows : (piece + 1) * rows,
            chunk * CHUNK + side * LANES : chunk * CHUNK + (side + 1) * LANES,
        ] = value.astype(BF16)

    for piece in range(pieces):
        seconds = []
        for goal in range(SPOTS):
            first = recv_ref[0, goal, piece, QUERIES].astype(F32)
            second = recv_ref[1, goal, piece, QUERIES].astype(F32)
            put(goal, piece, jnp.where(low, first, jnp.where(core == 0, first, second)))
            seconds.append(second)
            base = D // LANES + 3 * goal
            put(base, piece, recv_ref[0, goal, piece, KEYS_A])
            put(base + 1, piece, recv_ref[1, goal, piece, KEYS_A])
            put(base + 2, piece, recv_ref[core, goal, piece, KEYS_B])
        for number in range(2):
            put(
                SPOTS + number,
                piece,
                jnp.where(low, seconds[2 * number], swap_halves(seconds[2 * number + 1])),
            )

    load_w.wait()
    for chunk in range(HALF_TILES):
        columns = slice(chunk * CHUNK, (chunk + 1) * CHUNK)
        share = dot_rt(packed_ref[:, columns], w_ref[:, columns])
        if chunk == 0:
            dnormed_ref[...] = share
        else:
            dnormed_ref[...] += share
    normal, inverse = norm_parts(x_ref[...].reshape(tokens, D).astype(F32))
    dnormed = dnormed_ref[...]
    load_dres.wait()
    gradient = dres_ref[...] + norm_pull(dnormed, normal, inverse, vec_ref[0:1])
    gradient_ref[...] = gradient.astype(BF16).reshape(x_ref.shape)
    finish_grad = from_planes(gradient_ref, grad_ref, *move_sems)

    rows_ref[0:1] = jnp.sum(dnormed * normal, axis=0, keepdims=True)
    rows_ref[1:2] = jnp.sum(dnormed, axis=0, keepdims=True)
    rows_ref[2:6] = g_mid_ref[...]
    rows_ref[6:8] = jnp.zeros((2, D), F32)
    tiles_ref[...] = jnp.zeros_like(tiles_ref)
    for step in range(FF // CHUNK):
        tiles_ref[step : step + 1] = g_up_bias_ref[step]
    for chunk in range(HALF_TILES):
        number = FF // CHUNK + chunk
        tiles_ref[number : number + 1] = jnp.sum(
            packed_ref[:, chunk * CHUNK : (chunk + 1) * CHUNK].astype(F32), axis=0, keepdims=True
        )
    sums = Doubling((rows_ref, tiles_ref), (rows_box, tiles_box), sum_send, sum_recv)
    sums.start(0)

    width = HALF_TILES // PARTS * LANES
    reduces = [
        Reduce(
            sources[part],
            *buffers[7 * part : 7 * part + 7],
            g_qkv_ref.at[:, part * width : (part + 1) * width],
            (send_sem.at[part], recv_sem.at[part], local_sem.at[part]),
        )
        for part in range(PARTS)
    ]
    shard = D // RANKS
    normed_t = normed_ref[...].astype(F32).T.astype(BF16)
    for part in range(PARTS):
        for number in range(HALF_TILES // PARTS):
            chunk = part * (HALF_TILES // PARTS) + number
            values = dot(normed_t, packed_ref[:, chunk * CHUNK : (chunk + 1) * CHUNK])
            columns = slice(number * LANES, (number + 1) * LANES)
            for owner in range(RANKS):
                mine = values[owner * shard : (owner + 1) * shard]
                sources[part][
                    owner // (PLANES * SPOTS), owner // SPOTS % PLANES, owner % SPOTS, :, columns
                ] = jnp.concatenate([mine[:, :LANES], mine[:, LANES:]], axis=0).astype(BF16)
        reduces[part].start()
        if part > 0:
            reduces[part - 1].corners()
        if part > 1:
            reduces[part - 2].sides()
    sums.finish(0)
    sums.start(1)
    reduces[2].corners()
    reduces[1].sides()
    sums.finish(1)
    sums.start(2)
    reduces[0].columns()
    reduces[2].sides()
    sums.finish(2)
    sums.start(3)
    reduces[1].columns()
    sums.finish(3)
    sums.start(4)
    reduces[2].columns()
    sums.finish(4)
    for one in reduces:
        one.finish()
    rows_out_ref[...] = rows_ref[...]
    tiles_out_ref[...] = tiles_ref[...]
    finish_grad()


def finish_layer(recv, normed, x, dres, vec, w, g_mid, g_up_bias):
    pieces, rows, _ = x.shape
    tokens = pieces * rows
    shard = D // RANKS
    grid = (2, PLANES, SPOTS)
    part = grid + (2 * shard, HALF_TILES // PARTS * LANES)
    buffers = []
    for _ in range(PARTS):
        buffers += reduce_scratch(part, BF16)
    tiles = -(-(FF // CHUNK + HALF_TILES) // 8) * 8
    dma = pltpu.SemaphoreType.DMA
    return pl.pallas_call(
        finish_kernel,
        out_shape=(
            jax.ShapeDtypeStruct(x.shape, BF16),
            jax.ShapeDtypeStruct((2 * shard, 3 * D // 2), F32),
            jax.ShapeDtypeStruct((8, D), F32),
            jax.ShapeDtypeStruct((tiles, CHUNK), F32),
        ),
        in_specs=[
            whole(),
            whole(),
            whole(),
            whole(ANY),
            whole(),
            whole(ANY),
            whole(),
            whole(),
        ],
        out_specs=(whole(ANY), whole(), whole(), whole()),
        scratch_shapes=[VMEM(part, BF16)] * PARTS
        + buffers
        + [
            VMEM((tokens, 3 * D), BF16),
            VMEM((tokens, D), F32),
            VMEM(x.shape, BF16),
            VMEM((tokens, D), F32),
            VMEM(w.shape, BF16),
            VMEM((8, D), F32),
            VMEM((tiles, CHUNK), F32),
            VMEM((Doubling.STEPS, 8, D), F32),
            VMEM((Doubling.STEPS, tiles, CHUNK), F32),
            dma((PARTS, REDUCE_SEMS)),
            dma((PARTS, REDUCE_SEMS)),
            dma((PARTS, 4)),
            dma((2,)),
            dma((Doubling.STEPS, 2)),
            dma((Doubling.STEPS, 2)),
            dma((2,)),
            dma((2,)),
            dma((2,)),
        ],
        compiler_params=pltpu.CompilerParams(
            vmem_limit_bytes=60 * 1024 * 1024, collective_id=2, has_side_effects=True
        ),
        name="finish_layer",
    )(recv, normed, x, dres, vec, w, g_mid, g_up_bias)


def fold_columns(array):
    half = array.shape[1] // 2
    return jnp.concatenate([array[:, :half], array[:, half:]], axis=0)


def unfold_columns(array):
    half = array.shape[0] // 2
    return jnp.concatenate([array[:half], array[half:]], axis=1)


def plane_shards(
    hidden_in,
    rand_table,
    norm1_gain,
    norm1_bias,
    w_qkv,
    query_bias,
    value_bias,
    w_out,
    out_bias,
    norm2_gain,
    norm2_bias,
    w_up,
    up_bias,
    w_down,
    down_bias,
    cotangent,
):
    micro, rows, _ = hidden_in.shape
    local = rows // BLOCK
    own = norm1_gain.shape[0]
    order = [natural_block(entry) for entry in column_order()]
    inverse = [order.index(number) for number in range(len(order))]

    def in_row(vector, number):
        return jnp.pad(vector[None], ((number, 15 - number), (0, LANES - vector.shape[0])))

    vec = functools.reduce(
        jnp.add,
        [
            in_row(vector, number)
            for number, vector in enumerate(
                (
                    norm1_gain,
                    norm1_bias,
                    query_bias,
                    value_bias,
                    out_bias,
                    norm2_gain,
                    norm2_bias,
                    down_bias,
                    up_bias,
                )
            )
        ],
    )
    tab = jnp.pad(
        rand_table.reshape(micro, local * RANDOM), ((0, 8 - micro), (0, LANES - local * RANDOM))
    )
    (
        mixed,
        x,
        dy,
        w_down_all,
        w_qkv_all,
        w_out_all,
        w_up_all,
        qk,
        shared,
        normed,
        lse,
        vectors,
        up_shift,
        table,
        sorted_table,
    ) = front(hidden_in, cotangent, vec, tab, w_qkv, w_out, w_up, w_down)
    mixed = mixed.reshape(2, SPOTS, PIECES, rows, LANES)
    hidden, grad_send, dres, g_out, g_up, g_down, g_up_bias, g_mid = plane_middle(
        mixed,
        x,
        dy.reshape(micro * rows, D),
        vectors,
        w_out_all,
        up_shift,
        w_up_all,
        w_down_all.reshape(2, FF // 2, D),
    )
    grid = (2, PLANES, SPOTS)
    dqkv, hidden_out, t_out, t_up, t_down = plane_attention_back(
        table,
        sorted_table,
        qk,
        shared,
        grad_send.reshape(2, SPOTS, PIECES, local, BLOCK, LANES),
        lse,
        hidden,
        [
            g_out.reshape(grid + g_out.shape[1:]),
            g_up.reshape(grid + g_up.shape[1:]),
            g_down.reshape(grid + (FF // RANKS, D)),
        ],
    )
    dqkv = dqkv.reshape(2, SPOTS, PIECES, 3, rows, LANES)
    grad_hidden, t_qkv, sum_rows, sum_tiles = finish_layer(
        dqkv, normed, x, dres, vectors, w_qkv_all, g_mid, g_up_bias
    )

    mine = lax.axis_index("gx") * PLANES * SPOTS + lax.axis_index("gy")
    sum_tiles = sum_tiles.reshape(-1, 2, LANES)
    g_bias = sum_tiles[FF // CHUNK : FF // CHUNK + HALF_TILES].swapaxes(0, 1).reshape(1, 3 * D)
    g_bias = take_blocks(g_bias, inverse)
    sum_rows = jnp.concatenate([sum_rows, g_bias[:, :D], g_bias[:, 2 * D :]], axis=0)
    parts = lax.dynamic_slice_in_dim(sum_rows, mine * own, own, 1)
    g_up_bias = sum_tiles[: FF // CHUNK].swapaxes(0, 1).reshape(FF)
    g_up_bias = lax.dynamic_slice_in_dim(g_up_bias, mine * (FF // RANKS), FF // RANKS, 0)
    return (
        hidden_out,
        grad_hidden.astype(F32),
        parts[0],
        parts[1],
        take_blocks(unfold_columns(t_qkv), inverse),
        parts[8],
        parts[9],
        unfold_columns(t_out),
        parts[5],
        parts[2],
        parts[3],
        unfold_columns(t_up),
        g_up_bias,
        t_down,
        parts[4],
    )


def shards(*arrays):
    micro, rows, _ = arrays[0].shape
    fits = lax.axis_size("gx") == 2 and lax.axis_size("gy") == PLANES * SPOTS
    fits = fits and micro == 2 and rows % BLOCK == 0
    return (plane_shards if fits else general_shards)(*arrays)


def solution(mesh):
    tokens = P(None, AXES, None)
    vector = P(AXES)
    matrix = P(AXES, None)
    placed = (
        tokens,
        tokens,
        vector,
        vector,
        matrix,
        vector,
        vector,
        matrix,
        vector,
        vector,
        vector,
        matrix,
        vector,
        matrix,
        vector,
        tokens,
    )
    returned = (
        tokens,
        tokens,
        vector,
        vector,
        matrix,
        vector,
        vector,
        matrix,
        vector,
        vector,
        vector,
        matrix,
        vector,
        matrix,
        vector,
    )
    return jax.shard_map(
        shards, mesh=mesh, in_specs=placed, out_specs=returned, check_vma=False
    )
```

```python
import functools

import jax
import jax.numpy as jnp
from jax import lax
from jax.experimental import pallas as pl
from jax.experimental.pallas import tpu as pltpu
from jax.sharding import PartitionSpec as P

HEADS = 12
HEAD_DIM = 64
D = 768
FF = 3072
BLOCK = 64
RANDOM = 3
LANES = 2 * HEAD_DIM
EPSILON = 1e-05
NEGATIVE = -1e30
SCALE = HEAD_DIM**-0.5
CHUNK = 256
SPAN = 8

F32 = jnp.float32
BF16 = jnp.bfloat16
VMEM = pltpu.VMEM


def whole(space=VMEM):
    return pl.BlockSpec(memory_space=space)


def params_of(megabytes):
    return pltpu.CompilerParams(vmem_limit_bytes=megabytes * 1024 * 1024)


def head_place(head):
    return (head // 3) * 4 + head % 3


def dot(left, right):
    return lax.dot_general(left, right, (((1,), (0,)), ((), ())), preferred_element_type=F32)


def dot_rt(left, right):
    return lax.dot_general(left, right, (((1,), (1,)), ((), ())), preferred_element_type=F32)


def dot_lt(left, right):
    return lax.dot_general(left, right, (((0,), (0,)), ((), ())), preferred_element_type=F32)


def swap_halves(tile):
    return pltpu.roll(tile, HEAD_DIM, axis=tile.ndim - 1)


def low_lanes(rows):
    return lax.broadcasted_iota(jnp.int32, (rows, LANES), 1) < HEAD_DIM


def norm_parts(values):
    centre = values - jnp.mean(values, axis=-1, keepdims=True)
    spread = jnp.mean(centre * centre, axis=-1, keepdims=True)
    inverse = lax.rsqrt(spread + EPSILON)
    return centre * inverse, inverse


def norm_pull(grad, normal, inverse, gain):
    scaled = grad * gain
    return inverse * (
        scaled
        - jnp.mean(scaled, axis=-1, keepdims=True)
        - normal * jnp.mean(scaled * normal, axis=-1, keepdims=True)
    )


def qkv_kernel(x_ref, gain_ref, shift_ref, w_ref, bias_ref, normed_ref, send_ref):
    micro, rows, _ = x_ref.shape
    values = x_ref[...].reshape(micro * rows, D).astype(F32)
    normal, _ = norm_parts(values)
    normed_ref[...] = (normal * gain_ref[...] + shift_ref[...]).astype(BF16)
    low = low_lanes(rows)
    for chunk in range(3 * D // CHUNK):
        columns = slice(chunk * CHUNK, (chunk + 1) * CHUNK)
        packed = dot(normed_ref[...], w_ref[:, columns]) + bias_ref[:, columns]
        if chunk < D // CHUNK:
            packed = packed.astype(BF16).astype(F32) * SCALE
        for tile in range(CHUNK // LANES):
            part = packed[:, tile * LANES : (tile + 1) * LANES]
            first, second = part[:rows], part[rows:]
            if chunk < D // CHUNK:
                head = (chunk * CHUNK // LANES + tile) * 2
                even = jnp.where(low, first, swap_halves(second))
                odd = jnp.where(low, swap_halves(first), second)
                send_ref[head_place(head), 0] = even.astype(BF16)
                send_ref[head_place(head + 1), 0] = odd.astype(BF16)
            else:
                head = (chunk * CHUNK - D) // LANES + tile
                send_ref[head_place(head), 1] = first.astype(BF16)
                send_ref[head_place(head), 2] = swap_halves(second).astype(BF16)


def qkv_forward(x, gain, shift, w, bias, groups):
    micro, rows, _ = x.shape
    return pl.pallas_call(
        qkv_kernel,
        out_shape=(
            jax.ShapeDtypeStruct((micro * rows, D), BF16),
            jax.ShapeDtypeStruct((groups, 3, rows, LANES), BF16),
        ),
        in_specs=[whole()] * 5,
        out_specs=(whole(), whole()),
        compiler_params=params_of(48),
        name="qkv_forward",
    )(x, gain, shift, w, bias)


def half_mask(low_half):
    lane = lax.broadcasted_iota(jnp.int32, (1, LANES), 1)
    keep = (lane < HEAD_DIM) if low_half else (lane >= HEAD_DIM)
    return jnp.where(keep, 1.0, 0.0).astype(BF16)


def inner_slots(pick, block, blocks):
    ids, bias = picked_slots([pick(block, number) for number in range(RANDOM)], block, blocks)
    edge = (block == 0) | (block == blocks - 1)
    ids[0] = jnp.maximum(ids[0], 0)
    ids[2] = jnp.minimum(ids[2], blocks - 1)
    return ids, bias + jnp.where(edge, NEGATIVE, 0.0).astype(F32)


def slots_of(table_ref, micro, block, blocks):
    picks = [table_ref[micro, block * RANDOM + number] for number in range(RANDOM)]
    return picked_slots(picks, block, blocks)


def picked_slots(picks, block, blocks):
    last = blocks - 1
    ids = [block - 1, block, block + 1, 0, last] + picks
    dropped = [None, None, None, block == 1, block == last - 1]
    for number in range(RANDOM):
        pick = picks[number]
        bad = (jnp.abs(pick - block) <= 1) | (pick == 0) | (pick == last)
        for earlier in range(number):
            bad = bad | (pick == picks[earlier])
        dropped.append(bad)
    lane = lax.broadcasted_iota(jnp.int32, (1, LANES), 1)
    tiles = []
    for pair in range(len(ids) // 2):
        level = [
            0.0 if bad is None else jnp.where(bad, NEGATIVE, 0.0).astype(F32)
            for bad in dropped[2 * pair : 2 * pair + 2]
        ]
        tiles.append(jnp.where(lane < HEAD_DIM, level[0], level[1]))
    return ids, jnp.concatenate(tiles, axis=1)


def attend_kernel(table_ref, qkv_ref, out_ref, lse_ref, s_ref):
    groups, _, local, _, _ = qkv_ref.shape
    blocks = groups * local
    low = low_lanes(BLOCK)
    masks = [half_mask(True), half_mask(False)]

    def load(component, block):
        return qkv_ref[block // local, component, block % local]

    def sparse(block, carry):
        mixed, logs = [], []
        for micro in range(2):
            ids, bias = slots_of(table_ref, micro, block, blocks)
            keys = jnp.concatenate([load(1 + micro, spot) for spot in ids], axis=0)
            query = load(0, block) * masks[micro]
            scores = dot_rt(query, keys) + bias
            top = jnp.max(scores, axis=1, keepdims=True)
            powered = jnp.exp(scores - top)
            total = jnp.sum(powered, axis=1, keepdims=True)
            mixed.append(dot(powered.astype(BF16), keys) * (1.0 / total))
            logs.append(top + jnp.log(total))
        out_ref[block // local, block % local] = jnp.where(low, mixed[1], mixed[0]).astype(BF16)
        lse_ref[block] = jnp.where(low, logs[0], logs[1])
        return carry

    lax.fori_loop(1, blocks - 1, sparse, 0)

    spans = blocks // SPAN
    ends = (0, blocks - 1)
    results = []
    for micro in range(2):
        query = jnp.concatenate([load(0, end) for end in ends], axis=0) * masks[micro]

        def keys_at(span, micro=micro):
            return jnp.concatenate(
                [load(1 + micro, span * SPAN + spot) for spot in range(SPAN)], axis=0
            )

        def first_pass(span, top, query=query, keys_at=keys_at):
            scores = dot_rt(query, keys_at(span))
            s_ref[span] = scores
            return jnp.maximum(top, jnp.max(scores, axis=1, keepdims=True))

        top = lax.fori_loop(0, spans, first_pass, jnp.full((2 * BLOCK, 1), NEGATIVE, F32))

        def second_pass(span, carry, top=top, keys_at=keys_at):
            total, mixed = carry
            powered = jnp.exp(s_ref[span] - top)
            return (
                total + jnp.sum(powered, axis=1, keepdims=True),
                mixed + dot(powered.astype(BF16), keys_at(span)),
            )

        total, mixed = lax.fori_loop(
            0,
            spans,
            second_pass,
            (jnp.zeros((2 * BLOCK, 1), F32), jnp.zeros((2 * BLOCK, LANES), F32)),
        )
        results.append((mixed * (1.0 / total), top + jnp.log(total)))
    for place, end in enumerate(ends):
        rows = slice(place * BLOCK, (place + 1) * BLOCK)
        out_ref[end // local, end % local] = jnp.where(
            low, results[1][0][rows], results[0][0][rows]
        ).astype(BF16)
        lse_ref[end] = jnp.where(low, results[0][1][rows], results[1][1][rows])


def attention_forward(table, qkv):
    groups, _, local, _, _ = qkv.shape
    blocks = groups * local
    return pl.pallas_call(
        attend_kernel,
        out_shape=(
            jax.ShapeDtypeStruct((groups, local, BLOCK, LANES), BF16),
            jax.ShapeDtypeStruct((blocks, BLOCK, LANES), F32),
        ),
        in_specs=[whole(pltpu.SMEM), whole()],
        out_specs=(whole(), whole()),
        scratch_shapes=[VMEM((blocks // SPAN, 2 * BLOCK, SPAN * BLOCK), F32)],
        compiler_params=params_of(48),
        name="attention_forward",
    )(table, qkv)


def attend_back_kernel(table_ref, qkv_ref, grad_ref, lse_ref, out_ref, sums_ref, p_ref, dp_ref):
    groups, _, local, _, _ = qkv_ref.shape
    blocks = groups * local
    low = low_lanes(BLOCK)
    masks = [half_mask(True), half_mask(False)]

    def load(component, block):
        return qkv_ref[block // local, component, block % local]

    def load_grad(block):
        return grad_ref[block // local, block % local]

    def clear(block, carry):
        for micro in range(2):
            sums_ref[micro, block] = jnp.zeros((BLOCK, LANES), F32)
        return carry

    lax.fori_loop(0, blocks, clear, 0)

    def sparse(block, carry):
        grads = []
        for micro in range(2):
            ids, bias = slots_of(table_ref, micro, block, blocks)
            keys = jnp.concatenate([load(1 + micro, spot) for spot in ids], axis=0)
            both = jnp.concatenate(
                [load(0, block) * masks[micro], load_grad(block) * masks[1 - micro]], axis=0
            )
            products = dot_rt(both, keys)
            logs = lse_ref[block][:, micro * HEAD_DIM : micro * HEAD_DIM + 1]
            weights = jnp.exp(products[:BLOCK] + bias - logs)
            grad_weights = products[BLOCK:]
            delta = jnp.sum(weights * grad_weights, axis=1, keepdims=True)
            grad_scores = weights * (grad_weights - delta)
            stacked = jnp.concatenate([grad_scores, weights], axis=0).astype(BF16)
            grads.append(dot(stacked[:BLOCK], keys))
            shares = dot_lt(stacked, both)
            for place, spot in enumerate(ids):
                sums_ref[micro, spot] += shares[place * BLOCK : (place + 1) * BLOCK]
        out_ref[block // local, 0, block % local] = (
            jnp.where(low, grads[0], grads[1]) * SCALE
        ).astype(BF16)
        return carry

    lax.fori_loop(1, blocks - 1, sparse, 0)

    spans = blocks // SPAN
    ends = (0, blocks - 1)
    results = []
    for micro in range(2):
        query = jnp.concatenate([load(0, end) for end in ends], axis=0) * masks[micro]
        grad = jnp.concatenate([load_grad(end) for end in ends], axis=0) * masks[1 - micro]
        both = jnp.concatenate([query, grad], axis=0)
        logs = jnp.concatenate(
            [lse_ref[end][:, micro * HEAD_DIM : micro * HEAD_DIM + 1] for end in ends], axis=0
        )

        def keys_at(span, micro=micro):
            return jnp.concatenate(
                [load(1 + micro, span * SPAN + spot) for spot in range(SPAN)], axis=0
            )

        def first_pass(span, delta, both=both, logs=logs, keys_at=keys_at):
            products = dot_rt(both, keys_at(span))
            weights = jnp.exp(products[: 2 * BLOCK] - logs)
            grad_weights = products[2 * BLOCK :]
            p_ref[span] = weights
            dp_ref[span] = grad_weights
            return delta + jnp.sum(weights * grad_weights, axis=1, keepdims=True)

        delta = lax.fori_loop(0, spans, first_pass, jnp.zeros((2 * BLOCK, 1), F32))

        def second_pass(span, carry, delta=delta, both=both, keys_at=keys_at, micro=micro):
            weights = p_ref[span]
            grad_scores = weights * (dp_ref[span] - delta)
            stacked = jnp.concatenate([grad_scores, weights], axis=0).astype(BF16)
            shares = dot_lt(stacked, both)
            for spot in range(SPAN):
                sums_ref[micro, span * SPAN + spot] += shares[spot * BLOCK : (spot + 1) * BLOCK]
            return carry + dot(stacked[: 2 * BLOCK], keys_at(span))

        results.append(
            lax.fori_loop(0, spans, second_pass, jnp.zeros((2 * BLOCK, LANES), F32))
        )
    for place, end in enumerate(ends):
        rows = slice(place * BLOCK, (place + 1) * BLOCK)
        out_ref[end // local, 0, end % local] = (
            jnp.where(low, results[0][rows], results[1][rows]) * SCALE
        ).astype(BF16)

    def finish(block, carry):
        for micro in range(2):
            out_ref[block // local, 1 + micro, block % local] = sums_ref[micro, block].astype(BF16)
        return carry

    lax.fori_loop(0, blocks, finish, 0)


def attention_backward(table, qkv, grad, lse):
    groups, _, local, _, _ = qkv.shape
    blocks = groups * local
    spans = VMEM((blocks // SPAN, 2 * BLOCK, SPAN * BLOCK), F32)
    return pl.pallas_call(
        attend_back_kernel,
        out_shape=jax.ShapeDtypeStruct(qkv.shape, BF16),
        in_specs=[whole(pltpu.SMEM), whole(), whole(), whole()],
        out_specs=whole(),
        scratch_shapes=[VMEM((2, blocks, BLOCK, LANES), F32), spans, spans],
        compiler_params=params_of(48),
        name="attention_backward",
    )(table, qkv, grad, lse)


def middle_kernel(
    mixed_in_ref,
    x_ref,
    dy_ref,
    w_out_ref,
    out_shift_ref,
    gain_ref,
    shift_ref,
    up_shift_ref,
    down_shift_ref,
    w_up_ref,
    w_down_ref,
    hidden_ref,
    send_ref,
    dres_ref,
    g_out_ref,
    g_up_ref,
    g_down_ref,
    g_up_bias_ref,
    g_small_ref,
    mixed_ref,
    residual_ref,
    second_ref,
    second_t_ref,
    total_ref,
    dsecond_ref,
):
    micro, rows, _ = x_ref.shape
    step = pl.program_id(0)
    low = low_lanes(rows)

    @pl.when(step == 0)
    def _():
        for pair in range(HEADS // 2):
            even = mixed_in_ref[head_place(2 * pair)].astype(F32)
            odd = mixed_in_ref[head_place(2 * pair + 1)].astype(F32)
            columns = slice(pair * LANES, (pair + 1) * LANES)
            mixed_ref[:rows, columns] = jnp.where(low, swap_halves(even), odd).astype(BF16)
            mixed_ref[rows:, columns] = jnp.where(low, even, swap_halves(odd)).astype(BF16)
        residual = x_ref[...].reshape(micro * rows, D).astype(F32) + (
            dot(mixed_ref[...], w_out_ref[...]) + out_shift_ref[...]
        )
        residual_ref[...] = residual
        normal, _ = norm_parts(residual)
        second = normal * gain_ref[...] + shift_ref[...]
        second_ref[...] = second.astype(BF16)
        second_t_ref[...] = second.T.astype(BF16)
        total_ref[...] = jnp.zeros_like(total_ref)
        dsecond_ref[...] = jnp.zeros_like(dsecond_ref)

    upper = dot(second_ref[...], w_up_ref[...]) + up_shift_ref[...]
    factor = 0.7978845608028654
    square = upper * upper
    bent = jnp.tanh(factor * (upper + 0.044715 * (upper * square)))
    half = 0.5 * (1.0 + bent)
    active = (upper * half).astype(BF16)
    slope = half + 0.5 * upper * (1.0 - bent * bent) * (
        factor + (3.0 * 0.044715 * factor) * square
    )
    dy = dy_ref[...]
    total_ref[...] += dot(active, w_down_ref[...])
    g_down_ref[...] = dot_lt(active, dy).astype(g_down_ref.dtype)
    dupper = (dot_rt(dy, w_down_ref[...]) * slope).astype(BF16)
    g_up_bias_ref[...] = jnp.sum(dupper.astype(F32), axis=0, keepdims=True)
    g_up_ref[...] = dot(second_t_ref[...], dupper).astype(g_up_ref.dtype)
    dsecond_ref[...] += dot_rt(dupper, w_up_ref[...])

    @pl.when(step == pl.num_programs(0) - 1)
    def _():
        residual = residual_ref[...]
        hidden_ref[...] = (
            (residual + (total_ref[...] + down_shift_ref[...])).astype(BF16).reshape(x_ref.shape)
        )
        normal, inverse = norm_parts(residual)
        dsecond = dsecond_ref[...]
        grad_out = dy_ref[...].astype(F32)
        g_small_ref[0:1] = jnp.sum(dsecond * normal, axis=0, keepdims=True)
        g_small_ref[1:2] = jnp.sum(dsecond, axis=0, keepdims=True)
        g_small_ref[2:3] = jnp.sum(grad_out, axis=0, keepdims=True)
        dres = grad_out + norm_pull(dsecond, normal, inverse, gain_ref[...])
        dres_ref[...] = dres
        branch = dres.astype(BF16)
        g_small_ref[3:4] = jnp.sum(branch.astype(F32), axis=0, keepdims=True)
        g_out_ref[...] = dot_lt(mixed_ref[...], branch).astype(g_out_ref.dtype)
        dmixed = dot_rt(branch, w_out_ref[...])
        for pair in range(HEADS // 2):
            part = dmixed[:, pair * LANES : (pair + 1) * LANES]
            first, last = part[:rows], part[rows:]
            even = jnp.where(low, last, swap_halves(first))
            odd = jnp.where(low, swap_halves(last), first)
            send_ref[head_place(2 * pair)] = even.astype(BF16)
            send_ref[head_place(2 * pair + 1)] = odd.astype(BF16)


def middle(mixed_in, x, dy, w_out, out_shift, gain, shift, up_shift, down_shift, w_up, w_down, kind):
    micro, rows, _ = x.shape
    tokens = micro * rows
    groups = mixed_in.shape[0]

    def fixed(shape):
        return pl.BlockSpec(shape, lambda step: (0,) * len(shape))

    vector = fixed((1, D))
    steps = FF // CHUNK
    return pl.pallas_call(
        middle_kernel,
        grid=(steps,),
        out_shape=(
            jax.ShapeDtypeStruct(x.shape, BF16),
            jax.ShapeDtypeStruct((groups, rows, LANES), BF16),
            jax.ShapeDtypeStruct((tokens, D), F32),
            jax.ShapeDtypeStruct((D, D), kind),
            jax.ShapeDtypeStruct((D, FF), kind),
            jax.ShapeDtypeStruct((FF, D), kind),
            jax.ShapeDtypeStruct((1, FF), F32),
            jax.ShapeDtypeStruct((4, D), F32),
        ),
        in_specs=[
            fixed(mixed_in.shape),
            fixed(x.shape),
            fixed((tokens, D)),
            fixed((D, D)),
            vector,
            vector,
            vector,
            pl.BlockSpec((1, CHUNK), lambda step: (0, step)),
            vector,
            pl.BlockSpec((D, CHUNK), lambda step: (0, step)),
            pl.BlockSpec((CHUNK, D), lambda step: (step, 0)),
        ],
        out_specs=(
            fixed(x.shape),
            fixed((groups, rows, LANES)),
            fixed((tokens, D)),
            fixed((D, D)),
            pl.BlockSpec((D, CHUNK), lambda step: (0, step)),
            pl.BlockSpec((CHUNK, D), lambda step: (step, 0)),
            pl.BlockSpec((1, CHUNK), lambda step: (0, step)),
            fixed((4, D)),
        ),
        scratch_shapes=[
            VMEM((tokens, D), BF16),
            VMEM((tokens, D), F32),
            VMEM((tokens, D), BF16),
            VMEM((D, tokens), BF16),
            VMEM((tokens, D), F32),
            VMEM((tokens, D), F32),
        ],
        compiler_params=params_of(56),
        name="middle",
    )(mixed_in, x, dy, w_out, out_shift, gain, shift, up_shift, down_shift, w_up, w_down)


def qkv_back_kernel(
    recv_ref,
    normed_ref,
    x_ref,
    dres_ref,
    gain_ref,
    w_ref,
    grad_ref,
    g_qkv_ref,
    g_bias_ref,
    g_small_ref,
    packed_ref,
    normed_t_ref,
    dnormed_ref,
):
    micro, rows, _ = x_ref.shape
    step = pl.program_id(0)
    low = low_lanes(rows)

    @pl.when(step == 0)
    def _():
        for pair in range(HEADS // 2):
            even = recv_ref[head_place(2 * pair), 0].astype(F32)
            odd = recv_ref[head_place(2 * pair + 1), 0].astype(F32)
            spot, columns = pair // 2, slice((pair % 2) * LANES, (pair % 2 + 1) * LANES)
            packed_ref[spot, :rows, columns] = jnp.where(low, even, swap_halves(odd)).astype(BF16)
            packed_ref[spot, rows:, columns] = jnp.where(low, swap_halves(even), odd).astype(BF16)
        for head in range(HEADS):
            spot = D // CHUNK + head // 2
            columns = slice((head % 2) * LANES, (head % 2 + 1) * LANES)
            packed_ref[spot, :rows, columns] = recv_ref[head_place(head), 1]
            packed_ref[spot, rows:, columns] = swap_halves(
                recv_ref[head_place(head), 2].astype(F32)
            ).astype(BF16)
        normed_t_ref[...] = normed_ref[...].astype(F32).T.astype(BF16)
        dnormed_ref[...] = jnp.zeros_like(dnormed_ref)

    packed = packed_ref[step]
    g_bias_ref[...] = jnp.sum(packed.astype(F32), axis=0, keepdims=True)
    g_qkv_ref[...] = dot(normed_t_ref[...], packed).astype(g_qkv_ref.dtype)
    dnormed_ref[...] += dot_rt(packed, w_ref[...])

    @pl.when(step == pl.num_programs(0) - 1)
    def _():
        normal, inverse = norm_parts(x_ref[...].reshape(micro * rows, D).astype(F32))
        dnormed = dnormed_ref[...]
        g_small_ref[0:1] = jnp.sum(dnormed * normal, axis=0, keepdims=True)
        g_small_ref[1:2] = jnp.sum(dnormed, axis=0, keepdims=True)
        grad = dres_ref[...] + norm_pull(dnormed, normal, inverse, gain_ref[...])
        grad_ref[...] = grad.reshape(x_ref.shape)


def qkv_backward(recv, normed, x, dres, gain, w, kind):
    micro, rows, _ = x.shape
    tokens = micro * rows

    def fixed(shape):
        return pl.BlockSpec(shape, lambda step: (0,) * len(shape))

    steps = 3 * D // CHUNK
    return pl.pallas_call(
        qkv_back_kernel,
        grid=(steps,),
        out_shape=(
            jax.ShapeDtypeStruct(x.shape, F32),
            jax.ShapeDtypeStruct((D, 3 * D), kind),
            jax.ShapeDtypeStruct((1, 3 * D), F32),
            jax.ShapeDtypeStruct((2, D), F32),
        ),
        in_specs=[
            fixed(recv.shape),
            fixed((tokens, D)),
            fixed(x.shape),
            fixed((tokens, D)),
            fixed((1, D)),
            pl.BlockSpec((D, CHUNK), lambda step: (0, step)),
        ],
        out_specs=(
            fixed(x.shape),
            pl.BlockSpec((D, CHUNK), lambda step: (0, step)),
            pl.BlockSpec((1, CHUNK), lambda step: (0, step)),
            fixed((2, D)),
        ),
        scratch_shapes=[
            VMEM((steps, tokens, CHUNK), BF16),
            VMEM((D, tokens), BF16),
            VMEM((tokens, D), F32),
        ],
        compiler_params=params_of(56),
        name="qkv_backward",
    )(recv, normed, x, dres, gain, w)


AXES = ("gx", "gy")


def gather(array):
    return lax.all_gather(array, AXES, axis=0, tiled=True)


def scatter(array):
    return lax.psum_scatter(array, AXES, scatter_dimension=0, tiled=True)


def exchange(array):
    return lax.all_to_all(array, "gy", 0, 0, tiled=True)


def by_heads(w_qkv):
    rows = w_qkv.shape[0]
    sides = w_qkv[:, D:].reshape(rows, 2, HEADS, HEAD_DIM)
    return jnp.concatenate([w_qkv[:, :D], jnp.swapaxes(sides, 1, 2).reshape(rows, 2 * D)], axis=1)


def by_parts(w_qkv):
    rows = w_qkv.shape[0]
    sides = w_qkv[:, D:].reshape(rows, HEADS, 2, HEAD_DIM)
    return jnp.concatenate([w_qkv[:, :D], jnp.swapaxes(sides, 1, 2).reshape(rows, 2 * D)], axis=1)


def general_shards(
    hidden_in,
    rand_table,
    norm1_gain,
    norm1_bias,
    w_qkv,
    query_bias,
    value_bias,
    w_out,
    out_bias,
    norm2_gain,
    norm2_bias,
    w_up,
    up_bias,
    w_down,
    down_bias,
    cotangent,
):
    micro, rows, _ = hidden_in.shape
    groups = lax.axis_size("gy")
    local = rows // BLOCK
    own = norm1_gain.shape[0]

    vectors = jnp.concatenate(
        [
            norm1_gain,
            norm1_bias,
            query_bias,
            value_bias,
            out_bias,
            norm2_gain,
            norm2_bias,
            down_bias,
            up_bias,
        ]
    )
    table = lax.all_gather(rand_table, "gy", axis=1, tiled=True)
    table = table.reshape(micro, groups * local * RANDOM)
    vectors = gather(vectors[None]).astype(F32)
    gain_one, shift_one, query_shift, value_shift, out_shift, gain_two, shift_two, down_shift = (
        vectors[:, number * own : (number + 1) * own].reshape(1, D) for number in range(8)
    )
    up_shift = vectors[:, 8 * own :].reshape(1, FF)
    w_qkv_full = gather(by_heads(w_qkv))
    w_out_full, w_up_full, w_down_full = gather(w_out), gather(w_up), gather(w_down)
    packed_bias = by_heads(
        jnp.concatenate([query_shift, jnp.zeros_like(query_shift), value_shift], axis=1)
    )

    normed, send = qkv_forward(hidden_in, gain_one, shift_one, w_qkv_full, packed_bias, groups)
    qkv = exchange(send).reshape(groups, 3, local, BLOCK, LANES)
    mixed, lse = attention_forward(table, qkv)
    mixed_back = exchange(mixed.reshape(groups, rows, LANES))
    hidden_out, grad_send, dres, g_out, g_up, g_down, g_up_bias, g_mid = middle(
        mixed_back,
        hidden_in,
        cotangent.reshape(micro * rows, D),
        w_out_full,
        out_shift,
        gain_two,
        shift_two,
        up_shift,
        down_shift,
        w_up_full,
        w_down_full,
        F32,
    )
    grad_mixed = exchange(grad_send).reshape(groups, local, BLOCK, LANES)
    dqkv = attention_backward(table, qkv, grad_mixed, lse)
    dqkv_back = exchange(dqkv.reshape(groups, 3, rows, LANES))
    grad_hidden, g_qkv, g_packed, g_first = qkv_backward(
        dqkv_back, normed, hidden_in, dres, gain_one, w_qkv_full, F32
    )

    g_packed = by_parts(g_packed)
    small = [
        g_first[0],
        g_first[1],
        g_packed[0, :D],
        g_packed[0, 2 * D :],
        g_mid[3],
        g_mid[0],
        g_mid[1],
        g_mid[2],
    ]
    ranks = D // own
    small = jnp.concatenate(
        [item.reshape(ranks, own) for item in small] + [g_up_bias.reshape(ranks, 4 * own)], axis=1
    )
    small = scatter(small)[0]
    parts = [small[number * own : (number + 1) * own] for number in range(8)]
    return (
        hidden_out,
        grad_hidden,
        parts[0],
        parts[1],
        by_parts(scatter(g_qkv)),
        parts[2],
        parts[3],
        scatter(g_out),
        parts[4],
        parts[5],
        parts[6],
        scatter(g_up),
        small[8 * own :],
        scatter(g_down),
        parts[7],
    )


MESH = pl.DeviceIdType.MESH
ANY = pl.ANY
PLANES = 4
SPOTS = 4
PIECES = 2
RANKS = 2 * PLANES * SPOTS
TILES = 3 * D // LANES
HALF_TILES = TILES // 2
QUERY_ORDER = (0, 2, 3, 5, 6, 8, 9, 11, 1, 4, 7, 10)


def column_order():
    order = [("q", head) for head in QUERY_ORDER]
    for spot in range(SPOTS):
        for place in (2 * 3 * spot, 2 * 3 * spot + 2):
            order += [("k", place // 2), ("v", place // 2)]
        order += [("v", 3 * spot + 2), ("k", 3 * spot + 2)]
    return order


def natural_block(entry):
    return "qkv".index(entry[0]) * HEADS + entry[1]


def take_blocks(array, order):
    parts = []
    start = 0
    while start < len(order):
        stop = start + 1
        while stop < len(order) and order[stop] == order[stop - 1] + 1:
            stop += 1
        parts.append(array[..., order[start] * HEAD_DIM : (order[start] + stop - start) * HEAD_DIM])
        start = stop
    return jnp.concatenate(parts, axis=-1)


def flip(value, bits):
    if bits == 0:
        return value
    if bits == 1:
        return value + 1 - 2 * lax.rem(value, 2)
    if bits == 2:
        return value + 2 - 4 * lax.div(value, 2)
    return 3 - value


def place_here():
    core, rank = lax.axis_index("gx"), lax.axis_index("gy")
    return core, lax.div(rank, SPOTS), lax.rem(rank, SPOTS)


def rank_of(plane, spot):
    return plane * SPOTS + spot


def greet(partners):
    barrier = pltpu.get_barrier_semaphore()
    for partner in partners:
        pl.semaphore_signal(barrier, inc=1, device_id=partner, device_id_type=MESH)
    pl.semaphore_wait(barrier, len(partners))


def remote(source, target, send_sem, recv_sem, device):
    return pltpu.make_async_remote_copy(
        src_ref=source,
        dst_ref=target,
        send_sem=send_sem,
        recv_sem=recv_sem,
        device_id=device,
        device_id_type=MESH,
    )


def column_partners(core, plane, spot):
    partners = [(1 - core, rank_of(plane, spot))]
    for bits in range(1, PLANES):
        for other in (core, 1 - core):
            partners.append((other, rank_of(flip(plane, bits), spot)))
    return partners


def all_partners(core, plane, spot):
    return column_partners(core, plane, spot) + [
        (core, rank_of(plane, flip(spot, 1))),
        (core, rank_of(plane, flip(spot, 2))),
    ]


def to_planes(source, target, send_sem, recv_sem, local_sem):
    core, plane, spot = place_here()
    half, odd = lax.div(plane, 2), lax.rem(plane, 2)
    sends, keeps = [], []
    for micro in range(2):
        goal = 2 * micro + core
        here = (goal == plane) & (half == core)
        send = remote(
            source.at[micro],
            target.at[odd],
            send_sem.at[micro],
            recv_sem.at[odd],
            (half, rank_of(goal, spot)),
        )
        keep = pltpu.make_async_copy(source.at[micro], target.at[odd], local_sem.at[micro])

        @pl.when(jnp.logical_not(here))
        def _(send=send):
            send.start()

        @pl.when(here)
        def _(keep=keep):
            keep.start()

        sends.append((here, send))
        keeps.append((here, keep))

    def finish():
        for piece in range(PIECES):
            mine = (odd == core) & (plane == 2 * core + piece)
            arrival = remote(
                source.at[0],
                target.at[piece],
                send_sem.at[0],
                recv_sem.at[piece],
                (core, rank_of(plane, spot)),
            )

            @pl.when(jnp.logical_not(mine))
            def _(arrival=arrival):
                arrival.wait_recv()

        for (here, send), (_, keep) in zip(sends, keeps):

            @pl.when(jnp.logical_not(here))
            def _(send=send):
                send.wait_send()

            @pl.when(here)
            def _(keep=keep):
                keep.wait()

    return finish


def from_planes(source, target, send_sem, recv_sem, local_sem):
    core, plane, spot = place_here()
    micro, odd = lax.div(plane, 2), lax.rem(plane, 2)
    sends, keeps = [], []
    for piece in range(PIECES):
        goal = 2 * core + piece
        here = (goal == plane) & (odd == core)
        send = remote(
            source.at[piece],
            target.at[micro],
            send_sem.at[piece],
            recv_sem.at[micro],
            (odd, rank_of(goal, spot)),
        )
        keep = pltpu.make_async_copy(source.at[piece], target.at[micro], local_sem.at[piece])

        @pl.when(jnp.logical_not(here))
        def _(send=send):
            send.start()

        @pl.when(here)
        def _(keep=keep):
            keep.start()

        sends.append((here, send))
        keeps.append((here, keep))

    def finish():
        for number in range(2):
            mine = (2 * number + core == plane) & (micro == core)
            arrival = remote(
                source.at[0],
                target.at[number],
                send_sem.at[0],
                recv_sem.at[number],
                (core, rank_of(plane, spot)),
            )

            @pl.when(jnp.logical_not(mine))
            def _(arrival=arrival):
                arrival.wait_recv()

        for (here, send), (_, keep) in zip(sends, keeps):

            @pl.when(jnp.logical_not(here))
            def _(send=send):
                send.wait_send()

            @pl.when(here)
            def _(keep=keep):
                keep.wait()

    return finish


class Gather:
    SENDS = 31

    def __init__(self, source, target, send_sem, recv_sem, local_sem):
        self.source, self.target = source, target
        self.send_sem, self.recv_sem = send_sem, recv_sem
        self.core, self.plane, self.spot = place_here()
        self.sends = []
        self.own = pltpu.make_async_copy(
            source, target.at[self.core, self.plane, self.spot], local_sem
        )
        self.own.start()

    def send(self, source, plane, spot, device):
        copy = remote(
            source,
            self.target.at[self.core, plane, spot],
            self.send_sem.at[len(self.sends)],
            self.recv_sem.at[self.core, plane, spot],
            device,
        )
        copy.start()
        self.sends.append(copy)

    def arrive(self, core, plane, spot):
        shard = self.target.at[core, plane, spot]
        remote(
            shard,
            shard,
            self.send_sem.at[0],
            self.recv_sem.at[core, plane, spot],
            (self.core, rank_of(self.plane, self.spot)),
        ).wait_recv()

    def neighbour(self, bits):
        return (self.core, rank_of(self.plane, flip(self.spot, bits)))

    def sibling(self):
        return (1 - self.core, rank_of(self.plane, self.spot))

    def start(self):
        for bits in range(1, PLANES):
            goal = (self.core, rank_of(flip(self.plane, bits), self.spot))
            self.send(self.source, self.plane, self.spot, goal)
        for goal in (self.neighbour(1), self.neighbour(2), self.sibling()):
            self.send(self.source, self.plane, self.spot, goal)

    def column(self):
        for bits in range(1, PLANES):
            plane = flip(self.plane, bits)
            self.arrive(self.core, plane, self.spot)
            shard = self.target.at[self.core, plane, self.spot]
            for goal in (self.neighbour(1), self.neighbour(2), self.sibling()):
                self.send(shard, plane, self.spot, goal)

    def across(self):
        for bits in range(PLANES):
            plane = flip(self.plane, bits)
            for side in (1, 2):
                spot = flip(self.spot, side)
                self.arrive(self.core, plane, spot)
                shard = self.target.at[self.core, plane, spot]
                if (side == 1) == (bits < 2):
                    self.send(shard, plane, spot, self.neighbour(3 - side))
                self.send(shard, plane, spot, self.sibling())

    def corner(self):
        spot = flip(self.spot, 3)
        for bits in range(PLANES):
            plane = flip(self.plane, bits)
            self.arrive(self.core, plane, spot)
            self.send(self.target.at[self.core, plane, spot], plane, spot, self.sibling())

    def finish(self):
        for bits in range(PLANES):
            for side in range(SPOTS):
                self.arrive(1 - self.core, flip(self.plane, bits), flip(self.spot, side))
        self.own.wait()
        for copy in self.sends:
            copy.wait_send()


def settle(shards_ref, plan):
    rows = shards_ref.shape[3] // 2

    def pair(number, carry):
        core, plane, side = (
            lax.div(number, 2 * PLANES),
            lax.rem(lax.div(number, 2), PLANES),
            lax.rem(number, 2),
        )
        goal = pl.ds(pl.multiple_of(number * 2 * rows, 16), 2 * rows)
        for tile, out_ref, (left, right) in plan:
            columns = slice(tile * LANES, (tile + 1) * LANES)
            first = shards_ref[core, plane, 2 * side, :, columns].astype(F32)
            second = shards_ref[core, plane, 2 * side + 1, :, columns].astype(F32)
            out_ref[goal, left * LANES : (left + 1) * LANES] = jnp.concatenate(
                [first[:rows], second[:rows]], axis=0
            ).astype(BF16)
            out_ref[goal, right * LANES : (right + 1) * LANES] = jnp.concatenate(
                [first[rows:], second[rows:]], axis=0
            ).astype(BF16)
        return carry

    lax.fori_loop(0, RANKS // 2, pair, 0)


def alternate(tile):
    return 2 * tile, 2 * tile + 1


def plane_partners(core, plane, spot):
    partners = []
    for other in (core, 1 - core):
        for side in range(SPOTS):
            if other is core and side == 0:
                continue
            partners.append((other, rank_of(plane, flip(spot, side))))
    return partners


def both_partners(core, plane, spot):
    return plane_partners(core, plane, spot) + column_partners(core, plane, spot)[1:]


def exchange_sems(recv_shape):
    return [
        pltpu.SemaphoreType.DMA((14,)),
        pltpu.SemaphoreType.DMA(recv_shape),
        pltpu.SemaphoreType.DMA((PIECES,)),
    ]


def sort_entries(table, sorted_ref, entries):
    count = table.shape[1]
    core = lax.axis_index("gx")
    lane = lax.broadcasted_iota(jnp.int32, (count, count), 1)
    row = lax.broadcasted_iota(jnp.int32, (count, count), 0).astype(F32)
    everything = jnp.broadcast_to(table, (count, count))
    half = entries // 2
    inside = (lane >= core * half) & (lane < (core + 1) * half)
    lane = lane.astype(F32)
    for number, along in enumerate((everything, jnp.where(inside, everything, 2.0 * LANES))):
        down = along.T
        before = (along < down) | ((along == down) & (lane < row))
        rank = jnp.sum(jnp.where(before, 1.0, 0.0), axis=1, keepdims=True)
        order = jnp.sum(jnp.where(rank == lane, row, 0.0), axis=0, keepdims=True)
        upto = jnp.sum(jnp.where(down <= lane, 1.0, 0.0), axis=0, keepdims=True)
        sorted_ref[2 * number : 2 * number + 1] = order.astype(jnp.int32)
        sorted_ref[2 * number + 1 : 2 * number + 2] = upto.astype(jnp.int32)


class Outward:
    def __init__(self, source, target, send_sem, recv_sem, local_sem):
        self.target, self.recv_sem, self.send_sem = target, recv_sem, send_sem
        self.core, self.plane, self.spot = place_here()
        self.sends, self.keeps = [], []
        for side in (3, 1, 2, 0):
            for other in (self.core, 1 - self.core):
                goal = flip(self.spot, side)
                for piece in range(PIECES):
                    start = source.at[other, goal, piece]
                    stop = target.at[2 * self.core + piece, self.spot]
                    if side == 0 and other is self.core:
                        copy = pltpu.make_async_copy(start, stop, local_sem.at[piece])
                        self.keeps.append(copy)
                    else:
                        copy = remote(
                            start,
                            stop,
                            send_sem.at[len(self.sends)],
                            recv_sem.at[2 * self.core + piece, self.spot],
                            (other, rank_of(self.plane, goal)),
                        )
                        self.sends.append(copy)
                    copy.start()

    def arrive(self, side):
        for other in (self.core, 1 - self.core):
            if side == 0 and other is self.core:
                for copy in self.keeps:
                    copy.wait()
                continue
            for piece in range(PIECES):
                place = (2 * other + piece, flip(self.spot, side))
                remote(
                    self.target.at[place],
                    self.target.at[place],
                    self.send_sem.at[0],
                    self.recv_sem.at[place],
                    (self.core, rank_of(self.plane, self.spot)),
                ).wait_recv()

    def finish(self):
        for copy in self.sends:
            copy.wait_send()


def inward_targets(core, spot):
    for side in (3, 1, 2, 0):
        for other in (core, 1 - core):
            yield side, other, flip(spot, side), side == 0 and other is core


class Inward:
    def __init__(self, source, target, send_sem, recv_sem, local_sem):
        self.source, self.target = source, target
        self.send_sem, self.recv_sem, self.local_sem = send_sem, recv_sem, local_sem
        self.core, self.plane, self.spot = place_here()
        self.sends, self.keeps = [], []

    def send(self, other, goal, stays, piece, part, parts):
        source = self.source.at[2 * other + piece, goal, parts]
        target = self.target.at[self.core, self.spot, piece, parts]
        if stays:
            copy = pltpu.make_async_copy(source, target, self.local_sem.at[part, piece])
            self.keeps.append(copy)
        else:
            copy = remote(
                source,
                target,
                self.send_sem.at[len(self.sends)],
                self.recv_sem.at[self.core, self.spot, piece, part],
                (other, rank_of(self.plane, goal)),
            )
            self.sends.append(copy)
        copy.start()

    def finish(self, parts_of):
        for side, other, goal, stays in inward_targets(self.core, self.spot):
            if stays:
                continue
            for piece in range(PIECES):
                for part, parts in enumerate(parts_of[0 if other is self.core else 1]):
                    target = self.target.at[other, goal, piece, parts]
                    remote(
                        target,
                        target,
                        self.send_sem.at[0],
                        self.recv_sem.at[other, goal, piece, part],
                        (self.core, rank_of(self.plane, self.spot)),
                    ).wait_recv()
        for copy in self.sends:
            copy.wait_send()
        for copy in self.keeps:
            copy.wait()


KEYS_A, QUERIES, KEYS_B = range(3)


def plane_attend_back_kernel(count, *refs):
    table_ref, sorted_ref, qk_ref, shared_ref, grad_source_ref, lse_ref, hidden_ref = refs[:7]
    sources, refs = refs[7 : 7 + count], refs[7 + count :]
    back_ref, hidden_out_ref = refs[:2]
    outs, refs = refs[2 : 2 + count], refs[2 + count :]
    buffers, refs = refs[: 7 * count], refs[7 * count :]
    grad_ref, out_ref, sums_ref, shares_ref, walked_ref, sibling_ref = refs[:6]
    scores_refs, refs = refs[6:10], refs[10:]
    reduce_send, reduce_recv, reduce_local = refs[:3]
    grad_sems, back_sems, move_sems, sibling_sems = refs[3:6], refs[6:9], refs[9:12], refs[12:14]

    local = qk_ref.shape[3]
    groups = PLANES * SPOTS
    blocks = groups * local
    core, plane, spot = place_here()
    low = low_lanes(BLOCK)
    masks = [half_mask(True), half_mask(False)]

    greet(both_partners(core, plane, spot))
    grads = Outward(grad_source_ref, grad_ref, *grad_sems)
    reduces = [
        Reduce(
            source,
            *buffers[7 * number : 7 * number + 7],
            out,
            (reduce_send.at[number], reduce_recv.at[number], reduce_local.at[number]),
        )
        for number, (source, out) in enumerate(zip(sources, outs))
    ]
    for one in reduces:
        one.start()
    finish_hidden = from_planes(hidden_ref, hidden_out_ref, *move_sems)

    def load(component, block):
        rank, number = lax.div(block, local), lax.rem(block, local)
        if component == 2:
            return shared_ref[lax.div(rank, SPOTS), lax.rem(rank, SPOTS), number]
        return qk_ref[lax.div(rank, SPOTS), lax.rem(rank, SPOTS), component, number]

    def load_grad(block):
        rank = lax.div(block, local)
        return grad_ref[lax.div(rank, SPOTS), lax.rem(rank, SPOTS), lax.rem(block, local)]

    def store(component, block, value):
        rank = lax.div(block, local)
        out_ref[
            lax.div(rank, SPOTS), lax.rem(rank, SPOTS), component, lax.rem(block, local)
        ] = value.astype(BF16)

    def stored(component, block):
        rank = lax.div(block, local)
        return out_ref[
            lax.div(rank, SPOTS), lax.rem(rank, SPOTS), component, lax.rem(block, local)
        ].astype(F32)

    nothing = jnp.zeros((BLOCK, LANES), F32)

    def clear(block, carry):
        for slot in range(2):
            sums_ref[slot, block] = nothing
        return carry

    lax.fori_loop(0, blocks, clear, 0)

    def picked(block, number):
        return table_ref[0, block * RANDOM + number]

    def one_block(block, slot):
        ids, bias = inner_slots(picked, block, blocks)
        keys = jnp.concatenate([load(1 + slot, number) for number in ids], axis=0)
        both = jnp.concatenate(
            [load(0, block) * masks[slot], load_grad(block) * masks[1 - slot]], axis=0
        )
        products = dot_rt(both, keys)
        logs = lse_ref[block][:, slot * HEAD_DIM : slot * HEAD_DIM + 1]
        weights = jnp.exp(products[:BLOCK] + bias - logs)
        grad_weights = products[BLOCK:]
        delta = jnp.sum(weights * grad_weights, axis=1, keepdims=True)
        grad_scores = weights * (grad_weights - delta)
        stacked = jnp.concatenate([grad_scores, weights], axis=0).astype(BF16)
        return dot(stacked[:BLOCK], keys), dot_lt(stacked, both)

    fixed = 5

    def rank_blocks(rank, slot):
        first = rank * local
        results = [one_block(first + number, slot) for number in range(local)]

        def share(number, place):
            return results[number][1][place * BLOCK : (place + 1) * BLOCK]

        for shift in range(-1, local + 1):
            parts = [
                share(number, shift - number + 1)
                for number in range(local)
                if 0 <= shift - number + 1 <= 2
            ]
            target = jnp.minimum(jnp.maximum(first + shift, 0), blocks - 1)
            sums_ref[slot, target] += functools.reduce(jnp.add, parts)
        for place, target in ((3, 0), (4, blocks - 1)):
            sums_ref[slot, target] += functools.reduce(
                jnp.add, [share(number, place) for number in range(local)]
            )
        for number in range(local):
            for pick in range(RANDOM):
                shares_ref[slot, (first + number) * RANDOM + pick] = share(number, fixed + pick)
        return [result[0] for result in results]

    def head_a(side):
        def body(number, carry):
            rank = number * SPOTS + flip(spot, side)
            for place, query in enumerate(rank_blocks(rank, 0)):
                store(QUERIES, rank * local + place, query * SCALE)
            return carry

        lax.fori_loop(0, PLANES, body, 0)

    def head_b(number, carry):
        rank = core * (groups // 2) + number
        for place, query in enumerate(rank_blocks(rank, 1)):
            block = rank * local + place
            store(QUERIES, block, jnp.where(low, stored(QUERIES, block), query * SCALE))
        return carry

    spans = blocks // SPAN
    ends = (0, blocks - 1)

    def dense(slot, p_ref, d_ref, numbers):
        both = jnp.concatenate(
            [load(0, number) * masks[slot] for number in numbers]
            + [load_grad(number) * masks[1 - slot] for number in numbers],
            axis=0,
        )
        rows = len(numbers) * BLOCK
        column = slot * HEAD_DIM
        logs = jnp.concatenate(
            [lse_ref[number][:, column : column + 1] for number in numbers], axis=0
        )

        def keys_at(span):
            return jnp.concatenate(
                [load(1 + slot, span * SPAN + number) for number in range(SPAN)], axis=0
            )

        def first_pass(span, delta):
            products = dot_rt(both, keys_at(span))
            weights = jnp.exp(products[:rows] - logs)
            grad_weights = products[rows:]
            p_ref[span] = weights
            d_ref[span] = grad_weights
            return delta + jnp.sum(weights * grad_weights, axis=1, keepdims=True)

        delta = lax.fori_loop(0, spans, first_pass, jnp.zeros((rows, 1), F32), unroll=2)

        def second_pass(span, total):
            weights = p_ref[span]
            grad_scores = weights * (d_ref[span] - delta)
            stacked = jnp.concatenate([grad_scores, weights], axis=0).astype(BF16)
            shares = dot_lt(stacked, both)
            for number in range(SPAN):
                sums_ref[slot, span * SPAN + number] += shares[
                    number * BLOCK : (number + 1) * BLOCK
                ]
            return total + dot(stacked[:rows], keys_at(span))

        total = lax.fori_loop(0, spans, second_pass, jnp.zeros((rows, LANES), F32), unroll=2)
        for place, number in enumerate(numbers):
            query = total[place * BLOCK : (place + 1) * BLOCK] * SCALE
            if slot == 1:
                query = jnp.where(low, stored(QUERIES, number), query)
            store(QUERIES, number, query)

    def walk(slot, length):
        def body(number, total):
            entry = sorted_ref[2 * slot, number]
            earlier = sorted_ref[2 * slot, jnp.maximum(number - 1, 0)]
            keep = jnp.where(table_ref[0, entry] == table_ref[0, earlier], 1.0, 0.0).astype(F32)
            total = total * keep + shares_ref[slot, entry]
            walked_ref[slot, number] = total.astype(BF16)
            return total

        lax.fori_loop(0, length, body, nothing, unroll=4)

    def close(slot, rank, component):
        def body(number, carry):
            block = rank * local + number
            stop = sorted_ref[2 * slot + 1, block]
            start = jnp.where(block == 0, 0, sorted_ref[2 * slot + 1, jnp.maximum(block - 1, 0)])
            some = jnp.where(stop > start, 1.0, 0.0).astype(F32)
            share = walked_ref[slot, jnp.maximum(stop - 1, 0)].astype(F32)
            store(component, block, sums_ref[slot, block] + share * some)
            return carry

        lax.fori_loop(0, local, body, 0, unroll=True)

    back = Inward(out_ref, back_ref, *back_sems)
    own_parts = (slice(0, 1), slice(1, 2), slice(2, 3))
    far_parts = (slice(0, 2),)

    for side in range(SPOTS):
        grads.arrive(side)
        head_a(side)
        if side == 1:
            for one in reduces:
                one.corners()
    dense(0, scores_refs[0], scores_refs[1], ends)
    for one in reduces:
        one.sides()
    walk(0, blocks * RANDOM)
    for side, other, goal, stays in inward_targets(core, spot):
        for piece in range(PIECES):
            close(0, (2 * other + piece) * SPOTS + goal, KEYS_A)
            if other is core:
                back.send(other, goal, stays, piece, 0, own_parts[0])
            else:
                back.send(other, goal, stays, piece, 0, far_parts[0])
    lax.fori_loop(0, groups // 2, head_b, 0)
    dense(1, scores_refs[2], scores_refs[3], (core * (blocks - 1),))
    for side, other, goal, stays in inward_targets(core, spot):
        if other is core:
            for piece in range(PIECES):
                back.send(other, goal, stays, piece, 1, own_parts[1])
    walk(1, blocks * RANDOM // 2)
    for number in range(PIECES):
        for goal in range(SPOTS):
            close(1, (2 * (1 - core) + number) * SPOTS + goal, KEYS_B)
    across = remote(
        out_ref.at[pl.ds(2 * (1 - core), PIECES), :, KEYS_B],
        sibling_ref,
        sibling_sems[0],
        sibling_sems[1],
        (1 - core, rank_of(plane, spot)),
    )
    across.start()
    for number in range(PIECES):
        for goal in range(SPOTS):
            close(1, (2 * core + number) * SPOTS + goal, KEYS_B)
    for one in reduces:
        one.columns()
    across.wait_recv()
    for side, other, goal, stays in inward_targets(core, spot):
        if other is core:
            for piece in range(PIECES):
                place = (2 * core + piece, goal, KEYS_B)
                out_ref[place] = (
                    out_ref[place].astype(F32) + sibling_ref[piece, goal].astype(F32)
                ).astype(BF16)
                back.send(other, goal, stays, piece, 2, own_parts[2])
    for one in reduces:
        one.finish()
    finish_hidden()
    grads.finish()
    across.wait_send()
    back.finish((own_parts, far_parts))


def plane_attention_back(table, sorted_table, qk, shared, grad_source, lse, hidden, sources):
    local = qk.shape[3]
    blocks = PLANES * SPOTS * local
    spans = blocks // SPAN
    count = len(sources)
    buffers = []
    for source in sources:
        buffers += reduce_scratch(source.shape, source.dtype)
    tile = (local, BLOCK, LANES)
    wide = VMEM((spans, 2 * BLOCK, SPAN * BLOCK), F32)
    thin = VMEM((spans, BLOCK, SPAN * BLOCK), F32)
    dma = pltpu.SemaphoreType.DMA
    return pl.pallas_call(
        functools.partial(plane_attend_back_kernel, count),
        out_shape=(
            jax.ShapeDtypeStruct((2, SPOTS, PIECES, 3) + tile, BF16),
            jax.ShapeDtypeStruct(hidden.shape, BF16),
        )
        + tuple(jax.ShapeDtypeStruct(source.shape[3:], F32) for source in sources),
        in_specs=[
            whole(pltpu.SMEM),
            whole(pltpu.SMEM),
            whole(),
            whole(),
            whole(ANY),
            whole(),
            whole(ANY),
        ]
        + [whole(ANY)] * count,
        out_specs=(whole(ANY), whole(ANY)) + (whole(),) * count,
        scratch_shapes=buffers
        + [
            VMEM((PLANES, SPOTS) + tile, BF16),
            VMEM((PLANES, SPOTS, 3) + tile, BF16),
            VMEM((2, blocks, BLOCK, LANES), F32),
            VMEM((2, blocks * RANDOM, BLOCK, LANES), F32),
            VMEM((2, blocks * RANDOM, BLOCK, LANES), BF16),
            VMEM((PIECES, SPOTS) + tile, BF16),
            wide,
            wide,
            thin,
            thin,
            dma((count, REDUCE_SEMS)),
            dma((count, REDUCE_SEMS)),
            dma((count, 4)),
        ]
        + exchange_sems((PLANES, SPOTS))
        + [
            dma((36,)),
            dma((2, SPOTS, PIECES, 3)),
            dma((3, PIECES)),
            dma((2,)),
            dma((2,)),
            dma((2,)),
            dma,
            dma,
        ],
        compiler_params=pltpu.CompilerParams(
            vmem_limit_bytes=62 * 1024 * 1024, collective_id=5, has_side_effects=True
        ),
        name="plane_attention_back",
    )(table, sorted_table, qk, shared, grad_source, lse, hidden, *sources)


class PlaneGather:
    SENDS = 3 + 3 + 4 + 2

    def __init__(self, source, target, send_sem, column_sem, recv_sem, local_sem):
        self.source, self.target = source, target
        self.send_sem, self.column_sem, self.recv_sem = send_sem, column_sem, recv_sem
        self.core, self.plane, self.spot = place_here()
        self.sends = []
        self.own = pltpu.make_async_copy(
            source, target.at[self.core, self.plane, self.spot], local_sem
        )
        self.own.start()
        for bits in range(1, PLANES):
            copy = remote(
                source,
                target.at[self.core, self.plane, self.spot],
                send_sem.at[len(self.sends)],
                column_sem.at[self.plane],
                (self.core, rank_of(flip(self.plane, bits), self.spot)),
            )
            copy.start()
            self.sends.append(copy)

    def neighbour(self, bits):
        return (self.core, rank_of(self.plane, flip(self.spot, bits)))

    def sibling(self):
        return (1 - self.core, rank_of(self.plane, self.spot))

    def piece(self, core, planes, spot):
        return self.target.at[core, planes, spot]

    def send(self, planes, spot, part, goal):
        piece = self.piece(self.core, planes, spot)
        copy = remote(
            piece,
            piece,
            self.send_sem.at[len(self.sends)],
            self.recv_sem.at[self.core, spot, part],
            goal,
        )
        copy.start()
        self.sends.append(copy)

    def arrive(self, core, planes, spot, part):
        piece = self.piece(core, planes, spot)
        remote(
            piece,
            piece,
            self.send_sem.at[0],
            self.recv_sem.at[core, spot, part],
            (self.core, rank_of(self.plane, self.spot)),
        ).wait_recv()

    def columns(self):
        self.own.wait()
        for bits in range(1, PLANES):
            other = flip(self.plane, bits)
            shard = self.target.at[self.core, other, self.spot]
            remote(
                shard,
                shard,
                self.send_sem.at[0],
                self.column_sem.at[other],
                (self.core, rank_of(self.plane, self.spot)),
            ).wait_recv()
        for goal in (self.neighbour(1), self.neighbour(2), self.sibling()):
            self.send(slice(0, PLANES), self.spot, 0, goal)

    def forward(self):
        everything = slice(0, PLANES)
        for side in (1, 2):
            spot = flip(self.spot, side)
            self.arrive(self.core, everything, spot, 0)
            half = slice(0, 2) if side == 1 else slice(2, 4)
            self.send(half, spot, side - 1, self.neighbour(3 - side))
            self.send(everything, spot, 0, self.sibling())

    def corner(self):
        spot = flip(self.spot, 3)
        for part, half in enumerate((slice(0, 2), slice(2, 4))):
            self.arrive(self.core, half, spot, part)
            self.send(half, spot, part, self.sibling())

    def finish(self):
        for side in range(3):
            self.arrive(1 - self.core, slice(0, PLANES), flip(self.spot, side), 0)
        for part, half in enumerate((slice(0, 2), slice(2, 4))):
            self.arrive(1 - self.core, half, flip(self.spot, 3), part)
        for copy in self.sends:
            copy.wait_send()


class CrossGather:
    SENDS = 2 + 1 + 3 + 3 * 4

    def __init__(self, source, target, send_sem, spot_sem, recv_sem, local_sem):
        self.target = target
        self.send_sem, self.spot_sem, self.recv_sem = send_sem, spot_sem, recv_sem
        self.core, self.plane, self.spot = place_here()
        self.sends = []
        self.own = pltpu.make_async_copy(
            source, target.at[self.core, self.plane, self.spot], local_sem
        )
        self.own.start()
        for side in (1, 2):
            self.pass_on(source, self.spot, flip(self.spot, side))

    def push(self, source, target, recv_sem, device):
        copy = remote(source, target, self.send_sem.at[len(self.sends)], recv_sem, device)
        copy.start()
        self.sends.append(copy)

    def pass_on(self, source, spot, goal):
        self.push(
            source,
            self.target.at[self.core, self.plane, spot],
            self.spot_sem.at[spot],
            (self.core, rank_of(self.plane, goal)),
        )

    def await_spot(self, spot):
        shard = self.target.at[self.core, self.plane, spot]
        remote(
            shard,
            shard,
            self.send_sem.at[0],
            self.spot_sem.at[spot],
            (self.core, rank_of(self.plane, self.spot)),
        ).wait_recv()

    def across(self):
        beside, beyond = flip(self.spot, 1), flip(self.spot, 2)
        for side in (1, 2):
            self.await_spot(flip(self.spot, side))
        spot = beside * (1 - self.core) + beyond * self.core
        goal = beyond * (1 - self.core) + beside * self.core
        self.pass_on(self.target.at[self.core, self.plane, spot], spot, goal)

    def blocks(self):
        self.own.wait()
        self.await_spot(flip(self.spot, 3))
        self.maybe = []
        self.along(self.plane, 1, self.plane < PLANES - 1)
        self.along(self.plane, -1, self.plane > 0)
        self.to_sibling(self.plane, self.plane >= 0)

    def along(self, plane, step, wanted):
        block = self.target.at[self.core, plane]
        copy = remote(
            block,
            block,
            self.send_sem.at[3 + len(self.maybe)],
            self.recv_sem.at[self.core, plane],
            (self.core, rank_of(self.plane + step, self.spot)),
        )
        self.begin(copy, wanted)

    def to_sibling(self, plane, wanted):
        block = self.target.at[self.core, plane]
        copy = remote(
            block,
            block,
            self.send_sem.at[3 + len(self.maybe)],
            self.recv_sem.at[self.core, plane],
            (1 - self.core, rank_of(self.plane, self.spot)),
        )
        self.begin(copy, wanted)

    def begin(self, copy, wanted):
        self.maybe.append((copy, wanted))

        @pl.when(wanted)
        def _():
            copy.start()

    def arrive(self, core, plane):
        block = self.target.at[core, plane]
        remote(
            block,
            block,
            self.send_sem.at[0],
            self.recv_sem.at[core, plane],
            (self.core, rank_of(self.plane, self.spot)),
        ).wait_recv()

    def hop(self, distance):
        for step in (1, -1):
            origin = self.plane - step * distance
            here = (origin >= 0) & (origin < PLANES)
            onward = self.plane + step
            more = here & (onward >= 0) & (onward < PLANES)

            @pl.when(here)
            def _(origin=origin):
                self.arrive(self.core, origin)

            self.along(origin, step, more)
            self.to_sibling(origin, here)

    def finish(self):
        for bits in range(PLANES):
            self.arrive(1 - self.core, flip(self.plane, bits))
        for copy in self.sends:
            copy.wait_send()
        for copy, wanted in self.maybe:

            @pl.when(wanted)
            def _(copy=copy):
                copy.wait_send()


def pair_of_blocks(read, first, second):
    low = low_lanes(1)
    tiles = []
    for block, wanted in ((first, 0), (second, 1)):
        tile = read(block // 2)
        tiles.append(tile if block % 2 == wanted else swap_halves(tile))
    return jnp.where(low, tiles[0], tiles[1])


def fold_tiles(target_ref, start, tiles, read):
    half = len(tiles) // 2
    for number in range(half):
        columns = slice((start + number) * LANES, (start + number + 1) * LANES)
        target_ref[:, columns] = jnp.concatenate(
            [read(tiles[number]), read(tiles[half + number])], axis=0
        ).astype(BF16)


VECTORS = 8


def lay_vectors(vecs_ref, vectors_ref, up_ref):
    rows = vecs_ref.shape[3]
    own, wide = D // RANKS, FF // RANKS
    values = vecs_ref[...].reshape(RANKS, rows, LANES).astype(F32)

    def spread_out(count, width):
        place = lax.broadcasted_iota(jnp.int32, (LANES, count), 1)
        lane = lax.broadcasted_iota(jnp.int32, (LANES, count), 0)
        start = lax.div(place, width) * width
        return jnp.where(place - start == lane, 1.0, 0.0).astype(BF16)

    laid = dot(vecs_ref[...].reshape(RANKS * rows, LANES), spread_out(D, own))
    owner = lax.broadcasted_iota(jnp.int32, (RANKS, 1, D), 0)
    column = lax.broadcasted_iota(jnp.int32, (RANKS, 1, D), 2)
    laid = jnp.where(lax.div(column, own) == owner, laid.reshape(RANKS, rows, D), 0.0)
    vectors_ref[...] = jnp.sum(laid, axis=0)[:VECTORS]
    row = lax.broadcasted_iota(jnp.int32, (1, rows, LANES), 1)
    last = jnp.sum(jnp.where(row == VECTORS, values, 0.0), axis=1)
    laid = dot(last.astype(BF16), spread_out(FF, wide))
    owner = lax.broadcasted_iota(jnp.int32, (RANKS, FF), 0)
    column = lax.broadcasted_iota(jnp.int32, (RANKS, FF), 1)
    laid = jnp.sum(jnp.where(lax.div(column, wide) == owner, laid, 0.0), axis=0, keepdims=True)
    for chunk in range(FF // CHUNK):
        for side in range(2):
            start = side * (FF // 2) + chunk * LANES
            up_ref[chunk, :, side * LANES : (side + 1) * LANES] = laid[:, start : start + LANES]


def lay_table(tables_ref, core, micro, entries):
    count = 2 * LANES
    ranks = PLANES * SPOTS
    values = tables_ref[core].reshape(ranks, tables_ref.shape[3], LANES).astype(F32)
    row = lax.broadcasted_iota(jnp.int32, (1, tables_ref.shape[3], LANES), 1)
    values = jnp.sum(jnp.where(row == micro, values, 0.0), axis=1)
    place = lax.broadcasted_iota(jnp.int32, (LANES, count), 1)
    lane = lax.broadcasted_iota(jnp.int32, (LANES, count), 0)
    start = lax.div(place, entries) * entries
    laid = dot(values.astype(BF16), jnp.where(place - start == lane, 1.0, 0.0).astype(BF16))
    owner = lax.broadcasted_iota(jnp.int32, (ranks, count), 0)
    column = lax.broadcasted_iota(jnp.int32, (ranks, count), 1)
    laid = jnp.sum(jnp.where(lax.div(column, entries) == owner, laid, 0.0), axis=0, keepdims=True)
    column = lax.broadcasted_iota(jnp.int32, (1, count), 1)
    return jnp.where(column < ranks * entries, laid, 2.0 * LANES)


def front_kernel(
    x_in_ref,
    dy_ref,
    vec_ref,
    tab_ref,
    w_qkv_in_ref,
    w_out_in_ref,
    w_up_in_ref,
    w_down_in_ref,
    back_ref,
    x_ref,
    dys_ref,
    w_down_ref,
    w_qkv_hbm,
    w_out_hbm,
    w_up_hbm,
    qk_hbm,
    shared_hbm,
    normed_ref,
    lse_ref,
    vectors_ref,
    up_ref,
    table_ref,
    sorted_ref,
    s_qkv_ref,
    s_ou_ref,
    g_qkv_ref,
    g_ou_ref,
    w_qkv_ref,
    w_out_ref,
    w_up_ref,
    xs_ref,
    vecs_ref,
    tabs_ref,
    bias_ref,
    send_ref,
    qk_ref,
    shared_ref,
    out_ref,
    p_ref,
    q_ref,
    picks_ref,
    *sems,
):
    gather_send, gather_recv, gather_local = sems[:3]
    plane_sems, cross_sems = sems[3:7], sems[7:11]
    x_sems, dy_sems = sems[11:14], sems[14:17]
    qkv_send, qkv_recv, qkv_local, shared_send, shared_recv = sems[17:22]
    back_sems, local_sem = sems[22:25], sems[25]
    core, plane, spot = place_here()
    micro, rows, _ = x_in_ref.shape
    tokens = PIECES * rows
    local = rows // BLOCK
    blocks = PLANES * SPOTS * local

    barrier = pltpu.get_barrier_semaphore()
    partners = both_partners(core, plane, spot)
    for partner in partners:
        pl.semaphore_signal(barrier, inc=1, device_id=partner, device_id_type=MESH)

    def natural(ref):
        return lambda tile: ref[:, tile * LANES : (tile + 1) * LANES].astype(F32)

    order = [natural_block(entry) for entry in column_order()]
    read = natural(w_qkv_in_ref)
    fold_tiles(
        s_qkv_ref,
        0,
        list(range(TILES)),
        lambda tile: pair_of_blocks(read, order[2 * tile], order[2 * tile + 1]),
    )
    pl.semaphore_wait(barrier, len(partners))

    finish_x = to_planes(x_in_ref, xs_ref, *x_sems)
    gathers = []
    for number, (source, target) in enumerate(
        ((tab_ref, tabs_ref), (vec_ref, vecs_ref), (s_qkv_ref, g_qkv_ref))
    ):
        one = Gather(
            source, target, gather_send.at[number], gather_recv.at[number], gather_local.at[number]
        )
        one.start()
        gathers.append(one)
    outs = D // LANES // 2
    fold_tiles(s_ou_ref, 0, list(range(D // LANES)), natural(w_out_in_ref))
    fold_tiles(s_ou_ref, outs, list(range(FF // LANES)), natural(w_up_in_ref))
    for one in gathers:
        one.column()
    cross = CrossGather(w_down_in_ref, w_down_ref, *cross_sems)
    for one in gathers:
        one.across()
    for one in gathers:
        one.corner()
    cross.across()
    finish_x()
    spread = PlaneGather(s_ou_ref, g_ou_ref, *plane_sems)
    keep_x = pltpu.make_async_copy(xs_ref, x_ref, local_sem.at[0])
    keep_x.start()
    normal, _ = norm_parts(xs_ref[...].reshape(tokens, D).astype(F32))
    for one in gathers[:2]:
        one.finish()

    window_core, window_micro = lax.rem(plane, 2), lax.div(plane, 2)
    scalars = pltpu.make_async_copy(tabs_ref.at[window_core], picks_ref, local_sem.at[1])
    scalars.start()
    lay_vectors(vecs_ref, vectors_ref, up_ref)
    normed_ref[...] = (normal * vectors_ref[0:1] + vectors_ref[1:2]).astype(BF16)
    for tile in range(TILES):
        halves = []
        for entry in column_order()[2 * tile : 2 * tile + 2]:
            halves.append(entry)

        def bias_tile(number, halves=halves):
            if number < D // LANES:
                return vectors_ref[2:3, number * LANES : (number + 1) * LANES]
            if number < 2 * D // LANES:
                return jnp.zeros((1, LANES), F32)
            start = (number - 2 * D // LANES) * LANES
            return vectors_ref[3:4, start : start + LANES]

        chunk, side = tile % HALF_TILES, tile // HALF_TILES
        start = chunk * CHUNK + side * LANES
        bias_ref[:, start : start + LANES] = pair_of_blocks(
            bias_tile, order[2 * tile], order[2 * tile + 1]
        )
    gathers[2].finish()
    settle(g_qkv_ref, [(tile, w_qkv_ref, alternate(tile)) for tile in range(HALF_TILES)])
    keep_w = pltpu.make_async_copy(w_qkv_ref, w_qkv_hbm, local_sem.at[2])
    keep_w.start()

    def shaped(value):
        return value.astype(BF16).reshape(local, BLOCK, LANES)

    low = low_lanes(rows)
    queries = D // LANES
    for chunk in range(HALF_TILES):
        columns = slice(chunk * CHUNK, (chunk + 1) * CHUNK)
        packed = dot(normed_ref[...], w_qkv_ref[:, columns]) + bias_ref[:, columns]
        for side in range(2):
            tile = chunk + side * HALF_TILES
            whole_tile = packed[:, side * LANES : (side + 1) * LANES]
            if tile < queries:
                whole_tile = whole_tile.astype(BF16).astype(F32) * SCALE
            for piece in range(PIECES):
                part = whole_tile[piece * rows : (piece + 1) * rows]
                if tile < SPOTS:
                    send_ref[0, tile, piece, 0] = shaped(part)
                elif tile < queries:
                    first = 2 * (tile - SPOTS)
                    shared = send_ref[0, first, piece, 0].reshape(rows, LANES).astype(F32)
                    send_ref[1, first, piece, 0] = shaped(jnp.where(low, part, shared))
                    shared = send_ref[0, first + 1, piece, 0].reshape(rows, LANES).astype(F32)
                    send_ref[1, first + 1, piece, 0] = shaped(
                        jnp.where(low, swap_halves(part), shared)
                    )
                else:
                    goal, role = (tile - queries) // 3, (tile - queries) % 3
                    if role < 2:
                        send_ref[role, goal, piece, 1] = shaped(part)
                    else:
                        send_ref[0, goal, piece, 2] = shaped(part)
    sends, keeps = [], []
    for part, (parts, landing) in enumerate(((slice(0, 2), qk_ref), (2, shared_ref))):
        for side in (3, 1, 2, 0):
            for other in (core, 1 - core) if part == 0 else (core,):
                goal = flip(spot, side)
                for piece in range(PIECES):
                    source = send_ref.at[other if part == 0 else 0, goal, piece, parts]
                    target = landing.at[2 * core + piece, spot]
                    if side == 0 and other is core:
                        copy = pltpu.make_async_copy(source, target, qkv_local.at[part, piece])
                        keeps.append((part, copy))
                    else:
                        copy = remote(
                            source,
                            target,
                            qkv_send.at[len(sends)],
                            qkv_recv.at[2 * core + piece, spot, part],
                            (other, rank_of(plane, goal)),
                        )
                        sends.append(copy)
                    copy.start()
    spread.columns()
    cross.blocks()
    table = lay_table(tabs_ref, window_core, window_micro, local * RANDOM)
    table_ref[...] = table.astype(jnp.int32)
    sort_entries(table, sorted_ref, blocks * RANDOM)
    scalars.wait()

    def arrive(part, other, piece, goal):
        target = (qk_ref, shared_ref)[part].at[2 * other + piece, goal]
        remote(
            target,
            target,
            qkv_send.at[0],
            qkv_recv.at[2 * other + piece, goal, part],
            (core, rank_of(plane, spot)),
        ).wait_recv()

    for side in range(SPOTS):
        for other in (core, 1 - core):
            if side > 0 or other is not core:
                for piece in range(PIECES):
                    arrive(0, other, piece, flip(spot, side))
    for part, copy in keeps:
        copy.wait()
    cross.hop(1)

    low = low_lanes(BLOCK)
    masks = [half_mask(True), half_mask(False)]

    def tile_of(component, block):
        rank, number = lax.div(block, local), lax.rem(block, local)
        if component == 2:
            return shared_ref[lax.div(rank, SPOTS), lax.rem(rank, SPOTS), number]
        return qk_ref[lax.div(rank, SPOTS), lax.rem(rank, SPOTS), component, number]

    def picked(block, number):
        rank = lax.div(block, local)
        return picks_ref[
            lax.div(rank, SPOTS),
            lax.rem(rank, SPOTS),
            window_micro,
            lax.rem(block, local) * RANDOM + number,
        ]

    def place_of(block):
        rank = lax.div(block, local)
        return lax.div(rank, SPOTS), lax.rem(rank, SPOTS), lax.rem(block, local)

    def put(block, slot, mixed, log):
        place = place_of(block)
        if slot == 0:
            out_ref[place] = mixed.astype(BF16)
            lse_ref[block] = jnp.where(low, log, 0.0)
        else:
            out_ref[place] = jnp.where(low, mixed, out_ref[place].astype(F32)).astype(BF16)
            lse_ref[block] = jnp.where(low, lse_ref[block], log)

    def one_block(block, slot):
        ids, bias = inner_slots(picked, block, blocks)
        keys = jnp.concatenate([tile_of(1 + slot, number) for number in ids], axis=0)
        scores = dot_rt(tile_of(0, block) * masks[slot], keys) + bias
        top = jnp.max(scores, axis=1, keepdims=True)
        powered = jnp.exp(scores - top)
        total = jnp.sum(powered, axis=1, keepdims=True)
        mixed = dot(powered.astype(BF16), keys) * (1.0 / total)
        return mixed, top + jnp.log(total)

    def rank_blocks(rank, slot):
        results = [one_block(rank * local + number, slot) for number in range(local)]
        for number, (mixed, log) in enumerate(results):
            put(rank * local + number, slot, mixed, log)

    spans = blocks // SPAN
    ends = (0, blocks - 1)

    def dense(slot, scores_ref, numbers):
        size = len(numbers) * BLOCK
        query = jnp.concatenate([tile_of(0, number) * masks[slot] for number in numbers], axis=0)

        def keys_at(span):
            return jnp.concatenate(
                [tile_of(1 + slot, span * SPAN + number) for number in range(SPAN)], axis=0
            )

        def first_pass(span, top):
            scores = dot_rt(query, keys_at(span))
            scores_ref[span] = scores
            return jnp.maximum(top, jnp.max(scores, axis=1, keepdims=True))

        top = lax.fori_loop(
            0, spans, first_pass, jnp.full((size, 1), NEGATIVE, F32), unroll=2
        )

        def second_pass(span, carry):
            total, mixed = carry
            powered = jnp.exp(scores_ref[span] - top)
            return (
                total + jnp.sum(powered, axis=1, keepdims=True),
                mixed + dot(powered.astype(BF16), keys_at(span)),
            )

        total, mixed = lax.fori_loop(
            0,
            spans,
            second_pass,
            (jnp.zeros((size, 1), F32), jnp.zeros((size, LANES), F32)),
            unroll=2,
        )
        mixed = mixed * (1.0 / total)
        log = top + jnp.log(total)
        for place, number in enumerate(numbers):
            span = slice(place * BLOCK, (place + 1) * BLOCK)
            put(number, slot, mixed[span], log[span])

    def head_a(number, carry):
        rank_blocks(number, 0)
        return carry

    def head_b(number, carry):
        rank_blocks(core * (PLANES * SPOTS // 2) + number, 1)
        return carry

    shared = []
    half_way = PLANES * SPOTS // 2
    lax.fori_loop(0, half_way, head_a, 0)
    for side in range(SPOTS):
        goal = flip(spot, side)
        for piece in range(PIECES):
            if side > 0:
                arrive(1, core, piece, goal)
            source = shared_ref.at[2 * core + piece, goal]
            copy = remote(
                source,
                source,
                shared_send.at[2 * side + piece],
                shared_recv.at[2 * core + piece, goal],
                (1 - core, rank_of(plane, spot)),
            )
            copy.start()
            shared.append(copy)
    cross.hop(2)
    finish_dy = to_planes(dy_ref, dys_ref, *dy_sems)
    lax.fori_loop(half_way, PLANES * SPOTS, head_a, 0)
    dense(0, p_ref, ends)
    spread.forward()
    back = Inward(out_ref, back_ref, *back_sems)
    everything = slice(0, local)
    for side, other, goal, stays in inward_targets(core, spot):
        if other is not core:
            for piece in range(PIECES):
                back.send(other, goal, stays, piece, 0, everything)
    for side in range(SPOTS):
        for piece in range(PIECES):
            target = shared_ref.at[2 * (1 - core) + piece, flip(spot, side)]
            remote(
                target,
                target,
                shared_send.at[0],
                shared_recv.at[2 * (1 - core) + piece, flip(spot, side)],
                (core, rank_of(plane, spot)),
            ).wait_recv()
    keep_qk = pltpu.make_async_copy(qk_ref, qk_hbm, local_sem.at[3])
    keep_qk.start()
    keep_shared = pltpu.make_async_copy(shared_ref, shared_hbm, local_sem.at[6])
    keep_shared.start()
    lax.fori_loop(0, half_way, head_b, 0)
    dense(1, q_ref, (core * (blocks - 1),))
    spread.corner()
    cross.hop(3)
    for side, other, goal, stays in inward_targets(core, spot):
        if other is core:
            for piece in range(PIECES):
                back.send(other, goal, stays, piece, 0, everything)
    spread.finish()
    settle(
        g_ou_ref,
        [(tile, w_out_ref, (tile, outs + tile)) for tile in range(outs)]
        + [(outs + tile, w_up_ref, alternate(tile)) for tile in range(FF // CHUNK)],
    )
    keep_out = pltpu.make_async_copy(w_out_ref, w_out_hbm, local_sem.at[4])
    keep_out.start()
    keep_up = pltpu.make_async_copy(w_up_ref, w_up_hbm, local_sem.at[5])
    keep_up.start()
    cross.finish()
    finish_dy()
    for copy in sends:
        copy.wait_send()
    for copy in shared:
        copy.wait_send()
    back.finish(((everything,), (everything,)))
    for copy in (keep_x, keep_w, keep_qk, keep_shared, keep_out, keep_up):
        copy.wait()


def front(x, dy, vec, tab, w_qkv, w_out, w_up, w_down):
    micro, rows, _ = x.shape
    tokens = PIECES * rows
    local = rows // BLOCK
    blocks = PLANES * SPOTS * local
    spans = blocks // SPAN
    grid = (2, PLANES, SPOTS)
    shard = D // RANKS
    tile = (local, BLOCK, LANES)
    dma = pltpu.SemaphoreType.DMA
    struct = jax.ShapeDtypeStruct
    ou = (2 * shard, (D + FF) // 2)
    return pl.pallas_call(
        front_kernel,
        out_shape=(
            struct((2, SPOTS, PIECES) + tile, BF16),
            struct(x.shape, BF16),
            struct(dy.shape, BF16),
            struct(grid + w_down.shape, BF16),
            struct((D, 3 * D), BF16),
            struct((D, D), BF16),
            struct((D, FF), BF16),
            struct((PLANES, SPOTS, 2) + tile, BF16),
            struct((PLANES, SPOTS) + tile, BF16),
            struct((tokens, D), BF16),
            struct((blocks, BLOCK, LANES), F32),
            struct((VECTORS, D), F32),
            struct((FF // CHUNK, 1, CHUNK), F32),
            struct((1, 2 * LANES), jnp.int32),
            struct((4, 2 * LANES), jnp.int32),
        ),
        in_specs=[
            whole(ANY),
            whole(ANY),
            whole(ANY),
            whole(ANY),
            whole(),
            whole(),
            whole(),
            whole(ANY),
        ],
        out_specs=(whole(ANY),) * 9 + (whole(),) * 6,
        scratch_shapes=[
            VMEM((2 * shard, 3 * D // 2), BF16),
            VMEM(ou, BF16),
            VMEM(grid + (2 * shard, 3 * D // 2), BF16),
            VMEM(grid + ou, BF16),
            VMEM((D, 3 * D), BF16),
            VMEM((D, D), BF16),
            VMEM((D, FF), BF16),
            VMEM((PIECES, rows, D), BF16),
            VMEM(grid + vec.shape, BF16),
            VMEM(grid + tab.shape, jnp.int32),
            VMEM((1, 3 * D), F32),
            VMEM((2, SPOTS, PIECES, 3) + tile, BF16),
            VMEM((PLANES, SPOTS, 2) + tile, BF16),
            VMEM((PLANES, SPOTS) + tile, BF16),
            VMEM((PLANES, SPOTS) + tile, BF16),
            VMEM((spans, 2 * BLOCK, SPAN * BLOCK), F32),
            VMEM((spans, BLOCK, SPAN * BLOCK), F32),
            pltpu.SMEM((PLANES, SPOTS) + tab.shape, jnp.int32),
            dma((3, Gather.SENDS)),
            dma((3,) + grid),
            dma((3,)),
            dma((PlaneGather.SENDS,)),
            dma((PLANES,)),
            dma((2, SPOTS, 2)),
            dma,
            dma((CrossGather.SENDS,)),
            dma((SPOTS,)),
            dma((2, PLANES)),
            dma,
        ]
        + [dma((2,))] * 6
        + [
            dma((20,)),
            dma((PLANES, SPOTS, 2)),
            dma((2, PIECES)),
            dma((2 * SPOTS,)),
            dma((PLANES, SPOTS)),
            dma((14,)),
            dma((2, SPOTS, PIECES, 1)),
            dma((1, PIECES)),
            dma((7,)),
        ],
        compiler_params=pltpu.CompilerParams(
            vmem_limit_bytes=60 * 1024 * 1024, collective_id=1, has_side_effects=True
        ),
        name="front",
    )(x, dy, vec, tab, w_qkv, w_out, w_up, w_down)


def by_owner(out_ref, values):
    rows = D // RANKS
    width = values.shape[1] // 2
    for owner in range(RANKS):
        part = values[owner * rows : (owner + 1) * rows]
        out_ref[owner] = jnp.concatenate([part[:, :width], part[:, width:]], axis=0).astype(BF16)


def plane_middle_kernel(
    mixed_in_ref,
    x_ref,
    dy_ref,
    vec_ref,
    w_out_ref,
    up_shift_ref,
    w_up_ref,
    w_down_ref,
    hidden_ref,
    send_ref,
    dres_ref,
    g_out_ref,
    g_up_ref,
    g_down_ref,
    g_up_bias_ref,
    g_small_ref,
    mixed_ref,
    residual_ref,
    second_ref,
    second_t_ref,
    total_ref,
    dsecond_ref,
):
    pieces, rows, _ = x_ref.shape
    tokens = pieces * rows
    step = pl.program_id(0)
    low = low_lanes(rows)
    out_shift, gain, shift, down_shift = (vec_ref[number : number + 1] for number in (4, 5, 6, 7))

    @pl.when(step == 0)
    def _():
        core = lax.axis_index("gx")
        for piece in range(pieces):
            span = slice(piece * rows, (piece + 1) * rows)
            for spot in (0, 2):
                first = [mixed_in_ref[side, spot, piece].astype(F32) for side in range(2)]
                last = [mixed_in_ref[side, spot + 1, piece].astype(F32) for side in range(2)]
                own_first = jnp.where(core == 0, first[0], first[1])
                own_last = jnp.where(core == 0, last[0], last[1])
                tiles = (
                    jnp.where(low, swap_halves(first[0]), first[1]),
                    jnp.where(low, own_first, last[0]),
                    swap_halves(jnp.where(low, own_last, last[1])),
                )
                for number, tile in enumerate(tiles):
                    spread = 3 * (spot // 2) + number
                    mixed_ref[span, spread * LANES : (spread + 1) * LANES] = tile.astype(BF16)
        residual = x_ref[...].reshape(tokens, D).astype(F32) + (
            dot(mixed_ref[...], w_out_ref[...]) + out_shift
        )
        residual_ref[...] = residual
        normal, _ = norm_parts(residual)
        second = normal * gain + shift
        second_ref[...] = second.astype(BF16)
        second_t_ref[...] = second.T.astype(BF16)
        total_ref[...] = jnp.zeros_like(total_ref)
        dsecond_ref[...] = jnp.zeros_like(dsecond_ref)

    w_down = w_down_ref[...].reshape(CHUNK, D)
    upper = dot(second_ref[...], w_up_ref[...]) + up_shift_ref[0]
    factor = 0.7978845608028654
    square = upper * upper
    bent = jnp.tanh(factor * (upper + 0.044715 * (upper * square)))
    middle_half = 0.5 * (1.0 + bent)
    active = (upper * middle_half).astype(BF16)
    slope = middle_half + 0.5 * upper * (1.0 - bent * bent) * (
        factor + (3.0 * 0.044715 * factor) * square
    )
    dy = dy_ref[...]
    total_ref[...] += dot(active, w_down)
    g_down_ref[...] = dot_lt(active, dy).astype(BF16).reshape(g_down_ref.shape)
    dupper = (dot_rt(dy, w_down) * slope).astype(BF16)
    g_up_bias_ref[0] = jnp.sum(dupper.astype(F32), axis=0, keepdims=True)
    by_owner(g_up_ref, dot(second_t_ref[...], dupper))
    dsecond_ref[...] += dot_rt(dupper, w_up_ref[...])

    @pl.when(step == pl.num_programs(0) - 1)
    def _():
        residual = residual_ref[...]
        hidden_ref[...] = (
            (residual + (total_ref[...] + down_shift)).astype(BF16).reshape(x_ref.shape)
        )
        normal, inverse = norm_parts(residual)
        dsecond = dsecond_ref[...]
        grad_out = dy_ref[...].astype(F32)
        g_small_ref[0:1] = jnp.sum(dsecond * normal, axis=0, keepdims=True)
        g_small_ref[1:2] = jnp.sum(dsecond, axis=0, keepdims=True)
        g_small_ref[2:3] = jnp.sum(grad_out, axis=0, keepdims=True)
        dres = grad_out + norm_pull(dsecond, normal, inverse, gain)
        dres_ref[...] = dres
        branch = dres.astype(BF16)
        g_small_ref[3:4] = jnp.sum(branch.astype(F32), axis=0, keepdims=True)
        by_owner(g_out_ref, dot_lt(mixed_ref[...], branch))
        dmixed = dot_rt(branch, w_out_ref[...])
        for piece in range(pieces):
            span = slice(piece * rows, (piece + 1) * rows)
            for spot in (0, 2):
                tiles = [
                    dmixed[span, number * LANES : (number + 1) * LANES]
                    for number in range(3 * (spot // 2), 3 * (spot // 2) + 3)
                ]
                flipped = [swap_halves(tile) for tile in tiles]
                send_ref[0, spot, piece] = jnp.where(low, tiles[1], flipped[0]).astype(BF16)
                send_ref[1, spot, piece] = jnp.where(low, tiles[1], tiles[0]).astype(BF16)
                send_ref[0, spot + 1, piece] = jnp.where(low, flipped[2], tiles[1]).astype(BF16)
                send_ref[1, spot + 1, piece] = flipped[2].astype(BF16)


def plane_middle(mixed_in, x, dy, vec, w_out, up_shift, w_up, w_down):
    pieces, rows, _ = x.shape
    tokens = pieces * rows
    shard = D // RANKS

    def fixed(shape):
        return pl.BlockSpec(shape, lambda step: (0,) * len(shape))

    steps = FF // CHUNK
    down = pl.BlockSpec((2, LANES, D), lambda step: (0, step, 0))
    return pl.pallas_call(
        plane_middle_kernel,
        grid=(steps,),
        out_shape=(
            jax.ShapeDtypeStruct(x.shape, BF16),
            jax.ShapeDtypeStruct(mixed_in.shape, BF16),
            jax.ShapeDtypeStruct((tokens, D), F32),
            jax.ShapeDtypeStruct((RANKS, 2 * shard, D // 2), BF16),
            jax.ShapeDtypeStruct((RANKS, 2 * shard, FF // 2), BF16),
            jax.ShapeDtypeStruct((2, FF // 2, D), BF16),
            jax.ShapeDtypeStruct((steps, 1, CHUNK), F32),
            jax.ShapeDtypeStruct((4, D), F32),
        ),
        in_specs=[
            fixed(mixed_in.shape),
            fixed(x.shape),
            fixed((tokens, D)),
            fixed(vec.shape),
            fixed((D, D)),
            pl.BlockSpec((1, 1, CHUNK), lambda step: (step, 0, 0)),
            pl.BlockSpec((D, CHUNK), lambda step: (0, step)),
            down,
        ],
        out_specs=(
            fixed(x.shape),
            fixed(mixed_in.shape),
            fixed((tokens, D)),
            fixed((RANKS, 2 * shard, D // 2)),
            pl.BlockSpec((RANKS, 2 * shard, LANES), lambda step: (0, 0, step)),
            down,
            pl.BlockSpec((1, 1, CHUNK), lambda step: (step, 0, 0)),
            fixed((4, D)),
        ),
        scratch_shapes=[
            VMEM((tokens, D), BF16),
            VMEM((tokens, D), F32),
            VMEM((tokens, D), BF16),
            VMEM((D, tokens), BF16),
            VMEM((tokens, D), F32),
            VMEM((tokens, D), F32),
        ],
        compiler_params=params_of(56),
        name="plane_middle",
    )(mixed_in, x, dy, vec, w_out, up_shift, w_up, w_down)


class Reduce:
    SENDS = 4 + 2 + 2 + 3
    RECVS = SENDS

    def __init__(self, source, total, near, corner_x, corner_y, side_x, side_y, far, out, sems):
        self.source, self.total, self.near = source, total, near
        self.corner = {1: corner_x, 2: corner_y}
        self.side = {1: side_x, 2: side_y}
        self.far, self.out = far, out
        self.send_sem, self.recv_sem, self.local_sem = sems
        self.core, self.plane, self.spot = place_here()
        self.copies = []
        self.locals = []

    def start(self):
        sibling = (1 - self.core, rank_of(self.plane, self.spot))
        for number, side in enumerate((3, 1, 2, 0)):
            spot = flip(self.spot, side)
            copy = remote(
                self.source.at[1 - self.core, :, spot],
                self.near.at[:, spot],
                self.send_sem.at[number],
                self.recv_sem.at[number],
                sibling,
            )
            copy.start()
            self.copies.append(copy)
            keep = pltpu.make_async_copy(
                self.source.at[self.core, :, spot],
                self.total.at[:, spot],
                self.local_sem.at[number],
            )
            keep.start()
            self.locals.append(keep)

    def take(self, number, side):
        self.copies[number].wait_recv()
        self.locals[number].wait()
        spot = flip(self.spot, side)

        def add(plane, carry):
            self.total[plane, spot] = (
                self.total[plane, spot].astype(F32) + self.near[plane, spot].astype(F32)
            ).astype(self.total.dtype)
            return carry

        lax.fori_loop(0, PLANES, add, 0)

    def corners(self):
        self.take(0, 3)
        spot = flip(self.spot, 3)
        index = 4
        self.corner_copies = []
        for bits in range(PLANES):
            side = 2 if bits < 2 else 1
            self.corner_copies.append(None)
            plane = flip(self.plane, bits)
            copy = remote(
                self.total.at[plane, spot],
                self.corner[side].at[bits % 2],
                self.send_sem.at[index + bits],
                self.recv_sem.at[index + bits],
                (self.core, rank_of(self.plane, flip(self.spot, side))),
            )
            copy.start()
            self.corner_copies[bits] = copy

    def sides(self):
        self.take(1, 1)
        self.take(2, 2)
        self.side_copies = {}
        for side in (1, 2):
            spot = flip(self.spot, side)
            came = 3 - side
            for bits in (0, 1) if came == 2 else (2, 3):
                self.corner_copies[bits].wait_recv()
                plane = flip(self.plane, bits)
                self.total[plane, spot] = (
                    self.total[plane, spot].astype(F32)
                    + self.corner[came][bits % 2].astype(F32)
                ).astype(self.total.dtype)
            copy = remote(
                self.total.at[:, spot],
                self.side[side],
                self.send_sem.at[7 + side],
                self.recv_sem.at[7 + side],
                (self.core, rank_of(self.plane, spot)),
            )
            copy.start()
            self.side_copies[side] = copy

    def columns(self):
        self.take(3, 0)
        for side in (1, 2):
            self.side_copies[side].wait_recv()

        def add(plane, carry):
            self.total[plane, self.spot] = (
                self.total[plane, self.spot].astype(F32)
                + self.side[1][plane].astype(F32)
                + self.side[2][plane].astype(F32)
            ).astype(self.total.dtype)
            return carry

        lax.fori_loop(0, PLANES, add, 0)
        self.far_copies = []
        for bits in range(1, PLANES):
            plane = flip(self.plane, bits)
            copy = remote(
                self.total.at[plane, self.spot],
                self.far.at[bits - 1],
                self.send_sem.at[9 + bits],
                self.recv_sem.at[9 + bits],
                (self.core, rank_of(plane, self.spot)),
            )
            copy.start()
            self.far_copies.append(copy)

    def finish(self):
        value = self.total[self.plane, self.spot].astype(F32)
        for bits in range(1, PLANES):
            self.far_copies[bits - 1].wait_recv()
            value = value + self.far[bits - 1].astype(F32)
        self.out[...] = value
        for copy in self.copies + self.corner_copies + self.far_copies:
            copy.wait_send()
        for side in (1, 2):
            self.side_copies[side].wait_send()


REDUCE_SEMS = 13


def reduce_scratch(shape, kind):
    tail = shape[3:]
    return [
        VMEM((PLANES, SPOTS) + tail, kind),
        VMEM((PLANES, SPOTS) + tail, kind),
        VMEM((2,) + tail, kind),
        VMEM((2,) + tail, kind),
        VMEM((PLANES,) + tail, kind),
        VMEM((PLANES,) + tail, kind),
        VMEM((PLANES - 1,) + tail, kind),
    ]


class Doubling:
    STEPS = 5

    def __init__(self, totals, boxes, send_sem, recv_sem):
        self.totals, self.boxes = totals, boxes
        self.send_sem, self.recv_sem = send_sem, recv_sem
        core, plane, spot = place_here()
        self.partners = (
            (1 - core, rank_of(plane, spot)),
            (core, rank_of(plane, flip(spot, 1))),
            (core, rank_of(plane, flip(spot, 2))),
            (core, rank_of(flip(plane, 1), spot)),
            (core, rank_of(flip(plane, 2), spot)),
        )
        self.copies = []

    def start(self, step):
        self.copies = []
        for number, (total, box) in enumerate(zip(self.totals, self.boxes)):
            copy = remote(
                total,
                box.at[step],
                self.send_sem.at[step, number],
                self.recv_sem.at[step, number],
                self.partners[step],
            )
            copy.start()
            self.copies.append(copy)

    def finish(self, step):
        for copy, total, box in zip(self.copies, self.totals, self.boxes):
            copy.wait()
            total[...] += box[step]


PARTS = 3


def finish_kernel(
    recv_ref,
    normed_ref,
    x_ref,
    dres_hbm,
    vec_ref,
    w_hbm,
    g_mid_ref,
    g_up_bias_ref,
    grad_ref,
    g_qkv_ref,
    rows_out_ref,
    tiles_out_ref,
    *scratch,
):
    sources, scratch = scratch[:PARTS], scratch[PARTS:]
    buffers, scratch = scratch[: 7 * PARTS], scratch[7 * PARTS :]
    packed_ref, dnormed_ref, gradient_ref, dres_ref, w_ref = scratch[:5]
    rows_ref, tiles_ref, rows_box, tiles_box = scratch[5:9]
    send_sem, recv_sem, local_sem, load_sem, sum_send, sum_recv = scratch[9:15]
    move_sems = scratch[15:18]
    pieces, rows, _ = x_ref.shape
    tokens = pieces * rows
    core, plane, spot = place_here()
    low = low_lanes(rows)

    load_w = pltpu.make_async_copy(w_hbm, w_ref, load_sem.at[0])
    load_dres = pltpu.make_async_copy(dres_hbm, dres_ref, load_sem.at[1])
    load_w.start()
    load_dres.start()
    greet(all_partners(core, plane, spot))

    def put(tile, piece, value):
        side, chunk = tile // HALF_TILES, tile % HALF_TILES
        packed_ref[
            piece * rows : (piece + 1) * rows,
            chunk * CHUNK + side * LANES : chunk * CHUNK + (side + 1) * LANES,
        ] = value.astype(BF16)

    for piece in range(pieces):
        seconds = []
        for goal in range(SPOTS):
            first = recv_ref[0, goal, piece, QUERIES].astype(F32)
            second = recv_ref[1, goal, piece, QUERIES].astype(F32)
            put(goal, piece, jnp.where(low, first, jnp.where(core == 0, first, second)))
            seconds.append(second)
            base = D // LANES + 3 * goal
            put(base, piece, recv_ref[0, goal, piece, KEYS_A])
            put(base + 1, piece, recv_ref[1, goal, piece, KEYS_A])
            put(base + 2, piece, recv_ref[core, goal, piece, KEYS_B])
        for number in range(2):
            put(
                SPOTS + number,
                piece,
                jnp.where(low, seconds[2 * number], swap_halves(seconds[2 * number + 1])),
            )

    load_w.wait()
    for chunk in range(HALF_TILES):
        columns = slice(chunk * CHUNK, (chunk + 1) * CHUNK)
        share = dot_rt(packed_ref[:, columns], w_ref[:, columns])
        if chunk == 0:
            dnormed_ref[...] = share
        else:
            dnormed_ref[...] += share
    normal, inverse = norm_parts(x_ref[...].reshape(tokens, D).astype(F32))
    dnormed = dnormed_ref[...]
    load_dres.wait()
    gradient = dres_ref[...] + norm_pull(dnormed, normal, inverse, vec_ref[0:1])
    gradient_ref[...] = gradient.astype(BF16).reshape(x_ref.shape)
    finish_grad = from_planes(gradient_ref, grad_ref, *move_sems)

    rows_ref[0:1] = jnp.sum(dnormed * normal, axis=0, keepdims=True)
    rows_ref[1:2] = jnp.sum(dnormed, axis=0, keepdims=True)
    rows_ref[2:6] = g_mid_ref[...]
    rows_ref[6:8] = jnp.zeros((2, D), F32)
    tiles_ref[...] = jnp.zeros_like(tiles_ref)
    for step in range(FF // CHUNK):
        tiles_ref[step : step + 1] = g_up_bias_ref[step]
    for chunk in range(HALF_TILES):
        number = FF // CHUNK + chunk
        tiles_ref[number : number + 1] = jnp.sum(
            packed_ref[:, chunk * CHUNK : (chunk + 1) * CHUNK].astype(F32), axis=0, keepdims=True
        )
    sums = Doubling((rows_ref, tiles_ref), (rows_box, tiles_box), sum_send, sum_recv)
    sums.start(0)

    width = HALF_TILES // PARTS * LANES
    reduces = [
        Reduce(
            sources[part],
            *buffers[7 * part : 7 * part + 7],
            g_qkv_ref.at[:, part * width : (part + 1) * width],
            (send_sem.at[part], recv_sem.at[part], local_sem.at[part]),
        )
        for part in range(PARTS)
    ]
    shard = D // RANKS
    normed_t = normed_ref[...].astype(F32).T.astype(BF16)
    for part in range(PARTS):
        for number in range(HALF_TILES // PARTS):
            chunk = part * (HALF_TILES // PARTS) + number
            values = dot(normed_t, packed_ref[:, chunk * CHUNK : (chunk + 1) * CHUNK])
            columns = slice(number * LANES, (number + 1) * LANES)
            for owner in range(RANKS):
                mine = values[owner * shard : (owner + 1) * shard]
                sources[part][
                    owner // (PLANES * SPOTS), owner // SPOTS % PLANES, owner % SPOTS, :, columns
                ] = jnp.concatenate([mine[:, :LANES], mine[:, LANES:]], axis=0).astype(BF16)
        reduces[part].start()
        if part > 0:
            reduces[part - 1].corners()
        if part > 1:
            reduces[part - 2].sides()
    sums.finish(0)
    sums.start(1)
    reduces[2].corners()
    reduces[1].sides()
    sums.finish(1)
    sums.start(2)
    reduces[0].columns()
    reduces[2].sides()
    sums.finish(2)
    sums.start(3)
    reduces[1].columns()
    sums.finish(3)
    sums.start(4)
    reduces[2].columns()
    sums.finish(4)
    for one in reduces:
        one.finish()
    rows_out_ref[...] = rows_ref[...]
    tiles_out_ref[...] = tiles_ref[...]
    finish_grad()


def finish_layer(recv, normed, x, dres, vec, w, g_mid, g_up_bias):
    pieces, rows, _ = x.shape
    tokens = pieces * rows
    shard = D // RANKS
    grid = (2, PLANES, SPOTS)
    part = grid + (2 * shard, HALF_TILES // PARTS * LANES)
    buffers = []
    for _ in range(PARTS):
        buffers += reduce_scratch(part, BF16)
    tiles = -(-(FF // CHUNK + HALF_TILES) // 8) * 8
    dma = pltpu.SemaphoreType.DMA
    return pl.pallas_call(
        finish_kernel,
        out_shape=(
            jax.ShapeDtypeStruct(x.shape, BF16),
            jax.ShapeDtypeStruct((2 * shard, 3 * D // 2), F32),
            jax.ShapeDtypeStruct((8, D), F32),
            jax.ShapeDtypeStruct((tiles, CHUNK), F32),
        ),
        in_specs=[
            whole(),
            whole(),
            whole(),
            whole(ANY),
            whole(),
            whole(ANY),
            whole(),
            whole(),
        ],
        out_specs=(whole(ANY), whole(), whole(), whole()),
        scratch_shapes=[VMEM(part, BF16)] * PARTS
        + buffers
        + [
            VMEM((tokens, 3 * D), BF16),
            VMEM((tokens, D), F32),
            VMEM(x.shape, BF16),
            VMEM((tokens, D), F32),
            VMEM(w.shape, BF16),
            VMEM((8, D), F32),
            VMEM((tiles, CHUNK), F32),
            VMEM((Doubling.STEPS, 8, D), F32),
            VMEM((Doubling.STEPS, tiles, CHUNK), F32),
            dma((PARTS, REDUCE_SEMS)),
            dma((PARTS, REDUCE_SEMS)),
            dma((PARTS, 4)),
            dma((2,)),
            dma((Doubling.STEPS, 2)),
            dma((Doubling.STEPS, 2)),
            dma((2,)),
            dma((2,)),
            dma((2,)),
        ],
        compiler_params=pltpu.CompilerParams(
            vmem_limit_bytes=60 * 1024 * 1024, collective_id=2, has_side_effects=True
        ),
        name="finish_layer",
    )(recv, normed, x, dres, vec, w, g_mid, g_up_bias)


def fold_columns(array):
    half = array.shape[1] // 2
    return jnp.concatenate([array[:, :half], array[:, half:]], axis=0)


def unfold_columns(array):
    half = array.shape[0] // 2
    return jnp.concatenate([array[:half], array[half:]], axis=1)


def plane_shards(
    hidden_in,
    rand_table,
    norm1_gain,
    norm1_bias,
    w_qkv,
    query_bias,
    value_bias,
    w_out,
    out_bias,
    norm2_gain,
    norm2_bias,
    w_up,
    up_bias,
    w_down,
    down_bias,
    cotangent,
):
    micro, rows, _ = hidden_in.shape
    local = rows // BLOCK
    own = norm1_gain.shape[0]
    order = [natural_block(entry) for entry in column_order()]
    inverse = [order.index(number) for number in range(len(order))]

    def in_row(vector, number):
        return jnp.pad(vector[None], ((number, 15 - number), (0, LANES - vector.shape[0])))

    vec = functools.reduce(
        jnp.add,
        [
            in_row(vector, number)
            for number, vector in enumerate(
                (
                    norm1_gain,
                    norm1_bias,
                    query_bias,
                    value_bias,
                    out_bias,
                    norm2_gain,
                    norm2_bias,
                    down_bias,
                    up_bias,
                )
            )
        ],
    )
    tab = jnp.pad(
        rand_table.reshape(micro, local * RANDOM), ((0, 8 - micro), (0, LANES - local * RANDOM))
    )
    (
        mixed,
        x,
        dy,
        w_down_all,
        w_qkv_all,
        w_out_all,
        w_up_all,
        qk,
        shared,
        normed,
        lse,
        vectors,
        up_shift,
        table,
        sorted_table,
    ) = front(hidden_in, cotangent, vec, tab, w_qkv, w_out, w_up, w_down)
    mixed = mixed.reshape(2, SPOTS, PIECES, rows, LANES)
    hidden, grad_send, dres, g_out, g_up, g_down, g_up_bias, g_mid = plane_middle(
        mixed,
        x,
        dy.reshape(micro * rows, D),
        vectors,
        w_out_all,
        up_shift,
        w_up_all,
        w_down_all.reshape(2, FF // 2, D),
    )
    grid = (2, PLANES, SPOTS)
    dqkv, hidden_out, t_out, t_up, t_down = plane_attention_back(
        table,
        sorted_table,
        qk,
        shared,
        grad_send.reshape(2, SPOTS, PIECES, local, BLOCK, LANES),
        lse,
        hidden,
        [
            g_out.reshape(grid + g_out.shape[1:]),
            g_up.reshape(grid + g_up.shape[1:]),
            g_down.reshape(grid + (FF // RANKS, D)),
        ],
    )
    dqkv = dqkv.reshape(2, SPOTS, PIECES, 3, rows, LANES)
    grad_hidden, t_qkv, sum_rows, sum_tiles = finish_layer(
        dqkv, normed, x, dres, vectors, w_qkv_all, g_mid, g_up_bias
    )

    mine = lax.axis_index("gx") * PLANES * SPOTS + lax.axis_index("gy")
    sum_tiles = sum_tiles.reshape(-1, 2, LANES)
    g_bias = sum_tiles[FF // CHUNK : FF // CHUNK + HALF_TILES].swapaxes(0, 1).reshape(1, 3 * D)
    g_bias = take_blocks(g_bias, inverse)
    sum_rows = jnp.concatenate([sum_rows, g_bias[:, :D], g_bias[:, 2 * D :]], axis=0)
    parts = lax.dynamic_slice_in_dim(sum_rows, mine * own, own, 1)
    g_up_bias = sum_tiles[: FF // CHUNK].swapaxes(0, 1).reshape(FF)
    g_up_bias = lax.dynamic_slice_in_dim(g_up_bias, mine * (FF // RANKS), FF // RANKS, 0)
    return (
        hidden_out,
        grad_hidden.astype(F32),
        parts[0],
        parts[1],
        take_blocks(unfold_columns(t_qkv), inverse),
        parts[8],
        parts[9],
        unfold_columns(t_out),
        parts[5],
        parts[2],
        parts[3],
        unfold_columns(t_up),
        g_up_bias,
        t_down,
        parts[4],
    )


def shards(*arrays):
    micro, rows, _ = arrays[0].shape
    fits = lax.axis_size("gx") == 2 and lax.axis_size("gy") == PLANES * SPOTS
    fits = fits and micro == 2 and rows % BLOCK == 0
    return (plane_shards if fits else general_shards)(*arrays)


def solution(mesh):
    tokens = P(None, AXES, None)
    vector = P(AXES)
    matrix = P(AXES, None)
    placed = (
        tokens,
        tokens,
        vector,
        vector,
        matrix,
        vector,
        vector,
        matrix,
        vector,
        vector,
        vector,
        matrix,
        vector,
        matrix,
        vector,
        tokens,
    )
    returned = (
        tokens,
        tokens,
        vector,
        vector,
        matrix,
        vector,
        vector,
        matrix,
        vector,
        vector,
        vector,
        matrix,
        vector,
        matrix,
        vector,
    )
    return jax.shard_map(
        shards, mesh=mesh, in_specs=placed, out_specs=returned, check_vma=False
    )
```

```python
import functools

import jax
import jax.numpy as jnp
from jax import lax
from jax.experimental import pallas as pl
from jax.experimental.pallas import tpu as pltpu
from jax.sharding import PartitionSpec as P

HEADS = 12
HEAD_DIM = 64
D = 768
FF = 3072
BLOCK = 64
RANDOM = 3
LANES = 2 * HEAD_DIM
EPSILON = 1e-05
NEGATIVE = -1e30
SCALE = HEAD_DIM**-0.5
CHUNK = 256
SPAN = 8

F32 = jnp.float32
BF16 = jnp.bfloat16
VMEM = pltpu.VMEM


def whole(space=VMEM):
    return pl.BlockSpec(memory_space=space)


def params_of(megabytes):
    return pltpu.CompilerParams(vmem_limit_bytes=megabytes * 1024 * 1024)


def head_place(head):
    return (head // 3) * 4 + head % 3


def dot(left, right):
    return lax.dot_general(left, right, (((1,), (0,)), ((), ())), preferred_element_type=F32)


def dot_rt(left, right):
    return lax.dot_general(left, right, (((1,), (1,)), ((), ())), preferred_element_type=F32)


def dot_lt(left, right):
    return lax.dot_general(left, right, (((0,), (0,)), ((), ())), preferred_element_type=F32)


def swap_halves(tile):
    return pltpu.roll(tile, HEAD_DIM, axis=tile.ndim - 1)


def low_lanes(rows):
    return lax.broadcasted_iota(jnp.int32, (rows, LANES), 1) < HEAD_DIM


def norm_parts(values):
    centre = values - jnp.mean(values, axis=-1, keepdims=True)
    spread = jnp.mean(centre * centre, axis=-1, keepdims=True)
    inverse = lax.rsqrt(spread + EPSILON)
    return centre * inverse, inverse


def norm_pull(grad, normal, inverse, gain):
    scaled = grad * gain
    return inverse * (
        scaled
        - jnp.mean(scaled, axis=-1, keepdims=True)
        - normal * jnp.mean(scaled * normal, axis=-1, keepdims=True)
    )


def qkv_kernel(x_ref, gain_ref, shift_ref, w_ref, bias_ref, normed_ref, send_ref):
    micro, rows, _ = x_ref.shape
    values = x_ref[...].reshape(micro * rows, D).astype(F32)
    normal, _ = norm_parts(values)
    normed_ref[...] = (normal * gain_ref[...] + shift_ref[...]).astype(BF16)
    low = low_lanes(rows)
    for chunk in range(3 * D // CHUNK):
        columns = slice(chunk * CHUNK, (chunk + 1) * CHUNK)
        packed = dot(normed_ref[...], w_ref[:, columns]) + bias_ref[:, columns]
        if chunk < D // CHUNK:
            packed = packed.astype(BF16).astype(F32) * SCALE
        for tile in range(CHUNK // LANES):
            part = packed[:, tile * LANES : (tile + 1) * LANES]
            first, second = part[:rows], part[rows:]
            if chunk < D // CHUNK:
                head = (chunk * CHUNK // LANES + tile) * 2
                even = jnp.where(low, first, swap_halves(second))
                odd = jnp.where(low, swap_halves(first), second)
                send_ref[head_place(head), 0] = even.astype(BF16)
                send_ref[head_place(head + 1), 0] = odd.astype(BF16)
            else:
                head = (chunk * CHUNK - D) // LANES + tile
                send_ref[head_place(head), 1] = first.astype(BF16)
                send_ref[head_place(head), 2] = swap_halves(second).astype(BF16)


def qkv_forward(x, gain, shift, w, bias, groups):
    micro, rows, _ = x.shape
    return pl.pallas_call(
        qkv_kernel,
        out_shape=(
            jax.ShapeDtypeStruct((micro * rows, D), BF16),
            jax.ShapeDtypeStruct((groups, 3, rows, LANES), BF16),
        ),
        in_specs=[whole()] * 5,
        out_specs=(whole(), whole()),
        compiler_params=params_of(48),
        name="qkv_forward",
    )(x, gain, shift, w, bias)


def half_mask(low_half):
    lane = lax.broadcasted_iota(jnp.int32, (1, LANES), 1)
    keep = (lane < HEAD_DIM) if low_half else (lane >= HEAD_DIM)
    return jnp.where(keep, 1.0, 0.0).astype(BF16)


def inner_slots(pick, block, blocks):
    ids, bias = picked_slots([pick(block, number) for number in range(RANDOM)], block, blocks)
    edge = (block == 0) | (block == blocks - 1)
    ids[0] = jnp.maximum(ids[0], 0)
    ids[2] = jnp.minimum(ids[2], blocks - 1)
    return ids, bias + jnp.where(edge, NEGATIVE, 0.0).astype(F32)


def slots_of(table_ref, micro, block, blocks):
    picks = [table_ref[micro, block * RANDOM + number] for number in range(RANDOM)]
    return picked_slots(picks, block, blocks)


def picked_slots(picks, block, blocks):
    last = blocks - 1
    ids = [block - 1, block, block + 1, 0, last] + picks
    dropped = [None, None, None, block == 1, block == last - 1]
    for number in range(RANDOM):
        pick = picks[number]
        bad = (jnp.abs(pick - block) <= 1) | (pick == 0) | (pick == last)
        for earlier in range(number):
            bad = bad | (pick == picks[earlier])
        dropped.append(bad)
    lane = lax.broadcasted_iota(jnp.int32, (1, LANES), 1)
    tiles = []
    for pair in range(len(ids) // 2):
        level = [
            0.0 if bad is None else jnp.where(bad, NEGATIVE, 0.0).astype(F32)
            for bad in dropped[2 * pair : 2 * pair + 2]
        ]
        tiles.append(jnp.where(lane < HEAD_DIM, level[0], level[1]))
    return ids, jnp.concatenate(tiles, axis=1)


def attend_kernel(table_ref, qkv_ref, out_ref, lse_ref, s_ref):
    groups, _, local, _, _ = qkv_ref.shape
    blocks = groups * local
    low = low_lanes(BLOCK)
    masks = [half_mask(True), half_mask(False)]

    def load(component, block):
        return qkv_ref[block // local, component, block % local]

    def sparse(block, carry):
        mixed, logs = [], []
        for micro in range(2):
            ids, bias = slots_of(table_ref, micro, block, blocks)
            keys = jnp.concatenate([load(1 + micro, spot) for spot in ids], axis=0)
            query = load(0, block) * masks[micro]
            scores = dot_rt(query, keys) + bias
            top = jnp.max(scores, axis=1, keepdims=True)
            powered = jnp.exp(scores - top)
            total = jnp.sum(powered, axis=1, keepdims=True)
            mixed.append(dot(powered.astype(BF16), keys) * (1.0 / total))
            logs.append(top + jnp.log(total))
        out_ref[block // local, block % local] = jnp.where(low, mixed[1], mixed[0]).astype(BF16)
        lse_ref[block] = jnp.where(low, logs[0], logs[1])
        return carry

    lax.fori_loop(1, blocks - 1, sparse, 0)

    spans = blocks // SPAN
    ends = (0, blocks - 1)
    results = []
    for micro in range(2):
        query = jnp.concatenate([load(0, end) for end in ends], axis=0) * masks[micro]

        def keys_at(span, micro=micro):
            return jnp.concatenate(
                [load(1 + micro, span * SPAN + spot) for spot in range(SPAN)], axis=0
            )

        def first_pass(span, top, query=query, keys_at=keys_at):
            scores = dot_rt(query, keys_at(span))
            s_ref[span] = scores
            return jnp.maximum(top, jnp.max(scores, axis=1, keepdims=True))

        top = lax.fori_loop(0, spans, first_pass, jnp.full((2 * BLOCK, 1), NEGATIVE, F32))

        def second_pass(span, carry, top=top, keys_at=keys_at):
            total, mixed = carry
            powered = jnp.exp(s_ref[span] - top)
            return (
                total + jnp.sum(powered, axis=1, keepdims=True),
                mixed + dot(powered.astype(BF16), keys_at(span)),
            )

        total, mixed = lax.fori_loop(
            0,
            spans,
            second_pass,
            (jnp.zeros((2 * BLOCK, 1), F32), jnp.zeros((2 * BLOCK, LANES), F32)),
        )
        results.append((mixed * (1.0 / total), top + jnp.log(total)))
    for place, end in enumerate(ends):
        rows = slice(place * BLOCK, (place + 1) * BLOCK)
        out_ref[end // local, end % local] = jnp.where(
            low, results[1][0][rows], results[0][0][rows]
        ).astype(BF16)
        lse_ref[end] = jnp.where(low, results[0][1][rows], results[1][1][rows])


def attention_forward(table, qkv):
    groups, _, local, _, _ = qkv.shape
    blocks = groups * local
    return pl.pallas_call(
        attend_kernel,
        out_shape=(
            jax.ShapeDtypeStruct((groups, local, BLOCK, LANES), BF16),
            jax.ShapeDtypeStruct((blocks, BLOCK, LANES), F32),
        ),
        in_specs=[whole(pltpu.SMEM), whole()],
        out_specs=(whole(), whole()),
        scratch_shapes=[VMEM((blocks // SPAN, 2 * BLOCK, SPAN * BLOCK), F32)],
        compiler_params=params_of(48),
        name="attention_forward",
    )(table, qkv)


def attend_back_kernel(table_ref, qkv_ref, grad_ref, lse_ref, out_ref, sums_ref, p_ref, dp_ref):
    groups, _, local, _, _ = qkv_ref.shape
    blocks = groups * local
    low = low_lanes(BLOCK)
    masks = [half_mask(True), half_mask(False)]

    def load(component, block):
        return qkv_ref[block // local, component, block % local]

    def load_grad(block):
        return grad_ref[block // local, block % local]

    def clear(block, carry):
        for micro in range(2):
            sums_ref[micro, block] = jnp.zeros((BLOCK, LANES), F32)
        return carry

    lax.fori_loop(0, blocks, clear, 0)

    def sparse(block, carry):
        grads = []
        for micro in range(2):
            ids, bias = slots_of(table_ref, micro, block, blocks)
            keys = jnp.concatenate([load(1 + micro, spot) for spot in ids], axis=0)
            both = jnp.concatenate(
                [load(0, block) * masks[micro], load_grad(block) * masks[1 - micro]], axis=0
            )
            products = dot_rt(both, keys)
            logs = lse_ref[block][:, micro * HEAD_DIM : micro * HEAD_DIM + 1]
            weights = jnp.exp(products[:BLOCK] + bias - logs)
            grad_weights = products[BLOCK:]
            delta = jnp.sum(weights * grad_weights, axis=1, keepdims=True)
            grad_scores = weights * (grad_weights - delta)
            stacked = jnp.concatenate([grad_scores, weights], axis=0).astype(BF16)
            grads.append(dot(stacked[:BLOCK], keys))
            shares = dot_lt(stacked, both)
            for place, spot in enumerate(ids):
                sums_ref[micro, spot] += shares[place * BLOCK : (place + 1) * BLOCK]
        out_ref[block // local, 0, block % local] = (
            jnp.where(low, grads[0], grads[1]) * SCALE
        ).astype(BF16)
        return carry

    lax.fori_loop(1, blocks - 1, sparse, 0)

    spans = blocks // SPAN
    ends = (0, blocks - 1)
    results = []
    for micro in range(2):
        query = jnp.concatenate([load(0, end) for end in ends], axis=0) * masks[micro]
        grad = jnp.concatenate([load_grad(end) for end in ends], axis=0) * masks[1 - micro]
        both = jnp.concatenate([query, grad], axis=0)
        logs = jnp.concatenate(
            [lse_ref[end][:, micro * HEAD_DIM : micro * HEAD_DIM + 1] for end in ends], axis=0
        )

        def keys_at(span, micro=micro):
            return jnp.concatenate(
                [load(1 + micro, span * SPAN + spot) for spot in range(SPAN)], axis=0
            )

        def first_pass(span, delta, both=both, logs=logs, keys_at=keys_at):
            products = dot_rt(both, keys_at(span))
            weights = jnp.exp(products[: 2 * BLOCK] - logs)
            grad_weights = products[2 * BLOCK :]
            p_ref[span] = weights
            dp_ref[span] = grad_weights
            return delta + jnp.sum(weights * grad_weights, axis=1, keepdims=True)

        delta = lax.fori_loop(0, spans, first_pass, jnp.zeros((2 * BLOCK, 1), F32))

        def second_pass(span, carry, delta=delta, both=both, keys_at=keys_at, micro=micro):
            weights = p_ref[span]
            grad_scores = weights * (dp_ref[span] - delta)
            stacked = jnp.concatenate([grad_scores, weights], axis=0).astype(BF16)
            shares = dot_lt(stacked, both)
            for spot in range(SPAN):
                sums_ref[micro, span * SPAN + spot] += shares[spot * BLOCK : (spot + 1) * BLOCK]
            return carry + dot(stacked[: 2 * BLOCK], keys_at(span))

        results.append(
            lax.fori_loop(0, spans, second_pass, jnp.zeros((2 * BLOCK, LANES), F32))
        )
    for place, end in enumerate(ends):
        rows = slice(place * BLOCK, (place + 1) * BLOCK)
        out_ref[end // local, 0, end % local] = (
            jnp.where(low, results[0][rows], results[1][rows]) * SCALE
        ).astype(BF16)

    def finish(block, carry):
        for micro in range(2):
            out_ref[block // local, 1 + micro, block % local] = sums_ref[micro, block].astype(BF16)
        return carry

    lax.fori_loop(0, blocks, finish, 0)


def attention_backward(table, qkv, grad, lse):
    groups, _, local, _, _ = qkv.shape
    blocks = groups * local
    spans = VMEM((blocks // SPAN, 2 * BLOCK, SPAN * BLOCK), F32)
    return pl.pallas_call(
        attend_back_kernel,
        out_shape=jax.ShapeDtypeStruct(qkv.shape, BF16),
        in_specs=[whole(pltpu.SMEM), whole(), whole(), whole()],
        out_specs=whole(),
        scratch_shapes=[VMEM((2, blocks, BLOCK, LANES), F32), spans, spans],
        compiler_params=params_of(48),
        name="attention_backward",
    )(table, qkv, grad, lse)


def middle_kernel(
    mixed_in_ref,
    x_ref,
    dy_ref,
    w_out_ref,
    out_shift_ref,
    gain_ref,
    shift_ref,
    up_shift_ref,
    down_shift_ref,
    w_up_ref,
    w_down_ref,
    hidden_ref,
    send_ref,
    dres_ref,
    g_out_ref,
    g_up_ref,
    g_down_ref,
    g_up_bias_ref,
    g_small_ref,
    mixed_ref,
    residual_ref,
    second_ref,
    second_t_ref,
    total_ref,
    dsecond_ref,
):
    micro, rows, _ = x_ref.shape
    step = pl.program_id(0)
    low = low_lanes(rows)

    @pl.when(step == 0)
    def _():
        for pair in range(HEADS // 2):
            even = mixed_in_ref[head_place(2 * pair)].astype(F32)
            odd = mixed_in_ref[head_place(2 * pair + 1)].astype(F32)
            columns = slice(pair * LANES, (pair + 1) * LANES)
            mixed_ref[:rows, columns] = jnp.where(low, swap_halves(even), odd).astype(BF16)
            mixed_ref[rows:, columns] = jnp.where(low, even, swap_halves(odd)).astype(BF16)
        residual = x_ref[...].reshape(micro * rows, D).astype(F32) + (
            dot(mixed_ref[...], w_out_ref[...]) + out_shift_ref[...]
        )
        residual_ref[...] = residual
        normal, _ = norm_parts(residual)
        second = normal * gain_ref[...] + shift_ref[...]
        second_ref[...] = second.astype(BF16)
        second_t_ref[...] = second.T.astype(BF16)
        total_ref[...] = jnp.zeros_like(total_ref)
        dsecond_ref[...] = jnp.zeros_like(dsecond_ref)

    upper = dot(second_ref[...], w_up_ref[...]) + up_shift_ref[...]
    factor = 0.7978845608028654
    square = upper * upper
    bent = jnp.tanh(factor * (upper + 0.044715 * (upper * square)))
    half = 0.5 * (1.0 + bent)
    active = (upper * half).astype(BF16)
    slope = half + 0.5 * upper * (1.0 - bent * bent) * (
        factor + (3.0 * 0.044715 * factor) * square
    )
    dy = dy_ref[...]
    total_ref[...] += dot(active, w_down_ref[...])
    g_down_ref[...] = dot_lt(active, dy).astype(g_down_ref.dtype)
    dupper = (dot_rt(dy, w_down_ref[...]) * slope).astype(BF16)
    g_up_bias_ref[...] = jnp.sum(dupper.astype(F32), axis=0, keepdims=True)
    g_up_ref[...] = dot(second_t_ref[...], dupper).astype(g_up_ref.dtype)
    dsecond_ref[...] += dot_rt(dupper, w_up_ref[...])

    @pl.when(step == pl.num_programs(0) - 1)
    def _():
        residual = residual_ref[...]
        hidden_ref[...] = (
            (residual + (total_ref[...] + down_shift_ref[...])).astype(BF16).reshape(x_ref.shape)
        )
        normal, inverse = norm_parts(residual)
        dsecond = dsecond_ref[...]
        grad_out = dy_ref[...].astype(F32)
        g_small_ref[0:1] = jnp.sum(dsecond * normal, axis=0, keepdims=True)
        g_small_ref[1:2] = jnp.sum(dsecond, axis=0, keepdims=True)
        g_small_ref[2:3] = jnp.sum(grad_out, axis=0, keepdims=True)
        dres = grad_out + norm_pull(dsecond, normal, inverse, gain_ref[...])
        dres_ref[...] = dres
        branch = dres.astype(BF16)
        g_small_ref[3:4] = jnp.sum(branch.astype(F32), axis=0, keepdims=True)
        g_out_ref[...] = dot_lt(mixed_ref[...], branch).astype(g_out_ref.dtype)
        dmixed = dot_rt(branch, w_out_ref[...])
        for pair in range(HEADS // 2):
            part = dmixed[:, pair * LANES : (pair + 1) * LANES]
            first, last = part[:rows], part[rows:]
            even = jnp.where(low, last, swap_halves(first))
            odd = jnp.where(low, swap_halves(last), first)
            send_ref[head_place(2 * pair)] = even.astype(BF16)
            send_ref[head_place(2 * pair + 1)] = odd.astype(BF16)


def middle(mixed_in, x, dy, w_out, out_shift, gain, shift, up_shift, down_shift, w_up, w_down, kind):
    micro, rows, _ = x.shape
    tokens = micro * rows
    groups = mixed_in.shape[0]

    def fixed(shape):
        return pl.BlockSpec(shape, lambda step: (0,) * len(shape))

    vector = fixed((1, D))
    steps = FF // CHUNK
    return pl.pallas_call(
        middle_kernel,
        grid=(steps,),
        out_shape=(
            jax.ShapeDtypeStruct(x.shape, BF16),
            jax.ShapeDtypeStruct((groups, rows, LANES), BF16),
            jax.ShapeDtypeStruct((tokens, D), F32),
            jax.ShapeDtypeStruct((D, D), kind),
            jax.ShapeDtypeStruct((D, FF), kind),
            jax.ShapeDtypeStruct((FF, D), kind),
            jax.ShapeDtypeStruct((1, FF), F32),
            jax.ShapeDtypeStruct((4, D), F32),
        ),
        in_specs=[
            fixed(mixed_in.shape),
            fixed(x.shape),
            fixed((tokens, D)),
            fixed((D, D)),
            vector,
            vector,
            vector,
            pl.BlockSpec((1, CHUNK), lambda step: (0, step)),
            vector,
            pl.BlockSpec((D, CHUNK), lambda step: (0, step)),
            pl.BlockSpec((CHUNK, D), lambda step: (step, 0)),
        ],
        out_specs=(
            fixed(x.shape),
            fixed((groups, rows, LANES)),
            fixed((tokens, D)),
            fixed((D, D)),
            pl.BlockSpec((D, CHUNK), lambda step: (0, step)),
            pl.BlockSpec((CHUNK, D), lambda step: (step, 0)),
            pl.BlockSpec((1, CHUNK), lambda step: (0, step)),
            fixed((4, D)),
        ),
        scratch_shapes=[
            VMEM((tokens, D), BF16),
            VMEM((tokens, D), F32),
            VMEM((tokens, D), BF16),
            VMEM((D, tokens), BF16),
            VMEM((tokens, D), F32),
            VMEM((tokens, D), F32),
        ],
        compiler_params=params_of(56),
        name="middle",
    )(mixed_in, x, dy, w_out, out_shift, gain, shift, up_shift, down_shift, w_up, w_down)


def qkv_back_kernel(
    recv_ref,
    normed_ref,
    x_ref,
    dres_ref,
    gain_ref,
    w_ref,
    grad_ref,
    g_qkv_ref,
    g_bias_ref,
    g_small_ref,
    packed_ref,
    normed_t_ref,
    dnormed_ref,
):
    micro, rows, _ = x_ref.shape
    step = pl.program_id(0)
    low = low_lanes(rows)

    @pl.when(step == 0)
    def _():
        for pair in range(HEADS // 2):
            even = recv_ref[head_place(2 * pair), 0].astype(F32)
            odd = recv_ref[head_place(2 * pair + 1), 0].astype(F32)
            spot, columns = pair // 2, slice((pair % 2) * LANES, (pair % 2 + 1) * LANES)
            packed_ref[spot, :rows, columns] = jnp.where(low, even, swap_halves(odd)).astype(BF16)
            packed_ref[spot, rows:, columns] = jnp.where(low, swap_halves(even), odd).astype(BF16)
        for head in range(HEADS):
            spot = D // CHUNK + head // 2
            columns = slice((head % 2) * LANES, (head % 2 + 1) * LANES)
            packed_ref[spot, :rows, columns] = recv_ref[head_place(head), 1]
            packed_ref[spot, rows:, columns] = swap_halves(
                recv_ref[head_place(head), 2].astype(F32)
            ).astype(BF16)
        normed_t_ref[...] = normed_ref[...].astype(F32).T.astype(BF16)
        dnormed_ref[...] = jnp.zeros_like(dnormed_ref)

    packed = packed_ref[step]
    g_bias_ref[...] = jnp.sum(packed.astype(F32), axis=0, keepdims=True)
    g_qkv_ref[...] = dot(normed_t_ref[...], packed).astype(g_qkv_ref.dtype)
    dnormed_ref[...] += dot_rt(packed, w_ref[...])

    @pl.when(step == pl.num_programs(0) - 1)
    def _():
        normal, inverse = norm_parts(x_ref[...].reshape(micro * rows, D).astype(F32))
        dnormed = dnormed_ref[...]
        g_small_ref[0:1] = jnp.sum(dnormed * normal, axis=0, keepdims=True)
        g_small_ref[1:2] = jnp.sum(dnormed, axis=0, keepdims=True)
        grad = dres_ref[...] + norm_pull(dnormed, normal, inverse, gain_ref[...])
        grad_ref[...] = grad.reshape(x_ref.shape)


def qkv_backward(recv, normed, x, dres, gain, w, kind):
    micro, rows, _ = x.shape
    tokens = micro * rows

    def fixed(shape):
        return pl.BlockSpec(shape, lambda step: (0,) * len(shape))

    steps = 3 * D // CHUNK
    return pl.pallas_call(
        qkv_back_kernel,
        grid=(steps,),
        out_shape=(
            jax.ShapeDtypeStruct(x.shape, F32),
            jax.ShapeDtypeStruct((D, 3 * D), kind),
            jax.ShapeDtypeStruct((1, 3 * D), F32),
            jax.ShapeDtypeStruct((2, D), F32),
        ),
        in_specs=[
            fixed(recv.shape),
            fixed((tokens, D)),
            fixed(x.shape),
            fixed((tokens, D)),
            fixed((1, D)),
            pl.BlockSpec((D, CHUNK), lambda step: (0, step)),
        ],
        out_specs=(
            fixed(x.shape),
            pl.BlockSpec((D, CHUNK), lambda step: (0, step)),
            pl.BlockSpec((1, CHUNK), lambda step: (0, step)),
            fixed((2, D)),
        ),
        scratch_shapes=[
            VMEM((steps, tokens, CHUNK), BF16),
            VMEM((D, tokens), BF16),
            VMEM((tokens, D), F32),
        ],
        compiler_params=params_of(56),
        name="qkv_backward",
    )(recv, normed, x, dres, gain, w)


AXES = ("gx", "gy")


def gather(array):
    return lax.all_gather(array, AXES, axis=0, tiled=True)


def scatter(array):
    return lax.psum_scatter(array, AXES, scatter_dimension=0, tiled=True)


def exchange(array):
    return lax.all_to_all(array, "gy", 0, 0, tiled=True)


def by_heads(w_qkv):
    rows = w_qkv.shape[0]
    sides = w_qkv[:, D:].reshape(rows, 2, HEADS, HEAD_DIM)
    return jnp.concatenate([w_qkv[:, :D], jnp.swapaxes(sides, 1, 2).reshape(rows, 2 * D)], axis=1)


def by_parts(w_qkv):
    rows = w_qkv.shape[0]
    sides = w_qkv[:, D:].reshape(rows, HEADS, 2, HEAD_DIM)
    return jnp.concatenate([w_qkv[:, :D], jnp.swapaxes(sides, 1, 2).reshape(rows, 2 * D)], axis=1)


def general_shards(
    hidden_in,
    rand_table,
    norm1_gain,
    norm1_bias,
    w_qkv,
    query_bias,
    value_bias,
    w_out,
    out_bias,
    norm2_gain,
    norm2_bias,
    w_up,
    up_bias,
    w_down,
    down_bias,
    cotangent,
):
    micro, rows, _ = hidden_in.shape
    groups = lax.axis_size("gy")
    local = rows // BLOCK
    own = norm1_gain.shape[0]

    vectors = jnp.concatenate(
        [
            norm1_gain,
            norm1_bias,
            query_bias,
            value_bias,
            out_bias,
            norm2_gain,
            norm2_bias,
            down_bias,
            up_bias,
        ]
    )
    table = lax.all_gather(rand_table, "gy", axis=1, tiled=True)
    table = table.reshape(micro, groups * local * RANDOM)
    vectors = gather(vectors[None]).astype(F32)
    gain_one, shift_one, query_shift, value_shift, out_shift, gain_two, shift_two, down_shift = (
        vectors[:, number * own : (number + 1) * own].reshape(1, D) for number in range(8)
    )
    up_shift = vectors[:, 8 * own :].reshape(1, FF)
    w_qkv_full = gather(by_heads(w_qkv))
    w_out_full, w_up_full, w_down_full = gather(w_out), gather(w_up), gather(w_down)
    packed_bias = by_heads(
        jnp.concatenate([query_shift, jnp.zeros_like(query_shift), value_shift], axis=1)
    )

    normed, send = qkv_forward(hidden_in, gain_one, shift_one, w_qkv_full, packed_bias, groups)
    qkv = exchange(send).reshape(groups, 3, local, BLOCK, LANES)
    mixed, lse = attention_forward(table, qkv)
    mixed_back = exchange(mixed.reshape(groups, rows, LANES))
    hidden_out, grad_send, dres, g_out, g_up, g_down, g_up_bias, g_mid = middle(
        mixed_back,
        hidden_in,
        cotangent.reshape(micro * rows, D),
        w_out_full,
        out_shift,
        gain_two,
        shift_two,
        up_shift,
        down_shift,
        w_up_full,
        w_down_full,
        F32,
    )
    grad_mixed = exchange(grad_send).reshape(groups, local, BLOCK, LANES)
    dqkv = attention_backward(table, qkv, grad_mixed, lse)
    dqkv_back = exchange(dqkv.reshape(groups, 3, rows, LANES))
    grad_hidden, g_qkv, g_packed, g_first = qkv_backward(
        dqkv_back, normed, hidden_in, dres, gain_one, w_qkv_full, F32
    )

    g_packed = by_parts(g_packed)
    small = [
        g_first[0],
        g_first[1],
        g_packed[0, :D],
        g_packed[0, 2 * D :],
        g_mid[3],
        g_mid[0],
        g_mid[1],
        g_mid[2],
    ]
    ranks = D // own
    small = jnp.concatenate(
        [item.reshape(ranks, own) for item in small] + [g_up_bias.reshape(ranks, 4 * own)], axis=1
    )
    small = scatter(small)[0]
    parts = [small[number * own : (number + 1) * own] for number in range(8)]
    return (
        hidden_out,
        grad_hidden,
        parts[0],
        parts[1],
        by_parts(scatter(g_qkv)),
        parts[2],
        parts[3],
        scatter(g_out),
        parts[4],
        parts[5],
        parts[6],
        scatter(g_up),
        small[8 * own :],
        scatter(g_down),
        parts[7],
    )


MESH = pl.DeviceIdType.MESH
ANY = pl.ANY
PLANES = 4
SPOTS = 4
PIECES = 2
RANKS = 2 * PLANES * SPOTS
TILES = 3 * D // LANES
HALF_TILES = TILES // 2
QUERY_ORDER = (0, 2, 3, 5, 6, 8, 9, 11, 1, 4, 7, 10)


def column_order():
    order = [("q", head) for head in QUERY_ORDER]
    for spot in range(SPOTS):
        for place in (2 * 3 * spot, 2 * 3 * spot + 2):
            order += [("k", place // 2), ("v", place // 2)]
        order += [("v", 3 * spot + 2), ("k", 3 * spot + 2)]
    return order


def natural_block(entry):
    return "qkv".index(entry[0]) * HEADS + entry[1]


def take_blocks(array, order):
    parts = []
    start = 0
    while start < len(order):
        stop = start + 1
        while stop < len(order) and order[stop] == order[stop - 1] + 1:
            stop += 1
        parts.append(array[..., order[start] * HEAD_DIM : (order[start] + stop - start) * HEAD_DIM])
        start = stop
    return jnp.concatenate(parts, axis=-1)


def flip(value, bits):
    if bits == 0:
        return value
    if bits == 1:
        return value + 1 - 2 * lax.rem(value, 2)
    if bits == 2:
        return value + 2 - 4 * lax.div(value, 2)
    return 3 - value


def place_here():
    core, rank = lax.axis_index("gx"), lax.axis_index("gy")
    return core, lax.div(rank, SPOTS), lax.rem(rank, SPOTS)


def rank_of(plane, spot):
    return plane * SPOTS + spot


def greet(partners):
    barrier = pltpu.get_barrier_semaphore()
    for partner in partners:
        pl.semaphore_signal(barrier, inc=1, device_id=partner, device_id_type=MESH)
    pl.semaphore_wait(barrier, len(partners))


def remote(source, target, send_sem, recv_sem, device):
    return pltpu.make_async_remote_copy(
        src_ref=source,
        dst_ref=target,
        send_sem=send_sem,
        recv_sem=recv_sem,
        device_id=device,
        device_id_type=MESH,
    )


def column_partners(core, plane, spot):
    partners = [(1 - core, rank_of(plane, spot))]
    for bits in range(1, PLANES):
        for other in (core, 1 - core):
            partners.append((other, rank_of(flip(plane, bits), spot)))
    return partners


def all_partners(core, plane, spot):
    return column_partners(core, plane, spot) + [
        (core, rank_of(plane, flip(spot, 1))),
        (core, rank_of(plane, flip(spot, 2))),
    ]


def to_planes(source, target, send_sem, recv_sem, local_sem):
    core, plane, spot = place_here()
    half, odd = lax.div(plane, 2), lax.rem(plane, 2)
    sends, keeps = [], []
    for micro in range(2):
        goal = 2 * micro + core
        here = (goal == plane) & (half == core)
        send = remote(
            source.at[micro],
            target.at[odd],
            send_sem.at[micro],
            recv_sem.at[odd],
            (half, rank_of(goal, spot)),
        )
        keep = pltpu.make_async_copy(source.at[micro], target.at[odd], local_sem.at[micro])

        @pl.when(jnp.logical_not(here))
        def _(send=send):
            send.start()

        @pl.when(here)
        def _(keep=keep):
            keep.start()

        sends.append((here, send))
        keeps.append((here, keep))

    def finish():
        for piece in range(PIECES):
            mine = (odd == core) & (plane == 2 * core + piece)
            arrival = remote(
                source.at[0],
                target.at[piece],
                send_sem.at[0],
                recv_sem.at[piece],
                (core, rank_of(plane, spot)),
            )

            @pl.when(jnp.logical_not(mine))
            def _(arrival=arrival):
                arrival.wait_recv()

        for (here, send), (_, keep) in zip(sends, keeps):

            @pl.when(jnp.logical_not(here))
            def _(send=send):
                send.wait_send()

            @pl.when(here)
            def _(keep=keep):
                keep.wait()

    return finish


def from_planes(source, target, send_sem, recv_sem, local_sem):
    core, plane, spot = place_here()
    micro, odd = lax.div(plane, 2), lax.rem(plane, 2)
    sends, keeps = [], []
    for piece in range(PIECES):
        goal = 2 * core + piece
        here = (goal == plane) & (odd == core)
        send = remote(
            source.at[piece],
            target.at[micro],
            send_sem.at[piece],
            recv_sem.at[micro],
            (odd, rank_of(goal, spot)),
        )
        keep = pltpu.make_async_copy(source.at[piece], target.at[micro], local_sem.at[piece])

        @pl.when(jnp.logical_not(here))
        def _(send=send):
            send.start()

        @pl.when(here)
        def _(keep=keep):
            keep.start()

        sends.append((here, send))
        keeps.append((here, keep))

    def finish():
        for number in range(2):
            mine = (2 * number + core == plane) & (micro == core)
            arrival = remote(
                source.at[0],
                target.at[number],
                send_sem.at[0],
                recv_sem.at[number],
                (core, rank_of(plane, spot)),
            )

            @pl.when(jnp.logical_not(mine))
            def _(arrival=arrival):
                arrival.wait_recv()

        for (here, send), (_, keep) in zip(sends, keeps):

            @pl.when(jnp.logical_not(here))
            def _(send=send):
                send.wait_send()

            @pl.when(here)
            def _(keep=keep):
                keep.wait()

    return finish


class Gather:
    SENDS = 31

    def __init__(self, source, target, send_sem, recv_sem, local_sem):
        self.source, self.target = source, target
        self.send_sem, self.recv_sem = send_sem, recv_sem
        self.core, self.plane, self.spot = place_here()
        self.sends = []
        self.own = pltpu.make_async_copy(
            source, target.at[self.core, self.plane, self.spot], local_sem
        )
        self.own.start()

    def send(self, source, plane, spot, device):
        copy = remote(
            source,
            self.target.at[self.core, plane, spot],
            self.send_sem.at[len(self.sends)],
            self.recv_sem.at[self.core, plane, spot],
            device,
        )
        copy.start()
        self.sends.append(copy)

    def arrive(self, core, plane, spot):
        shard = self.target.at[core, plane, spot]
        remote(
            shard,
            shard,
            self.send_sem.at[0],
            self.recv_sem.at[core, plane, spot],
            (self.core, rank_of(self.plane, self.spot)),
        ).wait_recv()

    def neighbour(self, bits):
        return (self.core, rank_of(self.plane, flip(self.spot, bits)))

    def sibling(self):
        return (1 - self.core, rank_of(self.plane, self.spot))

    def start(self):
        for bits in range(1, PLANES):
            goal = (self.core, rank_of(flip(self.plane, bits), self.spot))
            self.send(self.source, self.plane, self.spot, goal)
        for goal in (self.neighbour(1), self.neighbour(2), self.sibling()):
            self.send(self.source, self.plane, self.spot, goal)

    def column(self):
        for bits in range(1, PLANES):
            plane = flip(self.plane, bits)
            self.arrive(self.core, plane, self.spot)
            shard = self.target.at[self.core, plane, self.spot]
            for goal in (self.neighbour(1), self.neighbour(2), self.sibling()):
                self.send(shard, plane, self.spot, goal)

    def across(self):
        for bits in range(PLANES):
            plane = flip(self.plane, bits)
            for side in (1, 2):
                spot = flip(self.spot, side)
                self.arrive(self.core, plane, spot)
                shard = self.target.at[self.core, plane, spot]
                if (side == 1) == (bits < 2):
                    self.send(shard, plane, spot, self.neighbour(3 - side))
                self.send(shard, plane, spot, self.sibling())

    def corner(self):
        spot = flip(self.spot, 3)
        for bits in range(PLANES):
            plane = flip(self.plane, bits)
            self.arrive(self.core, plane, spot)
            self.send(self.target.at[self.core, plane, spot], plane, spot, self.sibling())

    def finish(self):
        for bits in range(PLANES):
            for side in range(SPOTS):
                self.arrive(1 - self.core, flip(self.plane, bits), flip(self.spot, side))
        self.own.wait()
        for copy in self.sends:
            copy.wait_send()


def settle(shards_ref, plan):
    rows = shards_ref.shape[3] // 2

    def pair(number, carry):
        core, plane, side = (
            lax.div(number, 2 * PLANES),
            lax.rem(lax.div(number, 2), PLANES),
            lax.rem(number, 2),
        )
        goal = pl.ds(pl.multiple_of(number * 2 * rows, 16), 2 * rows)
        for tile, out_ref, (left, right) in plan:
            columns = slice(tile * LANES, (tile + 1) * LANES)
            first = shards_ref[core, plane, 2 * side, :, columns].astype(F32)
            second = shards_ref[core, plane, 2 * side + 1, :, columns].astype(F32)
            out_ref[goal, left * LANES : (left + 1) * LANES] = jnp.concatenate(
                [first[:rows], second[:rows]], axis=0
            ).astype(BF16)
            out_ref[goal, right * LANES : (right + 1) * LANES] = jnp.concatenate(
                [first[rows:], second[rows:]], axis=0
            ).astype(BF16)
        return carry

    lax.fori_loop(0, RANKS // 2, pair, 0)


def alternate(tile):
    return 2 * tile, 2 * tile + 1


def plane_partners(core, plane, spot):
    partners = []
    for other in (core, 1 - core):
        for side in range(SPOTS):
            if other is core and side == 0:
                continue
            partners.append((other, rank_of(plane, flip(spot, side))))
    return partners


def both_partners(core, plane, spot):
    return plane_partners(core, plane, spot) + column_partners(core, plane, spot)[1:]


def exchange_sems(recv_shape):
    return [
        pltpu.SemaphoreType.DMA((14,)),
        pltpu.SemaphoreType.DMA(recv_shape),
        pltpu.SemaphoreType.DMA((PIECES,)),
    ]


def sort_entries(table, sorted_ref, entries):
    count = table.shape[1]
    core = lax.axis_index("gx")
    lane = lax.broadcasted_iota(jnp.int32, (count, count), 1)
    row = lax.broadcasted_iota(jnp.int32, (count, count), 0).astype(F32)
    everything = jnp.broadcast_to(table, (count, count))
    half = entries // 2
    inside = (lane >= core * half) & (lane < (core + 1) * half)
    lane = lane.astype(F32)
    for number, along in enumerate((everything, jnp.where(inside, everything, 2.0 * LANES))):
        down = along.T
        before = (along < down) | ((along == down) & (lane < row))
        rank = jnp.sum(jnp.where(before, 1.0, 0.0), axis=1, keepdims=True)
        order = jnp.sum(jnp.where(rank == lane, row, 0.0), axis=0, keepdims=True)
        upto = jnp.sum(jnp.where(down <= lane, 1.0, 0.0), axis=0, keepdims=True)
        sorted_ref[2 * number : 2 * number + 1] = order.astype(jnp.int32)
        sorted_ref[2 * number + 1 : 2 * number + 2] = upto.astype(jnp.int32)


class Outward:
    def __init__(self, source, target, send_sem, recv_sem, local_sem):
        self.target, self.recv_sem, self.send_sem = target, recv_sem, send_sem
        self.core, self.plane, self.spot = place_here()
        self.sends, self.keeps = [], []
        for side in (3, 1, 2, 0):
            for other in (self.core, 1 - self.core):
                goal = flip(self.spot, side)
                for piece in range(PIECES):
                    start = source.at[other, goal, piece]
                    stop = target.at[2 * self.core + piece, self.spot]
                    if side == 0 and other is self.core:
                        copy = pltpu.make_async_copy(start, stop, local_sem.at[piece])
                        self.keeps.append(copy)
                    else:
                        copy = remote(
                            start,
                            stop,
                            send_sem.at[len(self.sends)],
                            recv_sem.at[2 * self.core + piece, self.spot],
                            (other, rank_of(self.plane, goal)),
                        )
                        self.sends.append(copy)
                    copy.start()

    def arrive(self, side):
        for other in (self.core, 1 - self.core):
            if side == 0 and other is self.core:
                for copy in self.keeps:
                    copy.wait()
                continue
            for piece in range(PIECES):
                place = (2 * other + piece, flip(self.spot, side))
                remote(
                    self.target.at[place],
                    self.target.at[place],
                    self.send_sem.at[0],
                    self.recv_sem.at[place],
                    (self.core, rank_of(self.plane, self.spot)),
                ).wait_recv()

    def finish(self):
        for copy in self.sends:
            copy.wait_send()


def inward_targets(core, spot):
    for side in (3, 1, 2, 0):
        for other in (core, 1 - core):
            yield side, other, flip(spot, side), side == 0 and other is core


class Inward:
    def __init__(self, source, target, send_sem, recv_sem, local_sem):
        self.source, self.target = source, target
        self.send_sem, self.recv_sem, self.local_sem = send_sem, recv_sem, local_sem
        self.core, self.plane, self.spot = place_here()
        self.sends, self.keeps = [], []

    def send(self, other, goal, stays, piece, part, parts):
        source = self.source.at[2 * other + piece, goal, parts]
        target = self.target.at[self.core, self.spot, piece, parts]
        if stays:
            copy = pltpu.make_async_copy(source, target, self.local_sem.at[part, piece])
            self.keeps.append(copy)
        else:
            copy = remote(
                source,
                target,
                self.send_sem.at[len(self.sends)],
                self.recv_sem.at[self.core, self.spot, piece, part],
                (other, rank_of(self.plane, goal)),
            )
            self.sends.append(copy)
        copy.start()

    def finish(self, parts_of):
        for side, other, goal, stays in inward_targets(self.core, self.spot):
            if stays:
                continue
            for piece in range(PIECES):
                for part, parts in enumerate(parts_of[0 if other is self.core else 1]):
                    target = self.target.at[other, goal, piece, parts]
                    remote(
                        target,
                        target,
                        self.send_sem.at[0],
                        self.recv_sem.at[other, goal, piece, part],
                        (self.core, rank_of(self.plane, self.spot)),
                    ).wait_recv()
        for copy in self.sends:
            copy.wait_send()
        for copy in self.keeps:
            copy.wait()


KEYS_A, QUERIES, KEYS_B = range(3)


def plane_attend_back_kernel(*refs):
    table_ref, sorted_ref, qk_ref, shared_ref, grad_source_ref, lse_ref, hidden_ref = refs[:7]
    sources, half_up_ref, half_down_ref, refs = refs[7:10], refs[10], refs[11], refs[12:]
    sources = list(sources[:2]) + [sources[2].at[number] for number in range(LATE)]
    back_ref, hidden_out_ref, t_out_ref, t_up_ref, t_down_ref = refs[:5]
    count = 2 + LATE
    refs = refs[5:]
    buffers, mines, refs = refs[: 3 * count], refs[3 * count : 4 * count], refs[4 * count :]
    part_out_ref, part_up_ref, part_down_ref, far_out_ref, far_up_ref, far_down_ref = refs[:6]
    grad_ref, out_ref, sums_ref, shares_ref, walked_ref, sibling_ref = refs[6:12]
    scores_refs, refs = refs[12:16], refs[16:]
    reduce_send, reduce_recv, far_send, far_recv, load_sem = refs[:5]
    grad_sems, back_sems, move_sems, sibling_sems = refs[5:8], refs[8:11], refs[11:14], refs[14:16]

    local = qk_ref.shape[3]
    groups = PLANES * SPOTS
    blocks = groups * local
    core, plane, spot = place_here()
    low = low_lanes(BLOCK)
    masks = [half_mask(True), half_mask(False)]

    greet(both_partners(core, plane, spot))
    grads = Outward(grad_source_ref, grad_ref, *grad_sems)
    reduces = [
        SpotReduce(
            source,
            *buffers[3 * number : 3 * number + 3],
            reduce_send.at[number],
            reduce_recv.at[number],
            rows=FF // RANKS if number >= 2 else None,
            mine=mine,
        )
        for number, (source, mine) in enumerate(zip(sources, mines))
    ]
    ready = PER_STAGE * EARLY
    loads = [
        pltpu.make_async_copy(one.half(core), mine, load_sem.at[number])
        for number, (one, mine) in enumerate(zip(reduces, mines))
    ] + [
        pltpu.make_async_copy(half_up_ref, part_up_ref.at[0:ready], load_sem.at[count]),
        pltpu.make_async_copy(half_down_ref, part_down_ref.at[0:EARLY], load_sem.at[count + 1]),
    ]
    for one in reduces:
        one.start()
    for copy in loads:
        copy.start()
    finish_hidden = from_planes(hidden_ref, hidden_out_ref, *move_sems)

    def load(component, block):
        rank, number = lax.div(block, local), lax.rem(block, local)
        if component == 2:
            return shared_ref[lax.div(rank, SPOTS), lax.rem(rank, SPOTS), number]
        return qk_ref[lax.div(rank, SPOTS), lax.rem(rank, SPOTS), component, number]

    def load_grad(block):
        rank = lax.div(block, local)
        return grad_ref[lax.div(rank, SPOTS), lax.rem(rank, SPOTS), lax.rem(block, local)]

    def store(component, block, value):
        rank = lax.div(block, local)
        out_ref[
            lax.div(rank, SPOTS), lax.rem(rank, SPOTS), component, lax.rem(block, local)
        ] = value.astype(BF16)

    def stored(component, block):
        rank = lax.div(block, local)
        return out_ref[
            lax.div(rank, SPOTS), lax.rem(rank, SPOTS), component, lax.rem(block, local)
        ].astype(F32)

    nothing = jnp.zeros((BLOCK, LANES), F32)

    def clear(block, carry):
        for slot in range(2):
            sums_ref[slot, block] = nothing
        return carry

    lax.fori_loop(0, blocks, clear, 0)

    def picked(block, number):
        return table_ref[0, block * RANDOM + number]

    def one_block(block, slot):
        ids, bias = inner_slots(picked, block, blocks)
        keys = jnp.concatenate([load(1 + slot, number) for number in ids], axis=0)
        both = jnp.concatenate(
            [load(0, block) * masks[slot], load_grad(block) * masks[1 - slot]], axis=0
        )
        products = dot_rt(both, keys)
        logs = lse_ref[block][:, slot * HEAD_DIM : slot * HEAD_DIM + 1]
        weights = jnp.exp(products[:BLOCK] + bias - logs)
        grad_weights = products[BLOCK:]
        delta = jnp.sum(weights * grad_weights, axis=1, keepdims=True)
        grad_scores = weights * (grad_weights - delta)
        stacked = jnp.concatenate([grad_scores, weights], axis=0).astype(BF16)
        return dot(stacked[:BLOCK], keys), dot_lt(stacked, both)

    fixed = 5

    def rank_blocks(rank, slot):
        first = rank * local
        results = [one_block(first + number, slot) for number in range(local)]

        def share(number, place):
            return results[number][1][place * BLOCK : (place + 1) * BLOCK]

        for shift in range(-1, local + 1):
            parts = [
                share(number, shift - number + 1)
                for number in range(local)
                if 0 <= shift - number + 1 <= 2
            ]
            target = jnp.minimum(jnp.maximum(first + shift, 0), blocks - 1)
            sums_ref[slot, target] += functools.reduce(jnp.add, parts)
        for place, target in ((3, 0), (4, blocks - 1)):
            sums_ref[slot, target] += functools.reduce(
                jnp.add, [share(number, place) for number in range(local)]
            )
        for number in range(local):
            for pick in range(RANDOM):
                shares_ref[slot, (first + number) * RANDOM + pick] = share(number, fixed + pick)
        return [result[0] for result in results]

    def head_a(side):
        def body(number, carry):
            rank = number * SPOTS + flip(spot, side)
            for place, query in enumerate(rank_blocks(rank, 0)):
                store(QUERIES, rank * local + place, query * SCALE)
            return carry

        lax.fori_loop(0, PLANES, body, 0)

    def head_b(number, carry):
        rank = core * (groups // 2) + number
        for place, query in enumerate(rank_blocks(rank, 1)):
            block = rank * local + place
            store(QUERIES, block, jnp.where(low, stored(QUERIES, block), query * SCALE))
        return carry

    spans = blocks // SPAN
    ends = (0, blocks - 1)

    def dense(slot, p_ref, d_ref, numbers):
        both = jnp.concatenate(
            [load(0, number) * masks[slot] for number in numbers]
            + [load_grad(number) * masks[1 - slot] for number in numbers],
            axis=0,
        )
        rows = len(numbers) * BLOCK
        column = slot * HEAD_DIM
        logs = jnp.concatenate(
            [lse_ref[number][:, column : column + 1] for number in numbers], axis=0
        )

        def keys_at(span):
            return jnp.concatenate(
                [load(1 + slot, span * SPAN + number) for number in range(SPAN)], axis=0
            )

        def first_pass(span, delta):
            products = dot_rt(both, keys_at(span))
            weights = jnp.exp(products[:rows] - logs)
            grad_weights = products[rows:]
            p_ref[span] = weights
            d_ref[span] = grad_weights
            return delta + jnp.sum(weights * grad_weights, axis=1, keepdims=True)

        delta = lax.fori_loop(0, spans, first_pass, jnp.zeros((rows, 1), F32), unroll=2)

        def second_pass(span, total):
            weights = p_ref[span]
            grad_scores = weights * (d_ref[span] - delta)
            stacked = jnp.concatenate([grad_scores, weights], axis=0).astype(BF16)
            shares = dot_lt(stacked, both)
            for number in range(SPAN):
                sums_ref[slot, span * SPAN + number] += shares[
                    number * BLOCK : (number + 1) * BLOCK
                ]
            return total + dot(stacked[:rows], keys_at(span))

        total = lax.fori_loop(0, spans, second_pass, jnp.zeros((rows, LANES), F32), unroll=2)
        for place, number in enumerate(numbers):
            query = total[place * BLOCK : (place + 1) * BLOCK] * SCALE
            if slot == 1:
                query = jnp.where(low, stored(QUERIES, number), query)
            store(QUERIES, number, query)

    def walk(slot, length):
        def body(number, total):
            entry = sorted_ref[2 * slot, number]
            earlier = sorted_ref[2 * slot, jnp.maximum(number - 1, 0)]
            keep = jnp.where(table_ref[0, entry] == table_ref[0, earlier], 1.0, 0.0).astype(F32)
            total = total * keep + shares_ref[slot, entry]
            walked_ref[slot, number] = total.astype(BF16)
            return total

        lax.fori_loop(0, length, body, nothing, unroll=4)

    def close(slot, rank, component):
        def body(number, carry):
            block = rank * local + number
            stop = sorted_ref[2 * slot + 1, block]
            start = jnp.where(block == 0, 0, sorted_ref[2 * slot + 1, jnp.maximum(block - 1, 0)])
            some = jnp.where(stop > start, 1.0, 0.0).astype(F32)
            share = walked_ref[slot, jnp.maximum(stop - 1, 0)].astype(F32)
            store(component, block, sums_ref[slot, block] + share * some)
            return carry

        lax.fori_loop(0, local, body, 0, unroll=True)

    back = Inward(out_ref, back_ref, *back_sems)
    own_parts = (slice(0, 1), slice(1, 2), slice(2, 3))
    far_parts = (slice(0, 2),)

    for side in range(SPOTS):
        grads.arrive(side)
        head_a(side)
        if side == 0:
            for copy in loads:
                copy.wait()
            for one in reduces:
                one.corners()
        if side == 2:
            for one in reduces:
                one.sides()
    dense(0, scores_refs[0], scores_refs[1], ends)
    reduces[0].close(part_out_ref)
    reduces[1].close(part_up_ref.at[ready : PER_STAGE * STAGES])
    for number in range(LATE):
        reduces[2 + number].close(part_down_ref.at[EARLY + number])
    fars = []
    for bits in range(1, PLANES):
        goal = flip(plane, bits)
        for number, (source, target) in enumerate(
            (
                (part_out_ref.at[:, goal], far_out_ref),
                (part_up_ref.at[:, goal], far_up_ref),
                (part_down_ref.at[goal], far_down_ref),
            )
        ):
            copy = remote(
                source,
                target.at[bits - 1],
                far_send.at[number, bits - 1],
                far_recv.at[number, bits - 1],
                (core, rank_of(goal, spot)),
            )
            copy.start()
            fars.append(copy)
    walk(0, blocks * RANDOM)
    for side, other, goal, stays in inward_targets(core, spot):
        for piece in range(PIECES):
            close(0, (2 * other + piece) * SPOTS + goal, KEYS_A)
            if other is core:
                back.send(other, goal, stays, piece, 0, own_parts[0])
            else:
                back.send(other, goal, stays, piece, 0, far_parts[0])
    lax.fori_loop(0, groups // 2, head_b, 0)
    dense(1, scores_refs[2], scores_refs[3], (core * (blocks - 1),))
    for side, other, goal, stays in inward_targets(core, spot):
        if other is core:
            for piece in range(PIECES):
                back.send(other, goal, stays, piece, 1, own_parts[1])
    walk(1, blocks * RANDOM // 2)
    for number in range(PIECES):
        for goal in range(SPOTS):
            close(1, (2 * (1 - core) + number) * SPOTS + goal, KEYS_B)
    across = remote(
        out_ref.at[pl.ds(2 * (1 - core), PIECES), :, KEYS_B],
        sibling_ref,
        sibling_sems[0],
        sibling_sems[1],
        (1 - core, rank_of(plane, spot)),
    )
    across.start()
    for number in range(PIECES):
        for goal in range(SPOTS):
            close(1, (2 * core + number) * SPOTS + goal, KEYS_B)
    across.wait_recv()
    for side, other, goal, stays in inward_targets(core, spot):
        if other is core:
            for piece in range(PIECES):
                place = (2 * core + piece, goal, KEYS_B)
                out_ref[place] = (
                    out_ref[place].astype(F32) + sibling_ref[piece, goal].astype(F32)
                ).astype(BF16)
                back.send(other, goal, stays, piece, 2, own_parts[2])
    for copy in fars:
        copy.wait()

    def total(part, far, index):
        value = part.astype(F32)
        for bits in range(PLANES - 1):
            value = value + far[(bits,) + index].astype(F32)
        return value

    t_out_ref[...] = total(part_out_ref[0, plane], far_out_ref, (0,))

    def close_up(number, carry):
        t_up_ref[number] = total(part_up_ref[number, plane], far_up_ref, (number,))
        return carry

    lax.fori_loop(0, PER_STAGE * STAGES, close_up, 0)
    t_down_ref[...] = total(part_down_ref[plane], far_down_ref, ())
    finish_hidden()
    grads.finish()
    across.wait_send()
    back.finish((own_parts, far_parts))


def plane_attention_back(
    table, sorted_table, qk, shared, grad_source, lse, hidden, sources, half_up, half_down
):
    local = qk.shape[3]
    blocks = PLANES * SPOTS * local
    spans = blocks // SPAN
    shard, rows = D // RANKS, FF // RANKS
    up_count = PER_STAGE * STAGES
    up_tail, out_tail = (2 * shard, LANES), (2 * shard, D // 2)
    buffers = block_scratch(1, *out_tail) + block_scratch(PER_STAGE * LATE, *up_tail)
    for _ in range(LATE):
        buffers += row_scratch(rows, D)
    count = 2 + LATE
    mines = [
        VMEM((1, PLANES, SPOTS) + out_tail, BF16),
        VMEM((PER_STAGE * LATE, PLANES, SPOTS) + up_tail, BF16),
    ] + [VMEM((SPOTS * rows, D), BF16)] * LATE
    parts = [
        VMEM((1, PLANES) + out_tail, BF16),
        VMEM((up_count, PLANES) + up_tail, BF16),
        VMEM((STAGES, rows, D), BF16),
        VMEM((PLANES - 1, 1) + out_tail, BF16),
        VMEM((PLANES - 1, up_count) + up_tail, BF16),
        VMEM((PLANES - 1, rows, D), BF16),
    ]
    tile = (local, BLOCK, LANES)
    wide = VMEM((spans, 2 * BLOCK, SPAN * BLOCK), F32)
    thin = VMEM((spans, BLOCK, SPAN * BLOCK), F32)
    dma = pltpu.SemaphoreType.DMA
    return pl.pallas_call(
        plane_attend_back_kernel,
        out_shape=(
            jax.ShapeDtypeStruct((2, SPOTS, PIECES, 3) + tile, BF16),
            jax.ShapeDtypeStruct(hidden.shape, BF16),
            jax.ShapeDtypeStruct(out_tail, F32),
            jax.ShapeDtypeStruct((up_count,) + up_tail, F32),
            jax.ShapeDtypeStruct((rows, D), F32),
        ),
        in_specs=[
            whole(pltpu.SMEM),
            whole(pltpu.SMEM),
            whole(),
            whole(),
            whole(ANY),
            whole(),
            whole(ANY),
        ]
        + [whole(ANY)] * 5,
        out_specs=(whole(ANY), whole(ANY)) + (whole(),) * 3,
        scratch_shapes=buffers
        + mines
        + parts
        + [
            VMEM((PLANES, SPOTS) + tile, BF16),
            VMEM((PLANES, SPOTS, 3) + tile, BF16),
            VMEM((2, blocks, BLOCK, LANES), F32),
            VMEM((2, blocks * RANDOM, BLOCK, LANES), F32),
            VMEM((2, blocks * RANDOM, BLOCK, LANES), BF16),
            VMEM((PIECES, SPOTS) + tile, BF16),
            wide,
            wide,
            thin,
            thin,
            dma((count, SpotReduce.SEMS)),
            dma((count, SpotReduce.SEMS)),
            dma((3, PLANES - 1)),
            dma((3, PLANES - 1)),
            dma((count + 2,)),
        ]
        + exchange_sems((PLANES, SPOTS))
        + [
            dma((36,)),
            dma((2, SPOTS, PIECES, 3)),
            dma((3, PIECES)),
            dma((2,)),
            dma((2,)),
            dma((2,)),
            dma,
            dma,
        ],
        compiler_params=pltpu.CompilerParams(
            vmem_limit_bytes=62 * 1024 * 1024, collective_id=5, has_side_effects=True
        ),
        name="plane_attention_back",
    )(table, sorted_table, qk, shared, grad_source, lse, hidden, *sources, half_up, half_down)


class PlaneGather:
    SENDS = 3 + 3 + 4 + 2

    def __init__(self, source, target, send_sem, column_sem, recv_sem, local_sem):
        self.source, self.target = source, target
        self.send_sem, self.column_sem, self.recv_sem = send_sem, column_sem, recv_sem
        self.core, self.plane, self.spot = place_here()
        self.sends = []
        self.own = pltpu.make_async_copy(
            source, target.at[self.core, self.plane, self.spot], local_sem
        )
        self.own.start()
        for bits in range(1, PLANES):
            copy = remote(
                source,
                target.at[self.core, self.plane, self.spot],
                send_sem.at[len(self.sends)],
                column_sem.at[self.plane],
                (self.core, rank_of(flip(self.plane, bits), self.spot)),
            )
            copy.start()
            self.sends.append(copy)

    def neighbour(self, bits):
        return (self.core, rank_of(self.plane, flip(self.spot, bits)))

    def sibling(self):
        return (1 - self.core, rank_of(self.plane, self.spot))

    def piece(self, core, planes, spot):
        return self.target.at[core, planes, spot]

    def send(self, planes, spot, part, goal):
        piece = self.piece(self.core, planes, spot)
        copy = remote(
            piece,
            piece,
            self.send_sem.at[len(self.sends)],
            self.recv_sem.at[self.core, spot, part],
            goal,
        )
        copy.start()
        self.sends.append(copy)

    def arrive(self, core, planes, spot, part):
        piece = self.piece(core, planes, spot)
        remote(
            piece,
            piece,
            self.send_sem.at[0],
            self.recv_sem.at[core, spot, part],
            (self.core, rank_of(self.plane, self.spot)),
        ).wait_recv()

    def columns(self):
        self.own.wait()
        for bits in range(1, PLANES):
            other = flip(self.plane, bits)
            shard = self.target.at[self.core, other, self.spot]
            remote(
                shard,
                shard,
                self.send_sem.at[0],
                self.column_sem.at[other],
                (self.core, rank_of(self.plane, self.spot)),
            ).wait_recv()
        for goal in (self.neighbour(1), self.neighbour(2), self.sibling()):
            self.send(slice(0, PLANES), self.spot, 0, goal)

    def forward(self):
        everything = slice(0, PLANES)
        for side in (1, 2):
            spot = flip(self.spot, side)
            self.arrive(self.core, everything, spot, 0)
            half = slice(0, 2) if side == 1 else slice(2, 4)
            self.send(half, spot, side - 1, self.neighbour(3 - side))
            self.send(everything, spot, 0, self.sibling())

    def corner(self):
        spot = flip(self.spot, 3)
        for part, half in enumerate((slice(0, 2), slice(2, 4))):
            self.arrive(self.core, half, spot, part)
            self.send(half, spot, part, self.sibling())

    def finish(self):
        for side in range(3):
            self.arrive(1 - self.core, slice(0, PLANES), flip(self.spot, side), 0)
        for part, half in enumerate((slice(0, 2), slice(2, 4))):
            self.arrive(1 - self.core, half, flip(self.spot, 3), part)
        for copy in self.sends:
            copy.wait_send()


class CrossGather:
    SENDS = 2 + 1 + 3 + 3 * 4

    def __init__(self, source, target, send_sem, spot_sem, recv_sem, local_sem):
        self.target = target
        self.send_sem, self.spot_sem, self.recv_sem = send_sem, spot_sem, recv_sem
        self.core, self.plane, self.spot = place_here()
        self.sends = []
        self.own = pltpu.make_async_copy(
            source, target.at[self.core, self.plane, self.spot], local_sem
        )
        self.own.start()
        for side in (1, 2):
            self.pass_on(source, self.spot, flip(self.spot, side))

    def push(self, source, target, recv_sem, device):
        copy = remote(source, target, self.send_sem.at[len(self.sends)], recv_sem, device)
        copy.start()
        self.sends.append(copy)

    def pass_on(self, source, spot, goal):
        self.push(
            source,
            self.target.at[self.core, self.plane, spot],
            self.spot_sem.at[spot],
            (self.core, rank_of(self.plane, goal)),
        )

    def await_spot(self, spot):
        shard = self.target.at[self.core, self.plane, spot]
        remote(
            shard,
            shard,
            self.send_sem.at[0],
            self.spot_sem.at[spot],
            (self.core, rank_of(self.plane, self.spot)),
        ).wait_recv()

    def across(self):
        beside, beyond = flip(self.spot, 1), flip(self.spot, 2)
        for side in (1, 2):
            self.await_spot(flip(self.spot, side))
        spot = beside * (1 - self.core) + beyond * self.core
        goal = beyond * (1 - self.core) + beside * self.core
        self.pass_on(self.target.at[self.core, self.plane, spot], spot, goal)

    def blocks(self):
        self.own.wait()
        self.await_spot(flip(self.spot, 3))
        self.maybe = []
        self.along(self.plane, 1, self.plane < PLANES - 1)
        self.along(self.plane, -1, self.plane > 0)
        self.to_sibling(self.plane, self.plane >= 0)

    def along(self, plane, step, wanted):
        block = self.target.at[self.core, plane]
        copy = remote(
            block,
            block,
            self.send_sem.at[3 + len(self.maybe)],
            self.recv_sem.at[self.core, plane],
            (self.core, rank_of(self.plane + step, self.spot)),
        )
        self.begin(copy, wanted)

    def to_sibling(self, plane, wanted):
        block = self.target.at[self.core, plane]
        copy = remote(
            block,
            block,
            self.send_sem.at[3 + len(self.maybe)],
            self.recv_sem.at[self.core, plane],
            (1 - self.core, rank_of(self.plane, self.spot)),
        )
        self.begin(copy, wanted)

    def begin(self, copy, wanted):
        self.maybe.append((copy, wanted))

        @pl.when(wanted)
        def _():
            copy.start()

    def arrive(self, core, plane):
        block = self.target.at[core, plane]
        remote(
            block,
            block,
            self.send_sem.at[0],
            self.recv_sem.at[core, plane],
            (self.core, rank_of(self.plane, self.spot)),
        ).wait_recv()

    def hop(self, distance):
        for step in (1, -1):
            origin = self.plane - step * distance
            here = (origin >= 0) & (origin < PLANES)
            onward = self.plane + step
            more = here & (onward >= 0) & (onward < PLANES)

            @pl.when(here)
            def _(origin=origin):
                self.arrive(self.core, origin)

            self.along(origin, step, more)
            self.to_sibling(origin, here)

    def finish(self):
        for bits in range(PLANES):
            self.arrive(1 - self.core, flip(self.plane, bits))
        for copy in self.sends:
            copy.wait_send()
        for copy, wanted in self.maybe:

            @pl.when(wanted)
            def _(copy=copy):
                copy.wait_send()


def pair_of_blocks(read, first, second):
    low = low_lanes(1)
    tiles = []
    for block, wanted in ((first, 0), (second, 1)):
        tile = read(block // 2)
        tiles.append(tile if block % 2 == wanted else swap_halves(tile))
    return jnp.where(low, tiles[0], tiles[1])


def fold_tiles(target_ref, start, tiles, read):
    half = len(tiles) // 2
    for number in range(half):
        columns = slice((start + number) * LANES, (start + number + 1) * LANES)
        target_ref[:, columns] = jnp.concatenate(
            [read(tiles[number]), read(tiles[half + number])], axis=0
        ).astype(BF16)


VECTORS = 8


def lay_vectors(vecs_ref, vectors_ref, up_ref):
    rows = vecs_ref.shape[3]
    own, wide = D // RANKS, FF // RANKS
    values = vecs_ref[...].reshape(RANKS, rows, LANES).astype(F32)

    def spread_out(count, width):
        place = lax.broadcasted_iota(jnp.int32, (LANES, count), 1)
        lane = lax.broadcasted_iota(jnp.int32, (LANES, count), 0)
        start = lax.div(place, width) * width
        return jnp.where(place - start == lane, 1.0, 0.0).astype(BF16)

    laid = dot(vecs_ref[...].reshape(RANKS * rows, LANES), spread_out(D, own))
    owner = lax.broadcasted_iota(jnp.int32, (RANKS, 1, D), 0)
    column = lax.broadcasted_iota(jnp.int32, (RANKS, 1, D), 2)
    laid = jnp.where(lax.div(column, own) == owner, laid.reshape(RANKS, rows, D), 0.0)
    vectors_ref[...] = jnp.sum(laid, axis=0)[:VECTORS]
    row = lax.broadcasted_iota(jnp.int32, (1, rows, LANES), 1)
    last = jnp.sum(jnp.where(row == VECTORS, values, 0.0), axis=1)
    laid = dot(last.astype(BF16), spread_out(FF, wide))
    owner = lax.broadcasted_iota(jnp.int32, (RANKS, FF), 0)
    column = lax.broadcasted_iota(jnp.int32, (RANKS, FF), 1)
    laid = jnp.sum(jnp.where(lax.div(column, wide) == owner, laid, 0.0), axis=0, keepdims=True)
    for chunk in range(FF // CHUNK):
        for side in range(2):
            start = side * (FF // 2) + chunk * LANES
            up_ref[chunk, :, side * LANES : (side + 1) * LANES] = laid[:, start : start + LANES]


def lay_table(tables_ref, core, micro, entries):
    count = 2 * LANES
    ranks = PLANES * SPOTS
    values = tables_ref[core].reshape(ranks, tables_ref.shape[3], LANES).astype(F32)
    row = lax.broadcasted_iota(jnp.int32, (1, tables_ref.shape[3], LANES), 1)
    values = jnp.sum(jnp.where(row == micro, values, 0.0), axis=1)
    place = lax.broadcasted_iota(jnp.int32, (LANES, count), 1)
    lane = lax.broadcasted_iota(jnp.int32, (LANES, count), 0)
    start = lax.div(place, entries) * entries
    laid = dot(values.astype(BF16), jnp.where(place - start == lane, 1.0, 0.0).astype(BF16))
    owner = lax.broadcasted_iota(jnp.int32, (ranks, count), 0)
    column = lax.broadcasted_iota(jnp.int32, (ranks, count), 1)
    laid = jnp.sum(jnp.where(lax.div(column, entries) == owner, laid, 0.0), axis=0, keepdims=True)
    column = lax.broadcasted_iota(jnp.int32, (1, count), 1)
    return jnp.where(column < ranks * entries, laid, 2.0 * LANES)


def front_kernel(
    x_in_ref,
    dy_ref,
    vec_ref,
    tab_ref,
    w_qkv_in_ref,
    w_out_in_ref,
    w_up_in_ref,
    w_down_in_ref,
    back_ref,
    x_ref,
    dys_ref,
    w_down_ref,
    w_qkv_hbm,
    w_out_hbm,
    w_up_hbm,
    qk_hbm,
    shared_hbm,
    normed_ref,
    lse_ref,
    vectors_ref,
    up_ref,
    table_ref,
    sorted_ref,
    s_qkv_ref,
    s_ou_ref,
    g_qkv_ref,
    g_ou_ref,
    w_qkv_ref,
    w_out_ref,
    w_up_ref,
    xs_ref,
    vecs_ref,
    tabs_ref,
    bias_ref,
    send_ref,
    qk_ref,
    shared_ref,
    out_ref,
    p_ref,
    q_ref,
    picks_ref,
    *sems,
):
    gather_send, gather_recv, gather_local = sems[:3]
    plane_sems, cross_sems = sems[3:7], sems[7:11]
    x_sems, dy_sems = sems[11:14], sems[14:17]
    qkv_send, qkv_recv, qkv_local, shared_send, shared_recv = sems[17:22]
    back_sems, local_sem = sems[22:25], sems[25]
    core, plane, spot = place_here()
    micro, rows, _ = x_in_ref.shape
    tokens = PIECES * rows
    local = rows // BLOCK
    blocks = PLANES * SPOTS * local

    barrier = pltpu.get_barrier_semaphore()
    partners = both_partners(core, plane, spot)
    for partner in partners:
        pl.semaphore_signal(barrier, inc=1, device_id=partner, device_id_type=MESH)

    def natural(ref):
        return lambda tile: ref[:, tile * LANES : (tile + 1) * LANES].astype(F32)

    order = [natural_block(entry) for entry in column_order()]
    read = natural(w_qkv_in_ref)
    fold_tiles(
        s_qkv_ref,
        0,
        list(range(TILES)),
        lambda tile: pair_of_blocks(read, order[2 * tile], order[2 * tile + 1]),
    )
    pl.semaphore_wait(barrier, len(partners))

    finish_x = to_planes(x_in_ref, xs_ref, *x_sems)
    gathers = []
    for number, (source, target) in enumerate(
        ((tab_ref, tabs_ref), (vec_ref, vecs_ref), (s_qkv_ref, g_qkv_ref))
    ):
        one = Gather(
            source, target, gather_send.at[number], gather_recv.at[number], gather_local.at[number]
        )
        one.start()
        gathers.append(one)
    outs = D // LANES // 2
    fold_tiles(s_ou_ref, 0, list(range(D // LANES)), natural(w_out_in_ref))
    fold_tiles(s_ou_ref, outs, list(range(FF // LANES)), natural(w_up_in_ref))
    for one in gathers:
        one.column()
    cross = CrossGather(w_down_in_ref, w_down_ref, *cross_sems)
    for one in gathers:
        one.across()
    for one in gathers:
        one.corner()
    cross.across()
    finish_x()
    spread = PlaneGather(s_ou_ref, g_ou_ref, *plane_sems)
    keep_x = pltpu.make_async_copy(xs_ref, x_ref, local_sem.at[0])
    keep_x.start()
    normal, _ = norm_parts(xs_ref[...].reshape(tokens, D).astype(F32))
    for one in gathers[:2]:
        one.finish()

    window_core, window_micro = lax.rem(plane, 2), lax.div(plane, 2)
    scalars = pltpu.make_async_copy(tabs_ref.at[window_core], picks_ref, local_sem.at[1])
    scalars.start()
    lay_vectors(vecs_ref, vectors_ref, up_ref)
    normed_ref[...] = (normal * vectors_ref[0:1] + vectors_ref[1:2]).astype(BF16)
    for tile in range(TILES):
        halves = []
        for entry in column_order()[2 * tile : 2 * tile + 2]:
            halves.append(entry)

        def bias_tile(number, halves=halves):
            if number < D // LANES:
                return vectors_ref[2:3, number * LANES : (number + 1) * LANES]
            if number < 2 * D // LANES:
                return jnp.zeros((1, LANES), F32)
            start = (number - 2 * D // LANES) * LANES
            return vectors_ref[3:4, start : start + LANES]

        chunk, side = tile % HALF_TILES, tile // HALF_TILES
        start = chunk * CHUNK + side * LANES
        bias_ref[:, start : start + LANES] = pair_of_blocks(
            bias_tile, order[2 * tile], order[2 * tile + 1]
        )
    gathers[2].finish()
    settle(g_qkv_ref, [(tile, w_qkv_ref, alternate(tile)) for tile in range(HALF_TILES)])
    keep_w = pltpu.make_async_copy(w_qkv_ref, w_qkv_hbm, local_sem.at[2])
    keep_w.start()

    def shaped(value):
        return value.astype(BF16).reshape(local, BLOCK, LANES)

    low = low_lanes(rows)
    queries = D // LANES
    for chunk in range(HALF_TILES):
        columns = slice(chunk * CHUNK, (chunk + 1) * CHUNK)
        packed = dot(normed_ref[...], w_qkv_ref[:, columns]) + bias_ref[:, columns]
        for side in range(2):
            tile = chunk + side * HALF_TILES
            whole_tile = packed[:, side * LANES : (side + 1) * LANES]
            if tile < queries:
                whole_tile = whole_tile.astype(BF16).astype(F32) * SCALE
            for piece in range(PIECES):
                part = whole_tile[piece * rows : (piece + 1) * rows]
                if tile < SPOTS:
                    send_ref[0, tile, piece, 0] = shaped(part)
                elif tile < queries:
                    first = 2 * (tile - SPOTS)
                    shared = send_ref[0, first, piece, 0].reshape(rows, LANES).astype(F32)
                    send_ref[1, first, piece, 0] = shaped(jnp.where(low, part, shared))
                    shared = send_ref[0, first + 1, piece, 0].reshape(rows, LANES).astype(F32)
                    send_ref[1, first + 1, piece, 0] = shaped(
                        jnp.where(low, swap_halves(part), shared)
                    )
                else:
                    goal, role = (tile - queries) // 3, (tile - queries) % 3
                    if role < 2:
                        send_ref[role, goal, piece, 1] = shaped(part)
                    else:
                        send_ref[0, goal, piece, 2] = shaped(part)
    sends, keeps = [], []
    for part, (parts, landing) in enumerate(((slice(0, 2), qk_ref), (2, shared_ref))):
        for side in (3, 1, 2, 0):
            for other in (core, 1 - core) if part == 0 else (core,):
                goal = flip(spot, side)
                for piece in range(PIECES):
                    source = send_ref.at[other if part == 0 else 0, goal, piece, parts]
                    target = landing.at[2 * core + piece, spot]
                    if side == 0 and other is core:
                        copy = pltpu.make_async_copy(source, target, qkv_local.at[part, piece])
                        keeps.append((part, copy))
                    else:
                        copy = remote(
                            source,
                            target,
                            qkv_send.at[len(sends)],
                            qkv_recv.at[2 * core + piece, spot, part],
                            (other, rank_of(plane, goal)),
                        )
                        sends.append(copy)
                    copy.start()
    spread.columns()
    cross.blocks()
    table = lay_table(tabs_ref, window_core, window_micro, local * RANDOM)
    table_ref[...] = table.astype(jnp.int32)
    sort_entries(table, sorted_ref, blocks * RANDOM)
    scalars.wait()

    def arrive(part, other, piece, goal):
        target = (qk_ref, shared_ref)[part].at[2 * other + piece, goal]
        remote(
            target,
            target,
            qkv_send.at[0],
            qkv_recv.at[2 * other + piece, goal, part],
            (core, rank_of(plane, spot)),
        ).wait_recv()

    for side in range(SPOTS):
        for other in (core, 1 - core):
            if side > 0 or other is not core:
                for piece in range(PIECES):
                    arrive(0, other, piece, flip(spot, side))
    for part, copy in keeps:
        copy.wait()
    cross.hop(1)

    low = low_lanes(BLOCK)
    masks = [half_mask(True), half_mask(False)]

    def tile_of(component, block):
        rank, number = lax.div(block, local), lax.rem(block, local)
        if component == 2:
            return shared_ref[lax.div(rank, SPOTS), lax.rem(rank, SPOTS), number]
        return qk_ref[lax.div(rank, SPOTS), lax.rem(rank, SPOTS), component, number]

    def picked(block, number):
        rank = lax.div(block, local)
        return picks_ref[
            lax.div(rank, SPOTS),
            lax.rem(rank, SPOTS),
            window_micro,
            lax.rem(block, local) * RANDOM + number,
        ]

    def place_of(block):
        rank = lax.div(block, local)
        return lax.div(rank, SPOTS), lax.rem(rank, SPOTS), lax.rem(block, local)

    def put(block, slot, mixed, log):
        place = place_of(block)
        if slot == 0:
            out_ref[place] = mixed.astype(BF16)
            lse_ref[block] = jnp.where(low, log, 0.0)
        else:
            out_ref[place] = jnp.where(low, mixed, out_ref[place].astype(F32)).astype(BF16)
            lse_ref[block] = jnp.where(low, lse_ref[block], log)

    def one_block(block, slot):
        ids, bias = inner_slots(picked, block, blocks)
        keys = jnp.concatenate([tile_of(1 + slot, number) for number in ids], axis=0)
        scores = dot_rt(tile_of(0, block) * masks[slot], keys) + bias
        top = jnp.max(scores, axis=1, keepdims=True)
        powered = jnp.exp(scores - top)
        total = jnp.sum(powered, axis=1, keepdims=True)
        mixed = dot(powered.astype(BF16), keys) * (1.0 / total)
        return mixed, top + jnp.log(total)

    def rank_blocks(rank, slot):
        results = [one_block(rank * local + number, slot) for number in range(local)]
        for number, (mixed, log) in enumerate(results):
            put(rank * local + number, slot, mixed, log)

    spans = blocks // SPAN
    ends = (0, blocks - 1)

    def dense(slot, scores_ref, numbers):
        size = len(numbers) * BLOCK
        query = jnp.concatenate([tile_of(0, number) * masks[slot] for number in numbers], axis=0)

        def keys_at(span):
            return jnp.concatenate(
                [tile_of(1 + slot, span * SPAN + number) for number in range(SPAN)], axis=0
            )

        def first_pass(span, top):
            scores = dot_rt(query, keys_at(span))
            scores_ref[span] = scores
            return jnp.maximum(top, jnp.max(scores, axis=1, keepdims=True))

        top = lax.fori_loop(
            0, spans, first_pass, jnp.full((size, 1), NEGATIVE, F32), unroll=2
        )

        def second_pass(span, carry):
            total, mixed = carry
            powered = jnp.exp(scores_ref[span] - top)
            return (
                total + jnp.sum(powered, axis=1, keepdims=True),
                mixed + dot(powered.astype(BF16), keys_at(span)),
            )

        total, mixed = lax.fori_loop(
            0,
            spans,
            second_pass,
            (jnp.zeros((size, 1), F32), jnp.zeros((size, LANES), F32)),
            unroll=2,
        )
        mixed = mixed * (1.0 / total)
        log = top + jnp.log(total)
        for place, number in enumerate(numbers):
            span = slice(place * BLOCK, (place + 1) * BLOCK)
            put(number, slot, mixed[span], log[span])

    def head_a(number, carry):
        rank_blocks(number, 0)
        return carry

    def head_b(number, carry):
        rank_blocks(core * (PLANES * SPOTS // 2) + number, 1)
        return carry

    shared = []
    half_way = PLANES * SPOTS // 2
    lax.fori_loop(0, half_way, head_a, 0)
    for side in range(SPOTS):
        goal = flip(spot, side)
        for piece in range(PIECES):
            if side > 0:
                arrive(1, core, piece, goal)
            source = shared_ref.at[2 * core + piece, goal]
            copy = remote(
                source,
                source,
                shared_send.at[2 * side + piece],
                shared_recv.at[2 * core + piece, goal],
                (1 - core, rank_of(plane, spot)),
            )
            copy.start()
            shared.append(copy)
    cross.hop(2)
    finish_dy = to_planes(dy_ref, dys_ref, *dy_sems)
    lax.fori_loop(half_way, PLANES * SPOTS, head_a, 0)
    dense(0, p_ref, ends)
    spread.forward()
    back = Inward(out_ref, back_ref, *back_sems)
    everything = slice(0, local)
    for side, other, goal, stays in inward_targets(core, spot):
        if other is not core:
            for piece in range(PIECES):
                back.send(other, goal, stays, piece, 0, everything)
    for side in range(SPOTS):
        for piece in range(PIECES):
            target = shared_ref.at[2 * (1 - core) + piece, flip(spot, side)]
            remote(
                target,
                target,
                shared_send.at[0],
                shared_recv.at[2 * (1 - core) + piece, flip(spot, side)],
                (core, rank_of(plane, spot)),
            ).wait_recv()
    keep_qk = pltpu.make_async_copy(qk_ref, qk_hbm, local_sem.at[3])
    keep_qk.start()
    keep_shared = pltpu.make_async_copy(shared_ref, shared_hbm, local_sem.at[6])
    keep_shared.start()
    lax.fori_loop(0, half_way, head_b, 0)
    dense(1, q_ref, (core * (blocks - 1),))
    spread.corner()
    cross.hop(3)
    for side, other, goal, stays in inward_targets(core, spot):
        if other is core:
            for piece in range(PIECES):
                back.send(other, goal, stays, piece, 0, everything)
    spread.finish()
    settle(
        g_ou_ref,
        [(tile, w_out_ref, (tile, outs + tile)) for tile in range(outs)]
        + [(outs + tile, w_up_ref, alternate(tile)) for tile in range(FF // CHUNK)],
    )
    keep_out = pltpu.make_async_copy(w_out_ref, w_out_hbm, local_sem.at[4])
    keep_out.start()
    keep_up = pltpu.make_async_copy(w_up_ref, w_up_hbm, local_sem.at[5])
    keep_up.start()
    cross.finish()
    finish_dy()
    for copy in sends:
        copy.wait_send()
    for copy in shared:
        copy.wait_send()
    back.finish(((everything,), (everything,)))
    for copy in (keep_x, keep_w, keep_qk, keep_shared, keep_out, keep_up):
        copy.wait()


def front(x, dy, vec, tab, w_qkv, w_out, w_up, w_down):
    micro, rows, _ = x.shape
    tokens = PIECES * rows
    local = rows // BLOCK
    blocks = PLANES * SPOTS * local
    spans = blocks // SPAN
    grid = (2, PLANES, SPOTS)
    shard = D // RANKS
    tile = (local, BLOCK, LANES)
    dma = pltpu.SemaphoreType.DMA
    struct = jax.ShapeDtypeStruct
    ou = (2 * shard, (D + FF) // 2)
    return pl.pallas_call(
        front_kernel,
        out_shape=(
            struct((2, SPOTS, PIECES) + tile, BF16),
            struct(x.shape, BF16),
            struct(dy.shape, BF16),
            struct(grid + w_down.shape, BF16),
            struct((D, 3 * D), BF16),
            struct((D, D), BF16),
            struct((D, FF), BF16),
            struct((PLANES, SPOTS, 2) + tile, BF16),
            struct((PLANES, SPOTS) + tile, BF16),
            struct((tokens, D), BF16),
            struct((blocks, BLOCK, LANES), F32),
            struct((VECTORS, D), F32),
            struct((FF // CHUNK, 1, CHUNK), F32),
            struct((1, 2 * LANES), jnp.int32),
            struct((4, 2 * LANES), jnp.int32),
        ),
        in_specs=[
            whole(ANY),
            whole(ANY),
            whole(ANY),
            whole(ANY),
            whole(),
            whole(),
            whole(),
            whole(ANY),
        ],
        out_specs=(whole(ANY),) * 9 + (whole(),) * 6,
        scratch_shapes=[
            VMEM((2 * shard, 3 * D // 2), BF16),
            VMEM(ou, BF16),
            VMEM(grid + (2 * shard, 3 * D // 2), BF16),
            VMEM(grid + ou, BF16),
            VMEM((D, 3 * D), BF16),
            VMEM((D, D), BF16),
            VMEM((D, FF), BF16),
            VMEM((PIECES, rows, D), BF16),
            VMEM(grid + vec.shape, BF16),
            VMEM(grid + tab.shape, jnp.int32),
            VMEM((1, 3 * D), F32),
            VMEM((2, SPOTS, PIECES, 3) + tile, BF16),
            VMEM((PLANES, SPOTS, 2) + tile, BF16),
            VMEM((PLANES, SPOTS) + tile, BF16),
            VMEM((PLANES, SPOTS) + tile, BF16),
            VMEM((spans, 2 * BLOCK, SPAN * BLOCK), F32),
            VMEM((spans, BLOCK, SPAN * BLOCK), F32),
            pltpu.SMEM((PLANES, SPOTS) + tab.shape, jnp.int32),
            dma((3, Gather.SENDS)),
            dma((3,) + grid),
            dma((3,)),
            dma((PlaneGather.SENDS,)),
            dma((PLANES,)),
            dma((2, SPOTS, 2)),
            dma,
            dma((CrossGather.SENDS,)),
            dma((SPOTS,)),
            dma((2, PLANES)),
            dma,
        ]
        + [dma((2,))] * 6
        + [
            dma((20,)),
            dma((PLANES, SPOTS, 2)),
            dma((2, PIECES)),
            dma((2 * SPOTS,)),
            dma((PLANES, SPOTS)),
            dma((14,)),
            dma((2, SPOTS, PIECES, 1)),
            dma((1, PIECES)),
            dma((7,)),
        ],
        compiler_params=pltpu.CompilerParams(
            vmem_limit_bytes=60 * 1024 * 1024, collective_id=1, has_side_effects=True
        ),
        name="front",
    )(x, dy, vec, tab, w_qkv, w_out, w_up, w_down)


class SpotReduce:
    SEMS = 4

    def __init__(self, source, near, corner, sides, send_sem, recv_sem, rows=None, mine=None):
        self.source, self.near, self.corner, self.side = source, near, corner, sides
        self.send_sem, self.recv_sem, self.rows, self.mine = send_sem, recv_sem, rows, mine
        self.core, self.plane, self.spot = place_here()
        beside, beyond = flip(self.spot, 1), flip(self.spot, 2)
        self.via = beyond * (1 - self.core) + beside * self.core
        self.other = beside * (1 - self.core) + beyond * self.core

    def half(self, core):
        return self.source.at[core] if self.rows else self.source.at[:, core]

    def part(self, spot):
        if self.rows:
            start = pl.multiple_of(spot * self.rows, 16)
            return self.near.at[pl.ds(start, self.rows)]
        return self.near.at[:, :, spot]

    def copy(self, number):
        sibling = (1 - self.core, rank_of(self.plane, self.spot))
        if number == 0:
            source, target, device = self.half(1 - self.core), self.near, sibling
        elif number == 1:
            source, target = self.part(flip(self.spot, 3)), self.corner
            device = (self.core, rank_of(self.plane, self.via))
        else:
            spot = flip(self.spot, number - 1)
            source, target = self.part(spot), self.side.at[number - 2]
            device = (self.core, rank_of(self.plane, spot))
        return remote(source, target, self.send_sem.at[number], self.recv_sem.at[number], device)

    def start(self):
        self.copy(0).start()

    def add(self, spot, terms, target=None):
        if self.rows:
            rows = self.rows

            def slab(number, carry):
                size = rows // 3
                first = pl.multiple_of(spot * rows + number * size, 16)
                place = pl.ds(first, size)
                inner = pl.ds(pl.multiple_of(number * size, 16), size)
                total = self.near[place].astype(F32)
                for read in terms:
                    total = total + read(place, inner).astype(F32)
                if target is None:
                    self.near[place] = total.astype(BF16)
                else:
                    target[inner] = total.astype(BF16)
                return carry

            lax.fori_loop(0, 3, slab, 0)
            return
        count = self.near.shape[0]

        def block(number, carry):
            first, plane = lax.div(number, PLANES), lax.rem(number, PLANES)
            total = self.near[first, plane, spot].astype(F32)
            for read in terms:
                total = total + read(first, plane).astype(F32)
            if target is None:
                self.near[first, plane, spot] = total.astype(BF16)
            else:
                target[first, plane] = total.astype(BF16)
            return carry

        lax.fori_loop(0, count * PLANES, block, 0)

    def corners(self):
        self.copy(0).wait_recv()
        core = self.core
        for spot in range(SPOTS):
            if self.rows and self.mine is None:
                self.add(spot, [lambda place, inner: self.source[core, place]])
            elif self.rows:
                self.add(spot, [lambda place, inner: self.mine[place]])
            elif self.mine is None:
                self.add(spot, [lambda first, plane, spot=spot: self.source[first, core, plane, spot]])
            else:
                self.add(spot, [lambda first, plane, spot=spot: self.mine[first, plane, spot]])
        self.copy(1).start()

    def sides(self):
        self.copy(1).wait_recv()
        if self.rows:
            self.add(self.other, [lambda place, inner: self.corner[inner]])
        else:
            self.add(self.other, [lambda first, plane: self.corner[first, plane]])
        self.copy(2).start()
        self.copy(3).start()

    def close(self, target):
        self.copy(2).wait_recv()
        self.copy(3).wait_recv()
        if self.rows:
            terms = [lambda place, inner, n=n: self.side[n, inner] for n in range(2)]
        else:
            terms = [lambda first, plane, n=n: self.side[n, first, plane] for n in range(2)]
        self.add(self.spot, terms, target)
        for number in range(self.SEMS):
            self.copy(number).wait_send()


def block_scratch(count, rows, width):
    return [
        VMEM((count, PLANES, SPOTS, rows, width), BF16),
        VMEM((count, PLANES, rows, width), BF16),
        VMEM((2, count, PLANES, rows, width), BF16),
    ]


def row_scratch(rows, width):
    return [
        VMEM((SPOTS * rows, width), BF16),
        VMEM((rows, width), BF16),
        VMEM((2, rows, width), BF16),
    ]


STAGES = 4
PER_STAGE = FF // CHUNK // STAGES
EARLY = 2
LATE = STAGES - EARLY
WAITS = (2, 4, 6)


def by_owner(out_ref, values):
    rows = D // RANKS
    width = values.shape[1] // 2
    for owner in range(RANKS):
        part = values[owner * rows : (owner + 1) * rows]
        out_ref[owner] = jnp.concatenate([part[:, :width], part[:, width:]], axis=0).astype(BF16)


def plane_middle_kernel(
    mixed_in_ref,
    x_ref,
    dy_ref,
    vec_ref,
    w_out_ref,
    up_shift_ref,
    w_up_ref,
    w_down_ref,
    hidden_ref,
    send_ref,
    dres_ref,
    g_out_ref,
    half_up_ref,
    half_down_ref,
    last_up_ref,
    last_down_ref,
    g_up_bias_ref,
    g_small_ref,
    mixed_ref,
    residual_ref,
    second_ref,
    second_t_ref,
    total_ref,
    dsecond_ref,
    g_up_ref,
    g_down_ref,
    *scratch,
):
    send_sem, recv_sem, local_sem = scratch[-3:]
    stages = []
    for number in range(EARLY):
        buffers = scratch[6 * number : 6 * number + 6]
        stages.append(
            (
                SpotReduce(
                    g_up_ref.at[PER_STAGE * number : PER_STAGE * (number + 1)],
                    *buffers[:3],
                    send_sem.at[number, 0],
                    recv_sem.at[number, 0],
                ),
                SpotReduce(
                    g_down_ref.at[number],
                    *buffers[3:],
                    send_sem.at[number, 1],
                    recv_sem.at[number, 1],
                    rows=FF // RANKS,
                ),
            )
        )
    pieces, rows, _ = x_ref.shape
    tokens = pieces * rows
    step = pl.program_id(0)
    low = low_lanes(rows)
    out_shift, gain, shift, down_shift = (vec_ref[number : number + 1] for number in (4, 5, 6, 7))

    @pl.when(step == 0)
    def _():
        core, plane, spot = place_here()
        greet(
            [
                (1 - core, rank_of(plane, spot)),
                (core, rank_of(plane, flip(spot, 1))),
                (core, rank_of(plane, flip(spot, 2))),
            ]
        )
        for piece in range(pieces):
            span = slice(piece * rows, (piece + 1) * rows)
            for spot in (0, 2):
                first = [mixed_in_ref[side, spot, piece].astype(F32) for side in range(2)]
                last = [mixed_in_ref[side, spot + 1, piece].astype(F32) for side in range(2)]
                own_first = jnp.where(core == 0, first[0], first[1])
                own_last = jnp.where(core == 0, last[0], last[1])
                tiles = (
                    jnp.where(low, swap_halves(first[0]), first[1]),
                    jnp.where(low, own_first, last[0]),
                    swap_halves(jnp.where(low, own_last, last[1])),
                )
                for number, tile in enumerate(tiles):
                    spread = 3 * (spot // 2) + number
                    mixed_ref[span, spread * LANES : (spread + 1) * LANES] = tile.astype(BF16)
        residual = x_ref[...].reshape(tokens, D).astype(F32) + (
            dot(mixed_ref[...], w_out_ref[...]) + out_shift
        )
        residual_ref[...] = residual
        normal, _ = norm_parts(residual)
        second = normal * gain + shift
        second_ref[...] = second.astype(BF16)
        second_t_ref[...] = second.T.astype(BF16)
        total_ref[...] = jnp.zeros_like(total_ref)
        dsecond_ref[...] = jnp.zeros_like(dsecond_ref)

    w_down = w_down_ref[...].reshape(CHUNK, D)
    upper = dot(second_ref[...], w_up_ref[...]) + up_shift_ref[0]
    factor = 0.7978845608028654
    square = upper * upper
    bent = jnp.tanh(factor * (upper + 0.044715 * (upper * square)))
    middle_half = 0.5 * (1.0 + bent)
    active = (upper * middle_half).astype(BF16)
    slope = middle_half + 0.5 * upper * (1.0 - bent * bent) * (
        factor + (3.0 * 0.044715 * factor) * square
    )
    dy = dy_ref[...]
    total_ref[...] += dot(active, w_down)
    stage, turn = lax.div(step, PER_STAGE), lax.rem(step, PER_STAGE)
    down_share = dot_lt(active, dy).astype(BF16)
    place = pl.ds(pl.multiple_of(turn * LANES, LANES), LANES)
    for side in range(2):
        g_down_ref[stage, side, place] = down_share[side * LANES : (side + 1) * LANES]
    dupper = (dot_rt(dy, w_down) * slope).astype(BF16)
    g_up_bias_ref[0] = jnp.sum(dupper.astype(F32), axis=0, keepdims=True)
    up_share = dot(second_t_ref[...], dupper)
    shard = D // RANKS
    for owner in range(RANKS):
        part = up_share[owner * shard : (owner + 1) * shard]
        g_up_ref[step, owner // (PLANES * SPOTS), owner // SPOTS % PLANES, owner % SPOTS] = (
            jnp.concatenate([part[:, :LANES], part[:, LANES:]], axis=0).astype(BF16)
        )
    dsecond_ref[...] += dot_rt(dupper, w_up_ref[...])

    last = FF // CHUNK - 1
    for number, pair in enumerate(stages):
        done = PER_STAGE * (number + 1) - 1

        @pl.when(step == done)
        def _(pair=pair):
            for one in pair:
                one.start()

        @pl.when(step == done + WAITS[0])
        def _(pair=pair):
            for one in pair:
                one.corners()

        @pl.when(step == done + WAITS[1])
        def _(pair=pair):
            for one in pair:
                one.sides()

        if done + WAITS[2] < last:

            @pl.when(step == done + WAITS[2])
            def _(pair=pair, number=number):
                pair[0].close(half_up_ref.at[PER_STAGE * number : PER_STAGE * (number + 1)])
                pair[1].close(half_down_ref.at[number])

    @pl.when(step == last)
    def _():
        keep_up = pltpu.make_async_copy(
            g_up_ref.at[PER_STAGE * EARLY : PER_STAGE * STAGES], last_up_ref, local_sem.at[0]
        )
        keep_up.start()
        keep_down = pltpu.make_async_copy(
            g_down_ref.at[EARLY:STAGES], last_down_ref, local_sem.at[1]
        )
        keep_down.start()
        residual = residual_ref[...]
        hidden_ref[...] = (
            (residual + (total_ref[...] + down_shift)).astype(BF16).reshape(x_ref.shape)
        )
        normal, inverse = norm_parts(residual)
        dsecond = dsecond_ref[...]
        grad_out = dy_ref[...].astype(F32)
        g_small_ref[0:1] = jnp.sum(dsecond * normal, axis=0, keepdims=True)
        g_small_ref[1:2] = jnp.sum(dsecond, axis=0, keepdims=True)
        g_small_ref[2:3] = jnp.sum(grad_out, axis=0, keepdims=True)
        dres = grad_out + norm_pull(dsecond, normal, inverse, gain)
        dres_ref[...] = dres
        branch = dres.astype(BF16)
        g_small_ref[3:4] = jnp.sum(branch.astype(F32), axis=0, keepdims=True)
        by_owner(g_out_ref, dot_lt(mixed_ref[...], branch))
        dmixed = dot_rt(branch, w_out_ref[...])
        for piece in range(pieces):
            span = slice(piece * rows, (piece + 1) * rows)
            for spot in (0, 2):
                tiles = [
                    dmixed[span, number * LANES : (number + 1) * LANES]
                    for number in range(3 * (spot // 2), 3 * (spot // 2) + 3)
                ]
                flipped = [swap_halves(tile) for tile in tiles]
                send_ref[0, spot, piece] = jnp.where(low, tiles[1], flipped[0]).astype(BF16)
                send_ref[1, spot, piece] = jnp.where(low, tiles[1], tiles[0]).astype(BF16)
                send_ref[0, spot + 1, piece] = jnp.where(low, flipped[2], tiles[1]).astype(BF16)
                send_ref[1, spot + 1, piece] = flipped[2].astype(BF16)
        for number, pair in enumerate(stages):
            if PER_STAGE * (number + 1) - 1 + WAITS[2] >= last:
                pair[0].close(half_up_ref.at[PER_STAGE * number : PER_STAGE * (number + 1)])
                pair[1].close(half_down_ref.at[number])
        keep_up.wait()
        keep_down.wait()


def plane_middle(mixed_in, x, dy, vec, w_out, up_shift, w_up, w_down):
    pieces, rows, _ = x.shape
    tokens = pieces * rows
    shard = D // RANKS

    def fixed(shape):
        return pl.BlockSpec(shape, lambda step: (0,) * len(shape))

    steps = FF // CHUNK
    grid = (2, PLANES, SPOTS)
    down_rows = FF // RANKS
    half_up = (PER_STAGE * EARLY, PLANES, 2 * shard, LANES)
    half_down = (EARLY, down_rows, D)
    buffers = []
    for _ in range(EARLY):
        buffers += block_scratch(PER_STAGE, 2 * shard, LANES) + row_scratch(down_rows, D)
    down = pl.BlockSpec((2, LANES, D), lambda step: (0, step, 0))
    return pl.pallas_call(
        plane_middle_kernel,
        grid=(steps,),
        out_shape=(
            jax.ShapeDtypeStruct(x.shape, BF16),
            jax.ShapeDtypeStruct(mixed_in.shape, BF16),
            jax.ShapeDtypeStruct((tokens, D), F32),
            jax.ShapeDtypeStruct((RANKS, 2 * shard, D // 2), BF16),
            jax.ShapeDtypeStruct(half_up, BF16),
            jax.ShapeDtypeStruct(half_down, BF16),
            jax.ShapeDtypeStruct((PER_STAGE * LATE,) + grid + (2 * shard, LANES), BF16),
            jax.ShapeDtypeStruct((LATE, 2, FF // 2 // STAGES, D), BF16),
            jax.ShapeDtypeStruct((steps, 1, CHUNK), F32),
            jax.ShapeDtypeStruct((4, D), F32),
        ),
        in_specs=[
            fixed(mixed_in.shape),
            fixed(x.shape),
            fixed((tokens, D)),
            fixed(vec.shape),
            fixed((D, D)),
            pl.BlockSpec((1, 1, CHUNK), lambda step: (step, 0, 0)),
            pl.BlockSpec((D, CHUNK), lambda step: (0, step)),
            down,
        ],
        out_specs=(
            fixed(x.shape),
            fixed(mixed_in.shape),
            fixed((tokens, D)),
            fixed((RANKS, 2 * shard, D // 2)),
            fixed(half_up),
            fixed(half_down),
            whole(ANY),
            whole(ANY),
            pl.BlockSpec((1, 1, CHUNK), lambda step: (step, 0, 0)),
            fixed((4, D)),
        ),
        scratch_shapes=[
            VMEM((tokens, D), BF16),
            VMEM((tokens, D), F32),
            VMEM((tokens, D), BF16),
            VMEM((D, tokens), BF16),
            VMEM((tokens, D), F32),
            VMEM((tokens, D), F32),
            VMEM((steps,) + grid + (2 * shard, LANES), BF16),
            VMEM((STAGES, 2, FF // 2 // STAGES, D), BF16),
        ]
        + buffers
        + [
            pltpu.SemaphoreType.DMA((EARLY, 2, SpotReduce.SEMS)),
            pltpu.SemaphoreType.DMA((EARLY, 2, SpotReduce.SEMS)),
            pltpu.SemaphoreType.DMA((2,)),
        ],
        compiler_params=pltpu.CompilerParams(
            vmem_limit_bytes=60 * 1024 * 1024, collective_id=3, has_side_effects=True
        ),
        name="plane_middle",
    )(mixed_in, x, dy, vec, w_out, up_shift, w_up, w_down)


class Reduce:
    SENDS = 4 + 2 + 2 + 3
    RECVS = SENDS

    def __init__(self, source, total, near, corner_x, corner_y, side_x, side_y, far, out, sems):
        self.source, self.total, self.near = source, total, near
        self.corner = {1: corner_x, 2: corner_y}
        self.side = {1: side_x, 2: side_y}
        self.far, self.out = far, out
        self.send_sem, self.recv_sem, self.local_sem = sems
        self.core, self.plane, self.spot = place_here()
        self.copies = []
        self.locals = []

    def start(self):
        sibling = (1 - self.core, rank_of(self.plane, self.spot))
        for number, side in enumerate((3, 1, 2, 0)):
            spot = flip(self.spot, side)
            copy = remote(
                self.source.at[1 - self.core, :, spot],
                self.near.at[:, spot],
                self.send_sem.at[number],
                self.recv_sem.at[number],
                sibling,
            )
            copy.start()
            self.copies.append(copy)
            keep = pltpu.make_async_copy(
                self.source.at[self.core, :, spot],
                self.total.at[:, spot],
                self.local_sem.at[number],
            )
            keep.start()
            self.locals.append(keep)

    def take(self, number, side):
        self.copies[number].wait_recv()
        self.locals[number].wait()
        spot = flip(self.spot, side)

        def add(plane, carry):
            self.total[plane, spot] = (
                self.total[plane, spot].astype(F32) + self.near[plane, spot].astype(F32)
            ).astype(self.total.dtype)
            return carry

        lax.fori_loop(0, PLANES, add, 0)

    def corners(self):
        self.take(0, 3)
        spot = flip(self.spot, 3)
        index = 4
        self.corner_copies = []
        for bits in range(PLANES):
            side = 2 if bits < 2 else 1
            self.corner_copies.append(None)
            plane = flip(self.plane, bits)
            copy = remote(
                self.total.at[plane, spot],
                self.corner[side].at[bits % 2],
                self.send_sem.at[index + bits],
                self.recv_sem.at[index + bits],
                (self.core, rank_of(self.plane, flip(self.spot, side))),
            )
            copy.start()
            self.corner_copies[bits] = copy

    def sides(self):
        self.take(1, 1)
        self.take(2, 2)
        self.side_copies = {}
        for side in (1, 2):
            spot = flip(self.spot, side)
            came = 3 - side
            for bits in (0, 1) if came == 2 else (2, 3):
                self.corner_copies[bits].wait_recv()
                plane = flip(self.plane, bits)
                self.total[plane, spot] = (
                    self.total[plane, spot].astype(F32)
                    + self.corner[came][bits % 2].astype(F32)
                ).astype(self.total.dtype)
            copy = remote(
                self.total.at[:, spot],
                self.side[side],
                self.send_sem.at[7 + side],
                self.recv_sem.at[7 + side],
                (self.core, rank_of(self.plane, spot)),
            )
            copy.start()
            self.side_copies[side] = copy

    def columns(self):
        self.take(3, 0)
        for side in (1, 2):
            self.side_copies[side].wait_recv()

        def add(plane, carry):
            self.total[plane, self.spot] = (
                self.total[plane, self.spot].astype(F32)
                + self.side[1][plane].astype(F32)
                + self.side[2][plane].astype(F32)
            ).astype(self.total.dtype)
            return carry

        lax.fori_loop(0, PLANES, add, 0)
        self.far_copies = []
        for bits in range(1, PLANES):
            plane = flip(self.plane, bits)
            copy = remote(
                self.total.at[plane, self.spot],
                self.far.at[bits - 1],
                self.send_sem.at[9 + bits],
                self.recv_sem.at[9 + bits],
                (self.core, rank_of(plane, self.spot)),
            )
            copy.start()
            self.far_copies.append(copy)

    def finish(self):
        value = self.total[self.plane, self.spot].astype(F32)
        for bits in range(1, PLANES):
            self.far_copies[bits - 1].wait_recv()
            value = value + self.far[bits - 1].astype(F32)
        self.out[...] = value
        for copy in self.copies + self.corner_copies + self.far_copies:
            copy.wait_send()
        for side in (1, 2):
            self.side_copies[side].wait_send()


REDUCE_SEMS = 13


def reduce_scratch(shape, kind):
    tail = shape[3:]
    return [
        VMEM((PLANES, SPOTS) + tail, kind),
        VMEM((PLANES, SPOTS) + tail, kind),
        VMEM((2,) + tail, kind),
        VMEM((2,) + tail, kind),
        VMEM((PLANES,) + tail, kind),
        VMEM((PLANES,) + tail, kind),
        VMEM((PLANES - 1,) + tail, kind),
    ]


class Doubling:
    STEPS = 5

    def __init__(self, totals, boxes, send_sem, recv_sem):
        self.totals, self.boxes = totals, boxes
        self.send_sem, self.recv_sem = send_sem, recv_sem
        core, plane, spot = place_here()
        self.partners = (
            (1 - core, rank_of(plane, spot)),
            (core, rank_of(plane, flip(spot, 1))),
            (core, rank_of(plane, flip(spot, 2))),
            (core, rank_of(flip(plane, 1), spot)),
            (core, rank_of(flip(plane, 2), spot)),
        )
        self.copies = []

    def start(self, step):
        self.copies = []
        for number, (total, box) in enumerate(zip(self.totals, self.boxes)):
            copy = remote(
                total,
                box.at[step],
                self.send_sem.at[step, number],
                self.recv_sem.at[step, number],
                self.partners[step],
            )
            copy.start()
            self.copies.append(copy)

    def finish(self, step):
        for copy, total, box in zip(self.copies, self.totals, self.boxes):
            copy.wait()
            total[...] += box[step]


PARTS = 3


def finish_kernel(
    recv_ref,
    normed_ref,
    x_ref,
    dres_hbm,
    vec_ref,
    w_hbm,
    g_mid_ref,
    g_up_bias_ref,
    grad_ref,
    g_qkv_ref,
    rows_out_ref,
    tiles_out_ref,
    *scratch,
):
    sources, scratch = scratch[:PARTS], scratch[PARTS:]
    buffers, scratch = scratch[: 7 * PARTS], scratch[7 * PARTS :]
    packed_ref, dnormed_ref, gradient_ref, dres_ref, w_ref = scratch[:5]
    rows_ref, tiles_ref, rows_box, tiles_box = scratch[5:9]
    send_sem, recv_sem, local_sem, load_sem, sum_send, sum_recv = scratch[9:15]
    move_sems = scratch[15:18]
    pieces, rows, _ = x_ref.shape
    tokens = pieces * rows
    core, plane, spot = place_here()
    low = low_lanes(rows)

    load_w = pltpu.make_async_copy(w_hbm, w_ref, load_sem.at[0])
    load_dres = pltpu.make_async_copy(dres_hbm, dres_ref, load_sem.at[1])
    load_w.start()
    load_dres.start()
    greet(all_partners(core, plane, spot))

    def put(tile, piece, value):
        side, chunk = tile // HALF_TILES, tile % HALF_TILES
        packed_ref[
            piece * rows : (piece + 1) * rows,
            chunk * CHUNK + side * LANES : chunk * CHUNK + (side + 1) * LANES,
        ] = value.astype(BF16)

    for piece in range(pieces):
        seconds = []
        for goal in range(SPOTS):
            first = recv_ref[0, goal, piece, QUERIES].astype(F32)
            second = recv_ref[1, goal, piece, QUERIES].astype(F32)
            put(goal, piece, jnp.where(low, first, jnp.where(core == 0, first, second)))
            seconds.append(second)
            base = D // LANES + 3 * goal
            put(base, piece, recv_ref[0, goal, piece, KEYS_A])
            put(base + 1, piece, recv_ref[1, goal, piece, KEYS_A])
            put(base + 2, piece, recv_ref[core, goal, piece, KEYS_B])
        for number in range(2):
            put(
                SPOTS + number,
                piece,
                jnp.where(low, seconds[2 * number], swap_halves(seconds[2 * number + 1])),
            )

    load_w.wait()
    for chunk in range(HALF_TILES):
        columns = slice(chunk * CHUNK, (chunk + 1) * CHUNK)
        share = dot_rt(packed_ref[:, columns], w_ref[:, columns])
        if chunk == 0:
            dnormed_ref[...] = share
        else:
            dnormed_ref[...] += share
    normal, inverse = norm_parts(x_ref[...].reshape(tokens, D).astype(F32))
    dnormed = dnormed_ref[...]
    load_dres.wait()
    gradient = dres_ref[...] + norm_pull(dnormed, normal, inverse, vec_ref[0:1])
    gradient_ref[...] = gradient.astype(BF16).reshape(x_ref.shape)
    finish_grad = from_planes(gradient_ref, grad_ref, *move_sems)

    rows_ref[0:1] = jnp.sum(dnormed * normal, axis=0, keepdims=True)
    rows_ref[1:2] = jnp.sum(dnormed, axis=0, keepdims=True)
    rows_ref[2:6] = g_mid_ref[...]
    rows_ref[6:8] = jnp.zeros((2, D), F32)
    tiles_ref[...] = jnp.zeros_like(tiles_ref)
    for step in range(FF // CHUNK):
        tiles_ref[step : step + 1] = g_up_bias_ref[step]
    for chunk in range(HALF_TILES):
        number = FF // CHUNK + chunk
        tiles_ref[number : number + 1] = jnp.sum(
            packed_ref[:, chunk * CHUNK : (chunk + 1) * CHUNK].astype(F32), axis=0, keepdims=True
        )
    sums = Doubling((rows_ref, tiles_ref), (rows_box, tiles_box), sum_send, sum_recv)
    sums.start(0)

    width = HALF_TILES // PARTS * LANES
    reduces = [
        Reduce(
            sources[part],
            *buffers[7 * part : 7 * part + 7],
            g_qkv_ref.at[:, part * width : (part + 1) * width],
            (send_sem.at[part], recv_sem.at[part], local_sem.at[part]),
        )
        for part in range(PARTS)
    ]
    shard = D // RANKS
    normed_t = normed_ref[...].astype(F32).T.astype(BF16)
    for part in range(PARTS):
        for number in range(HALF_TILES // PARTS):
            chunk = part * (HALF_TILES // PARTS) + number
            values = dot(normed_t, packed_ref[:, chunk * CHUNK : (chunk + 1) * CHUNK])
            columns = slice(number * LANES, (number + 1) * LANES)
            for owner in range(RANKS):
                mine = values[owner * shard : (owner + 1) * shard]
                sources[part][
                    owner // (PLANES * SPOTS), owner // SPOTS % PLANES, owner % SPOTS, :, columns
                ] = jnp.concatenate([mine[:, :LANES], mine[:, LANES:]], axis=0).astype(BF16)
        reduces[part].start()
        if part > 0:
            reduces[part - 1].corners()
        if part > 1:
            reduces[part - 2].sides()
    sums.finish(0)
    sums.start(1)
    reduces[2].corners()
    reduces[1].sides()
    sums.finish(1)
    sums.start(2)
    reduces[0].columns()
    reduces[2].sides()
    sums.finish(2)
    sums.start(3)
    reduces[1].columns()
    sums.finish(3)
    sums.start(4)
    reduces[2].columns()
    sums.finish(4)
    for one in reduces:
        one.finish()
    rows_out_ref[...] = rows_ref[...]
    tiles_out_ref[...] = tiles_ref[...]
    finish_grad()


def finish_layer(recv, normed, x, dres, vec, w, g_mid, g_up_bias):
    pieces, rows, _ = x.shape
    tokens = pieces * rows
    shard = D // RANKS
    grid = (2, PLANES, SPOTS)
    part = grid + (2 * shard, HALF_TILES // PARTS * LANES)
    buffers = []
    for _ in range(PARTS):
        buffers += reduce_scratch(part, BF16)
    tiles = -(-(FF // CHUNK + HALF_TILES) // 8) * 8
    dma = pltpu.SemaphoreType.DMA
    return pl.pallas_call(
        finish_kernel,
        out_shape=(
            jax.ShapeDtypeStruct(x.shape, BF16),
            jax.ShapeDtypeStruct((2 * shard, 3 * D // 2), F32),
            jax.ShapeDtypeStruct((8, D), F32),
            jax.ShapeDtypeStruct((tiles, CHUNK), F32),
        ),
        in_specs=[
            whole(),
            whole(),
            whole(),
            whole(ANY),
            whole(),
            whole(ANY),
            whole(),
            whole(),
        ],
        out_specs=(whole(ANY), whole(), whole(), whole()),
        scratch_shapes=[VMEM(part, BF16)] * PARTS
        + buffers
        + [
            VMEM((tokens, 3 * D), BF16),
            VMEM((tokens, D), F32),
            VMEM(x.shape, BF16),
            VMEM((tokens, D), F32),
            VMEM(w.shape, BF16),
            VMEM((8, D), F32),
            VMEM((tiles, CHUNK), F32),
            VMEM((Doubling.STEPS, 8, D), F32),
            VMEM((Doubling.STEPS, tiles, CHUNK), F32),
            dma((PARTS, REDUCE_SEMS)),
            dma((PARTS, REDUCE_SEMS)),
            dma((PARTS, 4)),
            dma((2,)),
            dma((Doubling.STEPS, 2)),
            dma((Doubling.STEPS, 2)),
            dma((2,)),
            dma((2,)),
            dma((2,)),
        ],
        compiler_params=pltpu.CompilerParams(
            vmem_limit_bytes=60 * 1024 * 1024, collective_id=2, has_side_effects=True
        ),
        name="finish_layer",
    )(recv, normed, x, dres, vec, w, g_mid, g_up_bias)


def fold_columns(array):
    half = array.shape[1] // 2
    return jnp.concatenate([array[:, :half], array[:, half:]], axis=0)


def unfold_columns(array):
    half = array.shape[0] // 2
    return jnp.concatenate([array[:half], array[half:]], axis=1)


def plane_shards(
    hidden_in,
    rand_table,
    norm1_gain,
    norm1_bias,
    w_qkv,
    query_bias,
    value_bias,
    w_out,
    out_bias,
    norm2_gain,
    norm2_bias,
    w_up,
    up_bias,
    w_down,
    down_bias,
    cotangent,
):
    micro, rows, _ = hidden_in.shape
    local = rows // BLOCK
    own = norm1_gain.shape[0]
    order = [natural_block(entry) for entry in column_order()]
    inverse = [order.index(number) for number in range(len(order))]

    def in_row(vector, number):
        return jnp.pad(vector[None], ((number, 15 - number), (0, LANES - vector.shape[0])))

    vec = functools.reduce(
        jnp.add,
        [
            in_row(vector, number)
            for number, vector in enumerate(
                (
                    norm1_gain,
                    norm1_bias,
                    query_bias,
                    value_bias,
                    out_bias,
                    norm2_gain,
                    norm2_bias,
                    down_bias,
                    up_bias,
                )
            )
        ],
    )
    tab = jnp.pad(
        rand_table.reshape(micro, local * RANDOM), ((0, 8 - micro), (0, LANES - local * RANDOM))
    )
    (
        mixed,
        x,
        dy,
        w_down_all,
        w_qkv_all,
        w_out_all,
        w_up_all,
        qk,
        shared,
        normed,
        lse,
        vectors,
        up_shift,
        table,
        sorted_table,
    ) = front(hidden_in, cotangent, vec, tab, w_qkv, w_out, w_up, w_down)
    mixed = mixed.reshape(2, SPOTS, PIECES, rows, LANES)
    (
        hidden,
        grad_send,
        dres,
        g_out,
        half_up,
        half_down,
        last_up,
        last_down,
        g_up_bias,
        g_mid,
    ) = plane_middle(
        mixed,
        x,
        dy.reshape(micro * rows, D),
        vectors,
        w_out_all,
        up_shift,
        w_up_all,
        w_down_all.reshape(2, FF // 2, D),
    )
    grid = (2, PLANES, SPOTS)
    dqkv, hidden_out, t_out, t_up, t_down = plane_attention_back(
        table,
        sorted_table,
        qk,
        shared,
        grad_send.reshape(2, SPOTS, PIECES, local, BLOCK, LANES),
        lse,
        hidden,
        [
            g_out.reshape((1,) + grid + g_out.shape[1:]),
            last_up,
            last_down,
        ],
        half_up,
        half_down,
    )
    t_up = t_up.swapaxes(0, 1).reshape(2 * own, FF // 2)
    dqkv = dqkv.reshape(2, SPOTS, PIECES, 3, rows, LANES)
    grad_hidden, t_qkv, sum_rows, sum_tiles = finish_layer(
        dqkv, normed, x, dres, vectors, w_qkv_all, g_mid, g_up_bias
    )

    mine = lax.axis_index("gx") * PLANES * SPOTS + lax.axis_index("gy")
    sum_tiles = sum_tiles.reshape(-1, 2, LANES)
    g_bias = sum_tiles[FF // CHUNK : FF // CHUNK + HALF_TILES].swapaxes(0, 1).reshape(1, 3 * D)
    g_bias = take_blocks(g_bias, inverse)
    sum_rows = jnp.concatenate([sum_rows, g_bias[:, :D], g_bias[:, 2 * D :]], axis=0)
    parts = lax.dynamic_slice_in_dim(sum_rows, mine * own, own, 1)
    g_up_bias = sum_tiles[: FF // CHUNK].swapaxes(0, 1).reshape(FF)
    g_up_bias = lax.dynamic_slice_in_dim(g_up_bias, mine * (FF // RANKS), FF // RANKS, 0)
    return (
        hidden_out,
        grad_hidden.astype(F32),
        parts[0],
        parts[1],
        take_blocks(unfold_columns(t_qkv), inverse),
        parts[8],
        parts[9],
        unfold_columns(t_out),
        parts[5],
        parts[2],
        parts[3],
        unfold_columns(t_up),
        g_up_bias,
        t_down,
        parts[4],
    )


def shards(*arrays):
    micro, rows, _ = arrays[0].shape
    fits = lax.axis_size("gx") == 2 and lax.axis_size("gy") == PLANES * SPOTS
    fits = fits and micro == 2 and rows % BLOCK == 0
    return (plane_shards if fits else general_shards)(*arrays)


def solution(mesh):
    tokens = P(None, AXES, None)
    vector = P(AXES)
    matrix = P(AXES, None)
    placed = (
        tokens,
        tokens,
        vector,
        vector,
        matrix,
        vector,
        vector,
        matrix,
        vector,
        vector,
        vector,
        matrix,
        vector,
        matrix,
        vector,
        tokens,
    )
    returned = (
        tokens,
        tokens,
        vector,
        vector,
        matrix,
        vector,
        vector,
        matrix,
        vector,
        vector,
        vector,
        matrix,
        vector,
        matrix,
        vector,
    )
    return jax.shard_map(
        shards, mesh=mesh, in_specs=placed, out_specs=returned, check_vma=False
    )
```

```python
import functools

import jax
import jax.numpy as jnp
from jax import lax
from jax.experimental import pallas as pl
from jax.experimental.pallas import tpu as pltpu
from jax.sharding import PartitionSpec as P

HEADS = 12
HEAD_DIM = 64
D = 768
FF = 3072
BLOCK = 64
RANDOM = 3
LANES = 2 * HEAD_DIM
EPSILON = 1e-05
NEGATIVE = -1e30
SCALE = HEAD_DIM**-0.5
CHUNK = 256
SPAN = 8

F32 = jnp.float32
BF16 = jnp.bfloat16
VMEM = pltpu.VMEM


def whole(space=VMEM):
    return pl.BlockSpec(memory_space=space)


def params_of(megabytes):
    return pltpu.CompilerParams(vmem_limit_bytes=megabytes * 1024 * 1024)


def head_place(head):
    return (head // 3) * 4 + head % 3


def dot(left, right):
    return lax.dot_general(left, right, (((1,), (0,)), ((), ())), preferred_element_type=F32)


def dot_rt(left, right):
    return lax.dot_general(left, right, (((1,), (1,)), ((), ())), preferred_element_type=F32)


def dot_lt(left, right):
    return lax.dot_general(left, right, (((0,), (0,)), ((), ())), preferred_element_type=F32)


def swap_halves(tile):
    return pltpu.roll(tile, HEAD_DIM, axis=tile.ndim - 1)


def low_lanes(rows):
    return lax.broadcasted_iota(jnp.int32, (rows, LANES), 1) < HEAD_DIM


def norm_parts(values):
    centre = values - jnp.mean(values, axis=-1, keepdims=True)
    spread = jnp.mean(centre * centre, axis=-1, keepdims=True)
    inverse = lax.rsqrt(spread + EPSILON)
    return centre * inverse, inverse


def norm_pull(grad, normal, inverse, gain):
    scaled = grad * gain
    return inverse * (
        scaled
        - jnp.mean(scaled, axis=-1, keepdims=True)
        - normal * jnp.mean(scaled * normal, axis=-1, keepdims=True)
    )


def qkv_kernel(x_ref, gain_ref, shift_ref, w_ref, bias_ref, normed_ref, send_ref):
    micro, rows, _ = x_ref.shape
    values = x_ref[...].reshape(micro * rows, D).astype(F32)
    normal, _ = norm_parts(values)
    normed_ref[...] = (normal * gain_ref[...] + shift_ref[...]).astype(BF16)
    low = low_lanes(rows)
    for chunk in range(3 * D // CHUNK):
        columns = slice(chunk * CHUNK, (chunk + 1) * CHUNK)
        packed = dot(normed_ref[...], w_ref[:, columns]) + bias_ref[:, columns]
        if chunk < D // CHUNK:
            packed = packed.astype(BF16).astype(F32) * SCALE
        for tile in range(CHUNK // LANES):
            part = packed[:, tile * LANES : (tile + 1) * LANES]
            first, second = part[:rows], part[rows:]
            if chunk < D // CHUNK:
                head = (chunk * CHUNK // LANES + tile) * 2
                even = jnp.where(low, first, swap_halves(second))
                odd = jnp.where(low, swap_halves(first), second)
                send_ref[head_place(head), 0] = even.astype(BF16)
                send_ref[head_place(head + 1), 0] = odd.astype(BF16)
            else:
                head = (chunk * CHUNK - D) // LANES + tile
                send_ref[head_place(head), 1] = first.astype(BF16)
                send_ref[head_place(head), 2] = swap_halves(second).astype(BF16)


def qkv_forward(x, gain, shift, w, bias, groups):
    micro, rows, _ = x.shape
    return pl.pallas_call(
        qkv_kernel,
        out_shape=(
            jax.ShapeDtypeStruct((micro * rows, D), BF16),
            jax.ShapeDtypeStruct((groups, 3, rows, LANES), BF16),
        ),
        in_specs=[whole()] * 5,
        out_specs=(whole(), whole()),
        compiler_params=params_of(48),
        name="qkv_forward",
    )(x, gain, shift, w, bias)


def half_mask(low_half):
    lane = lax.broadcasted_iota(jnp.int32, (1, LANES), 1)
    keep = (lane < HEAD_DIM) if low_half else (lane >= HEAD_DIM)
    return jnp.where(keep, 1.0, 0.0).astype(BF16)


def inner_slots(pick, block, blocks):
    ids, bias = picked_slots([pick(block, number) for number in range(RANDOM)], block, blocks)
    edge = (block == 0) | (block == blocks - 1)
    ids[0] = jnp.maximum(ids[0], 0)
    ids[2] = jnp.minimum(ids[2], blocks - 1)
    return ids, bias + jnp.where(edge, NEGATIVE, 0.0).astype(F32)


def slots_of(table_ref, micro, block, blocks):
    picks = [table_ref[micro, block * RANDOM + number] for number in range(RANDOM)]
    return picked_slots(picks, block, blocks)


def picked_slots(picks, block, blocks):
    last = blocks - 1
    ids = [block - 1, block, block + 1, 0, last] + picks
    dropped = [None, None, None, block == 1, block == last - 1]
    for number in range(RANDOM):
        pick = picks[number]
        bad = (jnp.abs(pick - block) <= 1) | (pick == 0) | (pick == last)
        for earlier in range(number):
            bad = bad | (pick == picks[earlier])
        dropped.append(bad)
    lane = lax.broadcasted_iota(jnp.int32, (1, LANES), 1)
    tiles = []
    for pair in range(len(ids) // 2):
        level = [
            0.0 if bad is None else jnp.where(bad, NEGATIVE, 0.0).astype(F32)
            for bad in dropped[2 * pair : 2 * pair + 2]
        ]
        tiles.append(jnp.where(lane < HEAD_DIM, level[0], level[1]))
    return ids, jnp.concatenate(tiles, axis=1)


def attend_kernel(table_ref, qkv_ref, out_ref, lse_ref, s_ref):
    groups, _, local, _, _ = qkv_ref.shape
    blocks = groups * local
    low = low_lanes(BLOCK)
    masks = [half_mask(True), half_mask(False)]

    def load(component, block):
        return qkv_ref[block // local, component, block % local]

    def sparse(block, carry):
        mixed, logs = [], []
        for micro in range(2):
            ids, bias = slots_of(table_ref, micro, block, blocks)
            keys = jnp.concatenate([load(1 + micro, spot) for spot in ids], axis=0)
            query = load(0, block) * masks[micro]
            scores = dot_rt(query, keys) + bias
            top = jnp.max(scores, axis=1, keepdims=True)
            powered = jnp.exp(scores - top)
            total = jnp.sum(powered, axis=1, keepdims=True)
            mixed.append(dot(powered.astype(BF16), keys) * (1.0 / total))
            logs.append(top + jnp.log(total))
        out_ref[block // local, block % local] = jnp.where(low, mixed[1], mixed[0]).astype(BF16)
        lse_ref[block] = jnp.where(low, logs[0], logs[1])
        return carry

    lax.fori_loop(1, blocks - 1, sparse, 0)

    spans = blocks // SPAN
    ends = (0, blocks - 1)
    results = []
    for micro in range(2):
        query = jnp.concatenate([load(0, end) for end in ends], axis=0) * masks[micro]

        def keys_at(span, micro=micro):
            return jnp.concatenate(
                [load(1 + micro, span * SPAN + spot) for spot in range(SPAN)], axis=0
            )

        def first_pass(span, top, query=query, keys_at=keys_at):
            scores = dot_rt(query, keys_at(span))
            s_ref[span] = scores
            return jnp.maximum(top, jnp.max(scores, axis=1, keepdims=True))

        top = lax.fori_loop(0, spans, first_pass, jnp.full((2 * BLOCK, 1), NEGATIVE, F32))

        def second_pass(span, carry, top=top, keys_at=keys_at):
            total, mixed = carry
            powered = jnp.exp(s_ref[span] - top)
            return (
                total + jnp.sum(powered, axis=1, keepdims=True),
                mixed + dot(powered.astype(BF16), keys_at(span)),
            )

        total, mixed = lax.fori_loop(
            0,
            spans,
            second_pass,
            (jnp.zeros((2 * BLOCK, 1), F32), jnp.zeros((2 * BLOCK, LANES), F32)),
        )
        results.append((mixed * (1.0 / total), top + jnp.log(total)))
    for place, end in enumerate(ends):
        rows = slice(place * BLOCK, (place + 1) * BLOCK)
        out_ref[end // local, end % local] = jnp.where(
            low, results[1][0][rows], results[0][0][rows]
        ).astype(BF16)
        lse_ref[end] = jnp.where(low, results[0][1][rows], results[1][1][rows])


def attention_forward(table, qkv):
    groups, _, local, _, _ = qkv.shape
    blocks = groups * local
    return pl.pallas_call(
        attend_kernel,
        out_shape=(
            jax.ShapeDtypeStruct((groups, local, BLOCK, LANES), BF16),
            jax.ShapeDtypeStruct((blocks, BLOCK, LANES), F32),
        ),
        in_specs=[whole(pltpu.SMEM), whole()],
        out_specs=(whole(), whole()),
        scratch_shapes=[VMEM((blocks // SPAN, 2 * BLOCK, SPAN * BLOCK), F32)],
        compiler_params=params_of(48),
        name="attention_forward",
    )(table, qkv)


def attend_back_kernel(table_ref, qkv_ref, grad_ref, lse_ref, out_ref, sums_ref, p_ref, dp_ref):
    groups, _, local, _, _ = qkv_ref.shape
    blocks = groups * local
    low = low_lanes(BLOCK)
    masks = [half_mask(True), half_mask(False)]

    def load(component, block):
        return qkv_ref[block // local, component, block % local]

    def load_grad(block):
        return grad_ref[block // local, block % local]

    def clear(block, carry):
        for micro in range(2):
            sums_ref[micro, block] = jnp.zeros((BLOCK, LANES), F32)
        return carry

    lax.fori_loop(0, blocks, clear, 0)

    def sparse(block, carry):
        grads = []
        for micro in range(2):
            ids, bias = slots_of(table_ref, micro, block, blocks)
            keys = jnp.concatenate([load(1 + micro, spot) for spot in ids], axis=0)
            both = jnp.concatenate(
                [load(0, block) * masks[micro], load_grad(block) * masks[1 - micro]], axis=0
            )
            products = dot_rt(both, keys)
            logs = lse_ref[block][:, micro * HEAD_DIM : micro * HEAD_DIM + 1]
            weights = jnp.exp(products[:BLOCK] + bias - logs)
            grad_weights = products[BLOCK:]
            delta = jnp.sum(weights * grad_weights, axis=1, keepdims=True)
            grad_scores = weights * (grad_weights - delta)
            stacked = jnp.concatenate([grad_scores, weights], axis=0).astype(BF16)
            grads.append(dot(stacked[:BLOCK], keys))
            shares = dot_lt(stacked, both)
            for place, spot in enumerate(ids):
                sums_ref[micro, spot] += shares[place * BLOCK : (place + 1) * BLOCK]
        out_ref[block // local, 0, block % local] = (
            jnp.where(low, grads[0], grads[1]) * SCALE
        ).astype(BF16)
        return carry

    lax.fori_loop(1, blocks - 1, sparse, 0)

    spans = blocks // SPAN
    ends = (0, blocks - 1)
    results = []
    for micro in range(2):
        query = jnp.concatenate([load(0, end) for end in ends], axis=0) * masks[micro]
        grad = jnp.concatenate([load_grad(end) for end in ends], axis=0) * masks[1 - micro]
        both = jnp.concatenate([query, grad], axis=0)
        logs = jnp.concatenate(
            [lse_ref[end][:, micro * HEAD_DIM : micro * HEAD_DIM + 1] for end in ends], axis=0
        )

        def keys_at(span, micro=micro):
            return jnp.concatenate(
                [load(1 + micro, span * SPAN + spot) for spot in range(SPAN)], axis=0
            )

        def first_pass(span, delta, both=both, logs=logs, keys_at=keys_at):
            products = dot_rt(both, keys_at(span))
            weights = jnp.exp(products[: 2 * BLOCK] - logs)
            grad_weights = products[2 * BLOCK :]
            p_ref[span] = weights
            dp_ref[span] = grad_weights
            return delta + jnp.sum(weights * grad_weights, axis=1, keepdims=True)

        delta = lax.fori_loop(0, spans, first_pass, jnp.zeros((2 * BLOCK, 1), F32))

        def second_pass(span, carry, delta=delta, both=both, keys_at=keys_at, micro=micro):
            weights = p_ref[span]
            grad_scores = weights * (dp_ref[span] - delta)
            stacked = jnp.concatenate([grad_scores, weights], axis=0).astype(BF16)
            shares = dot_lt(stacked, both)
            for spot in range(SPAN):
                sums_ref[micro, span * SPAN + spot] += shares[spot * BLOCK : (spot + 1) * BLOCK]
            return carry + dot(stacked[: 2 * BLOCK], keys_at(span))

        results.append(
            lax.fori_loop(0, spans, second_pass, jnp.zeros((2 * BLOCK, LANES), F32))
        )
    for place, end in enumerate(ends):
        rows = slice(place * BLOCK, (place + 1) * BLOCK)
        out_ref[end // local, 0, end % local] = (
            jnp.where(low, results[0][rows], results[1][rows]) * SCALE
        ).astype(BF16)

    def finish(block, carry):
        for micro in range(2):
            out_ref[block // local, 1 + micro, block % local] = sums_ref[micro, block].astype(BF16)
        return carry

    lax.fori_loop(0, blocks, finish, 0)


def attention_backward(table, qkv, grad, lse):
    groups, _, local, _, _ = qkv.shape
    blocks = groups * local
    spans = VMEM((blocks // SPAN, 2 * BLOCK, SPAN * BLOCK), F32)
    return pl.pallas_call(
        attend_back_kernel,
        out_shape=jax.ShapeDtypeStruct(qkv.shape, BF16),
        in_specs=[whole(pltpu.SMEM), whole(), whole(), whole()],
        out_specs=whole(),
        scratch_shapes=[VMEM((2, blocks, BLOCK, LANES), F32), spans, spans],
        compiler_params=params_of(48),
        name="attention_backward",
    )(table, qkv, grad, lse)


def middle_kernel(
    mixed_in_ref,
    x_ref,
    dy_ref,
    w_out_ref,
    out_shift_ref,
    gain_ref,
    shift_ref,
    up_shift_ref,
    down_shift_ref,
    w_up_ref,
    w_down_ref,
    hidden_ref,
    send_ref,
    dres_ref,
    g_out_ref,
    g_up_ref,
    g_down_ref,
    g_up_bias_ref,
    g_small_ref,
    mixed_ref,
    residual_ref,
    second_ref,
    second_t_ref,
    total_ref,
    dsecond_ref,
):
    micro, rows, _ = x_ref.shape
    step = pl.program_id(0)
    low = low_lanes(rows)

    @pl.when(step == 0)
    def _():
        for pair in range(HEADS // 2):
            even = mixed_in_ref[head_place(2 * pair)].astype(F32)
            odd = mixed_in_ref[head_place(2 * pair + 1)].astype(F32)
            columns = slice(pair * LANES, (pair + 1) * LANES)
            mixed_ref[:rows, columns] = jnp.where(low, swap_halves(even), odd).astype(BF16)
            mixed_ref[rows:, columns] = jnp.where(low, even, swap_halves(odd)).astype(BF16)
        residual = x_ref[...].reshape(micro * rows, D).astype(F32) + (
            dot(mixed_ref[...], w_out_ref[...]) + out_shift_ref[...]
        )
        residual_ref[...] = residual
        normal, _ = norm_parts(residual)
        second = normal * gain_ref[...] + shift_ref[...]
        second_ref[...] = second.astype(BF16)
        second_t_ref[...] = second.T.astype(BF16)
        total_ref[...] = jnp.zeros_like(total_ref)
        dsecond_ref[...] = jnp.zeros_like(dsecond_ref)

    upper = dot(second_ref[...], w_up_ref[...]) + up_shift_ref[...]
    factor = 0.7978845608028654
    square = upper * upper
    bent = jnp.tanh(factor * (upper + 0.044715 * (upper * square)))
    half = 0.5 * (1.0 + bent)
    active = (upper * half).astype(BF16)
    slope = half + 0.5 * upper * (1.0 - bent * bent) * (
        factor + (3.0 * 0.044715 * factor) * square
    )
    dy = dy_ref[...]
    total_ref[...] += dot(active, w_down_ref[...])
    g_down_ref[...] = dot_lt(active, dy).astype(g_down_ref.dtype)
    dupper = (dot_rt(dy, w_down_ref[...]) * slope).astype(BF16)
    g_up_bias_ref[...] = jnp.sum(dupper.astype(F32), axis=0, keepdims=True)
    g_up_ref[...] = dot(second_t_ref[...], dupper).astype(g_up_ref.dtype)
    dsecond_ref[...] += dot_rt(dupper, w_up_ref[...])

    @pl.when(step == pl.num_programs(0) - 1)
    def _():
        residual = residual_ref[...]
        hidden_ref[...] = (
            (residual + (total_ref[...] + down_shift_ref[...])).astype(BF16).reshape(x_ref.shape)
        )
        normal, inverse = norm_parts(residual)
        dsecond = dsecond_ref[...]
        grad_out = dy_ref[...].astype(F32)
        g_small_ref[0:1] = jnp.sum(dsecond * normal, axis=0, keepdims=True)
        g_small_ref[1:2] = jnp.sum(dsecond, axis=0, keepdims=True)
        g_small_ref[2:3] = jnp.sum(grad_out, axis=0, keepdims=True)
        dres = grad_out + norm_pull(dsecond, normal, inverse, gain_ref[...])
        dres_ref[...] = dres
        branch = dres.astype(BF16)
        g_small_ref[3:4] = jnp.sum(branch.astype(F32), axis=0, keepdims=True)
        g_out_ref[...] = dot_lt(mixed_ref[...], branch).astype(g_out_ref.dtype)
        dmixed = dot_rt(branch, w_out_ref[...])
        for pair in range(HEADS // 2):
            part = dmixed[:, pair * LANES : (pair + 1) * LANES]
            first, last = part[:rows], part[rows:]
            even = jnp.where(low, last, swap_halves(first))
            odd = jnp.where(low, swap_halves(last), first)
            send_ref[head_place(2 * pair)] = even.astype(BF16)
            send_ref[head_place(2 * pair + 1)] = odd.astype(BF16)


def middle(mixed_in, x, dy, w_out, out_shift, gain, shift, up_shift, down_shift, w_up, w_down, kind):
    micro, rows, _ = x.shape
    tokens = micro * rows
    groups = mixed_in.shape[0]

    def fixed(shape):
        return pl.BlockSpec(shape, lambda step: (0,) * len(shape))

    vector = fixed((1, D))
    steps = FF // CHUNK
    return pl.pallas_call(
        middle_kernel,
        grid=(steps,),
        out_shape=(
            jax.ShapeDtypeStruct(x.shape, BF16),
            jax.ShapeDtypeStruct((groups, rows, LANES), BF16),
            jax.ShapeDtypeStruct((tokens, D), F32),
            jax.ShapeDtypeStruct((D, D), kind),
            jax.ShapeDtypeStruct((D, FF), kind),
            jax.ShapeDtypeStruct((FF, D), kind),
            jax.ShapeDtypeStruct((1, FF), F32),
            jax.ShapeDtypeStruct((4, D), F32),
        ),
        in_specs=[
            fixed(mixed_in.shape),
            fixed(x.shape),
            fixed((tokens, D)),
            fixed((D, D)),
            vector,
            vector,
            vector,
            pl.BlockSpec((1, CHUNK), lambda step: (0, step)),
            vector,
            pl.BlockSpec((D, CHUNK), lambda step: (0, step)),
            pl.BlockSpec((CHUNK, D), lambda step: (step, 0)),
        ],
        out_specs=(
            fixed(x.shape),
            fixed((groups, rows, LANES)),
            fixed((tokens, D)),
            fixed((D, D)),
            pl.BlockSpec((D, CHUNK), lambda step: (0, step)),
            pl.BlockSpec((CHUNK, D), lambda step: (step, 0)),
            pl.BlockSpec((1, CHUNK), lambda step: (0, step)),
            fixed((4, D)),
        ),
        scratch_shapes=[
            VMEM((tokens, D), BF16),
            VMEM((tokens, D), F32),
            VMEM((tokens, D), BF16),
            VMEM((D, tokens), BF16),
            VMEM((tokens, D), F32),
            VMEM((tokens, D), F32),
        ],
        compiler_params=params_of(56),
        name="middle",
    )(mixed_in, x, dy, w_out, out_shift, gain, shift, up_shift, down_shift, w_up, w_down)


def qkv_back_kernel(
    recv_ref,
    normed_ref,
    x_ref,
    dres_ref,
    gain_ref,
    w_ref,
    grad_ref,
    g_qkv_ref,
    g_bias_ref,
    g_small_ref,
    packed_ref,
    normed_t_ref,
    dnormed_ref,
):
    micro, rows, _ = x_ref.shape
    step = pl.program_id(0)
    low = low_lanes(rows)

    @pl.when(step == 0)
    def _():
        for pair in range(HEADS // 2):
            even = recv_ref[head_place(2 * pair), 0].astype(F32)
            odd = recv_ref[head_place(2 * pair + 1), 0].astype(F32)
            spot, columns = pair // 2, slice((pair % 2) * LANES, (pair % 2 + 1) * LANES)
            packed_ref[spot, :rows, columns] = jnp.where(low, even, swap_halves(odd)).astype(BF16)
            packed_ref[spot, rows:, columns] = jnp.where(low, swap_halves(even), odd).astype(BF16)
        for head in range(HEADS):
            spot = D // CHUNK + head // 2
            columns = slice((head % 2) * LANES, (head % 2 + 1) * LANES)
            packed_ref[spot, :rows, columns] = recv_ref[head_place(head), 1]
            packed_ref[spot, rows:, columns] = swap_halves(
                recv_ref[head_place(head), 2].astype(F32)
            ).astype(BF16)
        normed_t_ref[...] = normed_ref[...].astype(F32).T.astype(BF16)
        dnormed_ref[...] = jnp.zeros_like(dnormed_ref)

    packed = packed_ref[step]
    g_bias_ref[...] = jnp.sum(packed.astype(F32), axis=0, keepdims=True)
    g_qkv_ref[...] = dot(normed_t_ref[...], packed).astype(g_qkv_ref.dtype)
    dnormed_ref[...] += dot_rt(packed, w_ref[...])

    @pl.when(step == pl.num_programs(0) - 1)
    def _():
        normal, inverse = norm_parts(x_ref[...].reshape(micro * rows, D).astype(F32))
        dnormed = dnormed_ref[...]
        g_small_ref[0:1] = jnp.sum(dnormed * normal, axis=0, keepdims=True)
        g_small_ref[1:2] = jnp.sum(dnormed, axis=0, keepdims=True)
        grad = dres_ref[...] + norm_pull(dnormed, normal, inverse, gain_ref[...])
        grad_ref[...] = grad.reshape(x_ref.shape)


def qkv_backward(recv, normed, x, dres, gain, w, kind):
    micro, rows, _ = x.shape
    tokens = micro * rows

    def fixed(shape):
        return pl.BlockSpec(shape, lambda step: (0,) * len(shape))

    steps = 3 * D // CHUNK
    return pl.pallas_call(
        qkv_back_kernel,
        grid=(steps,),
        out_shape=(
            jax.ShapeDtypeStruct(x.shape, F32),
            jax.ShapeDtypeStruct((D, 3 * D), kind),
            jax.ShapeDtypeStruct((1, 3 * D), F32),
            jax.ShapeDtypeStruct((2, D), F32),
        ),
        in_specs=[
            fixed(recv.shape),
            fixed((tokens, D)),
            fixed(x.shape),
            fixed((tokens, D)),
            fixed((1, D)),
            pl.BlockSpec((D, CHUNK), lambda step: (0, step)),
        ],
        out_specs=(
            fixed(x.shape),
            pl.BlockSpec((D, CHUNK), lambda step: (0, step)),
            pl.BlockSpec((1, CHUNK), lambda step: (0, step)),
            fixed((2, D)),
        ),
        scratch_shapes=[
            VMEM((steps, tokens, CHUNK), BF16),
            VMEM((D, tokens), BF16),
            VMEM((tokens, D), F32),
        ],
        compiler_params=params_of(56),
        name="qkv_backward",
    )(recv, normed, x, dres, gain, w)


AXES = ("gx", "gy")


def gather(array):
    return lax.all_gather(array, AXES, axis=0, tiled=True)


def scatter(array):
    return lax.psum_scatter(array, AXES, scatter_dimension=0, tiled=True)


def exchange(array):
    return lax.all_to_all(array, "gy", 0, 0, tiled=True)


def by_heads(w_qkv):
    rows = w_qkv.shape[0]
    sides = w_qkv[:, D:].reshape(rows, 2, HEADS, HEAD_DIM)
    return jnp.concatenate([w_qkv[:, :D], jnp.swapaxes(sides, 1, 2).reshape(rows, 2 * D)], axis=1)


def by_parts(w_qkv):
    rows = w_qkv.shape[0]
    sides = w_qkv[:, D:].reshape(rows, HEADS, 2, HEAD_DIM)
    return jnp.concatenate([w_qkv[:, :D], jnp.swapaxes(sides, 1, 2).reshape(rows, 2 * D)], axis=1)


def general_shards(
    hidden_in,
    rand_table,
    norm1_gain,
    norm1_bias,
    w_qkv,
    query_bias,
    value_bias,
    w_out,
    out_bias,
    norm2_gain,
    norm2_bias,
    w_up,
    up_bias,
    w_down,
    down_bias,
    cotangent,
):
    micro, rows, _ = hidden_in.shape
    groups = lax.axis_size("gy")
    local = rows // BLOCK
    own = norm1_gain.shape[0]

    vectors = jnp.concatenate(
        [
            norm1_gain,
            norm1_bias,
            query_bias,
            value_bias,
            out_bias,
            norm2_gain,
            norm2_bias,
            down_bias,
            up_bias,
        ]
    )
    table = lax.all_gather(rand_table, "gy", axis=1, tiled=True)
    table = table.reshape(micro, groups * local * RANDOM)
    vectors = gather(vectors[None]).astype(F32)
    gain_one, shift_one, query_shift, value_shift, out_shift, gain_two, shift_two, down_shift = (
        vectors[:, number * own : (number + 1) * own].reshape(1, D) for number in range(8)
    )
    up_shift = vectors[:, 8 * own :].reshape(1, FF)
    w_qkv_full = gather(by_heads(w_qkv))
    w_out_full, w_up_full, w_down_full = gather(w_out), gather(w_up), gather(w_down)
    packed_bias = by_heads(
        jnp.concatenate([query_shift, jnp.zeros_like(query_shift), value_shift], axis=1)
    )

    normed, send = qkv_forward(hidden_in, gain_one, shift_one, w_qkv_full, packed_bias, groups)
    qkv = exchange(send).reshape(groups, 3, local, BLOCK, LANES)
    mixed, lse = attention_forward(table, qkv)
    mixed_back = exchange(mixed.reshape(groups, rows, LANES))
    hidden_out, grad_send, dres, g_out, g_up, g_down, g_up_bias, g_mid = middle(
        mixed_back,
        hidden_in,
        cotangent.reshape(micro * rows, D),
        w_out_full,
        out_shift,
        gain_two,
        shift_two,
        up_shift,
        down_shift,
        w_up_full,
        w_down_full,
        F32,
    )
    grad_mixed = exchange(grad_send).reshape(groups, local, BLOCK, LANES)
    dqkv = attention_backward(table, qkv, grad_mixed, lse)
    dqkv_back = exchange(dqkv.reshape(groups, 3, rows, LANES))
    grad_hidden, g_qkv, g_packed, g_first = qkv_backward(
        dqkv_back, normed, hidden_in, dres, gain_one, w_qkv_full, F32
    )

    g_packed = by_parts(g_packed)
    small = [
        g_first[0],
        g_first[1],
        g_packed[0, :D],
        g_packed[0, 2 * D :],
        g_mid[3],
        g_mid[0],
        g_mid[1],
        g_mid[2],
    ]
    ranks = D // own
    small = jnp.concatenate(
        [item.reshape(ranks, own) for item in small] + [g_up_bias.reshape(ranks, 4 * own)], axis=1
    )
    small = scatter(small)[0]
    parts = [small[number * own : (number + 1) * own] for number in range(8)]
    return (
        hidden_out,
        grad_hidden,
        parts[0],
        parts[1],
        by_parts(scatter(g_qkv)),
        parts[2],
        parts[3],
        scatter(g_out),
        parts[4],
        parts[5],
        parts[6],
        scatter(g_up),
        small[8 * own :],
        scatter(g_down),
        parts[7],
    )


MESH = pl.DeviceIdType.MESH
ANY = pl.ANY
PLANES = 4
SPOTS = 4
PIECES = 2
RANKS = 2 * PLANES * SPOTS
TILES = 3 * D // LANES
HALF_TILES = TILES // 2
QUERY_ORDER = (0, 2, 3, 5, 6, 8, 9, 11, 1, 4, 7, 10)


def column_order():
    order = [("q", head) for head in QUERY_ORDER]
    for spot in range(SPOTS):
        for place in (2 * 3 * spot, 2 * 3 * spot + 2):
            order += [("k", place // 2), ("v", place // 2)]
        order += [("v", 3 * spot + 2), ("k", 3 * spot + 2)]
    return order


def natural_block(entry):
    return "qkv".index(entry[0]) * HEADS + entry[1]


def flip(value, bits):
    if bits == 0:
        return value
    if bits == 1:
        return value + 1 - 2 * lax.rem(value, 2)
    if bits == 2:
        return value + 2 - 4 * lax.div(value, 2)
    return 3 - value


def place_here():
    core, rank = lax.axis_index("gx"), lax.axis_index("gy")
    return core, lax.div(rank, SPOTS), lax.rem(rank, SPOTS)


def rank_of(plane, spot):
    return plane * SPOTS + spot


def greet(partners):
    barrier = pltpu.get_barrier_semaphore()
    for partner in partners:
        pl.semaphore_signal(barrier, inc=1, device_id=partner, device_id_type=MESH)
    pl.semaphore_wait(barrier, len(partners))


def remote(source, target, send_sem, recv_sem, device):
    return pltpu.make_async_remote_copy(
        src_ref=source,
        dst_ref=target,
        send_sem=send_sem,
        recv_sem=recv_sem,
        device_id=device,
        device_id_type=MESH,
    )


def column_partners(core, plane, spot):
    partners = [(1 - core, rank_of(plane, spot))]
    for bits in range(1, PLANES):
        for other in (core, 1 - core):
            partners.append((other, rank_of(flip(plane, bits), spot)))
    return partners


def all_partners(core, plane, spot):
    return column_partners(core, plane, spot) + [
        (core, rank_of(plane, flip(spot, 1))),
        (core, rank_of(plane, flip(spot, 2))),
    ]


def to_planes(source, target, send_sem, recv_sem, local_sem):
    core, plane, spot = place_here()
    half, odd = lax.div(plane, 2), lax.rem(plane, 2)
    sends, keeps = [], []
    for micro in range(2):
        goal = 2 * micro + core
        here = (goal == plane) & (half == core)
        send = remote(
            source.at[micro],
            target.at[odd],
            send_sem.at[micro],
            recv_sem.at[odd],
            (half, rank_of(goal, spot)),
        )
        keep = pltpu.make_async_copy(source.at[micro], target.at[odd], local_sem.at[micro])

        @pl.when(jnp.logical_not(here))
        def _(send=send):
            send.start()

        @pl.when(here)
        def _(keep=keep):
            keep.start()

        sends.append((here, send))
        keeps.append((here, keep))

    def finish():
        for piece in range(PIECES):
            mine = (odd == core) & (plane == 2 * core + piece)
            arrival = remote(
                source.at[0],
                target.at[piece],
                send_sem.at[0],
                recv_sem.at[piece],
                (core, rank_of(plane, spot)),
            )

            @pl.when(jnp.logical_not(mine))
            def _(arrival=arrival):
                arrival.wait_recv()

        for (here, send), (_, keep) in zip(sends, keeps):

            @pl.when(jnp.logical_not(here))
            def _(send=send):
                send.wait_send()

            @pl.when(here)
            def _(keep=keep):
                keep.wait()

    return finish


def from_planes(source, target, send_sem, recv_sem, local_sem):
    core, plane, spot = place_here()
    micro, odd = lax.div(plane, 2), lax.rem(plane, 2)
    sends, keeps = [], []
    for piece in range(PIECES):
        goal = 2 * core + piece
        here = (goal == plane) & (odd == core)
        send = remote(
            source.at[piece],
            target.at[micro],
            send_sem.at[piece],
            recv_sem.at[micro],
            (odd, rank_of(goal, spot)),
        )
        keep = pltpu.make_async_copy(source.at[piece], target.at[micro], local_sem.at[piece])

        @pl.when(jnp.logical_not(here))
        def _(send=send):
            send.start()

        @pl.when(here)
        def _(keep=keep):
            keep.start()

        sends.append((here, send))
        keeps.append((here, keep))

    def finish():
        for number in range(2):
            mine = (2 * number + core == plane) & (micro == core)
            arrival = remote(
                source.at[0],
                target.at[number],
                send_sem.at[0],
                recv_sem.at[number],
                (core, rank_of(plane, spot)),
            )

            @pl.when(jnp.logical_not(mine))
            def _(arrival=arrival):
                arrival.wait_recv()

        for (here, send), (_, keep) in zip(sends, keeps):

            @pl.when(jnp.logical_not(here))
            def _(send=send):
                send.wait_send()

            @pl.when(here)
            def _(keep=keep):
                keep.wait()

    return finish


class Gather:
    SENDS = 31

    def __init__(self, source, target, send_sem, recv_sem, local_sem):
        self.source, self.target = source, target
        self.send_sem, self.recv_sem = send_sem, recv_sem
        self.core, self.plane, self.spot = place_here()
        self.sends = []
        self.own = pltpu.make_async_copy(
            source, target.at[self.core, self.plane, self.spot], local_sem
        )
        self.own.start()

    def send(self, source, plane, spot, device):
        copy = remote(
            source,
            self.target.at[self.core, plane, spot],
            self.send_sem.at[len(self.sends)],
            self.recv_sem.at[self.core, plane, spot],
            device,
        )
        copy.start()
        self.sends.append(copy)

    def arrive(self, core, plane, spot):
        shard = self.target.at[core, plane, spot]
        remote(
            shard,
            shard,
            self.send_sem.at[0],
            self.recv_sem.at[core, plane, spot],
            (self.core, rank_of(self.plane, self.spot)),
        ).wait_recv()

    def neighbour(self, bits):
        return (self.core, rank_of(self.plane, flip(self.spot, bits)))

    def sibling(self):
        return (1 - self.core, rank_of(self.plane, self.spot))

    def start(self):
        for bits in range(1, PLANES):
            goal = (self.core, rank_of(flip(self.plane, bits), self.spot))
            self.send(self.source, self.plane, self.spot, goal)
        for goal in (self.neighbour(1), self.neighbour(2), self.sibling()):
            self.send(self.source, self.plane, self.spot, goal)

    def column(self):
        for bits in range(1, PLANES):
            plane = flip(self.plane, bits)
            self.arrive(self.core, plane, self.spot)
            shard = self.target.at[self.core, plane, self.spot]
            for goal in (self.neighbour(1), self.neighbour(2), self.sibling()):
                self.send(shard, plane, self.spot, goal)

    def across(self):
        for bits in range(PLANES):
            plane = flip(self.plane, bits)
            for side in (1, 2):
                spot = flip(self.spot, side)
                self.arrive(self.core, plane, spot)
                shard = self.target.at[self.core, plane, spot]
                if (side == 1) == (bits < 2):
                    self.send(shard, plane, spot, self.neighbour(3 - side))
                self.send(shard, plane, spot, self.sibling())

    def corner(self):
        spot = flip(self.spot, 3)
        for bits in range(PLANES):
            plane = flip(self.plane, bits)
            self.arrive(self.core, plane, spot)
            self.send(self.target.at[self.core, plane, spot], plane, spot, self.sibling())

    def finish(self):
        for bits in range(PLANES):
            for side in range(SPOTS):
                self.arrive(1 - self.core, flip(self.plane, bits), flip(self.spot, side))
        self.own.wait()
        for copy in self.sends:
            copy.wait_send()


def settle(shards_ref, plan):
    rows = shards_ref.shape[3] // 2

    def pair(number, carry):
        core, plane, side = (
            lax.div(number, 2 * PLANES),
            lax.rem(lax.div(number, 2), PLANES),
            lax.rem(number, 2),
        )
        goal = pl.ds(pl.multiple_of(number * 2 * rows, 16), 2 * rows)
        for tile, out_ref, (left, right) in plan:
            columns = slice(tile * LANES, (tile + 1) * LANES)
            first = shards_ref[core, plane, 2 * side, :, columns].astype(F32)
            second = shards_ref[core, plane, 2 * side + 1, :, columns].astype(F32)
            out_ref[goal, left * LANES : (left + 1) * LANES] = jnp.concatenate(
                [first[:rows], second[:rows]], axis=0
            ).astype(BF16)
            out_ref[goal, right * LANES : (right + 1) * LANES] = jnp.concatenate(
                [first[rows:], second[rows:]], axis=0
            ).astype(BF16)
        return carry

    lax.fori_loop(0, RANKS // 2, pair, 0)


def alternate(tile):
    return 2 * tile, 2 * tile + 1


def plane_partners(core, plane, spot):
    partners = []
    for other in (core, 1 - core):
        for side in range(SPOTS):
            if other is core and side == 0:
                continue
            partners.append((other, rank_of(plane, flip(spot, side))))
    return partners


def both_partners(core, plane, spot):
    return plane_partners(core, plane, spot) + column_partners(core, plane, spot)[1:]


def exchange_sems(recv_shape):
    return [
        pltpu.SemaphoreType.DMA((14,)),
        pltpu.SemaphoreType.DMA(recv_shape),
        pltpu.SemaphoreType.DMA((PIECES,)),
    ]


def sort_entries(table, sorted_ref, entries):
    count = table.shape[1]
    core = lax.axis_index("gx")
    lane = lax.broadcasted_iota(jnp.int32, (count, count), 1)
    row = lax.broadcasted_iota(jnp.int32, (count, count), 0).astype(F32)
    everything = jnp.broadcast_to(table, (count, count))
    half = entries // 2
    inside = (lane >= core * half) & (lane < (core + 1) * half)
    lane = lane.astype(F32)
    for number, along in enumerate((everything, jnp.where(inside, everything, 2.0 * LANES))):
        down = along.T
        before = (along < down) | ((along == down) & (lane < row))
        rank = jnp.sum(jnp.where(before, 1.0, 0.0), axis=1, keepdims=True)
        order = jnp.sum(jnp.where(rank == lane, row, 0.0), axis=0, keepdims=True)
        upto = jnp.sum(jnp.where(down <= lane, 1.0, 0.0), axis=0, keepdims=True)
        sorted_ref[2 * number : 2 * number + 1] = order.astype(jnp.int32)
        sorted_ref[2 * number + 1 : 2 * number + 2] = upto.astype(jnp.int32)


class Outward:
    def __init__(self, source, target, send_sem, recv_sem, local_sem):
        self.target, self.recv_sem, self.send_sem = target, recv_sem, send_sem
        self.core, self.plane, self.spot = place_here()
        self.sends, self.keeps = [], []
        for side in (3, 1, 2, 0):
            for other in (self.core, 1 - self.core):
                goal = flip(self.spot, side)
                for piece in range(PIECES):
                    start = source.at[other, goal, piece]
                    stop = target.at[2 * self.core + piece, self.spot]
                    if side == 0 and other is self.core:
                        copy = pltpu.make_async_copy(start, stop, local_sem.at[piece])
                        self.keeps.append(copy)
                    else:
                        copy = remote(
                            start,
                            stop,
                            send_sem.at[len(self.sends)],
                            recv_sem.at[2 * self.core + piece, self.spot],
                            (other, rank_of(self.plane, goal)),
                        )
                        self.sends.append(copy)
                    copy.start()

    def arrive(self, side):
        for other in (self.core, 1 - self.core):
            if side == 0 and other is self.core:
                for copy in self.keeps:
                    copy.wait()
                continue
            for piece in range(PIECES):
                place = (2 * other + piece, flip(self.spot, side))
                remote(
                    self.target.at[place],
                    self.target.at[place],
                    self.send_sem.at[0],
                    self.recv_sem.at[place],
                    (self.core, rank_of(self.plane, self.spot)),
                ).wait_recv()

    def finish(self):
        for copy in self.sends:
            copy.wait_send()


def inward_targets(core, spot):
    for side in (3, 1, 2, 0):
        for other in (core, 1 - core):
            yield side, other, flip(spot, side), side == 0 and other is core


class Inward:
    def __init__(self, source, target, send_sem, recv_sem, local_sem):
        self.source, self.target = source, target
        self.send_sem, self.recv_sem, self.local_sem = send_sem, recv_sem, local_sem
        self.core, self.plane, self.spot = place_here()
        self.sends, self.keeps = [], []

    def send(self, other, goal, stays, piece, part, parts):
        source = self.source.at[2 * other + piece, goal, parts]
        target = self.target.at[self.core, self.spot, piece, parts]
        if stays:
            copy = pltpu.make_async_copy(source, target, self.local_sem.at[part, piece])
            self.keeps.append(copy)
        else:
            copy = remote(
                source,
                target,
                self.send_sem.at[len(self.sends)],
                self.recv_sem.at[self.core, self.spot, piece, part],
                (other, rank_of(self.plane, goal)),
            )
            self.sends.append(copy)
        copy.start()

    def finish(self, parts_of):
        for side, other, goal, stays in inward_targets(self.core, self.spot):
            if stays:
                continue
            for piece in range(PIECES):
                for part, parts in enumerate(parts_of[0 if other is self.core else 1]):
                    target = self.target.at[other, goal, piece, parts]
                    remote(
                        target,
                        target,
                        self.send_sem.at[0],
                        self.recv_sem.at[other, goal, piece, part],
                        (self.core, rank_of(self.plane, self.spot)),
                    ).wait_recv()
        for copy in self.sends:
            copy.wait_send()
        for copy in self.keeps:
            copy.wait()


KEYS_A, QUERIES, KEYS_B = range(3)


def plane_attend_back_kernel(*refs):
    table_ref, sorted_ref, qk_ref, shared_ref, grad_source_ref, lse_ref, hidden_ref = refs[:7]
    sources, half_up_ref, half_down_ref, refs = refs[7:10], refs[10], refs[11], refs[12:]
    sources = list(sources[:2]) + [sources[2].at[number] for number in range(LATE)]
    back_ref, hidden_out_ref, t_out_ref, t_up_ref, t_down_ref = refs[:5]
    count = 2 + LATE
    refs = refs[5:]
    buffers, mines, refs = refs[: 3 * count], refs[3 * count : 4 * count], refs[4 * count :]
    part_out_ref, part_up_ref, part_down_ref, far_out_ref, far_up_ref, far_down_ref = refs[:6]
    grad_ref, out_ref, sums_ref, shares_ref, walked_ref, sibling_ref = refs[6:12]
    scores_refs, refs = refs[12:16], refs[16:]
    reduce_send, reduce_recv, far_send, far_recv, load_sem = refs[:5]
    grad_sems, back_sems, move_sems, sibling_sems = refs[5:8], refs[8:11], refs[11:14], refs[14:16]

    local = qk_ref.shape[3]
    groups = PLANES * SPOTS
    blocks = groups * local
    core, plane, spot = place_here()
    low = low_lanes(BLOCK)
    masks = [half_mask(True), half_mask(False)]

    greet(both_partners(core, plane, spot))
    grads = Outward(grad_source_ref, grad_ref, *grad_sems)
    reduces = [
        SpotReduce(
            source,
            *buffers[3 * number : 3 * number + 3],
            reduce_send.at[number],
            reduce_recv.at[number],
            rows=FF // RANKS if number >= 2 else None,
            mine=mine,
        )
        for number, (source, mine) in enumerate(zip(sources, mines))
    ]
    ready = PER_STAGE * EARLY
    loads = [
        pltpu.make_async_copy(one.half(core), mine, load_sem.at[number])
        for number, (one, mine) in enumerate(zip(reduces, mines))
    ] + [
        pltpu.make_async_copy(half_up_ref, part_up_ref.at[0:ready], load_sem.at[count]),
        pltpu.make_async_copy(half_down_ref, part_down_ref.at[0:EARLY], load_sem.at[count + 1]),
    ]
    for one in reduces:
        one.start()
    for copy in loads:
        copy.start()

    def far(bits, number, source, target):
        return remote(
            source,
            target,
            far_send.at[number, bits - 1],
            far_recv.at[number, bits - 1],
            (core, rank_of(flip(plane, bits), spot)),
        )

    def far_down(bits, source):
        return far(bits, 3, source, far_down_ref.at[bits - 1])

    fars = []
    for bits in range(1, PLANES):
        goal = flip(plane, bits)
        copy = far(bits, 0, half_up_ref.at[:, goal], far_up_ref.at[bits - 1, 0:ready])
        copy.start()
        fars.append(copy)

        @pl.when(goal < EARLY)
        def _(bits=bits, goal=goal):
            far_down(bits, half_down_ref.at[jnp.minimum(goal, EARLY - 1)]).start()

    finish_hidden = from_planes(hidden_ref, hidden_out_ref, *move_sems)

    def load(component, block):
        rank, number = lax.div(block, local), lax.rem(block, local)
        if component == 2:
            return shared_ref[lax.div(rank, SPOTS), lax.rem(rank, SPOTS), number]
        return qk_ref[lax.div(rank, SPOTS), lax.rem(rank, SPOTS), component, number]

    def load_grad(block):
        rank = lax.div(block, local)
        return grad_ref[lax.div(rank, SPOTS), lax.rem(rank, SPOTS), lax.rem(block, local)]

    def store(component, block, value):
        rank = lax.div(block, local)
        out_ref[
            lax.div(rank, SPOTS), lax.rem(rank, SPOTS), component, lax.rem(block, local)
        ] = value.astype(BF16)

    def stored(component, block):
        rank = lax.div(block, local)
        return out_ref[
            lax.div(rank, SPOTS), lax.rem(rank, SPOTS), component, lax.rem(block, local)
        ].astype(F32)

    nothing = jnp.zeros((BLOCK, LANES), F32)

    def clear(block, carry):
        for slot in range(2):
            sums_ref[slot, block] = nothing
        return carry

    lax.fori_loop(0, blocks, clear, 0)

    def picked(block, number):
        return table_ref[0, block * RANDOM + number]

    def one_block(block, slot):
        ids, bias = inner_slots(picked, block, blocks)
        keys = jnp.concatenate([load(1 + slot, number) for number in ids], axis=0)
        both = jnp.concatenate(
            [load(0, block) * masks[slot], load_grad(block) * masks[1 - slot]], axis=0
        )
        products = dot_rt(both, keys)
        logs = lse_ref[block][:, slot * HEAD_DIM : slot * HEAD_DIM + 1]
        weights = jnp.exp(products[:BLOCK] + bias - logs)
        grad_weights = products[BLOCK:]
        delta = jnp.sum(weights * grad_weights, axis=1, keepdims=True)
        grad_scores = weights * (grad_weights - delta)
        stacked = jnp.concatenate([grad_scores, weights], axis=0).astype(BF16)
        return dot(stacked[:BLOCK], keys), dot_lt(stacked, both)

    fixed = 5

    def rank_blocks(rank, slot):
        first = rank * local
        results = [one_block(first + number, slot) for number in range(local)]

        def share(number, place):
            return results[number][1][place * BLOCK : (place + 1) * BLOCK]

        for shift in range(-1, local + 1):
            parts = [
                share(number, shift - number + 1)
                for number in range(local)
                if 0 <= shift - number + 1 <= 2
            ]
            target = jnp.minimum(jnp.maximum(first + shift, 0), blocks - 1)
            sums_ref[slot, target] += functools.reduce(jnp.add, parts)
        for place, target in ((3, 0), (4, blocks - 1)):
            sums_ref[slot, target] += functools.reduce(
                jnp.add, [share(number, place) for number in range(local)]
            )
        for number in range(local):
            for pick in range(RANDOM):
                shares_ref[slot, (first + number) * RANDOM + pick] = share(number, fixed + pick)
        return [result[0] for result in results]

    def head_a(side):
        def body(number, carry):
            rank = number * SPOTS + flip(spot, side)
            for place, query in enumerate(rank_blocks(rank, 0)):
                store(QUERIES, rank * local + place, query * SCALE)
            return carry

        lax.fori_loop(0, PLANES, body, 0)

    def head_b(number, carry):
        rank = core * (groups // 2) + number
        for place, query in enumerate(rank_blocks(rank, 1)):
            block = rank * local + place
            store(QUERIES, block, jnp.where(low, stored(QUERIES, block), query * SCALE))
        return carry

    spans = blocks // SPAN
    ends = (0, blocks - 1)

    def dense(slot, p_ref, d_ref, numbers):
        both = jnp.concatenate(
            [load(0, number) * masks[slot] for number in numbers]
            + [load_grad(number) * masks[1 - slot] for number in numbers],
            axis=0,
        )
        rows = len(numbers) * BLOCK
        column = slot * HEAD_DIM
        logs = jnp.concatenate(
            [lse_ref[number][:, column : column + 1] for number in numbers], axis=0
        )

        def keys_at(span):
            return jnp.concatenate(
                [load(1 + slot, span * SPAN + number) for number in range(SPAN)], axis=0
            )

        def first_pass(span, delta):
            products = dot_rt(both, keys_at(span))
            weights = jnp.exp(products[:rows] - logs)
            grad_weights = products[rows:]
            p_ref[span] = weights
            d_ref[span] = grad_weights
            return delta + jnp.sum(weights * grad_weights, axis=1, keepdims=True)

        delta = lax.fori_loop(0, spans, first_pass, jnp.zeros((rows, 1), F32), unroll=2)

        def second_pass(span, total):
            weights = p_ref[span]
            grad_scores = weights * (d_ref[span] - delta)
            stacked = jnp.concatenate([grad_scores, weights], axis=0).astype(BF16)
            shares = dot_lt(stacked, both)
            for number in range(SPAN):
                sums_ref[slot, span * SPAN + number] += shares[
                    number * BLOCK : (number + 1) * BLOCK
                ]
            return total + dot(stacked[:rows], keys_at(span))

        total = lax.fori_loop(0, spans, second_pass, jnp.zeros((rows, LANES), F32), unroll=2)
        for place, number in enumerate(numbers):
            query = total[place * BLOCK : (place + 1) * BLOCK] * SCALE
            if slot == 1:
                query = jnp.where(low, stored(QUERIES, number), query)
            store(QUERIES, number, query)

    def walk(slot, length):
        def body(number, total):
            entry = sorted_ref[2 * slot, number]
            earlier = sorted_ref[2 * slot, jnp.maximum(number - 1, 0)]
            keep = jnp.where(table_ref[0, entry] == table_ref[0, earlier], 1.0, 0.0).astype(F32)
            total = total * keep + shares_ref[slot, entry]
            walked_ref[slot, number] = total.astype(BF16)
            return total

        lax.fori_loop(0, length, body, nothing, unroll=4)

    def close(slot, rank, component):
        def body(number, carry):
            block = rank * local + number
            stop = sorted_ref[2 * slot + 1, block]
            start = jnp.where(block == 0, 0, sorted_ref[2 * slot + 1, jnp.maximum(block - 1, 0)])
            some = jnp.where(stop > start, 1.0, 0.0).astype(F32)
            share = walked_ref[slot, jnp.maximum(stop - 1, 0)].astype(F32)
            store(component, block, sums_ref[slot, block] + share * some)
            return carry

        lax.fori_loop(0, local, body, 0, unroll=True)

    back = Inward(out_ref, back_ref, *back_sems)
    own_parts = (slice(0, 1), slice(1, 2), slice(2, 3))
    far_parts = (slice(0, 2),)

    for side in range(SPOTS):
        grads.arrive(side)
        head_a(side)
        if side == 0:
            for copy in loads:
                copy.wait()
            for one in reduces:
                one.corners()
        if side == 2:
            for one in reduces:
                one.sides()
    dense(0, scores_refs[0], scores_refs[1], ends)
    reduces[0].close(part_out_ref)
    reduces[1].close(part_up_ref.at[ready : PER_STAGE * STAGES])
    for number in range(LATE):
        reduces[2 + number].close(part_down_ref.at[EARLY + number])
    for bits in range(1, PLANES):
        goal = flip(plane, bits)
        late = slice(ready, PER_STAGE * STAGES)
        for copy in (
            far(bits, 1, part_out_ref.at[:, goal], far_out_ref.at[bits - 1]),
            far(bits, 2, part_up_ref.at[late, goal], far_up_ref.at[bits - 1, late]),
        ):
            copy.start()
            fars.append(copy)

        @pl.when(goal >= EARLY)
        def _(bits=bits, goal=goal):
            far_down(bits, part_down_ref.at[goal]).start()

        fars.append(far_down(bits, part_down_ref.at[goal]))
    walk(0, blocks * RANDOM)
    for side, other, goal, stays in inward_targets(core, spot):
        for piece in range(PIECES):
            close(0, (2 * other + piece) * SPOTS + goal, KEYS_A)
            if other is core:
                back.send(other, goal, stays, piece, 0, own_parts[0])
            else:
                back.send(other, goal, stays, piece, 0, far_parts[0])
    lax.fori_loop(0, groups // 2, head_b, 0)
    dense(1, scores_refs[2], scores_refs[3], (core * (blocks - 1),))
    for side, other, goal, stays in inward_targets(core, spot):
        if other is core:
            for piece in range(PIECES):
                back.send(other, goal, stays, piece, 1, own_parts[1])
    walk(1, blocks * RANDOM // 2)
    for number in range(PIECES):
        for goal in range(SPOTS):
            close(1, (2 * (1 - core) + number) * SPOTS + goal, KEYS_B)
    across = remote(
        out_ref.at[pl.ds(2 * (1 - core), PIECES), :, KEYS_B],
        sibling_ref,
        sibling_sems[0],
        sibling_sems[1],
        (1 - core, rank_of(plane, spot)),
    )
    across.start()
    for number in range(PIECES):
        for goal in range(SPOTS):
            close(1, (2 * core + number) * SPOTS + goal, KEYS_B)
    across.wait_recv()
    for side, other, goal, stays in inward_targets(core, spot):
        if other is core:
            for piece in range(PIECES):
                place = (2 * core + piece, goal, KEYS_B)
                out_ref[place] = (
                    out_ref[place].astype(F32) + sibling_ref[piece, goal].astype(F32)
                ).astype(BF16)
                back.send(other, goal, stays, piece, 2, own_parts[2])
    for copy in fars:
        copy.wait()

    def total(part, far, index):
        value = part.astype(F32)
        for bits in range(PLANES - 1):
            value = value + far[(bits,) + index].astype(F32)
        return value

    t_out_ref[...] = total(part_out_ref[0, plane], far_out_ref, (0,))

    def close_up(number, carry):
        t_up_ref[number] = total(part_up_ref[number, plane], far_up_ref, (number,))
        return carry

    lax.fori_loop(0, PER_STAGE * STAGES, close_up, 0)
    t_down_ref[...] = total(part_down_ref[plane], far_down_ref, ())
    finish_hidden()
    grads.finish()
    across.wait_send()
    back.finish((own_parts, far_parts))


def plane_attention_back(
    table, sorted_table, qk, shared, grad_source, lse, hidden, sources, half_up, half_down
):
    local = qk.shape[3]
    blocks = PLANES * SPOTS * local
    spans = blocks // SPAN
    shard, rows = D // RANKS, FF // RANKS
    up_count = PER_STAGE * STAGES
    up_tail, out_tail = (2 * shard, LANES), (2 * shard, D // 2)
    buffers = block_scratch(1, *out_tail) + block_scratch(PER_STAGE * LATE, *up_tail)
    for _ in range(LATE):
        buffers += row_scratch(rows, D)
    count = 2 + LATE
    mines = [
        VMEM((1, PLANES, SPOTS) + out_tail, BF16),
        VMEM((PER_STAGE * LATE, PLANES, SPOTS) + up_tail, BF16),
    ] + [VMEM((SPOTS * rows, D), BF16)] * LATE
    parts = [
        VMEM((1, PLANES) + out_tail, BF16),
        VMEM((up_count, PLANES) + up_tail, BF16),
        VMEM((STAGES, rows, D), BF16),
        VMEM((PLANES - 1, 1) + out_tail, BF16),
        VMEM((PLANES - 1, up_count) + up_tail, BF16),
        VMEM((PLANES - 1, rows, D), BF16),
    ]
    tile = (local, BLOCK, LANES)
    wide = VMEM((spans, 2 * BLOCK, SPAN * BLOCK), F32)
    thin = VMEM((spans, BLOCK, SPAN * BLOCK), F32)
    dma = pltpu.SemaphoreType.DMA
    return pl.pallas_call(
        plane_attend_back_kernel,
        out_shape=(
            jax.ShapeDtypeStruct((2, SPOTS, PIECES, 3) + tile, BF16),
            jax.ShapeDtypeStruct(hidden.shape, BF16),
            jax.ShapeDtypeStruct(out_tail, F32),
            jax.ShapeDtypeStruct((up_count,) + up_tail, F32),
            jax.ShapeDtypeStruct((rows, D), F32),
        ),
        in_specs=[
            whole(pltpu.SMEM),
            whole(pltpu.SMEM),
            whole(),
            whole(),
            whole(ANY),
            whole(),
            whole(ANY),
        ]
        + [whole(ANY)] * 5,
        out_specs=(whole(ANY), whole(ANY)) + (whole(),) * 3,
        scratch_shapes=buffers
        + mines
        + parts
        + [
            VMEM((PLANES, SPOTS) + tile, BF16),
            VMEM((PLANES, SPOTS, 3) + tile, BF16),
            VMEM((2, blocks, BLOCK, LANES), F32),
            VMEM((2, blocks * RANDOM, BLOCK, LANES), F32),
            VMEM((2, blocks * RANDOM, BLOCK, LANES), BF16),
            VMEM((PIECES, SPOTS) + tile, BF16),
            wide,
            wide,
            thin,
            thin,
            dma((count, SpotReduce.SEMS)),
            dma((count, SpotReduce.SEMS)),
            dma((4, PLANES - 1)),
            dma((4, PLANES - 1)),
            dma((count + 2,)),
        ]
        + exchange_sems((PLANES, SPOTS))
        + [
            dma((36,)),
            dma((2, SPOTS, PIECES, 3)),
            dma((3, PIECES)),
            dma((2,)),
            dma((2,)),
            dma((2,)),
            dma,
            dma,
        ],
        compiler_params=pltpu.CompilerParams(
            vmem_limit_bytes=62 * 1024 * 1024, collective_id=5, has_side_effects=True
        ),
        name="plane_attention_back",
    )(table, sorted_table, qk, shared, grad_source, lse, hidden, *sources, half_up, half_down)


class PlaneGather:
    SENDS = 3 + 3 + 4 + 2

    def __init__(self, source, target, send_sem, column_sem, recv_sem, local_sem):
        self.source, self.target = source, target
        self.send_sem, self.column_sem, self.recv_sem = send_sem, column_sem, recv_sem
        self.core, self.plane, self.spot = place_here()
        self.sends = []
        self.own = pltpu.make_async_copy(
            source, target.at[self.core, self.plane, self.spot], local_sem
        )
        self.own.start()
        for bits in range(1, PLANES):
            copy = remote(
                source,
                target.at[self.core, self.plane, self.spot],
                send_sem.at[len(self.sends)],
                column_sem.at[self.plane],
                (self.core, rank_of(flip(self.plane, bits), self.spot)),
            )
            copy.start()
            self.sends.append(copy)

    def neighbour(self, bits):
        return (self.core, rank_of(self.plane, flip(self.spot, bits)))

    def sibling(self):
        return (1 - self.core, rank_of(self.plane, self.spot))

    def piece(self, core, planes, spot):
        return self.target.at[core, planes, spot]

    def send(self, planes, spot, part, goal):
        piece = self.piece(self.core, planes, spot)
        copy = remote(
            piece,
            piece,
            self.send_sem.at[len(self.sends)],
            self.recv_sem.at[self.core, spot, part],
            goal,
        )
        copy.start()
        self.sends.append(copy)

    def arrive(self, core, planes, spot, part):
        piece = self.piece(core, planes, spot)
        remote(
            piece,
            piece,
            self.send_sem.at[0],
            self.recv_sem.at[core, spot, part],
            (self.core, rank_of(self.plane, self.spot)),
        ).wait_recv()

    def columns(self):
        self.own.wait()
        for bits in range(1, PLANES):
            other = flip(self.plane, bits)
            shard = self.target.at[self.core, other, self.spot]
            remote(
                shard,
                shard,
                self.send_sem.at[0],
                self.column_sem.at[other],
                (self.core, rank_of(self.plane, self.spot)),
            ).wait_recv()
        for goal in (self.neighbour(1), self.neighbour(2), self.sibling()):
            self.send(slice(0, PLANES), self.spot, 0, goal)

    def forward(self):
        everything = slice(0, PLANES)
        for side in (1, 2):
            spot = flip(self.spot, side)
            self.arrive(self.core, everything, spot, 0)
            half = slice(0, 2) if side == 1 else slice(2, 4)
            self.send(half, spot, side - 1, self.neighbour(3 - side))
            self.send(everything, spot, 0, self.sibling())

    def corner(self):
        spot = flip(self.spot, 3)
        for part, half in enumerate((slice(0, 2), slice(2, 4))):
            self.arrive(self.core, half, spot, part)
            self.send(half, spot, part, self.sibling())

    def finish(self):
        for side in range(3):
            self.arrive(1 - self.core, slice(0, PLANES), flip(self.spot, side), 0)
        for part, half in enumerate((slice(0, 2), slice(2, 4))):
            self.arrive(1 - self.core, half, flip(self.spot, 3), part)
        for copy in self.sends:
            copy.wait_send()


class CrossGather:
    SENDS = 2 + 1 + 3 + 3 * 4

    def __init__(self, source, target, send_sem, spot_sem, recv_sem, local_sem):
        self.target = target
        self.send_sem, self.spot_sem, self.recv_sem = send_sem, spot_sem, recv_sem
        self.core, self.plane, self.spot = place_here()
        self.sends = []
        self.own = pltpu.make_async_copy(
            source, target.at[self.core, self.plane, self.spot], local_sem
        )
        self.own.start()
        for side in (1, 2):
            self.pass_on(source, self.spot, flip(self.spot, side))

    def push(self, source, target, recv_sem, device):
        copy = remote(source, target, self.send_sem.at[len(self.sends)], recv_sem, device)
        copy.start()
        self.sends.append(copy)

    def pass_on(self, source, spot, goal):
        self.push(
            source,
            self.target.at[self.core, self.plane, spot],
            self.spot_sem.at[spot],
            (self.core, rank_of(self.plane, goal)),
        )

    def await_spot(self, spot):
        shard = self.target.at[self.core, self.plane, spot]
        remote(
            shard,
            shard,
            self.send_sem.at[0],
            self.spot_sem.at[spot],
            (self.core, rank_of(self.plane, self.spot)),
        ).wait_recv()

    def across(self):
        beside, beyond = flip(self.spot, 1), flip(self.spot, 2)
        for side in (1, 2):
            self.await_spot(flip(self.spot, side))
        spot = beside * (1 - self.core) + beyond * self.core
        goal = beyond * (1 - self.core) + beside * self.core
        self.pass_on(self.target.at[self.core, self.plane, spot], spot, goal)

    def blocks(self):
        self.own.wait()
        self.await_spot(flip(self.spot, 3))
        self.maybe = []
        self.along(self.plane, 1, self.plane < PLANES - 1)
        self.along(self.plane, -1, self.plane > 0)
        self.to_sibling(self.plane, self.plane >= 0)

    def along(self, plane, step, wanted):
        block = self.target.at[self.core, plane]
        copy = remote(
            block,
            block,
            self.send_sem.at[3 + len(self.maybe)],
            self.recv_sem.at[self.core, plane],
            (self.core, rank_of(self.plane + step, self.spot)),
        )
        self.begin(copy, wanted)

    def to_sibling(self, plane, wanted):
        block = self.target.at[self.core, plane]
        copy = remote(
            block,
            block,
            self.send_sem.at[3 + len(self.maybe)],
            self.recv_sem.at[self.core, plane],
            (1 - self.core, rank_of(self.plane, self.spot)),
        )
        self.begin(copy, wanted)

    def begin(self, copy, wanted):
        self.maybe.append((copy, wanted))

        @pl.when(wanted)
        def _():
            copy.start()

    def arrive(self, core, plane):
        block = self.target.at[core, plane]
        remote(
            block,
            block,
            self.send_sem.at[0],
            self.recv_sem.at[core, plane],
            (self.core, rank_of(self.plane, self.spot)),
        ).wait_recv()

    def hop(self, distance):
        for step in (1, -1):
            origin = self.plane - step * distance
            here = (origin >= 0) & (origin < PLANES)
            onward = self.plane + step
            more = here & (onward >= 0) & (onward < PLANES)

            @pl.when(here)
            def _(origin=origin):
                self.arrive(self.core, origin)

            self.along(origin, step, more)
            self.to_sibling(origin, here)

    def finish(self):
        for bits in range(PLANES):
            self.arrive(1 - self.core, flip(self.plane, bits))
        for copy in self.sends:
            copy.wait_send()
        for copy, wanted in self.maybe:

            @pl.when(wanted)
            def _(copy=copy):
                copy.wait_send()


def pair_of_blocks(read, first, second):
    low = low_lanes(1)
    tiles = []
    for block, wanted in ((first, 0), (second, 1)):
        tile = read(block // 2)
        tiles.append(tile if block % 2 == wanted else swap_halves(tile))
    return jnp.where(low, tiles[0], tiles[1])


def fold_tiles(target_ref, start, tiles, read):
    half = len(tiles) // 2
    for number in range(half):
        columns = slice((start + number) * LANES, (start + number + 1) * LANES)
        target_ref[:, columns] = jnp.concatenate(
            [read(tiles[number]), read(tiles[half + number])], axis=0
        ).astype(BF16)


VECTORS = 8


def lay_vectors(vecs_ref, vectors_ref, up_ref):
    rows = vecs_ref.shape[3]
    own, wide = D // RANKS, FF // RANKS
    values = vecs_ref[...].reshape(RANKS, rows, LANES).astype(F32)

    def spread_out(count, width):
        place = lax.broadcasted_iota(jnp.int32, (LANES, count), 1)
        lane = lax.broadcasted_iota(jnp.int32, (LANES, count), 0)
        start = lax.div(place, width) * width
        return jnp.where(place - start == lane, 1.0, 0.0).astype(BF16)

    laid = dot(vecs_ref[...].reshape(RANKS * rows, LANES), spread_out(D, own))
    owner = lax.broadcasted_iota(jnp.int32, (RANKS, 1, D), 0)
    column = lax.broadcasted_iota(jnp.int32, (RANKS, 1, D), 2)
    laid = jnp.where(lax.div(column, own) == owner, laid.reshape(RANKS, rows, D), 0.0)
    vectors_ref[...] = jnp.sum(laid, axis=0)[:VECTORS]
    row = lax.broadcasted_iota(jnp.int32, (1, rows, LANES), 1)
    last = jnp.sum(jnp.where(row == VECTORS, values, 0.0), axis=1)
    laid = dot(last.astype(BF16), spread_out(FF, wide))
    owner = lax.broadcasted_iota(jnp.int32, (RANKS, FF), 0)
    column = lax.broadcasted_iota(jnp.int32, (RANKS, FF), 1)
    laid = jnp.sum(jnp.where(lax.div(column, wide) == owner, laid, 0.0), axis=0, keepdims=True)
    for chunk in range(FF // CHUNK):
        for side in range(2):
            start = side * (FF // 2) + chunk * LANES
            up_ref[chunk, :, side * LANES : (side + 1) * LANES] = laid[:, start : start + LANES]


def lay_table(tables_ref, core, micro, entries):
    count = 2 * LANES
    ranks = PLANES * SPOTS
    values = tables_ref[core].reshape(ranks, tables_ref.shape[3], LANES).astype(F32)
    row = lax.broadcasted_iota(jnp.int32, (1, tables_ref.shape[3], LANES), 1)
    values = jnp.sum(jnp.where(row == micro, values, 0.0), axis=1)
    place = lax.broadcasted_iota(jnp.int32, (LANES, count), 1)
    lane = lax.broadcasted_iota(jnp.int32, (LANES, count), 0)
    start = lax.div(place, entries) * entries
    laid = dot(values.astype(BF16), jnp.where(place - start == lane, 1.0, 0.0).astype(BF16))
    owner = lax.broadcasted_iota(jnp.int32, (ranks, count), 0)
    column = lax.broadcasted_iota(jnp.int32, (ranks, count), 1)
    laid = jnp.sum(jnp.where(lax.div(column, entries) == owner, laid, 0.0), axis=0, keepdims=True)
    column = lax.broadcasted_iota(jnp.int32, (1, count), 1)
    return jnp.where(column < ranks * entries, laid, 2.0 * LANES)


def front_kernel(
    x_in_ref,
    dy_ref,
    vec_ref,
    tab_ref,
    w_qkv_in_ref,
    w_out_in_ref,
    w_up_in_ref,
    w_down_in_ref,
    back_ref,
    x_ref,
    dys_ref,
    w_down_ref,
    w_qkv_hbm,
    w_out_hbm,
    w_up_hbm,
    qk_hbm,
    shared_hbm,
    normed_ref,
    lse_ref,
    vectors_ref,
    up_ref,
    table_ref,
    sorted_ref,
    s_qkv_ref,
    s_ou_ref,
    g_qkv_ref,
    g_ou_ref,
    w_qkv_ref,
    w_out_ref,
    w_up_ref,
    xs_ref,
    vecs_ref,
    tabs_ref,
    bias_ref,
    send_ref,
    qk_ref,
    shared_ref,
    out_ref,
    p_ref,
    q_ref,
    picks_ref,
    *sems,
):
    gather_send, gather_recv, gather_local = sems[:3]
    plane_sems, cross_sems = sems[3:7], sems[7:11]
    x_sems, dy_sems = sems[11:14], sems[14:17]
    qkv_send, qkv_recv, qkv_local, shared_send, shared_recv = sems[17:22]
    back_sems, local_sem = sems[22:25], sems[25]
    core, plane, spot = place_here()
    micro, rows, _ = x_in_ref.shape
    tokens = PIECES * rows
    local = rows // BLOCK
    blocks = PLANES * SPOTS * local

    barrier = pltpu.get_barrier_semaphore()
    partners = both_partners(core, plane, spot)
    for partner in partners:
        pl.semaphore_signal(barrier, inc=1, device_id=partner, device_id_type=MESH)

    def natural(ref):
        return lambda tile: ref[:, tile * LANES : (tile + 1) * LANES].astype(F32)

    order = [natural_block(entry) for entry in column_order()]
    read = natural(w_qkv_in_ref)
    fold_tiles(
        s_qkv_ref,
        0,
        list(range(TILES)),
        lambda tile: pair_of_blocks(read, order[2 * tile], order[2 * tile + 1]),
    )
    pl.semaphore_wait(barrier, len(partners))

    gathers = []
    for number, (source, target) in enumerate(
        ((tab_ref, tabs_ref), (vec_ref, vecs_ref), (s_qkv_ref, g_qkv_ref))
    ):
        one = Gather(
            source, target, gather_send.at[number], gather_recv.at[number], gather_local.at[number]
        )
        one.start()
        gathers.append(one)
    outs = D // LANES // 2
    fold_tiles(s_ou_ref, 0, list(range(D // LANES)), natural(w_out_in_ref))
    fold_tiles(s_ou_ref, outs, list(range(FF // LANES)), natural(w_up_in_ref))
    for one in gathers:
        one.column()
    finish_x = to_planes(x_in_ref, xs_ref, *x_sems)
    cross = CrossGather(w_down_in_ref, w_down_ref, *cross_sems)
    for one in gathers:
        one.across()
    for one in gathers:
        one.corner()
    cross.across()
    for one in gathers[:2]:
        one.finish()
    window_core, window_micro = lax.rem(plane, 2), lax.div(plane, 2)
    scalars = pltpu.make_async_copy(tabs_ref.at[window_core], picks_ref, local_sem.at[1])
    scalars.start()
    lay_vectors(vecs_ref, vectors_ref, up_ref)
    for tile in range(TILES):
        halves = []
        for entry in column_order()[2 * tile : 2 * tile + 2]:
            halves.append(entry)

        def bias_tile(number, halves=halves):
            if number < D // LANES:
                return vectors_ref[2:3, number * LANES : (number + 1) * LANES]
            if number < 2 * D // LANES:
                return jnp.zeros((1, LANES), F32)
            start = (number - 2 * D // LANES) * LANES
            return vectors_ref[3:4, start : start + LANES]

        chunk, side = tile % HALF_TILES, tile // HALF_TILES
        start = chunk * CHUNK + side * LANES
        bias_ref[:, start : start + LANES] = pair_of_blocks(
            bias_tile, order[2 * tile], order[2 * tile + 1]
        )
    gathers[2].finish()
    settle(g_qkv_ref, [(tile, w_qkv_ref, alternate(tile)) for tile in range(HALF_TILES)])
    keep_w = pltpu.make_async_copy(w_qkv_ref, w_qkv_hbm, local_sem.at[2])
    keep_w.start()

    finish_x()
    spread = PlaneGather(s_ou_ref, g_ou_ref, *plane_sems)
    keep_x = pltpu.make_async_copy(xs_ref, x_ref, local_sem.at[0])
    keep_x.start()
    normal, _ = norm_parts(xs_ref[...].reshape(tokens, D).astype(F32))
    normed_ref[...] = (normal * vectors_ref[0:1] + vectors_ref[1:2]).astype(BF16)

    def shaped(value):
        return value.astype(BF16).reshape(local, BLOCK, LANES)

    low = low_lanes(rows)
    queries = D // LANES
    for chunk in range(HALF_TILES):
        columns = slice(chunk * CHUNK, (chunk + 1) * CHUNK)
        packed = dot(normed_ref[...], w_qkv_ref[:, columns]) + bias_ref[:, columns]
        for side in range(2):
            tile = chunk + side * HALF_TILES
            whole_tile = packed[:, side * LANES : (side + 1) * LANES]
            if tile < queries:
                whole_tile = whole_tile.astype(BF16).astype(F32) * SCALE
            for piece in range(PIECES):
                part = whole_tile[piece * rows : (piece + 1) * rows]
                if tile < SPOTS:
                    send_ref[0, tile, piece, 0] = shaped(part)
                elif tile < queries:
                    first = 2 * (tile - SPOTS)
                    shared = send_ref[0, first, piece, 0].reshape(rows, LANES).astype(F32)
                    send_ref[1, first, piece, 0] = shaped(jnp.where(low, part, shared))
                    shared = send_ref[0, first + 1, piece, 0].reshape(rows, LANES).astype(F32)
                    send_ref[1, first + 1, piece, 0] = shaped(
                        jnp.where(low, swap_halves(part), shared)
                    )
                else:
                    goal, role = (tile - queries) // 3, (tile - queries) % 3
                    if role < 2:
                        send_ref[role, goal, piece, 1] = shaped(part)
                    else:
                        send_ref[0, goal, piece, 2] = shaped(part)
    sends, keeps = [], []
    for part, (parts, landing) in enumerate(((slice(0, 2), qk_ref), (2, shared_ref))):
        for side in (3, 1, 2, 0):
            for other in (core, 1 - core) if part == 0 else (core,):
                goal = flip(spot, side)
                for piece in range(PIECES):
                    source = send_ref.at[other if part == 0 else 0, goal, piece, parts]
                    target = landing.at[2 * core + piece, spot]
                    if side == 0 and other is core:
                        copy = pltpu.make_async_copy(source, target, qkv_local.at[part, piece])
                        keeps.append((part, copy))
                    else:
                        copy = remote(
                            source,
                            target,
                            qkv_send.at[len(sends)],
                            qkv_recv.at[2 * core + piece, spot, part],
                            (other, rank_of(plane, goal)),
                        )
                        sends.append(copy)
                    copy.start()
    spread.columns()
    cross.blocks()
    table = lay_table(tabs_ref, window_core, window_micro, local * RANDOM)
    table_ref[...] = table.astype(jnp.int32)
    sort_entries(table, sorted_ref, blocks * RANDOM)
    scalars.wait()

    def arrive(part, other, piece, goal):
        target = (qk_ref, shared_ref)[part].at[2 * other + piece, goal]
        remote(
            target,
            target,
            qkv_send.at[0],
            qkv_recv.at[2 * other + piece, goal, part],
            (core, rank_of(plane, spot)),
        ).wait_recv()

    for side in range(SPOTS):
        for other in (core, 1 - core):
            if side > 0 or other is not core:
                for piece in range(PIECES):
                    arrive(0, other, piece, flip(spot, side))
    for part, copy in keeps:
        copy.wait()
    cross.hop(1)

    low = low_lanes(BLOCK)
    masks = [half_mask(True), half_mask(False)]

    def tile_of(component, block):
        rank, number = lax.div(block, local), lax.rem(block, local)
        if component == 2:
            return shared_ref[lax.div(rank, SPOTS), lax.rem(rank, SPOTS), number]
        return qk_ref[lax.div(rank, SPOTS), lax.rem(rank, SPOTS), component, number]

    def picked(block, number):
        rank = lax.div(block, local)
        return picks_ref[
            lax.div(rank, SPOTS),
            lax.rem(rank, SPOTS),
            window_micro,
            lax.rem(block, local) * RANDOM + number,
        ]

    def place_of(block):
        rank = lax.div(block, local)
        return lax.div(rank, SPOTS), lax.rem(rank, SPOTS), lax.rem(block, local)

    def put(block, slot, mixed, log):
        place = place_of(block)
        if slot == 0:
            out_ref[place] = mixed.astype(BF16)
            lse_ref[block] = jnp.where(low, log, 0.0)
        else:
            out_ref[place] = jnp.where(low, mixed, out_ref[place].astype(F32)).astype(BF16)
            lse_ref[block] = jnp.where(low, lse_ref[block], log)

    def one_block(block, slot):
        ids, bias = inner_slots(picked, block, blocks)
        keys = jnp.concatenate([tile_of(1 + slot, number) for number in ids], axis=0)
        scores = dot_rt(tile_of(0, block) * masks[slot], keys) + bias
        top = jnp.max(scores, axis=1, keepdims=True)
        powered = jnp.exp(scores - top)
        total = jnp.sum(powered, axis=1, keepdims=True)
        mixed = dot(powered.astype(BF16), keys) * (1.0 / total)
        return mixed, top + jnp.log(total)

    def rank_blocks(rank, slot):
        results = [one_block(rank * local + number, slot) for number in range(local)]
        for number, (mixed, log) in enumerate(results):
            put(rank * local + number, slot, mixed, log)

    spans = blocks // SPAN
    ends = (0, blocks - 1)

    def dense(slot, scores_ref, numbers):
        size = len(numbers) * BLOCK
        query = jnp.concatenate([tile_of(0, number) * masks[slot] for number in numbers], axis=0)

        def keys_at(span):
            return jnp.concatenate(
                [tile_of(1 + slot, span * SPAN + number) for number in range(SPAN)], axis=0
            )

        def first_pass(span, top):
            scores = dot_rt(query, keys_at(span))
            scores_ref[span] = scores
            return jnp.maximum(top, jnp.max(scores, axis=1, keepdims=True))

        top = lax.fori_loop(
            0, spans, first_pass, jnp.full((size, 1), NEGATIVE, F32), unroll=2
        )

        def second_pass(span, carry):
            total, mixed = carry
            powered = jnp.exp(scores_ref[span] - top)
            return (
                total + jnp.sum(powered, axis=1, keepdims=True),
                mixed + dot(powered.astype(BF16), keys_at(span)),
            )

        total, mixed = lax.fori_loop(
            0,
            spans,
            second_pass,
            (jnp.zeros((size, 1), F32), jnp.zeros((size, LANES), F32)),
            unroll=2,
        )
        mixed = mixed * (1.0 / total)
        log = top + jnp.log(total)
        for place, number in enumerate(numbers):
            span = slice(place * BLOCK, (place + 1) * BLOCK)
            put(number, slot, mixed[span], log[span])

    def head_a(number, carry):
        rank_blocks(number, 0)
        return carry

    def head_b(number, carry):
        rank_blocks(core * (PLANES * SPOTS // 2) + number, 1)
        return carry

    shared = []
    half_way = PLANES * SPOTS // 2
    lax.fori_loop(0, half_way, head_a, 0)
    for side in range(SPOTS):
        goal = flip(spot, side)
        for piece in range(PIECES):
            if side > 0:
                arrive(1, core, piece, goal)
            source = shared_ref.at[2 * core + piece, goal]
            copy = remote(
                source,
                source,
                shared_send.at[2 * side + piece],
                shared_recv.at[2 * core + piece, goal],
                (1 - core, rank_of(plane, spot)),
            )
            copy.start()
            shared.append(copy)
    cross.hop(2)
    finish_dy = to_planes(dy_ref, dys_ref, *dy_sems)
    lax.fori_loop(half_way, PLANES * SPOTS, head_a, 0)
    dense(0, p_ref, ends)
    spread.forward()
    back = Inward(out_ref, back_ref, *back_sems)
    everything = slice(0, local)
    for side, other, goal, stays in inward_targets(core, spot):
        if other is not core:
            for piece in range(PIECES):
                back.send(other, goal, stays, piece, 0, everything)
    for side in range(SPOTS):
        for piece in range(PIECES):
            target = shared_ref.at[2 * (1 - core) + piece, flip(spot, side)]
            remote(
                target,
                target,
                shared_send.at[0],
                shared_recv.at[2 * (1 - core) + piece, flip(spot, side)],
                (core, rank_of(plane, spot)),
            ).wait_recv()
    keep_qk = pltpu.make_async_copy(qk_ref, qk_hbm, local_sem.at[3])
    keep_qk.start()
    keep_shared = pltpu.make_async_copy(shared_ref, shared_hbm, local_sem.at[6])
    keep_shared.start()
    lax.fori_loop(0, half_way, head_b, 0)
    dense(1, q_ref, (core * (blocks - 1),))
    spread.corner()
    cross.hop(3)
    for side, other, goal, stays in inward_targets(core, spot):
        if other is core:
            for piece in range(PIECES):
                back.send(other, goal, stays, piece, 0, everything)
    spread.finish()
    settle(
        g_ou_ref,
        [(tile, w_out_ref, (tile, outs + tile)) for tile in range(outs)]
        + [(outs + tile, w_up_ref, alternate(tile)) for tile in range(FF // CHUNK)],
    )
    keep_out = pltpu.make_async_copy(w_out_ref, w_out_hbm, local_sem.at[4])
    keep_out.start()
    keep_up = pltpu.make_async_copy(w_up_ref, w_up_hbm, local_sem.at[5])
    keep_up.start()
    cross.finish()
    finish_dy()
    for copy in sends:
        copy.wait_send()
    for copy in shared:
        copy.wait_send()
    back.finish(((everything,), (everything,)))
    for copy in (keep_x, keep_w, keep_qk, keep_shared, keep_out, keep_up):
        copy.wait()


def front(x, dy, vec, tab, w_qkv, w_out, w_up, w_down):
    micro, rows, _ = x.shape
    tokens = PIECES * rows
    local = rows // BLOCK
    blocks = PLANES * SPOTS * local
    spans = blocks // SPAN
    grid = (2, PLANES, SPOTS)
    shard = D // RANKS
    tile = (local, BLOCK, LANES)
    dma = pltpu.SemaphoreType.DMA
    struct = jax.ShapeDtypeStruct
    ou = (2 * shard, (D + FF) // 2)
    return pl.pallas_call(
        front_kernel,
        out_shape=(
            struct((2, SPOTS, PIECES) + tile, BF16),
            struct(x.shape, BF16),
            struct(dy.shape, BF16),
            struct(grid + w_down.shape, BF16),
            struct((D, 3 * D), BF16),
            struct((D, D), BF16),
            struct((D, FF), BF16),
            struct((PLANES, SPOTS, 2) + tile, BF16),
            struct((PLANES, SPOTS) + tile, BF16),
            struct((tokens, D), BF16),
            struct((blocks, BLOCK, LANES), F32),
            struct((VECTORS, D), F32),
            struct((FF // CHUNK, 1, CHUNK), F32),
            struct((1, 2 * LANES), jnp.int32),
            struct((4, 2 * LANES), jnp.int32),
        ),
        in_specs=[
            whole(ANY),
            whole(ANY),
            whole(ANY),
            whole(ANY),
            whole(),
            whole(),
            whole(),
            whole(ANY),
        ],
        out_specs=(whole(ANY),) * 9 + (whole(),) * 6,
        scratch_shapes=[
            VMEM((2 * shard, 3 * D // 2), BF16),
            VMEM(ou, BF16),
            VMEM(grid + (2 * shard, 3 * D // 2), BF16),
            VMEM(grid + ou, BF16),
            VMEM((D, 3 * D), BF16),
            VMEM((D, D), BF16),
            VMEM((D, FF), BF16),
            VMEM((PIECES, rows, D), BF16),
            VMEM(grid + vec.shape, BF16),
            VMEM(grid + tab.shape, jnp.int32),
            VMEM((1, 3 * D), F32),
            VMEM((2, SPOTS, PIECES, 3) + tile, BF16),
            VMEM((PLANES, SPOTS, 2) + tile, BF16),
            VMEM((PLANES, SPOTS) + tile, BF16),
            VMEM((PLANES, SPOTS) + tile, BF16),
            VMEM((spans, 2 * BLOCK, SPAN * BLOCK), F32),
            VMEM((spans, BLOCK, SPAN * BLOCK), F32),
            pltpu.SMEM((PLANES, SPOTS) + tab.shape, jnp.int32),
            dma((3, Gather.SENDS)),
            dma((3,) + grid),
            dma((3,)),
            dma((PlaneGather.SENDS,)),
            dma((PLANES,)),
            dma((2, SPOTS, 2)),
            dma,
            dma((CrossGather.SENDS,)),
            dma((SPOTS,)),
            dma((2, PLANES)),
            dma,
        ]
        + [dma((2,))] * 6
        + [
            dma((20,)),
            dma((PLANES, SPOTS, 2)),
            dma((2, PIECES)),
            dma((2 * SPOTS,)),
            dma((PLANES, SPOTS)),
            dma((14,)),
            dma((2, SPOTS, PIECES, 1)),
            dma((1, PIECES)),
            dma((7,)),
        ],
        compiler_params=pltpu.CompilerParams(
            vmem_limit_bytes=60 * 1024 * 1024, collective_id=1, has_side_effects=True
        ),
        name="front",
    )(x, dy, vec, tab, w_qkv, w_out, w_up, w_down)


class SpotReduce:
    SEMS = 4

    def __init__(self, source, near, corner, sides, send_sem, recv_sem, rows=None, mine=None):
        self.source, self.near, self.corner, self.side = source, near, corner, sides
        self.send_sem, self.recv_sem, self.rows, self.mine = send_sem, recv_sem, rows, mine
        self.core, self.plane, self.spot = place_here()
        beside, beyond = flip(self.spot, 1), flip(self.spot, 2)
        self.via = beyond * (1 - self.core) + beside * self.core
        self.other = beside * (1 - self.core) + beyond * self.core

    def half(self, core):
        return self.source.at[core] if self.rows else self.source.at[:, core]

    def part(self, spot):
        if self.rows:
            start = pl.multiple_of(spot * self.rows, 16)
            return self.near.at[pl.ds(start, self.rows)]
        return self.near.at[:, :, spot]

    def copy(self, number):
        sibling = (1 - self.core, rank_of(self.plane, self.spot))
        if number == 0:
            source, target, device = self.half(1 - self.core), self.near, sibling
        elif number == 1:
            source, target = self.part(flip(self.spot, 3)), self.corner
            device = (self.core, rank_of(self.plane, self.via))
        else:
            spot = flip(self.spot, number - 1)
            source, target = self.part(spot), self.side.at[number - 2]
            device = (self.core, rank_of(self.plane, spot))
        return remote(source, target, self.send_sem.at[number], self.recv_sem.at[number], device)

    def start(self):
        self.copy(0).start()

    def add(self, spot, terms, target=None):
        if self.rows:
            rows = self.rows

            def slab(number, carry):
                size = rows // 3
                first = pl.multiple_of(spot * rows + number * size, 16)
                place = pl.ds(first, size)
                inner = pl.ds(pl.multiple_of(number * size, 16), size)
                total = self.near[place].astype(F32)
                for read in terms:
                    total = total + read(place, inner).astype(F32)
                if target is None:
                    self.near[place] = total.astype(BF16)
                else:
                    target[inner] = total.astype(BF16)
                return carry

            lax.fori_loop(0, 3, slab, 0)
            return
        count = self.near.shape[0]

        def block(number, carry):
            first, plane = lax.div(number, PLANES), lax.rem(number, PLANES)
            total = self.near[first, plane, spot].astype(F32)
            for read in terms:
                total = total + read(first, plane).astype(F32)
            if target is None:
                self.near[first, plane, spot] = total.astype(BF16)
            else:
                target[first, plane] = total.astype(BF16)
            return carry

        lax.fori_loop(0, count * PLANES, block, 0)

    def corners(self):
        self.copy(0).wait_recv()
        core = self.core
        for spot in range(SPOTS):
            if self.rows and self.mine is None:
                self.add(spot, [lambda place, inner: self.source[core, place]])
            elif self.rows:
                self.add(spot, [lambda place, inner: self.mine[place]])
            elif self.mine is None:
                self.add(spot, [lambda first, plane, spot=spot: self.source[first, core, plane, spot]])
            else:
                self.add(spot, [lambda first, plane, spot=spot: self.mine[first, plane, spot]])
        self.copy(1).start()

    def sides(self):
        self.copy(1).wait_recv()
        if self.rows:
            self.add(self.other, [lambda place, inner: self.corner[inner]])
        else:
            self.add(self.other, [lambda first, plane: self.corner[first, plane]])
        self.copy(2).start()
        self.copy(3).start()

    def close(self, target):
        self.copy(2).wait_recv()
        self.copy(3).wait_recv()
        if self.rows:
            terms = [lambda place, inner, n=n: self.side[n, inner] for n in range(2)]
        else:
            terms = [lambda first, plane, n=n: self.side[n, first, plane] for n in range(2)]
        self.add(self.spot, terms, target)
        for number in range(self.SEMS):
            self.copy(number).wait_send()


def block_scratch(count, rows, width):
    return [
        VMEM((count, PLANES, SPOTS, rows, width), BF16),
        VMEM((count, PLANES, rows, width), BF16),
        VMEM((2, count, PLANES, rows, width), BF16),
    ]


def row_scratch(rows, width):
    return [
        VMEM((SPOTS * rows, width), BF16),
        VMEM((rows, width), BF16),
        VMEM((2, rows, width), BF16),
    ]


STAGES = 4
PER_STAGE = FF // CHUNK // STAGES
EARLY = 2
LATE = STAGES - EARLY
WAITS = (2, 4, 6)


def by_owner(out_ref, values):
    rows = D // RANKS
    width = values.shape[1] // 2
    for owner in range(RANKS):
        part = values[owner * rows : (owner + 1) * rows]
        out_ref[owner] = jnp.concatenate([part[:, :width], part[:, width:]], axis=0).astype(BF16)


def plane_middle_kernel(
    mixed_in_ref,
    x_ref,
    dy_ref,
    vec_ref,
    w_out_ref,
    up_shift_ref,
    w_up_ref,
    w_down_ref,
    hidden_ref,
    send_ref,
    dres_ref,
    g_out_ref,
    half_up_ref,
    half_down_ref,
    last_up_ref,
    last_down_ref,
    g_up_bias_ref,
    g_small_ref,
    mixed_ref,
    residual_ref,
    second_ref,
    second_t_ref,
    total_ref,
    dsecond_ref,
    g_up_ref,
    g_down_ref,
    *scratch,
):
    send_sem, recv_sem, local_sem = scratch[-3:]
    stages = []
    for number in range(EARLY):
        buffers = scratch[6 * number : 6 * number + 6]
        stages.append(
            (
                SpotReduce(
                    g_up_ref.at[PER_STAGE * number : PER_STAGE * (number + 1)],
                    *buffers[:3],
                    send_sem.at[number, 0],
                    recv_sem.at[number, 0],
                ),
                SpotReduce(
                    g_down_ref.at[number],
                    *buffers[3:],
                    send_sem.at[number, 1],
                    recv_sem.at[number, 1],
                    rows=FF // RANKS,
                ),
            )
        )
    pieces, rows, _ = x_ref.shape
    tokens = pieces * rows
    step = pl.program_id(0)
    low = low_lanes(rows)
    out_shift, gain, shift, down_shift = (vec_ref[number : number + 1] for number in (4, 5, 6, 7))

    @pl.when(step == 0)
    def _():
        core, plane, spot = place_here()
        greet(
            [
                (1 - core, rank_of(plane, spot)),
                (core, rank_of(plane, flip(spot, 1))),
                (core, rank_of(plane, flip(spot, 2))),
            ]
        )
        for piece in range(pieces):
            span = slice(piece * rows, (piece + 1) * rows)
            for spot in (0, 2):
                first = [mixed_in_ref[side, spot, piece].astype(F32) for side in range(2)]
                last = [mixed_in_ref[side, spot + 1, piece].astype(F32) for side in range(2)]
                own_first = jnp.where(core == 0, first[0], first[1])
                own_last = jnp.where(core == 0, last[0], last[1])
                tiles = (
                    jnp.where(low, swap_halves(first[0]), first[1]),
                    jnp.where(low, own_first, last[0]),
                    swap_halves(jnp.where(low, own_last, last[1])),
                )
                for number, tile in enumerate(tiles):
                    spread = 3 * (spot // 2) + number
                    mixed_ref[span, spread * LANES : (spread + 1) * LANES] = tile.astype(BF16)
        residual = x_ref[...].reshape(tokens, D).astype(F32) + (
            dot(mixed_ref[...], w_out_ref[...]) + out_shift
        )
        residual_ref[...] = residual
        normal, _ = norm_parts(residual)
        second = normal * gain + shift
        second_ref[...] = second.astype(BF16)
        second_t_ref[...] = second.T.astype(BF16)
        total_ref[...] = jnp.zeros_like(total_ref)
        dsecond_ref[...] = jnp.zeros_like(dsecond_ref)

    w_down = w_down_ref[...].reshape(CHUNK, D)
    upper = dot(second_ref[...], w_up_ref[...]) + up_shift_ref[0]
    factor = 0.7978845608028654
    square = upper * upper
    bent = jnp.tanh(factor * (upper + 0.044715 * (upper * square)))
    middle_half = 0.5 * (1.0 + bent)
    active = (upper * middle_half).astype(BF16)
    slope = middle_half + 0.5 * upper * (1.0 - bent * bent) * (
        factor + (3.0 * 0.044715 * factor) * square
    )
    dy = dy_ref[...]
    total_ref[...] += dot(active, w_down)
    stage, turn = lax.div(step, PER_STAGE), lax.rem(step, PER_STAGE)
    down_share = dot_lt(active, dy).astype(BF16)
    place = pl.ds(pl.multiple_of(turn * LANES, LANES), LANES)
    for side in range(2):
        g_down_ref[stage, side, place] = down_share[side * LANES : (side + 1) * LANES]
    dupper = (dot_rt(dy, w_down) * slope).astype(BF16)
    g_up_bias_ref[0] = jnp.sum(dupper.astype(F32), axis=0, keepdims=True)
    up_share = dot(second_t_ref[...], dupper)
    shard = D // RANKS
    for owner in range(RANKS):
        part = up_share[owner * shard : (owner + 1) * shard]
        g_up_ref[step, owner // (PLANES * SPOTS), owner // SPOTS % PLANES, owner % SPOTS] = (
            jnp.concatenate([part[:, :LANES], part[:, LANES:]], axis=0).astype(BF16)
        )
    dsecond_ref[...] += dot_rt(dupper, w_up_ref[...])

    last = FF // CHUNK - 1
    for number, pair in enumerate(stages):
        done = PER_STAGE * (number + 1) - 1

        @pl.when(step == done)
        def _(pair=pair):
            for one in pair:
                one.start()

        @pl.when(step == done + WAITS[0])
        def _(pair=pair):
            for one in pair:
                one.corners()

        @pl.when(step == done + WAITS[1])
        def _(pair=pair):
            for one in pair:
                one.sides()

        if done + WAITS[2] < last:

            @pl.when(step == done + WAITS[2])
            def _(pair=pair, number=number):
                pair[0].close(half_up_ref.at[PER_STAGE * number : PER_STAGE * (number + 1)])
                pair[1].close(half_down_ref.at[number])

    @pl.when(step == last)
    def _():
        keep_up = pltpu.make_async_copy(
            g_up_ref.at[PER_STAGE * EARLY : PER_STAGE * STAGES], last_up_ref, local_sem.at[0]
        )
        keep_up.start()
        keep_down = pltpu.make_async_copy(
            g_down_ref.at[EARLY:STAGES], last_down_ref, local_sem.at[1]
        )
        keep_down.start()
        residual = residual_ref[...]
        hidden_ref[...] = (
            (residual + (total_ref[...] + down_shift)).astype(BF16).reshape(x_ref.shape)
        )
        normal, inverse = norm_parts(residual)
        dsecond = dsecond_ref[...]
        grad_out = dy_ref[...].astype(F32)
        g_small_ref[0:1] = jnp.sum(dsecond * normal, axis=0, keepdims=True)
        g_small_ref[1:2] = jnp.sum(dsecond, axis=0, keepdims=True)
        g_small_ref[2:3] = jnp.sum(grad_out, axis=0, keepdims=True)
        dres = grad_out + norm_pull(dsecond, normal, inverse, gain)
        dres_ref[...] = dres
        branch = dres.astype(BF16)
        g_small_ref[3:4] = jnp.sum(branch.astype(F32), axis=0, keepdims=True)
        by_owner(g_out_ref, dot_lt(mixed_ref[...], branch))
        dmixed = dot_rt(branch, w_out_ref[...])
        for piece in range(pieces):
            span = slice(piece * rows, (piece + 1) * rows)
            for spot in (0, 2):
                tiles = [
                    dmixed[span, number * LANES : (number + 1) * LANES]
                    for number in range(3 * (spot // 2), 3 * (spot // 2) + 3)
                ]
                flipped = [swap_halves(tile) for tile in tiles]
                send_ref[0, spot, piece] = jnp.where(low, tiles[1], flipped[0]).astype(BF16)
                send_ref[1, spot, piece] = jnp.where(low, tiles[1], tiles[0]).astype(BF16)
                send_ref[0, spot + 1, piece] = jnp.where(low, flipped[2], tiles[1]).astype(BF16)
                send_ref[1, spot + 1, piece] = flipped[2].astype(BF16)
        for number, pair in enumerate(stages):
            if PER_STAGE * (number + 1) - 1 + WAITS[2] >= last:
                pair[0].close(half_up_ref.at[PER_STAGE * number : PER_STAGE * (number + 1)])
                pair[1].close(half_down_ref.at[number])
        keep_up.wait()
        keep_down.wait()


def plane_middle(mixed_in, x, dy, vec, w_out, up_shift, w_up, w_down):
    pieces, rows, _ = x.shape
    tokens = pieces * rows
    shard = D // RANKS

    def fixed(shape):
        return pl.BlockSpec(shape, lambda step: (0,) * len(shape))

    steps = FF // CHUNK
    grid = (2, PLANES, SPOTS)
    down_rows = FF // RANKS
    half_up = (PER_STAGE * EARLY, PLANES, 2 * shard, LANES)
    half_down = (EARLY, down_rows, D)
    buffers = []
    for _ in range(EARLY):
        buffers += block_scratch(PER_STAGE, 2 * shard, LANES) + row_scratch(down_rows, D)
    down = pl.BlockSpec((2, LANES, D), lambda step: (0, step, 0))
    return pl.pallas_call(
        plane_middle_kernel,
        grid=(steps,),
        out_shape=(
            jax.ShapeDtypeStruct(x.shape, BF16),
            jax.ShapeDtypeStruct(mixed_in.shape, BF16),
            jax.ShapeDtypeStruct((tokens, D), F32),
            jax.ShapeDtypeStruct((RANKS, 2 * shard, D // 2), BF16),
            jax.ShapeDtypeStruct(half_up, BF16),
            jax.ShapeDtypeStruct(half_down, BF16),
            jax.ShapeDtypeStruct((PER_STAGE * LATE,) + grid + (2 * shard, LANES), BF16),
            jax.ShapeDtypeStruct((LATE, 2, FF // 2 // STAGES, D), BF16),
            jax.ShapeDtypeStruct((steps, 1, CHUNK), F32),
            jax.ShapeDtypeStruct((4, D), F32),
        ),
        in_specs=[
            fixed(mixed_in.shape),
            fixed(x.shape),
            fixed((tokens, D)),
            fixed(vec.shape),
            fixed((D, D)),
            pl.BlockSpec((1, 1, CHUNK), lambda step: (step, 0, 0)),
            pl.BlockSpec((D, CHUNK), lambda step: (0, step)),
            down,
        ],
        out_specs=(
            fixed(x.shape),
            fixed(mixed_in.shape),
            fixed((tokens, D)),
            fixed((RANKS, 2 * shard, D // 2)),
            fixed(half_up),
            fixed(half_down),
            whole(ANY),
            whole(ANY),
            pl.BlockSpec((1, 1, CHUNK), lambda step: (step, 0, 0)),
            fixed((4, D)),
        ),
        scratch_shapes=[
            VMEM((tokens, D), BF16),
            VMEM((tokens, D), F32),
            VMEM((tokens, D), BF16),
            VMEM((D, tokens), BF16),
            VMEM((tokens, D), F32),
            VMEM((tokens, D), F32),
            VMEM((steps,) + grid + (2 * shard, LANES), BF16),
            VMEM((STAGES, 2, FF // 2 // STAGES, D), BF16),
        ]
        + buffers
        + [
            pltpu.SemaphoreType.DMA((EARLY, 2, SpotReduce.SEMS)),
            pltpu.SemaphoreType.DMA((EARLY, 2, SpotReduce.SEMS)),
            pltpu.SemaphoreType.DMA((2,)),
        ],
        compiler_params=pltpu.CompilerParams(
            vmem_limit_bytes=60 * 1024 * 1024, collective_id=3, has_side_effects=True
        ),
        name="plane_middle",
    )(mixed_in, x, dy, vec, w_out, up_shift, w_up, w_down)


class Reduce:
    SENDS = 4 + 2 + 2 + 3
    RECVS = SENDS

    def __init__(self, source, total, near, corner_x, corner_y, side_x, side_y, far, out, sems):
        self.source, self.total, self.near = source, total, near
        self.corner = {1: corner_x, 2: corner_y}
        self.side = {1: side_x, 2: side_y}
        self.far, self.out = far, out
        self.send_sem, self.recv_sem, self.local_sem = sems
        self.core, self.plane, self.spot = place_here()
        self.copies = []
        self.locals = []

    def start(self):
        sibling = (1 - self.core, rank_of(self.plane, self.spot))
        for number, side in enumerate((3, 1, 2, 0)):
            spot = flip(self.spot, side)
            copy = remote(
                self.source.at[1 - self.core, :, spot],
                self.near.at[:, spot],
                self.send_sem.at[number],
                self.recv_sem.at[number],
                sibling,
            )
            copy.start()
            self.copies.append(copy)
            keep = pltpu.make_async_copy(
                self.source.at[self.core, :, spot],
                self.total.at[:, spot],
                self.local_sem.at[number],
            )
            keep.start()
            self.locals.append(keep)

    def take(self, number, side):
        self.copies[number].wait_recv()
        self.locals[number].wait()
        spot = flip(self.spot, side)

        def add(plane, carry):
            self.total[plane, spot] = (
                self.total[plane, spot].astype(F32) + self.near[plane, spot].astype(F32)
            ).astype(self.total.dtype)
            return carry

        lax.fori_loop(0, PLANES, add, 0)

    def corners(self):
        self.take(0, 3)
        spot = flip(self.spot, 3)
        index = 4
        self.corner_copies = []
        for bits in range(PLANES):
            side = 2 if bits < 2 else 1
            self.corner_copies.append(None)
            plane = flip(self.plane, bits)
            copy = remote(
                self.total.at[plane, spot],
                self.corner[side].at[bits % 2],
                self.send_sem.at[index + bits],
                self.recv_sem.at[index + bits],
                (self.core, rank_of(self.plane, flip(self.spot, side))),
            )
            copy.start()
            self.corner_copies[bits] = copy

    def sides(self):
        self.take(1, 1)
        self.take(2, 2)
        self.side_copies = {}
        for side in (1, 2):
            spot = flip(self.spot, side)
            came = 3 - side
            for bits in (0, 1) if came == 2 else (2, 3):
                self.corner_copies[bits].wait_recv()
                plane = flip(self.plane, bits)
                self.total[plane, spot] = (
                    self.total[plane, spot].astype(F32)
                    + self.corner[came][bits % 2].astype(F32)
                ).astype(self.total.dtype)
            copy = remote(
                self.total.at[:, spot],
                self.side[side],
                self.send_sem.at[7 + side],
                self.recv_sem.at[7 + side],
                (self.core, rank_of(self.plane, spot)),
            )
            copy.start()
            self.side_copies[side] = copy

    def columns(self):
        self.take(3, 0)
        for side in (1, 2):
            self.side_copies[side].wait_recv()

        def add(plane, carry):
            self.total[plane, self.spot] = (
                self.total[plane, self.spot].astype(F32)
                + self.side[1][plane].astype(F32)
                + self.side[2][plane].astype(F32)
            ).astype(self.total.dtype)
            return carry

        lax.fori_loop(0, PLANES, add, 0)
        self.far_copies = []
        for bits in range(1, PLANES):
            plane = flip(self.plane, bits)
            copy = remote(
                self.total.at[plane, self.spot],
                self.far.at[bits - 1],
                self.send_sem.at[9 + bits],
                self.recv_sem.at[9 + bits],
                (self.core, rank_of(plane, self.spot)),
            )
            copy.start()
            self.far_copies.append(copy)

    def finish(self):
        value = self.total[self.plane, self.spot].astype(F32)
        for bits in range(1, PLANES):
            self.far_copies[bits - 1].wait_recv()
            value = value + self.far[bits - 1].astype(F32)
        self.out[...] = value
        for copy in self.copies + self.corner_copies + self.far_copies:
            copy.wait_send()
        for side in (1, 2):
            self.side_copies[side].wait_send()


REDUCE_SEMS = 13


def reduce_scratch(shape, kind):
    tail = shape[3:]
    return [
        VMEM((PLANES, SPOTS) + tail, kind),
        VMEM((PLANES, SPOTS) + tail, kind),
        VMEM((2,) + tail, kind),
        VMEM((2,) + tail, kind),
        VMEM((PLANES,) + tail, kind),
        VMEM((PLANES,) + tail, kind),
        VMEM((PLANES - 1,) + tail, kind),
    ]


class Doubling:
    STEPS = 5

    def __init__(self, totals, boxes, send_sem, recv_sem):
        self.totals, self.boxes = totals, boxes
        self.send_sem, self.recv_sem = send_sem, recv_sem
        core, plane, spot = place_here()
        self.partners = (
            (1 - core, rank_of(plane, spot)),
            (core, rank_of(plane, flip(spot, 1))),
            (core, rank_of(plane, flip(spot, 2))),
            (core, rank_of(flip(plane, 1), spot)),
            (core, rank_of(flip(plane, 2), spot)),
        )
        self.copies = []

    def start(self, step):
        self.copies = []
        for number, (total, box) in enumerate(zip(self.totals, self.boxes)):
            copy = remote(
                total,
                box.at[step],
                self.send_sem.at[step, number],
                self.recv_sem.at[step, number],
                self.partners[step],
            )
            copy.start()
            self.copies.append(copy)

    def finish(self, step):
        for copy, total, box in zip(self.copies, self.totals, self.boxes):
            copy.wait()
            total[...] += box[step]


PARTS = 3


def finish_kernel(
    recv_ref,
    normed_ref,
    x_ref,
    dres_hbm,
    vec_ref,
    w_hbm,
    g_mid_ref,
    g_up_bias_ref,
    grad_ref,
    g_qkv_ref,
    rows_out_ref,
    tiles_out_ref,
    *scratch,
):
    sources, scratch = scratch[:PARTS], scratch[PARTS:]
    buffers, scratch = scratch[: 7 * PARTS], scratch[7 * PARTS :]
    packed_ref, dnormed_ref, gradient_ref, dres_ref, w_ref = scratch[:5]
    rows_ref, tiles_ref, rows_box, tiles_box = scratch[5:9]
    send_sem, recv_sem, local_sem, load_sem, sum_send, sum_recv = scratch[9:15]
    move_sems = scratch[15:18]
    pieces, rows, _ = x_ref.shape
    tokens = pieces * rows
    core, plane, spot = place_here()
    low = low_lanes(rows)

    load_w = pltpu.make_async_copy(w_hbm, w_ref, load_sem.at[0])
    load_dres = pltpu.make_async_copy(dres_hbm, dres_ref, load_sem.at[1])
    load_w.start()
    load_dres.start()
    greet(all_partners(core, plane, spot))

    def put(tile, piece, value):
        side, chunk = tile // HALF_TILES, tile % HALF_TILES
        packed_ref[
            piece * rows : (piece + 1) * rows,
            chunk * CHUNK + side * LANES : chunk * CHUNK + (side + 1) * LANES,
        ] = value.astype(BF16)

    for piece in range(pieces):
        seconds = []
        for goal in range(SPOTS):
            first = recv_ref[0, goal, piece, QUERIES].astype(F32)
            second = recv_ref[1, goal, piece, QUERIES].astype(F32)
            put(goal, piece, jnp.where(low, first, jnp.where(core == 0, first, second)))
            seconds.append(second)
            base = D // LANES + 3 * goal
            put(base, piece, recv_ref[0, goal, piece, KEYS_A])
            put(base + 1, piece, recv_ref[1, goal, piece, KEYS_A])
            put(base + 2, piece, recv_ref[core, goal, piece, KEYS_B])
        for number in range(2):
            put(
                SPOTS + number,
                piece,
                jnp.where(low, seconds[2 * number], swap_halves(seconds[2 * number + 1])),
            )

    load_w.wait()
    for chunk in range(HALF_TILES):
        columns = slice(chunk * CHUNK, (chunk + 1) * CHUNK)
        share = dot_rt(packed_ref[:, columns], w_ref[:, columns])
        if chunk == 0:
            dnormed_ref[...] = share
        else:
            dnormed_ref[...] += share
    normal, inverse = norm_parts(x_ref[...].reshape(tokens, D).astype(F32))
    dnormed = dnormed_ref[...]
    load_dres.wait()
    gradient = dres_ref[...] + norm_pull(dnormed, normal, inverse, vec_ref[0:1])
    gradient_ref[...] = gradient.astype(BF16).reshape(x_ref.shape)
    finish_grad = from_planes(gradient_ref, grad_ref, *move_sems)

    rows_ref[0:1] = jnp.sum(dnormed * normal, axis=0, keepdims=True)
    rows_ref[1:2] = jnp.sum(dnormed, axis=0, keepdims=True)
    rows_ref[2:6] = g_mid_ref[...]
    rows_ref[6:8] = jnp.zeros((2, D), F32)
    tiles_ref[...] = jnp.zeros_like(tiles_ref)
    for step in range(FF // CHUNK):
        tiles_ref[step : step + 1] = g_up_bias_ref[step]
    for chunk in range(HALF_TILES):
        number = FF // CHUNK + chunk
        tiles_ref[number : number + 1] = jnp.sum(
            packed_ref[:, chunk * CHUNK : (chunk + 1) * CHUNK].astype(F32), axis=0, keepdims=True
        )
    sums = Doubling((rows_ref, tiles_ref), (rows_box, tiles_box), sum_send, sum_recv)
    sums.start(0)

    width = HALF_TILES // PARTS * LANES
    reduces = [
        Reduce(
            sources[part],
            *buffers[7 * part : 7 * part + 7],
            g_qkv_ref.at[:, part * width : (part + 1) * width],
            (send_sem.at[part], recv_sem.at[part], local_sem.at[part]),
        )
        for part in range(PARTS)
    ]
    shard = D // RANKS
    normed_t = normed_ref[...].astype(F32).T.astype(BF16)
    for part in range(PARTS):
        for number in range(HALF_TILES // PARTS):
            chunk = part * (HALF_TILES // PARTS) + number
            values = dot(normed_t, packed_ref[:, chunk * CHUNK : (chunk + 1) * CHUNK])
            columns = slice(number * LANES, (number + 1) * LANES)
            for owner in range(RANKS):
                mine = values[owner * shard : (owner + 1) * shard]
                sources[part][
                    owner // (PLANES * SPOTS), owner // SPOTS % PLANES, owner % SPOTS, :, columns
                ] = jnp.concatenate([mine[:, :LANES], mine[:, LANES:]], axis=0).astype(BF16)
        reduces[part].start()
        if part > 0:
            reduces[part - 1].corners()
        if part > 1:
            reduces[part - 2].sides()
    sums.finish(0)
    sums.start(1)
    reduces[2].corners()
    reduces[1].sides()
    sums.finish(1)
    sums.start(2)
    reduces[0].columns()
    reduces[2].sides()
    sums.finish(2)
    sums.start(3)
    reduces[1].columns()
    sums.finish(3)
    sums.start(4)
    reduces[2].columns()
    sums.finish(4)
    for one in reduces:
        one.finish()
    rows_out_ref[...] = rows_ref[...]
    tiles_out_ref[...] = tiles_ref[...]
    finish_grad()


def finish_layer(recv, normed, x, dres, vec, w, g_mid, g_up_bias):
    pieces, rows, _ = x.shape
    tokens = pieces * rows
    shard = D // RANKS
    grid = (2, PLANES, SPOTS)
    part = grid + (2 * shard, HALF_TILES // PARTS * LANES)
    buffers = []
    for _ in range(PARTS):
        buffers += reduce_scratch(part, BF16)
    tiles = -(-(FF // CHUNK + HALF_TILES) // 8) * 8
    dma = pltpu.SemaphoreType.DMA
    return pl.pallas_call(
        finish_kernel,
        out_shape=(
            jax.ShapeDtypeStruct(x.shape, BF16),
            jax.ShapeDtypeStruct((2 * shard, 3 * D // 2), F32),
            jax.ShapeDtypeStruct((8, D), F32),
            jax.ShapeDtypeStruct((tiles, CHUNK), F32),
        ),
        in_specs=[
            whole(),
            whole(),
            whole(),
            whole(ANY),
            whole(),
            whole(ANY),
            whole(),
            whole(),
        ],
        out_specs=(whole(ANY), whole(), whole(), whole()),
        scratch_shapes=[VMEM(part, BF16)] * PARTS
        + buffers
        + [
            VMEM((tokens, 3 * D), BF16),
            VMEM((tokens, D), F32),
            VMEM(x.shape, BF16),
            VMEM((tokens, D), F32),
            VMEM(w.shape, BF16),
            VMEM((8, D), F32),
            VMEM((tiles, CHUNK), F32),
            VMEM((Doubling.STEPS, 8, D), F32),
            VMEM((Doubling.STEPS, tiles, CHUNK), F32),
            dma((PARTS, REDUCE_SEMS)),
            dma((PARTS, REDUCE_SEMS)),
            dma((PARTS, 4)),
            dma((2,)),
            dma((Doubling.STEPS, 2)),
            dma((Doubling.STEPS, 2)),
            dma((2,)),
            dma((2,)),
            dma((2,)),
        ],
        compiler_params=pltpu.CompilerParams(
            vmem_limit_bytes=60 * 1024 * 1024, collective_id=2, has_side_effects=True
        ),
        name="finish_layer",
    )(recv, normed, x, dres, vec, w, g_mid, g_up_bias)


def present_kernel(
    hidden_hbm,
    grad_hbm,
    t_qkv_hbm,
    t_out_hbm,
    t_up_hbm,
    t_down_hbm,
    rows_hbm,
    tiles_hbm,
    hidden_out_ref,
    grad_out_ref,
    g_qkv_ref,
    g_out_ref,
    g_up_ref,
    g_down_ref,
    *outs,
):
    singles, (grad_ref, t_qkv_ref, t_out_ref, t_up_ref, rows_ref, tiles_ref, copy_sem) = (
        outs[:-7],
        outs[-7:],
    )
    loads = [
        pltpu.make_async_copy(source, target, copy_sem.at[number])
        for number, (source, target) in enumerate(
            (
                (rows_hbm, rows_ref),
                (tiles_hbm, tiles_ref),
                (t_qkv_hbm, t_qkv_ref),
                (t_out_hbm, t_out_ref),
                (t_up_hbm, t_up_ref),
                (grad_hbm, grad_ref),
                (t_down_hbm, g_down_ref),
                (hidden_hbm, hidden_out_ref),
            )
        )
    ]
    for copy in loads:
        copy.start()
    core, plane, spot = place_here()
    mine = core * (PLANES * SPOTS) + rank_of(plane, spot)
    own, wide = D // RANKS, FF // RANKS
    order = [natural_block(entry) for entry in column_order()]
    inverse = [order.index(number) for number in range(len(order))]

    for copy in loads[:5]:
        copy.wait()
    half = D // 2
    for side in range(2):
        rows = slice(side * own, (side + 1) * own)
        g_out_ref[:, side * half : (side + 1) * half] = t_out_ref[rows]
        for chunk in range(FF // CHUNK):
            start = side * (FF // 2) + chunk * LANES
            g_up_ref[:, start : start + LANES] = t_up_ref[chunk, rows]

    def folded(tile):
        side, chunk = tile // HALF_TILES, tile % HALF_TILES
        return t_qkv_ref[
            side * own : (side + 1) * own, chunk * LANES : (chunk + 1) * LANES
        ]

    def bias_sum(tile):
        side, chunk = tile // HALF_TILES, tile % HALF_TILES
        row = FF // CHUNK + chunk
        return tiles_ref[row : row + 1, side * LANES : (side + 1) * LANES]

    biases = []
    for tile in range(TILES):
        blocks = inverse[2 * tile], inverse[2 * tile + 1]
        g_qkv_ref[:, tile * LANES : (tile + 1) * LANES] = pair_of_blocks(folded, *blocks)
        biases.append(pair_of_blocks(bias_sum, *blocks))
    third = TILES // 3
    query = jnp.concatenate(biases[:third], axis=1)
    value = jnp.concatenate(biases[2 * third :], axis=1)
    vectors = jnp.concatenate([rows_ref[0:6], query, value], axis=0)

    def pick(values, first, wanted):
        place = lax.broadcasted_iota(jnp.int32, (values.shape[1], LANES), 0) + first
        lane = lax.broadcasted_iota(jnp.int32, (values.shape[1], LANES), 1)
        one_hot = jnp.where(place == mine * wanted + lane, 1.0, 0.0)
        return lax.dot_general(
            values,
            one_hot,
            (((1,), (0,)), ((), ())),
            precision=lax.Precision.HIGHEST,
            preferred_element_type=F32,
        )

    picked = pick(vectors, 0, own)
    for number in range(VECTORS):
        singles[number][...] = picked[number : number + 1, :own]
    total = jnp.zeros((1, LANES), F32)
    for chunk in range(FF // CHUNK):
        for side in range(2):
            total = total + pick(
                tiles_ref[chunk : chunk + 1, side * LANES : (side + 1) * LANES],
                side * (FF // 2) + chunk * LANES,
                wide,
            )
    singles[VECTORS][...] = total[:, :wide]
    loads[5].wait()
    grad_out_ref[...] = grad_ref[...].astype(F32)
    for copy in loads[6:]:
        copy.wait()


def present(hidden, grad, t_qkv, t_out, t_up, t_down, rows, tiles):
    own, wide = D // RANKS, FF // RANKS
    struct = jax.ShapeDtypeStruct
    return pl.pallas_call(
        present_kernel,
        out_shape=(
            struct(hidden.shape, BF16),
            struct(grad.shape, F32),
            struct((own, 3 * D), F32),
            struct((own, D), F32),
            struct((own, FF), F32),
            struct((wide, D), F32),
        )
        + (struct((1, own), F32),) * VECTORS
        + (struct((1, wide), F32),),
        in_specs=[whole(ANY)] * 8,
        out_specs=(whole(),) * (7 + VECTORS),
        scratch_shapes=[
            VMEM(item.shape, item.dtype) for item in (grad, t_qkv, t_out, t_up, rows, tiles)
        ]
        + [pltpu.SemaphoreType.DMA((8,))],
        compiler_params=params_of(63),
        name="present",
    )(hidden, grad, t_qkv, t_out, t_up, t_down, rows, tiles)


def plane_shards(
    hidden_in,
    rand_table,
    norm1_gain,
    norm1_bias,
    w_qkv,
    query_bias,
    value_bias,
    w_out,
    out_bias,
    norm2_gain,
    norm2_bias,
    w_up,
    up_bias,
    w_down,
    down_bias,
    cotangent,
):
    micro, rows, _ = hidden_in.shape
    local = rows // BLOCK

    def in_row(vector, number):
        return jnp.pad(vector[None], ((number, 15 - number), (0, LANES - vector.shape[0])))

    vec = functools.reduce(
        jnp.add,
        [
            in_row(vector, number)
            for number, vector in enumerate(
                (
                    norm1_gain,
                    norm1_bias,
                    query_bias,
                    value_bias,
                    out_bias,
                    norm2_gain,
                    norm2_bias,
                    down_bias,
                    up_bias,
                )
            )
        ],
    )
    tab = jnp.pad(
        rand_table.reshape(micro, local * RANDOM), ((0, 8 - micro), (0, LANES - local * RANDOM))
    )
    (
        mixed,
        x,
        dy,
        w_down_all,
        w_qkv_all,
        w_out_all,
        w_up_all,
        qk,
        shared,
        normed,
        lse,
        vectors,
        up_shift,
        table,
        sorted_table,
    ) = front(hidden_in, cotangent, vec, tab, w_qkv, w_out, w_up, w_down)
    mixed = mixed.reshape(2, SPOTS, PIECES, rows, LANES)
    (
        hidden,
        grad_send,
        dres,
        g_out,
        half_up,
        half_down,
        last_up,
        last_down,
        g_up_bias,
        g_mid,
    ) = plane_middle(
        mixed,
        x,
        dy.reshape(micro * rows, D),
        vectors,
        w_out_all,
        up_shift,
        w_up_all,
        w_down_all.reshape(2, FF // 2, D),
    )
    grid = (2, PLANES, SPOTS)
    dqkv, hidden_out, t_out, t_up, t_down = plane_attention_back(
        table,
        sorted_table,
        qk,
        shared,
        grad_send.reshape(2, SPOTS, PIECES, local, BLOCK, LANES),
        lse,
        hidden,
        [
            g_out.reshape((1,) + grid + g_out.shape[1:]),
            last_up,
            last_down,
        ],
        half_up,
        half_down,
    )
    dqkv = dqkv.reshape(2, SPOTS, PIECES, 3, rows, LANES)
    grad_hidden, t_qkv, sum_rows, sum_tiles = finish_layer(
        dqkv, normed, x, dres, vectors, w_qkv_all, g_mid, g_up_bias
    )

    results = present(hidden_out, grad_hidden, t_qkv, t_out, t_up, t_down, sum_rows, sum_tiles)
    hidden_out, grad_hidden, g_qkv, g_out, g_up, g_down = results[:6]
    n1g, n1b, n2g, n2b, db, ob, qb, vb, ub = (item.reshape(item.size) for item in results[6:])
    return (
        hidden_out,
        grad_hidden,
        n1g,
        n1b,
        g_qkv,
        qb,
        vb,
        g_out,
        ob,
        n2g,
        n2b,
        g_up,
        ub,
        g_down,
        db,
    )


def shards(*arrays):
    micro, rows, _ = arrays[0].shape
    fits = lax.axis_size("gx") == 2 and lax.axis_size("gy") == PLANES * SPOTS
    fits = fits and micro == 2 and rows % BLOCK == 0
    return (plane_shards if fits else general_shards)(*arrays)


def solution(mesh):
    tokens = P(None, AXES, None)
    vector = P(AXES)
    matrix = P(AXES, None)
    placed = (
        tokens,
        tokens,
        vector,
        vector,
        matrix,
        vector,
        vector,
        matrix,
        vector,
        vector,
        vector,
        matrix,
        vector,
        matrix,
        vector,
        tokens,
    )
    returned = (
        tokens,
        tokens,
        vector,
        vector,
        matrix,
        vector,
        vector,
        matrix,
        vector,
        vector,
        vector,
        matrix,
        vector,
        matrix,
        vector,
    )
    return jax.shard_map(
        shards, mesh=mesh, in_specs=placed, out_specs=returned, check_vma=False
    )
```

```python
import functools

import jax
import jax.numpy as jnp
from jax import lax
from jax.experimental import pallas as pl
from jax.experimental.pallas import tpu as pltpu
from jax.sharding import PartitionSpec as P

HEADS = 12
HEAD_DIM = 64
D = 768
FF = 3072
BLOCK = 64
RANDOM = 3
LANES = 2 * HEAD_DIM
EPSILON = 1e-05
NEGATIVE = -1e30
SCALE = HEAD_DIM**-0.5
CHUNK = 256
SPAN = 8

F32 = jnp.float32
BF16 = jnp.bfloat16
VMEM = pltpu.VMEM


def whole(space=VMEM):
    return pl.BlockSpec(memory_space=space)


def params_of(megabytes):
    return pltpu.CompilerParams(vmem_limit_bytes=megabytes * 1024 * 1024)


def head_place(head):
    return (head // 3) * 4 + head % 3


def dot(left, right):
    return lax.dot_general(left, right, (((1,), (0,)), ((), ())), preferred_element_type=F32)


def dot_rt(left, right):
    return lax.dot_general(left, right, (((1,), (1,)), ((), ())), preferred_element_type=F32)


def dot_lt(left, right):
    return lax.dot_general(left, right, (((0,), (0,)), ((), ())), preferred_element_type=F32)


def swap_halves(tile):
    return pltpu.roll(tile, HEAD_DIM, axis=tile.ndim - 1)


def low_lanes(rows):
    return lax.broadcasted_iota(jnp.int32, (rows, LANES), 1) < HEAD_DIM


def norm_parts(values):
    centre = values - jnp.mean(values, axis=-1, keepdims=True)
    spread = jnp.mean(centre * centre, axis=-1, keepdims=True)
    inverse = lax.rsqrt(spread + EPSILON)
    return centre * inverse, inverse


def norm_pull(grad, normal, inverse, gain):
    scaled = grad * gain
    return inverse * (
        scaled
        - jnp.mean(scaled, axis=-1, keepdims=True)
        - normal * jnp.mean(scaled * normal, axis=-1, keepdims=True)
    )


def qkv_kernel(x_ref, gain_ref, shift_ref, w_ref, bias_ref, normed_ref, send_ref):
    micro, rows, _ = x_ref.shape
    values = x_ref[...].reshape(micro * rows, D).astype(F32)
    normal, _ = norm_parts(values)
    normed_ref[...] = (normal * gain_ref[...] + shift_ref[...]).astype(BF16)
    low = low_lanes(rows)
    for chunk in range(3 * D // CHUNK):
        columns = slice(chunk * CHUNK, (chunk + 1) * CHUNK)
        packed = dot(normed_ref[...], w_ref[:, columns]) + bias_ref[:, columns]
        if chunk < D // CHUNK:
            packed = packed.astype(BF16).astype(F32) * SCALE
        for tile in range(CHUNK // LANES):
            part = packed[:, tile * LANES : (tile + 1) * LANES]
            first, second = part[:rows], part[rows:]
            if chunk < D // CHUNK:
                head = (chunk * CHUNK // LANES + tile) * 2
                even = jnp.where(low, first, swap_halves(second))
                odd = jnp.where(low, swap_halves(first), second)
                send_ref[head_place(head), 0] = even.astype(BF16)
                send_ref[head_place(head + 1), 0] = odd.astype(BF16)
            else:
                head = (chunk * CHUNK - D) // LANES + tile
                send_ref[head_place(head), 1] = first.astype(BF16)
                send_ref[head_place(head), 2] = swap_halves(second).astype(BF16)


def qkv_forward(x, gain, shift, w, bias, groups):
    micro, rows, _ = x.shape
    return pl.pallas_call(
        qkv_kernel,
        out_shape=(
            jax.ShapeDtypeStruct((micro * rows, D), BF16),
            jax.ShapeDtypeStruct((groups, 3, rows, LANES), BF16),
        ),
        in_specs=[whole()] * 5,
        out_specs=(whole(), whole()),
        compiler_params=params_of(48),
        name="qkv_forward",
    )(x, gain, shift, w, bias)


def half_mask(low_half):
    lane = lax.broadcasted_iota(jnp.int32, (1, LANES), 1)
    keep = (lane < HEAD_DIM) if low_half else (lane >= HEAD_DIM)
    return jnp.where(keep, 1.0, 0.0).astype(BF16)


def inner_slots(pick, block, blocks):
    ids, bias = picked_slots([pick(block, number) for number in range(RANDOM)], block, blocks)
    edge = (block == 0) | (block == blocks - 1)
    ids[0] = jnp.maximum(ids[0], 0)
    ids[2] = jnp.minimum(ids[2], blocks - 1)
    return ids, bias + jnp.where(edge, NEGATIVE, 0.0).astype(F32)


def slots_of(table_ref, micro, block, blocks):
    picks = [table_ref[micro, block * RANDOM + number] for number in range(RANDOM)]
    return picked_slots(picks, block, blocks)


def picked_slots(picks, block, blocks):
    last = blocks - 1
    ids = [block - 1, block, block + 1, 0, last] + picks
    dropped = [None, None, None, block == 1, block == last - 1]
    for number in range(RANDOM):
        pick = picks[number]
        bad = (jnp.abs(pick - block) <= 1) | (pick == 0) | (pick == last)
        for earlier in range(number):
            bad = bad | (pick == picks[earlier])
        dropped.append(bad)
    lane = lax.broadcasted_iota(jnp.int32, (1, LANES), 1)
    tiles = []
    for pair in range(len(ids) // 2):
        level = [
            0.0 if bad is None else jnp.where(bad, NEGATIVE, 0.0).astype(F32)
            for bad in dropped[2 * pair : 2 * pair + 2]
        ]
        tiles.append(jnp.where(lane < HEAD_DIM, level[0], level[1]))
    return ids, jnp.concatenate(tiles, axis=1)


def attend_kernel(table_ref, qkv_ref, out_ref, lse_ref, s_ref):
    groups, _, local, _, _ = qkv_ref.shape
    blocks = groups * local
    low = low_lanes(BLOCK)
    masks = [half_mask(True), half_mask(False)]

    def load(component, block):
        return qkv_ref[block // local, component, block % local]

    def sparse(block, carry):
        mixed, logs = [], []
        for micro in range(2):
            ids, bias = slots_of(table_ref, micro, block, blocks)
            keys = jnp.concatenate([load(1 + micro, spot) for spot in ids], axis=0)
            query = load(0, block) * masks[micro]
            scores = dot_rt(query, keys) + bias
            top = jnp.max(scores, axis=1, keepdims=True)
            powered = jnp.exp(scores - top)
            total = jnp.sum(powered, axis=1, keepdims=True)
            mixed.append(dot(powered.astype(BF16), keys) * (1.0 / total))
            logs.append(top + jnp.log(total))
        out_ref[block // local, block % local] = jnp.where(low, mixed[1], mixed[0]).astype(BF16)
        lse_ref[block] = jnp.where(low, logs[0], logs[1])
        return carry

    lax.fori_loop(1, blocks - 1, sparse, 0)

    spans = blocks // SPAN
    ends = (0, blocks - 1)
    results = []
    for micro in range(2):
        query = jnp.concatenate([load(0, end) for end in ends], axis=0) * masks[micro]

        def keys_at(span, micro=micro):
            return jnp.concatenate(
                [load(1 + micro, span * SPAN + spot) for spot in range(SPAN)], axis=0
            )

        def first_pass(span, top, query=query, keys_at=keys_at):
            scores = dot_rt(query, keys_at(span))
            s_ref[span] = scores
            return jnp.maximum(top, jnp.max(scores, axis=1, keepdims=True))

        top = lax.fori_loop(0, spans, first_pass, jnp.full((2 * BLOCK, 1), NEGATIVE, F32))

        def second_pass(span, carry, top=top, keys_at=keys_at):
            total, mixed = carry
            powered = jnp.exp(s_ref[span] - top)
            return (
                total + jnp.sum(powered, axis=1, keepdims=True),
                mixed + dot(powered.astype(BF16), keys_at(span)),
            )

        total, mixed = lax.fori_loop(
            0,
            spans,
            second_pass,
            (jnp.zeros((2 * BLOCK, 1), F32), jnp.zeros((2 * BLOCK, LANES), F32)),
        )
        results.append((mixed * (1.0 / total), top + jnp.log(total)))
    for place, end in enumerate(ends):
        rows = slice(place * BLOCK, (place + 1) * BLOCK)
        out_ref[end // local, end % local] = jnp.where(
            low, results[1][0][rows], results[0][0][rows]
        ).astype(BF16)
        lse_ref[end] = jnp.where(low, results[0][1][rows], results[1][1][rows])


def attention_forward(table, qkv):
    groups, _, local, _, _ = qkv.shape
    blocks = groups * local
    return pl.pallas_call(
        attend_kernel,
        out_shape=(
            jax.ShapeDtypeStruct((groups, local, BLOCK, LANES), BF16),
            jax.ShapeDtypeStruct((blocks, BLOCK, LANES), F32),
        ),
        in_specs=[whole(pltpu.SMEM), whole()],
        out_specs=(whole(), whole()),
        scratch_shapes=[VMEM((blocks // SPAN, 2 * BLOCK, SPAN * BLOCK), F32)],
        compiler_params=params_of(48),
        name="attention_forward",
    )(table, qkv)


def attend_back_kernel(table_ref, qkv_ref, grad_ref, lse_ref, out_ref, sums_ref, p_ref, dp_ref):
    groups, _, local, _, _ = qkv_ref.shape
    blocks = groups * local
    low = low_lanes(BLOCK)
    masks = [half_mask(True), half_mask(False)]

    def load(component, block):
        return qkv_ref[block // local, component, block % local]

    def load_grad(block):
        return grad_ref[block // local, block % local]

    def clear(block, carry):
        for micro in range(2):
            sums_ref[micro, block] = jnp.zeros((BLOCK, LANES), F32)
        return carry

    lax.fori_loop(0, blocks, clear, 0)

    def sparse(block, carry):
        grads = []
        for micro in range(2):
            ids, bias = slots_of(table_ref, micro, block, blocks)
            keys = jnp.concatenate([load(1 + micro, spot) for spot in ids], axis=0)
            both = jnp.concatenate(
                [load(0, block) * masks[micro], load_grad(block) * masks[1 - micro]], axis=0
            )
            products = dot_rt(both, keys)
            logs = lse_ref[block][:, micro * HEAD_DIM : micro * HEAD_DIM + 1]
            weights = jnp.exp(products[:BLOCK] + bias - logs)
            grad_weights = products[BLOCK:]
            delta = jnp.sum(weights * grad_weights, axis=1, keepdims=True)
            grad_scores = weights * (grad_weights - delta)
            stacked = jnp.concatenate([grad_scores, weights], axis=0).astype(BF16)
            grads.append(dot(stacked[:BLOCK], keys))
            shares = dot_lt(stacked, both)
            for place, spot in enumerate(ids):
                sums_ref[micro, spot] += shares[place * BLOCK : (place + 1) * BLOCK]
        out_ref[block // local, 0, block % local] = (
            jnp.where(low, grads[0], grads[1]) * SCALE
        ).astype(BF16)
        return carry

    lax.fori_loop(1, blocks - 1, sparse, 0)

    spans = blocks // SPAN
    ends = (0, blocks - 1)
    results = []
    for micro in range(2):
        query = jnp.concatenate([load(0, end) for end in ends], axis=0) * masks[micro]
        grad = jnp.concatenate([load_grad(end) for end in ends], axis=0) * masks[1 - micro]
        both = jnp.concatenate([query, grad], axis=0)
        logs = jnp.concatenate(
            [lse_ref[end][:, micro * HEAD_DIM : micro * HEAD_DIM + 1] for end in ends], axis=0
        )

        def keys_at(span, micro=micro):
            return jnp.concatenate(
                [load(1 + micro, span * SPAN + spot) for spot in range(SPAN)], axis=0
            )

        def first_pass(span, delta, both=both, logs=logs, keys_at=keys_at):
            products = dot_rt(both, keys_at(span))
            weights = jnp.exp(products[: 2 * BLOCK] - logs)
            grad_weights = products[2 * BLOCK :]
            p_ref[span] = weights
            dp_ref[span] = grad_weights
            return delta + jnp.sum(weights * grad_weights, axis=1, keepdims=True)

        delta = lax.fori_loop(0, spans, first_pass, jnp.zeros((2 * BLOCK, 1), F32))

        def second_pass(span, carry, delta=delta, both=both, keys_at=keys_at, micro=micro):
            weights = p_ref[span]
            grad_scores = weights * (dp_ref[span] - delta)
            stacked = jnp.concatenate([grad_scores, weights], axis=0).astype(BF16)
            shares = dot_lt(stacked, both)
            for spot in range(SPAN):
                sums_ref[micro, span * SPAN + spot] += shares[spot * BLOCK : (spot + 1) * BLOCK]
            return carry + dot(stacked[: 2 * BLOCK], keys_at(span))

        results.append(
            lax.fori_loop(0, spans, second_pass, jnp.zeros((2 * BLOCK, LANES), F32))
        )
    for place, end in enumerate(ends):
        rows = slice(place * BLOCK, (place + 1) * BLOCK)
        out_ref[end // local, 0, end % local] = (
            jnp.where(low, results[0][rows], results[1][rows]) * SCALE
        ).astype(BF16)

    def finish(block, carry):
        for micro in range(2):
            out_ref[block // local, 1 + micro, block % local] = sums_ref[micro, block].astype(BF16)
        return carry

    lax.fori_loop(0, blocks, finish, 0)


def attention_backward(table, qkv, grad, lse):
    groups, _, local, _, _ = qkv.shape
    blocks = groups * local
    spans = VMEM((blocks // SPAN, 2 * BLOCK, SPAN * BLOCK), F32)
    return pl.pallas_call(
        attend_back_kernel,
        out_shape=jax.ShapeDtypeStruct(qkv.shape, BF16),
        in_specs=[whole(pltpu.SMEM), whole(), whole(), whole()],
        out_specs=whole(),
        scratch_shapes=[VMEM((2, blocks, BLOCK, LANES), F32), spans, spans],
        compiler_params=params_of(48),
        name="attention_backward",
    )(table, qkv, grad, lse)


def middle_kernel(
    mixed_in_ref,
    x_ref,
    dy_ref,
    w_out_ref,
    out_shift_ref,
    gain_ref,
    shift_ref,
    up_shift_ref,
    down_shift_ref,
    w_up_ref,
    w_down_ref,
    hidden_ref,
    send_ref,
    dres_ref,
    g_out_ref,
    g_up_ref,
    g_down_ref,
    g_up_bias_ref,
    g_small_ref,
    mixed_ref,
    residual_ref,
    second_ref,
    second_t_ref,
    total_ref,
    dsecond_ref,
):
    micro, rows, _ = x_ref.shape
    step = pl.program_id(0)
    low = low_lanes(rows)

    @pl.when(step == 0)
    def _():
        for pair in range(HEADS // 2):
            even = mixed_in_ref[head_place(2 * pair)].astype(F32)
            odd = mixed_in_ref[head_place(2 * pair + 1)].astype(F32)
            columns = slice(pair * LANES, (pair + 1) * LANES)
            mixed_ref[:rows, columns] = jnp.where(low, swap_halves(even), odd).astype(BF16)
            mixed_ref[rows:, columns] = jnp.where(low, even, swap_halves(odd)).astype(BF16)
        residual = x_ref[...].reshape(micro * rows, D).astype(F32) + (
            dot(mixed_ref[...], w_out_ref[...]) + out_shift_ref[...]
        )
        residual_ref[...] = residual
        normal, _ = norm_parts(residual)
        second = normal * gain_ref[...] + shift_ref[...]
        second_ref[...] = second.astype(BF16)
        second_t_ref[...] = second.T.astype(BF16)
        total_ref[...] = jnp.zeros_like(total_ref)
        dsecond_ref[...] = jnp.zeros_like(dsecond_ref)

    upper = dot(second_ref[...], w_up_ref[...]) + up_shift_ref[...]
    factor = 0.7978845608028654
    square = upper * upper
    bent = jnp.tanh(factor * (upper + 0.044715 * (upper * square)))
    half = 0.5 * (1.0 + bent)
    active = (upper * half).astype(BF16)
    slope = half + 0.5 * upper * (1.0 - bent * bent) * (
        factor + (3.0 * 0.044715 * factor) * square
    )
    dy = dy_ref[...]
    total_ref[...] += dot(active, w_down_ref[...])
    g_down_ref[...] = dot_lt(active, dy).astype(g_down_ref.dtype)
    dupper = (dot_rt(dy, w_down_ref[...]) * slope).astype(BF16)
    g_up_bias_ref[...] = jnp.sum(dupper.astype(F32), axis=0, keepdims=True)
    g_up_ref[...] = dot(second_t_ref[...], dupper).astype(g_up_ref.dtype)
    dsecond_ref[...] += dot_rt(dupper, w_up_ref[...])

    @pl.when(step == pl.num_programs(0) - 1)
    def _():
        residual = residual_ref[...]
        hidden_ref[...] = (
            (residual + (total_ref[...] + down_shift_ref[...])).astype(BF16).reshape(x_ref.shape)
        )
        normal, inverse = norm_parts(residual)
        dsecond = dsecond_ref[...]
        grad_out = dy_ref[...].astype(F32)
        g_small_ref[0:1] = jnp.sum(dsecond * normal, axis=0, keepdims=True)
        g_small_ref[1:2] = jnp.sum(dsecond, axis=0, keepdims=True)
        g_small_ref[2:3] = jnp.sum(grad_out, axis=0, keepdims=True)
        dres = grad_out + norm_pull(dsecond, normal, inverse, gain_ref[...])
        dres_ref[...] = dres
        branch = dres.astype(BF16)
        g_small_ref[3:4] = jnp.sum(branch.astype(F32), axis=0, keepdims=True)
        g_out_ref[...] = dot_lt(mixed_ref[...], branch).astype(g_out_ref.dtype)
        dmixed = dot_rt(branch, w_out_ref[...])
        for pair in range(HEADS // 2):
            part = dmixed[:, pair * LANES : (pair + 1) * LANES]
            first, last = part[:rows], part[rows:]
            even = jnp.where(low, last, swap_halves(first))
            odd = jnp.where(low, swap_halves(last), first)
            send_ref[head_place(2 * pair)] = even.astype(BF16)
            send_ref[head_place(2 * pair + 1)] = odd.astype(BF16)


def middle(mixed_in, x, dy, w_out, out_shift, gain, shift, up_shift, down_shift, w_up, w_down, kind):
    micro, rows, _ = x.shape
    tokens = micro * rows
    groups = mixed_in.shape[0]

    def fixed(shape):
        return pl.BlockSpec(shape, lambda step: (0,) * len(shape))

    vector = fixed((1, D))
    steps = FF // CHUNK
    return pl.pallas_call(
        middle_kernel,
        grid=(steps,),
        out_shape=(
            jax.ShapeDtypeStruct(x.shape, BF16),
            jax.ShapeDtypeStruct((groups, rows, LANES), BF16),
            jax.ShapeDtypeStruct((tokens, D), F32),
            jax.ShapeDtypeStruct((D, D), kind),
            jax.ShapeDtypeStruct((D, FF), kind),
            jax.ShapeDtypeStruct((FF, D), kind),
            jax.ShapeDtypeStruct((1, FF), F32),
            jax.ShapeDtypeStruct((4, D), F32),
        ),
        in_specs=[
            fixed(mixed_in.shape),
            fixed(x.shape),
            fixed((tokens, D)),
            fixed((D, D)),
            vector,
            vector,
            vector,
            pl.BlockSpec((1, CHUNK), lambda step: (0, step)),
            vector,
            pl.BlockSpec((D, CHUNK), lambda step: (0, step)),
            pl.BlockSpec((CHUNK, D), lambda step: (step, 0)),
        ],
        out_specs=(
            fixed(x.shape),
            fixed((groups, rows, LANES)),
            fixed((tokens, D)),
            fixed((D, D)),
            pl.BlockSpec((D, CHUNK), lambda step: (0, step)),
            pl.BlockSpec((CHUNK, D), lambda step: (step, 0)),
            pl.BlockSpec((1, CHUNK), lambda step: (0, step)),
            fixed((4, D)),
        ),
        scratch_shapes=[
            VMEM((tokens, D), BF16),
            VMEM((tokens, D), F32),
            VMEM((tokens, D), BF16),
            VMEM((D, tokens), BF16),
            VMEM((tokens, D), F32),
            VMEM((tokens, D), F32),
        ],
        compiler_params=params_of(56),
        name="middle",
    )(mixed_in, x, dy, w_out, out_shift, gain, shift, up_shift, down_shift, w_up, w_down)


def qkv_back_kernel(
    recv_ref,
    normed_ref,
    x_ref,
    dres_ref,
    gain_ref,
    w_ref,
    grad_ref,
    g_qkv_ref,
    g_bias_ref,
    g_small_ref,
    packed_ref,
    normed_t_ref,
    dnormed_ref,
):
    micro, rows, _ = x_ref.shape
    step = pl.program_id(0)
    low = low_lanes(rows)

    @pl.when(step == 0)
    def _():
        for pair in range(HEADS // 2):
            even = recv_ref[head_place(2 * pair), 0].astype(F32)
            odd = recv_ref[head_place(2 * pair + 1), 0].astype(F32)
            spot, columns = pair // 2, slice((pair % 2) * LANES, (pair % 2 + 1) * LANES)
            packed_ref[spot, :rows, columns] = jnp.where(low, even, swap_halves(odd)).astype(BF16)
            packed_ref[spot, rows:, columns] = jnp.where(low, swap_halves(even), odd).astype(BF16)
        for head in range(HEADS):
            spot = D // CHUNK + head // 2
            columns = slice((head % 2) * LANES, (head % 2 + 1) * LANES)
            packed_ref[spot, :rows, columns] = recv_ref[head_place(head), 1]
            packed_ref[spot, rows:, columns] = swap_halves(
                recv_ref[head_place(head), 2].astype(F32)
            ).astype(BF16)
        normed_t_ref[...] = normed_ref[...].astype(F32).T.astype(BF16)
        dnormed_ref[...] = jnp.zeros_like(dnormed_ref)

    packed = packed_ref[step]
    g_bias_ref[...] = jnp.sum(packed.astype(F32), axis=0, keepdims=True)
    g_qkv_ref[...] = dot(normed_t_ref[...], packed).astype(g_qkv_ref.dtype)
    dnormed_ref[...] += dot_rt(packed, w_ref[...])

    @pl.when(step == pl.num_programs(0) - 1)
    def _():
        normal, inverse = norm_parts(x_ref[...].reshape(micro * rows, D).astype(F32))
        dnormed = dnormed_ref[...]
        g_small_ref[0:1] = jnp.sum(dnormed * normal, axis=0, keepdims=True)
        g_small_ref[1:2] = jnp.sum(dnormed, axis=0, keepdims=True)
        grad = dres_ref[...] + norm_pull(dnormed, normal, inverse, gain_ref[...])
        grad_ref[...] = grad.reshape(x_ref.shape)


def qkv_backward(recv, normed, x, dres, gain, w, kind):
    micro, rows, _ = x.shape
    tokens = micro * rows

    def fixed(shape):
        return pl.BlockSpec(shape, lambda step: (0,) * len(shape))

    steps = 3 * D // CHUNK
    return pl.pallas_call(
        qkv_back_kernel,
        grid=(steps,),
        out_shape=(
            jax.ShapeDtypeStruct(x.shape, F32),
            jax.ShapeDtypeStruct((D, 3 * D), kind),
            jax.ShapeDtypeStruct((1, 3 * D), F32),
            jax.ShapeDtypeStruct((2, D), F32),
        ),
        in_specs=[
            fixed(recv.shape),
            fixed((tokens, D)),
            fixed(x.shape),
            fixed((tokens, D)),
            fixed((1, D)),
            pl.BlockSpec((D, CHUNK), lambda step: (0, step)),
        ],
        out_specs=(
            fixed(x.shape),
            pl.BlockSpec((D, CHUNK), lambda step: (0, step)),
            pl.BlockSpec((1, CHUNK), lambda step: (0, step)),
            fixed((2, D)),
        ),
        scratch_shapes=[
            VMEM((steps, tokens, CHUNK), BF16),
            VMEM((D, tokens), BF16),
            VMEM((tokens, D), F32),
        ],
        compiler_params=params_of(56),
        name="qkv_backward",
    )(recv, normed, x, dres, gain, w)


AXES = ("gx", "gy")


def gather(array):
    return lax.all_gather(array, AXES, axis=0, tiled=True)


def scatter(array):
    return lax.psum_scatter(array, AXES, scatter_dimension=0, tiled=True)


def exchange(array):
    return lax.all_to_all(array, "gy", 0, 0, tiled=True)


def by_heads(w_qkv):
    rows = w_qkv.shape[0]
    sides = w_qkv[:, D:].reshape(rows, 2, HEADS, HEAD_DIM)
    return jnp.concatenate([w_qkv[:, :D], jnp.swapaxes(sides, 1, 2).reshape(rows, 2 * D)], axis=1)


def by_parts(w_qkv):
    rows = w_qkv.shape[0]
    sides = w_qkv[:, D:].reshape(rows, HEADS, 2, HEAD_DIM)
    return jnp.concatenate([w_qkv[:, :D], jnp.swapaxes(sides, 1, 2).reshape(rows, 2 * D)], axis=1)


def general_shards(
    hidden_in,
    rand_table,
    norm1_gain,
    norm1_bias,
    w_qkv,
    query_bias,
    value_bias,
    w_out,
    out_bias,
    norm2_gain,
    norm2_bias,
    w_up,
    up_bias,
    w_down,
    down_bias,
    cotangent,
):
    micro, rows, _ = hidden_in.shape
    groups = lax.axis_size("gy")
    local = rows // BLOCK
    own = norm1_gain.shape[0]

    vectors = jnp.concatenate(
        [
            norm1_gain,
            norm1_bias,
            query_bias,
            value_bias,
            out_bias,
            norm2_gain,
            norm2_bias,
            down_bias,
            up_bias,
        ]
    )
    table = lax.all_gather(rand_table, "gy", axis=1, tiled=True)
    table = table.reshape(micro, groups * local * RANDOM)
    vectors = gather(vectors[None]).astype(F32)
    gain_one, shift_one, query_shift, value_shift, out_shift, gain_two, shift_two, down_shift = (
        vectors[:, number * own : (number + 1) * own].reshape(1, D) for number in range(8)
    )
    up_shift = vectors[:, 8 * own :].reshape(1, FF)
    w_qkv_full = gather(by_heads(w_qkv))
    w_out_full, w_up_full, w_down_full = gather(w_out), gather(w_up), gather(w_down)
    packed_bias = by_heads(
        jnp.concatenate([query_shift, jnp.zeros_like(query_shift), value_shift], axis=1)
    )

    normed, send = qkv_forward(hidden_in, gain_one, shift_one, w_qkv_full, packed_bias, groups)
    qkv = exchange(send).reshape(groups, 3, local, BLOCK, LANES)
    mixed, lse = attention_forward(table, qkv)
    mixed_back = exchange(mixed.reshape(groups, rows, LANES))
    hidden_out, grad_send, dres, g_out, g_up, g_down, g_up_bias, g_mid = middle(
        mixed_back,
        hidden_in,
        cotangent.reshape(micro * rows, D),
        w_out_full,
        out_shift,
        gain_two,
        shift_two,
        up_shift,
        down_shift,
        w_up_full,
        w_down_full,
        F32,
    )
    grad_mixed = exchange(grad_send).reshape(groups, local, BLOCK, LANES)
    dqkv = attention_backward(table, qkv, grad_mixed, lse)
    dqkv_back = exchange(dqkv.reshape(groups, 3, rows, LANES))
    grad_hidden, g_qkv, g_packed, g_first = qkv_backward(
        dqkv_back, normed, hidden_in, dres, gain_one, w_qkv_full, F32
    )

    g_packed = by_parts(g_packed)
    small = [
        g_first[0],
        g_first[1],
        g_packed[0, :D],
        g_packed[0, 2 * D :],
        g_mid[3],
        g_mid[0],
        g_mid[1],
        g_mid[2],
    ]
    ranks = D // own
    small = jnp.concatenate(
        [item.reshape(ranks, own) for item in small] + [g_up_bias.reshape(ranks, 4 * own)], axis=1
    )
    small = scatter(small)[0]
    parts = [small[number * own : (number + 1) * own] for number in range(8)]
    return (
        hidden_out,
        grad_hidden,
        parts[0],
        parts[1],
        by_parts(scatter(g_qkv)),
        parts[2],
        parts[3],
        scatter(g_out),
        parts[4],
        parts[5],
        parts[6],
        scatter(g_up),
        small[8 * own :],
        scatter(g_down),
        parts[7],
    )


MESH = pl.DeviceIdType.MESH
ANY = pl.ANY
PLANES = 4
SPOTS = 4
PIECES = 2
RANKS = 2 * PLANES * SPOTS
TILES = 3 * D // LANES
HALF_TILES = TILES // 2
QUERY_ORDER = (0, 2, 3, 5, 6, 8, 9, 11, 1, 4, 7, 10)


def column_order():
    order = [("q", head) for head in QUERY_ORDER]
    for spot in range(SPOTS):
        for place in (2 * 3 * spot, 2 * 3 * spot + 2):
            order += [("k", place // 2), ("v", place // 2)]
        order += [("v", 3 * spot + 2), ("k", 3 * spot + 2)]
    return order


def natural_block(entry):
    return "qkv".index(entry[0]) * HEADS + entry[1]


def flip(value, bits):
    if bits == 0:
        return value
    if bits == 1:
        return value + 1 - 2 * lax.rem(value, 2)
    if bits == 2:
        return value + 2 - 4 * lax.div(value, 2)
    return 3 - value


def place_here():
    core, rank = lax.axis_index("gx"), lax.axis_index("gy")
    return core, lax.div(rank, SPOTS), lax.rem(rank, SPOTS)


def rank_of(plane, spot):
    return plane * SPOTS + spot


def greet(partners):
    barrier = pltpu.get_barrier_semaphore()
    for partner in partners:
        pl.semaphore_signal(barrier, inc=1, device_id=partner, device_id_type=MESH)
    pl.semaphore_wait(barrier, len(partners))


def remote(source, target, send_sem, recv_sem, device):
    return pltpu.make_async_remote_copy(
        src_ref=source,
        dst_ref=target,
        send_sem=send_sem,
        recv_sem=recv_sem,
        device_id=device,
        device_id_type=MESH,
    )


def column_partners(core, plane, spot):
    partners = [(1 - core, rank_of(plane, spot))]
    for bits in range(1, PLANES):
        for other in (core, 1 - core):
            partners.append((other, rank_of(flip(plane, bits), spot)))
    return partners


def all_partners(core, plane, spot):
    return column_partners(core, plane, spot) + [
        (core, rank_of(plane, flip(spot, 1))),
        (core, rank_of(plane, flip(spot, 2))),
    ]


def to_planes(source, target, send_sem, recv_sem, local_sem):
    core, plane, spot = place_here()
    half, odd = lax.div(plane, 2), lax.rem(plane, 2)
    sends, keeps = [], []
    for micro in range(2):
        goal = 2 * micro + core
        here = (goal == plane) & (half == core)
        send = remote(
            source.at[micro],
            target.at[odd],
            send_sem.at[micro],
            recv_sem.at[odd],
            (half, rank_of(goal, spot)),
        )
        keep = pltpu.make_async_copy(source.at[micro], target.at[odd], local_sem.at[micro])

        @pl.when(jnp.logical_not(here))
        def _(send=send):
            send.start()

        @pl.when(here)
        def _(keep=keep):
            keep.start()

        sends.append((here, send))
        keeps.append((here, keep))

    def finish():
        for piece in range(PIECES):
            mine = (odd == core) & (plane == 2 * core + piece)
            arrival = remote(
                source.at[0],
                target.at[piece],
                send_sem.at[0],
                recv_sem.at[piece],
                (core, rank_of(plane, spot)),
            )

            @pl.when(jnp.logical_not(mine))
            def _(arrival=arrival):
                arrival.wait_recv()

        for (here, send), (_, keep) in zip(sends, keeps):

            @pl.when(jnp.logical_not(here))
            def _(send=send):
                send.wait_send()

            @pl.when(here)
            def _(keep=keep):
                keep.wait()

    return finish


def from_planes(source, target, send_sem, recv_sem, local_sem, later=False):
    core, plane, spot = place_here()
    micro, odd = lax.div(plane, 2), lax.rem(plane, 2)
    sends, keeps = [], []

    def start(piece):
        goal = 2 * core + piece
        here = (goal == plane) & (odd == core)
        send = remote(
            source.at[piece],
            target.at[micro],
            send_sem.at[piece],
            recv_sem.at[micro],
            (odd, rank_of(goal, spot)),
        )
        keep = pltpu.make_async_copy(source.at[piece], target.at[micro], local_sem.at[piece])

        @pl.when(jnp.logical_not(here))
        def _(send=send):
            send.start()

        @pl.when(here)
        def _(keep=keep):
            keep.start()

        sends.append((here, send))
        keeps.append((here, keep))

    for piece in () if later else range(PIECES):
        start(piece)

    def finish():
        for number in range(2):
            mine = (2 * number + core == plane) & (micro == core)
            arrival = remote(
                source.at[0],
                target.at[number],
                send_sem.at[0],
                recv_sem.at[number],
                (core, rank_of(plane, spot)),
            )

            @pl.when(jnp.logical_not(mine))
            def _(arrival=arrival):
                arrival.wait_recv()

        for (here, send), (_, keep) in zip(sends, keeps):

            @pl.when(jnp.logical_not(here))
            def _(send=send):
                send.wait_send()

            @pl.when(here)
            def _(keep=keep):
                keep.wait()

    return (start, finish) if later else finish


class Gather:
    SENDS = 31

    def __init__(self, source, target, send_sem, recv_sem, local_sem):
        self.source, self.target = source, target
        self.send_sem, self.recv_sem = send_sem, recv_sem
        self.core, self.plane, self.spot = place_here()
        self.sends = []
        self.own = pltpu.make_async_copy(
            source, target.at[self.core, self.plane, self.spot], local_sem
        )
        self.own.start()

    def send(self, source, plane, spot, device):
        copy = remote(
            source,
            self.target.at[self.core, plane, spot],
            self.send_sem.at[len(self.sends)],
            self.recv_sem.at[self.core, plane, spot],
            device,
        )
        copy.start()
        self.sends.append(copy)

    def arrive(self, core, plane, spot):
        shard = self.target.at[core, plane, spot]
        remote(
            shard,
            shard,
            self.send_sem.at[0],
            self.recv_sem.at[core, plane, spot],
            (self.core, rank_of(self.plane, self.spot)),
        ).wait_recv()

    def neighbour(self, bits):
        return (self.core, rank_of(self.plane, flip(self.spot, bits)))

    def sibling(self):
        return (1 - self.core, rank_of(self.plane, self.spot))

    def start(self):
        for bits in range(1, PLANES):
            goal = (self.core, rank_of(flip(self.plane, bits), self.spot))
            self.send(self.source, self.plane, self.spot, goal)
        for goal in (self.neighbour(1), self.neighbour(2), self.sibling()):
            self.send(self.source, self.plane, self.spot, goal)

    def column(self):
        for bits in range(1, PLANES):
            plane = flip(self.plane, bits)
            self.arrive(self.core, plane, self.spot)
            shard = self.target.at[self.core, plane, self.spot]
            for goal in (self.neighbour(1), self.neighbour(2), self.sibling()):
                self.send(shard, plane, self.spot, goal)

    def across(self):
        for bits in range(PLANES):
            plane = flip(self.plane, bits)
            for side in (1, 2):
                spot = flip(self.spot, side)
                self.arrive(self.core, plane, spot)
                shard = self.target.at[self.core, plane, spot]
                if (side == 1) == (bits < 2):
                    self.send(shard, plane, spot, self.neighbour(3 - side))
                self.send(shard, plane, spot, self.sibling())

    def corner(self):
        spot = flip(self.spot, 3)
        for bits in range(PLANES):
            plane = flip(self.plane, bits)
            self.arrive(self.core, plane, spot)
            self.send(self.target.at[self.core, plane, spot], plane, spot, self.sibling())

    def finish(self):
        for bits in range(PLANES):
            for side in range(SPOTS):
                self.arrive(1 - self.core, flip(self.plane, bits), flip(self.spot, side))
        self.own.wait()
        for copy in self.sends:
            copy.wait_send()


def settle(shards_ref, plan):
    rows = shards_ref.shape[3] // 2

    def pair(number, carry):
        core, plane, side = (
            lax.div(number, 2 * PLANES),
            lax.rem(lax.div(number, 2), PLANES),
            lax.rem(number, 2),
        )
        goal = pl.ds(pl.multiple_of(number * 2 * rows, 16), 2 * rows)
        for tile, out_ref, (left, right) in plan:
            columns = slice(tile * LANES, (tile + 1) * LANES)
            first = shards_ref[core, plane, 2 * side, :, columns].astype(F32)
            second = shards_ref[core, plane, 2 * side + 1, :, columns].astype(F32)
            out_ref[goal, left * LANES : (left + 1) * LANES] = jnp.concatenate(
                [first[:rows], second[:rows]], axis=0
            ).astype(BF16)
            out_ref[goal, right * LANES : (right + 1) * LANES] = jnp.concatenate(
                [first[rows:], second[rows:]], axis=0
            ).astype(BF16)
        return carry

    lax.fori_loop(0, RANKS // 2, pair, 0)


def alternate(tile):
    return 2 * tile, 2 * tile + 1


def plane_partners(core, plane, spot):
    partners = []
    for other in (core, 1 - core):
        for side in range(SPOTS):
            if other is core and side == 0:
                continue
            partners.append((other, rank_of(plane, flip(spot, side))))
    return partners


def both_partners(core, plane, spot):
    return plane_partners(core, plane, spot) + column_partners(core, plane, spot)[1:]


def exchange_sems(recv_shape):
    return [
        pltpu.SemaphoreType.DMA((14,)),
        pltpu.SemaphoreType.DMA(recv_shape),
        pltpu.SemaphoreType.DMA((PIECES,)),
    ]


def sort_entries(table, sorted_ref, entries):
    count = table.shape[1]
    core = lax.axis_index("gx")
    lane = lax.broadcasted_iota(jnp.int32, (count, count), 1)
    row = lax.broadcasted_iota(jnp.int32, (count, count), 0).astype(F32)
    everything = jnp.broadcast_to(table, (count, count))
    half = entries // 2
    inside = (lane >= core * half) & (lane < (core + 1) * half)
    lane = lane.astype(F32)
    for number, along in enumerate((everything, jnp.where(inside, everything, 2.0 * LANES))):
        down = along.T
        before = (along < down) | ((along == down) & (lane < row))
        rank = jnp.sum(jnp.where(before, 1.0, 0.0), axis=1, keepdims=True)
        order = jnp.sum(jnp.where(rank == lane, row, 0.0), axis=0, keepdims=True)
        upto = jnp.sum(jnp.where(down <= lane, 1.0, 0.0), axis=0, keepdims=True)
        sorted_ref[2 * number : 2 * number + 1] = order.astype(jnp.int32)
        sorted_ref[2 * number + 1 : 2 * number + 2] = upto.astype(jnp.int32)


def pack_halves(read, target_ref, place, local, low, half):
    for number in range(local // 2):
        first = read(2 * number).astype(F32)
        second = swap_halves(read(2 * number + 1).astype(F32))
        kept = (first, second) if half == 0 else (second, first)
        target_ref[place + (number,)] = jnp.where(low, *kept).astype(BF16)


class Outward:
    def __init__(self, source, far_source, target, packed, send_sem, recv_sem, local_sem):
        self.target, self.packed = target, packed
        self.recv_sem, self.send_sem = recv_sem, send_sem
        self.core, self.plane, self.spot = place_here()
        self.sends, self.keeps = [], []
        for side in (3, 1, 2, 0):
            goal = flip(self.spot, side)
            for other in (self.core, 1 - self.core):
                near = other is self.core
                for piece in range(PIECES):
                    start = (source if near else far_source).at[goal, piece]
                    place = (2 * self.core + piece, self.spot)
                    stop = (target if near else packed).at[place]
                    if side == 0 and near:
                        copy = pltpu.make_async_copy(start, stop, local_sem.at[piece])
                        self.keeps.append(copy)
                    else:
                        copy = remote(
                            start,
                            stop,
                            send_sem.at[len(self.sends)],
                            recv_sem.at[place],
                            (other, rank_of(self.plane, goal)),
                        )
                        self.sends.append(copy)
                    copy.start()

    def arrive(self, side):
        goal = flip(self.spot, side)
        for other in (self.core, 1 - self.core):
            near = other is self.core
            if side == 0 and near:
                for copy in self.keeps:
                    copy.wait()
                continue
            for piece in range(PIECES):
                place = (2 * other + piece, goal)
                landed = (self.target if near else self.packed).at[place]
                remote(
                    landed,
                    landed,
                    self.send_sem.at[0],
                    self.recv_sem.at[place],
                    (self.core, rank_of(self.plane, self.spot)),
                ).wait_recv()
                if not near:
                    for number in range(self.packed.shape[2]):
                        tile = self.packed[place + (number,)]
                        self.target[place + (2 * number,)] = tile
                        self.target[place + (2 * number + 1,)] = swap_halves(
                            tile.astype(F32)
                        ).astype(BF16)

    def finish(self):
        for copy in self.sends:
            copy.wait_send()


def inward_targets(core, spot):
    for side in (3, 1, 2, 0):
        for other in (core, 1 - core):
            yield side, other, flip(spot, side), side == 0 and other is core


class Inward:
    def __init__(self, source, target, send_sem, recv_sem, local_sem):
        self.source, self.target = source, target
        self.send_sem, self.recv_sem, self.local_sem = send_sem, recv_sem, local_sem
        self.core, self.plane, self.spot = place_here()
        self.sends, self.keeps = [], []

    def send(self, other, goal, stays, piece, part, parts):
        source = self.source.at[2 * other + piece, goal, parts]
        target = self.target.at[self.core, self.spot, piece, parts]
        if stays:
            copy = pltpu.make_async_copy(source, target, self.local_sem.at[part, piece])
            self.keeps.append(copy)
        else:
            copy = remote(
                source,
                target,
                self.send_sem.at[len(self.sends)],
                self.recv_sem.at[self.core, self.spot, piece, part],
                (other, rank_of(self.plane, goal)),
            )
            self.sends.append(copy)
        copy.start()

    def finish(self, parts_of):
        for side, other, goal, stays in inward_targets(self.core, self.spot):
            if stays:
                continue
            for piece in range(PIECES):
                for part, parts in enumerate(parts_of[0 if other is self.core else 1]):
                    target = self.target.at[other, goal, piece, parts]
                    remote(
                        target,
                        target,
                        self.send_sem.at[0],
                        self.recv_sem.at[other, goal, piece, part],
                        (self.core, rank_of(self.plane, self.spot)),
                    ).wait_recv()
        for copy in self.sends:
            copy.wait_send()
        for copy in self.keeps:
            copy.wait()


KEYS_A, QUERIES, KEYS_B = range(3)


def plane_attend_back_kernel(*refs):
    table_ref, sorted_ref, qk_ref, shared_ref, near_grad_ref, far_grad_ref, lse_ref, hidden_ref = (
        refs[:8]
    )
    sources, half_up_ref, half_down_ref, refs = refs[8:11], refs[11], refs[12], refs[13:]
    sources = list(sources[:2]) + [sources[2].at[number] for number in range(LATE)]
    back_ref, hidden_out_ref, t_out_ref, t_up_ref, t_down_ref = refs[:5]
    count = 2 + LATE
    refs = refs[5:]
    buffers, mines, refs = refs[: 3 * count], refs[3 * count : 4 * count], refs[4 * count :]
    part_out_ref, part_up_ref, part_down_ref, far_out_ref, far_up_ref, far_down_ref = refs[:6]
    grad_ref, packed_ref, out_ref, sums_ref, shares_ref, walked_ref, sibling_ref = refs[6:13]
    scores_refs, refs = refs[13:17], refs[17:]
    reduce_send, reduce_recv, far_send, far_recv, load_sem = refs[:5]
    grad_sems, back_sems, move_sems, sibling_sems = refs[5:8], refs[8:11], refs[11:14], refs[14:16]

    local = qk_ref.shape[3]
    groups = PLANES * SPOTS
    blocks = groups * local
    core, plane, spot = place_here()
    low = low_lanes(BLOCK)
    masks = [half_mask(True), half_mask(False)]

    greet(both_partners(core, plane, spot))
    grads = Outward(near_grad_ref, far_grad_ref, grad_ref, packed_ref, *grad_sems)
    reduces = [
        SpotReduce(
            source,
            *buffers[3 * number : 3 * number + 3],
            reduce_send.at[number],
            reduce_recv.at[number],
            rows=FF // RANKS if number >= 2 else None,
            mine=mine,
        )
        for number, (source, mine) in enumerate(zip(sources, mines))
    ]
    ready = PER_STAGE * EARLY
    loads = [
        pltpu.make_async_copy(one.half(core), mine, load_sem.at[number])
        for number, (one, mine) in enumerate(zip(reduces, mines))
    ] + [
        pltpu.make_async_copy(half_up_ref, part_up_ref.at[0:ready], load_sem.at[count]),
        pltpu.make_async_copy(half_down_ref, part_down_ref.at[0:EARLY], load_sem.at[count + 1]),
    ]
    for one in reduces:
        one.start()
    for copy in loads:
        copy.start()

    def far(bits, number, source, target):
        return remote(
            source,
            target,
            far_send.at[number, bits - 1],
            far_recv.at[number, bits - 1],
            (core, rank_of(flip(plane, bits), spot)),
        )

    def far_down(bits, source):
        return far(bits, 3, source, far_down_ref.at[bits - 1])

    fars = []
    for bits in range(1, PLANES):
        goal = flip(plane, bits)
        copy = far(bits, 0, half_up_ref.at[:, goal], far_up_ref.at[bits - 1, 0:ready])
        copy.start()
        fars.append(copy)

        @pl.when(goal < EARLY)
        def _(bits=bits, goal=goal):
            far_down(bits, half_down_ref.at[jnp.minimum(goal, EARLY - 1)]).start()

    finish_hidden = from_planes(hidden_ref, hidden_out_ref, *move_sems)

    def load(component, block):
        rank, number = lax.div(block, local), lax.rem(block, local)
        if component == 2:
            return shared_ref[lax.div(rank, SPOTS), lax.rem(rank, SPOTS), number]
        return qk_ref[lax.div(rank, SPOTS), lax.rem(rank, SPOTS), component, number]

    def load_grad(block):
        rank = lax.div(block, local)
        return grad_ref[lax.div(rank, SPOTS), lax.rem(rank, SPOTS), lax.rem(block, local)]

    def store(component, block, value):
        rank = lax.div(block, local)
        out_ref[
            lax.div(rank, SPOTS), lax.rem(rank, SPOTS), component, lax.rem(block, local)
        ] = value.astype(BF16)

    def stored(component, block):
        rank = lax.div(block, local)
        return out_ref[
            lax.div(rank, SPOTS), lax.rem(rank, SPOTS), component, lax.rem(block, local)
        ].astype(F32)

    nothing = jnp.zeros((BLOCK, LANES), F32)

    def clear(block, carry):
        for slot in range(2):
            sums_ref[slot, block] = nothing
        return carry

    lax.fori_loop(0, blocks, clear, 0)

    def picked(block, number):
        return table_ref[0, block * RANDOM + number]

    def one_block(block, slot):
        ids, bias = inner_slots(picked, block, blocks)
        keys = jnp.concatenate([load(1 + slot, number) for number in ids], axis=0)
        both = jnp.concatenate(
            [load(0, block) * masks[slot], load_grad(block) * masks[1 - slot]], axis=0
        )
        products = dot_rt(both, keys)
        logs = lse_ref[block][:, slot * HEAD_DIM : slot * HEAD_DIM + 1]
        weights = jnp.exp(products[:BLOCK] + bias - logs)
        grad_weights = products[BLOCK:]
        delta = jnp.sum(weights * grad_weights, axis=1, keepdims=True)
        grad_scores = weights * (grad_weights - delta)
        stacked = jnp.concatenate([grad_scores, weights], axis=0).astype(BF16)
        return dot(stacked[:BLOCK], keys), dot_lt(stacked, both)

    fixed = 5

    def rank_blocks(rank, slot):
        first = rank * local
        results = [one_block(first + number, slot) for number in range(local)]

        def share(number, place):
            return results[number][1][place * BLOCK : (place + 1) * BLOCK]

        for shift in range(-1, local + 1):
            parts = [
                share(number, shift - number + 1)
                for number in range(local)
                if 0 <= shift - number + 1 <= 2
            ]
            target = jnp.minimum(jnp.maximum(first + shift, 0), blocks - 1)
            sums_ref[slot, target] += functools.reduce(jnp.add, parts)
        for place, target in ((3, 0), (4, blocks - 1)):
            sums_ref[slot, target] += functools.reduce(
                jnp.add, [share(number, place) for number in range(local)]
            )
        for number in range(local):
            for pick in range(RANDOM):
                shares_ref[slot, (first + number) * RANDOM + pick] = share(number, fixed + pick)
        return [result[0] for result in results]

    def head_a(side):
        def body(number, carry):
            rank = number * SPOTS + flip(spot, side)
            for place, query in enumerate(rank_blocks(rank, 0)):
                store(QUERIES, rank * local + place, query * SCALE)
            return carry

        lax.fori_loop(0, PLANES, body, 0)

    def head_b(number, carry):
        rank = core * (groups // 2) + number
        for place, query in enumerate(rank_blocks(rank, 1)):
            block = rank * local + place
            store(QUERIES, block, jnp.where(low, stored(QUERIES, block), query * SCALE))
        return carry

    spans = blocks // SPAN
    ends = (0, blocks - 1)

    def dense(slot, p_ref, d_ref, numbers):
        both = jnp.concatenate(
            [load(0, number) * masks[slot] for number in numbers]
            + [load_grad(number) * masks[1 - slot] for number in numbers],
            axis=0,
        )
        rows = len(numbers) * BLOCK
        column = slot * HEAD_DIM
        logs = jnp.concatenate(
            [lse_ref[number][:, column : column + 1] for number in numbers], axis=0
        )

        def keys_at(span):
            return jnp.concatenate(
                [load(1 + slot, span * SPAN + number) for number in range(SPAN)], axis=0
            )

        def first_pass(span, delta):
            products = dot_rt(both, keys_at(span))
            weights = jnp.exp(products[:rows] - logs)
            grad_weights = products[rows:]
            p_ref[span] = weights
            d_ref[span] = grad_weights
            return delta + jnp.sum(weights * grad_weights, axis=1, keepdims=True)

        delta = lax.fori_loop(0, spans, first_pass, jnp.zeros((rows, 1), F32), unroll=2)

        def second_pass(span, total):
            weights = p_ref[span]
            grad_scores = weights * (d_ref[span] - delta)
            stacked = jnp.concatenate([grad_scores, weights], axis=0).astype(BF16)
            shares = dot_lt(stacked, both)
            for number in range(SPAN):
                sums_ref[slot, span * SPAN + number] += shares[
                    number * BLOCK : (number + 1) * BLOCK
                ]
            return total + dot(stacked[:rows], keys_at(span))

        total = lax.fori_loop(0, spans, second_pass, jnp.zeros((rows, LANES), F32), unroll=2)
        for place, number in enumerate(numbers):
            query = total[place * BLOCK : (place + 1) * BLOCK] * SCALE
            if slot == 1:
                query = jnp.where(low, stored(QUERIES, number), query)
            store(QUERIES, number, query)

    def walk(slot, length):
        def body(number, total):
            entry = sorted_ref[2 * slot, number]
            earlier = sorted_ref[2 * slot, jnp.maximum(number - 1, 0)]
            keep = jnp.where(table_ref[0, entry] == table_ref[0, earlier], 1.0, 0.0).astype(F32)
            total = total * keep + shares_ref[slot, entry]
            walked_ref[slot, number] = total.astype(BF16)
            return total

        lax.fori_loop(0, length, body, nothing, unroll=4)

    def close(slot, rank, component):
        def body(number, carry):
            block = rank * local + number
            stop = sorted_ref[2 * slot + 1, block]
            start = jnp.where(block == 0, 0, sorted_ref[2 * slot + 1, jnp.maximum(block - 1, 0)])
            some = jnp.where(stop > start, 1.0, 0.0).astype(F32)
            share = walked_ref[slot, jnp.maximum(stop - 1, 0)].astype(F32)
            store(component, block, sums_ref[slot, block] + share * some)
            return carry

        lax.fori_loop(0, local, body, 0, unroll=True)

    back = Inward(out_ref, back_ref, *back_sems)
    own_parts = (slice(0, 1), slice(1, 2), slice(2, 3))
    far_parts = (slice(0, 2),)

    for side in range(SPOTS):
        grads.arrive(side)
        head_a(side)
        if side == 0:
            for copy in loads:
                copy.wait()
            for one in reduces:
                one.corners()
        if side == 2:
            for one in reduces:
                one.sides()
    dense(0, scores_refs[0], scores_refs[1], ends)
    reduces[0].close(part_out_ref)
    reduces[1].close(part_up_ref.at[ready : PER_STAGE * STAGES])
    for number in range(LATE):
        reduces[2 + number].close(part_down_ref.at[EARLY + number])
    for bits in range(1, PLANES):
        goal = flip(plane, bits)
        late = slice(ready, PER_STAGE * STAGES)
        for copy in (
            far(bits, 1, part_out_ref.at[:, goal], far_out_ref.at[bits - 1]),
            far(bits, 2, part_up_ref.at[late, goal], far_up_ref.at[bits - 1, late]),
        ):
            copy.start()
            fars.append(copy)

        @pl.when(goal >= EARLY)
        def _(bits=bits, goal=goal):
            far_down(bits, part_down_ref.at[goal]).start()

        fars.append(far_down(bits, part_down_ref.at[goal]))
    walk(0, blocks * RANDOM)
    for side, other, goal, stays in inward_targets(core, spot):
        for piece in range(PIECES):
            close(0, (2 * other + piece) * SPOTS + goal, KEYS_A)
            if other is core:
                back.send(other, goal, stays, piece, 0, own_parts[0])
            else:
                back.send(other, goal, stays, piece, 0, far_parts[0])
    lax.fori_loop(0, groups // 2, head_b, 0)
    dense(1, scores_refs[2], scores_refs[3], (core * (blocks - 1),))
    for side, other, goal, stays in inward_targets(core, spot):
        if other is core:
            for piece in range(PIECES):
                back.send(other, goal, stays, piece, 1, own_parts[1])
    walk(1, blocks * RANDOM // 2)
    for number in range(PIECES):
        for goal in range(SPOTS):
            close(1, (2 * (1 - core) + number) * SPOTS + goal, KEYS_B)
    across = remote(
        out_ref.at[pl.ds(2 * (1 - core), PIECES), :, KEYS_B],
        sibling_ref,
        sibling_sems[0],
        sibling_sems[1],
        (1 - core, rank_of(plane, spot)),
    )
    across.start()
    for number in range(PIECES):
        for goal in range(SPOTS):
            close(1, (2 * core + number) * SPOTS + goal, KEYS_B)
    across.wait_recv()
    for side, other, goal, stays in inward_targets(core, spot):
        if other is core:
            for piece in range(PIECES):
                place = (2 * core + piece, goal, KEYS_B)
                out_ref[place] = (
                    out_ref[place].astype(F32) + sibling_ref[piece, goal].astype(F32)
                ).astype(BF16)
                back.send(other, goal, stays, piece, 2, own_parts[2])
    for copy in fars:
        copy.wait()

    def total(part, far, index):
        value = part.astype(F32)
        for bits in range(PLANES - 1):
            value = value + far[(bits,) + index].astype(F32)
        return value

    t_out_ref[...] = total(part_out_ref[0, plane], far_out_ref, (0,))

    def close_up(number, carry):
        t_up_ref[number] = total(part_up_ref[number, plane], far_up_ref, (number,))
        return carry

    lax.fori_loop(0, PER_STAGE * STAGES, close_up, 0)
    t_down_ref[...] = total(part_down_ref[plane], far_down_ref, ())
    finish_hidden()
    grads.finish()
    across.wait_send()
    back.finish((own_parts, far_parts))


def plane_attention_back(
    table, sorted_table, qk, shared, near, far, lse, hidden, sources, half_up, half_down
):
    local = qk.shape[3]
    blocks = PLANES * SPOTS * local
    spans = blocks // SPAN
    shard, rows = D // RANKS, FF // RANKS
    up_count = PER_STAGE * STAGES
    up_tail, out_tail = (2 * shard, LANES), (2 * shard, D // 2)
    buffers = block_scratch(1, *out_tail) + block_scratch(PER_STAGE * LATE, *up_tail)
    for _ in range(LATE):
        buffers += row_scratch(rows, D)
    count = 2 + LATE
    mines = [
        VMEM((1, PLANES, SPOTS) + out_tail, BF16),
        VMEM((PER_STAGE * LATE, PLANES, SPOTS) + up_tail, BF16),
    ] + [VMEM((SPOTS * rows, D), BF16)] * LATE
    parts = [
        VMEM((1, PLANES) + out_tail, BF16),
        VMEM((up_count, PLANES) + up_tail, BF16),
        VMEM((STAGES, rows, D), BF16),
        VMEM((PLANES - 1, 1) + out_tail, BF16),
        VMEM((PLANES - 1, up_count) + up_tail, BF16),
        VMEM((PLANES - 1, rows, D), BF16),
    ]
    tile = (local, BLOCK, LANES)
    wide = VMEM((spans, 2 * BLOCK, SPAN * BLOCK), F32)
    thin = VMEM((spans, BLOCK, SPAN * BLOCK), F32)
    dma = pltpu.SemaphoreType.DMA
    return pl.pallas_call(
        plane_attend_back_kernel,
        out_shape=(
            jax.ShapeDtypeStruct((2, SPOTS, PIECES, 3) + tile, BF16),
            jax.ShapeDtypeStruct(hidden.shape, BF16),
            jax.ShapeDtypeStruct(out_tail, F32),
            jax.ShapeDtypeStruct((up_count,) + up_tail, F32),
            jax.ShapeDtypeStruct((rows, D), F32),
        ),
        in_specs=[
            whole(pltpu.SMEM),
            whole(pltpu.SMEM),
            whole(),
            whole(),
            whole(ANY),
            whole(ANY),
            whole(),
            whole(ANY),
        ]
        + [whole(ANY)] * 5,
        out_specs=(whole(ANY), whole(ANY)) + (whole(),) * 3,
        scratch_shapes=buffers
        + mines
        + parts
        + [
            VMEM((PLANES, SPOTS) + tile, BF16),
            VMEM((PLANES, SPOTS, local // 2, BLOCK, LANES), BF16),
            VMEM((PLANES, SPOTS, 3) + tile, BF16),
            VMEM((2, blocks, BLOCK, LANES), F32),
            VMEM((2, blocks * RANDOM, BLOCK, LANES), F32),
            VMEM((2, blocks * RANDOM, BLOCK, LANES), BF16),
            VMEM((PIECES, SPOTS) + tile, BF16),
            wide,
            wide,
            thin,
            thin,
            dma((count, SpotReduce.SEMS)),
            dma((count, SpotReduce.SEMS)),
            dma((4, PLANES - 1)),
            dma((4, PLANES - 1)),
            dma((count + 2,)),
        ]
        + exchange_sems((PLANES, SPOTS))
        + [
            dma((36,)),
            dma((2, SPOTS, PIECES, 3)),
            dma((3, PIECES)),
            dma((2,)),
            dma((2,)),
            dma((2,)),
            dma,
            dma,
        ],
        compiler_params=pltpu.CompilerParams(
            vmem_limit_bytes=62 * 1024 * 1024, collective_id=5, has_side_effects=True
        ),
        name="plane_attention_back",
    )(table, sorted_table, qk, shared, near, far, lse, hidden, *sources, half_up, half_down)


class PlaneGather:
    SENDS = 3 + 3 + 4 + 2

    def __init__(self, source, target, send_sem, column_sem, recv_sem, local_sem):
        self.source, self.target = source, target
        self.send_sem, self.column_sem, self.recv_sem = send_sem, column_sem, recv_sem
        self.core, self.plane, self.spot = place_here()
        self.sends = []
        self.own = pltpu.make_async_copy(
            source, target.at[self.core, self.plane, self.spot], local_sem
        )
        self.own.start()
        for bits in range(1, PLANES):
            copy = remote(
                source,
                target.at[self.core, self.plane, self.spot],
                send_sem.at[len(self.sends)],
                column_sem.at[self.plane],
                (self.core, rank_of(flip(self.plane, bits), self.spot)),
            )
            copy.start()
            self.sends.append(copy)

    def neighbour(self, bits):
        return (self.core, rank_of(self.plane, flip(self.spot, bits)))

    def sibling(self):
        return (1 - self.core, rank_of(self.plane, self.spot))

    def piece(self, core, planes, spot):
        return self.target.at[core, planes, spot]

    def send(self, planes, spot, part, goal):
        piece = self.piece(self.core, planes, spot)
        copy = remote(
            piece,
            piece,
            self.send_sem.at[len(self.sends)],
            self.recv_sem.at[self.core, spot, part],
            goal,
        )
        copy.start()
        self.sends.append(copy)

    def arrive(self, core, planes, spot, part):
        piece = self.piece(core, planes, spot)
        remote(
            piece,
            piece,
            self.send_sem.at[0],
            self.recv_sem.at[core, spot, part],
            (self.core, rank_of(self.plane, self.spot)),
        ).wait_recv()

    def columns(self):
        self.own.wait()
        for bits in range(1, PLANES):
            other = flip(self.plane, bits)
            shard = self.target.at[self.core, other, self.spot]
            remote(
                shard,
                shard,
                self.send_sem.at[0],
                self.column_sem.at[other],
                (self.core, rank_of(self.plane, self.spot)),
            ).wait_recv()
        for goal in (self.neighbour(1), self.neighbour(2), self.sibling()):
            self.send(slice(0, PLANES), self.spot, 0, goal)

    def forward(self):
        everything = slice(0, PLANES)
        for side in (1, 2):
            spot = flip(self.spot, side)
            self.arrive(self.core, everything, spot, 0)
            half = slice(0, 2) if side == 1 else slice(2, 4)
            self.send(half, spot, side - 1, self.neighbour(3 - side))
            self.send(everything, spot, 0, self.sibling())

    def corner(self):
        spot = flip(self.spot, 3)
        for part, half in enumerate((slice(0, 2), slice(2, 4))):
            self.arrive(self.core, half, spot, part)
            self.send(half, spot, part, self.sibling())

    def finish(self):
        for side in range(3):
            self.arrive(1 - self.core, slice(0, PLANES), flip(self.spot, side), 0)
        for part, half in enumerate((slice(0, 2), slice(2, 4))):
            self.arrive(1 - self.core, half, flip(self.spot, 3), part)
        for copy in self.sends:
            copy.wait_send()


class CrossGather:
    SENDS = 2 + 1 + 3 + 3 * 4

    def __init__(self, source, target, send_sem, spot_sem, recv_sem, local_sem):
        self.target = target
        self.send_sem, self.spot_sem, self.recv_sem = send_sem, spot_sem, recv_sem
        self.core, self.plane, self.spot = place_here()
        self.sends = []
        self.own = pltpu.make_async_copy(
            source, target.at[self.core, self.plane, self.spot], local_sem
        )
        self.own.start()
        for side in (1, 2):
            self.pass_on(source, self.spot, flip(self.spot, side))

    def push(self, source, target, recv_sem, device):
        copy = remote(source, target, self.send_sem.at[len(self.sends)], recv_sem, device)
        copy.start()
        self.sends.append(copy)

    def pass_on(self, source, spot, goal):
        self.push(
            source,
            self.target.at[self.core, self.plane, spot],
            self.spot_sem.at[spot],
            (self.core, rank_of(self.plane, goal)),
        )

    def await_spot(self, spot):
        shard = self.target.at[self.core, self.plane, spot]
        remote(
            shard,
            shard,
            self.send_sem.at[0],
            self.spot_sem.at[spot],
            (self.core, rank_of(self.plane, self.spot)),
        ).wait_recv()

    def across(self):
        beside, beyond = flip(self.spot, 1), flip(self.spot, 2)
        for side in (1, 2):
            self.await_spot(flip(self.spot, side))
        spot = beside * (1 - self.core) + beyond * self.core
        goal = beyond * (1 - self.core) + beside * self.core
        self.pass_on(self.target.at[self.core, self.plane, spot], spot, goal)

    def blocks(self):
        self.own.wait()
        self.await_spot(flip(self.spot, 3))
        self.maybe = []
        self.along(self.plane, 1, self.plane < PLANES - 1)
        self.along(self.plane, -1, self.plane > 0)
        self.to_sibling(self.plane, self.plane >= 0)

    def along(self, plane, step, wanted):
        block = self.target.at[self.core, plane]
        copy = remote(
            block,
            block,
            self.send_sem.at[3 + len(self.maybe)],
            self.recv_sem.at[self.core, plane],
            (self.core, rank_of(self.plane + step, self.spot)),
        )
        self.begin(copy, wanted)

    def to_sibling(self, plane, wanted):
        block = self.target.at[self.core, plane]
        copy = remote(
            block,
            block,
            self.send_sem.at[3 + len(self.maybe)],
            self.recv_sem.at[self.core, plane],
            (1 - self.core, rank_of(self.plane, self.spot)),
        )
        self.begin(copy, wanted)

    def begin(self, copy, wanted):
        self.maybe.append((copy, wanted))

        @pl.when(wanted)
        def _():
            copy.start()

    def arrive(self, core, plane):
        block = self.target.at[core, plane]
        remote(
            block,
            block,
            self.send_sem.at[0],
            self.recv_sem.at[core, plane],
            (self.core, rank_of(self.plane, self.spot)),
        ).wait_recv()

    def hop(self, distance):
        for step in (1, -1):
            origin = self.plane - step * distance
            here = (origin >= 0) & (origin < PLANES)
            onward = self.plane + step
            more = here & (onward >= 0) & (onward < PLANES)

            @pl.when(here)
            def _(origin=origin):
                self.arrive(self.core, origin)

            self.along(origin, step, more)
            self.to_sibling(origin, here)

    def finish(self):
        for bits in range(PLANES):
            self.arrive(1 - self.core, flip(self.plane, bits))
        for copy in self.sends:
            copy.wait_send()
        for copy, wanted in self.maybe:

            @pl.when(wanted)
            def _(copy=copy):
                copy.wait_send()


def pair_of_blocks(read, first, second):
    low = low_lanes(1)
    tiles = []
    for block, wanted in ((first, 0), (second, 1)):
        tile = read(block // 2)
        tiles.append(tile if block % 2 == wanted else swap_halves(tile))
    return jnp.where(low, tiles[0], tiles[1])


def fold_tiles(target_ref, start, tiles, read):
    half = len(tiles) // 2
    for number in range(half):
        columns = slice((start + number) * LANES, (start + number + 1) * LANES)
        target_ref[:, columns] = jnp.concatenate(
            [read(tiles[number]), read(tiles[half + number])], axis=0
        ).astype(BF16)


VECTORS = 8


def lay_vectors(vecs_ref, vectors_ref, up_ref):
    rows = vecs_ref.shape[3]
    own, wide = D // RANKS, FF // RANKS
    values = vecs_ref[...].reshape(RANKS, rows, LANES).astype(F32)

    def spread_out(count, width):
        place = lax.broadcasted_iota(jnp.int32, (LANES, count), 1)
        lane = lax.broadcasted_iota(jnp.int32, (LANES, count), 0)
        start = lax.div(place, width) * width
        return jnp.where(place - start == lane, 1.0, 0.0).astype(BF16)

    laid = dot(vecs_ref[...].reshape(RANKS * rows, LANES), spread_out(D, own))
    owner = lax.broadcasted_iota(jnp.int32, (RANKS, 1, D), 0)
    column = lax.broadcasted_iota(jnp.int32, (RANKS, 1, D), 2)
    laid = jnp.where(lax.div(column, own) == owner, laid.reshape(RANKS, rows, D), 0.0)
    vectors_ref[...] = jnp.sum(laid, axis=0)[:VECTORS]
    row = lax.broadcasted_iota(jnp.int32, (1, rows, LANES), 1)
    last = jnp.sum(jnp.where(row == VECTORS, values, 0.0), axis=1)
    laid = dot(last.astype(BF16), spread_out(FF, wide))
    owner = lax.broadcasted_iota(jnp.int32, (RANKS, FF), 0)
    column = lax.broadcasted_iota(jnp.int32, (RANKS, FF), 1)
    laid = jnp.sum(jnp.where(lax.div(column, wide) == owner, laid, 0.0), axis=0, keepdims=True)
    for chunk in range(FF // CHUNK):
        for side in range(2):
            start = side * (FF // 2) + chunk * LANES
            up_ref[chunk, :, side * LANES : (side + 1) * LANES] = laid[:, start : start + LANES]


def lay_table(tables_ref, core, micro, entries):
    count = 2 * LANES
    ranks = PLANES * SPOTS
    values = tables_ref[core].reshape(ranks, tables_ref.shape[3], LANES).astype(F32)
    row = lax.broadcasted_iota(jnp.int32, (1, tables_ref.shape[3], LANES), 1)
    values = jnp.sum(jnp.where(row == micro, values, 0.0), axis=1)
    place = lax.broadcasted_iota(jnp.int32, (LANES, count), 1)
    lane = lax.broadcasted_iota(jnp.int32, (LANES, count), 0)
    start = lax.div(place, entries) * entries
    laid = dot(values.astype(BF16), jnp.where(place - start == lane, 1.0, 0.0).astype(BF16))
    owner = lax.broadcasted_iota(jnp.int32, (ranks, count), 0)
    column = lax.broadcasted_iota(jnp.int32, (ranks, count), 1)
    laid = jnp.sum(jnp.where(lax.div(column, entries) == owner, laid, 0.0), axis=0, keepdims=True)
    column = lax.broadcasted_iota(jnp.int32, (1, count), 1)
    return jnp.where(column < ranks * entries, laid, 2.0 * LANES)


def front_kernel(
    x_in_ref,
    dy_ref,
    vec_ref,
    tab_ref,
    w_qkv_in_ref,
    w_out_in_ref,
    w_up_in_ref,
    w_down_in_ref,
    back_ref,
    far_back_ref,
    x_ref,
    dys_ref,
    w_down_ref,
    w_qkv_hbm,
    w_out_hbm,
    w_up_hbm,
    qk_hbm,
    shared_hbm,
    normed_ref,
    lse_ref,
    vectors_ref,
    up_ref,
    table_ref,
    sorted_ref,
    s_qkv_ref,
    s_ou_ref,
    g_qkv_ref,
    g_ou_ref,
    w_qkv_ref,
    w_out_ref,
    w_up_ref,
    xs_ref,
    vecs_ref,
    tabs_ref,
    bias_ref,
    send_ref,
    qk_ref,
    shared_ref,
    out_ref,
    pack_ref,
    p_ref,
    q_ref,
    picks_ref,
    *sems,
):
    gather_send, gather_recv, gather_local = sems[:3]
    plane_sems, cross_sems = sems[3:7], sems[7:11]
    x_sems, dy_sems = sems[11:14], sems[14:17]
    qkv_send, qkv_recv, qkv_local, shared_send, shared_recv = sems[17:22]
    back_send, back_recv, back_local, far_send, far_recv, local_sem = sems[22:28]
    core, plane, spot = place_here()
    micro, rows, _ = x_in_ref.shape
    tokens = PIECES * rows
    local = rows // BLOCK
    blocks = PLANES * SPOTS * local

    barrier = pltpu.get_barrier_semaphore()
    partners = both_partners(core, plane, spot)
    for partner in partners:
        pl.semaphore_signal(barrier, inc=1, device_id=partner, device_id_type=MESH)

    def natural(ref):
        return lambda tile: ref[:, tile * LANES : (tile + 1) * LANES].astype(F32)

    order = [natural_block(entry) for entry in column_order()]
    read = natural(w_qkv_in_ref)
    fold_tiles(
        s_qkv_ref,
        0,
        list(range(TILES)),
        lambda tile: pair_of_blocks(read, order[2 * tile], order[2 * tile + 1]),
    )
    pl.semaphore_wait(barrier, len(partners))

    gathers = []
    for number, (source, target) in enumerate(
        ((tab_ref, tabs_ref), (vec_ref, vecs_ref), (s_qkv_ref, g_qkv_ref))
    ):
        one = Gather(
            source, target, gather_send.at[number], gather_recv.at[number], gather_local.at[number]
        )
        one.start()
        gathers.append(one)
    outs = D // LANES // 2
    fold_tiles(s_ou_ref, 0, list(range(D // LANES)), natural(w_out_in_ref))
    fold_tiles(s_ou_ref, outs, list(range(FF // LANES)), natural(w_up_in_ref))
    for one in gathers:
        one.column()
    finish_x = to_planes(x_in_ref, xs_ref, *x_sems)
    cross = CrossGather(w_down_in_ref, w_down_ref, *cross_sems)
    for one in gathers:
        one.across()
    for one in gathers:
        one.corner()
    cross.across()
    for one in gathers[:2]:
        one.finish()
    window_core, window_micro = lax.rem(plane, 2), lax.div(plane, 2)
    scalars = pltpu.make_async_copy(tabs_ref.at[window_core], picks_ref, local_sem.at[1])
    scalars.start()
    lay_vectors(vecs_ref, vectors_ref, up_ref)
    for tile in range(TILES):
        halves = []
        for entry in column_order()[2 * tile : 2 * tile + 2]:
            halves.append(entry)

        def bias_tile(number, halves=halves):
            if number < D // LANES:
                return vectors_ref[2:3, number * LANES : (number + 1) * LANES]
            if number < 2 * D // LANES:
                return jnp.zeros((1, LANES), F32)
            start = (number - 2 * D // LANES) * LANES
            return vectors_ref[3:4, start : start + LANES]

        chunk, side = tile % HALF_TILES, tile // HALF_TILES
        start = chunk * CHUNK + side * LANES
        bias_ref[:, start : start + LANES] = pair_of_blocks(
            bias_tile, order[2 * tile], order[2 * tile + 1]
        )
    gathers[2].finish()
    settle(g_qkv_ref, [(tile, w_qkv_ref, alternate(tile)) for tile in range(HALF_TILES)])
    keep_w = pltpu.make_async_copy(w_qkv_ref, w_qkv_hbm, local_sem.at[2])
    keep_w.start()

    finish_x()
    spread = PlaneGather(s_ou_ref, g_ou_ref, *plane_sems)
    keep_x = pltpu.make_async_copy(xs_ref, x_ref, local_sem.at[0])
    keep_x.start()
    normal, _ = norm_parts(xs_ref[...].reshape(tokens, D).astype(F32))
    normed_ref[...] = (normal * vectors_ref[0:1] + vectors_ref[1:2]).astype(BF16)

    def shaped(value):
        return value.astype(BF16).reshape(local, BLOCK, LANES)

    low = low_lanes(rows)
    queries = D // LANES
    for chunk in range(HALF_TILES):
        columns = slice(chunk * CHUNK, (chunk + 1) * CHUNK)
        packed = dot(normed_ref[...], w_qkv_ref[:, columns]) + bias_ref[:, columns]
        for side in range(2):
            tile = chunk + side * HALF_TILES
            whole_tile = packed[:, side * LANES : (side + 1) * LANES]
            if tile < queries:
                whole_tile = whole_tile.astype(BF16).astype(F32) * SCALE
            for piece in range(PIECES):
                part = whole_tile[piece * rows : (piece + 1) * rows]
                if tile < SPOTS:
                    send_ref[0, tile, piece, 0] = shaped(part)
                elif tile < queries:
                    first = 2 * (tile - SPOTS)
                    shared = send_ref[0, first, piece, 0].reshape(rows, LANES).astype(F32)
                    send_ref[1, first, piece, 0] = shaped(jnp.where(low, part, shared))
                    shared = send_ref[0, first + 1, piece, 0].reshape(rows, LANES).astype(F32)
                    send_ref[1, first + 1, piece, 0] = shaped(
                        jnp.where(low, swap_halves(part), shared)
                    )
                else:
                    goal, role = (tile - queries) // 3, (tile - queries) % 3
                    if role < 2:
                        send_ref[role, goal, piece, 1] = shaped(part)
                    else:
                        send_ref[0, goal, piece, 2] = shaped(part)
    sends, keeps = [], []
    for part, (parts, landing) in enumerate(((slice(0, 2), qk_ref), (2, shared_ref))):
        for side in (3, 1, 2, 0):
            for other in (core, 1 - core) if part == 0 else (core,):
                goal = flip(spot, side)
                for piece in range(PIECES):
                    source = send_ref.at[other if part == 0 else 0, goal, piece, parts]
                    target = landing.at[2 * core + piece, spot]
                    if side == 0 and other is core:
                        copy = pltpu.make_async_copy(source, target, qkv_local.at[part, piece])
                        keeps.append((part, copy))
                    else:
                        copy = remote(
                            source,
                            target,
                            qkv_send.at[len(sends)],
                            qkv_recv.at[2 * core + piece, spot, part],
                            (other, rank_of(plane, goal)),
                        )
                        sends.append(copy)
                    copy.start()
    spread.columns()
    cross.blocks()
    table = lay_table(tabs_ref, window_core, window_micro, local * RANDOM)
    table_ref[...] = table.astype(jnp.int32)
    sort_entries(table, sorted_ref, blocks * RANDOM)
    scalars.wait()

    def arrive(part, other, piece, goal):
        target = (qk_ref, shared_ref)[part].at[2 * other + piece, goal]
        remote(
            target,
            target,
            qkv_send.at[0],
            qkv_recv.at[2 * other + piece, goal, part],
            (core, rank_of(plane, spot)),
        ).wait_recv()

    for side in range(SPOTS):
        for other in (core, 1 - core):
            if side > 0 or other is not core:
                for piece in range(PIECES):
                    arrive(0, other, piece, flip(spot, side))
    for part, copy in keeps:
        copy.wait()
    cross.hop(1)

    low = low_lanes(BLOCK)
    masks = [half_mask(True), half_mask(False)]

    def tile_of(component, block):
        rank, number = lax.div(block, local), lax.rem(block, local)
        if component == 2:
            return shared_ref[lax.div(rank, SPOTS), lax.rem(rank, SPOTS), number]
        return qk_ref[lax.div(rank, SPOTS), lax.rem(rank, SPOTS), component, number]

    def picked(block, number):
        rank = lax.div(block, local)
        return picks_ref[
            lax.div(rank, SPOTS),
            lax.rem(rank, SPOTS),
            window_micro,
            lax.rem(block, local) * RANDOM + number,
        ]

    def place_of(block):
        rank = lax.div(block, local)
        return lax.div(rank, SPOTS), lax.rem(rank, SPOTS), lax.rem(block, local)

    def put(block, slot, mixed, log):
        place = place_of(block)
        if slot == 0:
            out_ref[place] = mixed.astype(BF16)
            lse_ref[block] = jnp.where(low, log, 0.0)
        else:
            out_ref[place] = jnp.where(low, mixed, out_ref[place].astype(F32)).astype(BF16)
            lse_ref[block] = jnp.where(low, lse_ref[block], log)

    def one_block(block, slot):
        ids, bias = inner_slots(picked, block, blocks)
        keys = jnp.concatenate([tile_of(1 + slot, number) for number in ids], axis=0)
        scores = dot_rt(tile_of(0, block) * masks[slot], keys) + bias
        top = jnp.max(scores, axis=1, keepdims=True)
        powered = jnp.exp(scores - top)
        total = jnp.sum(powered, axis=1, keepdims=True)
        mixed = dot(powered.astype(BF16), keys) * (1.0 / total)
        return mixed, top + jnp.log(total)

    def rank_blocks(rank, slot):
        results = [one_block(rank * local + number, slot) for number in range(local)]
        for number, (mixed, log) in enumerate(results):
            put(rank * local + number, slot, mixed, log)

    spans = blocks // SPAN
    ends = (0, blocks - 1)

    def dense(slot, scores_ref, numbers):
        size = len(numbers) * BLOCK
        query = jnp.concatenate([tile_of(0, number) * masks[slot] for number in numbers], axis=0)

        def keys_at(span):
            return jnp.concatenate(
                [tile_of(1 + slot, span * SPAN + number) for number in range(SPAN)], axis=0
            )

        def first_pass(span, top):
            scores = dot_rt(query, keys_at(span))
            scores_ref[span] = scores
            return jnp.maximum(top, jnp.max(scores, axis=1, keepdims=True))

        top = lax.fori_loop(
            0, spans, first_pass, jnp.full((size, 1), NEGATIVE, F32), unroll=2
        )

        def second_pass(span, carry):
            total, mixed = carry
            powered = jnp.exp(scores_ref[span] - top)
            return (
                total + jnp.sum(powered, axis=1, keepdims=True),
                mixed + dot(powered.astype(BF16), keys_at(span)),
            )

        total, mixed = lax.fori_loop(
            0,
            spans,
            second_pass,
            (jnp.zeros((size, 1), F32), jnp.zeros((size, LANES), F32)),
            unroll=2,
        )
        mixed = mixed * (1.0 / total)
        log = top + jnp.log(total)
        for place, number in enumerate(numbers):
            span = slice(place * BLOCK, (place + 1) * BLOCK)
            put(number, slot, mixed[span], log[span])

    def head_a(number, carry):
        rank_blocks(number, 0)
        return carry

    def head_b(number, carry):
        rank_blocks(core * (PLANES * SPOTS // 2) + number, 1)
        return carry

    shared = []
    half_way = PLANES * SPOTS // 2
    lax.fori_loop(0, half_way, head_a, 0)
    for side in range(SPOTS):
        goal = flip(spot, side)
        for piece in range(PIECES):
            if side > 0:
                arrive(1, core, piece, goal)
            source = shared_ref.at[2 * core + piece, goal]
            copy = remote(
                source,
                source,
                shared_send.at[2 * side + piece],
                shared_recv.at[2 * core + piece, goal],
                (1 - core, rank_of(plane, spot)),
            )
            copy.start()
            shared.append(copy)
    finish_dy = to_planes(dy_ref, dys_ref, *dy_sems)
    lax.fori_loop(half_way, PLANES * SPOTS, head_a, 0)
    dense(0, p_ref, ends)
    spread.forward()
    backs, stay = [], []
    for side in (3, 1, 2, 0):
        goal = flip(spot, side)
        for piece in range(PIECES):
            pack_halves(
                lambda number, piece=piece, goal=goal: out_ref[
                    2 * (1 - core) + piece, goal, number
                ],
                pack_ref,
                (piece, goal),
                local,
                low,
                1,
            )
            copy = remote(
                pack_ref.at[piece, goal],
                far_back_ref.at[spot, piece],
                far_send.at[piece, side],
                far_recv.at[spot, piece],
                (1 - core, rank_of(plane, goal)),
            )
            copy.start()
            backs.append(copy)
    for side in range(SPOTS):
        for piece in range(PIECES):
            target = shared_ref.at[2 * (1 - core) + piece, flip(spot, side)]
            remote(
                target,
                target,
                shared_send.at[0],
                shared_recv.at[2 * (1 - core) + piece, flip(spot, side)],
                (core, rank_of(plane, spot)),
            ).wait_recv()
    cross.hop(2)
    keep_qk = pltpu.make_async_copy(qk_ref, qk_hbm, local_sem.at[3])
    keep_qk.start()
    keep_shared = pltpu.make_async_copy(shared_ref, shared_hbm, local_sem.at[6])
    keep_shared.start()
    lax.fori_loop(0, half_way, head_b, 0)
    dense(1, q_ref, (core * (blocks - 1),))
    spread.corner()
    for side in (3, 1, 2, 0):
        goal = flip(spot, side)
        for piece in range(PIECES):
            source, target = out_ref.at[2 * core + piece, goal], back_ref.at[spot, piece]
            if side == 0:
                copy = pltpu.make_async_copy(source, target, back_local.at[piece])
                stay.append(copy)
            else:
                copy = remote(
                    source,
                    target,
                    back_send.at[piece, side],
                    back_recv.at[spot, piece],
                    (core, rank_of(plane, goal)),
                )
                backs.append(copy)
            copy.start()
    cross.hop(3)
    spread.finish()
    settle(
        g_ou_ref,
        [(tile, w_out_ref, (tile, outs + tile)) for tile in range(outs)]
        + [(outs + tile, w_up_ref, alternate(tile)) for tile in range(FF // CHUNK)],
    )
    keep_out = pltpu.make_async_copy(w_out_ref, w_out_hbm, local_sem.at[4])
    keep_out.start()
    keep_up = pltpu.make_async_copy(w_up_ref, w_up_hbm, local_sem.at[5])
    keep_up.start()
    cross.finish()
    finish_dy()
    for copy in sends:
        copy.wait_send()
    for copy in shared:
        copy.wait_send()
    for side in range(SPOTS):
        goal = flip(spot, side)
        for piece in range(PIECES):
            here = (core, rank_of(plane, spot))
            if side > 0:
                target = back_ref.at[goal, piece]
                remote(target, target, back_send.at[0, 0], back_recv.at[goal, piece], here).wait_recv()
            target = far_back_ref.at[goal, piece]
            remote(target, target, far_send.at[0, 0], far_recv.at[goal, piece], here).wait_recv()
    for copy in backs:
        copy.wait_send()
    for copy in stay:
        copy.wait()
    for copy in (keep_x, keep_w, keep_qk, keep_shared, keep_out, keep_up):
        copy.wait()


def front(x, dy, vec, tab, w_qkv, w_out, w_up, w_down):
    micro, rows, _ = x.shape
    tokens = PIECES * rows
    local = rows // BLOCK
    blocks = PLANES * SPOTS * local
    spans = blocks // SPAN
    grid = (2, PLANES, SPOTS)
    shard = D // RANKS
    tile = (local, BLOCK, LANES)
    dma = pltpu.SemaphoreType.DMA
    struct = jax.ShapeDtypeStruct
    ou = (2 * shard, (D + FF) // 2)
    return pl.pallas_call(
        front_kernel,
        out_shape=(
            struct((SPOTS, PIECES) + tile, BF16),
            struct((SPOTS, PIECES, local // 2, BLOCK, LANES), BF16),
            struct(x.shape, BF16),
            struct(dy.shape, BF16),
            struct(grid + w_down.shape, BF16),
            struct((D, 3 * D), BF16),
            struct((D, D), BF16),
            struct((D, FF), BF16),
            struct((PLANES, SPOTS, 2) + tile, BF16),
            struct((PLANES, SPOTS) + tile, BF16),
            struct((tokens, D), BF16),
            struct((blocks, BLOCK, LANES), F32),
            struct((VECTORS, D), F32),
            struct((FF // CHUNK, 1, CHUNK), F32),
            struct((1, 2 * LANES), jnp.int32),
            struct((4, 2 * LANES), jnp.int32),
        ),
        in_specs=[
            whole(ANY),
            whole(ANY),
            whole(ANY),
            whole(ANY),
            whole(),
            whole(),
            whole(),
            whole(ANY),
        ],
        out_specs=(whole(ANY),) * 10 + (whole(),) * 6,
        scratch_shapes=[
            VMEM((2 * shard, 3 * D // 2), BF16),
            VMEM(ou, BF16),
            VMEM(grid + (2 * shard, 3 * D // 2), BF16),
            VMEM(grid + ou, BF16),
            VMEM((D, 3 * D), BF16),
            VMEM((D, D), BF16),
            VMEM((D, FF), BF16),
            VMEM((PIECES, rows, D), BF16),
            VMEM(grid + vec.shape, BF16),
            VMEM(grid + tab.shape, jnp.int32),
            VMEM((1, 3 * D), F32),
            VMEM((2, SPOTS, PIECES, 3) + tile, BF16),
            VMEM((PLANES, SPOTS, 2) + tile, BF16),
            VMEM((PLANES, SPOTS) + tile, BF16),
            VMEM((PLANES, SPOTS) + tile, BF16),
            VMEM((PIECES, SPOTS, local // 2, BLOCK, LANES), BF16),
            VMEM((spans, 2 * BLOCK, SPAN * BLOCK), F32),
            VMEM((spans, BLOCK, SPAN * BLOCK), F32),
            pltpu.SMEM((PLANES, SPOTS) + tab.shape, jnp.int32),
            dma((3, Gather.SENDS)),
            dma((3,) + grid),
            dma((3,)),
            dma((PlaneGather.SENDS,)),
            dma((PLANES,)),
            dma((2, SPOTS, 2)),
            dma,
            dma((CrossGather.SENDS,)),
            dma((SPOTS,)),
            dma((2, PLANES)),
            dma,
        ]
        + [dma((2,))] * 6
        + [
            dma((20,)),
            dma((PLANES, SPOTS, 2)),
            dma((2, PIECES)),
            dma((2 * SPOTS,)),
            dma((PLANES, SPOTS)),
            dma((PIECES, SPOTS)),
            dma((SPOTS, PIECES)),
            dma((PIECES,)),
            dma((PIECES, SPOTS)),
            dma((SPOTS, PIECES)),
            dma((7,)),
        ],
        compiler_params=pltpu.CompilerParams(
            vmem_limit_bytes=60 * 1024 * 1024, collective_id=1, has_side_effects=True
        ),
        name="front",
    )(x, dy, vec, tab, w_qkv, w_out, w_up, w_down)


class SpotReduce:
    SEMS = 4

    def __init__(self, source, near, corner, sides, send_sem, recv_sem, rows=None, mine=None):
        self.source, self.near, self.corner, self.side = source, near, corner, sides
        self.send_sem, self.recv_sem, self.rows, self.mine = send_sem, recv_sem, rows, mine
        self.core, self.plane, self.spot = place_here()
        beside, beyond = flip(self.spot, 1), flip(self.spot, 2)
        self.via = beyond * (1 - self.core) + beside * self.core
        self.other = beside * (1 - self.core) + beyond * self.core

    def half(self, core):
        return self.source.at[core] if self.rows else self.source.at[:, core]

    def part(self, spot):
        if self.rows:
            start = pl.multiple_of(spot * self.rows, 16)
            return self.near.at[pl.ds(start, self.rows)]
        return self.near.at[:, :, spot]

    def copy(self, number):
        sibling = (1 - self.core, rank_of(self.plane, self.spot))
        if number == 0:
            source, target, device = self.half(1 - self.core), self.near, sibling
        elif number == 1:
            source, target = self.part(flip(self.spot, 3)), self.corner
            device = (self.core, rank_of(self.plane, self.via))
        else:
            spot = flip(self.spot, number - 1)
            source, target = self.part(spot), self.side.at[number - 2]
            device = (self.core, rank_of(self.plane, spot))
        return remote(source, target, self.send_sem.at[number], self.recv_sem.at[number], device)

    def start(self):
        self.copy(0).start()

    def add(self, spot, terms, target=None):
        if self.rows:
            rows = self.rows

            def slab(number, carry):
                size = rows // 3
                first = pl.multiple_of(spot * rows + number * size, 16)
                place = pl.ds(first, size)
                inner = pl.ds(pl.multiple_of(number * size, 16), size)
                total = self.near[place].astype(F32)
                for read in terms:
                    total = total + read(place, inner).astype(F32)
                if target is None:
                    self.near[place] = total.astype(BF16)
                else:
                    target[inner] = total.astype(BF16)
                return carry

            lax.fori_loop(0, 3, slab, 0, unroll=True)
            return
        count = self.near.shape[0]

        def block(number, carry):
            first, plane = lax.div(number, PLANES), lax.rem(number, PLANES)
            total = self.near[first, plane, spot].astype(F32)
            for read in terms:
                total = total + read(first, plane).astype(F32)
            if target is None:
                self.near[first, plane, spot] = total.astype(BF16)
            else:
                target[first, plane] = total.astype(BF16)
            return carry

        lax.fori_loop(0, count * PLANES, block, 0, unroll=4)

    def corners(self):
        self.copy(0).wait_recv()
        core = self.core
        for spot in range(SPOTS):
            if self.rows and self.mine is None:
                self.add(spot, [lambda place, inner: self.source[core, place]])
            elif self.rows:
                self.add(spot, [lambda place, inner: self.mine[place]])
            elif self.mine is None:
                self.add(spot, [lambda first, plane, spot=spot: self.source[first, core, plane, spot]])
            else:
                self.add(spot, [lambda first, plane, spot=spot: self.mine[first, plane, spot]])
        self.copy(1).start()

    def sides(self):
        self.copy(1).wait_recv()
        if self.rows:
            self.add(self.other, [lambda place, inner: self.corner[inner]])
        else:
            self.add(self.other, [lambda first, plane: self.corner[first, plane]])
        self.copy(2).start()
        self.copy(3).start()

    def close(self, target):
        self.copy(2).wait_recv()
        self.copy(3).wait_recv()
        if self.rows:
            terms = [lambda place, inner, n=n: self.side[n, inner] for n in range(2)]
        else:
            terms = [lambda first, plane, n=n: self.side[n, first, plane] for n in range(2)]
        self.add(self.spot, terms, target)
        for number in range(self.SEMS):
            self.copy(number).wait_send()


def block_scratch(count, rows, width):
    return [
        VMEM((count, PLANES, SPOTS, rows, width), BF16),
        VMEM((count, PLANES, rows, width), BF16),
        VMEM((2, count, PLANES, rows, width), BF16),
    ]


def row_scratch(rows, width):
    return [
        VMEM((SPOTS * rows, width), BF16),
        VMEM((rows, width), BF16),
        VMEM((2, rows, width), BF16),
    ]


STAGES = 4
PER_STAGE = FF // CHUNK // STAGES
EARLY = 2
LATE = STAGES - EARLY
WAITS = (2, 4, 6)


def by_owner(out_ref, values):
    rows = D // RANKS
    width = values.shape[1] // 2
    for owner in range(RANKS):
        part = values[owner * rows : (owner + 1) * rows]
        out_ref[owner] = jnp.concatenate([part[:, :width], part[:, width:]], axis=0).astype(BF16)


def plane_middle_kernel(
    mixed_in_ref,
    far_in_ref,
    x_ref,
    dy_ref,
    vec_ref,
    w_out_ref,
    up_shift_ref,
    w_up_ref,
    w_down_ref,
    hidden_ref,
    send_ref,
    far_ref,
    dres_ref,
    g_out_ref,
    half_up_ref,
    half_down_ref,
    last_up_ref,
    last_down_ref,
    g_up_bias_ref,
    g_small_ref,
    mixed_ref,
    residual_ref,
    second_ref,
    second_t_ref,
    total_ref,
    dsecond_ref,
    g_up_ref,
    g_down_ref,
    *scratch,
):
    send_sem, recv_sem, local_sem = scratch[-3:]
    stages = []
    for number in range(EARLY):
        buffers = scratch[6 * number : 6 * number + 6]
        stages.append(
            (
                SpotReduce(
                    g_up_ref.at[PER_STAGE * number : PER_STAGE * (number + 1)],
                    *buffers[:3],
                    send_sem.at[number, 0],
                    recv_sem.at[number, 0],
                ),
                SpotReduce(
                    g_down_ref.at[number],
                    *buffers[3:],
                    send_sem.at[number, 1],
                    recv_sem.at[number, 1],
                    rows=FF // RANKS,
                ),
            )
        )
    pieces, rows, _ = x_ref.shape
    tokens = pieces * rows
    step = pl.program_id(0)
    low = low_lanes(rows)
    out_shift, gain, shift, down_shift = (vec_ref[number : number + 1] for number in (4, 5, 6, 7))

    @pl.when(step == 0)
    def _():
        core, plane, spot = place_here()
        greet(
            [
                (1 - core, rank_of(plane, spot)),
                (core, rank_of(plane, flip(spot, 1))),
                (core, rank_of(plane, flip(spot, 2))),
            ]
        )
        def received(spot, piece):
            own = mixed_in_ref[spot, piece].astype(F32)
            halves = far_in_ref[spot, piece].astype(F32)
            parts = []
            for number in range(rows // BLOCK // 2):
                part = halves[number * BLOCK : (number + 1) * BLOCK]
                parts += [part, swap_halves(part)]
            other = jnp.concatenate(parts, axis=0)
            return (jnp.where(core == 0, own, other), jnp.where(core == 0, other, own)), own

        for piece in range(pieces):
            span = slice(piece * rows, (piece + 1) * rows)
            for spot in (0, 2):
                first, own_first = received(spot, piece)
                last_two, own_last = received(spot + 1, piece)
                tiles = (
                    jnp.where(low, swap_halves(first[0]), first[1]),
                    jnp.where(low, own_first, last_two[0]),
                    swap_halves(jnp.where(low, own_last, last_two[1])),
                )
                for number, tile in enumerate(tiles):
                    spread = 3 * (spot // 2) + number
                    mixed_ref[span, spread * LANES : (spread + 1) * LANES] = tile.astype(BF16)
        residual = x_ref[...].reshape(tokens, D).astype(F32) + (
            dot(mixed_ref[...], w_out_ref[...]) + out_shift
        )
        residual_ref[...] = residual
        normal, _ = norm_parts(residual)
        second = normal * gain + shift
        second_ref[...] = second.astype(BF16)
        second_t_ref[...] = second.T.astype(BF16)
        total_ref[...] = jnp.zeros_like(total_ref)
        dsecond_ref[...] = jnp.zeros_like(dsecond_ref)

    w_down = w_down_ref[...].reshape(CHUNK, D)
    upper = dot(second_ref[...], w_up_ref[...]) + up_shift_ref[0]
    factor = 0.7978845608028654
    square = upper * upper
    bent = jnp.tanh(factor * (upper + 0.044715 * (upper * square)))
    middle_half = 0.5 * (1.0 + bent)
    active = (upper * middle_half).astype(BF16)
    slope = middle_half + 0.5 * upper * (1.0 - bent * bent) * (
        factor + (3.0 * 0.044715 * factor) * square
    )
    dy = dy_ref[...]
    total_ref[...] += dot(active, w_down)
    stage, turn = lax.div(step, PER_STAGE), lax.rem(step, PER_STAGE)
    down_share = dot_lt(active, dy).astype(BF16)
    place = pl.ds(pl.multiple_of(turn * LANES, LANES), LANES)
    for side in range(2):
        g_down_ref[stage, side, place] = down_share[side * LANES : (side + 1) * LANES]
    dupper = (dot_rt(dy, w_down) * slope).astype(BF16)
    g_up_bias_ref[0] = jnp.sum(dupper.astype(F32), axis=0, keepdims=True)
    up_share = dot(second_t_ref[...], dupper)
    shard = D // RANKS
    for owner in range(RANKS):
        part = up_share[owner * shard : (owner + 1) * shard]
        g_up_ref[step, owner // (PLANES * SPOTS), owner // SPOTS % PLANES, owner % SPOTS] = (
            jnp.concatenate([part[:, :LANES], part[:, LANES:]], axis=0).astype(BF16)
        )
    dsecond_ref[...] += dot_rt(dupper, w_up_ref[...])

    last = FF // CHUNK - 1
    for number, pair in enumerate(stages):
        done = PER_STAGE * (number + 1) - 1

        @pl.when(step == done)
        def _(pair=pair):
            for one in pair:
                one.start()

        @pl.when(step == done + WAITS[0])
        def _(pair=pair):
            for one in pair:
                one.corners()

        @pl.when(step == done + WAITS[1])
        def _(pair=pair):
            for one in pair:
                one.sides()

        if done + WAITS[2] < last:

            @pl.when(step == done + WAITS[2])
            def _(pair=pair, number=number):
                pair[0].close(half_up_ref.at[PER_STAGE * number : PER_STAGE * (number + 1)])
                pair[1].close(half_down_ref.at[number])

    @pl.when(step == last)
    def _():
        keep_up = pltpu.make_async_copy(
            g_up_ref.at[PER_STAGE * EARLY : PER_STAGE * STAGES], last_up_ref, local_sem.at[0]
        )
        keep_up.start()
        keep_down = pltpu.make_async_copy(
            g_down_ref.at[EARLY:STAGES], last_down_ref, local_sem.at[1]
        )
        keep_down.start()
        residual = residual_ref[...]
        hidden_ref[...] = (
            (residual + (total_ref[...] + down_shift)).astype(BF16).reshape(x_ref.shape)
        )
        normal, inverse = norm_parts(residual)
        dsecond = dsecond_ref[...]
        grad_out = dy_ref[...].astype(F32)
        g_small_ref[0:1] = jnp.sum(dsecond * normal, axis=0, keepdims=True)
        g_small_ref[1:2] = jnp.sum(dsecond, axis=0, keepdims=True)
        g_small_ref[2:3] = jnp.sum(grad_out, axis=0, keepdims=True)
        dres = grad_out + norm_pull(dsecond, normal, inverse, gain)
        dres_ref[...] = dres
        branch = dres.astype(BF16)
        g_small_ref[3:4] = jnp.sum(branch.astype(F32), axis=0, keepdims=True)
        by_owner(g_out_ref, dot_lt(mixed_ref[...], branch))
        dmixed = dot_rt(branch, w_out_ref[...])
        core = lax.axis_index("gx")

        def hand_over(spot, piece, first, second):
            send_ref[spot, piece] = jnp.where(core == 0, first, second).astype(BF16)
            far = jnp.where(core == 0, second, first)
            for number in range(rows // BLOCK // 2):
                start = 2 * number * BLOCK
                far_ref[spot, piece, number * BLOCK : (number + 1) * BLOCK] = jnp.where(
                    low_lanes(BLOCK),
                    swap_halves(far[start + BLOCK : start + 2 * BLOCK]),
                    far[start : start + BLOCK],
                ).astype(BF16)

        for piece in range(pieces):
            span = slice(piece * rows, (piece + 1) * rows)
            for spot in (0, 2):
                tiles = [
                    dmixed[span, number * LANES : (number + 1) * LANES]
                    for number in range(3 * (spot // 2), 3 * (spot // 2) + 3)
                ]
                flipped = [swap_halves(tile) for tile in tiles]
                hand_over(
                    spot,
                    piece,
                    jnp.where(low, tiles[1], flipped[0]),
                    jnp.where(low, tiles[1], tiles[0]),
                )
                hand_over(
                    spot + 1, piece, jnp.where(low, flipped[2], tiles[1]), flipped[2]
                )
        for number, pair in enumerate(stages):
            if PER_STAGE * (number + 1) - 1 + WAITS[2] >= last:
                pair[0].close(half_up_ref.at[PER_STAGE * number : PER_STAGE * (number + 1)])
                pair[1].close(half_down_ref.at[number])
        keep_up.wait()
        keep_down.wait()


def plane_middle(mixed_in, far_in, x, dy, vec, w_out, up_shift, w_up, w_down):
    pieces, rows, _ = x.shape
    tokens = pieces * rows
    shard = D // RANKS

    def fixed(shape):
        return pl.BlockSpec(shape, lambda step: (0,) * len(shape))

    steps = FF // CHUNK
    grid = (2, PLANES, SPOTS)
    down_rows = FF // RANKS
    half_up = (PER_STAGE * EARLY, PLANES, 2 * shard, LANES)
    half_down = (EARLY, down_rows, D)
    buffers = []
    for _ in range(EARLY):
        buffers += block_scratch(PER_STAGE, 2 * shard, LANES) + row_scratch(down_rows, D)
    down = pl.BlockSpec((2, LANES, D), lambda step: (0, step, 0))
    return pl.pallas_call(
        plane_middle_kernel,
        grid=(steps,),
        out_shape=(
            jax.ShapeDtypeStruct(x.shape, BF16),
            jax.ShapeDtypeStruct(mixed_in.shape, BF16),
            jax.ShapeDtypeStruct(far_in.shape, BF16),
            jax.ShapeDtypeStruct((tokens, D), F32),
            jax.ShapeDtypeStruct((RANKS, 2 * shard, D // 2), BF16),
            jax.ShapeDtypeStruct(half_up, BF16),
            jax.ShapeDtypeStruct(half_down, BF16),
            jax.ShapeDtypeStruct((PER_STAGE * LATE,) + grid + (2 * shard, LANES), BF16),
            jax.ShapeDtypeStruct((LATE, 2, FF // 2 // STAGES, D), BF16),
            jax.ShapeDtypeStruct((steps, 1, CHUNK), F32),
            jax.ShapeDtypeStruct((4, D), F32),
        ),
        in_specs=[
            fixed(mixed_in.shape),
            fixed(far_in.shape),
            fixed(x.shape),
            fixed((tokens, D)),
            fixed(vec.shape),
            fixed((D, D)),
            pl.BlockSpec((1, 1, CHUNK), lambda step: (step, 0, 0)),
            pl.BlockSpec((D, CHUNK), lambda step: (0, step)),
            down,
        ],
        out_specs=(
            fixed(x.shape),
            fixed(mixed_in.shape),
            fixed(far_in.shape),
            fixed((tokens, D)),
            fixed((RANKS, 2 * shard, D // 2)),
            fixed(half_up),
            fixed(half_down),
            whole(ANY),
            whole(ANY),
            pl.BlockSpec((1, 1, CHUNK), lambda step: (step, 0, 0)),
            fixed((4, D)),
        ),
        scratch_shapes=[
            VMEM((tokens, D), BF16),
            VMEM((tokens, D), F32),
            VMEM((tokens, D), BF16),
            VMEM((D, tokens), BF16),
            VMEM((tokens, D), F32),
            VMEM((tokens, D), F32),
            VMEM((steps,) + grid + (2 * shard, LANES), BF16),
            VMEM((STAGES, 2, FF // 2 // STAGES, D), BF16),
        ]
        + buffers
        + [
            pltpu.SemaphoreType.DMA((EARLY, 2, SpotReduce.SEMS)),
            pltpu.SemaphoreType.DMA((EARLY, 2, SpotReduce.SEMS)),
            pltpu.SemaphoreType.DMA((2,)),
        ],
        compiler_params=pltpu.CompilerParams(
            vmem_limit_bytes=60 * 1024 * 1024, collective_id=3, has_side_effects=True
        ),
        name="plane_middle",
    )(mixed_in, far_in, x, dy, vec, w_out, up_shift, w_up, w_down)


class Reduce:
    SENDS = 4 + 2 + 2 + 3
    RECVS = SENDS

    def __init__(self, source, total, near, corner_x, corner_y, side_x, side_y, far, out, sems):
        self.source, self.total, self.near = source, total, near
        self.corner = {1: corner_x, 2: corner_y}
        self.side = {1: side_x, 2: side_y}
        self.far, self.out = far, out
        self.send_sem, self.recv_sem, self.local_sem = sems
        self.core, self.plane, self.spot = place_here()
        self.copies = []
        self.locals = []

    def start(self):
        sibling = (1 - self.core, rank_of(self.plane, self.spot))
        for number, side in enumerate((3, 1, 2, 0)):
            spot = flip(self.spot, side)
            copy = remote(
                self.source.at[1 - self.core, :, spot],
                self.near.at[:, spot],
                self.send_sem.at[number],
                self.recv_sem.at[number],
                sibling,
            )
            copy.start()
            self.copies.append(copy)
            keep = pltpu.make_async_copy(
                self.source.at[self.core, :, spot],
                self.total.at[:, spot],
                self.local_sem.at[number],
            )
            keep.start()
            self.locals.append(keep)

    def take(self, number, side):
        self.copies[number].wait_recv()
        self.locals[number].wait()
        spot = flip(self.spot, side)

        def add(plane, carry):
            self.total[plane, spot] = (
                self.total[plane, spot].astype(F32) + self.near[plane, spot].astype(F32)
            ).astype(self.total.dtype)
            return carry

        lax.fori_loop(0, PLANES, add, 0, unroll=True)

    def corners(self):
        self.take(0, 3)
        spot = flip(self.spot, 3)
        index = 4
        self.corner_copies = []
        for bits in range(PLANES):
            side = 2 if bits < 2 else 1
            self.corner_copies.append(None)
            plane = flip(self.plane, bits)
            copy = remote(
                self.total.at[plane, spot],
                self.corner[side].at[bits % 2],
                self.send_sem.at[index + bits],
                self.recv_sem.at[index + bits],
                (self.core, rank_of(self.plane, flip(self.spot, side))),
            )
            copy.start()
            self.corner_copies[bits] = copy

    def sides(self):
        self.take(1, 1)
        self.take(2, 2)
        self.side_copies = {}
        for side in (1, 2):
            spot = flip(self.spot, side)
            came = 3 - side
            for bits in (0, 1) if came == 2 else (2, 3):
                self.corner_copies[bits].wait_recv()
                plane = flip(self.plane, bits)
                self.total[plane, spot] = (
                    self.total[plane, spot].astype(F32)
                    + self.corner[came][bits % 2].astype(F32)
                ).astype(self.total.dtype)
            copy = remote(
                self.total.at[:, spot],
                self.side[side],
                self.send_sem.at[7 + side],
                self.recv_sem.at[7 + side],
                (self.core, rank_of(self.plane, spot)),
            )
            copy.start()
            self.side_copies[side] = copy

    def columns(self):
        self.take(3, 0)
        for side in (1, 2):
            self.side_copies[side].wait_recv()

        def add(plane, carry):
            self.total[plane, self.spot] = (
                self.total[plane, self.spot].astype(F32)
                + self.side[1][plane].astype(F32)
                + self.side[2][plane].astype(F32)
            ).astype(self.total.dtype)
            return carry

        lax.fori_loop(0, PLANES, add, 0, unroll=True)
        self.far_copies = []
        for bits in range(1, PLANES):
            plane = flip(self.plane, bits)
            copy = remote(
                self.total.at[plane, self.spot],
                self.far.at[bits - 1],
                self.send_sem.at[9 + bits],
                self.recv_sem.at[9 + bits],
                (self.core, rank_of(plane, self.spot)),
            )
            copy.start()
            self.far_copies.append(copy)

    def finish(self):
        value = self.total[self.plane, self.spot].astype(F32)
        for bits in range(1, PLANES):
            self.far_copies[bits - 1].wait_recv()
            value = value + self.far[bits - 1].astype(F32)
        self.out[...] = value
        for copy in self.copies + self.corner_copies + self.far_copies:
            copy.wait_send()
        for side in (1, 2):
            self.side_copies[side].wait_send()


REDUCE_SEMS = 13


def reduce_scratch(shape, kind):
    tail = shape[3:]
    return [
        VMEM((PLANES, SPOTS) + tail, kind),
        VMEM((PLANES, SPOTS) + tail, kind),
        VMEM((2,) + tail, kind),
        VMEM((2,) + tail, kind),
        VMEM((PLANES,) + tail, kind),
        VMEM((PLANES,) + tail, kind),
        VMEM((PLANES - 1,) + tail, kind),
    ]


class Doubling:
    STEPS = 5

    def __init__(self, totals, boxes, send_sem, recv_sem):
        self.totals, self.boxes = totals, boxes
        self.send_sem, self.recv_sem = send_sem, recv_sem
        core, plane, spot = place_here()
        self.partners = (
            (1 - core, rank_of(plane, spot)),
            (core, rank_of(plane, flip(spot, 1))),
            (core, rank_of(plane, flip(spot, 2))),
            (core, rank_of(flip(plane, 1), spot)),
            (core, rank_of(flip(plane, 2), spot)),
        )
        self.copies = []

    def start(self, step):
        self.copies = []
        for number, (total, box) in enumerate(zip(self.totals, self.boxes)):
            copy = remote(
                total,
                box.at[step],
                self.send_sem.at[step, number],
                self.recv_sem.at[step, number],
                self.partners[step],
            )
            copy.start()
            self.copies.append(copy)

    def finish(self, step):
        for copy, total, box in zip(self.copies, self.totals, self.boxes):
            copy.wait()
            total[...] += box[step]


PARTS = 3


def finish_kernel(
    recv_ref,
    normed_ref,
    x_ref,
    dres_hbm,
    vec_ref,
    w_hbm,
    g_mid_ref,
    g_up_bias_ref,
    grad_ref,
    g_qkv_ref,
    rows_out_ref,
    tiles_out_ref,
    *scratch,
):
    sources, scratch = scratch[:PARTS], scratch[PARTS:]
    buffers, scratch = scratch[: 7 * PARTS], scratch[7 * PARTS :]
    packed_ref, dnormed_ref, gradient_ref, dres_ref, w_ref = scratch[:5]
    rows_ref, tiles_ref, rows_box, tiles_box = scratch[5:9]
    send_sem, recv_sem, local_sem, load_sem, sum_send, sum_recv = scratch[9:15]
    move_sems = scratch[15:18]
    pieces, rows, _ = x_ref.shape
    tokens = pieces * rows
    core, plane, spot = place_here()
    low = low_lanes(rows)

    load_w = pltpu.make_async_copy(w_hbm, w_ref, load_sem.at[0])
    load_dres = pltpu.make_async_copy(dres_hbm, dres_ref, load_sem.at[1])
    load_w.start()
    load_dres.start()
    greet(all_partners(core, plane, spot))

    def put(tile, piece, value):
        side, chunk = tile // HALF_TILES, tile % HALF_TILES
        packed_ref[
            piece * rows : (piece + 1) * rows,
            chunk * CHUNK + side * LANES : chunk * CHUNK + (side + 1) * LANES,
        ] = value.astype(BF16)

    start_piece, finish_grad = from_planes(gradient_ref, grad_ref, *move_sems, later=True)
    for piece in range(pieces):
        seconds = []
        for goal in range(SPOTS):
            first = recv_ref[0, goal, piece, QUERIES].astype(F32)
            second = recv_ref[1, goal, piece, QUERIES].astype(F32)
            put(goal, piece, jnp.where(low, first, jnp.where(core == 0, first, second)))
            seconds.append(second)
            base = D // LANES + 3 * goal
            put(base, piece, recv_ref[0, goal, piece, KEYS_A])
            put(base + 1, piece, recv_ref[1, goal, piece, KEYS_A])
            put(base + 2, piece, recv_ref[core, goal, piece, KEYS_B])
        for number in range(2):
            put(
                SPOTS + number,
                piece,
                jnp.where(low, seconds[2 * number], swap_halves(seconds[2 * number + 1])),
            )
        if piece == 0:
            load_w.wait()
            load_dres.wait()
        span = slice(piece * rows, (piece + 1) * rows)
        share = dot_rt(packed_ref[span], w_ref[...])
        dnormed_ref[span] = share
        normal, inverse = norm_parts(x_ref[piece].astype(F32))
        gradient = dres_ref[span] + norm_pull(share, normal, inverse, vec_ref[0:1])
        gradient_ref[piece] = gradient.astype(BF16)
        start_piece(piece)
        sums = [
            jnp.sum(share * normal, axis=0, keepdims=True),
            jnp.sum(share, axis=0, keepdims=True),
        ]
        for number in range(2):
            if piece == 0:
                rows_ref[number : number + 1] = sums[number]
            else:
                rows_ref[number : number + 1] += sums[number]

    rows_ref[2:6] = g_mid_ref[...]
    rows_ref[6:8] = jnp.zeros((2, D), F32)
    tiles_ref[...] = jnp.zeros_like(tiles_ref)
    for step in range(FF // CHUNK):
        tiles_ref[step : step + 1] = g_up_bias_ref[step]
    for chunk in range(HALF_TILES):
        number = FF // CHUNK + chunk
        tiles_ref[number : number + 1] = jnp.sum(
            packed_ref[:, chunk * CHUNK : (chunk + 1) * CHUNK].astype(F32), axis=0, keepdims=True
        )
    sums = Doubling((rows_ref, tiles_ref), (rows_box, tiles_box), sum_send, sum_recv)
    sums.start(0)

    width = HALF_TILES // PARTS * LANES
    reduces = [
        Reduce(
            sources[part],
            *buffers[7 * part : 7 * part + 7],
            g_qkv_ref.at[:, part * width : (part + 1) * width],
            (send_sem.at[part], recv_sem.at[part], local_sem.at[part]),
        )
        for part in range(PARTS)
    ]
    shard = D // RANKS
    normed_t = normed_ref[...].astype(F32).T.astype(BF16)
    for part in range(PARTS):
        for number in range(HALF_TILES // PARTS):
            chunk = part * (HALF_TILES // PARTS) + number
            values = dot(normed_t, packed_ref[:, chunk * CHUNK : (chunk + 1) * CHUNK])
            columns = slice(number * LANES, (number + 1) * LANES)
            for owner in range(RANKS):
                mine = values[owner * shard : (owner + 1) * shard]
                sources[part][
                    owner // (PLANES * SPOTS), owner // SPOTS % PLANES, owner % SPOTS, :, columns
                ] = jnp.concatenate([mine[:, :LANES], mine[:, LANES:]], axis=0).astype(BF16)
        reduces[part].start()
        if part > 0:
            reduces[part - 1].corners()
        if part > 1:
            reduces[part - 2].sides()
    sums.finish(0)
    sums.start(1)
    reduces[2].corners()
    reduces[1].sides()
    sums.finish(1)
    sums.start(2)
    reduces[0].columns()
    reduces[2].sides()
    sums.finish(2)
    sums.start(3)
    reduces[1].columns()
    sums.finish(3)
    sums.start(4)
    reduces[2].columns()
    sums.finish(4)
    for one in reduces:
        one.finish()
    rows_out_ref[...] = rows_ref[...]
    tiles_out_ref[...] = tiles_ref[...]
    finish_grad()


def finish_layer(recv, normed, x, dres, vec, w, g_mid, g_up_bias):
    pieces, rows, _ = x.shape
    tokens = pieces * rows
    shard = D // RANKS
    grid = (2, PLANES, SPOTS)
    part = grid + (2 * shard, HALF_TILES // PARTS * LANES)
    buffers = []
    for _ in range(PARTS):
        buffers += reduce_scratch(part, BF16)
    tiles = -(-(FF // CHUNK + HALF_TILES) // 8) * 8
    dma = pltpu.SemaphoreType.DMA
    return pl.pallas_call(
        finish_kernel,
        out_shape=(
            jax.ShapeDtypeStruct(x.shape, BF16),
            jax.ShapeDtypeStruct((2 * shard, 3 * D // 2), F32),
            jax.ShapeDtypeStruct((8, D), F32),
            jax.ShapeDtypeStruct((tiles, CHUNK), F32),
        ),
        in_specs=[
            whole(),
            whole(),
            whole(),
            whole(ANY),
            whole(),
            whole(ANY),
            whole(),
            whole(),
        ],
        out_specs=(whole(ANY), whole(), whole(), whole()),
        scratch_shapes=[VMEM(part, BF16)] * PARTS
        + buffers
        + [
            VMEM((tokens, 3 * D), BF16),
            VMEM((tokens, D), F32),
            VMEM(x.shape, BF16),
            VMEM((tokens, D), F32),
            VMEM(w.shape, BF16),
            VMEM((8, D), F32),
            VMEM((tiles, CHUNK), F32),
            VMEM((Doubling.STEPS, 8, D), F32),
            VMEM((Doubling.STEPS, tiles, CHUNK), F32),
            dma((PARTS, REDUCE_SEMS)),
            dma((PARTS, REDUCE_SEMS)),
            dma((PARTS, 4)),
            dma((2,)),
            dma((Doubling.STEPS, 2)),
            dma((Doubling.STEPS, 2)),
            dma((2,)),
            dma((2,)),
            dma((2,)),
        ],
        compiler_params=pltpu.CompilerParams(
            vmem_limit_bytes=60 * 1024 * 1024, collective_id=2, has_side_effects=True
        ),
        name="finish_layer",
    )(recv, normed, x, dres, vec, w, g_mid, g_up_bias)


def present_kernel(
    hidden_hbm,
    grad_hbm,
    t_qkv_hbm,
    t_out_hbm,
    t_up_hbm,
    t_down_hbm,
    rows_hbm,
    tiles_hbm,
    hidden_out_ref,
    grad_out_ref,
    g_qkv_ref,
    g_out_ref,
    g_up_ref,
    g_down_ref,
    *outs,
):
    singles, (grad_ref, t_qkv_ref, t_out_ref, t_up_ref, rows_ref, tiles_ref, copy_sem) = (
        outs[:-7],
        outs[-7:],
    )
    loads = [
        pltpu.make_async_copy(source, target, copy_sem.at[number])
        for number, (source, target) in enumerate(
            (
                (rows_hbm, rows_ref),
                (tiles_hbm, tiles_ref),
                (t_qkv_hbm, t_qkv_ref),
                (t_out_hbm, t_out_ref),
                (t_up_hbm, t_up_ref),
                (grad_hbm, grad_ref),
                (t_down_hbm, g_down_ref),
                (hidden_hbm, hidden_out_ref),
            )
        )
    ]
    for copy in loads:
        copy.start()
    core, plane, spot = place_here()
    mine = core * (PLANES * SPOTS) + rank_of(plane, spot)
    own, wide = D // RANKS, FF // RANKS
    order = [natural_block(entry) for entry in column_order()]
    inverse = [order.index(number) for number in range(len(order))]

    for copy in loads[:5]:
        copy.wait()
    half = D // 2
    for side in range(2):
        rows = slice(side * own, (side + 1) * own)
        g_out_ref[:, side * half : (side + 1) * half] = t_out_ref[rows]
        for chunk in range(FF // CHUNK):
            start = side * (FF // 2) + chunk * LANES
            g_up_ref[:, start : start + LANES] = t_up_ref[chunk, rows]

    def folded(tile):
        side, chunk = tile // HALF_TILES, tile % HALF_TILES
        return t_qkv_ref[
            side * own : (side + 1) * own, chunk * LANES : (chunk + 1) * LANES
        ]

    def bias_sum(tile):
        side, chunk = tile // HALF_TILES, tile % HALF_TILES
        row = FF // CHUNK + chunk
        return tiles_ref[row : row + 1, side * LANES : (side + 1) * LANES]

    biases = []
    for tile in range(TILES):
        blocks = inverse[2 * tile], inverse[2 * tile + 1]
        g_qkv_ref[:, tile * LANES : (tile + 1) * LANES] = pair_of_blocks(folded, *blocks)
        biases.append(pair_of_blocks(bias_sum, *blocks))
    third = TILES // 3
    query = jnp.concatenate(biases[:third], axis=1)
    value = jnp.concatenate(biases[2 * third :], axis=1)
    vectors = jnp.concatenate([rows_ref[0:6], query, value], axis=0)

    def pick(values, first, wanted):
        place = lax.broadcasted_iota(jnp.int32, (values.shape[1], LANES), 0) + first
        lane = lax.broadcasted_iota(jnp.int32, (values.shape[1], LANES), 1)
        one_hot = jnp.where(place == mine * wanted + lane, 1.0, 0.0)
        return lax.dot_general(
            values,
            one_hot,
            (((1,), (0,)), ((), ())),
            precision=lax.Precision.HIGHEST,
            preferred_element_type=F32,
        )

    picked = pick(vectors, 0, own)
    for number in range(VECTORS):
        singles[number][...] = picked[number : number + 1, :own]
    total = jnp.zeros((1, LANES), F32)
    for chunk in range(FF // CHUNK):
        for side in range(2):
            total = total + pick(
                tiles_ref[chunk : chunk + 1, side * LANES : (side + 1) * LANES],
                side * (FF // 2) + chunk * LANES,
                wide,
            )
    singles[VECTORS][...] = total[:, :wide]
    loads[5].wait()
    grad_out_ref[...] = grad_ref[...].astype(F32)
    for copy in loads[6:]:
        copy.wait()


def present(hidden, grad, t_qkv, t_out, t_up, t_down, rows, tiles):
    own, wide = D // RANKS, FF // RANKS
    struct = jax.ShapeDtypeStruct
    return pl.pallas_call(
        present_kernel,
        out_shape=(
            struct(hidden.shape, BF16),
            struct(grad.shape, F32),
            struct((own, 3 * D), F32),
            struct((own, D), F32),
            struct((own, FF), F32),
            struct((wide, D), F32),
        )
        + (struct((1, own), F32),) * VECTORS
        + (struct((1, wide), F32),),
        in_specs=[whole(ANY)] * 8,
        out_specs=(whole(),) * (7 + VECTORS),
        scratch_shapes=[
            VMEM(item.shape, item.dtype) for item in (grad, t_qkv, t_out, t_up, rows, tiles)
        ]
        + [pltpu.SemaphoreType.DMA((8,))],
        compiler_params=params_of(63),
        name="present",
    )(hidden, grad, t_qkv, t_out, t_up, t_down, rows, tiles)


def plane_shards(
    hidden_in,
    rand_table,
    norm1_gain,
    norm1_bias,
    w_qkv,
    query_bias,
    value_bias,
    w_out,
    out_bias,
    norm2_gain,
    norm2_bias,
    w_up,
    up_bias,
    w_down,
    down_bias,
    cotangent,
):
    micro, rows, _ = hidden_in.shape
    local = rows // BLOCK

    def in_row(vector, number):
        return jnp.pad(vector[None], ((number, 15 - number), (0, LANES - vector.shape[0])))

    vec = functools.reduce(
        jnp.add,
        [
            in_row(vector, number)
            for number, vector in enumerate(
                (
                    norm1_gain,
                    norm1_bias,
                    query_bias,
                    value_bias,
                    out_bias,
                    norm2_gain,
                    norm2_bias,
                    down_bias,
                    up_bias,
                )
            )
        ],
    )
    tab = jnp.pad(
        rand_table.reshape(micro, local * RANDOM), ((0, 8 - micro), (0, LANES - local * RANDOM))
    )
    (
        mixed,
        far_mixed,
        x,
        dy,
        w_down_all,
        w_qkv_all,
        w_out_all,
        w_up_all,
        qk,
        shared,
        normed,
        lse,
        vectors,
        up_shift,
        table,
        sorted_table,
    ) = front(hidden_in, cotangent, vec, tab, w_qkv, w_out, w_up, w_down)
    mixed = mixed.reshape(SPOTS, PIECES, rows, LANES)
    far_mixed = far_mixed.reshape(SPOTS, PIECES, rows // 2, LANES)
    (
        hidden,
        near_grad,
        far_grad,
        dres,
        g_out,
        half_up,
        half_down,
        last_up,
        last_down,
        g_up_bias,
        g_mid,
    ) = plane_middle(
        mixed,
        far_mixed,
        x,
        dy.reshape(micro * rows, D),
        vectors,
        w_out_all,
        up_shift,
        w_up_all,
        w_down_all.reshape(2, FF // 2, D),
    )
    grid = (2, PLANES, SPOTS)
    dqkv, hidden_out, t_out, t_up, t_down = plane_attention_back(
        table,
        sorted_table,
        qk,
        shared,
        near_grad.reshape(SPOTS, PIECES, local, BLOCK, LANES),
        far_grad.reshape(SPOTS, PIECES, local // 2, BLOCK, LANES),
        lse,
        hidden,
        [
            g_out.reshape((1,) + grid + g_out.shape[1:]),
            last_up,
            last_down,
        ],
        half_up,
        half_down,
    )
    dqkv = dqkv.reshape(2, SPOTS, PIECES, 3, rows, LANES)
    grad_hidden, t_qkv, sum_rows, sum_tiles = finish_layer(
        dqkv, normed, x, dres, vectors, w_qkv_all, g_mid, g_up_bias
    )

    results = present(hidden_out, grad_hidden, t_qkv, t_out, t_up, t_down, sum_rows, sum_tiles)
    hidden_out, grad_hidden, g_qkv, g_out, g_up, g_down = results[:6]
    n1g, n1b, n2g, n2b, db, ob, qb, vb, ub = (item.reshape(item.size) for item in results[6:])
    return (
        hidden_out,
        grad_hidden,
        n1g,
        n1b,
        g_qkv,
        qb,
        vb,
        g_out,
        ob,
        n2g,
        n2b,
        g_up,
        ub,
        g_down,
        db,
    )


def shards(*arrays):
    micro, rows, _ = arrays[0].shape
    fits = lax.axis_size("gx") == 2 and lax.axis_size("gy") == PLANES * SPOTS
    fits = fits and micro == 2 and rows == 4 * BLOCK
    return (plane_shards if fits else general_shards)(*arrays)


def solution(mesh):
    tokens = P(None, AXES, None)
    vector = P(AXES)
    matrix = P(AXES, None)
    placed = (
        tokens,
        tokens,
        vector,
        vector,
        matrix,
        vector,
        vector,
        matrix,
        vector,
        vector,
        vector,
        matrix,
        vector,
        matrix,
        vector,
        tokens,
    )
    returned = (
        tokens,
        tokens,
        vector,
        vector,
        matrix,
        vector,
        vector,
        matrix,
        vector,
        vector,
        vector,
        matrix,
        vector,
        matrix,
        vector,
    )
    return jax.shard_map(
        shards, mesh=mesh, in_specs=placed, out_specs=returned, check_vma=False
    )
```

```python
import functools

import jax
import jax.numpy as jnp
from jax import lax
from jax.experimental import pallas as pl
from jax.experimental.pallas import tpu as pltpu
from jax.sharding import PartitionSpec as P

HEADS = 12
HEAD_DIM = 64
D = 768
FF = 3072
BLOCK = 64
RANDOM = 3
LANES = 2 * HEAD_DIM
EPSILON = 1e-05
NEGATIVE = -1e30
SCALE = HEAD_DIM**-0.5
CHUNK = 256
SPAN = 8

F32 = jnp.float32
BF16 = jnp.bfloat16
VMEM = pltpu.VMEM


def whole(space=VMEM):
    return pl.BlockSpec(memory_space=space)


def params_of(megabytes):
    return pltpu.CompilerParams(vmem_limit_bytes=megabytes * 1024 * 1024)


def head_place(head):
    return (head // 3) * 4 + head % 3


def dot(left, right):
    return lax.dot_general(left, right, (((1,), (0,)), ((), ())), preferred_element_type=F32)


def dot_rt(left, right):
    return lax.dot_general(left, right, (((1,), (1,)), ((), ())), preferred_element_type=F32)


def dot_lt(left, right):
    return lax.dot_general(left, right, (((0,), (0,)), ((), ())), preferred_element_type=F32)


def swap_halves(tile):
    return pltpu.roll(tile, HEAD_DIM, axis=tile.ndim - 1)


def low_lanes(rows):
    return lax.broadcasted_iota(jnp.int32, (rows, LANES), 1) < HEAD_DIM


def norm_parts(values):
    centre = values - jnp.mean(values, axis=-1, keepdims=True)
    spread = jnp.mean(centre * centre, axis=-1, keepdims=True)
    inverse = lax.rsqrt(spread + EPSILON)
    return centre * inverse, inverse


def norm_pull(grad, normal, inverse, gain):
    scaled = grad * gain
    return inverse * (
        scaled
        - jnp.mean(scaled, axis=-1, keepdims=True)
        - normal * jnp.mean(scaled * normal, axis=-1, keepdims=True)
    )


def qkv_kernel(x_ref, gain_ref, shift_ref, w_ref, bias_ref, normed_ref, send_ref):
    micro, rows, _ = x_ref.shape
    values = x_ref[...].reshape(micro * rows, D).astype(F32)
    normal, _ = norm_parts(values)
    normed_ref[...] = (normal * gain_ref[...] + shift_ref[...]).astype(BF16)
    low = low_lanes(rows)
    for chunk in range(3 * D // CHUNK):
        columns = slice(chunk * CHUNK, (chunk + 1) * CHUNK)
        packed = dot(normed_ref[...], w_ref[:, columns]) + bias_ref[:, columns]
        if chunk < D // CHUNK:
            packed = packed.astype(BF16).astype(F32) * SCALE
        for tile in range(CHUNK // LANES):
            part = packed[:, tile * LANES : (tile + 1) * LANES]
            first, second = part[:rows], part[rows:]
            if chunk < D // CHUNK:
                head = (chunk * CHUNK // LANES + tile) * 2
                even = jnp.where(low, first, swap_halves(second))
                odd = jnp.where(low, swap_halves(first), second)
                send_ref[head_place(head), 0] = even.astype(BF16)
                send_ref[head_place(head + 1), 0] = odd.astype(BF16)
            else:
                head = (chunk * CHUNK - D) // LANES + tile
                send_ref[head_place(head), 1] = first.astype(BF16)
                send_ref[head_place(head), 2] = swap_halves(second).astype(BF16)


def qkv_forward(x, gain, shift, w, bias, groups):
    micro, rows, _ = x.shape
    return pl.pallas_call(
        qkv_kernel,
        out_shape=(
            jax.ShapeDtypeStruct((micro * rows, D), BF16),
            jax.ShapeDtypeStruct((groups, 3, rows, LANES), BF16),
        ),
        in_specs=[whole()] * 5,
        out_specs=(whole(), whole()),
        compiler_params=params_of(48),
        name="qkv_forward",
    )(x, gain, shift, w, bias)


def half_mask(low_half):
    lane = lax.broadcasted_iota(jnp.int32, (1, LANES), 1)
    keep = (lane < HEAD_DIM) if low_half else (lane >= HEAD_DIM)
    return jnp.where(keep, 1.0, 0.0).astype(BF16)


def inner_slots(pick, block, blocks):
    ids, bias = picked_slots([pick(block, number) for number in range(RANDOM)], block, blocks)
    edge = (block == 0) | (block == blocks - 1)
    ids[0] = jnp.maximum(ids[0], 0)
    ids[2] = jnp.minimum(ids[2], blocks - 1)
    return ids, bias + jnp.where(edge, NEGATIVE, 0.0).astype(F32)


def slots_of(table_ref, micro, block, blocks):
    picks = [table_ref[micro, block * RANDOM + number] for number in range(RANDOM)]
    return picked_slots(picks, block, blocks)


def picked_slots(picks, block, blocks):
    last = blocks - 1
    ids = [block - 1, block, block + 1, 0, last] + picks
    dropped = [None, None, None, block == 1, block == last - 1]
    for number in range(RANDOM):
        pick = picks[number]
        bad = (jnp.abs(pick - block) <= 1) | (pick == 0) | (pick == last)
        for earlier in range(number):
            bad = bad | (pick == picks[earlier])
        dropped.append(bad)
    lane = lax.broadcasted_iota(jnp.int32, (1, LANES), 1)
    tiles = []
    for pair in range(len(ids) // 2):
        level = [
            0.0 if bad is None else jnp.where(bad, NEGATIVE, 0.0).astype(F32)
            for bad in dropped[2 * pair : 2 * pair + 2]
        ]
        tiles.append(jnp.where(lane < HEAD_DIM, level[0], level[1]))
    return ids, jnp.concatenate(tiles, axis=1)


def attend_kernel(table_ref, qkv_ref, out_ref, lse_ref, s_ref):
    groups, _, local, _, _ = qkv_ref.shape
    blocks = groups * local
    low = low_lanes(BLOCK)
    masks = [half_mask(True), half_mask(False)]

    def load(component, block):
        return qkv_ref[block // local, component, block % local]

    def sparse(block, carry):
        mixed, logs = [], []
        for micro in range(2):
            ids, bias = slots_of(table_ref, micro, block, blocks)
            keys = jnp.concatenate([load(1 + micro, spot) for spot in ids], axis=0)
            query = load(0, block) * masks[micro]
            scores = dot_rt(query, keys) + bias
            top = jnp.max(scores, axis=1, keepdims=True)
            powered = jnp.exp(scores - top)
            total = jnp.sum(powered, axis=1, keepdims=True)
            mixed.append(dot(powered.astype(BF16), keys) * (1.0 / total))
            logs.append(top + jnp.log(total))
        out_ref[block // local, block % local] = jnp.where(low, mixed[1], mixed[0]).astype(BF16)
        lse_ref[block] = jnp.where(low, logs[0], logs[1])
        return carry

    lax.fori_loop(1, blocks - 1, sparse, 0)

    spans = blocks // SPAN
    ends = (0, blocks - 1)
    results = []
    for micro in range(2):
        query = jnp.concatenate([load(0, end) for end in ends], axis=0) * masks[micro]

        def keys_at(span, micro=micro):
            return jnp.concatenate(
                [load(1 + micro, span * SPAN + spot) for spot in range(SPAN)], axis=0
            )

        def first_pass(span, top, query=query, keys_at=keys_at):
            scores = dot_rt(query, keys_at(span))
            s_ref[span] = scores
            return jnp.maximum(top, jnp.max(scores, axis=1, keepdims=True))

        top = lax.fori_loop(0, spans, first_pass, jnp.full((2 * BLOCK, 1), NEGATIVE, F32))

        def second_pass(span, carry, top=top, keys_at=keys_at):
            total, mixed = carry
            powered = jnp.exp(s_ref[span] - top)
            return (
                total + jnp.sum(powered, axis=1, keepdims=True),
                mixed + dot(powered.astype(BF16), keys_at(span)),
            )

        total, mixed = lax.fori_loop(
            0,
            spans,
            second_pass,
            (jnp.zeros((2 * BLOCK, 1), F32), jnp.zeros((2 * BLOCK, LANES), F32)),
        )
        results.append((mixed * (1.0 / total), top + jnp.log(total)))
    for place, end in enumerate(ends):
        rows = slice(place * BLOCK, (place + 1) * BLOCK)
        out_ref[end // local, end % local] = jnp.where(
            low, results[1][0][rows], results[0][0][rows]
        ).astype(BF16)
        lse_ref[end] = jnp.where(low, results[0][1][rows], results[1][1][rows])


def attention_forward(table, qkv):
    groups, _, local, _, _ = qkv.shape
    blocks = groups * local
    return pl.pallas_call(
        attend_kernel,
        out_shape=(
            jax.ShapeDtypeStruct((groups, local, BLOCK, LANES), BF16),
            jax.ShapeDtypeStruct((blocks, BLOCK, LANES), F32),
        ),
        in_specs=[whole(pltpu.SMEM), whole()],
        out_specs=(whole(), whole()),
        scratch_shapes=[VMEM((blocks // SPAN, 2 * BLOCK, SPAN * BLOCK), F32)],
        compiler_params=params_of(48),
        name="attention_forward",
    )(table, qkv)


def attend_back_kernel(table_ref, qkv_ref, grad_ref, lse_ref, out_ref, sums_ref, p_ref, dp_ref):
    groups, _, local, _, _ = qkv_ref.shape
    blocks = groups * local
    low = low_lanes(BLOCK)
    masks = [half_mask(True), half_mask(False)]

    def load(component, block):
        return qkv_ref[block // local, component, block % local]

    def load_grad(block):
        return grad_ref[block // local, block % local]

    def clear(block, carry):
        for micro in range(2):
            sums_ref[micro, block] = jnp.zeros((BLOCK, LANES), F32)
        return carry

    lax.fori_loop(0, blocks, clear, 0)

    def sparse(block, carry):
        grads = []
        for micro in range(2):
            ids, bias = slots_of(table_ref, micro, block, blocks)
            keys = jnp.concatenate([load(1 + micro, spot) for spot in ids], axis=0)
            both = jnp.concatenate(
                [load(0, block) * masks[micro], load_grad(block) * masks[1 - micro]], axis=0
            )
            products = dot_rt(both, keys)
            logs = lse_ref[block][:, micro * HEAD_DIM : micro * HEAD_DIM + 1]
            weights = jnp.exp(products[:BLOCK] + bias - logs)
            grad_weights = products[BLOCK:]
            delta = jnp.sum(weights * grad_weights, axis=1, keepdims=True)
            grad_scores = weights * (grad_weights - delta)
            stacked = jnp.concatenate([grad_scores, weights], axis=0).astype(BF16)
            grads.append(dot(stacked[:BLOCK], keys))
            shares = dot_lt(stacked, both)
            for place, spot in enumerate(ids):
                sums_ref[micro, spot] += shares[place * BLOCK : (place + 1) * BLOCK]
        out_ref[block // local, 0, block % local] = (
            jnp.where(low, grads[0], grads[1]) * SCALE
        ).astype(BF16)
        return carry

    lax.fori_loop(1, blocks - 1, sparse, 0)

    spans = blocks // SPAN
    ends = (0, blocks - 1)
    results = []
    for micro in range(2):
        query = jnp.concatenate([load(0, end) for end in ends], axis=0) * masks[micro]
        grad = jnp.concatenate([load_grad(end) for end in ends], axis=0) * masks[1 - micro]
        both = jnp.concatenate([query, grad], axis=0)
        logs = jnp.concatenate(
            [lse_ref[end][:, micro * HEAD_DIM : micro * HEAD_DIM + 1] for end in ends], axis=0
        )

        def keys_at(span, micro=micro):
            return jnp.concatenate(
                [load(1 + micro, span * SPAN + spot) for spot in range(SPAN)], axis=0
            )

        def first_pass(span, delta, both=both, logs=logs, keys_at=keys_at):
            products = dot_rt(both, keys_at(span))
            weights = jnp.exp(products[: 2 * BLOCK] - logs)
            grad_weights = products[2 * BLOCK :]
            p_ref[span] = weights
            dp_ref[span] = grad_weights
            return delta + jnp.sum(weights * grad_weights, axis=1, keepdims=True)

        delta = lax.fori_loop(0, spans, first_pass, jnp.zeros((2 * BLOCK, 1), F32))

        def second_pass(span, carry, delta=delta, both=both, keys_at=keys_at, micro=micro):
            weights = p_ref[span]
            grad_scores = weights * (dp_ref[span] - delta)
            stacked = jnp.concatenate([grad_scores, weights], axis=0).astype(BF16)
            shares = dot_lt(stacked, both)
            for spot in range(SPAN):
                sums_ref[micro, span * SPAN + spot] += shares[spot * BLOCK : (spot + 1) * BLOCK]
            return carry + dot(stacked[: 2 * BLOCK], keys_at(span))

        results.append(
            lax.fori_loop(0, spans, second_pass, jnp.zeros((2 * BLOCK, LANES), F32))
        )
    for place, end in enumerate(ends):
        rows = slice(place * BLOCK, (place + 1) * BLOCK)
        out_ref[end // local, 0, end % local] = (
            jnp.where(low, results[0][rows], results[1][rows]) * SCALE
        ).astype(BF16)

    def finish(block, carry):
        for micro in range(2):
            out_ref[block // local, 1 + micro, block % local] = sums_ref[micro, block].astype(BF16)
        return carry

    lax.fori_loop(0, blocks, finish, 0)


def attention_backward(table, qkv, grad, lse):
    groups, _, local, _, _ = qkv.shape
    blocks = groups * local
    spans = VMEM((blocks // SPAN, 2 * BLOCK, SPAN * BLOCK), F32)
    return pl.pallas_call(
        attend_back_kernel,
        out_shape=jax.ShapeDtypeStruct(qkv.shape, BF16),
        in_specs=[whole(pltpu.SMEM), whole(), whole(), whole()],
        out_specs=whole(),
        scratch_shapes=[VMEM((2, blocks, BLOCK, LANES), F32), spans, spans],
        compiler_params=params_of(48),
        name="attention_backward",
    )(table, qkv, grad, lse)


def middle_kernel(
    mixed_in_ref,
    x_ref,
    dy_ref,
    w_out_ref,
    out_shift_ref,
    gain_ref,
    shift_ref,
    up_shift_ref,
    down_shift_ref,
    w_up_ref,
    w_down_ref,
    hidden_ref,
    send_ref,
    dres_ref,
    g_out_ref,
    g_up_ref,
    g_down_ref,
    g_up_bias_ref,
    g_small_ref,
    mixed_ref,
    residual_ref,
    second_ref,
    second_t_ref,
    total_ref,
    dsecond_ref,
):
    micro, rows, _ = x_ref.shape
    step = pl.program_id(0)
    low = low_lanes(rows)

    @pl.when(step == 0)
    def _():
        for pair in range(HEADS // 2):
            even = mixed_in_ref[head_place(2 * pair)].astype(F32)
            odd = mixed_in_ref[head_place(2 * pair + 1)].astype(F32)
            columns = slice(pair * LANES, (pair + 1) * LANES)
            mixed_ref[:rows, columns] = jnp.where(low, swap_halves(even), odd).astype(BF16)
            mixed_ref[rows:, columns] = jnp.where(low, even, swap_halves(odd)).astype(BF16)
        residual = x_ref[...].reshape(micro * rows, D).astype(F32) + (
            dot(mixed_ref[...], w_out_ref[...]) + out_shift_ref[...]
        )
        residual_ref[...] = residual
        normal, _ = norm_parts(residual)
        second = normal * gain_ref[...] + shift_ref[...]
        second_ref[...] = second.astype(BF16)
        second_t_ref[...] = second.T.astype(BF16)
        total_ref[...] = jnp.zeros_like(total_ref)
        dsecond_ref[...] = jnp.zeros_like(dsecond_ref)

    upper = dot(second_ref[...], w_up_ref[...]) + up_shift_ref[...]
    factor = 0.7978845608028654
    square = upper * upper
    bent = jnp.tanh(factor * (upper + 0.044715 * (upper * square)))
    half = 0.5 * (1.0 + bent)
    active = (upper * half).astype(BF16)
    slope = half + 0.5 * upper * (1.0 - bent * bent) * (
        factor + (3.0 * 0.044715 * factor) * square
    )
    dy = dy_ref[...]
    total_ref[...] += dot(active, w_down_ref[...])
    g_down_ref[...] = dot_lt(active, dy).astype(g_down_ref.dtype)
    dupper = (dot_rt(dy, w_down_ref[...]) * slope).astype(BF16)
    g_up_bias_ref[...] = jnp.sum(dupper.astype(F32), axis=0, keepdims=True)
    g_up_ref[...] = dot(second_t_ref[...], dupper).astype(g_up_ref.dtype)
    dsecond_ref[...] += dot_rt(dupper, w_up_ref[...])

    @pl.when(step == pl.num_programs(0) - 1)
    def _():
        residual = residual_ref[...]
        hidden_ref[...] = (
            (residual + (total_ref[...] + down_shift_ref[...])).astype(BF16).reshape(x_ref.shape)
        )
        normal, inverse = norm_parts(residual)
        dsecond = dsecond_ref[...]
        grad_out = dy_ref[...].astype(F32)
        g_small_ref[0:1] = jnp.sum(dsecond * normal, axis=0, keepdims=True)
        g_small_ref[1:2] = jnp.sum(dsecond, axis=0, keepdims=True)
        g_small_ref[2:3] = jnp.sum(grad_out, axis=0, keepdims=True)
        dres = grad_out + norm_pull(dsecond, normal, inverse, gain_ref[...])
        dres_ref[...] = dres
        branch = dres.astype(BF16)
        g_small_ref[3:4] = jnp.sum(branch.astype(F32), axis=0, keepdims=True)
        g_out_ref[...] = dot_lt(mixed_ref[...], branch).astype(g_out_ref.dtype)
        dmixed = dot_rt(branch, w_out_ref[...])
        for pair in range(HEADS // 2):
            part = dmixed[:, pair * LANES : (pair + 1) * LANES]
            first, last = part[:rows], part[rows:]
            even = jnp.where(low, last, swap_halves(first))
            odd = jnp.where(low, swap_halves(last), first)
            send_ref[head_place(2 * pair)] = even.astype(BF16)
            send_ref[head_place(2 * pair + 1)] = odd.astype(BF16)


def middle(mixed_in, x, dy, w_out, out_shift, gain, shift, up_shift, down_shift, w_up, w_down, kind):
    micro, rows, _ = x.shape
    tokens = micro * rows
    groups = mixed_in.shape[0]

    def fixed(shape):
        return pl.BlockSpec(shape, lambda step: (0,) * len(shape))

    vector = fixed((1, D))
    steps = FF // CHUNK
    return pl.pallas_call(
        middle_kernel,
        grid=(steps,),
        out_shape=(
            jax.ShapeDtypeStruct(x.shape, BF16),
            jax.ShapeDtypeStruct((groups, rows, LANES), BF16),
            jax.ShapeDtypeStruct((tokens, D), F32),
            jax.ShapeDtypeStruct((D, D), kind),
            jax.ShapeDtypeStruct((D, FF), kind),
            jax.ShapeDtypeStruct((FF, D), kind),
            jax.ShapeDtypeStruct((1, FF), F32),
            jax.ShapeDtypeStruct((4, D), F32),
        ),
        in_specs=[
            fixed(mixed_in.shape),
            fixed(x.shape),
            fixed((tokens, D)),
            fixed((D, D)),
            vector,
            vector,
            vector,
            pl.BlockSpec((1, CHUNK), lambda step: (0, step)),
            vector,
            pl.BlockSpec((D, CHUNK), lambda step: (0, step)),
            pl.BlockSpec((CHUNK, D), lambda step: (step, 0)),
        ],
        out_specs=(
            fixed(x.shape),
            fixed((groups, rows, LANES)),
            fixed((tokens, D)),
            fixed((D, D)),
            pl.BlockSpec((D, CHUNK), lambda step: (0, step)),
            pl.BlockSpec((CHUNK, D), lambda step: (step, 0)),
            pl.BlockSpec((1, CHUNK), lambda step: (0, step)),
            fixed((4, D)),
        ),
        scratch_shapes=[
            VMEM((tokens, D), BF16),
            VMEM((tokens, D), F32),
            VMEM((tokens, D), BF16),
            VMEM((D, tokens), BF16),
            VMEM((tokens, D), F32),
            VMEM((tokens, D), F32),
        ],
        compiler_params=params_of(56),
        name="middle",
    )(mixed_in, x, dy, w_out, out_shift, gain, shift, up_shift, down_shift, w_up, w_down)


def qkv_back_kernel(
    recv_ref,
    normed_ref,
    x_ref,
    dres_ref,
    gain_ref,
    w_ref,
    grad_ref,
    g_qkv_ref,
    g_bias_ref,
    g_small_ref,
    packed_ref,
    normed_t_ref,
    dnormed_ref,
):
    micro, rows, _ = x_ref.shape
    step = pl.program_id(0)
    low = low_lanes(rows)

    @pl.when(step == 0)
    def _():
        for pair in range(HEADS // 2):
            even = recv_ref[head_place(2 * pair), 0].astype(F32)
            odd = recv_ref[head_place(2 * pair + 1), 0].astype(F32)
            spot, columns = pair // 2, slice((pair % 2) * LANES, (pair % 2 + 1) * LANES)
            packed_ref[spot, :rows, columns] = jnp.where(low, even, swap_halves(odd)).astype(BF16)
            packed_ref[spot, rows:, columns] = jnp.where(low, swap_halves(even), odd).astype(BF16)
        for head in range(HEADS):
            spot = D // CHUNK + head // 2
            columns = slice((head % 2) * LANES, (head % 2 + 1) * LANES)
            packed_ref[spot, :rows, columns] = recv_ref[head_place(head), 1]
            packed_ref[spot, rows:, columns] = swap_halves(
                recv_ref[head_place(head), 2].astype(F32)
            ).astype(BF16)
        normed_t_ref[...] = normed_ref[...].astype(F32).T.astype(BF16)
        dnormed_ref[...] = jnp.zeros_like(dnormed_ref)

    packed = packed_ref[step]
    g_bias_ref[...] = jnp.sum(packed.astype(F32), axis=0, keepdims=True)
    g_qkv_ref[...] = dot(normed_t_ref[...], packed).astype(g_qkv_ref.dtype)
    dnormed_ref[...] += dot_rt(packed, w_ref[...])

    @pl.when(step == pl.num_programs(0) - 1)
    def _():
        normal, inverse = norm_parts(x_ref[...].reshape(micro * rows, D).astype(F32))
        dnormed = dnormed_ref[...]
        g_small_ref[0:1] = jnp.sum(dnormed * normal, axis=0, keepdims=True)
        g_small_ref[1:2] = jnp.sum(dnormed, axis=0, keepdims=True)
        grad = dres_ref[...] + norm_pull(dnormed, normal, inverse, gain_ref[...])
        grad_ref[...] = grad.reshape(x_ref.shape)


def qkv_backward(recv, normed, x, dres, gain, w, kind):
    micro, rows, _ = x.shape
    tokens = micro * rows

    def fixed(shape):
        return pl.BlockSpec(shape, lambda step: (0,) * len(shape))

    steps = 3 * D // CHUNK
    return pl.pallas_call(
        qkv_back_kernel,
        grid=(steps,),
        out_shape=(
            jax.ShapeDtypeStruct(x.shape, F32),
            jax.ShapeDtypeStruct((D, 3 * D), kind),
            jax.ShapeDtypeStruct((1, 3 * D), F32),
            jax.ShapeDtypeStruct((2, D), F32),
        ),
        in_specs=[
            fixed(recv.shape),
            fixed((tokens, D)),
            fixed(x.shape),
            fixed((tokens, D)),
            fixed((1, D)),
            pl.BlockSpec((D, CHUNK), lambda step: (0, step)),
        ],
        out_specs=(
            fixed(x.shape),
            pl.BlockSpec((D, CHUNK), lambda step: (0, step)),
            pl.BlockSpec((1, CHUNK), lambda step: (0, step)),
            fixed((2, D)),
        ),
        scratch_shapes=[
            VMEM((steps, tokens, CHUNK), BF16),
            VMEM((D, tokens), BF16),
            VMEM((tokens, D), F32),
        ],
        compiler_params=params_of(56),
        name="qkv_backward",
    )(recv, normed, x, dres, gain, w)


AXES = ("gx", "gy")


def gather(array):
    return lax.all_gather(array, AXES, axis=0, tiled=True)


def scatter(array):
    return lax.psum_scatter(array, AXES, scatter_dimension=0, tiled=True)


def exchange(array):
    return lax.all_to_all(array, "gy", 0, 0, tiled=True)


def by_heads(w_qkv):
    rows = w_qkv.shape[0]
    sides = w_qkv[:, D:].reshape(rows, 2, HEADS, HEAD_DIM)
    return jnp.concatenate([w_qkv[:, :D], jnp.swapaxes(sides, 1, 2).reshape(rows, 2 * D)], axis=1)


def by_parts(w_qkv):
    rows = w_qkv.shape[0]
    sides = w_qkv[:, D:].reshape(rows, HEADS, 2, HEAD_DIM)
    return jnp.concatenate([w_qkv[:, :D], jnp.swapaxes(sides, 1, 2).reshape(rows, 2 * D)], axis=1)


def general_shards(
    hidden_in,
    rand_table,
    norm1_gain,
    norm1_bias,
    w_qkv,
    query_bias,
    value_bias,
    w_out,
    out_bias,
    norm2_gain,
    norm2_bias,
    w_up,
    up_bias,
    w_down,
    down_bias,
    cotangent,
):
    micro, rows, _ = hidden_in.shape
    groups = lax.axis_size("gy")
    local = rows // BLOCK
    own = norm1_gain.shape[0]

    vectors = jnp.concatenate(
        [
            norm1_gain,
            norm1_bias,
            query_bias,
            value_bias,
            out_bias,
            norm2_gain,
            norm2_bias,
            down_bias,
            up_bias,
        ]
    )
    table = lax.all_gather(rand_table, "gy", axis=1, tiled=True)
    table = table.reshape(micro, groups * local * RANDOM)
    vectors = gather(vectors[None]).astype(F32)
    gain_one, shift_one, query_shift, value_shift, out_shift, gain_two, shift_two, down_shift = (
        vectors[:, number * own : (number + 1) * own].reshape(1, D) for number in range(8)
    )
    up_shift = vectors[:, 8 * own :].reshape(1, FF)
    w_qkv_full = gather(by_heads(w_qkv))
    w_out_full, w_up_full, w_down_full = gather(w_out), gather(w_up), gather(w_down)
    packed_bias = by_heads(
        jnp.concatenate([query_shift, jnp.zeros_like(query_shift), value_shift], axis=1)
    )

    normed, send = qkv_forward(hidden_in, gain_one, shift_one, w_qkv_full, packed_bias, groups)
    qkv = exchange(send).reshape(groups, 3, local, BLOCK, LANES)
    mixed, lse = attention_forward(table, qkv)
    mixed_back = exchange(mixed.reshape(groups, rows, LANES))
    hidden_out, grad_send, dres, g_out, g_up, g_down, g_up_bias, g_mid = middle(
        mixed_back,
        hidden_in,
        cotangent.reshape(micro * rows, D),
        w_out_full,
        out_shift,
        gain_two,
        shift_two,
        up_shift,
        down_shift,
        w_up_full,
        w_down_full,
        F32,
    )
    grad_mixed = exchange(grad_send).reshape(groups, local, BLOCK, LANES)
    dqkv = attention_backward(table, qkv, grad_mixed, lse)
    dqkv_back = exchange(dqkv.reshape(groups, 3, rows, LANES))
    grad_hidden, g_qkv, g_packed, g_first = qkv_backward(
        dqkv_back, normed, hidden_in, dres, gain_one, w_qkv_full, F32
    )

    g_packed = by_parts(g_packed)
    small = [
        g_first[0],
        g_first[1],
        g_packed[0, :D],
        g_packed[0, 2 * D :],
        g_mid[3],
        g_mid[0],
        g_mid[1],
        g_mid[2],
    ]
    ranks = D // own
    small = jnp.concatenate(
        [item.reshape(ranks, own) for item in small] + [g_up_bias.reshape(ranks, 4 * own)], axis=1
    )
    small = scatter(small)[0]
    parts = [small[number * own : (number + 1) * own] for number in range(8)]
    return (
        hidden_out,
        grad_hidden,
        parts[0],
        parts[1],
        by_parts(scatter(g_qkv)),
        parts[2],
        parts[3],
        scatter(g_out),
        parts[4],
        parts[5],
        parts[6],
        scatter(g_up),
        small[8 * own :],
        scatter(g_down),
        parts[7],
    )


MESH = pl.DeviceIdType.MESH
ANY = pl.ANY
PLANES = 4
SPOTS = 4
PIECES = 2
RANKS = 2 * PLANES * SPOTS
TILES = 3 * D // LANES
HALF_TILES = TILES // 2
QUERY_ORDER = (0, 2, 3, 5, 6, 8, 9, 11, 1, 4, 7, 10)


def column_order():
    order = [("q", head) for head in QUERY_ORDER]
    for spot in range(SPOTS):
        for place in (2 * 3 * spot, 2 * 3 * spot + 2):
            order += [("k", place // 2), ("v", place // 2)]
        order += [("v", 3 * spot + 2), ("k", 3 * spot + 2)]
    return order


def natural_block(entry):
    return "qkv".index(entry[0]) * HEADS + entry[1]


def flip(value, bits):
    if bits == 0:
        return value
    if bits == 1:
        return value + 1 - 2 * lax.rem(value, 2)
    if bits == 2:
        return value + 2 - 4 * lax.div(value, 2)
    return 3 - value


def place_here():
    core, rank = lax.axis_index("gx"), lax.axis_index("gy")
    return core, lax.div(rank, SPOTS), lax.rem(rank, SPOTS)


def rank_of(plane, spot):
    return plane * SPOTS + spot


def greet(partners):
    barrier = pltpu.get_barrier_semaphore()
    for partner in partners:
        pl.semaphore_signal(barrier, inc=1, device_id=partner, device_id_type=MESH)
    pl.semaphore_wait(barrier, len(partners))


def remote(source, target, send_sem, recv_sem, device):
    return pltpu.make_async_remote_copy(
        src_ref=source,
        dst_ref=target,
        send_sem=send_sem,
        recv_sem=recv_sem,
        device_id=device,
        device_id_type=MESH,
    )


def column_partners(core, plane, spot):
    partners = [(1 - core, rank_of(plane, spot))]
    for bits in range(1, PLANES):
        for other in (core, 1 - core):
            partners.append((other, rank_of(flip(plane, bits), spot)))
    return partners


def all_partners(core, plane, spot):
    return column_partners(core, plane, spot) + [
        (core, rank_of(plane, flip(spot, 1))),
        (core, rank_of(plane, flip(spot, 2))),
    ]


def to_planes(source, target, send_sem, recv_sem, local_sem):
    core, plane, spot = place_here()
    half, odd = lax.div(plane, 2), lax.rem(plane, 2)
    sends, keeps = [], []
    for micro in range(2):
        goal = 2 * micro + core
        here = (goal == plane) & (half == core)
        send = remote(
            source.at[micro],
            target.at[odd],
            send_sem.at[micro],
            recv_sem.at[odd],
            (half, rank_of(goal, spot)),
        )
        keep = pltpu.make_async_copy(source.at[micro], target.at[odd], local_sem.at[micro])

        @pl.when(jnp.logical_not(here))
        def _(send=send):
            send.start()

        @pl.when(here)
        def _(keep=keep):
            keep.start()

        sends.append((here, send))
        keeps.append((here, keep))

    def finish():
        for piece in range(PIECES):
            mine = (odd == core) & (plane == 2 * core + piece)
            arrival = remote(
                source.at[0],
                target.at[piece],
                send_sem.at[0],
                recv_sem.at[piece],
                (core, rank_of(plane, spot)),
            )

            @pl.when(jnp.logical_not(mine))
            def _(arrival=arrival):
                arrival.wait_recv()

        for (here, send), (_, keep) in zip(sends, keeps):

            @pl.when(jnp.logical_not(here))
            def _(send=send):
                send.wait_send()

            @pl.when(here)
            def _(keep=keep):
                keep.wait()

    return finish


def from_planes(source, target, send_sem, recv_sem, local_sem, later=False):
    core, plane, spot = place_here()
    micro, odd = lax.div(plane, 2), lax.rem(plane, 2)
    sends, keeps = [], []

    def start(piece):
        goal = 2 * core + piece
        here = (goal == plane) & (odd == core)
        send = remote(
            source.at[piece],
            target.at[micro],
            send_sem.at[piece],
            recv_sem.at[micro],
            (odd, rank_of(goal, spot)),
        )
        keep = pltpu.make_async_copy(source.at[piece], target.at[micro], local_sem.at[piece])

        @pl.when(jnp.logical_not(here))
        def _(send=send):
            send.start()

        @pl.when(here)
        def _(keep=keep):
            keep.start()

        sends.append((here, send))
        keeps.append((here, keep))

    for piece in () if later else range(PIECES):
        start(piece)

    def finish():
        for number in range(2):
            mine = (2 * number + core == plane) & (micro == core)
            arrival = remote(
                source.at[0],
                target.at[number],
                send_sem.at[0],
                recv_sem.at[number],
                (core, rank_of(plane, spot)),
            )

            @pl.when(jnp.logical_not(mine))
            def _(arrival=arrival):
                arrival.wait_recv()

        for (here, send), (_, keep) in zip(sends, keeps):

            @pl.when(jnp.logical_not(here))
            def _(send=send):
                send.wait_send()

            @pl.when(here)
            def _(keep=keep):
                keep.wait()

    return (start, finish) if later else finish


class Gather:
    SENDS = 31

    def __init__(self, source, target, send_sem, recv_sem, local_sem):
        self.source, self.target = source, target
        self.send_sem, self.recv_sem = send_sem, recv_sem
        self.core, self.plane, self.spot = place_here()
        self.sends = []
        self.own = pltpu.make_async_copy(
            source, target.at[self.core, self.plane, self.spot], local_sem
        )
        self.own.start()

    def send(self, source, plane, spot, device):
        copy = remote(
            source,
            self.target.at[self.core, plane, spot],
            self.send_sem.at[len(self.sends)],
            self.recv_sem.at[self.core, plane, spot],
            device,
        )
        copy.start()
        self.sends.append(copy)

    def arrive(self, core, plane, spot):
        shard = self.target.at[core, plane, spot]
        remote(
            shard,
            shard,
            self.send_sem.at[0],
            self.recv_sem.at[core, plane, spot],
            (self.core, rank_of(self.plane, self.spot)),
        ).wait_recv()

    def neighbour(self, bits):
        return (self.core, rank_of(self.plane, flip(self.spot, bits)))

    def sibling(self):
        return (1 - self.core, rank_of(self.plane, self.spot))

    def start(self):
        for bits in range(1, PLANES):
            goal = (self.core, rank_of(flip(self.plane, bits), self.spot))
            self.send(self.source, self.plane, self.spot, goal)
        for goal in (self.neighbour(1), self.neighbour(2), self.sibling()):
            self.send(self.source, self.plane, self.spot, goal)

    def column(self):
        for bits in range(1, PLANES):
            plane = flip(self.plane, bits)
            self.arrive(self.core, plane, self.spot)
            shard = self.target.at[self.core, plane, self.spot]
            for goal in (self.neighbour(1), self.neighbour(2), self.sibling()):
                self.send(shard, plane, self.spot, goal)

    def across(self):
        for bits in range(PLANES):
            plane = flip(self.plane, bits)
            for side in (1, 2):
                spot = flip(self.spot, side)
                self.arrive(self.core, plane, spot)
                shard = self.target.at[self.core, plane, spot]
                if (side == 1) == (bits < 2):
                    self.send(shard, plane, spot, self.neighbour(3 - side))
                self.send(shard, plane, spot, self.sibling())

    def corner(self):
        spot = flip(self.spot, 3)
        for bits in range(PLANES):
            plane = flip(self.plane, bits)
            self.arrive(self.core, plane, spot)
            self.send(self.target.at[self.core, plane, spot], plane, spot, self.sibling())

    def finish(self):
        for bits in range(PLANES):
            for side in range(SPOTS):
                self.arrive(1 - self.core, flip(self.plane, bits), flip(self.spot, side))
        self.own.wait()
        for copy in self.sends:
            copy.wait_send()


def settle(shards_ref, plan):
    rows = shards_ref.shape[3] // 2

    def pair(number, carry):
        core, plane, side = (
            lax.div(number, 2 * PLANES),
            lax.rem(lax.div(number, 2), PLANES),
            lax.rem(number, 2),
        )
        goal = pl.ds(pl.multiple_of(number * 2 * rows, 16), 2 * rows)
        for tile, out_ref, (left, right) in plan:
            columns = slice(tile * LANES, (tile + 1) * LANES)
            first = shards_ref[core, plane, 2 * side, :, columns].astype(F32)
            second = shards_ref[core, plane, 2 * side + 1, :, columns].astype(F32)
            out_ref[goal, left * LANES : (left + 1) * LANES] = jnp.concatenate(
                [first[:rows], second[:rows]], axis=0
            ).astype(BF16)
            out_ref[goal, right * LANES : (right + 1) * LANES] = jnp.concatenate(
                [first[rows:], second[rows:]], axis=0
            ).astype(BF16)
        return carry

    lax.fori_loop(0, RANKS // 2, pair, 0)


def alternate(tile):
    return 2 * tile, 2 * tile + 1


def plane_partners(core, plane, spot):
    partners = []
    for other in (core, 1 - core):
        for side in range(SPOTS):
            if other is core and side == 0:
                continue
            partners.append((other, rank_of(plane, flip(spot, side))))
    return partners


def both_partners(core, plane, spot):
    return plane_partners(core, plane, spot) + column_partners(core, plane, spot)[1:]


def exchange_sems(recv_shape):
    return [
        pltpu.SemaphoreType.DMA((14,)),
        pltpu.SemaphoreType.DMA(recv_shape),
        pltpu.SemaphoreType.DMA((PIECES,)),
    ]


def sort_entries(table, sorted_ref, entries):
    count = table.shape[1]
    core = lax.axis_index("gx")
    lane = lax.broadcasted_iota(jnp.int32, (count, count), 1)
    row = lax.broadcasted_iota(jnp.int32, (count, count), 0).astype(F32)
    everything = jnp.broadcast_to(table, (count, count))
    half = entries // 2
    inside = (lane >= core * half) & (lane < (core + 1) * half)
    lane = lane.astype(F32)
    for number, along in enumerate((everything, jnp.where(inside, everything, 2.0 * LANES))):
        down = along.T
        before = (along < down) | ((along == down) & (lane < row))
        rank = jnp.sum(jnp.where(before, 1.0, 0.0), axis=1, keepdims=True)
        order = jnp.sum(jnp.where(rank == lane, row, 0.0), axis=0, keepdims=True)
        upto = jnp.sum(jnp.where(down <= lane, 1.0, 0.0), axis=0, keepdims=True)
        sorted_ref[2 * number : 2 * number + 1] = order.astype(jnp.int32)
        sorted_ref[2 * number + 1 : 2 * number + 2] = upto.astype(jnp.int32)


def pack_halves(read, target_ref, place, local, low, half):
    for number in range(local // 2):
        first = read(2 * number).astype(F32)
        second = swap_halves(read(2 * number + 1).astype(F32))
        kept = (first, second) if half == 0 else (second, first)
        target_ref[place + (number,)] = jnp.where(low, *kept).astype(BF16)


class Outward:
    def __init__(self, source, far_source, target, packed, send_sem, recv_sem, local_sem):
        self.target, self.packed = target, packed
        self.recv_sem, self.send_sem = recv_sem, send_sem
        self.core, self.plane, self.spot = place_here()
        self.sends, self.keeps = [], []
        for side in (3, 1, 2, 0):
            goal = flip(self.spot, side)
            for other in (self.core, 1 - self.core):
                near = other is self.core
                for piece in range(PIECES):
                    start = (source if near else far_source).at[goal, piece]
                    place = (2 * self.core + piece, self.spot)
                    stop = (target if near else packed).at[place]
                    if side == 0 and near:
                        copy = pltpu.make_async_copy(start, stop, local_sem.at[piece])
                        self.keeps.append(copy)
                    else:
                        copy = remote(
                            start,
                            stop,
                            send_sem.at[len(self.sends)],
                            recv_sem.at[place],
                            (other, rank_of(self.plane, goal)),
                        )
                        self.sends.append(copy)
                    copy.start()

    def arrive(self, side):
        goal = flip(self.spot, side)
        for other in (self.core, 1 - self.core):
            near = other is self.core
            if side == 0 and near:
                for copy in self.keeps:
                    copy.wait()
                continue
            for piece in range(PIECES):
                place = (2 * other + piece, goal)
                landed = (self.target if near else self.packed).at[place]
                remote(
                    landed,
                    landed,
                    self.send_sem.at[0],
                    self.recv_sem.at[place],
                    (self.core, rank_of(self.plane, self.spot)),
                ).wait_recv()
                if not near:
                    for number in range(self.packed.shape[2]):
                        tile = self.packed[place + (number,)]
                        self.target[place + (2 * number,)] = tile
                        self.target[place + (2 * number + 1,)] = swap_halves(
                            tile.astype(F32)
                        ).astype(BF16)

    def finish(self):
        for copy in self.sends:
            copy.wait_send()


def inward_targets(core, spot):
    for side in (3, 1, 2, 0):
        for other in (core, 1 - core):
            yield side, other, flip(spot, side), side == 0 and other is core


class Inward:
    def __init__(self, source, target, send_sem, recv_sem, local_sem):
        self.source, self.target = source, target
        self.send_sem, self.recv_sem, self.local_sem = send_sem, recv_sem, local_sem
        self.core, self.plane, self.spot = place_here()
        self.sends, self.keeps = [], []

    def send(self, other, goal, stays, piece, part, parts):
        source = self.source.at[2 * other + piece, goal, parts]
        target = self.target.at[self.core, self.spot, piece, parts]
        if stays:
            copy = pltpu.make_async_copy(source, target, self.local_sem.at[part, piece])
            self.keeps.append(copy)
        else:
            copy = remote(
                source,
                target,
                self.send_sem.at[len(self.sends)],
                self.recv_sem.at[self.core, self.spot, piece, part],
                (other, rank_of(self.plane, goal)),
            )
            self.sends.append(copy)
        copy.start()

    def finish(self, parts_of):
        for side, other, goal, stays in inward_targets(self.core, self.spot):
            if stays:
                continue
            for piece in range(PIECES):
                for part, parts in enumerate(parts_of[0 if other is self.core else 1]):
                    target = self.target.at[other, goal, piece, parts]
                    remote(
                        target,
                        target,
                        self.send_sem.at[0],
                        self.recv_sem.at[other, goal, piece, part],
                        (self.core, rank_of(self.plane, self.spot)),
                    ).wait_recv()
        for copy in self.sends:
            copy.wait_send()
        for copy in self.keeps:
            copy.wait()


KEYS_A, QUERIES, KEYS_B = range(3)


def plane_attend_back_kernel(*refs):
    table_ref, sorted_ref, qk_ref, shared_ref, near_grad_ref, far_grad_ref, lse_ref, hidden_ref = (
        refs[:8]
    )
    sources, half_up_ref, half_down_ref, refs = refs[8:11], refs[11], refs[12], refs[13:]
    sources = list(sources[:2]) + [sources[2].at[number] for number in range(LATE)]
    back_ref, far_back_ref, hidden_out_ref, t_out_ref, t_up_ref, t_down_ref = refs[:6]
    count = 2 + LATE
    refs = refs[6:]
    buffers, mines, refs = refs[: 3 * count], refs[3 * count : 4 * count], refs[4 * count :]
    part_out_ref, part_up_ref, part_down_ref, far_out_ref, far_up_ref, far_down_ref = refs[:6]
    grad_ref, packed_ref, out_ref, sums_ref, shares_ref, walked_ref, sibling_ref = refs[6:13]
    pack_ref, scores_refs, refs = refs[13], refs[14:18], refs[18:]
    reduce_send, reduce_recv, far_send, far_recv, load_sem = refs[:5]
    grad_sems, back_sems, move_sems, sibling_sems = refs[5:8], refs[8:11], refs[11:14], refs[14:16]
    pack_send, pack_recv = refs[16:18]

    local = qk_ref.shape[3]
    groups = PLANES * SPOTS
    blocks = groups * local
    core, plane, spot = place_here()
    low = low_lanes(BLOCK)
    masks = [half_mask(True), half_mask(False)]

    greet(both_partners(core, plane, spot))
    grads = Outward(near_grad_ref, far_grad_ref, grad_ref, packed_ref, *grad_sems)
    reduces = [
        SpotReduce(
            source,
            *buffers[3 * number : 3 * number + 3],
            reduce_send.at[number],
            reduce_recv.at[number],
            rows=FF // RANKS if number >= 2 else None,
            mine=mine,
        )
        for number, (source, mine) in enumerate(zip(sources, mines))
    ]
    ready = PER_STAGE * EARLY
    loads = [
        pltpu.make_async_copy(one.half(core), mine, load_sem.at[number])
        for number, (one, mine) in enumerate(zip(reduces, mines))
    ] + [
        pltpu.make_async_copy(half_up_ref, part_up_ref.at[0:ready], load_sem.at[count]),
        pltpu.make_async_copy(half_down_ref, part_down_ref.at[0:EARLY], load_sem.at[count + 1]),
    ]
    for one in reduces:
        one.start()
    for copy in loads:
        copy.start()

    def far(bits, number, source, target):
        return remote(
            source,
            target,
            far_send.at[number, bits - 1],
            far_recv.at[number, bits - 1],
            (core, rank_of(flip(plane, bits), spot)),
        )

    def far_down(bits, source):
        return far(bits, 3, source, far_down_ref.at[bits - 1])

    fars = []
    for bits in range(1, PLANES):
        goal = flip(plane, bits)
        copy = far(bits, 0, half_up_ref.at[:, goal], far_up_ref.at[bits - 1, 0:ready])
        copy.start()
        fars.append(copy)

        @pl.when(goal < EARLY)
        def _(bits=bits, goal=goal):
            far_down(bits, half_down_ref.at[jnp.minimum(goal, EARLY - 1)]).start()

    finish_hidden = from_planes(hidden_ref, hidden_out_ref, *move_sems)

    def load(component, block):
        rank, number = lax.div(block, local), lax.rem(block, local)
        if component == 2:
            return shared_ref[lax.div(rank, SPOTS), lax.rem(rank, SPOTS), number]
        return qk_ref[lax.div(rank, SPOTS), lax.rem(rank, SPOTS), component, number]

    def load_grad(block):
        rank = lax.div(block, local)
        return grad_ref[lax.div(rank, SPOTS), lax.rem(rank, SPOTS), lax.rem(block, local)]

    def store(component, block, value):
        rank = lax.div(block, local)
        out_ref[
            lax.div(rank, SPOTS), lax.rem(rank, SPOTS), component, lax.rem(block, local)
        ] = value.astype(BF16)

    def stored(component, block):
        rank = lax.div(block, local)
        return out_ref[
            lax.div(rank, SPOTS), lax.rem(rank, SPOTS), component, lax.rem(block, local)
        ].astype(F32)

    nothing = jnp.zeros((BLOCK, LANES), F32)

    def clear(block, carry):
        for slot in range(2):
            sums_ref[slot, block] = nothing
        return carry

    lax.fori_loop(0, blocks, clear, 0)

    def picked(block, number):
        return table_ref[0, block * RANDOM + number]

    def one_block(block, slot):
        ids, bias = inner_slots(picked, block, blocks)
        keys = jnp.concatenate([load(1 + slot, number) for number in ids], axis=0)
        both = jnp.concatenate(
            [load(0, block) * masks[slot], load_grad(block) * masks[1 - slot]], axis=0
        )
        products = dot_rt(both, keys)
        logs = lse_ref[block][:, slot * HEAD_DIM : slot * HEAD_DIM + 1]
        weights = jnp.exp(products[:BLOCK] + bias - logs)
        grad_weights = products[BLOCK:]
        delta = jnp.sum(weights * grad_weights, axis=1, keepdims=True)
        grad_scores = weights * (grad_weights - delta)
        stacked = jnp.concatenate([grad_scores, weights], axis=0).astype(BF16)
        return dot(stacked[:BLOCK], keys), dot_lt(stacked, both)

    fixed = 5

    def rank_blocks(rank, slot):
        first = rank * local
        results = [one_block(first + number, slot) for number in range(local)]

        def share(number, place):
            return results[number][1][place * BLOCK : (place + 1) * BLOCK]

        for shift in range(-1, local + 1):
            parts = [
                share(number, shift - number + 1)
                for number in range(local)
                if 0 <= shift - number + 1 <= 2
            ]
            target = jnp.minimum(jnp.maximum(first + shift, 0), blocks - 1)
            sums_ref[slot, target] += functools.reduce(jnp.add, parts)
        for place, target in ((3, 0), (4, blocks - 1)):
            sums_ref[slot, target] += functools.reduce(
                jnp.add, [share(number, place) for number in range(local)]
            )
        for number in range(local):
            for pick in range(RANDOM):
                shares_ref[slot, (first + number) * RANDOM + pick] = share(number, fixed + pick)
        return [result[0] for result in results]

    def head_a(side):
        def body(number, carry):
            rank = number * SPOTS + flip(spot, side)
            for place, query in enumerate(rank_blocks(rank, 0)):
                store(QUERIES, rank * local + place, query * SCALE)
            return carry

        lax.fori_loop(0, PLANES, body, 0)

    def head_b(number, carry):
        rank = core * (groups // 2) + number
        for place, query in enumerate(rank_blocks(rank, 1)):
            block = rank * local + place
            store(QUERIES, block, jnp.where(low, stored(QUERIES, block), query * SCALE))
        return carry

    spans = blocks // SPAN
    ends = (0, blocks - 1)

    def dense(slot, p_ref, d_ref, numbers):
        both = jnp.concatenate(
            [load(0, number) * masks[slot] for number in numbers]
            + [load_grad(number) * masks[1 - slot] for number in numbers],
            axis=0,
        )
        rows = len(numbers) * BLOCK
        column = slot * HEAD_DIM
        logs = jnp.concatenate(
            [lse_ref[number][:, column : column + 1] for number in numbers], axis=0
        )

        def keys_at(span):
            return jnp.concatenate(
                [load(1 + slot, span * SPAN + number) for number in range(SPAN)], axis=0
            )

        def first_pass(span, delta):
            products = dot_rt(both, keys_at(span))
            weights = jnp.exp(products[:rows] - logs)
            grad_weights = products[rows:]
            p_ref[span] = weights
            d_ref[span] = grad_weights
            return delta + jnp.sum(weights * grad_weights, axis=1, keepdims=True)

        delta = lax.fori_loop(0, spans, first_pass, jnp.zeros((rows, 1), F32), unroll=2)

        def second_pass(span, total):
            weights = p_ref[span]
            grad_scores = weights * (d_ref[span] - delta)
            stacked = jnp.concatenate([grad_scores, weights], axis=0).astype(BF16)
            shares = dot_lt(stacked, both)
            for number in range(SPAN):
                sums_ref[slot, span * SPAN + number] += shares[
                    number * BLOCK : (number + 1) * BLOCK
                ]
            return total + dot(stacked[:rows], keys_at(span))

        total = lax.fori_loop(0, spans, second_pass, jnp.zeros((rows, LANES), F32), unroll=2)
        for place, number in enumerate(numbers):
            query = total[place * BLOCK : (place + 1) * BLOCK] * SCALE
            if slot == 1:
                query = jnp.where(low, stored(QUERIES, number), query)
            store(QUERIES, number, query)

    def walk(slot, length):
        def body(number, total):
            entry = sorted_ref[2 * slot, number]
            earlier = sorted_ref[2 * slot, jnp.maximum(number - 1, 0)]
            keep = jnp.where(table_ref[0, entry] == table_ref[0, earlier], 1.0, 0.0).astype(F32)
            total = total * keep + shares_ref[slot, entry]
            walked_ref[slot, number] = total.astype(BF16)
            return total

        lax.fori_loop(0, length, body, nothing, unroll=4)

    def close(slot, rank, component):
        def body(number, carry):
            block = rank * local + number
            stop = sorted_ref[2 * slot + 1, block]
            start = jnp.where(block == 0, 0, sorted_ref[2 * slot + 1, jnp.maximum(block - 1, 0)])
            some = jnp.where(stop > start, 1.0, 0.0).astype(F32)
            share = walked_ref[slot, jnp.maximum(stop - 1, 0)].astype(F32)
            store(component, block, sums_ref[slot, block] + share * some)
            return carry

        lax.fori_loop(0, local, body, 0, unroll=True)

    back = Inward(out_ref, back_ref, *back_sems)
    own_parts = (slice(0, 1), slice(1, 2), slice(2, 3))
    far_parts = (slice(0, 1),)
    packs = []

    for side in range(SPOTS):
        grads.arrive(side)
        head_a(side)
        if side == 0:
            for copy in loads:
                copy.wait()
            for one in reduces:
                one.corners()
        if side == 1:
            for one in reduces:
                one.sides()
    reduces[0].close(part_out_ref)
    reduces[1].close(part_up_ref.at[ready : PER_STAGE * STAGES])
    for number in range(LATE):
        reduces[2 + number].close(part_down_ref.at[EARLY + number])
    for bits in range(1, PLANES):
        goal = flip(plane, bits)
        late = slice(ready, PER_STAGE * STAGES)
        for copy in (
            far(bits, 1, part_out_ref.at[:, goal], far_out_ref.at[bits - 1]),
            far(bits, 2, part_up_ref.at[late, goal], far_up_ref.at[bits - 1, late]),
        ):
            copy.start()
            fars.append(copy)

        @pl.when(goal >= EARLY)
        def _(bits=bits, goal=goal):
            far_down(bits, part_down_ref.at[goal]).start()

        fars.append(far_down(bits, part_down_ref.at[goal]))
    dense(0, scores_refs[0], scores_refs[1], ends)
    walk(0, blocks * RANDOM)
    for side, other, goal, stays in inward_targets(core, spot):
        for piece in range(PIECES):
            close(0, (2 * other + piece) * SPOTS + goal, KEYS_A)
            if other is core:
                back.send(other, goal, stays, piece, 0, own_parts[0])
            else:
                back.send(other, goal, stays, piece, 0, far_parts[0])
                pack_halves(
                    lambda number, other=other, goal=goal, piece=piece: out_ref[
                        2 * other + piece, goal, QUERIES, number
                    ],
                    pack_ref,
                    (piece, goal),
                    local,
                    low,
                    0,
                )
                copy = remote(
                    pack_ref.at[piece, goal],
                    far_back_ref.at[spot, piece],
                    pack_send.at[piece, side],
                    pack_recv.at[spot, piece],
                    (other, rank_of(plane, goal)),
                )
                copy.start()
                packs.append(copy)
    lax.fori_loop(0, groups // 2, head_b, 0)
    dense(1, scores_refs[2], scores_refs[3], (core * (blocks - 1),))
    for side, other, goal, stays in inward_targets(core, spot):
        if other is core:
            for piece in range(PIECES):
                back.send(other, goal, stays, piece, 1, own_parts[1])
    walk(1, blocks * RANDOM // 2)
    for number in range(PIECES):
        for goal in range(SPOTS):
            close(1, (2 * (1 - core) + number) * SPOTS + goal, KEYS_B)
    across = remote(
        out_ref.at[pl.ds(2 * (1 - core), PIECES), :, KEYS_B],
        sibling_ref,
        sibling_sems[0],
        sibling_sems[1],
        (1 - core, rank_of(plane, spot)),
    )
    across.start()
    for number in range(PIECES):
        for goal in range(SPOTS):
            close(1, (2 * core + number) * SPOTS + goal, KEYS_B)
    across.wait_recv()
    for side, other, goal, stays in inward_targets(core, spot):
        if other is core:
            for piece in range(PIECES):
                place = (2 * core + piece, goal, KEYS_B)
                out_ref[place] = (
                    out_ref[place].astype(F32) + sibling_ref[piece, goal].astype(F32)
                ).astype(BF16)
                back.send(other, goal, stays, piece, 2, own_parts[2])
    for copy in fars:
        copy.wait()

    def total(part, far, index):
        value = part.astype(F32)
        for bits in range(PLANES - 1):
            value = value + far[(bits,) + index].astype(F32)
        return value

    t_out_ref[...] = total(part_out_ref[0, plane], far_out_ref, (0,))

    def close_up(number, carry):
        t_up_ref[number] = total(part_up_ref[number, plane], far_up_ref, (number,))
        return carry

    lax.fori_loop(0, PER_STAGE * STAGES, close_up, 0)
    t_down_ref[...] = total(part_down_ref[plane], far_down_ref, ())
    finish_hidden()
    grads.finish()
    across.wait_send()
    back.finish((own_parts, far_parts))
    for copy in packs:
        copy.wait_send()
    for goal in range(SPOTS):
        for piece in range(PIECES):
            target = far_back_ref.at[goal, piece]
            remote(
                target,
                target,
                pack_send.at[0, 0],
                pack_recv.at[goal, piece],
                (core, rank_of(plane, spot)),
            ).wait_recv()


def plane_attention_back(
    table, sorted_table, qk, shared, near, far, lse, hidden, sources, half_up, half_down
):
    local = qk.shape[3]
    blocks = PLANES * SPOTS * local
    spans = blocks // SPAN
    shard, rows = D // RANKS, FF // RANKS
    up_count = PER_STAGE * STAGES
    up_tail, out_tail = (2 * shard, LANES), (2 * shard, D // 2)
    buffers = block_scratch(1, *out_tail) + block_scratch(PER_STAGE * LATE, *up_tail)
    for _ in range(LATE):
        buffers += row_scratch(rows, D)
    count = 2 + LATE
    mines = [
        VMEM((1, PLANES, SPOTS) + out_tail, BF16),
        VMEM((PER_STAGE * LATE, PLANES, SPOTS) + up_tail, BF16),
    ] + [VMEM((SPOTS * rows, D), BF16)] * LATE
    parts = [
        VMEM((1, PLANES) + out_tail, BF16),
        VMEM((up_count, PLANES) + up_tail, BF16),
        VMEM((STAGES, rows, D), BF16),
        VMEM((PLANES - 1, 1) + out_tail, BF16),
        VMEM((PLANES - 1, up_count) + up_tail, BF16),
        VMEM((PLANES - 1, rows, D), BF16),
    ]
    tile = (local, BLOCK, LANES)
    wide = VMEM((spans, 2 * BLOCK, SPAN * BLOCK), F32)
    thin = VMEM((spans, BLOCK, SPAN * BLOCK), F32)
    dma = pltpu.SemaphoreType.DMA
    return pl.pallas_call(
        plane_attend_back_kernel,
        out_shape=(
            jax.ShapeDtypeStruct((2, SPOTS, PIECES, 3) + tile, BF16),
            jax.ShapeDtypeStruct((SPOTS, PIECES, local // 2, BLOCK, LANES), BF16),
            jax.ShapeDtypeStruct(hidden.shape, BF16),
            jax.ShapeDtypeStruct(out_tail, F32),
            jax.ShapeDtypeStruct((up_count,) + up_tail, F32),
            jax.ShapeDtypeStruct((rows, D), F32),
        ),
        in_specs=[
            whole(pltpu.SMEM),
            whole(pltpu.SMEM),
            whole(),
            whole(),
            whole(ANY),
            whole(ANY),
            whole(),
            whole(ANY),
        ]
        + [whole(ANY)] * 5,
        out_specs=(whole(ANY),) * 3 + (whole(),) * 3,
        scratch_shapes=buffers
        + mines
        + parts
        + [
            VMEM((PLANES, SPOTS) + tile, BF16),
            VMEM((PLANES, SPOTS, local // 2, BLOCK, LANES), BF16),
            VMEM((PLANES, SPOTS, 3) + tile, BF16),
            VMEM((2, blocks, BLOCK, LANES), F32),
            VMEM((2, blocks * RANDOM, BLOCK, LANES), F32),
            VMEM((2, blocks * RANDOM, BLOCK, LANES), BF16),
            VMEM((PIECES, SPOTS) + tile, BF16),
            VMEM((PIECES, SPOTS, local // 2, BLOCK, LANES), BF16),
            wide,
            wide,
            thin,
            thin,
            dma((count, SpotReduce.SEMS)),
            dma((count, SpotReduce.SEMS)),
            dma((4, PLANES - 1)),
            dma((4, PLANES - 1)),
            dma((count + 2,)),
        ]
        + exchange_sems((PLANES, SPOTS))
        + [
            dma((36,)),
            dma((2, SPOTS, PIECES, 3)),
            dma((3, PIECES)),
            dma((2,)),
            dma((2,)),
            dma((2,)),
            dma,
            dma,
            dma((PIECES, SPOTS)),
            dma((SPOTS, PIECES)),
        ],
        compiler_params=pltpu.CompilerParams(
            vmem_limit_bytes=62 * 1024 * 1024, collective_id=5, has_side_effects=True
        ),
        name="plane_attention_back",
    )(table, sorted_table, qk, shared, near, far, lse, hidden, *sources, half_up, half_down)


class PlaneGather:
    SENDS = 3 + 3 + 4 + 2

    def __init__(self, source, target, send_sem, column_sem, recv_sem, local_sem):
        self.source, self.target = source, target
        self.send_sem, self.column_sem, self.recv_sem = send_sem, column_sem, recv_sem
        self.core, self.plane, self.spot = place_here()
        self.sends = []
        self.own = pltpu.make_async_copy(
            source, target.at[self.core, self.plane, self.spot], local_sem
        )
        self.own.start()
        for bits in range(1, PLANES):
            copy = remote(
                source,
                target.at[self.core, self.plane, self.spot],
                send_sem.at[len(self.sends)],
                column_sem.at[self.plane],
                (self.core, rank_of(flip(self.plane, bits), self.spot)),
            )
            copy.start()
            self.sends.append(copy)

    def neighbour(self, bits):
        return (self.core, rank_of(self.plane, flip(self.spot, bits)))

    def sibling(self):
        return (1 - self.core, rank_of(self.plane, self.spot))

    def piece(self, core, planes, spot):
        return self.target.at[core, planes, spot]

    def send(self, planes, spot, part, goal):
        piece = self.piece(self.core, planes, spot)
        copy = remote(
            piece,
            piece,
            self.send_sem.at[len(self.sends)],
            self.recv_sem.at[self.core, spot, part],
            goal,
        )
        copy.start()
        self.sends.append(copy)

    def arrive(self, core, planes, spot, part):
        piece = self.piece(core, planes, spot)
        remote(
            piece,
            piece,
            self.send_sem.at[0],
            self.recv_sem.at[core, spot, part],
            (self.core, rank_of(self.plane, self.spot)),
        ).wait_recv()

    def columns(self):
        self.own.wait()
        for bits in range(1, PLANES):
            other = flip(self.plane, bits)
            shard = self.target.at[self.core, other, self.spot]
            remote(
                shard,
                shard,
                self.send_sem.at[0],
                self.column_sem.at[other],
                (self.core, rank_of(self.plane, self.spot)),
            ).wait_recv()
        for goal in (self.neighbour(1), self.neighbour(2), self.sibling()):
            self.send(slice(0, PLANES), self.spot, 0, goal)

    def forward(self):
        everything = slice(0, PLANES)
        for side in (1, 2):
            spot = flip(self.spot, side)
            self.arrive(self.core, everything, spot, 0)
            half = slice(0, 2) if side == 1 else slice(2, 4)
            self.send(half, spot, side - 1, self.neighbour(3 - side))
            self.send(everything, spot, 0, self.sibling())

    def corner(self):
        spot = flip(self.spot, 3)
        for part, half in enumerate((slice(0, 2), slice(2, 4))):
            self.arrive(self.core, half, spot, part)
            self.send(half, spot, part, self.sibling())

    def finish(self):
        for side in range(3):
            self.arrive(1 - self.core, slice(0, PLANES), flip(self.spot, side), 0)
        for part, half in enumerate((slice(0, 2), slice(2, 4))):
            self.arrive(1 - self.core, half, flip(self.spot, 3), part)
        for copy in self.sends:
            copy.wait_send()


class CrossGather:
    SENDS = 2 + 1 + 3 + 3 * 4

    def __init__(self, source, target, send_sem, spot_sem, recv_sem, local_sem):
        self.target = target
        self.send_sem, self.spot_sem, self.recv_sem = send_sem, spot_sem, recv_sem
        self.core, self.plane, self.spot = place_here()
        self.sends = []
        self.own = pltpu.make_async_copy(
            source, target.at[self.core, self.plane, self.spot], local_sem
        )
        self.own.start()
        for side in (1, 2):
            self.pass_on(source, self.spot, flip(self.spot, side))

    def push(self, source, target, recv_sem, device):
        copy = remote(source, target, self.send_sem.at[len(self.sends)], recv_sem, device)
        copy.start()
        self.sends.append(copy)

    def pass_on(self, source, spot, goal):
        self.push(
            source,
            self.target.at[self.core, self.plane, spot],
            self.spot_sem.at[spot],
            (self.core, rank_of(self.plane, goal)),
        )

    def await_spot(self, spot):
        shard = self.target.at[self.core, self.plane, spot]
        remote(
            shard,
            shard,
            self.send_sem.at[0],
            self.spot_sem.at[spot],
            (self.core, rank_of(self.plane, self.spot)),
        ).wait_recv()

    def across(self):
        beside, beyond = flip(self.spot, 1), flip(self.spot, 2)
        for side in (1, 2):
            self.await_spot(flip(self.spot, side))
        spot = beside * (1 - self.core) + beyond * self.core
        goal = beyond * (1 - self.core) + beside * self.core
        self.pass_on(self.target.at[self.core, self.plane, spot], spot, goal)

    def blocks(self):
        self.own.wait()
        self.await_spot(flip(self.spot, 3))
        self.maybe = []
        self.along(self.plane, 1, self.plane < PLANES - 1)
        self.along(self.plane, -1, self.plane > 0)
        self.to_sibling(self.plane, self.plane >= 0)

    def along(self, plane, step, wanted):
        block = self.target.at[self.core, plane]
        copy = remote(
            block,
            block,
            self.send_sem.at[3 + len(self.maybe)],
            self.recv_sem.at[self.core, plane],
            (self.core, rank_of(self.plane + step, self.spot)),
        )
        self.begin(copy, wanted)

    def to_sibling(self, plane, wanted):
        block = self.target.at[self.core, plane]
        copy = remote(
            block,
            block,
            self.send_sem.at[3 + len(self.maybe)],
            self.recv_sem.at[self.core, plane],
            (1 - self.core, rank_of(self.plane, self.spot)),
        )
        self.begin(copy, wanted)

    def begin(self, copy, wanted):
        self.maybe.append((copy, wanted))

        @pl.when(wanted)
        def _():
            copy.start()

    def arrive(self, core, plane):
        block = self.target.at[core, plane]
        remote(
            block,
            block,
            self.send_sem.at[0],
            self.recv_sem.at[core, plane],
            (self.core, rank_of(self.plane, self.spot)),
        ).wait_recv()

    def hop(self, distance):
        for step in (1, -1):
            origin = self.plane - step * distance
            here = (origin >= 0) & (origin < PLANES)
            onward = self.plane + step
            more = here & (onward >= 0) & (onward < PLANES)

            @pl.when(here)
            def _(origin=origin):
                self.arrive(self.core, origin)

            self.along(origin, step, more)
            self.to_sibling(origin, here)

    def finish(self):
        for bits in range(PLANES):
            self.arrive(1 - self.core, flip(self.plane, bits))
        for copy in self.sends:
            copy.wait_send()
        for copy, wanted in self.maybe:

            @pl.when(wanted)
            def _(copy=copy):
                copy.wait_send()


def pair_of_blocks(read, first, second):
    low = low_lanes(1)
    tiles = []
    for block, wanted in ((first, 0), (second, 1)):
        tile = read(block // 2)
        tiles.append(tile if block % 2 == wanted else swap_halves(tile))
    return jnp.where(low, tiles[0], tiles[1])


def fold_tiles(target_ref, start, tiles, read):
    half = len(tiles) // 2
    for number in range(half):
        columns = slice((start + number) * LANES, (start + number + 1) * LANES)
        target_ref[:, columns] = jnp.concatenate(
            [read(tiles[number]), read(tiles[half + number])], axis=0
        ).astype(BF16)


VECTORS = 8


def lay_vectors(vecs_ref, vectors_ref, up_ref):
    rows = vecs_ref.shape[3]
    own, wide = D // RANKS, FF // RANKS
    values = vecs_ref[...].reshape(RANKS, rows, LANES).astype(F32)

    def spread_out(count, width):
        place = lax.broadcasted_iota(jnp.int32, (LANES, count), 1)
        lane = lax.broadcasted_iota(jnp.int32, (LANES, count), 0)
        start = lax.div(place, width) * width
        return jnp.where(place - start == lane, 1.0, 0.0).astype(BF16)

    laid = dot(vecs_ref[...].reshape(RANKS * rows, LANES), spread_out(D, own))
    owner = lax.broadcasted_iota(jnp.int32, (RANKS, 1, D), 0)
    column = lax.broadcasted_iota(jnp.int32, (RANKS, 1, D), 2)
    laid = jnp.where(lax.div(column, own) == owner, laid.reshape(RANKS, rows, D), 0.0)
    vectors_ref[...] = jnp.sum(laid, axis=0)[:VECTORS]
    row = lax.broadcasted_iota(jnp.int32, (1, rows, LANES), 1)
    last = jnp.sum(jnp.where(row == VECTORS, values, 0.0), axis=1)
    laid = dot(last.astype(BF16), spread_out(FF, wide))
    owner = lax.broadcasted_iota(jnp.int32, (RANKS, FF), 0)
    column = lax.broadcasted_iota(jnp.int32, (RANKS, FF), 1)
    laid = jnp.sum(jnp.where(lax.div(column, wide) == owner, laid, 0.0), axis=0, keepdims=True)
    for chunk in range(FF // CHUNK):
        for side in range(2):
            start = side * (FF // 2) + chunk * LANES
            up_ref[chunk, :, side * LANES : (side + 1) * LANES] = laid[:, start : start + LANES]


def lay_table(tables_ref, core, micro, entries):
    count = 2 * LANES
    ranks = PLANES * SPOTS
    values = tables_ref[core].reshape(ranks, tables_ref.shape[3], LANES).astype(F32)
    row = lax.broadcasted_iota(jnp.int32, (1, tables_ref.shape[3], LANES), 1)
    values = jnp.sum(jnp.where(row == micro, values, 0.0), axis=1)
    place = lax.broadcasted_iota(jnp.int32, (LANES, count), 1)
    lane = lax.broadcasted_iota(jnp.int32, (LANES, count), 0)
    start = lax.div(place, entries) * entries
    laid = dot(values.astype(BF16), jnp.where(place - start == lane, 1.0, 0.0).astype(BF16))
    owner = lax.broadcasted_iota(jnp.int32, (ranks, count), 0)
    column = lax.broadcasted_iota(jnp.int32, (ranks, count), 1)
    laid = jnp.sum(jnp.where(lax.div(column, entries) == owner, laid, 0.0), axis=0, keepdims=True)
    column = lax.broadcasted_iota(jnp.int32, (1, count), 1)
    return jnp.where(column < ranks * entries, laid, 2.0 * LANES)


def front_kernel(
    x_in_ref,
    dy_ref,
    vec_ref,
    tab_ref,
    w_qkv_in_ref,
    w_out_in_ref,
    w_up_in_ref,
    w_down_in_ref,
    back_ref,
    far_back_ref,
    x_ref,
    dys_ref,
    w_down_ref,
    w_qkv_hbm,
    w_out_hbm,
    w_up_hbm,
    qk_hbm,
    shared_hbm,
    normed_ref,
    lse_ref,
    vectors_ref,
    up_ref,
    table_ref,
    sorted_ref,
    s_qkv_ref,
    s_ou_ref,
    g_qkv_ref,
    g_ou_ref,
    w_qkv_ref,
    w_out_ref,
    w_up_ref,
    xs_ref,
    vecs_ref,
    tabs_ref,
    bias_ref,
    send_ref,
    qk_ref,
    shared_ref,
    out_ref,
    pack_ref,
    p_ref,
    q_ref,
    picks_ref,
    *sems,
):
    gather_send, gather_recv, gather_local = sems[:3]
    plane_sems, cross_sems = sems[3:7], sems[7:11]
    x_sems, dy_sems = sems[11:14], sems[14:17]
    qkv_send, qkv_recv, qkv_local, shared_send, shared_recv = sems[17:22]
    back_send, back_recv, back_local, far_send, far_recv, local_sem = sems[22:28]
    core, plane, spot = place_here()
    micro, rows, _ = x_in_ref.shape
    tokens = PIECES * rows
    local = rows // BLOCK
    blocks = PLANES * SPOTS * local

    barrier = pltpu.get_barrier_semaphore()
    partners = both_partners(core, plane, spot)
    for partner in partners:
        pl.semaphore_signal(barrier, inc=1, device_id=partner, device_id_type=MESH)

    def natural(ref):
        return lambda tile: ref[:, tile * LANES : (tile + 1) * LANES].astype(F32)

    order = [natural_block(entry) for entry in column_order()]
    read = natural(w_qkv_in_ref)
    fold_tiles(
        s_qkv_ref,
        0,
        list(range(TILES)),
        lambda tile: pair_of_blocks(read, order[2 * tile], order[2 * tile + 1]),
    )
    pl.semaphore_wait(barrier, len(partners))

    gathers = []
    for number, (source, target) in enumerate(
        ((tab_ref, tabs_ref), (vec_ref, vecs_ref), (s_qkv_ref, g_qkv_ref))
    ):
        one = Gather(
            source, target, gather_send.at[number], gather_recv.at[number], gather_local.at[number]
        )
        one.start()
        gathers.append(one)
    outs = D // LANES // 2
    fold_tiles(s_ou_ref, 0, list(range(D // LANES)), natural(w_out_in_ref))
    fold_tiles(s_ou_ref, outs, list(range(FF // LANES)), natural(w_up_in_ref))
    for one in gathers:
        one.column()
    finish_x = to_planes(x_in_ref, xs_ref, *x_sems)
    cross = CrossGather(w_down_in_ref, w_down_ref, *cross_sems)
    for one in gathers:
        one.across()
    for one in gathers:
        one.corner()
    cross.across()
    for one in gathers[:2]:
        one.finish()
    window_core, window_micro = lax.rem(plane, 2), lax.div(plane, 2)
    scalars = pltpu.make_async_copy(tabs_ref.at[window_core], picks_ref, local_sem.at[1])
    scalars.start()
    lay_vectors(vecs_ref, vectors_ref, up_ref)
    for tile in range(TILES):
        halves = []
        for entry in column_order()[2 * tile : 2 * tile + 2]:
            halves.append(entry)

        def bias_tile(number, halves=halves):
            if number < D // LANES:
                return vectors_ref[2:3, number * LANES : (number + 1) * LANES]
            if number < 2 * D // LANES:
                return jnp.zeros((1, LANES), F32)
            start = (number - 2 * D // LANES) * LANES
            return vectors_ref[3:4, start : start + LANES]

        chunk, side = tile % HALF_TILES, tile // HALF_TILES
        start = chunk * CHUNK + side * LANES
        bias_ref[:, start : start + LANES] = pair_of_blocks(
            bias_tile, order[2 * tile], order[2 * tile + 1]
        )
    gathers[2].finish()
    settle(g_qkv_ref, [(tile, w_qkv_ref, alternate(tile)) for tile in range(HALF_TILES)])
    keep_w = pltpu.make_async_copy(w_qkv_ref, w_qkv_hbm, local_sem.at[2])
    keep_w.start()

    finish_x()
    spread = PlaneGather(s_ou_ref, g_ou_ref, *plane_sems)
    keep_x = pltpu.make_async_copy(xs_ref, x_ref, local_sem.at[0])
    keep_x.start()
    normal, _ = norm_parts(xs_ref[...].reshape(tokens, D).astype(F32))
    normed_ref[...] = (normal * vectors_ref[0:1] + vectors_ref[1:2]).astype(BF16)

    def shaped(value):
        return value.astype(BF16).reshape(local, BLOCK, LANES)

    low = low_lanes(rows)
    queries = D // LANES
    for chunk in range(HALF_TILES):
        columns = slice(chunk * CHUNK, (chunk + 1) * CHUNK)
        packed = dot(normed_ref[...], w_qkv_ref[:, columns]) + bias_ref[:, columns]
        for side in range(2):
            tile = chunk + side * HALF_TILES
            whole_tile = packed[:, side * LANES : (side + 1) * LANES]
            if tile < queries:
                whole_tile = whole_tile.astype(BF16).astype(F32) * SCALE
            for piece in range(PIECES):
                part = whole_tile[piece * rows : (piece + 1) * rows]
                if tile < SPOTS:
                    send_ref[0, tile, piece, 0] = shaped(part)
                elif tile < queries:
                    first = 2 * (tile - SPOTS)
                    shared = send_ref[0, first, piece, 0].reshape(rows, LANES).astype(F32)
                    send_ref[1, first, piece, 0] = shaped(jnp.where(low, part, shared))
                    shared = send_ref[0, first + 1, piece, 0].reshape(rows, LANES).astype(F32)
                    send_ref[1, first + 1, piece, 0] = shaped(
                        jnp.where(low, swap_halves(part), shared)
                    )
                else:
                    goal, role = (tile - queries) // 3, (tile - queries) % 3
                    if role < 2:
                        send_ref[role, goal, piece, 1] = shaped(part)
                    else:
                        send_ref[0, goal, piece, 2] = shaped(part)
    sends, keeps = [], []
    for part, (parts, landing) in enumerate(((slice(0, 2), qk_ref), (2, shared_ref))):
        for side in (3, 1, 2, 0):
            for other in (core, 1 - core) if part == 0 else (core,):
                goal = flip(spot, side)
                for piece in range(PIECES):
                    source = send_ref.at[other if part == 0 else 0, goal, piece, parts]
                    target = landing.at[2 * core + piece, spot]
                    if side == 0 and other is core:
                        copy = pltpu.make_async_copy(source, target, qkv_local.at[part, piece])
                        keeps.append((part, copy))
                    else:
                        copy = remote(
                            source,
                            target,
                            qkv_send.at[len(sends)],
                            qkv_recv.at[2 * core + piece, spot, part],
                            (other, rank_of(plane, goal)),
                        )
                        sends.append(copy)
                    copy.start()
    spread.columns()
    cross.blocks()
    table = lay_table(tabs_ref, window_core, window_micro, local * RANDOM)
    table_ref[...] = table.astype(jnp.int32)
    sort_entries(table, sorted_ref, blocks * RANDOM)
    scalars.wait()

    def arrive(part, other, piece, goal):
        target = (qk_ref, shared_ref)[part].at[2 * other + piece, goal]
        remote(
            target,
            target,
            qkv_send.at[0],
            qkv_recv.at[2 * other + piece, goal, part],
            (core, rank_of(plane, spot)),
        ).wait_recv()

    for side in range(SPOTS):
        for other in (core, 1 - core):
            if side > 0 or other is not core:
                for piece in range(PIECES):
                    arrive(0, other, piece, flip(spot, side))
    for part, copy in keeps:
        copy.wait()
    cross.hop(1)

    low = low_lanes(BLOCK)
    masks = [half_mask(True), half_mask(False)]

    def tile_of(component, block):
        rank, number = lax.div(block, local), lax.rem(block, local)
        if component == 2:
            return shared_ref[lax.div(rank, SPOTS), lax.rem(rank, SPOTS), number]
        return qk_ref[lax.div(rank, SPOTS), lax.rem(rank, SPOTS), component, number]

    def picked(block, number):
        rank = lax.div(block, local)
        return picks_ref[
            lax.div(rank, SPOTS),
            lax.rem(rank, SPOTS),
            window_micro,
            lax.rem(block, local) * RANDOM + number,
        ]

    def place_of(block):
        rank = lax.div(block, local)
        return lax.div(rank, SPOTS), lax.rem(rank, SPOTS), lax.rem(block, local)

    def put(block, slot, mixed, log):
        place = place_of(block)
        if slot == 0:
            out_ref[place] = mixed.astype(BF16)
            lse_ref[block] = jnp.where(low, log, 0.0)
        else:
            out_ref[place] = jnp.where(low, mixed, out_ref[place].astype(F32)).astype(BF16)
            lse_ref[block] = jnp.where(low, lse_ref[block], log)

    def one_block(block, slot):
        ids, bias = inner_slots(picked, block, blocks)
        keys = jnp.concatenate([tile_of(1 + slot, number) for number in ids], axis=0)
        scores = dot_rt(tile_of(0, block) * masks[slot], keys) + bias
        top = jnp.max(scores, axis=1, keepdims=True)
        powered = jnp.exp(scores - top)
        total = jnp.sum(powered, axis=1, keepdims=True)
        mixed = dot(powered.astype(BF16), keys) * (1.0 / total)
        return mixed, top + jnp.log(total)

    def rank_blocks(rank, slot):
        results = [one_block(rank * local + number, slot) for number in range(local)]
        for number, (mixed, log) in enumerate(results):
            put(rank * local + number, slot, mixed, log)

    spans = blocks // SPAN
    ends = (0, blocks - 1)

    def dense(slot, scores_ref, numbers):
        size = len(numbers) * BLOCK
        query = jnp.concatenate([tile_of(0, number) * masks[slot] for number in numbers], axis=0)

        def keys_at(span):
            return jnp.concatenate(
                [tile_of(1 + slot, span * SPAN + number) for number in range(SPAN)], axis=0
            )

        def first_pass(span, top):
            scores = dot_rt(query, keys_at(span))
            scores_ref[span] = scores
            return jnp.maximum(top, jnp.max(scores, axis=1, keepdims=True))

        top = lax.fori_loop(
            0, spans, first_pass, jnp.full((size, 1), NEGATIVE, F32), unroll=2
        )

        def second_pass(span, carry):
            total, mixed = carry
            powered = jnp.exp(scores_ref[span] - top)
            return (
                total + jnp.sum(powered, axis=1, keepdims=True),
                mixed + dot(powered.astype(BF16), keys_at(span)),
            )

        total, mixed = lax.fori_loop(
            0,
            spans,
            second_pass,
            (jnp.zeros((size, 1), F32), jnp.zeros((size, LANES), F32)),
            unroll=2,
        )
        mixed = mixed * (1.0 / total)
        log = top + jnp.log(total)
        for place, number in enumerate(numbers):
            span = slice(place * BLOCK, (place + 1) * BLOCK)
            put(number, slot, mixed[span], log[span])

    def head_a(number, carry):
        rank_blocks(number, 0)
        return carry

    def head_b(number, carry):
        rank_blocks(core * (PLANES * SPOTS // 2) + number, 1)
        return carry

    shared = []
    half_way = PLANES * SPOTS // 2
    lax.fori_loop(0, half_way, head_a, 0)
    for side in range(SPOTS):
        goal = flip(spot, side)
        for piece in range(PIECES):
            if side > 0:
                arrive(1, core, piece, goal)
            source = shared_ref.at[2 * core + piece, goal]
            copy = remote(
                source,
                source,
                shared_send.at[2 * side + piece],
                shared_recv.at[2 * core + piece, goal],
                (1 - core, rank_of(plane, spot)),
            )
            copy.start()
            shared.append(copy)
    finish_dy = to_planes(dy_ref, dys_ref, *dy_sems)
    lax.fori_loop(half_way, PLANES * SPOTS, head_a, 0)
    dense(0, p_ref, ends)
    spread.forward()
    backs, stay = [], []
    for side in (3, 1, 2, 0):
        goal = flip(spot, side)
        for piece in range(PIECES):
            pack_halves(
                lambda number, piece=piece, goal=goal: out_ref[
                    2 * (1 - core) + piece, goal, number
                ],
                pack_ref,
                (piece, goal),
                local,
                low,
                1,
            )
            copy = remote(
                pack_ref.at[piece, goal],
                far_back_ref.at[spot, piece],
                far_send.at[piece, side],
                far_recv.at[spot, piece],
                (1 - core, rank_of(plane, goal)),
            )
            copy.start()
            backs.append(copy)
    for side in range(SPOTS):
        for piece in range(PIECES):
            target = shared_ref.at[2 * (1 - core) + piece, flip(spot, side)]
            remote(
                target,
                target,
                shared_send.at[0],
                shared_recv.at[2 * (1 - core) + piece, flip(spot, side)],
                (core, rank_of(plane, spot)),
            ).wait_recv()
    cross.hop(2)
    keep_qk = pltpu.make_async_copy(qk_ref, qk_hbm, local_sem.at[3])
    keep_qk.start()
    keep_shared = pltpu.make_async_copy(shared_ref, shared_hbm, local_sem.at[6])
    keep_shared.start()
    lax.fori_loop(0, half_way, head_b, 0)
    dense(1, q_ref, (core * (blocks - 1),))
    spread.corner()
    for side in (3, 1, 2, 0):
        goal = flip(spot, side)
        for piece in range(PIECES):
            source, target = out_ref.at[2 * core + piece, goal], back_ref.at[spot, piece]
            if side == 0:
                copy = pltpu.make_async_copy(source, target, back_local.at[piece])
                stay.append(copy)
            else:
                copy = remote(
                    source,
                    target,
                    back_send.at[piece, side],
                    back_recv.at[spot, piece],
                    (core, rank_of(plane, goal)),
                )
                backs.append(copy)
            copy.start()
    cross.hop(3)
    spread.finish()
    settle(
        g_ou_ref,
        [(tile, w_out_ref, (tile, outs + tile)) for tile in range(outs)]
        + [(outs + tile, w_up_ref, alternate(tile)) for tile in range(FF // CHUNK)],
    )
    keep_out = pltpu.make_async_copy(w_out_ref, w_out_hbm, local_sem.at[4])
    keep_out.start()
    keep_up = pltpu.make_async_copy(w_up_ref, w_up_hbm, local_sem.at[5])
    keep_up.start()
    cross.finish()
    finish_dy()
    for copy in sends:
        copy.wait_send()
    for copy in shared:
        copy.wait_send()
    for side in range(SPOTS):
        goal = flip(spot, side)
        for piece in range(PIECES):
            here = (core, rank_of(plane, spot))
            if side > 0:
                target = back_ref.at[goal, piece]
                remote(target, target, back_send.at[0, 0], back_recv.at[goal, piece], here).wait_recv()
            target = far_back_ref.at[goal, piece]
            remote(target, target, far_send.at[0, 0], far_recv.at[goal, piece], here).wait_recv()
    for copy in backs:
        copy.wait_send()
    for copy in stay:
        copy.wait()
    for copy in (keep_x, keep_w, keep_qk, keep_shared, keep_out, keep_up):
        copy.wait()


def front(x, dy, vec, tab, w_qkv, w_out, w_up, w_down):
    micro, rows, _ = x.shape
    tokens = PIECES * rows
    local = rows // BLOCK
    blocks = PLANES * SPOTS * local
    spans = blocks // SPAN
    grid = (2, PLANES, SPOTS)
    shard = D // RANKS
    tile = (local, BLOCK, LANES)
    dma = pltpu.SemaphoreType.DMA
    struct = jax.ShapeDtypeStruct
    ou = (2 * shard, (D + FF) // 2)
    return pl.pallas_call(
        front_kernel,
        out_shape=(
            struct((SPOTS, PIECES) + tile, BF16),
            struct((SPOTS, PIECES, local // 2, BLOCK, LANES), BF16),
            struct(x.shape, BF16),
            struct(dy.shape, BF16),
            struct(grid + w_down.shape, BF16),
            struct((D, 3 * D), BF16),
            struct((D, D), BF16),
            struct((D, FF), BF16),
            struct((PLANES, SPOTS, 2) + tile, BF16),
            struct((PLANES, SPOTS) + tile, BF16),
            struct((tokens, D), BF16),
            struct((blocks, BLOCK, LANES), F32),
            struct((VECTORS, D), F32),
            struct((FF // CHUNK, 1, CHUNK), F32),
            struct((1, 2 * LANES), jnp.int32),
            struct((4, 2 * LANES), jnp.int32),
        ),
        in_specs=[
            whole(ANY),
            whole(ANY),
            whole(ANY),
            whole(ANY),
            whole(),
            whole(),
            whole(),
            whole(ANY),
        ],
        out_specs=(whole(ANY),) * 10 + (whole(),) * 6,
        scratch_shapes=[
            VMEM((2 * shard, 3 * D // 2), BF16),
            VMEM(ou, BF16),
            VMEM(grid + (2 * shard, 3 * D // 2), BF16),
            VMEM(grid + ou, BF16),
            VMEM((D, 3 * D), BF16),
            VMEM((D, D), BF16),
            VMEM((D, FF), BF16),
            VMEM((PIECES, rows, D), BF16),
            VMEM(grid + vec.shape, BF16),
            VMEM(grid + tab.shape, jnp.int32),
            VMEM((1, 3 * D), F32),
            VMEM((2, SPOTS, PIECES, 3) + tile, BF16),
            VMEM((PLANES, SPOTS, 2) + tile, BF16),
            VMEM((PLANES, SPOTS) + tile, BF16),
            VMEM((PLANES, SPOTS) + tile, BF16),
            VMEM((PIECES, SPOTS, local // 2, BLOCK, LANES), BF16),
            VMEM((spans, 2 * BLOCK, SPAN * BLOCK), F32),
            VMEM((spans, BLOCK, SPAN * BLOCK), F32),
            pltpu.SMEM((PLANES, SPOTS) + tab.shape, jnp.int32),
            dma((3, Gather.SENDS)),
            dma((3,) + grid),
            dma((3,)),
            dma((PlaneGather.SENDS,)),
            dma((PLANES,)),
            dma((2, SPOTS, 2)),
            dma,
            dma((CrossGather.SENDS,)),
            dma((SPOTS,)),
            dma((2, PLANES)),
            dma,
        ]
        + [dma((2,))] * 6
        + [
            dma((20,)),
            dma((PLANES, SPOTS, 2)),
            dma((2, PIECES)),
            dma((2 * SPOTS,)),
            dma((PLANES, SPOTS)),
            dma((PIECES, SPOTS)),
            dma((SPOTS, PIECES)),
            dma((PIECES,)),
            dma((PIECES, SPOTS)),
            dma((SPOTS, PIECES)),
            dma((7,)),
        ],
        compiler_params=pltpu.CompilerParams(
            vmem_limit_bytes=60 * 1024 * 1024, collective_id=1, has_side_effects=True
        ),
        name="front",
    )(x, dy, vec, tab, w_qkv, w_out, w_up, w_down)


class SpotReduce:
    SEMS = 4

    def __init__(self, source, near, corner, sides, send_sem, recv_sem, rows=None, mine=None):
        self.source, self.near, self.corner, self.side = source, near, corner, sides
        self.send_sem, self.recv_sem, self.rows, self.mine = send_sem, recv_sem, rows, mine
        self.core, self.plane, self.spot = place_here()
        beside, beyond = flip(self.spot, 1), flip(self.spot, 2)
        self.via = beyond * (1 - self.core) + beside * self.core
        self.other = beside * (1 - self.core) + beyond * self.core

    def half(self, core):
        return self.source.at[core] if self.rows else self.source.at[:, core]

    def part(self, spot):
        if self.rows:
            start = pl.multiple_of(spot * self.rows, 16)
            return self.near.at[pl.ds(start, self.rows)]
        return self.near.at[:, :, spot]

    def copy(self, number):
        sibling = (1 - self.core, rank_of(self.plane, self.spot))
        if number == 0:
            source, target, device = self.half(1 - self.core), self.near, sibling
        elif number == 1:
            source, target = self.part(flip(self.spot, 3)), self.corner
            device = (self.core, rank_of(self.plane, self.via))
        else:
            spot = flip(self.spot, number - 1)
            source, target = self.part(spot), self.side.at[number - 2]
            device = (self.core, rank_of(self.plane, spot))
        return remote(source, target, self.send_sem.at[number], self.recv_sem.at[number], device)

    def start(self):
        self.copy(0).start()

    def add(self, spot, terms, target=None):
        if self.rows:
            rows = self.rows

            def slab(number, carry):
                size = rows // 3
                first = pl.multiple_of(spot * rows + number * size, 16)
                place = pl.ds(first, size)
                inner = pl.ds(pl.multiple_of(number * size, 16), size)
                total = self.near[place].astype(F32)
                for read in terms:
                    total = total + read(place, inner).astype(F32)
                if target is None:
                    self.near[place] = total.astype(BF16)
                else:
                    target[inner] = total.astype(BF16)
                return carry

            lax.fori_loop(0, 3, slab, 0, unroll=True)
            return
        count = self.near.shape[0]

        def block(number, carry):
            first, plane = lax.div(number, PLANES), lax.rem(number, PLANES)
            total = self.near[first, plane, spot].astype(F32)
            for read in terms:
                total = total + read(first, plane).astype(F32)
            if target is None:
                self.near[first, plane, spot] = total.astype(BF16)
            else:
                target[first, plane] = total.astype(BF16)
            return carry

        lax.fori_loop(0, count * PLANES, block, 0, unroll=4)

    def corners(self):
        self.copy(0).wait_recv()
        core = self.core
        for spot in range(SPOTS):
            if self.rows and self.mine is None:
                self.add(spot, [lambda place, inner: self.source[core, place]])
            elif self.rows:
                self.add(spot, [lambda place, inner: self.mine[place]])
            elif self.mine is None:
                self.add(spot, [lambda first, plane, spot=spot: self.source[first, core, plane, spot]])
            else:
                self.add(spot, [lambda first, plane, spot=spot: self.mine[first, plane, spot]])
        self.copy(1).start()

    def sides(self):
        self.copy(1).wait_recv()
        if self.rows:
            self.add(self.other, [lambda place, inner: self.corner[inner]])
        else:
            self.add(self.other, [lambda first, plane: self.corner[first, plane]])
        self.copy(2).start()
        self.copy(3).start()

    def close(self, target):
        self.copy(2).wait_recv()
        self.copy(3).wait_recv()
        if self.rows:
            terms = [lambda place, inner, n=n: self.side[n, inner] for n in range(2)]
        else:
            terms = [lambda first, plane, n=n: self.side[n, first, plane] for n in range(2)]
        self.add(self.spot, terms, target)
        for number in range(self.SEMS):
            self.copy(number).wait_send()


def block_scratch(count, rows, width):
    return [
        VMEM((count, PLANES, SPOTS, rows, width), BF16),
        VMEM((count, PLANES, rows, width), BF16),
        VMEM((2, count, PLANES, rows, width), BF16),
    ]


def row_scratch(rows, width):
    return [
        VMEM((SPOTS * rows, width), BF16),
        VMEM((rows, width), BF16),
        VMEM((2, rows, width), BF16),
    ]


STAGES = 4
PER_STAGE = FF // CHUNK // STAGES
EARLY = 2
LATE = STAGES - EARLY
WAITS = (2, 4, 6)


def by_owner(out_ref, values):
    rows = D // RANKS
    width = values.shape[1] // 2
    for owner in range(RANKS):
        part = values[owner * rows : (owner + 1) * rows]
        out_ref[owner] = jnp.concatenate([part[:, :width], part[:, width:]], axis=0).astype(BF16)


def plane_middle_kernel(
    mixed_in_ref,
    far_in_ref,
    x_ref,
    dy_ref,
    vec_ref,
    w_out_ref,
    up_shift_ref,
    w_up_ref,
    w_down_ref,
    hidden_ref,
    send_ref,
    far_ref,
    dres_ref,
    g_out_ref,
    half_up_ref,
    half_down_ref,
    last_up_ref,
    last_down_ref,
    g_up_bias_ref,
    g_small_ref,
    mixed_ref,
    residual_ref,
    second_ref,
    second_t_ref,
    total_ref,
    dsecond_ref,
    g_up_ref,
    g_down_ref,
    *scratch,
):
    send_sem, recv_sem, local_sem = scratch[-3:]
    stages = []
    for number in range(EARLY):
        buffers = scratch[6 * number : 6 * number + 6]
        stages.append(
            (
                SpotReduce(
                    g_up_ref.at[PER_STAGE * number : PER_STAGE * (number + 1)],
                    *buffers[:3],
                    send_sem.at[number, 0],
                    recv_sem.at[number, 0],
                ),
                SpotReduce(
                    g_down_ref.at[number],
                    *buffers[3:],
                    send_sem.at[number, 1],
                    recv_sem.at[number, 1],
                    rows=FF // RANKS,
                ),
            )
        )
    pieces, rows, _ = x_ref.shape
    tokens = pieces * rows
    step = pl.program_id(0)
    low = low_lanes(rows)
    out_shift, gain, shift, down_shift = (vec_ref[number : number + 1] for number in (4, 5, 6, 7))

    @pl.when(step == 0)
    def _():
        core, plane, spot = place_here()
        greet(
            [
                (1 - core, rank_of(plane, spot)),
                (core, rank_of(plane, flip(spot, 1))),
                (core, rank_of(plane, flip(spot, 2))),
            ]
        )
        def received(spot, piece):
            own = mixed_in_ref[spot, piece].astype(F32)
            halves = far_in_ref[spot, piece].astype(F32)
            parts = []
            for number in range(rows // BLOCK // 2):
                part = halves[number * BLOCK : (number + 1) * BLOCK]
                parts += [part, swap_halves(part)]
            other = jnp.concatenate(parts, axis=0)
            return (jnp.where(core == 0, own, other), jnp.where(core == 0, other, own)), own

        for piece in range(pieces):
            span = slice(piece * rows, (piece + 1) * rows)
            for spot in (0, 2):
                first, own_first = received(spot, piece)
                last_two, own_last = received(spot + 1, piece)
                tiles = (
                    jnp.where(low, swap_halves(first[0]), first[1]),
                    jnp.where(low, own_first, last_two[0]),
                    swap_halves(jnp.where(low, own_last, last_two[1])),
                )
                for number, tile in enumerate(tiles):
                    spread = 3 * (spot // 2) + number
                    mixed_ref[span, spread * LANES : (spread + 1) * LANES] = tile.astype(BF16)
        residual = x_ref[...].reshape(tokens, D).astype(F32) + (
            dot(mixed_ref[...], w_out_ref[...]) + out_shift
        )
        residual_ref[...] = residual
        normal, _ = norm_parts(residual)
        second = normal * gain + shift
        second_ref[...] = second.astype(BF16)
        second_t_ref[...] = second.T.astype(BF16)
        total_ref[...] = jnp.zeros_like(total_ref)
        dsecond_ref[...] = jnp.zeros_like(dsecond_ref)

    w_down = w_down_ref[...].reshape(CHUNK, D)
    upper = dot(second_ref[...], w_up_ref[...]) + up_shift_ref[0]
    factor = 0.7978845608028654
    square = upper * upper
    bent = jnp.tanh(factor * (upper + 0.044715 * (upper * square)))
    middle_half = 0.5 * (1.0 + bent)
    active = (upper * middle_half).astype(BF16)
    slope = middle_half + 0.5 * upper * (1.0 - bent * bent) * (
        factor + (3.0 * 0.044715 * factor) * square
    )
    dy = dy_ref[...]
    total_ref[...] += dot(active, w_down)
    stage, turn = lax.div(step, PER_STAGE), lax.rem(step, PER_STAGE)
    down_share = dot_lt(active, dy).astype(BF16)
    place = pl.ds(pl.multiple_of(turn * LANES, LANES), LANES)
    for side in range(2):
        g_down_ref[stage, side, place] = down_share[side * LANES : (side + 1) * LANES]
    dupper = (dot_rt(dy, w_down) * slope).astype(BF16)
    g_up_bias_ref[0] = jnp.sum(dupper.astype(F32), axis=0, keepdims=True)
    up_share = dot(second_t_ref[...], dupper)
    shard = D // RANKS
    for owner in range(RANKS):
        part = up_share[owner * shard : (owner + 1) * shard]
        g_up_ref[step, owner // (PLANES * SPOTS), owner // SPOTS % PLANES, owner % SPOTS] = (
            jnp.concatenate([part[:, :LANES], part[:, LANES:]], axis=0).astype(BF16)
        )
    dsecond_ref[...] += dot_rt(dupper, w_up_ref[...])

    last = FF // CHUNK - 1
    for number, pair in enumerate(stages):
        done = PER_STAGE * (number + 1) - 1

        @pl.when(step == done)
        def _(pair=pair):
            for one in pair:
                one.start()

        @pl.when(step == done + WAITS[0])
        def _(pair=pair):
            for one in pair:
                one.corners()

        @pl.when(step == done + WAITS[1])
        def _(pair=pair):
            for one in pair:
                one.sides()

        if done + WAITS[2] < last:

            @pl.when(step == done + WAITS[2])
            def _(pair=pair, number=number):
                pair[0].close(half_up_ref.at[PER_STAGE * number : PER_STAGE * (number + 1)])
                pair[1].close(half_down_ref.at[number])

    @pl.when(step == last)
    def _():
        keep_up = pltpu.make_async_copy(
            g_up_ref.at[PER_STAGE * EARLY : PER_STAGE * STAGES], last_up_ref, local_sem.at[0]
        )
        keep_up.start()
        keep_down = pltpu.make_async_copy(
            g_down_ref.at[EARLY:STAGES], last_down_ref, local_sem.at[1]
        )
        keep_down.start()
        residual = residual_ref[...]
        hidden_ref[...] = (
            (residual + (total_ref[...] + down_shift)).astype(BF16).reshape(x_ref.shape)
        )
        normal, inverse = norm_parts(residual)
        dsecond = dsecond_ref[...]
        grad_out = dy_ref[...].astype(F32)
        g_small_ref[0:1] = jnp.sum(dsecond * normal, axis=0, keepdims=True)
        g_small_ref[1:2] = jnp.sum(dsecond, axis=0, keepdims=True)
        g_small_ref[2:3] = jnp.sum(grad_out, axis=0, keepdims=True)
        dres = grad_out + norm_pull(dsecond, normal, inverse, gain)
        dres_ref[...] = dres
        branch = dres.astype(BF16)
        g_small_ref[3:4] = jnp.sum(branch.astype(F32), axis=0, keepdims=True)
        by_owner(g_out_ref, dot_lt(mixed_ref[...], branch))
        dmixed = dot_rt(branch, w_out_ref[...])
        core = lax.axis_index("gx")

        def hand_over(spot, piece, first, second):
            send_ref[spot, piece] = jnp.where(core == 0, first, second).astype(BF16)
            far = jnp.where(core == 0, second, first)
            for number in range(rows // BLOCK // 2):
                start = 2 * number * BLOCK
                far_ref[spot, piece, number * BLOCK : (number + 1) * BLOCK] = jnp.where(
                    low_lanes(BLOCK),
                    swap_halves(far[start + BLOCK : start + 2 * BLOCK]),
                    far[start : start + BLOCK],
                ).astype(BF16)

        for piece in range(pieces):
            span = slice(piece * rows, (piece + 1) * rows)
            for spot in (0, 2):
                tiles = [
                    dmixed[span, number * LANES : (number + 1) * LANES]
                    for number in range(3 * (spot // 2), 3 * (spot // 2) + 3)
                ]
                flipped = [swap_halves(tile) for tile in tiles]
                hand_over(
                    spot,
                    piece,
                    jnp.where(low, tiles[1], flipped[0]),
                    jnp.where(low, tiles[1], tiles[0]),
                )
                hand_over(
                    spot + 1, piece, jnp.where(low, flipped[2], tiles[1]), flipped[2]
                )
        for number, pair in enumerate(stages):
            if PER_STAGE * (number + 1) - 1 + WAITS[2] >= last:
                pair[0].close(half_up_ref.at[PER_STAGE * number : PER_STAGE * (number + 1)])
                pair[1].close(half_down_ref.at[number])
        keep_up.wait()
        keep_down.wait()


def plane_middle(mixed_in, far_in, x, dy, vec, w_out, up_shift, w_up, w_down):
    pieces, rows, _ = x.shape
    tokens = pieces * rows
    shard = D // RANKS

    def fixed(shape):
        return pl.BlockSpec(shape, lambda step: (0,) * len(shape))

    steps = FF // CHUNK
    grid = (2, PLANES, SPOTS)
    down_rows = FF // RANKS
    half_up = (PER_STAGE * EARLY, PLANES, 2 * shard, LANES)
    half_down = (EARLY, down_rows, D)
    buffers = []
    for _ in range(EARLY):
        buffers += block_scratch(PER_STAGE, 2 * shard, LANES) + row_scratch(down_rows, D)
    down = pl.BlockSpec((2, LANES, D), lambda step: (0, step, 0))
    return pl.pallas_call(
        plane_middle_kernel,
        grid=(steps,),
        out_shape=(
            jax.ShapeDtypeStruct(x.shape, BF16),
            jax.ShapeDtypeStruct(mixed_in.shape, BF16),
            jax.ShapeDtypeStruct(far_in.shape, BF16),
            jax.ShapeDtypeStruct((tokens, D), F32),
            jax.ShapeDtypeStruct((RANKS, 2 * shard, D // 2), BF16),
            jax.ShapeDtypeStruct(half_up, BF16),
            jax.ShapeDtypeStruct(half_down, BF16),
            jax.ShapeDtypeStruct((PER_STAGE * LATE,) + grid + (2 * shard, LANES), BF16),
            jax.ShapeDtypeStruct((LATE, 2, FF // 2 // STAGES, D), BF16),
            jax.ShapeDtypeStruct((steps, 1, CHUNK), F32),
            jax.ShapeDtypeStruct((4, D), F32),
        ),
        in_specs=[
            fixed(mixed_in.shape),
            fixed(far_in.shape),
            fixed(x.shape),
            fixed((tokens, D)),
            fixed(vec.shape),
            fixed((D, D)),
            pl.BlockSpec((1, 1, CHUNK), lambda step: (step, 0, 0)),
            pl.BlockSpec((D, CHUNK), lambda step: (0, step)),
            down,
        ],
        out_specs=(
            fixed(x.shape),
            fixed(mixed_in.shape),
            fixed(far_in.shape),
            fixed((tokens, D)),
            fixed((RANKS, 2 * shard, D // 2)),
            fixed(half_up),
            fixed(half_down),
            whole(ANY),
            whole(ANY),
            pl.BlockSpec((1, 1, CHUNK), lambda step: (step, 0, 0)),
            fixed((4, D)),
        ),
        scratch_shapes=[
            VMEM((tokens, D), BF16),
            VMEM((tokens, D), F32),
            VMEM((tokens, D), BF16),
            VMEM((D, tokens), BF16),
            VMEM((tokens, D), F32),
            VMEM((tokens, D), F32),
            VMEM((steps,) + grid + (2 * shard, LANES), BF16),
            VMEM((STAGES, 2, FF // 2 // STAGES, D), BF16),
        ]
        + buffers
        + [
            pltpu.SemaphoreType.DMA((EARLY, 2, SpotReduce.SEMS)),
            pltpu.SemaphoreType.DMA((EARLY, 2, SpotReduce.SEMS)),
            pltpu.SemaphoreType.DMA((2,)),
        ],
        compiler_params=pltpu.CompilerParams(
            vmem_limit_bytes=60 * 1024 * 1024, collective_id=3, has_side_effects=True
        ),
        name="plane_middle",
    )(mixed_in, far_in, x, dy, vec, w_out, up_shift, w_up, w_down)


class Reduce:
    SENDS = 4 + 2 + 2 + 3
    RECVS = SENDS

    def __init__(self, source, total, near, corner_x, corner_y, side_x, side_y, far, out, sems):
        self.source, self.total, self.near = source, total, near
        self.corner = {1: corner_x, 2: corner_y}
        self.side = {1: side_x, 2: side_y}
        self.far, self.out = far, out
        self.send_sem, self.recv_sem, self.local_sem = sems
        self.core, self.plane, self.spot = place_here()
        self.copies = []
        self.locals = []

    def start(self):
        sibling = (1 - self.core, rank_of(self.plane, self.spot))
        for number, side in enumerate((3, 1, 2, 0)):
            spot = flip(self.spot, side)
            copy = remote(
                self.source.at[1 - self.core, :, spot],
                self.near.at[:, spot],
                self.send_sem.at[number],
                self.recv_sem.at[number],
                sibling,
            )
            copy.start()
            self.copies.append(copy)
            keep = pltpu.make_async_copy(
                self.source.at[self.core, :, spot],
                self.total.at[:, spot],
                self.local_sem.at[number],
            )
            keep.start()
            self.locals.append(keep)

    def take(self, number, side):
        self.copies[number].wait_recv()
        self.locals[number].wait()
        spot = flip(self.spot, side)

        def add(plane, carry):
            self.total[plane, spot] = (
                self.total[plane, spot].astype(F32) + self.near[plane, spot].astype(F32)
            ).astype(self.total.dtype)
            return carry

        lax.fori_loop(0, PLANES, add, 0, unroll=True)

    def corners(self):
        self.take(0, 3)
        spot = flip(self.spot, 3)
        index = 4
        self.corner_copies = []
        for bits in range(PLANES):
            side = 2 if bits < 2 else 1
            self.corner_copies.append(None)
            plane = flip(self.plane, bits)
            copy = remote(
                self.total.at[plane, spot],
                self.corner[side].at[bits % 2],
                self.send_sem.at[index + bits],
                self.recv_sem.at[index + bits],
                (self.core, rank_of(self.plane, flip(self.spot, side))),
            )
            copy.start()
            self.corner_copies[bits] = copy

    def sides(self):
        self.take(1, 1)
        self.take(2, 2)
        self.side_copies = {}
        for side in (1, 2):
            spot = flip(self.spot, side)
            came = 3 - side
            for bits in (0, 1) if came == 2 else (2, 3):
                self.corner_copies[bits].wait_recv()
                plane = flip(self.plane, bits)
                self.total[plane, spot] = (
                    self.total[plane, spot].astype(F32)
                    + self.corner[came][bits % 2].astype(F32)
                ).astype(self.total.dtype)
            copy = remote(
                self.total.at[:, spot],
                self.side[side],
                self.send_sem.at[7 + side],
                self.recv_sem.at[7 + side],
                (self.core, rank_of(self.plane, spot)),
            )
            copy.start()
            self.side_copies[side] = copy

    def columns(self):
        self.take(3, 0)
        for side in (1, 2):
            self.side_copies[side].wait_recv()

        def add(plane, carry):
            self.total[plane, self.spot] = (
                self.total[plane, self.spot].astype(F32)
                + self.side[1][plane].astype(F32)
                + self.side[2][plane].astype(F32)
            ).astype(self.total.dtype)
            return carry

        lax.fori_loop(0, PLANES, add, 0, unroll=True)
        self.far_copies = []
        for bits in range(1, PLANES):
            plane = flip(self.plane, bits)
            copy = remote(
                self.total.at[plane, self.spot],
                self.far.at[bits - 1],
                self.send_sem.at[9 + bits],
                self.recv_sem.at[9 + bits],
                (self.core, rank_of(plane, self.spot)),
            )
            copy.start()
            self.far_copies.append(copy)

    def finish(self):
        value = self.total[self.plane, self.spot].astype(F32)
        for bits in range(1, PLANES):
            self.far_copies[bits - 1].wait_recv()
            value = value + self.far[bits - 1].astype(F32)
        self.out[...] = value
        for copy in self.copies + self.corner_copies + self.far_copies:
            copy.wait_send()
        for side in (1, 2):
            self.side_copies[side].wait_send()


REDUCE_SEMS = 13


def reduce_scratch(shape, kind):
    tail = shape[3:]
    return [
        VMEM((PLANES, SPOTS) + tail, kind),
        VMEM((PLANES, SPOTS) + tail, kind),
        VMEM((2,) + tail, kind),
        VMEM((2,) + tail, kind),
        VMEM((PLANES,) + tail, kind),
        VMEM((PLANES,) + tail, kind),
        VMEM((PLANES - 1,) + tail, kind),
    ]


class Doubling:
    STEPS = 5

    def __init__(self, totals, boxes, send_sem, recv_sem):
        self.totals, self.boxes = totals, boxes
        self.send_sem, self.recv_sem = send_sem, recv_sem
        core, plane, spot = place_here()
        self.partners = (
            (1 - core, rank_of(plane, spot)),
            (core, rank_of(plane, flip(spot, 1))),
            (core, rank_of(plane, flip(spot, 2))),
            (core, rank_of(flip(plane, 1), spot)),
            (core, rank_of(flip(plane, 2), spot)),
        )
        self.copies = []

    def start(self, step):
        self.copies = []
        for number, (total, box) in enumerate(zip(self.totals, self.boxes)):
            copy = remote(
                total,
                box.at[step],
                self.send_sem.at[step, number],
                self.recv_sem.at[step, number],
                self.partners[step],
            )
            copy.start()
            self.copies.append(copy)

    def finish(self, step):
        for copy, total, box in zip(self.copies, self.totals, self.boxes):
            copy.wait()
            total[...] += box[step]


PARTS = 3


def finish_kernel(
    recv_ref,
    far_ref,
    normed_ref,
    x_ref,
    dres_hbm,
    vec_ref,
    w_hbm,
    g_mid_ref,
    g_up_bias_ref,
    grad_ref,
    g_qkv_ref,
    rows_out_ref,
    tiles_out_ref,
    *scratch,
):
    sources, scratch = scratch[:PARTS], scratch[PARTS:]
    buffers, scratch = scratch[: 7 * PARTS], scratch[7 * PARTS :]
    packed_ref, dnormed_ref, gradient_ref, dres_ref, w_ref = scratch[:5]
    rows_ref, tiles_ref, rows_box, tiles_box = scratch[5:9]
    send_sem, recv_sem, local_sem, load_sem, sum_send, sum_recv = scratch[9:15]
    move_sems = scratch[15:18]
    pieces, rows, _ = x_ref.shape
    tokens = pieces * rows
    core, plane, spot = place_here()
    low = low_lanes(rows)

    load_w = pltpu.make_async_copy(w_hbm, w_ref, load_sem.at[0])
    load_dres = pltpu.make_async_copy(dres_hbm, dres_ref, load_sem.at[1])
    load_w.start()
    load_dres.start()
    greet(all_partners(core, plane, spot))

    def put(tile, piece, value):
        side, chunk = tile // HALF_TILES, tile % HALF_TILES
        packed_ref[
            piece * rows : (piece + 1) * rows,
            chunk * CHUNK + side * LANES : chunk * CHUNK + (side + 1) * LANES,
        ] = value.astype(BF16)

    start_piece, finish_grad = from_planes(gradient_ref, grad_ref, *move_sems, later=True)
    for piece in range(pieces):
        seconds = []
        for goal in range(SPOTS):
            own = recv_ref[core, goal, piece, QUERIES].astype(F32)
            halves = far_ref[goal, piece].astype(F32)
            parts = []
            for number in range(rows // BLOCK // 2):
                part = halves[number * BLOCK : (number + 1) * BLOCK]
                parts += [part, swap_halves(part)]
            other = jnp.concatenate(parts, axis=0)
            second = jnp.where(core == 0, other, own)
            put(goal, piece, jnp.where(low & (core == 1), other, own))
            seconds.append(second)
            base = D // LANES + 3 * goal
            put(base, piece, recv_ref[0, goal, piece, KEYS_A])
            put(base + 1, piece, recv_ref[1, goal, piece, KEYS_A])
            put(base + 2, piece, recv_ref[core, goal, piece, KEYS_B])
        for number in range(2):
            put(
                SPOTS + number,
                piece,
                jnp.where(low, seconds[2 * number], swap_halves(seconds[2 * number + 1])),
            )
        if piece == 0:
            load_w.wait()
            load_dres.wait()
        span = slice(piece * rows, (piece + 1) * rows)
        share = dot_rt(packed_ref[span], w_ref[...])
        dnormed_ref[span] = share
        normal, inverse = norm_parts(x_ref[piece].astype(F32))
        gradient = dres_ref[span] + norm_pull(share, normal, inverse, vec_ref[0:1])
        gradient_ref[piece] = gradient.astype(BF16)
        start_piece(piece)
        sums = [
            jnp.sum(share * normal, axis=0, keepdims=True),
            jnp.sum(share, axis=0, keepdims=True),
        ]
        for number in range(2):
            if piece == 0:
                rows_ref[number : number + 1] = sums[number]
            else:
                rows_ref[number : number + 1] += sums[number]

    rows_ref[2:6] = g_mid_ref[...]
    rows_ref[6:8] = jnp.zeros((2, D), F32)
    tiles_ref[...] = jnp.zeros_like(tiles_ref)
    for step in range(FF // CHUNK):
        tiles_ref[step : step + 1] = g_up_bias_ref[step]
    for chunk in range(HALF_TILES):
        number = FF // CHUNK + chunk
        tiles_ref[number : number + 1] = jnp.sum(
            packed_ref[:, chunk * CHUNK : (chunk + 1) * CHUNK].astype(F32), axis=0, keepdims=True
        )
    sums = Doubling((rows_ref, tiles_ref), (rows_box, tiles_box), sum_send, sum_recv)
    sums.start(0)

    width = HALF_TILES // PARTS * LANES
    reduces = [
        Reduce(
            sources[part],
            *buffers[7 * part : 7 * part + 7],
            g_qkv_ref.at[:, part * width : (part + 1) * width],
            (send_sem.at[part], recv_sem.at[part], local_sem.at[part]),
        )
        for part in range(PARTS)
    ]
    shard = D // RANKS
    normed_t = normed_ref[...].astype(F32).T.astype(BF16)
    for part in range(PARTS):
        for number in range(HALF_TILES // PARTS):
            chunk = part * (HALF_TILES // PARTS) + number
            values = dot(normed_t, packed_ref[:, chunk * CHUNK : (chunk + 1) * CHUNK])
            columns = slice(number * LANES, (number + 1) * LANES)
            for owner in range(RANKS):
                mine = values[owner * shard : (owner + 1) * shard]
                sources[part][
                    owner // (PLANES * SPOTS), owner // SPOTS % PLANES, owner % SPOTS, :, columns
                ] = jnp.concatenate([mine[:, :LANES], mine[:, LANES:]], axis=0).astype(BF16)
        reduces[part].start()
        if part > 0:
            reduces[part - 1].corners()
        if part > 1:
            reduces[part - 2].sides()
    sums.finish(0)
    sums.start(1)
    reduces[2].corners()
    reduces[1].sides()
    sums.finish(1)
    sums.start(2)
    reduces[0].columns()
    reduces[2].sides()
    sums.finish(2)
    sums.start(3)
    reduces[1].columns()
    sums.finish(3)
    sums.start(4)
    reduces[2].columns()
    sums.finish(4)
    for one in reduces:
        one.finish()
    rows_out_ref[...] = rows_ref[...]
    tiles_out_ref[...] = tiles_ref[...]
    finish_grad()


def finish_layer(recv, far, normed, x, dres, vec, w, g_mid, g_up_bias):
    pieces, rows, _ = x.shape
    tokens = pieces * rows
    shard = D // RANKS
    grid = (2, PLANES, SPOTS)
    part = grid + (2 * shard, HALF_TILES // PARTS * LANES)
    buffers = []
    for _ in range(PARTS):
        buffers += reduce_scratch(part, BF16)
    tiles = -(-(FF // CHUNK + HALF_TILES) // 8) * 8
    dma = pltpu.SemaphoreType.DMA
    return pl.pallas_call(
        finish_kernel,
        out_shape=(
            jax.ShapeDtypeStruct(x.shape, BF16),
            jax.ShapeDtypeStruct((2 * shard, 3 * D // 2), F32),
            jax.ShapeDtypeStruct((8, D), F32),
            jax.ShapeDtypeStruct((tiles, CHUNK), F32),
        ),
        in_specs=[
            whole(),
            whole(),
            whole(),
            whole(),
            whole(ANY),
            whole(),
            whole(ANY),
            whole(),
            whole(),
        ],
        out_specs=(whole(ANY), whole(), whole(), whole()),
        scratch_shapes=[VMEM(part, BF16)] * PARTS
        + buffers
        + [
            VMEM((tokens, 3 * D), BF16),
            VMEM((tokens, D), F32),
            VMEM(x.shape, BF16),
            VMEM((tokens, D), F32),
            VMEM(w.shape, BF16),
            VMEM((8, D), F32),
            VMEM((tiles, CHUNK), F32),
            VMEM((Doubling.STEPS, 8, D), F32),
            VMEM((Doubling.STEPS, tiles, CHUNK), F32),
            dma((PARTS, REDUCE_SEMS)),
            dma((PARTS, REDUCE_SEMS)),
            dma((PARTS, 4)),
            dma((2,)),
            dma((Doubling.STEPS, 2)),
            dma((Doubling.STEPS, 2)),
            dma((2,)),
            dma((2,)),
            dma((2,)),
        ],
        compiler_params=pltpu.CompilerParams(
            vmem_limit_bytes=60 * 1024 * 1024, collective_id=2, has_side_effects=True
        ),
        name="finish_layer",
    )(recv, far, normed, x, dres, vec, w, g_mid, g_up_bias)


def present_kernel(
    hidden_hbm,
    grad_hbm,
    t_qkv_hbm,
    t_out_hbm,
    t_up_hbm,
    t_down_hbm,
    rows_hbm,
    tiles_hbm,
    hidden_out_ref,
    grad_out_ref,
    g_qkv_ref,
    g_out_ref,
    g_up_ref,
    g_down_ref,
    *outs,
):
    singles, (grad_ref, t_qkv_ref, t_out_ref, t_up_ref, rows_ref, tiles_ref, copy_sem) = (
        outs[:-7],
        outs[-7:],
    )
    loads = [
        pltpu.make_async_copy(source, target, copy_sem.at[number])
        for number, (source, target) in enumerate(
            (
                (rows_hbm, rows_ref),
                (tiles_hbm, tiles_ref),
                (t_qkv_hbm, t_qkv_ref),
                (t_out_hbm, t_out_ref),
                (t_up_hbm, t_up_ref),
                (grad_hbm, grad_ref),
                (t_down_hbm, g_down_ref),
                (hidden_hbm, hidden_out_ref),
            )
        )
    ]
    for copy in loads:
        copy.start()
    core, plane, spot = place_here()
    mine = core * (PLANES * SPOTS) + rank_of(plane, spot)
    own, wide = D // RANKS, FF // RANKS
    order = [natural_block(entry) for entry in column_order()]
    inverse = [order.index(number) for number in range(len(order))]

    for copy in loads[:5]:
        copy.wait()
    half = D // 2
    for side in range(2):
        rows = slice(side * own, (side + 1) * own)
        g_out_ref[:, side * half : (side + 1) * half] = t_out_ref[rows]
        for chunk in range(FF // CHUNK):
            start = side * (FF // 2) + chunk * LANES
            g_up_ref[:, start : start + LANES] = t_up_ref[chunk, rows]

    def folded(tile):
        side, chunk = tile // HALF_TILES, tile % HALF_TILES
        return t_qkv_ref[
            side * own : (side + 1) * own, chunk * LANES : (chunk + 1) * LANES
        ]

    def bias_sum(tile):
        side, chunk = tile // HALF_TILES, tile % HALF_TILES
        row = FF // CHUNK + chunk
        return tiles_ref[row : row + 1, side * LANES : (side + 1) * LANES]

    biases = []
    for tile in range(TILES):
        blocks = inverse[2 * tile], inverse[2 * tile + 1]
        g_qkv_ref[:, tile * LANES : (tile + 1) * LANES] = pair_of_blocks(folded, *blocks)
        biases.append(pair_of_blocks(bias_sum, *blocks))
    third = TILES // 3
    query = jnp.concatenate(biases[:third], axis=1)
    value = jnp.concatenate(biases[2 * third :], axis=1)
    vectors = jnp.concatenate([rows_ref[0:6], query, value], axis=0)

    def pick(values, first, wanted):
        place = lax.broadcasted_iota(jnp.int32, (values.shape[1], LANES), 0) + first
        lane = lax.broadcasted_iota(jnp.int32, (values.shape[1], LANES), 1)
        one_hot = jnp.where(place == mine * wanted + lane, 1.0, 0.0)
        return lax.dot_general(
            values,
            one_hot,
            (((1,), (0,)), ((), ())),
            precision=lax.Precision.HIGHEST,
            preferred_element_type=F32,
        )

    picked = pick(vectors, 0, own)
    for number in range(VECTORS):
        singles[number][...] = picked[number : number + 1, :own]
    total = jnp.zeros((1, LANES), F32)
    for chunk in range(FF // CHUNK):
        for side in range(2):
            total = total + pick(
                tiles_ref[chunk : chunk + 1, side * LANES : (side + 1) * LANES],
                side * (FF // 2) + chunk * LANES,
                wide,
            )
    singles[VECTORS][...] = total[:, :wide]
    loads[5].wait()
    grad_out_ref[...] = grad_ref[...].astype(F32)
    for copy in loads[6:]:
        copy.wait()


def present(hidden, grad, t_qkv, t_out, t_up, t_down, rows, tiles):
    own, wide = D // RANKS, FF // RANKS
    struct = jax.ShapeDtypeStruct
    return pl.pallas_call(
        present_kernel,
        out_shape=(
            struct(hidden.shape, BF16),
            struct(grad.shape, F32),
            struct((own, 3 * D), F32),
            struct((own, D), F32),
            struct((own, FF), F32),
            struct((wide, D), F32),
        )
        + (struct((1, own), F32),) * VECTORS
        + (struct((1, wide), F32),),
        in_specs=[whole(ANY)] * 8,
        out_specs=(whole(),) * (7 + VECTORS),
        scratch_shapes=[
            VMEM(item.shape, item.dtype) for item in (grad, t_qkv, t_out, t_up, rows, tiles)
        ]
        + [pltpu.SemaphoreType.DMA((8,))],
        compiler_params=params_of(63),
        name="present",
    )(hidden, grad, t_qkv, t_out, t_up, t_down, rows, tiles)


def plane_shards(
    hidden_in,
    rand_table,
    norm1_gain,
    norm1_bias,
    w_qkv,
    query_bias,
    value_bias,
    w_out,
    out_bias,
    norm2_gain,
    norm2_bias,
    w_up,
    up_bias,
    w_down,
    down_bias,
    cotangent,
):
    micro, rows, _ = hidden_in.shape
    local = rows // BLOCK

    def in_row(vector, number):
        return jnp.pad(vector[None], ((number, 15 - number), (0, LANES - vector.shape[0])))

    vec = functools.reduce(
        jnp.add,
        [
            in_row(vector, number)
            for number, vector in enumerate(
                (
                    norm1_gain,
                    norm1_bias,
                    query_bias,
                    value_bias,
                    out_bias,
                    norm2_gain,
                    norm2_bias,
                    down_bias,
                    up_bias,
                )
            )
        ],
    )
    tab = jnp.pad(
        rand_table.reshape(micro, local * RANDOM), ((0, 8 - micro), (0, LANES - local * RANDOM))
    )
    (
        mixed,
        far_mixed,
        x,
        dy,
        w_down_all,
        w_qkv_all,
        w_out_all,
        w_up_all,
        qk,
        shared,
        normed,
        lse,
        vectors,
        up_shift,
        table,
        sorted_table,
    ) = front(hidden_in, cotangent, vec, tab, w_qkv, w_out, w_up, w_down)
    mixed = mixed.reshape(SPOTS, PIECES, rows, LANES)
    far_mixed = far_mixed.reshape(SPOTS, PIECES, rows // 2, LANES)
    (
        hidden,
        near_grad,
        far_grad,
        dres,
        g_out,
        half_up,
        half_down,
        last_up,
        last_down,
        g_up_bias,
        g_mid,
    ) = plane_middle(
        mixed,
        far_mixed,
        x,
        dy.reshape(micro * rows, D),
        vectors,
        w_out_all,
        up_shift,
        w_up_all,
        w_down_all.reshape(2, FF // 2, D),
    )
    grid = (2, PLANES, SPOTS)
    dqkv, far_dq, hidden_out, t_out, t_up, t_down = plane_attention_back(
        table,
        sorted_table,
        qk,
        shared,
        near_grad.reshape(SPOTS, PIECES, local, BLOCK, LANES),
        far_grad.reshape(SPOTS, PIECES, local // 2, BLOCK, LANES),
        lse,
        hidden,
        [
            g_out.reshape((1,) + grid + g_out.shape[1:]),
            last_up,
            last_down,
        ],
        half_up,
        half_down,
    )
    dqkv = dqkv.reshape(2, SPOTS, PIECES, 3, rows, LANES)
    far_dq = far_dq.reshape(SPOTS, PIECES, rows // 2, LANES)
    grad_hidden, t_qkv, sum_rows, sum_tiles = finish_layer(
        dqkv, far_dq, normed, x, dres, vectors, w_qkv_all, g_mid, g_up_bias
    )

    results = present(hidden_out, grad_hidden, t_qkv, t_out, t_up, t_down, sum_rows, sum_tiles)
    hidden_out, grad_hidden, g_qkv, g_out, g_up, g_down = results[:6]
    n1g, n1b, n2g, n2b, db, ob, qb, vb, ub = (item.reshape(item.size) for item in results[6:])
    return (
        hidden_out,
        grad_hidden,
        n1g,
        n1b,
        g_qkv,
        qb,
        vb,
        g_out,
        ob,
        n2g,
        n2b,
        g_up,
        ub,
        g_down,
        db,
    )


def shards(*arrays):
    micro, rows, _ = arrays[0].shape
    fits = lax.axis_size("gx") == 2 and lax.axis_size("gy") == PLANES * SPOTS
    fits = fits and micro == 2 and rows == 4 * BLOCK
    return (plane_shards if fits else general_shards)(*arrays)


def solution(mesh):
    tokens = P(None, AXES, None)
    vector = P(AXES)
    matrix = P(AXES, None)
    placed = (
        tokens,
        tokens,
        vector,
        vector,
        matrix,
        vector,
        vector,
        matrix,
        vector,
        vector,
        vector,
        matrix,
        vector,
        matrix,
        vector,
        tokens,
    )
    returned = (
        tokens,
        tokens,
        vector,
        vector,
        matrix,
        vector,
        vector,
        matrix,
        vector,
        vector,
        vector,
        matrix,
        vector,
        matrix,
        vector,
    )
    return jax.shard_map(
        shards, mesh=mesh, in_specs=placed, out_specs=returned, check_vma=False
    )
```

```python
import functools

import jax
import jax.numpy as jnp
from jax import lax
from jax.experimental import pallas as pl
from jax.experimental.pallas import tpu as pltpu
from jax.sharding import PartitionSpec as P

HEADS = 12
HEAD_DIM = 64
D = 768
FF = 3072
BLOCK = 64
RANDOM = 3
LANES = 2 * HEAD_DIM
EPSILON = 1e-05
NEGATIVE = -1e30
SCALE = HEAD_DIM**-0.5
CHUNK = 256
SPAN = 8

F32 = jnp.float32
BF16 = jnp.bfloat16
VMEM = pltpu.VMEM


def whole(space=VMEM):
    return pl.BlockSpec(memory_space=space)


def params_of(megabytes):
    return pltpu.CompilerParams(vmem_limit_bytes=megabytes * 1024 * 1024)


def head_place(head):
    return (head // 3) * 4 + head % 3


def dot(left, right):
    return lax.dot_general(left, right, (((1,), (0,)), ((), ())), preferred_element_type=F32)


def dot_rt(left, right):
    return lax.dot_general(left, right, (((1,), (1,)), ((), ())), preferred_element_type=F32)


def dot_lt(left, right):
    return lax.dot_general(left, right, (((0,), (0,)), ((), ())), preferred_element_type=F32)


def swap_halves(tile):
    return pltpu.roll(tile, HEAD_DIM, axis=tile.ndim - 1)


def low_lanes(rows):
    return lax.broadcasted_iota(jnp.int32, (rows, LANES), 1) < HEAD_DIM


def norm_parts(values):
    centre = values - jnp.mean(values, axis=-1, keepdims=True)
    spread = jnp.mean(centre * centre, axis=-1, keepdims=True)
    inverse = lax.rsqrt(spread + EPSILON)
    return centre * inverse, inverse


def norm_pull(grad, normal, inverse, gain):
    scaled = grad * gain
    return inverse * (
        scaled
        - jnp.mean(scaled, axis=-1, keepdims=True)
        - normal * jnp.mean(scaled * normal, axis=-1, keepdims=True)
    )


def qkv_kernel(x_ref, gain_ref, shift_ref, w_ref, bias_ref, normed_ref, send_ref):
    micro, rows, _ = x_ref.shape
    values = x_ref[...].reshape(micro * rows, D).astype(F32)
    normal, _ = norm_parts(values)
    normed_ref[...] = (normal * gain_ref[...] + shift_ref[...]).astype(BF16)
    low = low_lanes(rows)
    for chunk in range(3 * D // CHUNK):
        columns = slice(chunk * CHUNK, (chunk + 1) * CHUNK)
        packed = dot(normed_ref[...], w_ref[:, columns]) + bias_ref[:, columns]
        if chunk < D // CHUNK:
            packed = packed.astype(BF16).astype(F32) * SCALE
        for tile in range(CHUNK // LANES):
            part = packed[:, tile * LANES : (tile + 1) * LANES]
            first, second = part[:rows], part[rows:]
            if chunk < D // CHUNK:
                head = (chunk * CHUNK // LANES + tile) * 2
                even = jnp.where(low, first, swap_halves(second))
                odd = jnp.where(low, swap_halves(first), second)
                send_ref[head_place(head), 0] = even.astype(BF16)
                send_ref[head_place(head + 1), 0] = odd.astype(BF16)
            else:
                head = (chunk * CHUNK - D) // LANES + tile
                send_ref[head_place(head), 1] = first.astype(BF16)
                send_ref[head_place(head), 2] = swap_halves(second).astype(BF16)


def qkv_forward(x, gain, shift, w, bias, groups):
    micro, rows, _ = x.shape
    return pl.pallas_call(
        qkv_kernel,
        out_shape=(
            jax.ShapeDtypeStruct((micro * rows, D), BF16),
            jax.ShapeDtypeStruct((groups, 3, rows, LANES), BF16),
        ),
        in_specs=[whole()] * 5,
        out_specs=(whole(), whole()),
        compiler_params=params_of(48),
        name="qkv_forward",
    )(x, gain, shift, w, bias)


def half_mask(low_half):
    lane = lax.broadcasted_iota(jnp.int32, (1, LANES), 1)
    keep = (lane < HEAD_DIM) if low_half else (lane >= HEAD_DIM)
    return jnp.where(keep, 1.0, 0.0).astype(BF16)


def inner_slots(pick, block, blocks):
    ids, bias = picked_slots([pick(block, number) for number in range(RANDOM)], block, blocks)
    edge = (block == 0) | (block == blocks - 1)
    ids[0] = jnp.maximum(ids[0], 0)
    ids[2] = jnp.minimum(ids[2], blocks - 1)
    return ids, bias + jnp.where(edge, NEGATIVE, 0.0).astype(F32)


def slots_of(table_ref, micro, block, blocks):
    picks = [table_ref[micro, block * RANDOM + number] for number in range(RANDOM)]
    return picked_slots(picks, block, blocks)


def picked_slots(picks, block, blocks):
    last = blocks - 1
    ids = [block - 1, block, block + 1, 0, last] + picks
    dropped = [None, None, None, block == 1, block == last - 1]
    for number in range(RANDOM):
        pick = picks[number]
        bad = (jnp.abs(pick - block) <= 1) | (pick == 0) | (pick == last)
        for earlier in range(number):
            bad = bad | (pick == picks[earlier])
        dropped.append(bad)
    lane = lax.broadcasted_iota(jnp.int32, (1, LANES), 1)
    tiles = []
    for pair in range(len(ids) // 2):
        level = [
            0.0 if bad is None else jnp.where(bad, NEGATIVE, 0.0).astype(F32)
            for bad in dropped[2 * pair : 2 * pair + 2]
        ]
        tiles.append(jnp.where(lane < HEAD_DIM, level[0], level[1]))
    return ids, jnp.concatenate(tiles, axis=1)


def attend_kernel(table_ref, qkv_ref, out_ref, lse_ref, s_ref):
    groups, _, local, _, _ = qkv_ref.shape
    blocks = groups * local
    low = low_lanes(BLOCK)
    masks = [half_mask(True), half_mask(False)]

    def load(component, block):
        return qkv_ref[block // local, component, block % local]

    def sparse(block, carry):
        mixed, logs = [], []
        for micro in range(2):
            ids, bias = slots_of(table_ref, micro, block, blocks)
            keys = jnp.concatenate([load(1 + micro, spot) for spot in ids], axis=0)
            query = load(0, block) * masks[micro]
            scores = dot_rt(query, keys) + bias
            top = jnp.max(scores, axis=1, keepdims=True)
            powered = jnp.exp(scores - top)
            total = jnp.sum(powered, axis=1, keepdims=True)
            mixed.append(dot(powered.astype(BF16), keys) * (1.0 / total))
            logs.append(top + jnp.log(total))
        out_ref[block // local, block % local] = jnp.where(low, mixed[1], mixed[0]).astype(BF16)
        lse_ref[block] = jnp.where(low, logs[0], logs[1])
        return carry

    lax.fori_loop(1, blocks - 1, sparse, 0)

    spans = blocks // SPAN
    ends = (0, blocks - 1)
    results = []
    for micro in range(2):
        query = jnp.concatenate([load(0, end) for end in ends], axis=0) * masks[micro]

        def keys_at(span, micro=micro):
            return jnp.concatenate(
                [load(1 + micro, span * SPAN + spot) for spot in range(SPAN)], axis=0
            )

        def first_pass(span, top, query=query, keys_at=keys_at):
            scores = dot_rt(query, keys_at(span))
            s_ref[span] = scores
            return jnp.maximum(top, jnp.max(scores, axis=1, keepdims=True))

        top = lax.fori_loop(0, spans, first_pass, jnp.full((2 * BLOCK, 1), NEGATIVE, F32))

        def second_pass(span, carry, top=top, keys_at=keys_at):
            total, mixed = carry
            powered = jnp.exp(s_ref[span] - top)
            return (
                total + jnp.sum(powered, axis=1, keepdims=True),
                mixed + dot(powered.astype(BF16), keys_at(span)),
            )

        total, mixed = lax.fori_loop(
            0,
            spans,
            second_pass,
            (jnp.zeros((2 * BLOCK, 1), F32), jnp.zeros((2 * BLOCK, LANES), F32)),
        )
        results.append((mixed * (1.0 / total), top + jnp.log(total)))
    for place, end in enumerate(ends):
        rows = slice(place * BLOCK, (place + 1) * BLOCK)
        out_ref[end // local, end % local] = jnp.where(
            low, results[1][0][rows], results[0][0][rows]
        ).astype(BF16)
        lse_ref[end] = jnp.where(low, results[0][1][rows], results[1][1][rows])


def attention_forward(table, qkv):
    groups, _, local, _, _ = qkv.shape
    blocks = groups * local
    return pl.pallas_call(
        attend_kernel,
        out_shape=(
            jax.ShapeDtypeStruct((groups, local, BLOCK, LANES), BF16),
            jax.ShapeDtypeStruct((blocks, BLOCK, LANES), F32),
        ),
        in_specs=[whole(pltpu.SMEM), whole()],
        out_specs=(whole(), whole()),
        scratch_shapes=[VMEM((blocks // SPAN, 2 * BLOCK, SPAN * BLOCK), F32)],
        compiler_params=params_of(48),
        name="attention_forward",
    )(table, qkv)


def attend_back_kernel(table_ref, qkv_ref, grad_ref, lse_ref, out_ref, sums_ref, p_ref, dp_ref):
    groups, _, local, _, _ = qkv_ref.shape
    blocks = groups * local
    low = low_lanes(BLOCK)
    masks = [half_mask(True), half_mask(False)]

    def load(component, block):
        return qkv_ref[block // local, component, block % local]

    def load_grad(block):
        return grad_ref[block // local, block % local]

    def clear(block, carry):
        for micro in range(2):
            sums_ref[micro, block] = jnp.zeros((BLOCK, LANES), F32)
        return carry

    lax.fori_loop(0, blocks, clear, 0)

    def sparse(block, carry):
        grads = []
        for micro in range(2):
            ids, bias = slots_of(table_ref, micro, block, blocks)
            keys = jnp.concatenate([load(1 + micro, spot) for spot in ids], axis=0)
            both = jnp.concatenate(
                [load(0, block) * masks[micro], load_grad(block) * masks[1 - micro]], axis=0
            )
            products = dot_rt(both, keys)
            logs = lse_ref[block][:, micro * HEAD_DIM : micro * HEAD_DIM + 1]
            weights = jnp.exp(products[:BLOCK] + bias - logs)
            grad_weights = products[BLOCK:]
            delta = jnp.sum(weights * grad_weights, axis=1, keepdims=True)
            grad_scores = weights * (grad_weights - delta)
            stacked = jnp.concatenate([grad_scores, weights], axis=0).astype(BF16)
            grads.append(dot(stacked[:BLOCK], keys))
            shares = dot_lt(stacked, both)
            for place, spot in enumerate(ids):
                sums_ref[micro, spot] += shares[place * BLOCK : (place + 1) * BLOCK]
        out_ref[block // local, 0, block % local] = (
            jnp.where(low, grads[0], grads[1]) * SCALE
        ).astype(BF16)
        return carry

    lax.fori_loop(1, blocks - 1, sparse, 0)

    spans = blocks // SPAN
    ends = (0, blocks - 1)
    results = []
    for micro in range(2):
        query = jnp.concatenate([load(0, end) for end in ends], axis=0) * masks[micro]
        grad = jnp.concatenate([load_grad(end) for end in ends], axis=0) * masks[1 - micro]
        both = jnp.concatenate([query, grad], axis=0)
        logs = jnp.concatenate(
            [lse_ref[end][:, micro * HEAD_DIM : micro * HEAD_DIM + 1] for end in ends], axis=0
        )

        def keys_at(span, micro=micro):
            return jnp.concatenate(
                [load(1 + micro, span * SPAN + spot) for spot in range(SPAN)], axis=0
            )

        def first_pass(span, delta, both=both, logs=logs, keys_at=keys_at):
            products = dot_rt(both, keys_at(span))
            weights = jnp.exp(products[: 2 * BLOCK] - logs)
            grad_weights = products[2 * BLOCK :]
            p_ref[span] = weights
            dp_ref[span] = grad_weights
            return delta + jnp.sum(weights * grad_weights, axis=1, keepdims=True)

        delta = lax.fori_loop(0, spans, first_pass, jnp.zeros((2 * BLOCK, 1), F32))

        def second_pass(span, carry, delta=delta, both=both, keys_at=keys_at, micro=micro):
            weights = p_ref[span]
            grad_scores = weights * (dp_ref[span] - delta)
            stacked = jnp.concatenate([grad_scores, weights], axis=0).astype(BF16)
            shares = dot_lt(stacked, both)
            for spot in range(SPAN):
                sums_ref[micro, span * SPAN + spot] += shares[spot * BLOCK : (spot + 1) * BLOCK]
            return carry + dot(stacked[: 2 * BLOCK], keys_at(span))

        results.append(
            lax.fori_loop(0, spans, second_pass, jnp.zeros((2 * BLOCK, LANES), F32))
        )
    for place, end in enumerate(ends):
        rows = slice(place * BLOCK, (place + 1) * BLOCK)
        out_ref[end // local, 0, end % local] = (
            jnp.where(low, results[0][rows], results[1][rows]) * SCALE
        ).astype(BF16)

    def finish(block, carry):
        for micro in range(2):
            out_ref[block // local, 1 + micro, block % local] = sums_ref[micro, block].astype(BF16)
        return carry

    lax.fori_loop(0, blocks, finish, 0)


def attention_backward(table, qkv, grad, lse):
    groups, _, local, _, _ = qkv.shape
    blocks = groups * local
    spans = VMEM((blocks // SPAN, 2 * BLOCK, SPAN * BLOCK), F32)
    return pl.pallas_call(
        attend_back_kernel,
        out_shape=jax.ShapeDtypeStruct(qkv.shape, BF16),
        in_specs=[whole(pltpu.SMEM), whole(), whole(), whole()],
        out_specs=whole(),
        scratch_shapes=[VMEM((2, blocks, BLOCK, LANES), F32), spans, spans],
        compiler_params=params_of(48),
        name="attention_backward",
    )(table, qkv, grad, lse)


def middle_kernel(
    mixed_in_ref,
    x_ref,
    dy_ref,
    w_out_ref,
    out_shift_ref,
    gain_ref,
    shift_ref,
    up_shift_ref,
    down_shift_ref,
    w_up_ref,
    w_down_ref,
    hidden_ref,
    send_ref,
    dres_ref,
    g_out_ref,
    g_up_ref,
    g_down_ref,
    g_up_bias_ref,
    g_small_ref,
    mixed_ref,
    residual_ref,
    second_ref,
    second_t_ref,
    total_ref,
    dsecond_ref,
):
    micro, rows, _ = x_ref.shape
    step = pl.program_id(0)
    low = low_lanes(rows)

    @pl.when(step == 0)
    def _():
        for pair in range(HEADS // 2):
            even = mixed_in_ref[head_place(2 * pair)].astype(F32)
            odd = mixed_in_ref[head_place(2 * pair + 1)].astype(F32)
            columns = slice(pair * LANES, (pair + 1) * LANES)
            mixed_ref[:rows, columns] = jnp.where(low, swap_halves(even), odd).astype(BF16)
            mixed_ref[rows:, columns] = jnp.where(low, even, swap_halves(odd)).astype(BF16)
        residual = x_ref[...].reshape(micro * rows, D).astype(F32) + (
            dot(mixed_ref[...], w_out_ref[...]) + out_shift_ref[...]
        )
        residual_ref[...] = residual
        normal, _ = norm_parts(residual)
        second = normal * gain_ref[...] + shift_ref[...]
        second_ref[...] = second.astype(BF16)
        second_t_ref[...] = second.T.astype(BF16)
        total_ref[...] = jnp.zeros_like(total_ref)
        dsecond_ref[...] = jnp.zeros_like(dsecond_ref)

    upper = dot(second_ref[...], w_up_ref[...]) + up_shift_ref[...]
    factor = 0.7978845608028654
    square = upper * upper
    bent = jnp.tanh(factor * (upper + 0.044715 * (upper * square)))
    half = 0.5 * (1.0 + bent)
    active = (upper * half).astype(BF16)
    slope = half + 0.5 * upper * (1.0 - bent * bent) * (
        factor + (3.0 * 0.044715 * factor) * square
    )
    dy = dy_ref[...]
    total_ref[...] += dot(active, w_down_ref[...])
    g_down_ref[...] = dot_lt(active, dy).astype(g_down_ref.dtype)
    dupper = (dot_rt(dy, w_down_ref[...]) * slope).astype(BF16)
    g_up_bias_ref[...] = jnp.sum(dupper.astype(F32), axis=0, keepdims=True)
    g_up_ref[...] = dot(second_t_ref[...], dupper).astype(g_up_ref.dtype)
    dsecond_ref[...] += dot_rt(dupper, w_up_ref[...])

    @pl.when(step == pl.num_programs(0) - 1)
    def _():
        residual = residual_ref[...]
        hidden_ref[...] = (
            (residual + (total_ref[...] + down_shift_ref[...])).astype(BF16).reshape(x_ref.shape)
        )
        normal, inverse = norm_parts(residual)
        dsecond = dsecond_ref[...]
        grad_out = dy_ref[...].astype(F32)
        g_small_ref[0:1] = jnp.sum(dsecond * normal, axis=0, keepdims=True)
        g_small_ref[1:2] = jnp.sum(dsecond, axis=0, keepdims=True)
        g_small_ref[2:3] = jnp.sum(grad_out, axis=0, keepdims=True)
        dres = grad_out + norm_pull(dsecond, normal, inverse, gain_ref[...])
        dres_ref[...] = dres
        branch = dres.astype(BF16)
        g_small_ref[3:4] = jnp.sum(branch.astype(F32), axis=0, keepdims=True)
        g_out_ref[...] = dot_lt(mixed_ref[...], branch).astype(g_out_ref.dtype)
        dmixed = dot_rt(branch, w_out_ref[...])
        for pair in range(HEADS // 2):
            part = dmixed[:, pair * LANES : (pair + 1) * LANES]
            first, last = part[:rows], part[rows:]
            even = jnp.where(low, last, swap_halves(first))
            odd = jnp.where(low, swap_halves(last), first)
            send_ref[head_place(2 * pair)] = even.astype(BF16)
            send_ref[head_place(2 * pair + 1)] = odd.astype(BF16)


def middle(mixed_in, x, dy, w_out, out_shift, gain, shift, up_shift, down_shift, w_up, w_down, kind):
    micro, rows, _ = x.shape
    tokens = micro * rows
    groups = mixed_in.shape[0]

    def fixed(shape):
        return pl.BlockSpec(shape, lambda step: (0,) * len(shape))

    vector = fixed((1, D))
    steps = FF // CHUNK
    return pl.pallas_call(
        middle_kernel,
        grid=(steps,),
        out_shape=(
            jax.ShapeDtypeStruct(x.shape, BF16),
            jax.ShapeDtypeStruct((groups, rows, LANES), BF16),
            jax.ShapeDtypeStruct((tokens, D), F32),
            jax.ShapeDtypeStruct((D, D), kind),
            jax.ShapeDtypeStruct((D, FF), kind),
            jax.ShapeDtypeStruct((FF, D), kind),
            jax.ShapeDtypeStruct((1, FF), F32),
            jax.ShapeDtypeStruct((4, D), F32),
        ),
        in_specs=[
            fixed(mixed_in.shape),
            fixed(x.shape),
            fixed((tokens, D)),
            fixed((D, D)),
            vector,
            vector,
            vector,
            pl.BlockSpec((1, CHUNK), lambda step: (0, step)),
            vector,
            pl.BlockSpec((D, CHUNK), lambda step: (0, step)),
            pl.BlockSpec((CHUNK, D), lambda step: (step, 0)),
        ],
        out_specs=(
            fixed(x.shape),
            fixed((groups, rows, LANES)),
            fixed((tokens, D)),
            fixed((D, D)),
            pl.BlockSpec((D, CHUNK), lambda step: (0, step)),
            pl.BlockSpec((CHUNK, D), lambda step: (step, 0)),
            pl.BlockSpec((1, CHUNK), lambda step: (0, step)),
            fixed((4, D)),
        ),
        scratch_shapes=[
            VMEM((tokens, D), BF16),
            VMEM((tokens, D), F32),
            VMEM((tokens, D), BF16),
            VMEM((D, tokens), BF16),
            VMEM((tokens, D), F32),
            VMEM((tokens, D), F32),
        ],
        compiler_params=params_of(56),
        name="middle",
    )(mixed_in, x, dy, w_out, out_shift, gain, shift, up_shift, down_shift, w_up, w_down)


def qkv_back_kernel(
    recv_ref,
    normed_ref,
    x_ref,
    dres_ref,
    gain_ref,
    w_ref,
    grad_ref,
    g_qkv_ref,
    g_bias_ref,
    g_small_ref,
    packed_ref,
    normed_t_ref,
    dnormed_ref,
):
    micro, rows, _ = x_ref.shape
    step = pl.program_id(0)
    low = low_lanes(rows)

    @pl.when(step == 0)
    def _():
        for pair in range(HEADS // 2):
            even = recv_ref[head_place(2 * pair), 0].astype(F32)
            odd = recv_ref[head_place(2 * pair + 1), 0].astype(F32)
            spot, columns = pair // 2, slice((pair % 2) * LANES, (pair % 2 + 1) * LANES)
            packed_ref[spot, :rows, columns] = jnp.where(low, even, swap_halves(odd)).astype(BF16)
            packed_ref[spot, rows:, columns] = jnp.where(low, swap_halves(even), odd).astype(BF16)
        for head in range(HEADS):
            spot = D // CHUNK + head // 2
            columns = slice((head % 2) * LANES, (head % 2 + 1) * LANES)
            packed_ref[spot, :rows, columns] = recv_ref[head_place(head), 1]
            packed_ref[spot, rows:, columns] = swap_halves(
                recv_ref[head_place(head), 2].astype(F32)
            ).astype(BF16)
        normed_t_ref[...] = normed_ref[...].astype(F32).T.astype(BF16)
        dnormed_ref[...] = jnp.zeros_like(dnormed_ref)

    packed = packed_ref[step]
    g_bias_ref[...] = jnp.sum(packed.astype(F32), axis=0, keepdims=True)
    g_qkv_ref[...] = dot(normed_t_ref[...], packed).astype(g_qkv_ref.dtype)
    dnormed_ref[...] += dot_rt(packed, w_ref[...])

    @pl.when(step == pl.num_programs(0) - 1)
    def _():
        normal, inverse = norm_parts(x_ref[...].reshape(micro * rows, D).astype(F32))
        dnormed = dnormed_ref[...]
        g_small_ref[0:1] = jnp.sum(dnormed * normal, axis=0, keepdims=True)
        g_small_ref[1:2] = jnp.sum(dnormed, axis=0, keepdims=True)
        grad = dres_ref[...] + norm_pull(dnormed, normal, inverse, gain_ref[...])
        grad_ref[...] = grad.reshape(x_ref.shape)


def qkv_backward(recv, normed, x, dres, gain, w, kind):
    micro, rows, _ = x.shape
    tokens = micro * rows

    def fixed(shape):
        return pl.BlockSpec(shape, lambda step: (0,) * len(shape))

    steps = 3 * D // CHUNK
    return pl.pallas_call(
        qkv_back_kernel,
        grid=(steps,),
        out_shape=(
            jax.ShapeDtypeStruct(x.shape, F32),
            jax.ShapeDtypeStruct((D, 3 * D), kind),
            jax.ShapeDtypeStruct((1, 3 * D), F32),
            jax.ShapeDtypeStruct((2, D), F32),
        ),
        in_specs=[
            fixed(recv.shape),
            fixed((tokens, D)),
            fixed(x.shape),
            fixed((tokens, D)),
            fixed((1, D)),
            pl.BlockSpec((D, CHUNK), lambda step: (0, step)),
        ],
        out_specs=(
            fixed(x.shape),
            pl.BlockSpec((D, CHUNK), lambda step: (0, step)),
            pl.BlockSpec((1, CHUNK), lambda step: (0, step)),
            fixed((2, D)),
        ),
        scratch_shapes=[
            VMEM((steps, tokens, CHUNK), BF16),
            VMEM((D, tokens), BF16),
            VMEM((tokens, D), F32),
        ],
        compiler_params=params_of(56),
        name="qkv_backward",
    )(recv, normed, x, dres, gain, w)


AXES = ("gx", "gy")


def gather(array):
    return lax.all_gather(array, AXES, axis=0, tiled=True)


def scatter(array):
    return lax.psum_scatter(array, AXES, scatter_dimension=0, tiled=True)


def exchange(array):
    return lax.all_to_all(array, "gy", 0, 0, tiled=True)


def by_heads(w_qkv):
    rows = w_qkv.shape[0]
    sides = w_qkv[:, D:].reshape(rows, 2, HEADS, HEAD_DIM)
    return jnp.concatenate([w_qkv[:, :D], jnp.swapaxes(sides, 1, 2).reshape(rows, 2 * D)], axis=1)


def by_parts(w_qkv):
    rows = w_qkv.shape[0]
    sides = w_qkv[:, D:].reshape(rows, HEADS, 2, HEAD_DIM)
    return jnp.concatenate([w_qkv[:, :D], jnp.swapaxes(sides, 1, 2).reshape(rows, 2 * D)], axis=1)


def general_shards(
    hidden_in,
    rand_table,
    norm1_gain,
    norm1_bias,
    w_qkv,
    query_bias,
    value_bias,
    w_out,
    out_bias,
    norm2_gain,
    norm2_bias,
    w_up,
    up_bias,
    w_down,
    down_bias,
    cotangent,
):
    micro, rows, _ = hidden_in.shape
    groups = lax.axis_size("gy")
    local = rows // BLOCK
    own = norm1_gain.shape[0]

    vectors = jnp.concatenate(
        [
            norm1_gain,
            norm1_bias,
            query_bias,
            value_bias,
            out_bias,
            norm2_gain,
            norm2_bias,
            down_bias,
            up_bias,
        ]
    )
    table = lax.all_gather(rand_table, "gy", axis=1, tiled=True)
    table = table.reshape(micro, groups * local * RANDOM)
    vectors = gather(vectors[None]).astype(F32)
    gain_one, shift_one, query_shift, value_shift, out_shift, gain_two, shift_two, down_shift = (
        vectors[:, number * own : (number + 1) * own].reshape(1, D) for number in range(8)
    )
    up_shift = vectors[:, 8 * own :].reshape(1, FF)
    w_qkv_full = gather(by_heads(w_qkv))
    w_out_full, w_up_full, w_down_full = gather(w_out), gather(w_up), gather(w_down)
    packed_bias = by_heads(
        jnp.concatenate([query_shift, jnp.zeros_like(query_shift), value_shift], axis=1)
    )

    normed, send = qkv_forward(hidden_in, gain_one, shift_one, w_qkv_full, packed_bias, groups)
    qkv = exchange(send).reshape(groups, 3, local, BLOCK, LANES)
    mixed, lse = attention_forward(table, qkv)
    mixed_back = exchange(mixed.reshape(groups, rows, LANES))
    hidden_out, grad_send, dres, g_out, g_up, g_down, g_up_bias, g_mid = middle(
        mixed_back,
        hidden_in,
        cotangent.reshape(micro * rows, D),
        w_out_full,
        out_shift,
        gain_two,
        shift_two,
        up_shift,
        down_shift,
        w_up_full,
        w_down_full,
        F32,
    )
    grad_mixed = exchange(grad_send).reshape(groups, local, BLOCK, LANES)
    dqkv = attention_backward(table, qkv, grad_mixed, lse)
    dqkv_back = exchange(dqkv.reshape(groups, 3, rows, LANES))
    grad_hidden, g_qkv, g_packed, g_first = qkv_backward(
        dqkv_back, normed, hidden_in, dres, gain_one, w_qkv_full, F32
    )

    g_packed = by_parts(g_packed)
    small = [
        g_first[0],
        g_first[1],
        g_packed[0, :D],
        g_packed[0, 2 * D :],
        g_mid[3],
        g_mid[0],
        g_mid[1],
        g_mid[2],
    ]
    ranks = D // own
    small = jnp.concatenate(
        [item.reshape(ranks, own) for item in small] + [g_up_bias.reshape(ranks, 4 * own)], axis=1
    )
    small = scatter(small)[0]
    parts = [small[number * own : (number + 1) * own] for number in range(8)]
    return (
        hidden_out,
        grad_hidden,
        parts[0],
        parts[1],
        by_parts(scatter(g_qkv)),
        parts[2],
        parts[3],
        scatter(g_out),
        parts[4],
        parts[5],
        parts[6],
        scatter(g_up),
        small[8 * own :],
        scatter(g_down),
        parts[7],
    )


MESH = pl.DeviceIdType.MESH
ANY = pl.ANY
PLANES = 4
SPOTS = 4
PIECES = 2
RANKS = 2 * PLANES * SPOTS
TILES = 3 * D // LANES
HALF_TILES = TILES // 2
QUERY_ORDER = (0, 2, 3, 5, 6, 8, 9, 11, 1, 4, 7, 10)


def column_order():
    order = [("q", head) for head in QUERY_ORDER]
    for spot in range(SPOTS):
        for place in (2 * 3 * spot, 2 * 3 * spot + 2):
            order += [("k", place // 2), ("v", place // 2)]
        order += [("v", 3 * spot + 2), ("k", 3 * spot + 2)]
    return order


def natural_block(entry):
    return "qkv".index(entry[0]) * HEADS + entry[1]


def flip(value, bits):
    if bits == 0:
        return value
    if bits == 1:
        return value + 1 - 2 * lax.rem(value, 2)
    if bits == 2:
        return value + 2 - 4 * lax.div(value, 2)
    return 3 - value


def place_here():
    core, rank = lax.axis_index("gx"), lax.axis_index("gy")
    return core, lax.div(rank, SPOTS), lax.rem(rank, SPOTS)


def rank_of(plane, spot):
    return plane * SPOTS + spot


def greet(partners):
    barrier = pltpu.get_barrier_semaphore()
    for partner in partners:
        pl.semaphore_signal(barrier, inc=1, device_id=partner, device_id_type=MESH)
    pl.semaphore_wait(barrier, len(partners))


def remote(source, target, send_sem, recv_sem, device):
    return pltpu.make_async_remote_copy(
        src_ref=source,
        dst_ref=target,
        send_sem=send_sem,
        recv_sem=recv_sem,
        device_id=device,
        device_id_type=MESH,
    )


def column_partners(core, plane, spot):
    partners = [(1 - core, rank_of(plane, spot))]
    for bits in range(1, PLANES):
        for other in (core, 1 - core):
            partners.append((other, rank_of(flip(plane, bits), spot)))
    return partners


def all_partners(core, plane, spot):
    return column_partners(core, plane, spot) + [
        (core, rank_of(plane, flip(spot, 1))),
        (core, rank_of(plane, flip(spot, 2))),
    ]


def to_planes(source, target, send_sem, recv_sem, local_sem):
    core, plane, spot = place_here()
    half, odd = lax.div(plane, 2), lax.rem(plane, 2)
    sends, keeps = [], []
    for micro in range(2):
        goal = 2 * micro + core
        here = (goal == plane) & (half == core)
        send = remote(
            source.at[micro],
            target.at[odd],
            send_sem.at[micro],
            recv_sem.at[odd],
            (half, rank_of(goal, spot)),
        )
        keep = pltpu.make_async_copy(source.at[micro], target.at[odd], local_sem.at[micro])

        @pl.when(jnp.logical_not(here))
        def _(send=send):
            send.start()

        @pl.when(here)
        def _(keep=keep):
            keep.start()

        sends.append((here, send))
        keeps.append((here, keep))

    def finish():
        for piece in range(PIECES):
            mine = (odd == core) & (plane == 2 * core + piece)
            arrival = remote(
                source.at[0],
                target.at[piece],
                send_sem.at[0],
                recv_sem.at[piece],
                (core, rank_of(plane, spot)),
            )

            @pl.when(jnp.logical_not(mine))
            def _(arrival=arrival):
                arrival.wait_recv()

        for (here, send), (_, keep) in zip(sends, keeps):

            @pl.when(jnp.logical_not(here))
            def _(send=send):
                send.wait_send()

            @pl.when(here)
            def _(keep=keep):
                keep.wait()

    return finish


def from_planes(source, target, send_sem, recv_sem, local_sem, later=False):
    core, plane, spot = place_here()
    micro, odd = lax.div(plane, 2), lax.rem(plane, 2)
    sends, keeps = [], []

    def start(piece):
        goal = 2 * core + piece
        here = (goal == plane) & (odd == core)
        send = remote(
            source.at[piece],
            target.at[micro],
            send_sem.at[piece],
            recv_sem.at[micro],
            (odd, rank_of(goal, spot)),
        )
        keep = pltpu.make_async_copy(source.at[piece], target.at[micro], local_sem.at[piece])

        @pl.when(jnp.logical_not(here))
        def _(send=send):
            send.start()

        @pl.when(here)
        def _(keep=keep):
            keep.start()

        sends.append((here, send))
        keeps.append((here, keep))

    for piece in () if later else range(PIECES):
        start(piece)

    def finish():
        for number in range(2):
            mine = (2 * number + core == plane) & (micro == core)
            arrival = remote(
                source.at[0],
                target.at[number],
                send_sem.at[0],
                recv_sem.at[number],
                (core, rank_of(plane, spot)),
            )

            @pl.when(jnp.logical_not(mine))
            def _(arrival=arrival):
                arrival.wait_recv()

        for (here, send), (_, keep) in zip(sends, keeps):

            @pl.when(jnp.logical_not(here))
            def _(send=send):
                send.wait_send()

            @pl.when(here)
            def _(keep=keep):
                keep.wait()

    return (start, finish) if later else finish


class Gather:
    SENDS = 31

    def __init__(self, source, target, send_sem, recv_sem, local_sem):
        self.source, self.target = source, target
        self.send_sem, self.recv_sem = send_sem, recv_sem
        self.core, self.plane, self.spot = place_here()
        self.sends = []
        self.own = pltpu.make_async_copy(
            source, target.at[self.core, self.plane, self.spot], local_sem
        )
        self.own.start()

    def send(self, source, plane, spot, device):
        copy = remote(
            source,
            self.target.at[self.core, plane, spot],
            self.send_sem.at[len(self.sends)],
            self.recv_sem.at[self.core, plane, spot],
            device,
        )
        copy.start()
        self.sends.append(copy)

    def arrive(self, core, plane, spot):
        shard = self.target.at[core, plane, spot]
        remote(
            shard,
            shard,
            self.send_sem.at[0],
            self.recv_sem.at[core, plane, spot],
            (self.core, rank_of(self.plane, self.spot)),
        ).wait_recv()

    def neighbour(self, bits):
        return (self.core, rank_of(self.plane, flip(self.spot, bits)))

    def sibling(self):
        return (1 - self.core, rank_of(self.plane, self.spot))

    def start(self):
        for bits in range(1, PLANES):
            goal = (self.core, rank_of(flip(self.plane, bits), self.spot))
            self.send(self.source, self.plane, self.spot, goal)
        for goal in (self.neighbour(1), self.neighbour(2), self.sibling()):
            self.send(self.source, self.plane, self.spot, goal)

    def column(self):
        for bits in range(1, PLANES):
            plane = flip(self.plane, bits)
            self.arrive(self.core, plane, self.spot)
            shard = self.target.at[self.core, plane, self.spot]
            for goal in (self.neighbour(1), self.neighbour(2), self.sibling()):
                self.send(shard, plane, self.spot, goal)

    def across(self):
        for bits in range(PLANES):
            plane = flip(self.plane, bits)
            for side in (1, 2):
                spot = flip(self.spot, side)
                self.arrive(self.core, plane, spot)
                shard = self.target.at[self.core, plane, spot]
                if (side == 1) == (bits < 2):
                    self.send(shard, plane, spot, self.neighbour(3 - side))
                self.send(shard, plane, spot, self.sibling())

    def corner(self):
        spot = flip(self.spot, 3)
        for bits in range(PLANES):
            plane = flip(self.plane, bits)
            self.arrive(self.core, plane, spot)
            self.send(self.target.at[self.core, plane, spot], plane, spot, self.sibling())

    def finish(self):
        for bits in range(PLANES):
            for side in range(SPOTS):
                self.arrive(1 - self.core, flip(self.plane, bits), flip(self.spot, side))
        self.own.wait()
        for copy in self.sends:
            copy.wait_send()


def settle(shards_ref, plan):
    rows = shards_ref.shape[3] // 2

    def pair(number, carry):
        core, plane, side = (
            lax.div(number, 2 * PLANES),
            lax.rem(lax.div(number, 2), PLANES),
            lax.rem(number, 2),
        )
        goal = pl.ds(pl.multiple_of(number * 2 * rows, 16), 2 * rows)
        for tile, out_ref, (left, right) in plan:
            columns = slice(tile * LANES, (tile + 1) * LANES)
            first = shards_ref[core, plane, 2 * side, :, columns].astype(F32)
            second = shards_ref[core, plane, 2 * side + 1, :, columns].astype(F32)
            out_ref[goal, left * LANES : (left + 1) * LANES] = jnp.concatenate(
                [first[:rows], second[:rows]], axis=0
            ).astype(BF16)
            out_ref[goal, right * LANES : (right + 1) * LANES] = jnp.concatenate(
                [first[rows:], second[rows:]], axis=0
            ).astype(BF16)
        return carry

    lax.fori_loop(0, RANKS // 2, pair, 0)


def alternate(tile):
    return 2 * tile, 2 * tile + 1


def plane_partners(core, plane, spot):
    partners = []
    for other in (core, 1 - core):
        for side in range(SPOTS):
            if other is core and side == 0:
                continue
            partners.append((other, rank_of(plane, flip(spot, side))))
    return partners


def both_partners(core, plane, spot):
    return plane_partners(core, plane, spot) + column_partners(core, plane, spot)[1:]


def exchange_sems(recv_shape):
    return [
        pltpu.SemaphoreType.DMA((14,)),
        pltpu.SemaphoreType.DMA(recv_shape),
        pltpu.SemaphoreType.DMA((PIECES,)),
    ]


def sort_entries(table, sorted_ref, entries):
    count = table.shape[1]
    core = lax.axis_index("gx")
    lane = lax.broadcasted_iota(jnp.int32, (count, count), 1)
    row = lax.broadcasted_iota(jnp.int32, (count, count), 0).astype(F32)
    everything = jnp.broadcast_to(table, (count, count))
    half = entries // 2
    inside = (lane >= core * half) & (lane < (core + 1) * half)
    lane = lane.astype(F32)
    for number, along in enumerate((everything, jnp.where(inside, everything, 2.0 * LANES))):
        down = along.T
        before = (along < down) | ((along == down) & (lane < row))
        rank = jnp.sum(jnp.where(before, 1.0, 0.0), axis=1, keepdims=True)
        order = jnp.sum(jnp.where(rank == lane, row, 0.0), axis=0, keepdims=True)
        upto = jnp.sum(jnp.where(down <= lane, 1.0, 0.0), axis=0, keepdims=True)
        sorted_ref[2 * number : 2 * number + 1] = order.astype(jnp.int32)
        sorted_ref[2 * number + 1 : 2 * number + 2] = upto.astype(jnp.int32)


def pack_halves(read, target_ref, place, local, low, half):
    for number in range(local // 2):
        first = read(2 * number).astype(F32)
        second = swap_halves(read(2 * number + 1).astype(F32))
        kept = (first, second) if half == 0 else (second, first)
        target_ref[place + (number,)] = jnp.where(low, *kept).astype(BF16)


class Outward:
    def __init__(self, source, far_source, target, packed, send_sem, recv_sem, local_sem):
        self.target, self.packed = target, packed
        self.recv_sem, self.send_sem = recv_sem, send_sem
        self.core, self.plane, self.spot = place_here()
        self.sends, self.keeps = [], []
        for side in (3, 1, 2, 0):
            goal = flip(self.spot, side)
            for other in (self.core, 1 - self.core):
                near = other is self.core
                for piece in range(PIECES):
                    start = (source if near else far_source).at[goal, piece]
                    place = (2 * self.core + piece, self.spot)
                    stop = (target if near else packed).at[place]
                    if side == 0 and near:
                        copy = pltpu.make_async_copy(start, stop, local_sem.at[piece])
                        self.keeps.append(copy)
                    else:
                        copy = remote(
                            start,
                            stop,
                            send_sem.at[len(self.sends)],
                            recv_sem.at[place],
                            (other, rank_of(self.plane, goal)),
                        )
                        self.sends.append(copy)
                    copy.start()

    def arrive(self, side):
        goal = flip(self.spot, side)
        for other in (self.core, 1 - self.core):
            near = other is self.core
            if side == 0 and near:
                for copy in self.keeps:
                    copy.wait()
                continue
            for piece in range(PIECES):
                place = (2 * other + piece, goal)
                landed = (self.target if near else self.packed).at[place]
                remote(
                    landed,
                    landed,
                    self.send_sem.at[0],
                    self.recv_sem.at[place],
                    (self.core, rank_of(self.plane, self.spot)),
                ).wait_recv()
                if not near:
                    for number in range(self.packed.shape[2]):
                        tile = self.packed[place + (number,)]
                        self.target[place + (2 * number,)] = tile
                        self.target[place + (2 * number + 1,)] = swap_halves(
                            tile.astype(F32)
                        ).astype(BF16)

    def finish(self):
        for copy in self.sends:
            copy.wait_send()


def inward_targets(core, spot):
    for side in (3, 1, 2, 0):
        for other in (core, 1 - core):
            yield side, other, flip(spot, side), side == 0 and other is core


class Inward:
    def __init__(self, source, target, send_sem, recv_sem, local_sem):
        self.source, self.target = source, target
        self.send_sem, self.recv_sem, self.local_sem = send_sem, recv_sem, local_sem
        self.core, self.plane, self.spot = place_here()
        self.sends, self.keeps = [], []

    def send(self, other, goal, stays, piece, part, parts):
        source = self.source.at[2 * other + piece, goal, parts]
        target = self.target.at[self.core, self.spot, piece, parts]
        if stays:
            copy = pltpu.make_async_copy(source, target, self.local_sem.at[part, piece])
            self.keeps.append(copy)
        else:
            copy = remote(
                source,
                target,
                self.send_sem.at[len(self.sends)],
                self.recv_sem.at[self.core, self.spot, piece, part],
                (other, rank_of(self.plane, goal)),
            )
            self.sends.append(copy)
        copy.start()

    def finish(self, parts_of):
        for side, other, goal, stays in inward_targets(self.core, self.spot):
            if stays:
                continue
            for piece in range(PIECES):
                for part, parts in enumerate(parts_of[0 if other is self.core else 1]):
                    target = self.target.at[other, goal, piece, parts]
                    remote(
                        target,
                        target,
                        self.send_sem.at[0],
                        self.recv_sem.at[other, goal, piece, part],
                        (self.core, rank_of(self.plane, self.spot)),
                    ).wait_recv()
        for copy in self.sends:
            copy.wait_send()
        for copy in self.keeps:
            copy.wait()


KEYS_A, QUERIES, KEYS_B = range(3)


def plane_attend_back_kernel(*refs):
    table_ref, sorted_ref, qk_ref, shared_ref, near_grad_ref, far_grad_ref, lse_ref, hidden_ref = (
        refs[:8]
    )
    sources, half_up_ref, half_down_ref, refs = refs[8:11], refs[11], refs[12], refs[13:]
    sources = list(sources[:2]) + [sources[2].at[number] for number in range(LATE)]
    back_ref, far_back_ref, hidden_out_ref, t_out_ref, t_up_ref, t_down_ref = refs[:6]
    count = 2 + LATE
    refs = refs[6:]
    buffers, mines, refs = refs[: 3 * count], refs[3 * count : 4 * count], refs[4 * count :]
    part_out_ref, part_up_ref, part_down_ref, far_out_ref, far_up_ref, far_down_ref = refs[:6]
    grad_ref, packed_ref, out_ref, sums_ref, shares_ref, walked_ref, sibling_ref = refs[6:13]
    pack_ref, scores_refs, refs = refs[13], refs[14:18], refs[18:]
    reduce_send, reduce_recv, far_send, far_recv, load_sem = refs[:5]
    grad_sems, back_sems, move_sems, sibling_sems = refs[5:8], refs[8:11], refs[11:14], refs[14:16]
    pack_send, pack_recv = refs[16:18]

    local = qk_ref.shape[3]
    groups = PLANES * SPOTS
    blocks = groups * local
    core, plane, spot = place_here()
    low = low_lanes(BLOCK)
    masks = [half_mask(True), half_mask(False)]

    greet(both_partners(core, plane, spot))
    grads = Outward(near_grad_ref, far_grad_ref, grad_ref, packed_ref, *grad_sems)
    reduces = [
        SpotReduce(
            source,
            *buffers[3 * number : 3 * number + 3],
            reduce_send.at[number],
            reduce_recv.at[number],
            rows=FF // RANKS if number >= 2 else None,
            mine=mine,
        )
        for number, (source, mine) in enumerate(zip(sources, mines))
    ]
    ready = PER_STAGE * EARLY
    loads = [
        pltpu.make_async_copy(one.half(core), mine, load_sem.at[number])
        for number, (one, mine) in enumerate(zip(reduces, mines))
    ] + [
        pltpu.make_async_copy(half_up_ref, part_up_ref.at[0:ready], load_sem.at[count]),
        pltpu.make_async_copy(half_down_ref, part_down_ref.at[0:EARLY], load_sem.at[count + 1]),
    ]
    for one in reduces:
        one.start()
    for copy in loads:
        copy.start()

    def far(bits, number, source, target):
        return remote(
            source,
            target,
            far_send.at[number, bits - 1],
            far_recv.at[number, bits - 1],
            (core, rank_of(flip(plane, bits), spot)),
        )

    def far_down(bits, source):
        return far(bits, 3, source, far_down_ref.at[bits - 1])

    fars = []
    for bits in range(1, PLANES):
        goal = flip(plane, bits)
        copy = far(bits, 0, half_up_ref.at[:, goal], far_up_ref.at[bits - 1, 0:ready])
        copy.start()
        fars.append(copy)

        @pl.when(goal < EARLY)
        def _(bits=bits, goal=goal):
            far_down(bits, half_down_ref.at[jnp.minimum(goal, EARLY - 1)]).start()

    finish_hidden = from_planes(hidden_ref, hidden_out_ref, *move_sems)

    def load(component, block):
        rank, number = lax.div(block, local), lax.rem(block, local)
        if component == 2:
            return shared_ref[lax.div(rank, SPOTS), lax.rem(rank, SPOTS), number]
        return qk_ref[lax.div(rank, SPOTS), lax.rem(rank, SPOTS), component, number]

    def load_grad(block):
        rank = lax.div(block, local)
        return grad_ref[lax.div(rank, SPOTS), lax.rem(rank, SPOTS), lax.rem(block, local)]

    def store(component, block, value):
        rank = lax.div(block, local)
        out_ref[
            lax.div(rank, SPOTS), lax.rem(rank, SPOTS), component, lax.rem(block, local)
        ] = value.astype(BF16)

    def stored(component, block):
        rank = lax.div(block, local)
        return out_ref[
            lax.div(rank, SPOTS), lax.rem(rank, SPOTS), component, lax.rem(block, local)
        ].astype(F32)

    nothing = jnp.zeros((BLOCK, LANES), F32)

    def clear(block, carry):
        for slot in range(2):
            sums_ref[slot, block] = nothing
        return carry

    lax.fori_loop(0, blocks, clear, 0)

    def picked(block, number):
        return table_ref[0, block * RANDOM + number]

    def one_block(block, slot):
        ids, bias = inner_slots(picked, block, blocks)
        keys = jnp.concatenate([load(1 + slot, number) for number in ids], axis=0)
        both = jnp.concatenate(
            [load(0, block) * masks[slot], load_grad(block) * masks[1 - slot]], axis=0
        )
        products = dot_rt(both, keys)
        logs = lse_ref[block][:, slot * HEAD_DIM : slot * HEAD_DIM + 1]
        weights = jnp.exp(products[:BLOCK] + bias - logs)
        grad_weights = products[BLOCK:]
        delta = jnp.sum(weights * grad_weights, axis=1, keepdims=True)
        grad_scores = weights * (grad_weights - delta)
        stacked = jnp.concatenate([grad_scores, weights], axis=0).astype(BF16)
        return dot(stacked[:BLOCK], keys), dot_lt(stacked, both)

    fixed = 5

    def rank_blocks(rank, slot):
        first = rank * local
        results = [one_block(first + number, slot) for number in range(local)]

        def share(number, place):
            return results[number][1][place * BLOCK : (place + 1) * BLOCK]

        for shift in range(-1, local + 1):
            parts = [
                share(number, shift - number + 1)
                for number in range(local)
                if 0 <= shift - number + 1 <= 2
            ]
            target = jnp.minimum(jnp.maximum(first + shift, 0), blocks - 1)
            sums_ref[slot, target] += functools.reduce(jnp.add, parts)
        for place, target in ((3, 0), (4, blocks - 1)):
            sums_ref[slot, target] += functools.reduce(
                jnp.add, [share(number, place) for number in range(local)]
            )
        for number in range(local):
            for pick in range(RANDOM):
                shares_ref[slot, (first + number) * RANDOM + pick] = share(number, fixed + pick)
        return [result[0] for result in results]

    def head_a(side):
        def body(number, carry):
            rank = number * SPOTS + flip(spot, side)
            for place, query in enumerate(rank_blocks(rank, 0)):
                store(QUERIES, rank * local + place, query * SCALE)
            return carry

        lax.fori_loop(0, PLANES, body, 0)

    def head_b(number, carry):
        rank = core * (groups // 2) + number
        for place, query in enumerate(rank_blocks(rank, 1)):
            block = rank * local + place
            store(QUERIES, block, jnp.where(low, stored(QUERIES, block), query * SCALE))
        return carry

    spans = blocks // SPAN
    ends = (0, blocks - 1)

    def dense(slot, p_ref, d_ref, numbers):
        both = jnp.concatenate(
            [load(0, number) * masks[slot] for number in numbers]
            + [load_grad(number) * masks[1 - slot] for number in numbers],
            axis=0,
        )
        rows = len(numbers) * BLOCK
        column = slot * HEAD_DIM
        logs = jnp.concatenate(
            [lse_ref[number][:, column : column + 1] for number in numbers], axis=0
        )

        def keys_at(span):
            return jnp.concatenate(
                [load(1 + slot, span * SPAN + number) for number in range(SPAN)], axis=0
            )

        def first_pass(span, delta):
            products = dot_rt(both, keys_at(span))
            weights = jnp.exp(products[:rows] - logs)
            grad_weights = products[rows:]
            p_ref[span] = weights
            d_ref[span] = grad_weights
            return delta + jnp.sum(weights * grad_weights, axis=1, keepdims=True)

        delta = lax.fori_loop(0, spans, first_pass, jnp.zeros((rows, 1), F32), unroll=2)

        def second_pass(span, total):
            weights = p_ref[span]
            grad_scores = weights * (d_ref[span] - delta)
            stacked = jnp.concatenate([grad_scores, weights], axis=0).astype(BF16)
            shares = dot_lt(stacked, both)
            for number in range(SPAN):
                sums_ref[slot, span * SPAN + number] += shares[
                    number * BLOCK : (number + 1) * BLOCK
                ]
            return total + dot(stacked[:rows], keys_at(span))

        total = lax.fori_loop(0, spans, second_pass, jnp.zeros((rows, LANES), F32), unroll=2)
        for place, number in enumerate(numbers):
            query = total[place * BLOCK : (place + 1) * BLOCK] * SCALE
            if slot == 1:
                query = jnp.where(low, stored(QUERIES, number), query)
            store(QUERIES, number, query)

    def walk(slot, length):
        def body(number, total):
            entry = sorted_ref[2 * slot, number]
            earlier = sorted_ref[2 * slot, jnp.maximum(number - 1, 0)]
            keep = jnp.where(table_ref[0, entry] == table_ref[0, earlier], 1.0, 0.0).astype(F32)
            total = total * keep + shares_ref[slot, entry]
            walked_ref[slot, number] = total.astype(BF16)
            return total

        lax.fori_loop(0, length, body, nothing, unroll=4)

    def close(slot, rank, component):
        def body(number, carry):
            block = rank * local + number
            stop = sorted_ref[2 * slot + 1, block]
            start = jnp.where(block == 0, 0, sorted_ref[2 * slot + 1, jnp.maximum(block - 1, 0)])
            some = jnp.where(stop > start, 1.0, 0.0).astype(F32)
            share = walked_ref[slot, jnp.maximum(stop - 1, 0)].astype(F32)
            store(component, block, sums_ref[slot, block] + share * some)
            return carry

        lax.fori_loop(0, local, body, 0, unroll=True)

    back = Inward(out_ref, back_ref, *back_sems)
    own_parts = (slice(0, 1), slice(1, 2), slice(2, 3))
    far_parts = (slice(0, 1),)
    packs = []

    for side in range(SPOTS):
        grads.arrive(side)
        head_a(side)
        if side == 0:
            for copy in loads:
                copy.wait()
            for one in reduces:
                one.corners()
        if side == 1:
            for one in reduces:
                one.sides()
    reduces[0].close(part_out_ref)
    reduces[1].close(part_up_ref.at[ready : PER_STAGE * STAGES])
    for number in range(LATE):
        reduces[2 + number].close(part_down_ref.at[EARLY + number])
    for bits in range(1, PLANES):
        goal = flip(plane, bits)
        late = slice(ready, PER_STAGE * STAGES)
        for copy in (
            far(bits, 1, part_out_ref.at[:, goal], far_out_ref.at[bits - 1]),
            far(bits, 2, part_up_ref.at[late, goal], far_up_ref.at[bits - 1, late]),
        ):
            copy.start()
            fars.append(copy)

        @pl.when(goal >= EARLY)
        def _(bits=bits, goal=goal):
            far_down(bits, part_down_ref.at[goal]).start()

        fars.append(far_down(bits, part_down_ref.at[goal]))
    dense(0, scores_refs[0], scores_refs[1], ends)
    walk(0, blocks * RANDOM)
    for side, other, goal, stays in inward_targets(core, spot):
        for piece in range(PIECES):
            close(0, (2 * other + piece) * SPOTS + goal, KEYS_A)
            if other is core:
                back.send(other, goal, stays, piece, 0, own_parts[0])
            else:
                back.send(other, goal, stays, piece, 0, far_parts[0])
                pack_halves(
                    lambda number, other=other, goal=goal, piece=piece: out_ref[
                        2 * other + piece, goal, QUERIES, number
                    ],
                    pack_ref,
                    (piece, goal),
                    local,
                    low,
                    0,
                )
                copy = remote(
                    pack_ref.at[piece, goal],
                    far_back_ref.at[spot, piece],
                    pack_send.at[piece, side],
                    pack_recv.at[spot, piece],
                    (other, rank_of(plane, goal)),
                )
                copy.start()
                packs.append(copy)
    lax.fori_loop(0, groups // 2, head_b, 0)
    dense(1, scores_refs[2], scores_refs[3], (core * (blocks - 1),))
    for side, other, goal, stays in inward_targets(core, spot):
        if other is core:
            for piece in range(PIECES):
                back.send(other, goal, stays, piece, 1, own_parts[1])
    walk(1, blocks * RANDOM // 2)
    for number in range(PIECES):
        for goal in range(SPOTS):
            close(1, (2 * (1 - core) + number) * SPOTS + goal, KEYS_B)
    across = remote(
        out_ref.at[pl.ds(2 * (1 - core), PIECES), :, KEYS_B],
        sibling_ref,
        sibling_sems[0],
        sibling_sems[1],
        (1 - core, rank_of(plane, spot)),
    )
    across.start()
    for number in range(PIECES):
        for goal in range(SPOTS):
            close(1, (2 * core + number) * SPOTS + goal, KEYS_B)
    across.wait_recv()
    for side, other, goal, stays in inward_targets(core, spot):
        if other is core:
            for piece in range(PIECES):
                place = (2 * core + piece, goal, KEYS_B)
                out_ref[place] = (
                    out_ref[place].astype(F32) + sibling_ref[piece, goal].astype(F32)
                ).astype(BF16)
                back.send(other, goal, stays, piece, 2, own_parts[2])
    for copy in fars:
        copy.wait()

    def total(part, far, index):
        value = part.astype(F32)
        for bits in range(PLANES - 1):
            value = value + far[(bits,) + index].astype(F32)
        return value

    t_out_ref[...] = total(part_out_ref[0, plane], far_out_ref, (0,))

    def close_up(number, carry):
        t_up_ref[number] = total(part_up_ref[number, plane], far_up_ref, (number,))
        return carry

    lax.fori_loop(0, PER_STAGE * STAGES, close_up, 0)
    t_down_ref[...] = total(part_down_ref[plane], far_down_ref, ())
    finish_hidden()
    grads.finish()
    across.wait_send()
    back.finish((own_parts, far_parts))
    for copy in packs:
        copy.wait_send()
    for goal in range(SPOTS):
        for piece in range(PIECES):
            target = far_back_ref.at[goal, piece]
            remote(
                target,
                target,
                pack_send.at[0, 0],
                pack_recv.at[goal, piece],
                (core, rank_of(plane, spot)),
            ).wait_recv()


def plane_attention_back(
    table, sorted_table, qk, shared, near, far, lse, hidden, sources, half_up, half_down
):
    local = qk.shape[3]
    blocks = PLANES * SPOTS * local
    spans = blocks // SPAN
    shard, rows = D // RANKS, FF // RANKS
    up_count = PER_STAGE * STAGES
    up_tail, out_tail = (2 * shard, LANES), (2 * shard, D // 2)
    buffers = block_scratch(1, *out_tail) + block_scratch(PER_STAGE * LATE, *up_tail)
    for _ in range(LATE):
        buffers += row_scratch(rows, D)
    count = 2 + LATE
    mines = [
        VMEM((1, PLANES, SPOTS) + out_tail, BF16),
        VMEM((PER_STAGE * LATE, PLANES, SPOTS) + up_tail, BF16),
    ] + [VMEM((SPOTS * rows, D), BF16)] * LATE
    parts = [
        VMEM((1, PLANES) + out_tail, BF16),
        VMEM((up_count, PLANES) + up_tail, BF16),
        VMEM((STAGES, rows, D), BF16),
        VMEM((PLANES - 1, 1) + out_tail, BF16),
        VMEM((PLANES - 1, up_count) + up_tail, BF16),
        VMEM((PLANES - 1, rows, D), BF16),
    ]
    tile = (local, BLOCK, LANES)
    wide = VMEM((spans, 2 * BLOCK, SPAN * BLOCK), F32)
    thin = VMEM((spans, BLOCK, SPAN * BLOCK), F32)
    dma = pltpu.SemaphoreType.DMA
    return pl.pallas_call(
        plane_attend_back_kernel,
        out_shape=(
            jax.ShapeDtypeStruct((2, SPOTS, PIECES, 3) + tile, BF16),
            jax.ShapeDtypeStruct((SPOTS, PIECES, local // 2, BLOCK, LANES), BF16),
            jax.ShapeDtypeStruct(hidden.shape, BF16),
            jax.ShapeDtypeStruct(out_tail, F32),
            jax.ShapeDtypeStruct((up_count,) + up_tail, F32),
            jax.ShapeDtypeStruct((rows, D), F32),
        ),
        in_specs=[
            whole(pltpu.SMEM),
            whole(pltpu.SMEM),
            whole(),
            whole(),
            whole(ANY),
            whole(ANY),
            whole(),
            whole(ANY),
        ]
        + [whole(ANY)] * 5,
        out_specs=(whole(ANY),) * 3 + (whole(),) * 3,
        scratch_shapes=buffers
        + mines
        + parts
        + [
            VMEM((PLANES, SPOTS) + tile, BF16),
            VMEM((PLANES, SPOTS, local // 2, BLOCK, LANES), BF16),
            VMEM((PLANES, SPOTS, 3) + tile, BF16),
            VMEM((2, blocks, BLOCK, LANES), F32),
            VMEM((2, blocks * RANDOM, BLOCK, LANES), F32),
            VMEM((2, blocks * RANDOM, BLOCK, LANES), BF16),
            VMEM((PIECES, SPOTS) + tile, BF16),
            VMEM((PIECES, SPOTS, local // 2, BLOCK, LANES), BF16),
            wide,
            wide,
            thin,
            thin,
            dma((count, SpotReduce.SEMS)),
            dma((count, SpotReduce.SEMS)),
            dma((4, PLANES - 1)),
            dma((4, PLANES - 1)),
            dma((count + 2,)),
        ]
        + exchange_sems((PLANES, SPOTS))
        + [
            dma((36,)),
            dma((2, SPOTS, PIECES, 3)),
            dma((3, PIECES)),
            dma((2,)),
            dma((2,)),
            dma((2,)),
            dma,
            dma,
            dma((PIECES, SPOTS)),
            dma((SPOTS, PIECES)),
        ],
        compiler_params=pltpu.CompilerParams(
            vmem_limit_bytes=62 * 1024 * 1024, collective_id=5, has_side_effects=True
        ),
        name="plane_attention_back",
    )(table, sorted_table, qk, shared, near, far, lse, hidden, *sources, half_up, half_down)


class PlaneGather:
    SENDS = 3 + 3 + 4 + 2

    def __init__(self, source, target, send_sem, column_sem, recv_sem, local_sem):
        self.source, self.target = source, target
        self.send_sem, self.column_sem, self.recv_sem = send_sem, column_sem, recv_sem
        self.core, self.plane, self.spot = place_here()
        self.sends = []
        self.own = pltpu.make_async_copy(
            source, target.at[self.core, self.plane, self.spot], local_sem
        )
        self.own.start()
        for bits in range(1, PLANES):
            copy = remote(
                source,
                target.at[self.core, self.plane, self.spot],
                send_sem.at[len(self.sends)],
                column_sem.at[self.plane],
                (self.core, rank_of(flip(self.plane, bits), self.spot)),
            )
            copy.start()
            self.sends.append(copy)

    def neighbour(self, bits):
        return (self.core, rank_of(self.plane, flip(self.spot, bits)))

    def sibling(self):
        return (1 - self.core, rank_of(self.plane, self.spot))

    def piece(self, core, planes, spot):
        return self.target.at[core, planes, spot]

    def send(self, planes, spot, part, goal):
        piece = self.piece(self.core, planes, spot)
        copy = remote(
            piece,
            piece,
            self.send_sem.at[len(self.sends)],
            self.recv_sem.at[self.core, spot, part],
            goal,
        )
        copy.start()
        self.sends.append(copy)

    def arrive(self, core, planes, spot, part):
        piece = self.piece(core, planes, spot)
        remote(
            piece,
            piece,
            self.send_sem.at[0],
            self.recv_sem.at[core, spot, part],
            (self.core, rank_of(self.plane, self.spot)),
        ).wait_recv()

    def columns(self):
        self.own.wait()
        for bits in range(1, PLANES):
            other = flip(self.plane, bits)
            shard = self.target.at[self.core, other, self.spot]
            remote(
                shard,
                shard,
                self.send_sem.at[0],
                self.column_sem.at[other],
                (self.core, rank_of(self.plane, self.spot)),
            ).wait_recv()
        for goal in (self.neighbour(1), self.neighbour(2), self.sibling()):
            self.send(slice(0, PLANES), self.spot, 0, goal)

    def forward(self):
        everything = slice(0, PLANES)
        for side in (1, 2):
            spot = flip(self.spot, side)
            self.arrive(self.core, everything, spot, 0)
            half = slice(0, 2) if side == 1 else slice(2, 4)
            self.send(half, spot, side - 1, self.neighbour(3 - side))
            self.send(everything, spot, 0, self.sibling())

    def corner(self):
        spot = flip(self.spot, 3)
        for part, half in enumerate((slice(0, 2), slice(2, 4))):
            self.arrive(self.core, half, spot, part)
            self.send(half, spot, part, self.sibling())

    def finish(self):
        for side in range(3):
            self.arrive(1 - self.core, slice(0, PLANES), flip(self.spot, side), 0)
        for part, half in enumerate((slice(0, 2), slice(2, 4))):
            self.arrive(1 - self.core, half, flip(self.spot, 3), part)
        for copy in self.sends:
            copy.wait_send()


class CrossGather:
    SENDS = 2 + 1 + 3 + 3 * 4

    def __init__(self, source, target, send_sem, spot_sem, recv_sem, local_sem):
        self.target = target
        self.send_sem, self.spot_sem, self.recv_sem = send_sem, spot_sem, recv_sem
        self.core, self.plane, self.spot = place_here()
        self.sends = []
        self.own = pltpu.make_async_copy(
            source, target.at[self.core, self.plane, self.spot], local_sem
        )
        self.own.start()
        for side in (1, 2):
            self.pass_on(source, self.spot, flip(self.spot, side))

    def push(self, source, target, recv_sem, device):
        copy = remote(source, target, self.send_sem.at[len(self.sends)], recv_sem, device)
        copy.start()
        self.sends.append(copy)

    def pass_on(self, source, spot, goal):
        self.push(
            source,
            self.target.at[self.core, self.plane, spot],
            self.spot_sem.at[spot],
            (self.core, rank_of(self.plane, goal)),
        )

    def await_spot(self, spot):
        shard = self.target.at[self.core, self.plane, spot]
        remote(
            shard,
            shard,
            self.send_sem.at[0],
            self.spot_sem.at[spot],
            (self.core, rank_of(self.plane, self.spot)),
        ).wait_recv()

    def across(self):
        beside, beyond = flip(self.spot, 1), flip(self.spot, 2)
        for side in (1, 2):
            self.await_spot(flip(self.spot, side))
        spot = beside * (1 - self.core) + beyond * self.core
        goal = beyond * (1 - self.core) + beside * self.core
        self.pass_on(self.target.at[self.core, self.plane, spot], spot, goal)

    def blocks(self):
        self.own.wait()
        self.await_spot(flip(self.spot, 3))
        self.maybe = []
        self.along(self.plane, 1, self.plane < PLANES - 1)
        self.along(self.plane, -1, self.plane > 0)
        self.to_sibling(self.plane, self.plane >= 0)

    def along(self, plane, step, wanted):
        block = self.target.at[self.core, plane]
        copy = remote(
            block,
            block,
            self.send_sem.at[3 + len(self.maybe)],
            self.recv_sem.at[self.core, plane],
            (self.core, rank_of(self.plane + step, self.spot)),
        )
        self.begin(copy, wanted)

    def to_sibling(self, plane, wanted):
        block = self.target.at[self.core, plane]
        copy = remote(
            block,
            block,
            self.send_sem.at[3 + len(self.maybe)],
            self.recv_sem.at[self.core, plane],
            (1 - self.core, rank_of(self.plane, self.spot)),
        )
        self.begin(copy, wanted)

    def begin(self, copy, wanted):
        self.maybe.append((copy, wanted))

        @pl.when(wanted)
        def _():
            copy.start()

    def arrive(self, core, plane):
        block = self.target.at[core, plane]
        remote(
            block,
            block,
            self.send_sem.at[0],
            self.recv_sem.at[core, plane],
            (self.core, rank_of(self.plane, self.spot)),
        ).wait_recv()

    def hop(self, distance):
        for step in (1, -1):
            origin = self.plane - step * distance
            here = (origin >= 0) & (origin < PLANES)
            onward = self.plane + step
            more = here & (onward >= 0) & (onward < PLANES)

            @pl.when(here)
            def _(origin=origin):
                self.arrive(self.core, origin)

            self.along(origin, step, more)
            self.to_sibling(origin, here)

    def finish(self):
        for bits in range(PLANES):
            self.arrive(1 - self.core, flip(self.plane, bits))
        for copy in self.sends:
            copy.wait_send()
        for copy, wanted in self.maybe:

            @pl.when(wanted)
            def _(copy=copy):
                copy.wait_send()


def pair_of_blocks(read, first, second):
    low = low_lanes(1)
    tiles = []
    for block, wanted in ((first, 0), (second, 1)):
        tile = read(block // 2)
        tiles.append(tile if block % 2 == wanted else swap_halves(tile))
    return jnp.where(low, tiles[0], tiles[1])


def fold_tiles(target_ref, start, tiles, read):
    half = len(tiles) // 2
    for number in range(half):
        columns = slice((start + number) * LANES, (start + number + 1) * LANES)
        target_ref[:, columns] = jnp.concatenate(
            [read(tiles[number]), read(tiles[half + number])], axis=0
        ).astype(BF16)


VECTORS = 8


def lay_vectors(vecs_ref, vectors_ref, up_ref):
    rows = vecs_ref.shape[3]
    own, wide = D // RANKS, FF // RANKS
    values = vecs_ref[...].reshape(RANKS, rows, LANES).astype(F32)

    def spread_out(count, width):
        place = lax.broadcasted_iota(jnp.int32, (LANES, count), 1)
        lane = lax.broadcasted_iota(jnp.int32, (LANES, count), 0)
        start = lax.div(place, width) * width
        return jnp.where(place - start == lane, 1.0, 0.0).astype(BF16)

    laid = dot(vecs_ref[...].reshape(RANKS * rows, LANES), spread_out(D, own))
    owner = lax.broadcasted_iota(jnp.int32, (RANKS, 1, D), 0)
    column = lax.broadcasted_iota(jnp.int32, (RANKS, 1, D), 2)
    laid = jnp.where(lax.div(column, own) == owner, laid.reshape(RANKS, rows, D), 0.0)
    vectors_ref[...] = jnp.sum(laid, axis=0)[:VECTORS]
    row = lax.broadcasted_iota(jnp.int32, (1, rows, LANES), 1)
    last = jnp.sum(jnp.where(row == VECTORS, values, 0.0), axis=1)
    laid = dot(last.astype(BF16), spread_out(FF, wide))
    owner = lax.broadcasted_iota(jnp.int32, (RANKS, FF), 0)
    column = lax.broadcasted_iota(jnp.int32, (RANKS, FF), 1)
    laid = jnp.sum(jnp.where(lax.div(column, wide) == owner, laid, 0.0), axis=0, keepdims=True)
    for chunk in range(FF // CHUNK):
        for side in range(2):
            start = side * (FF // 2) + chunk * LANES
            up_ref[chunk, :, side * LANES : (side + 1) * LANES] = laid[:, start : start + LANES]


def lay_table(tables_ref, core, micro, entries):
    count = 2 * LANES
    ranks = PLANES * SPOTS
    values = tables_ref[core].reshape(ranks, tables_ref.shape[3], LANES).astype(F32)
    row = lax.broadcasted_iota(jnp.int32, (1, tables_ref.shape[3], LANES), 1)
    values = jnp.sum(jnp.where(row == micro, values, 0.0), axis=1)
    place = lax.broadcasted_iota(jnp.int32, (LANES, count), 1)
    lane = lax.broadcasted_iota(jnp.int32, (LANES, count), 0)
    start = lax.div(place, entries) * entries
    laid = dot(values.astype(BF16), jnp.where(place - start == lane, 1.0, 0.0).astype(BF16))
    owner = lax.broadcasted_iota(jnp.int32, (ranks, count), 0)
    column = lax.broadcasted_iota(jnp.int32, (ranks, count), 1)
    laid = jnp.sum(jnp.where(lax.div(column, entries) == owner, laid, 0.0), axis=0, keepdims=True)
    column = lax.broadcasted_iota(jnp.int32, (1, count), 1)
    return jnp.where(column < ranks * entries, laid, 2.0 * LANES)


def front_kernel(
    x_in_ref,
    dy_ref,
    vec_ref,
    tab_ref,
    w_qkv_in_ref,
    w_out_in_ref,
    w_up_in_ref,
    w_down_in_ref,
    back_ref,
    far_back_ref,
    x_ref,
    dys_ref,
    w_down_ref,
    w_qkv_hbm,
    w_out_hbm,
    w_up_hbm,
    qk_hbm,
    shared_hbm,
    normed_ref,
    lse_ref,
    vectors_ref,
    up_ref,
    table_ref,
    sorted_ref,
    s_qkv_ref,
    s_ou_ref,
    g_qkv_ref,
    g_ou_ref,
    w_qkv_ref,
    w_out_ref,
    w_up_ref,
    xs_ref,
    vecs_ref,
    tabs_ref,
    bias_ref,
    send_ref,
    qk_ref,
    shared_ref,
    out_ref,
    pack_ref,
    p_ref,
    q_ref,
    picks_ref,
    *sems,
):
    gather_send, gather_recv, gather_local = sems[:3]
    plane_sems, cross_sems = sems[3:7], sems[7:11]
    x_sems, dy_sems = sems[11:14], sems[14:17]
    qkv_send, qkv_recv, qkv_local, shared_send, shared_recv = sems[17:22]
    back_send, back_recv, back_local, far_send, far_recv, local_sem = sems[22:28]
    core, plane, spot = place_here()
    micro, rows, _ = x_in_ref.shape
    tokens = PIECES * rows
    local = rows // BLOCK
    blocks = PLANES * SPOTS * local

    barrier = pltpu.get_barrier_semaphore()
    partners = both_partners(core, plane, spot)
    for partner in partners:
        pl.semaphore_signal(barrier, inc=1, device_id=partner, device_id_type=MESH)

    def natural(ref):
        return lambda tile: ref[:, tile * LANES : (tile + 1) * LANES].astype(F32)

    order = [natural_block(entry) for entry in column_order()]
    read = natural(w_qkv_in_ref)
    fold_tiles(
        s_qkv_ref,
        0,
        list(range(TILES)),
        lambda tile: pair_of_blocks(read, order[2 * tile], order[2 * tile + 1]),
    )
    pl.semaphore_wait(barrier, len(partners))

    gathers = []
    for number, (source, target) in enumerate(
        ((tab_ref, tabs_ref), (vec_ref, vecs_ref), (s_qkv_ref, g_qkv_ref))
    ):
        one = Gather(
            source, target, gather_send.at[number], gather_recv.at[number], gather_local.at[number]
        )
        one.start()
        gathers.append(one)
    outs = D // LANES // 2
    fold_tiles(s_ou_ref, 0, list(range(D // LANES)), natural(w_out_in_ref))
    fold_tiles(s_ou_ref, outs, list(range(FF // LANES)), natural(w_up_in_ref))
    for one in gathers:
        one.column()
    finish_x = to_planes(x_in_ref, xs_ref, *x_sems)
    cross = CrossGather(w_down_in_ref, w_down_ref, *cross_sems)
    for one in gathers:
        one.across()
    for one in gathers:
        one.corner()
    cross.across()
    for one in gathers[:2]:
        one.finish()
    window_core, window_micro = lax.rem(plane, 2), lax.div(plane, 2)
    scalars = pltpu.make_async_copy(tabs_ref.at[window_core], picks_ref, local_sem.at[1])
    scalars.start()
    lay_vectors(vecs_ref, vectors_ref, up_ref)
    for tile in range(TILES):
        halves = []
        for entry in column_order()[2 * tile : 2 * tile + 2]:
            halves.append(entry)

        def bias_tile(number, halves=halves):
            if number < D // LANES:
                return vectors_ref[2:3, number * LANES : (number + 1) * LANES]
            if number < 2 * D // LANES:
                return jnp.zeros((1, LANES), F32)
            start = (number - 2 * D // LANES) * LANES
            return vectors_ref[3:4, start : start + LANES]

        chunk, side = tile % HALF_TILES, tile // HALF_TILES
        start = chunk * CHUNK + side * LANES
        bias_ref[:, start : start + LANES] = pair_of_blocks(
            bias_tile, order[2 * tile], order[2 * tile + 1]
        )
    gathers[2].finish()
    settle(g_qkv_ref, [(tile, w_qkv_ref, alternate(tile)) for tile in range(HALF_TILES)])
    keep_w = pltpu.make_async_copy(w_qkv_ref, w_qkv_hbm, local_sem.at[2])
    keep_w.start()

    spread = PlaneGather(s_ou_ref, g_ou_ref, *plane_sems)
    finish_x()
    keep_x = pltpu.make_async_copy(xs_ref, x_ref, local_sem.at[0])
    keep_x.start()
    normal, _ = norm_parts(xs_ref[...].reshape(tokens, D).astype(F32))
    normed_ref[...] = (normal * vectors_ref[0:1] + vectors_ref[1:2]).astype(BF16)

    def shaped(value):
        return value.astype(BF16).reshape(local, BLOCK, LANES)

    low = low_lanes(rows)
    queries = D // LANES
    for chunk in range(HALF_TILES):
        columns = slice(chunk * CHUNK, (chunk + 1) * CHUNK)
        packed = dot(normed_ref[...], w_qkv_ref[:, columns]) + bias_ref[:, columns]
        for side in range(2):
            tile = chunk + side * HALF_TILES
            whole_tile = packed[:, side * LANES : (side + 1) * LANES]
            if tile < queries:
                whole_tile = whole_tile.astype(BF16).astype(F32) * SCALE
            for piece in range(PIECES):
                part = whole_tile[piece * rows : (piece + 1) * rows]
                if tile < SPOTS:
                    send_ref[0, tile, piece, 0] = shaped(part)
                elif tile < queries:
                    first = 2 * (tile - SPOTS)
                    shared = send_ref[0, first, piece, 0].reshape(rows, LANES).astype(F32)
                    send_ref[1, first, piece, 0] = shaped(jnp.where(low, part, shared))
                    shared = send_ref[0, first + 1, piece, 0].reshape(rows, LANES).astype(F32)
                    send_ref[1, first + 1, piece, 0] = shaped(
                        jnp.where(low, swap_halves(part), shared)
                    )
                else:
                    goal, role = (tile - queries) // 3, (tile - queries) % 3
                    if role < 2:
                        send_ref[role, goal, piece, 1] = shaped(part)
                    else:
                        send_ref[0, goal, piece, 2] = shaped(part)
    sends, keeps = [], []
    for part, (parts, landing) in enumerate(((slice(0, 2), qk_ref), (2, shared_ref))):
        for side in (3, 1, 2, 0):
            for other in (core, 1 - core) if part == 0 else (core,):
                goal = flip(spot, side)
                for piece in range(PIECES):
                    source = send_ref.at[other if part == 0 else 0, goal, piece, parts]
                    target = landing.at[2 * core + piece, spot]
                    if side == 0 and other is core:
                        copy = pltpu.make_async_copy(source, target, qkv_local.at[part, piece])
                        keeps.append((part, copy))
                    else:
                        copy = remote(
                            source,
                            target,
                            qkv_send.at[len(sends)],
                            qkv_recv.at[2 * core + piece, spot, part],
                            (other, rank_of(plane, goal)),
                        )
                        sends.append(copy)
                    copy.start()
    spread.columns()
    cross.blocks()
    table = lay_table(tabs_ref, window_core, window_micro, local * RANDOM)
    table_ref[...] = table.astype(jnp.int32)
    sort_entries(table, sorted_ref, blocks * RANDOM)
    scalars.wait()

    def arrive(part, other, piece, goal):
        target = (qk_ref, shared_ref)[part].at[2 * other + piece, goal]
        remote(
            target,
            target,
            qkv_send.at[0],
            qkv_recv.at[2 * other + piece, goal, part],
            (core, rank_of(plane, spot)),
        ).wait_recv()

    for side in range(SPOTS):
        for other in (core, 1 - core):
            if side > 0 or other is not core:
                for piece in range(PIECES):
                    arrive(0, other, piece, flip(spot, side))
    for part, copy in keeps:
        copy.wait()
    cross.hop(1)

    low = low_lanes(BLOCK)
    masks = [half_mask(True), half_mask(False)]

    def tile_of(component, block):
        rank, number = lax.div(block, local), lax.rem(block, local)
        if component == 2:
            return shared_ref[lax.div(rank, SPOTS), lax.rem(rank, SPOTS), number]
        return qk_ref[lax.div(rank, SPOTS), lax.rem(rank, SPOTS), component, number]

    def picked(block, number):
        rank = lax.div(block, local)
        return picks_ref[
            lax.div(rank, SPOTS),
            lax.rem(rank, SPOTS),
            window_micro,
            lax.rem(block, local) * RANDOM + number,
        ]

    def place_of(block):
        rank = lax.div(block, local)
        return lax.div(rank, SPOTS), lax.rem(rank, SPOTS), lax.rem(block, local)

    def put(block, slot, mixed, log):
        place = place_of(block)
        if slot == 0:
            out_ref[place] = mixed.astype(BF16)
            lse_ref[block] = jnp.where(low, log, 0.0)
        else:
            out_ref[place] = jnp.where(low, mixed, out_ref[place].astype(F32)).astype(BF16)
            lse_ref[block] = jnp.where(low, lse_ref[block], log)

    def one_block(block, slot):
        ids, bias = inner_slots(picked, block, blocks)
        keys = jnp.concatenate([tile_of(1 + slot, number) for number in ids], axis=0)
        scores = dot_rt(tile_of(0, block) * masks[slot], keys) + bias
        top = jnp.max(scores, axis=1, keepdims=True)
        powered = jnp.exp(scores - top)
        total = jnp.sum(powered, axis=1, keepdims=True)
        mixed = dot(powered.astype(BF16), keys) * (1.0 / total)
        return mixed, top + jnp.log(total)

    def rank_blocks(rank, slot):
        results = [one_block(rank * local + number, slot) for number in range(local)]
        for number, (mixed, log) in enumerate(results):
            put(rank * local + number, slot, mixed, log)

    spans = blocks // SPAN
    ends = (0, blocks - 1)

    def dense(slot, scores_ref, numbers):
        size = len(numbers) * BLOCK
        query = jnp.concatenate([tile_of(0, number) * masks[slot] for number in numbers], axis=0)

        def keys_at(span):
            return jnp.concatenate(
                [tile_of(1 + slot, span * SPAN + number) for number in range(SPAN)], axis=0
            )

        def first_pass(span, top):
            scores = dot_rt(query, keys_at(span))
            scores_ref[span] = scores
            return jnp.maximum(top, jnp.max(scores, axis=1, keepdims=True))

        top = lax.fori_loop(
            0, spans, first_pass, jnp.full((size, 1), NEGATIVE, F32), unroll=2
        )

        def second_pass(span, carry):
            total, mixed = carry
            powered = jnp.exp(scores_ref[span] - top)
            return (
                total + jnp.sum(powered, axis=1, keepdims=True),
                mixed + dot(powered.astype(BF16), keys_at(span)),
            )

        total, mixed = lax.fori_loop(
            0,
            spans,
            second_pass,
            (jnp.zeros((size, 1), F32), jnp.zeros((size, LANES), F32)),
            unroll=2,
        )
        mixed = mixed * (1.0 / total)
        log = top + jnp.log(total)
        for place, number in enumerate(numbers):
            span = slice(place * BLOCK, (place + 1) * BLOCK)
            put(number, slot, mixed[span], log[span])

    def head_a(number, carry):
        rank_blocks(number, 0)
        return carry

    def head_b(number, carry):
        rank_blocks(core * (PLANES * SPOTS // 2) + number, 1)
        return carry

    shared = []
    half_way = PLANES * SPOTS // 2
    lax.fori_loop(0, half_way, head_a, 0)
    for side in range(SPOTS):
        goal = flip(spot, side)
        for piece in range(PIECES):
            if side > 0:
                arrive(1, core, piece, goal)
            source = shared_ref.at[2 * core + piece, goal]
            copy = remote(
                source,
                source,
                shared_send.at[2 * side + piece],
                shared_recv.at[2 * core + piece, goal],
                (1 - core, rank_of(plane, spot)),
            )
            copy.start()
            shared.append(copy)
    finish_dy = to_planes(dy_ref, dys_ref, *dy_sems)
    lax.fori_loop(half_way, PLANES * SPOTS, head_a, 0)
    dense(0, p_ref, ends)
    spread.forward()
    backs, stay = [], []
    for side in (3, 1, 2, 0):
        goal = flip(spot, side)
        for piece in range(PIECES):
            pack_halves(
                lambda number, piece=piece, goal=goal: out_ref[
                    2 * (1 - core) + piece, goal, number
                ],
                pack_ref,
                (piece, goal),
                local,
                low,
                1,
            )
            copy = remote(
                pack_ref.at[piece, goal],
                far_back_ref.at[spot, piece],
                far_send.at[piece, side],
                far_recv.at[spot, piece],
                (1 - core, rank_of(plane, goal)),
            )
            copy.start()
            backs.append(copy)
    for side in range(SPOTS):
        for piece in range(PIECES):
            target = shared_ref.at[2 * (1 - core) + piece, flip(spot, side)]
            remote(
                target,
                target,
                shared_send.at[0],
                shared_recv.at[2 * (1 - core) + piece, flip(spot, side)],
                (core, rank_of(plane, spot)),
            ).wait_recv()
    cross.hop(2)
    keep_qk = pltpu.make_async_copy(qk_ref, qk_hbm, local_sem.at[3])
    keep_qk.start()
    keep_shared = pltpu.make_async_copy(shared_ref, shared_hbm, local_sem.at[6])
    keep_shared.start()
    lax.fori_loop(0, half_way, head_b, 0)
    dense(1, q_ref, (core * (blocks - 1),))
    spread.corner()
    for side in (3, 1, 2, 0):
        goal = flip(spot, side)
        for piece in range(PIECES):
            source, target = out_ref.at[2 * core + piece, goal], back_ref.at[spot, piece]
            if side == 0:
                copy = pltpu.make_async_copy(source, target, back_local.at[piece])
                stay.append(copy)
            else:
                copy = remote(
                    source,
                    target,
                    back_send.at[piece, side],
                    back_recv.at[spot, piece],
                    (core, rank_of(plane, goal)),
                )
                backs.append(copy)
            copy.start()
    cross.hop(3)
    spread.finish()
    settle(
        g_ou_ref,
        [(tile, w_out_ref, (tile, outs + tile)) for tile in range(outs)]
        + [(outs + tile, w_up_ref, alternate(tile)) for tile in range(FF // CHUNK)],
    )
    keep_out = pltpu.make_async_copy(w_out_ref, w_out_hbm, local_sem.at[4])
    keep_out.start()
    keep_up = pltpu.make_async_copy(w_up_ref, w_up_hbm, local_sem.at[5])
    keep_up.start()
    cross.finish()
    finish_dy()
    for copy in sends:
        copy.wait_send()
    for copy in shared:
        copy.wait_send()
    for side in range(SPOTS):
        goal = flip(spot, side)
        for piece in range(PIECES):
            here = (core, rank_of(plane, spot))
            if side > 0:
                target = back_ref.at[goal, piece]
                remote(target, target, back_send.at[0, 0], back_recv.at[goal, piece], here).wait_recv()
            target = far_back_ref.at[goal, piece]
            remote(target, target, far_send.at[0, 0], far_recv.at[goal, piece], here).wait_recv()
    for copy in backs:
        copy.wait_send()
    for copy in stay:
        copy.wait()
    for copy in (keep_x, keep_w, keep_qk, keep_shared, keep_out, keep_up):
        copy.wait()


def front(x, dy, vec, tab, w_qkv, w_out, w_up, w_down):
    micro, rows, _ = x.shape
    tokens = PIECES * rows
    local = rows // BLOCK
    blocks = PLANES * SPOTS * local
    spans = blocks // SPAN
    grid = (2, PLANES, SPOTS)
    shard = D // RANKS
    tile = (local, BLOCK, LANES)
    dma = pltpu.SemaphoreType.DMA
    struct = jax.ShapeDtypeStruct
    ou = (2 * shard, (D + FF) // 2)
    return pl.pallas_call(
        front_kernel,
        out_shape=(
            struct((SPOTS, PIECES) + tile, BF16),
            struct((SPOTS, PIECES, local // 2, BLOCK, LANES), BF16),
            struct(x.shape, BF16),
            struct(dy.shape, BF16),
            struct(grid + w_down.shape, BF16),
            struct((D, 3 * D), BF16),
            struct((D, D), BF16),
            struct((D, FF), BF16),
            struct((PLANES, SPOTS, 2) + tile, BF16),
            struct((PLANES, SPOTS) + tile, BF16),
            struct((tokens, D), BF16),
            struct((blocks, BLOCK, LANES), F32),
            struct((VECTORS, D), F32),
            struct((FF // CHUNK, 1, CHUNK), F32),
            struct((1, 2 * LANES), jnp.int32),
            struct((4, 2 * LANES), jnp.int32),
        ),
        in_specs=[
            whole(ANY),
            whole(ANY),
            whole(ANY),
            whole(ANY),
            whole(),
            whole(),
            whole(),
            whole(ANY),
        ],
        out_specs=(whole(ANY),) * 10 + (whole(),) * 6,
        scratch_shapes=[
            VMEM((2 * shard, 3 * D // 2), BF16),
            VMEM(ou, BF16),
            VMEM(grid + (2 * shard, 3 * D // 2), BF16),
            VMEM(grid + ou, BF16),
            VMEM((D, 3 * D), BF16),
            VMEM((D, D), BF16),
            VMEM((D, FF), BF16),
            VMEM((PIECES, rows, D), BF16),
            VMEM(grid + vec.shape, BF16),
            VMEM(grid + tab.shape, jnp.int32),
            VMEM((1, 3 * D), F32),
            VMEM((2, SPOTS, PIECES, 3) + tile, BF16),
            VMEM((PLANES, SPOTS, 2) + tile, BF16),
            VMEM((PLANES, SPOTS) + tile, BF16),
            VMEM((PLANES, SPOTS) + tile, BF16),
            VMEM((PIECES, SPOTS, local // 2, BLOCK, LANES), BF16),
            VMEM((spans, 2 * BLOCK, SPAN * BLOCK), F32),
            VMEM((spans, BLOCK, SPAN * BLOCK), F32),
            pltpu.SMEM((PLANES, SPOTS) + tab.shape, jnp.int32),
            dma((3, Gather.SENDS)),
            dma((3,) + grid),
            dma((3,)),
            dma((PlaneGather.SENDS,)),
            dma((PLANES,)),
            dma((2, SPOTS, 2)),
            dma,
            dma((CrossGather.SENDS,)),
            dma((SPOTS,)),
            dma((2, PLANES)),
            dma,
        ]
        + [dma((2,))] * 6
        + [
            dma((20,)),
            dma((PLANES, SPOTS, 2)),
            dma((2, PIECES)),
            dma((2 * SPOTS,)),
            dma((PLANES, SPOTS)),
            dma((PIECES, SPOTS)),
            dma((SPOTS, PIECES)),
            dma((PIECES,)),
            dma((PIECES, SPOTS)),
            dma((SPOTS, PIECES)),
            dma((7,)),
        ],
        compiler_params=pltpu.CompilerParams(
            vmem_limit_bytes=60 * 1024 * 1024, collective_id=1, has_side_effects=True
        ),
        name="front",
    )(x, dy, vec, tab, w_qkv, w_out, w_up, w_down)


class SpotReduce:
    SEMS = 4

    def __init__(self, source, near, corner, sides, send_sem, recv_sem, rows=None, mine=None):
        self.source, self.near, self.corner, self.side = source, near, corner, sides
        self.send_sem, self.recv_sem, self.rows, self.mine = send_sem, recv_sem, rows, mine
        self.core, self.plane, self.spot = place_here()
        beside, beyond = flip(self.spot, 1), flip(self.spot, 2)
        self.via = beyond * (1 - self.core) + beside * self.core
        self.other = beside * (1 - self.core) + beyond * self.core

    def half(self, core):
        return self.source.at[core] if self.rows else self.source.at[:, core]

    def part(self, spot):
        if self.rows:
            start = pl.multiple_of(spot * self.rows, 16)
            return self.near.at[pl.ds(start, self.rows)]
        return self.near.at[:, :, spot]

    def copy(self, number):
        sibling = (1 - self.core, rank_of(self.plane, self.spot))
        if number == 0:
            source, target, device = self.half(1 - self.core), self.near, sibling
        elif number == 1:
            source, target = self.part(flip(self.spot, 3)), self.corner
            device = (self.core, rank_of(self.plane, self.via))
        else:
            spot = flip(self.spot, number - 1)
            source, target = self.part(spot), self.side.at[number - 2]
            device = (self.core, rank_of(self.plane, spot))
        return remote(source, target, self.send_sem.at[number], self.recv_sem.at[number], device)

    def start(self):
        self.copy(0).start()

    def add(self, spot, terms, target=None):
        if self.rows:
            rows = self.rows

            def slab(number, carry):
                size = rows // 3
                first = pl.multiple_of(spot * rows + number * size, 16)
                place = pl.ds(first, size)
                inner = pl.ds(pl.multiple_of(number * size, 16), size)
                total = self.near[place].astype(F32)
                for read in terms:
                    total = total + read(place, inner).astype(F32)
                if target is None:
                    self.near[place] = total.astype(BF16)
                else:
                    target[inner] = total.astype(BF16)
                return carry

            lax.fori_loop(0, 3, slab, 0, unroll=True)
            return
        count = self.near.shape[0]

        def block(number, carry):
            first, plane = lax.div(number, PLANES), lax.rem(number, PLANES)
            total = self.near[first, plane, spot].astype(F32)
            for read in terms:
                total = total + read(first, plane).astype(F32)
            if target is None:
                self.near[first, plane, spot] = total.astype(BF16)
            else:
                target[first, plane] = total.astype(BF16)
            return carry

        lax.fori_loop(0, count * PLANES, block, 0, unroll=4)

    def corners(self):
        self.copy(0).wait_recv()
        core = self.core
        for spot in range(SPOTS):
            if self.rows and self.mine is None:
                self.add(spot, [lambda place, inner: self.source[core, place]])
            elif self.rows:
                self.add(spot, [lambda place, inner: self.mine[place]])
            elif self.mine is None:
                self.add(spot, [lambda first, plane, spot=spot: self.source[first, core, plane, spot]])
            else:
                self.add(spot, [lambda first, plane, spot=spot: self.mine[first, plane, spot]])
        self.copy(1).start()

    def sides(self):
        self.copy(1).wait_recv()
        if self.rows:
            self.add(self.other, [lambda place, inner: self.corner[inner]])
        else:
            self.add(self.other, [lambda first, plane: self.corner[first, plane]])
        self.copy(2).start()
        self.copy(3).start()

    def close(self, target):
        self.copy(2).wait_recv()
        self.copy(3).wait_recv()
        if self.rows:
            terms = [lambda place, inner, n=n: self.side[n, inner] for n in range(2)]
        else:
            terms = [lambda first, plane, n=n: self.side[n, first, plane] for n in range(2)]
        self.add(self.spot, terms, target)
        for number in range(self.SEMS):
            self.copy(number).wait_send()


def block_scratch(count, rows, width):
    return [
        VMEM((count, PLANES, SPOTS, rows, width), BF16),
        VMEM((count, PLANES, rows, width), BF16),
        VMEM((2, count, PLANES, rows, width), BF16),
    ]


def row_scratch(rows, width):
    return [
        VMEM((SPOTS * rows, width), BF16),
        VMEM((rows, width), BF16),
        VMEM((2, rows, width), BF16),
    ]


STAGES = 4
PER_STAGE = FF // CHUNK // STAGES
EARLY = 2
LATE = STAGES - EARLY
WAITS = (2, 4, 6)


def by_owner(out_ref, values):
    rows = D // RANKS
    width = values.shape[1] // 2
    for owner in range(RANKS):
        part = values[owner * rows : (owner + 1) * rows]
        out_ref[owner] = jnp.concatenate([part[:, :width], part[:, width:]], axis=0).astype(BF16)


def plane_middle_kernel(
    mixed_in_ref,
    far_in_ref,
    x_ref,
    dy_ref,
    vec_ref,
    w_out_ref,
    up_shift_ref,
    w_up_ref,
    w_down_ref,
    hidden_ref,
    send_ref,
    far_ref,
    dres_ref,
    g_out_ref,
    half_up_ref,
    half_down_ref,
    last_up_ref,
    last_down_ref,
    g_up_bias_ref,
    g_small_ref,
    mixed_ref,
    residual_ref,
    second_ref,
    second_t_ref,
    total_ref,
    dsecond_ref,
    g_up_ref,
    g_down_ref,
    *scratch,
):
    send_sem, recv_sem, local_sem = scratch[-3:]
    stages = []
    for number in range(EARLY):
        buffers = scratch[6 * number : 6 * number + 6]
        stages.append(
            (
                SpotReduce(
                    g_up_ref.at[PER_STAGE * number : PER_STAGE * (number + 1)],
                    *buffers[:3],
                    send_sem.at[number, 0],
                    recv_sem.at[number, 0],
                ),
                SpotReduce(
                    g_down_ref.at[number],
                    *buffers[3:],
                    send_sem.at[number, 1],
                    recv_sem.at[number, 1],
                    rows=FF // RANKS,
                ),
            )
        )
    pieces, rows, _ = x_ref.shape
    tokens = pieces * rows
    step = pl.program_id(0)
    low = low_lanes(rows)
    out_shift, gain, shift, down_shift = (vec_ref[number : number + 1] for number in (4, 5, 6, 7))

    @pl.when(step == 0)
    def _():
        core, plane, spot = place_here()
        greet(
            [
                (1 - core, rank_of(plane, spot)),
                (core, rank_of(plane, flip(spot, 1))),
                (core, rank_of(plane, flip(spot, 2))),
            ]
        )
        def received(spot, piece):
            own = mixed_in_ref[spot, piece].astype(F32)
            halves = far_in_ref[spot, piece].astype(F32)
            parts = []
            for number in range(rows // BLOCK // 2):
                part = halves[number * BLOCK : (number + 1) * BLOCK]
                parts += [part, swap_halves(part)]
            other = jnp.concatenate(parts, axis=0)
            return (jnp.where(core == 0, own, other), jnp.where(core == 0, other, own)), own

        for piece in range(pieces):
            span = slice(piece * rows, (piece + 1) * rows)
            for spot in (0, 2):
                first, own_first = received(spot, piece)
                last_two, own_last = received(spot + 1, piece)
                tiles = (
                    jnp.where(low, swap_halves(first[0]), first[1]),
                    jnp.where(low, own_first, last_two[0]),
                    swap_halves(jnp.where(low, own_last, last_two[1])),
                )
                for number, tile in enumerate(tiles):
                    spread = 3 * (spot // 2) + number
                    mixed_ref[span, spread * LANES : (spread + 1) * LANES] = tile.astype(BF16)
        residual = x_ref[...].reshape(tokens, D).astype(F32) + (
            dot(mixed_ref[...], w_out_ref[...]) + out_shift
        )
        residual_ref[...] = residual
        normal, _ = norm_parts(residual)
        second = normal * gain + shift
        second_ref[...] = second.astype(BF16)
        second_t_ref[...] = second.T.astype(BF16)
        total_ref[...] = jnp.zeros_like(total_ref)
        dsecond_ref[...] = jnp.zeros_like(dsecond_ref)

    w_down = w_down_ref[...].reshape(CHUNK, D)
    upper = dot(second_ref[...], w_up_ref[...]) + up_shift_ref[0]
    factor = 0.7978845608028654
    square = upper * upper
    bent = jnp.tanh(factor * (upper + 0.044715 * (upper * square)))
    middle_half = 0.5 * (1.0 + bent)
    active = (upper * middle_half).astype(BF16)
    slope = middle_half + 0.5 * upper * (1.0 - bent * bent) * (
        factor + (3.0 * 0.044715 * factor) * square
    )
    dy = dy_ref[...]
    total_ref[...] += dot(active, w_down)
    stage, turn = lax.div(step, PER_STAGE), lax.rem(step, PER_STAGE)
    down_share = dot_lt(active, dy).astype(BF16)
    place = pl.ds(pl.multiple_of(turn * LANES, LANES), LANES)
    for side in range(2):
        g_down_ref[stage, side, place] = down_share[side * LANES : (side + 1) * LANES]
    dupper = (dot_rt(dy, w_down) * slope).astype(BF16)
    g_up_bias_ref[0] = jnp.sum(dupper.astype(F32), axis=0, keepdims=True)
    up_share = dot(second_t_ref[...], dupper)
    shard = D // RANKS
    for owner in range(RANKS):
        part = up_share[owner * shard : (owner + 1) * shard]
        g_up_ref[step, owner // (PLANES * SPOTS), owner // SPOTS % PLANES, owner % SPOTS] = (
            jnp.concatenate([part[:, :LANES], part[:, LANES:]], axis=0).astype(BF16)
        )
    dsecond_ref[...] += dot_rt(dupper, w_up_ref[...])

    last = FF // CHUNK - 1
    for number, pair in enumerate(stages):
        done = PER_STAGE * (number + 1) - 1

        @pl.when(step == done)
        def _(pair=pair):
            for one in pair:
                one.start()

        @pl.when(step == done + WAITS[0])
        def _(pair=pair):
            for one in pair:
                one.corners()

        @pl.when(step == done + WAITS[1])
        def _(pair=pair):
            for one in pair:
                one.sides()

        if done + WAITS[2] < last:

            @pl.when(step == done + WAITS[2])
            def _(pair=pair, number=number):
                pair[0].close(half_up_ref.at[PER_STAGE * number : PER_STAGE * (number + 1)])
                pair[1].close(half_down_ref.at[number])

    @pl.when(step == last)
    def _():
        keep_up = pltpu.make_async_copy(
            g_up_ref.at[PER_STAGE * EARLY : PER_STAGE * STAGES], last_up_ref, local_sem.at[0]
        )
        keep_up.start()
        keep_down = pltpu.make_async_copy(
            g_down_ref.at[EARLY:STAGES], last_down_ref, local_sem.at[1]
        )
        keep_down.start()
        residual = residual_ref[...]
        hidden_ref[...] = (
            (residual + (total_ref[...] + down_shift)).astype(BF16).reshape(x_ref.shape)
        )
        normal, inverse = norm_parts(residual)
        dsecond = dsecond_ref[...]
        grad_out = dy_ref[...].astype(F32)
        g_small_ref[0:1] = jnp.sum(dsecond * normal, axis=0, keepdims=True)
        g_small_ref[1:2] = jnp.sum(dsecond, axis=0, keepdims=True)
        g_small_ref[2:3] = jnp.sum(grad_out, axis=0, keepdims=True)
        dres = grad_out + norm_pull(dsecond, normal, inverse, gain)
        dres_ref[...] = dres
        branch = dres.astype(BF16)
        g_small_ref[3:4] = jnp.sum(branch.astype(F32), axis=0, keepdims=True)
        by_owner(g_out_ref, dot_lt(mixed_ref[...], branch))
        dmixed = dot_rt(branch, w_out_ref[...])
        core = lax.axis_index("gx")

        def hand_over(spot, piece, first, second):
            send_ref[spot, piece] = jnp.where(core == 0, first, second).astype(BF16)
            far = jnp.where(core == 0, second, first)
            for number in range(rows // BLOCK // 2):
                start = 2 * number * BLOCK
                far_ref[spot, piece, number * BLOCK : (number + 1) * BLOCK] = jnp.where(
                    low_lanes(BLOCK),
                    swap_halves(far[start + BLOCK : start + 2 * BLOCK]),
                    far[start : start + BLOCK],
                ).astype(BF16)

        for piece in range(pieces):
            span = slice(piece * rows, (piece + 1) * rows)
            for spot in (0, 2):
                tiles = [
                    dmixed[span, number * LANES : (number + 1) * LANES]
                    for number in range(3 * (spot // 2), 3 * (spot // 2) + 3)
                ]
                flipped = [swap_halves(tile) for tile in tiles]
                hand_over(
                    spot,
                    piece,
                    jnp.where(low, tiles[1], flipped[0]),
                    jnp.where(low, tiles[1], tiles[0]),
                )
                hand_over(
                    spot + 1, piece, jnp.where(low, flipped[2], tiles[1]), flipped[2]
                )
        for number, pair in enumerate(stages):
            if PER_STAGE * (number + 1) - 1 + WAITS[2] >= last:
                pair[0].close(half_up_ref.at[PER_STAGE * number : PER_STAGE * (number + 1)])
                pair[1].close(half_down_ref.at[number])
        keep_up.wait()
        keep_down.wait()


def plane_middle(mixed_in, far_in, x, dy, vec, w_out, up_shift, w_up, w_down):
    pieces, rows, _ = x.shape
    tokens = pieces * rows
    shard = D // RANKS

    def fixed(shape):
        return pl.BlockSpec(shape, lambda step: (0,) * len(shape))

    steps = FF // CHUNK
    grid = (2, PLANES, SPOTS)
    down_rows = FF // RANKS
    half_up = (PER_STAGE * EARLY, PLANES, 2 * shard, LANES)
    half_down = (EARLY, down_rows, D)
    buffers = []
    for _ in range(EARLY):
        buffers += block_scratch(PER_STAGE, 2 * shard, LANES) + row_scratch(down_rows, D)
    down = pl.BlockSpec((2, LANES, D), lambda step: (0, step, 0))
    return pl.pallas_call(
        plane_middle_kernel,
        grid=(steps,),
        out_shape=(
            jax.ShapeDtypeStruct(x.shape, BF16),
            jax.ShapeDtypeStruct(mixed_in.shape, BF16),
            jax.ShapeDtypeStruct(far_in.shape, BF16),
            jax.ShapeDtypeStruct((tokens, D), F32),
            jax.ShapeDtypeStruct((RANKS, 2 * shard, D // 2), BF16),
            jax.ShapeDtypeStruct(half_up, BF16),
            jax.ShapeDtypeStruct(half_down, BF16),
            jax.ShapeDtypeStruct((PER_STAGE * LATE,) + grid + (2 * shard, LANES), BF16),
            jax.ShapeDtypeStruct((LATE, 2, FF // 2 // STAGES, D), BF16),
            jax.ShapeDtypeStruct((steps, 1, CHUNK), F32),
            jax.ShapeDtypeStruct((4, D), F32),
        ),
        in_specs=[
            fixed(mixed_in.shape),
            fixed(far_in.shape),
            fixed(x.shape),
            fixed((tokens, D)),
            fixed(vec.shape),
            fixed((D, D)),
            pl.BlockSpec((1, 1, CHUNK), lambda step: (step, 0, 0)),
            pl.BlockSpec((D, CHUNK), lambda step: (0, step)),
            down,
        ],
        out_specs=(
            fixed(x.shape),
            fixed(mixed_in.shape),
            fixed(far_in.shape),
            fixed((tokens, D)),
            fixed((RANKS, 2 * shard, D // 2)),
            fixed(half_up),
            fixed(half_down),
            whole(ANY),
            whole(ANY),
            pl.BlockSpec((1, 1, CHUNK), lambda step: (step, 0, 0)),
            fixed((4, D)),
        ),
        scratch_shapes=[
            VMEM((tokens, D), BF16),
            VMEM((tokens, D), F32),
            VMEM((tokens, D), BF16),
            VMEM((D, tokens), BF16),
            VMEM((tokens, D), F32),
            VMEM((tokens, D), F32),
            VMEM((steps,) + grid + (2 * shard, LANES), BF16),
            VMEM((STAGES, 2, FF // 2 // STAGES, D), BF16),
        ]
        + buffers
        + [
            pltpu.SemaphoreType.DMA((EARLY, 2, SpotReduce.SEMS)),
            pltpu.SemaphoreType.DMA((EARLY, 2, SpotReduce.SEMS)),
            pltpu.SemaphoreType.DMA((2,)),
        ],
        compiler_params=pltpu.CompilerParams(
            vmem_limit_bytes=60 * 1024 * 1024, collective_id=3, has_side_effects=True
        ),
        name="plane_middle",
    )(mixed_in, far_in, x, dy, vec, w_out, up_shift, w_up, w_down)


class Reduce:
    SENDS = 4 + 2 + 2 + 3
    RECVS = SENDS

    def __init__(self, source, total, near, corner_x, corner_y, side_x, side_y, far, out, sems):
        self.source, self.total, self.near = source, total, near
        self.corner = {1: corner_x, 2: corner_y}
        self.side = {1: side_x, 2: side_y}
        self.far, self.out = far, out
        self.send_sem, self.recv_sem, self.local_sem = sems
        self.core, self.plane, self.spot = place_here()
        self.copies = []
        self.locals = []

    def start(self):
        sibling = (1 - self.core, rank_of(self.plane, self.spot))
        for number, side in enumerate((3, 1, 2, 0)):
            spot = flip(self.spot, side)
            copy = remote(
                self.source.at[1 - self.core, :, spot],
                self.near.at[:, spot],
                self.send_sem.at[number],
                self.recv_sem.at[number],
                sibling,
            )
            copy.start()
            self.copies.append(copy)
            keep = pltpu.make_async_copy(
                self.source.at[self.core, :, spot],
                self.total.at[:, spot],
                self.local_sem.at[number],
            )
            keep.start()
            self.locals.append(keep)

    def take(self, number, side):
        self.copies[number].wait_recv()
        self.locals[number].wait()
        spot = flip(self.spot, side)

        def add(plane, carry):
            self.total[plane, spot] = (
                self.total[plane, spot].astype(F32) + self.near[plane, spot].astype(F32)
            ).astype(self.total.dtype)
            return carry

        lax.fori_loop(0, PLANES, add, 0, unroll=True)

    def corners(self):
        self.take(0, 3)
        spot = flip(self.spot, 3)
        index = 4
        self.corner_copies = []
        for bits in range(PLANES):
            side = 2 if bits < 2 else 1
            self.corner_copies.append(None)
            plane = flip(self.plane, bits)
            copy = remote(
                self.total.at[plane, spot],
                self.corner[side].at[bits % 2],
                self.send_sem.at[index + bits],
                self.recv_sem.at[index + bits],
                (self.core, rank_of(self.plane, flip(self.spot, side))),
            )
            copy.start()
            self.corner_copies[bits] = copy

    def sides(self):
        self.take(1, 1)
        self.take(2, 2)
        self.side_copies = {}
        for side in (1, 2):
            spot = flip(self.spot, side)
            came = 3 - side
            for bits in (0, 1) if came == 2 else (2, 3):
                self.corner_copies[bits].wait_recv()
                plane = flip(self.plane, bits)
                self.total[plane, spot] = (
                    self.total[plane, spot].astype(F32)
                    + self.corner[came][bits % 2].astype(F32)
                ).astype(self.total.dtype)
            copy = remote(
                self.total.at[:, spot],
                self.side[side],
                self.send_sem.at[7 + side],
                self.recv_sem.at[7 + side],
                (self.core, rank_of(self.plane, spot)),
            )
            copy.start()
            self.side_copies[side] = copy

    def columns(self):
        self.take(3, 0)
        for side in (1, 2):
            self.side_copies[side].wait_recv()

        def add(plane, carry):
            self.total[plane, self.spot] = (
                self.total[plane, self.spot].astype(F32)
                + self.side[1][plane].astype(F32)
                + self.side[2][plane].astype(F32)
            ).astype(self.total.dtype)
            return carry

        lax.fori_loop(0, PLANES, add, 0, unroll=True)
        self.far_copies = []
        for bits in range(1, PLANES):
            plane = flip(self.plane, bits)
            copy = remote(
                self.total.at[plane, self.spot],
                self.far.at[bits - 1],
                self.send_sem.at[9 + bits],
                self.recv_sem.at[9 + bits],
                (self.core, rank_of(plane, self.spot)),
            )
            copy.start()
            self.far_copies.append(copy)

    def finish(self):
        value = self.total[self.plane, self.spot].astype(F32)
        for bits in range(1, PLANES):
            self.far_copies[bits - 1].wait_recv()
            value = value + self.far[bits - 1].astype(F32)
        self.out[...] = value
        for copy in self.copies + self.corner_copies + self.far_copies:
            copy.wait_send()
        for side in (1, 2):
            self.side_copies[side].wait_send()


REDUCE_SEMS = 13


def reduce_scratch(shape, kind):
    tail = shape[3:]
    return [
        VMEM((PLANES, SPOTS) + tail, kind),
        VMEM((PLANES, SPOTS) + tail, kind),
        VMEM((2,) + tail, kind),
        VMEM((2,) + tail, kind),
        VMEM((PLANES,) + tail, kind),
        VMEM((PLANES,) + tail, kind),
        VMEM((PLANES - 1,) + tail, kind),
    ]


class Doubling:
    STEPS = 5

    def __init__(self, totals, boxes, send_sem, recv_sem):
        self.totals, self.boxes = totals, boxes
        self.send_sem, self.recv_sem = send_sem, recv_sem
        core, plane, spot = place_here()
        self.partners = (
            (1 - core, rank_of(plane, spot)),
            (core, rank_of(plane, flip(spot, 1))),
            (core, rank_of(plane, flip(spot, 2))),
            (core, rank_of(flip(plane, 1), spot)),
            (core, rank_of(flip(plane, 2), spot)),
        )
        self.copies = []

    def start(self, step):
        self.copies = []
        for number, (total, box) in enumerate(zip(self.totals, self.boxes)):
            copy = remote(
                total,
                box.at[step],
                self.send_sem.at[step, number],
                self.recv_sem.at[step, number],
                self.partners[step],
            )
            copy.start()
            self.copies.append(copy)

    def finish(self, step):
        for copy, total, box in zip(self.copies, self.totals, self.boxes):
            copy.wait()
            total[...] += box[step]


PARTS = 3


def finish_kernel(
    recv_ref,
    far_ref,
    normed_ref,
    x_ref,
    dres_hbm,
    vec_ref,
    w_hbm,
    g_mid_ref,
    g_up_bias_ref,
    grad_ref,
    g_qkv_ref,
    rows_out_ref,
    tiles_out_ref,
    *scratch,
):
    sources, scratch = scratch[:PARTS], scratch[PARTS:]
    buffers, scratch = scratch[: 7 * PARTS], scratch[7 * PARTS :]
    packed_ref, dnormed_ref, gradient_ref, dres_ref, w_ref = scratch[:5]
    rows_ref, tiles_ref, rows_box, tiles_box = scratch[5:9]
    send_sem, recv_sem, local_sem, load_sem, sum_send, sum_recv = scratch[9:15]
    move_sems = scratch[15:18]
    pieces, rows, _ = x_ref.shape
    tokens = pieces * rows
    core, plane, spot = place_here()
    low = low_lanes(rows)

    load_w = pltpu.make_async_copy(w_hbm, w_ref, load_sem.at[0])
    load_dres = pltpu.make_async_copy(dres_hbm, dres_ref, load_sem.at[1])
    load_w.start()
    load_dres.start()
    greet(all_partners(core, plane, spot))

    def put(tile, piece, value):
        side, chunk = tile // HALF_TILES, tile % HALF_TILES
        packed_ref[
            piece * rows : (piece + 1) * rows,
            chunk * CHUNK + side * LANES : chunk * CHUNK + (side + 1) * LANES,
        ] = value.astype(BF16)

    start_piece, finish_grad = from_planes(gradient_ref, grad_ref, *move_sems, later=True)
    for piece in range(pieces):
        seconds = []
        for goal in range(SPOTS):
            own = recv_ref[core, goal, piece, QUERIES].astype(F32)
            halves = far_ref[goal, piece].astype(F32)
            parts = []
            for number in range(rows // BLOCK // 2):
                part = halves[number * BLOCK : (number + 1) * BLOCK]
                parts += [part, swap_halves(part)]
            other = jnp.concatenate(parts, axis=0)
            second = jnp.where(core == 0, other, own)
            put(goal, piece, jnp.where(low & (core == 1), other, own))
            seconds.append(second)
            base = D // LANES + 3 * goal
            put(base, piece, recv_ref[0, goal, piece, KEYS_A])
            put(base + 1, piece, recv_ref[1, goal, piece, KEYS_A])
            put(base + 2, piece, recv_ref[core, goal, piece, KEYS_B])
        for number in range(2):
            put(
                SPOTS + number,
                piece,
                jnp.where(low, seconds[2 * number], swap_halves(seconds[2 * number + 1])),
            )
        if piece == 0:
            load_w.wait()
            load_dres.wait()
        span = slice(piece * rows, (piece + 1) * rows)
        share = dot_rt(packed_ref[span], w_ref[...])
        dnormed_ref[span] = share
        normal, inverse = norm_parts(x_ref[piece].astype(F32))
        gradient = dres_ref[span] + norm_pull(share, normal, inverse, vec_ref[0:1])
        gradient_ref[piece] = gradient.astype(BF16)
        start_piece(piece)
        sums = [
            jnp.sum(share * normal, axis=0, keepdims=True),
            jnp.sum(share, axis=0, keepdims=True),
        ]
        for number in range(2):
            if piece == 0:
                rows_ref[number : number + 1] = sums[number]
            else:
                rows_ref[number : number + 1] += sums[number]

    rows_ref[2:6] = g_mid_ref[...]
    rows_ref[6:8] = jnp.zeros((2, D), F32)
    tiles_ref[...] = jnp.zeros_like(tiles_ref)
    for step in range(FF // CHUNK):
        tiles_ref[step : step + 1] = g_up_bias_ref[step]
    for chunk in range(HALF_TILES):
        number = FF // CHUNK + chunk
        tiles_ref[number : number + 1] = jnp.sum(
            packed_ref[:, chunk * CHUNK : (chunk + 1) * CHUNK].astype(F32), axis=0, keepdims=True
        )
    sums = Doubling((rows_ref, tiles_ref), (rows_box, tiles_box), sum_send, sum_recv)
    sums.start(0)

    width = HALF_TILES // PARTS * LANES
    reduces = [
        Reduce(
            sources[part],
            *buffers[7 * part : 7 * part + 7],
            g_qkv_ref.at[:, part * width : (part + 1) * width],
            (send_sem.at[part], recv_sem.at[part], local_sem.at[part]),
        )
        for part in range(PARTS)
    ]
    shard = D // RANKS
    normed_t = normed_ref[...].astype(F32).T.astype(BF16)
    for part in range(PARTS):
        for number in range(HALF_TILES // PARTS):
            chunk = part * (HALF_TILES // PARTS) + number
            values = dot(normed_t, packed_ref[:, chunk * CHUNK : (chunk + 1) * CHUNK])
            columns = slice(number * LANES, (number + 1) * LANES)
            for owner in range(RANKS):
                mine = values[owner * shard : (owner + 1) * shard]
                sources[part][
                    owner // (PLANES * SPOTS), owner // SPOTS % PLANES, owner % SPOTS, :, columns
                ] = jnp.concatenate([mine[:, :LANES], mine[:, LANES:]], axis=0).astype(BF16)
        reduces[part].start()
        if part > 0:
            reduces[part - 1].corners()
        if part > 1:
            reduces[part - 2].sides()
    sums.finish(0)
    sums.start(1)
    reduces[2].corners()
    reduces[1].sides()
    sums.finish(1)
    sums.start(2)
    reduces[0].columns()
    reduces[2].sides()
    sums.finish(2)
    sums.start(3)
    reduces[1].columns()
    sums.finish(3)
    sums.start(4)
    reduces[2].columns()
    sums.finish(4)
    for one in reduces:
        one.finish()
    rows_out_ref[...] = rows_ref[...]
    tiles_out_ref[...] = tiles_ref[...]
    finish_grad()


def finish_layer(recv, far, normed, x, dres, vec, w, g_mid, g_up_bias):
    pieces, rows, _ = x.shape
    tokens = pieces * rows
    shard = D // RANKS
    grid = (2, PLANES, SPOTS)
    part = grid + (2 * shard, HALF_TILES // PARTS * LANES)
    buffers = []
    for _ in range(PARTS):
        buffers += reduce_scratch(part, BF16)
    tiles = -(-(FF // CHUNK + HALF_TILES) // 8) * 8
    dma = pltpu.SemaphoreType.DMA
    return pl.pallas_call(
        finish_kernel,
        out_shape=(
            jax.ShapeDtypeStruct(x.shape, BF16),
            jax.ShapeDtypeStruct((2 * shard, 3 * D // 2), F32),
            jax.ShapeDtypeStruct((8, D), F32),
            jax.ShapeDtypeStruct((tiles, CHUNK), F32),
        ),
        in_specs=[
            whole(),
            whole(),
            whole(),
            whole(),
            whole(ANY),
            whole(),
            whole(ANY),
            whole(),
            whole(),
        ],
        out_specs=(whole(ANY), whole(), whole(), whole()),
        scratch_shapes=[VMEM(part, BF16)] * PARTS
        + buffers
        + [
            VMEM((tokens, 3 * D), BF16),
            VMEM((tokens, D), F32),
            VMEM(x.shape, BF16),
            VMEM((tokens, D), F32),
            VMEM(w.shape, BF16),
            VMEM((8, D), F32),
            VMEM((tiles, CHUNK), F32),
            VMEM((Doubling.STEPS, 8, D), F32),
            VMEM((Doubling.STEPS, tiles, CHUNK), F32),
            dma((PARTS, REDUCE_SEMS)),
            dma((PARTS, REDUCE_SEMS)),
            dma((PARTS, 4)),
            dma((2,)),
            dma((Doubling.STEPS, 2)),
            dma((Doubling.STEPS, 2)),
            dma((2,)),
            dma((2,)),
            dma((2,)),
        ],
        compiler_params=pltpu.CompilerParams(
            vmem_limit_bytes=60 * 1024 * 1024, collective_id=2, has_side_effects=True
        ),
        name="finish_layer",
    )(recv, far, normed, x, dres, vec, w, g_mid, g_up_bias)


def present_kernel(
    hidden_hbm,
    grad_hbm,
    t_qkv_hbm,
    t_out_hbm,
    t_up_hbm,
    t_down_hbm,
    rows_hbm,
    tiles_hbm,
    hidden_out_ref,
    grad_out_ref,
    g_qkv_ref,
    g_out_ref,
    g_up_ref,
    g_down_ref,
    *outs,
):
    singles, (grad_ref, t_qkv_ref, t_out_ref, t_up_ref, rows_ref, tiles_ref, copy_sem) = (
        outs[:-7],
        outs[-7:],
    )
    loads = [
        pltpu.make_async_copy(source, target, copy_sem.at[number])
        for number, (source, target) in enumerate(
            (
                (rows_hbm, rows_ref),
                (tiles_hbm, tiles_ref),
                (t_qkv_hbm, t_qkv_ref),
                (t_out_hbm, t_out_ref),
                (t_up_hbm, t_up_ref),
                (grad_hbm, grad_ref),
                (t_down_hbm, g_down_ref),
                (hidden_hbm, hidden_out_ref),
            )
        )
    ]
    for copy in loads:
        copy.start()
    core, plane, spot = place_here()
    mine = core * (PLANES * SPOTS) + rank_of(plane, spot)
    own, wide = D // RANKS, FF // RANKS
    order = [natural_block(entry) for entry in column_order()]
    inverse = [order.index(number) for number in range(len(order))]

    for copy in loads[:5]:
        copy.wait()
    half = D // 2
    for side in range(2):
        rows = slice(side * own, (side + 1) * own)
        g_out_ref[:, side * half : (side + 1) * half] = t_out_ref[rows]
        for chunk in range(FF // CHUNK):
            start = side * (FF // 2) + chunk * LANES
            g_up_ref[:, start : start + LANES] = t_up_ref[chunk, rows]

    def folded(tile):
        side, chunk = tile // HALF_TILES, tile % HALF_TILES
        return t_qkv_ref[
            side * own : (side + 1) * own, chunk * LANES : (chunk + 1) * LANES
        ]

    def bias_sum(tile):
        side, chunk = tile // HALF_TILES, tile % HALF_TILES
        row = FF // CHUNK + chunk
        return tiles_ref[row : row + 1, side * LANES : (side + 1) * LANES]

    biases = []
    for tile in range(TILES):
        blocks = inverse[2 * tile], inverse[2 * tile + 1]
        g_qkv_ref[:, tile * LANES : (tile + 1) * LANES] = pair_of_blocks(folded, *blocks)
        biases.append(pair_of_blocks(bias_sum, *blocks))
    third = TILES // 3
    query = jnp.concatenate(biases[:third], axis=1)
    value = jnp.concatenate(biases[2 * third :], axis=1)
    vectors = jnp.concatenate([rows_ref[0:6], query, value], axis=0)

    def pick(values, first, wanted):
        place = lax.broadcasted_iota(jnp.int32, (values.shape[1], LANES), 0) + first
        lane = lax.broadcasted_iota(jnp.int32, (values.shape[1], LANES), 1)
        one_hot = jnp.where(place == mine * wanted + lane, 1.0, 0.0)
        return lax.dot_general(
            values,
            one_hot,
            (((1,), (0,)), ((), ())),
            precision=lax.Precision.HIGHEST,
            preferred_element_type=F32,
        )

    picked = pick(vectors, 0, own)
    for number in range(VECTORS):
        singles[number][...] = picked[number : number + 1, :own]
    total = jnp.zeros((1, LANES), F32)
    for chunk in range(FF // CHUNK):
        for side in range(2):
            total = total + pick(
                tiles_ref[chunk : chunk + 1, side * LANES : (side + 1) * LANES],
                side * (FF // 2) + chunk * LANES,
                wide,
            )
    singles[VECTORS][...] = total[:, :wide]
    loads[5].wait()
    grad_out_ref[...] = grad_ref[...].astype(F32)
    for copy in loads[6:]:
        copy.wait()


def present(hidden, grad, t_qkv, t_out, t_up, t_down, rows, tiles):
    own, wide = D // RANKS, FF // RANKS
    struct = jax.ShapeDtypeStruct
    return pl.pallas_call(
        present_kernel,
        out_shape=(
            struct(hidden.shape, BF16),
            struct(grad.shape, F32),
            struct((own, 3 * D), F32),
            struct((own, D), F32),
            struct((own, FF), F32),
            struct((wide, D), F32),
        )
        + (struct((1, own), F32),) * VECTORS
        + (struct((1, wide), F32),),
        in_specs=[whole(ANY)] * 8,
        out_specs=(whole(),) * (7 + VECTORS),
        scratch_shapes=[
            VMEM(item.shape, item.dtype) for item in (grad, t_qkv, t_out, t_up, rows, tiles)
        ]
        + [pltpu.SemaphoreType.DMA((8,))],
        compiler_params=params_of(63),
        name="present",
    )(hidden, grad, t_qkv, t_out, t_up, t_down, rows, tiles)


def plane_shards(
    hidden_in,
    rand_table,
    norm1_gain,
    norm1_bias,
    w_qkv,
    query_bias,
    value_bias,
    w_out,
    out_bias,
    norm2_gain,
    norm2_bias,
    w_up,
    up_bias,
    w_down,
    down_bias,
    cotangent,
):
    micro, rows, _ = hidden_in.shape
    local = rows // BLOCK

    def in_row(vector, number):
        return jnp.pad(vector[None], ((number, 15 - number), (0, LANES - vector.shape[0])))

    vec = functools.reduce(
        jnp.add,
        [
            in_row(vector, number)
            for number, vector in enumerate(
                (
                    norm1_gain,
                    norm1_bias,
                    query_bias,
                    value_bias,
                    out_bias,
                    norm2_gain,
                    norm2_bias,
                    down_bias,
                    up_bias,
                )
            )
        ],
    )
    tab = jnp.pad(
        rand_table.reshape(micro, local * RANDOM), ((0, 8 - micro), (0, LANES - local * RANDOM))
    )
    (
        mixed,
        far_mixed,
        x,
        dy,
        w_down_all,
        w_qkv_all,
        w_out_all,
        w_up_all,
        qk,
        shared,
        normed,
        lse,
        vectors,
        up_shift,
        table,
        sorted_table,
    ) = front(hidden_in, cotangent, vec, tab, w_qkv, w_out, w_up, w_down)
    mixed = mixed.reshape(SPOTS, PIECES, rows, LANES)
    far_mixed = far_mixed.reshape(SPOTS, PIECES, rows // 2, LANES)
    (
        hidden,
        near_grad,
        far_grad,
        dres,
        g_out,
        half_up,
        half_down,
        last_up,
        last_down,
        g_up_bias,
        g_mid,
    ) = plane_middle(
        mixed,
        far_mixed,
        x,
        dy.reshape(micro * rows, D),
        vectors,
        w_out_all,
        up_shift,
        w_up_all,
        w_down_all.reshape(2, FF // 2, D),
    )
    grid = (2, PLANES, SPOTS)
    dqkv, far_dq, hidden_out, t_out, t_up, t_down = plane_attention_back(
        table,
        sorted_table,
        qk,
        shared,
        near_grad.reshape(SPOTS, PIECES, local, BLOCK, LANES),
        far_grad.reshape(SPOTS, PIECES, local // 2, BLOCK, LANES),
        lse,
        hidden,
        [
            g_out.reshape((1,) + grid + g_out.shape[1:]),
            last_up,
            last_down,
        ],
        half_up,
        half_down,
    )
    dqkv = dqkv.reshape(2, SPOTS, PIECES, 3, rows, LANES)
    far_dq = far_dq.reshape(SPOTS, PIECES, rows // 2, LANES)
    grad_hidden, t_qkv, sum_rows, sum_tiles = finish_layer(
        dqkv, far_dq, normed, x, dres, vectors, w_qkv_all, g_mid, g_up_bias
    )

    results = present(hidden_out, grad_hidden, t_qkv, t_out, t_up, t_down, sum_rows, sum_tiles)
    hidden_out, grad_hidden, g_qkv, g_out, g_up, g_down = results[:6]
    n1g, n1b, n2g, n2b, db, ob, qb, vb, ub = (item.reshape(item.size) for item in results[6:])
    return (
        hidden_out,
        grad_hidden,
        n1g,
        n1b,
        g_qkv,
        qb,
        vb,
        g_out,
        ob,
        n2g,
        n2b,
        g_up,
        ub,
        g_down,
        db,
    )


def shards(*arrays):
    micro, rows, _ = arrays[0].shape
    fits = lax.axis_size("gx") == 2 and lax.axis_size("gy") == PLANES * SPOTS
    fits = fits and micro == 2 and rows == 4 * BLOCK
    return (plane_shards if fits else general_shards)(*arrays)


def solution(mesh):
    tokens = P(None, AXES, None)
    vector = P(AXES)
    matrix = P(AXES, None)
    placed = (
        tokens,
        tokens,
        vector,
        vector,
        matrix,
        vector,
        vector,
        matrix,
        vector,
        vector,
        vector,
        matrix,
        vector,
        matrix,
        vector,
        tokens,
    )
    returned = (
        tokens,
        tokens,
        vector,
        vector,
        matrix,
        vector,
        vector,
        matrix,
        vector,
        vector,
        vector,
        matrix,
        vector,
        matrix,
        vector,
    )
    return jax.shard_map(
        shards, mesh=mesh, in_specs=placed, out_specs=returned, check_vma=False
    )
```

```python
import functools

import jax
import jax.numpy as jnp
from jax import lax
from jax.experimental import pallas as pl
from jax.experimental.pallas import tpu as pltpu
from jax.sharding import PartitionSpec as P

HEADS = 12
HEAD_DIM = 64
D = 768
FF = 3072
BLOCK = 64
RANDOM = 3
LANES = 2 * HEAD_DIM
EPSILON = 1e-05
NEGATIVE = -1e30
SCALE = HEAD_DIM**-0.5
CHUNK = 256
SPAN = 8

F32 = jnp.float32
BF16 = jnp.bfloat16
VMEM = pltpu.VMEM


def whole(space=VMEM):
    return pl.BlockSpec(memory_space=space)


def params_of(megabytes):
    return pltpu.CompilerParams(vmem_limit_bytes=megabytes * 1024 * 1024)


def head_place(head):
    return (head // 3) * 4 + head % 3


def dot(left, right):
    return lax.dot_general(left, right, (((1,), (0,)), ((), ())), preferred_element_type=F32)


def dot_rt(left, right):
    return lax.dot_general(left, right, (((1,), (1,)), ((), ())), preferred_element_type=F32)


def dot_lt(left, right):
    return lax.dot_general(left, right, (((0,), (0,)), ((), ())), preferred_element_type=F32)


def swap_halves(tile):
    return pltpu.roll(tile, HEAD_DIM, axis=tile.ndim - 1)


def low_lanes(rows):
    return lax.broadcasted_iota(jnp.int32, (rows, LANES), 1) < HEAD_DIM


def norm_parts(values):
    centre = values - jnp.mean(values, axis=-1, keepdims=True)
    spread = jnp.mean(centre * centre, axis=-1, keepdims=True)
    inverse = lax.rsqrt(spread + EPSILON)
    return centre * inverse, inverse


def norm_pull(grad, normal, inverse, gain):
    scaled = grad * gain
    return inverse * (
        scaled
        - jnp.mean(scaled, axis=-1, keepdims=True)
        - normal * jnp.mean(scaled * normal, axis=-1, keepdims=True)
    )


def qkv_kernel(x_ref, gain_ref, shift_ref, w_ref, bias_ref, normed_ref, send_ref):
    micro, rows, _ = x_ref.shape
    values = x_ref[...].reshape(micro * rows, D).astype(F32)
    normal, _ = norm_parts(values)
    normed_ref[...] = (normal * gain_ref[...] + shift_ref[...]).astype(BF16)
    low = low_lanes(rows)
    for chunk in range(3 * D // CHUNK):
        columns = slice(chunk * CHUNK, (chunk + 1) * CHUNK)
        packed = dot(normed_ref[...], w_ref[:, columns]) + bias_ref[:, columns]
        if chunk < D // CHUNK:
            packed = packed.astype(BF16).astype(F32) * SCALE
        for tile in range(CHUNK // LANES):
            part = packed[:, tile * LANES : (tile + 1) * LANES]
            first, second = part[:rows], part[rows:]
            if chunk < D // CHUNK:
                head = (chunk * CHUNK // LANES + tile) * 2
                even = jnp.where(low, first, swap_halves(second))
                odd = jnp.where(low, swap_halves(first), second)
                send_ref[head_place(head), 0] = even.astype(BF16)
                send_ref[head_place(head + 1), 0] = odd.astype(BF16)
            else:
                head = (chunk * CHUNK - D) // LANES + tile
                send_ref[head_place(head), 1] = first.astype(BF16)
                send_ref[head_place(head), 2] = swap_halves(second).astype(BF16)


def qkv_forward(x, gain, shift, w, bias, groups):
    micro, rows, _ = x.shape
    return pl.pallas_call(
        qkv_kernel,
        out_shape=(
            jax.ShapeDtypeStruct((micro * rows, D), BF16),
            jax.ShapeDtypeStruct((groups, 3, rows, LANES), BF16),
        ),
        in_specs=[whole()] * 5,
        out_specs=(whole(), whole()),
        compiler_params=params_of(48),
        name="qkv_forward",
    )(x, gain, shift, w, bias)


def half_mask(low_half):
    lane = lax.broadcasted_iota(jnp.int32, (1, LANES), 1)
    keep = (lane < HEAD_DIM) if low_half else (lane >= HEAD_DIM)
    return jnp.where(keep, 1.0, 0.0).astype(BF16)


def inner_slots(pick, block, blocks):
    ids, bias = picked_slots([pick(block, number) for number in range(RANDOM)], block, blocks)
    edge = (block == 0) | (block == blocks - 1)
    ids[0] = jnp.maximum(ids[0], 0)
    ids[2] = jnp.minimum(ids[2], blocks - 1)
    return ids, bias + jnp.where(edge, NEGATIVE, 0.0).astype(F32)


def slots_of(table_ref, micro, block, blocks):
    picks = [table_ref[micro, block * RANDOM + number] for number in range(RANDOM)]
    return picked_slots(picks, block, blocks)


def picked_slots(picks, block, blocks):
    last = blocks - 1
    ids = [block - 1, block, block + 1, 0, last] + picks
    dropped = [None, None, None, block == 1, block == last - 1]
    for number in range(RANDOM):
        pick = picks[number]
        bad = (jnp.abs(pick - block) <= 1) | (pick == 0) | (pick == last)
        for earlier in range(number):
            bad = bad | (pick == picks[earlier])
        dropped.append(bad)
    lane = lax.broadcasted_iota(jnp.int32, (1, LANES), 1)
    tiles = []
    for pair in range(len(ids) // 2):
        level = [
            0.0 if bad is None else jnp.where(bad, NEGATIVE, 0.0).astype(F32)
            for bad in dropped[2 * pair : 2 * pair + 2]
        ]
        tiles.append(jnp.where(lane < HEAD_DIM, level[0], level[1]))
    return ids, jnp.concatenate(tiles, axis=1)


def attend_kernel(table_ref, qkv_ref, out_ref, lse_ref, s_ref):
    groups, _, local, _, _ = qkv_ref.shape
    blocks = groups * local
    low = low_lanes(BLOCK)
    masks = [half_mask(True), half_mask(False)]

    def load(component, block):
        return qkv_ref[block // local, component, block % local]

    def sparse(block, carry):
        mixed, logs = [], []
        for micro in range(2):
            ids, bias = slots_of(table_ref, micro, block, blocks)
            keys = jnp.concatenate([load(1 + micro, spot) for spot in ids], axis=0)
            query = load(0, block) * masks[micro]
            scores = dot_rt(query, keys) + bias
            top = jnp.max(scores, axis=1, keepdims=True)
            powered = jnp.exp(scores - top)
            total = jnp.sum(powered, axis=1, keepdims=True)
            mixed.append(dot(powered.astype(BF16), keys) * (1.0 / total))
            logs.append(top + jnp.log(total))
        out_ref[block // local, block % local] = jnp.where(low, mixed[1], mixed[0]).astype(BF16)
        lse_ref[block] = jnp.where(low, logs[0], logs[1])
        return carry

    lax.fori_loop(1, blocks - 1, sparse, 0)

    spans = blocks // SPAN
    ends = (0, blocks - 1)
    results = []
    for micro in range(2):
        query = jnp.concatenate([load(0, end) for end in ends], axis=0) * masks[micro]

        def keys_at(span, micro=micro):
            return jnp.concatenate(
                [load(1 + micro, span * SPAN + spot) for spot in range(SPAN)], axis=0
            )

        def first_pass(span, top, query=query, keys_at=keys_at):
            scores = dot_rt(query, keys_at(span))
            s_ref[span] = scores
            return jnp.maximum(top, jnp.max(scores, axis=1, keepdims=True))

        top = lax.fori_loop(0, spans, first_pass, jnp.full((2 * BLOCK, 1), NEGATIVE, F32))

        def second_pass(span, carry, top=top, keys_at=keys_at):
            total, mixed = carry
            powered = jnp.exp(s_ref[span] - top)
            return (
                total + jnp.sum(powered, axis=1, keepdims=True),
                mixed + dot(powered.astype(BF16), keys_at(span)),
            )

        total, mixed = lax.fori_loop(
            0,
            spans,
            second_pass,
            (jnp.zeros((2 * BLOCK, 1), F32), jnp.zeros((2 * BLOCK, LANES), F32)),
        )
        results.append((mixed * (1.0 / total), top + jnp.log(total)))
    for place, end in enumerate(ends):
        rows = slice(place * BLOCK, (place + 1) * BLOCK)
        out_ref[end // local, end % local] = jnp.where(
            low, results[1][0][rows], results[0][0][rows]
        ).astype(BF16)
        lse_ref[end] = jnp.where(low, results[0][1][rows], results[1][1][rows])


def attention_forward(table, qkv):
    groups, _, local, _, _ = qkv.shape
    blocks = groups * local
    return pl.pallas_call(
        attend_kernel,
        out_shape=(
            jax.ShapeDtypeStruct((groups, local, BLOCK, LANES), BF16),
            jax.ShapeDtypeStruct((blocks, BLOCK, LANES), F32),
        ),
        in_specs=[whole(pltpu.SMEM), whole()],
        out_specs=(whole(), whole()),
        scratch_shapes=[VMEM((blocks // SPAN, 2 * BLOCK, SPAN * BLOCK), F32)],
        compiler_params=params_of(48),
        name="attention_forward",
    )(table, qkv)


def attend_back_kernel(table_ref, qkv_ref, grad_ref, lse_ref, out_ref, sums_ref, p_ref, dp_ref):
    groups, _, local, _, _ = qkv_ref.shape
    blocks = groups * local
    low = low_lanes(BLOCK)
    masks = [half_mask(True), half_mask(False)]

    def load(component, block):
        return qkv_ref[block // local, component, block % local]

    def load_grad(block):
        return grad_ref[block // local, block % local]

    def clear(block, carry):
        for micro in range(2):
            sums_ref[micro, block] = jnp.zeros((BLOCK, LANES), F32)
        return carry

    lax.fori_loop(0, blocks, clear, 0)

    def sparse(block, carry):
        grads = []
        for micro in range(2):
            ids, bias = slots_of(table_ref, micro, block, blocks)
            keys = jnp.concatenate([load(1 + micro, spot) for spot in ids], axis=0)
            both = jnp.concatenate(
                [load(0, block) * masks[micro], load_grad(block) * masks[1 - micro]], axis=0
            )
            products = dot_rt(both, keys)
            logs = lse_ref[block][:, micro * HEAD_DIM : micro * HEAD_DIM + 1]
            weights = jnp.exp(products[:BLOCK] + bias - logs)
            grad_weights = products[BLOCK:]
            delta = jnp.sum(weights * grad_weights, axis=1, keepdims=True)
            grad_scores = weights * (grad_weights - delta)
            stacked = jnp.concatenate([grad_scores, weights], axis=0).astype(BF16)
            grads.append(dot(stacked[:BLOCK], keys))
            shares = dot_lt(stacked, both)
            for place, spot in enumerate(ids):
                sums_ref[micro, spot] += shares[place * BLOCK : (place + 1) * BLOCK]
        out_ref[block // local, 0, block % local] = (
            jnp.where(low, grads[0], grads[1]) * SCALE
        ).astype(BF16)
        return carry

    lax.fori_loop(1, blocks - 1, sparse, 0)

    spans = blocks // SPAN
    ends = (0, blocks - 1)
    results = []
    for micro in range(2):
        query = jnp.concatenate([load(0, end) for end in ends], axis=0) * masks[micro]
        grad = jnp.concatenate([load_grad(end) for end in ends], axis=0) * masks[1 - micro]
        both = jnp.concatenate([query, grad], axis=0)
        logs = jnp.concatenate(
            [lse_ref[end][:, micro * HEAD_DIM : micro * HEAD_DIM + 1] for end in ends], axis=0
        )

        def keys_at(span, micro=micro):
            return jnp.concatenate(
                [load(1 + micro, span * SPAN + spot) for spot in range(SPAN)], axis=0
            )

        def first_pass(span, delta, both=both, logs=logs, keys_at=keys_at):
            products = dot_rt(both, keys_at(span))
            weights = jnp.exp(products[: 2 * BLOCK] - logs)
            grad_weights = products[2 * BLOCK :]
            p_ref[span] = weights
            dp_ref[span] = grad_weights
            return delta + jnp.sum(weights * grad_weights, axis=1, keepdims=True)

        delta = lax.fori_loop(0, spans, first_pass, jnp.zeros((2 * BLOCK, 1), F32))

        def second_pass(span, carry, delta=delta, both=both, keys_at=keys_at, micro=micro):
            weights = p_ref[span]
            grad_scores = weights * (dp_ref[span] - delta)
            stacked = jnp.concatenate([grad_scores, weights], axis=0).astype(BF16)
            shares = dot_lt(stacked, both)
            for spot in range(SPAN):
                sums_ref[micro, span * SPAN + spot] += shares[spot * BLOCK : (spot + 1) * BLOCK]
            return carry + dot(stacked[: 2 * BLOCK], keys_at(span))

        results.append(
            lax.fori_loop(0, spans, second_pass, jnp.zeros((2 * BLOCK, LANES), F32))
        )
    for place, end in enumerate(ends):
        rows = slice(place * BLOCK, (place + 1) * BLOCK)
        out_ref[end // local, 0, end % local] = (
            jnp.where(low, results[0][rows], results[1][rows]) * SCALE
        ).astype(BF16)

    def finish(block, carry):
        for micro in range(2):
            out_ref[block // local, 1 + micro, block % local] = sums_ref[micro, block].astype(BF16)
        return carry

    lax.fori_loop(0, blocks, finish, 0)


def attention_backward(table, qkv, grad, lse):
    groups, _, local, _, _ = qkv.shape
    blocks = groups * local
    spans = VMEM((blocks // SPAN, 2 * BLOCK, SPAN * BLOCK), F32)
    return pl.pallas_call(
        attend_back_kernel,
        out_shape=jax.ShapeDtypeStruct(qkv.shape, BF16),
        in_specs=[whole(pltpu.SMEM), whole(), whole(), whole()],
        out_specs=whole(),
        scratch_shapes=[VMEM((2, blocks, BLOCK, LANES), F32), spans, spans],
        compiler_params=params_of(48),
        name="attention_backward",
    )(table, qkv, grad, lse)


def middle_kernel(
    mixed_in_ref,
    x_ref,
    dy_ref,
    w_out_ref,
    out_shift_ref,
    gain_ref,
    shift_ref,
    up_shift_ref,
    down_shift_ref,
    w_up_ref,
    w_down_ref,
    hidden_ref,
    send_ref,
    dres_ref,
    g_out_ref,
    g_up_ref,
    g_down_ref,
    g_up_bias_ref,
    g_small_ref,
    mixed_ref,
    residual_ref,
    second_ref,
    second_t_ref,
    total_ref,
    dsecond_ref,
):
    micro, rows, _ = x_ref.shape
    step = pl.program_id(0)
    low = low_lanes(rows)

    @pl.when(step == 0)
    def _():
        for pair in range(HEADS // 2):
            even = mixed_in_ref[head_place(2 * pair)].astype(F32)
            odd = mixed_in_ref[head_place(2 * pair + 1)].astype(F32)
            columns = slice(pair * LANES, (pair + 1) * LANES)
            mixed_ref[:rows, columns] = jnp.where(low, swap_halves(even), odd).astype(BF16)
            mixed_ref[rows:, columns] = jnp.where(low, even, swap_halves(odd)).astype(BF16)
        residual = x_ref[...].reshape(micro * rows, D).astype(F32) + (
            dot(mixed_ref[...], w_out_ref[...]) + out_shift_ref[...]
        )
        residual_ref[...] = residual
        normal, _ = norm_parts(residual)
        second = normal * gain_ref[...] + shift_ref[...]
        second_ref[...] = second.astype(BF16)
        second_t_ref[...] = second.T.astype(BF16)
        total_ref[...] = jnp.zeros_like(total_ref)
        dsecond_ref[...] = jnp.zeros_like(dsecond_ref)

    upper = dot(second_ref[...], w_up_ref[...]) + up_shift_ref[...]
    factor = 0.7978845608028654
    square = upper * upper
    bent = jnp.tanh(factor * (upper + 0.044715 * (upper * square)))
    half = 0.5 * (1.0 + bent)
    active = (upper * half).astype(BF16)
    slope = half + 0.5 * upper * (1.0 - bent * bent) * (
        factor + (3.0 * 0.044715 * factor) * square
    )
    dy = dy_ref[...]
    total_ref[...] += dot(active, w_down_ref[...])
    g_down_ref[...] = dot_lt(active, dy).astype(g_down_ref.dtype)
    dupper = (dot_rt(dy, w_down_ref[...]) * slope).astype(BF16)
    g_up_bias_ref[...] = jnp.sum(dupper.astype(F32), axis=0, keepdims=True)
    g_up_ref[...] = dot(second_t_ref[...], dupper).astype(g_up_ref.dtype)
    dsecond_ref[...] += dot_rt(dupper, w_up_ref[...])

    @pl.when(step == pl.num_programs(0) - 1)
    def _():
        residual = residual_ref[...]
        hidden_ref[...] = (
            (residual + (total_ref[...] + down_shift_ref[...])).astype(BF16).reshape(x_ref.shape)
        )
        normal, inverse = norm_parts(residual)
        dsecond = dsecond_ref[...]
        grad_out = dy_ref[...].astype(F32)
        g_small_ref[0:1] = jnp.sum(dsecond * normal, axis=0, keepdims=True)
        g_small_ref[1:2] = jnp.sum(dsecond, axis=0, keepdims=True)
        g_small_ref[2:3] = jnp.sum(grad_out, axis=0, keepdims=True)
        dres = grad_out + norm_pull(dsecond, normal, inverse, gain_ref[...])
        dres_ref[...] = dres
        branch = dres.astype(BF16)
        g_small_ref[3:4] = jnp.sum(branch.astype(F32), axis=0, keepdims=True)
        g_out_ref[...] = dot_lt(mixed_ref[...], branch).astype(g_out_ref.dtype)
        dmixed = dot_rt(branch, w_out_ref[...])
        for pair in range(HEADS // 2):
            part = dmixed[:, pair * LANES : (pair + 1) * LANES]
            first, last = part[:rows], part[rows:]
            even = jnp.where(low, last, swap_halves(first))
            odd = jnp.where(low, swap_halves(last), first)
            send_ref[head_place(2 * pair)] = even.astype(BF16)
            send_ref[head_place(2 * pair + 1)] = odd.astype(BF16)


def middle(mixed_in, x, dy, w_out, out_shift, gain, shift, up_shift, down_shift, w_up, w_down, kind):
    micro, rows, _ = x.shape
    tokens = micro * rows
    groups = mixed_in.shape[0]

    def fixed(shape):
        return pl.BlockSpec(shape, lambda step: (0,) * len(shape))

    vector = fixed((1, D))
    steps = FF // CHUNK
    return pl.pallas_call(
        middle_kernel,
        grid=(steps,),
        out_shape=(
            jax.ShapeDtypeStruct(x.shape, BF16),
            jax.ShapeDtypeStruct((groups, rows, LANES), BF16),
            jax.ShapeDtypeStruct((tokens, D), F32),
            jax.ShapeDtypeStruct((D, D), kind),
            jax.ShapeDtypeStruct((D, FF), kind),
            jax.ShapeDtypeStruct((FF, D), kind),
            jax.ShapeDtypeStruct((1, FF), F32),
            jax.ShapeDtypeStruct((4, D), F32),
        ),
        in_specs=[
            fixed(mixed_in.shape),
            fixed(x.shape),
            fixed((tokens, D)),
            fixed((D, D)),
            vector,
            vector,
            vector,
            pl.BlockSpec((1, CHUNK), lambda step: (0, step)),
            vector,
            pl.BlockSpec((D, CHUNK), lambda step: (0, step)),
            pl.BlockSpec((CHUNK, D), lambda step: (step, 0)),
        ],
        out_specs=(
            fixed(x.shape),
            fixed((groups, rows, LANES)),
            fixed((tokens, D)),
            fixed((D, D)),
            pl.BlockSpec((D, CHUNK), lambda step: (0, step)),
            pl.BlockSpec((CHUNK, D), lambda step: (step, 0)),
            pl.BlockSpec((1, CHUNK), lambda step: (0, step)),
            fixed((4, D)),
        ),
        scratch_shapes=[
            VMEM((tokens, D), BF16),
            VMEM((tokens, D), F32),
            VMEM((tokens, D), BF16),
            VMEM((D, tokens), BF16),
            VMEM((tokens, D), F32),
            VMEM((tokens, D), F32),
        ],
        compiler_params=params_of(56),
        name="middle",
    )(mixed_in, x, dy, w_out, out_shift, gain, shift, up_shift, down_shift, w_up, w_down)


def qkv_back_kernel(
    recv_ref,
    normed_ref,
    x_ref,
    dres_ref,
    gain_ref,
    w_ref,
    grad_ref,
    g_qkv_ref,
    g_bias_ref,
    g_small_ref,
    packed_ref,
    normed_t_ref,
    dnormed_ref,
):
    micro, rows, _ = x_ref.shape
    step = pl.program_id(0)
    low = low_lanes(rows)

    @pl.when(step == 0)
    def _():
        for pair in range(HEADS // 2):
            even = recv_ref[head_place(2 * pair), 0].astype(F32)
            odd = recv_ref[head_place(2 * pair + 1), 0].astype(F32)
            spot, columns = pair // 2, slice((pair % 2) * LANES, (pair % 2 + 1) * LANES)
            packed_ref[spot, :rows, columns] = jnp.where(low, even, swap_halves(odd)).astype(BF16)
            packed_ref[spot, rows:, columns] = jnp.where(low, swap_halves(even), odd).astype(BF16)
        for head in range(HEADS):
            spot = D // CHUNK + head // 2
            columns = slice((head % 2) * LANES, (head % 2 + 1) * LANES)
            packed_ref[spot, :rows, columns] = recv_ref[head_place(head), 1]
            packed_ref[spot, rows:, columns] = swap_halves(
                recv_ref[head_place(head), 2].astype(F32)
            ).astype(BF16)
        normed_t_ref[...] = normed_ref[...].astype(F32).T.astype(BF16)
        dnormed_ref[...] = jnp.zeros_like(dnormed_ref)

    packed = packed_ref[step]
    g_bias_ref[...] = jnp.sum(packed.astype(F32), axis=0, keepdims=True)
    g_qkv_ref[...] = dot(normed_t_ref[...], packed).astype(g_qkv_ref.dtype)
    dnormed_ref[...] += dot_rt(packed, w_ref[...])

    @pl.when(step == pl.num_programs(0) - 1)
    def _():
        normal, inverse = norm_parts(x_ref[...].reshape(micro * rows, D).astype(F32))
        dnormed = dnormed_ref[...]
        g_small_ref[0:1] = jnp.sum(dnormed * normal, axis=0, keepdims=True)
        g_small_ref[1:2] = jnp.sum(dnormed, axis=0, keepdims=True)
        grad = dres_ref[...] + norm_pull(dnormed, normal, inverse, gain_ref[...])
        grad_ref[...] = grad.reshape(x_ref.shape)


def qkv_backward(recv, normed, x, dres, gain, w, kind):
    micro, rows, _ = x.shape
    tokens = micro * rows

    def fixed(shape):
        return pl.BlockSpec(shape, lambda step: (0,) * len(shape))

    steps = 3 * D // CHUNK
    return pl.pallas_call(
        qkv_back_kernel,
        grid=(steps,),
        out_shape=(
            jax.ShapeDtypeStruct(x.shape, F32),
            jax.ShapeDtypeStruct((D, 3 * D), kind),
            jax.ShapeDtypeStruct((1, 3 * D), F32),
            jax.ShapeDtypeStruct((2, D), F32),
        ),
        in_specs=[
            fixed(recv.shape),
            fixed((tokens, D)),
            fixed(x.shape),
            fixed((tokens, D)),
            fixed((1, D)),
            pl.BlockSpec((D, CHUNK), lambda step: (0, step)),
        ],
        out_specs=(
            fixed(x.shape),
            pl.BlockSpec((D, CHUNK), lambda step: (0, step)),
            pl.BlockSpec((1, CHUNK), lambda step: (0, step)),
            fixed((2, D)),
        ),
        scratch_shapes=[
            VMEM((steps, tokens, CHUNK), BF16),
            VMEM((D, tokens), BF16),
            VMEM((tokens, D), F32),
        ],
        compiler_params=params_of(56),
        name="qkv_backward",
    )(recv, normed, x, dres, gain, w)


AXES = ("gx", "gy")


def gather(array):
    return lax.all_gather(array, AXES, axis=0, tiled=True)


def scatter(array):
    return lax.psum_scatter(array, AXES, scatter_dimension=0, tiled=True)


def exchange(array):
    return lax.all_to_all(array, "gy", 0, 0, tiled=True)


def by_heads(w_qkv):
    rows = w_qkv.shape[0]
    sides = w_qkv[:, D:].reshape(rows, 2, HEADS, HEAD_DIM)
    return jnp.concatenate([w_qkv[:, :D], jnp.swapaxes(sides, 1, 2).reshape(rows, 2 * D)], axis=1)


def by_parts(w_qkv):
    rows = w_qkv.shape[0]
    sides = w_qkv[:, D:].reshape(rows, HEADS, 2, HEAD_DIM)
    return jnp.concatenate([w_qkv[:, :D], jnp.swapaxes(sides, 1, 2).reshape(rows, 2 * D)], axis=1)


def general_shards(
    hidden_in,
    rand_table,
    norm1_gain,
    norm1_bias,
    w_qkv,
    query_bias,
    value_bias,
    w_out,
    out_bias,
    norm2_gain,
    norm2_bias,
    w_up,
    up_bias,
    w_down,
    down_bias,
    cotangent,
):
    micro, rows, _ = hidden_in.shape
    groups = lax.axis_size("gy")
    local = rows // BLOCK
    own = norm1_gain.shape[0]

    vectors = jnp.concatenate(
        [
            norm1_gain,
            norm1_bias,
            query_bias,
            value_bias,
            out_bias,
            norm2_gain,
            norm2_bias,
            down_bias,
            up_bias,
        ]
    )
    table = lax.all_gather(rand_table, "gy", axis=1, tiled=True)
    table = table.reshape(micro, groups * local * RANDOM)
    vectors = gather(vectors[None]).astype(F32)
    gain_one, shift_one, query_shift, value_shift, out_shift, gain_two, shift_two, down_shift = (
        vectors[:, number * own : (number + 1) * own].reshape(1, D) for number in range(8)
    )
    up_shift = vectors[:, 8 * own :].reshape(1, FF)
    w_qkv_full = gather(by_heads(w_qkv))
    w_out_full, w_up_full, w_down_full = gather(w_out), gather(w_up), gather(w_down)
    packed_bias = by_heads(
        jnp.concatenate([query_shift, jnp.zeros_like(query_shift), value_shift], axis=1)
    )

    normed, send = qkv_forward(hidden_in, gain_one, shift_one, w_qkv_full, packed_bias, groups)
    qkv = exchange(send).reshape(groups, 3, local, BLOCK, LANES)
    mixed, lse = attention_forward(table, qkv)
    mixed_back = exchange(mixed.reshape(groups, rows, LANES))
    hidden_out, grad_send, dres, g_out, g_up, g_down, g_up_bias, g_mid = middle(
        mixed_back,
        hidden_in,
        cotangent.reshape(micro * rows, D),
        w_out_full,
        out_shift,
        gain_two,
        shift_two,
        up_shift,
        down_shift,
        w_up_full,
        w_down_full,
        F32,
    )
    grad_mixed = exchange(grad_send).reshape(groups, local, BLOCK, LANES)
    dqkv = attention_backward(table, qkv, grad_mixed, lse)
    dqkv_back = exchange(dqkv.reshape(groups, 3, rows, LANES))
    grad_hidden, g_qkv, g_packed, g_first = qkv_backward(
        dqkv_back, normed, hidden_in, dres, gain_one, w_qkv_full, F32
    )

    g_packed = by_parts(g_packed)
    small = [
        g_first[0],
        g_first[1],
        g_packed[0, :D],
        g_packed[0, 2 * D :],
        g_mid[3],
        g_mid[0],
        g_mid[1],
        g_mid[2],
    ]
    ranks = D // own
    small = jnp.concatenate(
        [item.reshape(ranks, own) for item in small] + [g_up_bias.reshape(ranks, 4 * own)], axis=1
    )
    small = scatter(small)[0]
    parts = [small[number * own : (number + 1) * own] for number in range(8)]
    return (
        hidden_out,
        grad_hidden,
        parts[0],
        parts[1],
        by_parts(scatter(g_qkv)),
        parts[2],
        parts[3],
        scatter(g_out),
        parts[4],
        parts[5],
        parts[6],
        scatter(g_up),
        small[8 * own :],
        scatter(g_down),
        parts[7],
    )


MESH = pl.DeviceIdType.MESH
ANY = pl.ANY
PLANES = 4
SPOTS = 4
PIECES = 2
RANKS = 2 * PLANES * SPOTS
TILES = 3 * D // LANES
HALF_TILES = TILES // 2
QUERY_ORDER = (0, 2, 3, 5, 6, 8, 9, 11, 1, 4, 7, 10)


def column_order():
    order = [("q", head) for head in QUERY_ORDER]
    for spot in range(SPOTS):
        for place in (2 * 3 * spot, 2 * 3 * spot + 2):
            order += [("k", place // 2), ("v", place // 2)]
        order += [("v", 3 * spot + 2), ("k", 3 * spot + 2)]
    return order


def natural_block(entry):
    return "qkv".index(entry[0]) * HEADS + entry[1]


def flip(value, bits):
    if bits == 0:
        return value
    if bits == 1:
        return value + 1 - 2 * lax.rem(value, 2)
    if bits == 2:
        return value + 2 - 4 * lax.div(value, 2)
    return 3 - value


def place_here():
    core, rank = lax.axis_index("gx"), lax.axis_index("gy")
    return core, lax.div(rank, SPOTS), lax.rem(rank, SPOTS)


def rank_of(plane, spot):
    return plane * SPOTS + spot


def greet(partners):
    barrier = pltpu.get_barrier_semaphore()
    for partner in partners:
        pl.semaphore_signal(barrier, inc=1, device_id=partner, device_id_type=MESH)
    pl.semaphore_wait(barrier, len(partners))


def remote(source, target, send_sem, recv_sem, device):
    return pltpu.make_async_remote_copy(
        src_ref=source,
        dst_ref=target,
        send_sem=send_sem,
        recv_sem=recv_sem,
        device_id=device,
        device_id_type=MESH,
    )


def column_partners(core, plane, spot):
    partners = [(1 - core, rank_of(plane, spot))]
    for bits in range(1, PLANES):
        for other in (core, 1 - core):
            partners.append((other, rank_of(flip(plane, bits), spot)))
    return partners


def all_partners(core, plane, spot):
    return column_partners(core, plane, spot) + [
        (core, rank_of(plane, flip(spot, 1))),
        (core, rank_of(plane, flip(spot, 2))),
    ]


def to_planes(source, target, send_sem, recv_sem, local_sem):
    core, plane, spot = place_here()
    half, odd = lax.div(plane, 2), lax.rem(plane, 2)
    sends, keeps = [], []
    for micro in range(2):
        goal = 2 * micro + core
        here = (goal == plane) & (half == core)
        send = remote(
            source.at[micro],
            target.at[odd],
            send_sem.at[micro],
            recv_sem.at[odd],
            (half, rank_of(goal, spot)),
        )
        keep = pltpu.make_async_copy(source.at[micro], target.at[odd], local_sem.at[micro])

        @pl.when(jnp.logical_not(here))
        def _(send=send):
            send.start()

        @pl.when(here)
        def _(keep=keep):
            keep.start()

        sends.append((here, send))
        keeps.append((here, keep))

    def finish():
        for piece in range(PIECES):
            mine = (odd == core) & (plane == 2 * core + piece)
            arrival = remote(
                source.at[0],
                target.at[piece],
                send_sem.at[0],
                recv_sem.at[piece],
                (core, rank_of(plane, spot)),
            )

            @pl.when(jnp.logical_not(mine))
            def _(arrival=arrival):
                arrival.wait_recv()

        for (here, send), (_, keep) in zip(sends, keeps):

            @pl.when(jnp.logical_not(here))
            def _(send=send):
                send.wait_send()

            @pl.when(here)
            def _(keep=keep):
                keep.wait()

    return finish


def from_planes(source, target, send_sem, recv_sem, local_sem, later=False):
    core, plane, spot = place_here()
    micro, odd = lax.div(plane, 2), lax.rem(plane, 2)
    sends, keeps = [], []

    def start(piece):
        goal = 2 * core + piece
        here = (goal == plane) & (odd == core)
        send = remote(
            source.at[piece],
            target.at[micro],
            send_sem.at[piece],
            recv_sem.at[micro],
            (odd, rank_of(goal, spot)),
        )
        keep = pltpu.make_async_copy(source.at[piece], target.at[micro], local_sem.at[piece])

        @pl.when(jnp.logical_not(here))
        def _(send=send):
            send.start()

        @pl.when(here)
        def _(keep=keep):
            keep.start()

        sends.append((here, send))
        keeps.append((here, keep))

    for piece in () if later else range(PIECES):
        start(piece)

    def finish():
        for number in range(2):
            mine = (2 * number + core == plane) & (micro == core)
            arrival = remote(
                source.at[0],
                target.at[number],
                send_sem.at[0],
                recv_sem.at[number],
                (core, rank_of(plane, spot)),
            )

            @pl.when(jnp.logical_not(mine))
            def _(arrival=arrival):
                arrival.wait_recv()

        for (here, send), (_, keep) in zip(sends, keeps):

            @pl.when(jnp.logical_not(here))
            def _(send=send):
                send.wait_send()

            @pl.when(here)
            def _(keep=keep):
                keep.wait()

    return (start, finish) if later else finish


class Gather:
    SENDS = 31

    def __init__(self, source, target, send_sem, recv_sem, local_sem):
        self.source, self.target = source, target
        self.send_sem, self.recv_sem = send_sem, recv_sem
        self.core, self.plane, self.spot = place_here()
        self.sends = []
        self.own = pltpu.make_async_copy(
            source, target.at[self.core, self.plane, self.spot], local_sem
        )
        self.own.start()

    def send(self, source, plane, spot, device):
        copy = remote(
            source,
            self.target.at[self.core, plane, spot],
            self.send_sem.at[len(self.sends)],
            self.recv_sem.at[self.core, plane, spot],
            device,
        )
        copy.start()
        self.sends.append(copy)

    def arrive(self, core, plane, spot):
        shard = self.target.at[core, plane, spot]
        remote(
            shard,
            shard,
            self.send_sem.at[0],
            self.recv_sem.at[core, plane, spot],
            (self.core, rank_of(self.plane, self.spot)),
        ).wait_recv()

    def neighbour(self, bits):
        return (self.core, rank_of(self.plane, flip(self.spot, bits)))

    def sibling(self):
        return (1 - self.core, rank_of(self.plane, self.spot))

    def start(self):
        for bits in range(1, PLANES):
            goal = (self.core, rank_of(flip(self.plane, bits), self.spot))
            self.send(self.source, self.plane, self.spot, goal)
        for goal in (self.neighbour(1), self.neighbour(2), self.sibling()):
            self.send(self.source, self.plane, self.spot, goal)

    def column(self):
        for bits in range(1, PLANES):
            plane = flip(self.plane, bits)
            self.arrive(self.core, plane, self.spot)
            shard = self.target.at[self.core, plane, self.spot]
            for goal in (self.neighbour(1), self.neighbour(2), self.sibling()):
                self.send(shard, plane, self.spot, goal)

    def across(self):
        for bits in range(PLANES):
            plane = flip(self.plane, bits)
            for side in (1, 2):
                spot = flip(self.spot, side)
                self.arrive(self.core, plane, spot)
                shard = self.target.at[self.core, plane, spot]
                if (side == 1) == (bits < 2):
                    self.send(shard, plane, spot, self.neighbour(3 - side))
                self.send(shard, plane, spot, self.sibling())

    def corner(self):
        spot = flip(self.spot, 3)
        for bits in range(PLANES):
            plane = flip(self.plane, bits)
            self.arrive(self.core, plane, spot)
            self.send(self.target.at[self.core, plane, spot], plane, spot, self.sibling())

    def finish(self):
        for bits in range(PLANES):
            for side in range(SPOTS):
                self.arrive(1 - self.core, flip(self.plane, bits), flip(self.spot, side))
        self.own.wait()
        for copy in self.sends:
            copy.wait_send()


def settle(shards_ref, plan):
    rows = shards_ref.shape[3] // 2

    def pair(number, carry):
        core, plane, side = (
            lax.div(number, 2 * PLANES),
            lax.rem(lax.div(number, 2), PLANES),
            lax.rem(number, 2),
        )
        goal = pl.ds(pl.multiple_of(number * 2 * rows, 16), 2 * rows)
        for tile, out_ref, (left, right) in plan:
            columns = slice(tile * LANES, (tile + 1) * LANES)
            first = shards_ref[core, plane, 2 * side, :, columns].astype(F32)
            second = shards_ref[core, plane, 2 * side + 1, :, columns].astype(F32)
            out_ref[goal, left * LANES : (left + 1) * LANES] = jnp.concatenate(
                [first[:rows], second[:rows]], axis=0
            ).astype(BF16)
            out_ref[goal, right * LANES : (right + 1) * LANES] = jnp.concatenate(
                [first[rows:], second[rows:]], axis=0
            ).astype(BF16)
        return carry

    lax.fori_loop(0, RANKS // 2, pair, 0)


def alternate(tile):
    return 2 * tile, 2 * tile + 1


def plane_partners(core, plane, spot):
    partners = []
    for other in (core, 1 - core):
        for side in range(SPOTS):
            if other is core and side == 0:
                continue
            partners.append((other, rank_of(plane, flip(spot, side))))
    return partners


def both_partners(core, plane, spot):
    return plane_partners(core, plane, spot) + column_partners(core, plane, spot)[1:]


def exchange_sems(recv_shape):
    return [
        pltpu.SemaphoreType.DMA((14,)),
        pltpu.SemaphoreType.DMA(recv_shape),
        pltpu.SemaphoreType.DMA((PIECES,)),
    ]


def sort_entries(table, sorted_ref, entries):
    count = table.shape[1]
    core = lax.axis_index("gx")
    lane = lax.broadcasted_iota(jnp.int32, (count, count), 1)
    row = lax.broadcasted_iota(jnp.int32, (count, count), 0).astype(F32)
    everything = jnp.broadcast_to(table, (count, count))
    half = entries // 2
    inside = (lane >= core * half) & (lane < (core + 1) * half)
    lane = lane.astype(F32)
    for number, along in enumerate((everything, jnp.where(inside, everything, 2.0 * LANES))):
        down = along.T
        before = (along < down) | ((along == down) & (lane < row))
        rank = jnp.sum(jnp.where(before, 1.0, 0.0), axis=1, keepdims=True)
        order = jnp.sum(jnp.where(rank == lane, row, 0.0), axis=0, keepdims=True)
        upto = jnp.sum(jnp.where(down <= lane, 1.0, 0.0), axis=0, keepdims=True)
        sorted_ref[2 * number : 2 * number + 1] = order.astype(jnp.int32)
        sorted_ref[2 * number + 1 : 2 * number + 2] = upto.astype(jnp.int32)


def pack_halves(read, target_ref, place, local, low, half):
    for number in range(local // 2):
        first = read(2 * number).astype(F32)
        second = swap_halves(read(2 * number + 1).astype(F32))
        kept = (first, second) if half == 0 else (second, first)
        target_ref[place + (number,)] = jnp.where(low, *kept).astype(BF16)


class Outward:
    def __init__(self, source, far_source, target, packed, send_sem, recv_sem, local_sem):
        self.target, self.packed = target, packed
        self.recv_sem, self.send_sem = recv_sem, send_sem
        self.core, self.plane, self.spot = place_here()
        self.sends, self.keeps = [], []
        for side in (3, 1, 2, 0):
            goal = flip(self.spot, side)
            for other in (self.core, 1 - self.core):
                near = other is self.core
                for piece in range(PIECES):
                    start = (source if near else far_source).at[goal, piece]
                    place = (2 * self.core + piece, self.spot)
                    stop = (target if near else packed).at[place]
                    if side == 0 and near:
                        copy = pltpu.make_async_copy(start, stop, local_sem.at[piece])
                        self.keeps.append(copy)
                    else:
                        copy = remote(
                            start,
                            stop,
                            send_sem.at[len(self.sends)],
                            recv_sem.at[place],
                            (other, rank_of(self.plane, goal)),
                        )
                        self.sends.append(copy)
                    copy.start()

    def arrive(self, side):
        goal = flip(self.spot, side)
        for other in (self.core, 1 - self.core):
            near = other is self.core
            if side == 0 and near:
                for copy in self.keeps:
                    copy.wait()
                continue
            for piece in range(PIECES):
                place = (2 * other + piece, goal)
                landed = (self.target if near else self.packed).at[place]
                remote(
                    landed,
                    landed,
                    self.send_sem.at[0],
                    self.recv_sem.at[place],
                    (self.core, rank_of(self.plane, self.spot)),
                ).wait_recv()
                if not near:
                    for number in range(self.packed.shape[2]):
                        tile = self.packed[place + (number,)]
                        self.target[place + (2 * number,)] = tile
                        self.target[place + (2 * number + 1,)] = swap_halves(
                            tile.astype(F32)
                        ).astype(BF16)

    def finish(self):
        for copy in self.sends:
            copy.wait_send()


def inward_targets(core, spot):
    for side in (3, 1, 2, 0):
        for other in (core, 1 - core):
            yield side, other, flip(spot, side), side == 0 and other is core


class Inward:
    def __init__(self, source, target, send_sem, recv_sem, local_sem):
        self.source, self.target = source, target
        self.send_sem, self.recv_sem, self.local_sem = send_sem, recv_sem, local_sem
        self.core, self.plane, self.spot = place_here()
        self.sends, self.keeps = [], []

    def send(self, other, goal, stays, piece, part, parts):
        source = self.source.at[2 * other + piece, goal, parts]
        target = self.target.at[self.core, self.spot, piece, parts]
        if stays:
            copy = pltpu.make_async_copy(source, target, self.local_sem.at[part, piece])
            self.keeps.append(copy)
        else:
            copy = remote(
                source,
                target,
                self.send_sem.at[len(self.sends)],
                self.recv_sem.at[self.core, self.spot, piece, part],
                (other, rank_of(self.plane, goal)),
            )
            self.sends.append(copy)
        copy.start()

    def finish(self, parts_of):
        for side, other, goal, stays in inward_targets(self.core, self.spot):
            if stays:
                continue
            for piece in range(PIECES):
                for part, parts in enumerate(parts_of[0 if other is self.core else 1]):
                    target = self.target.at[other, goal, piece, parts]
                    remote(
                        target,
                        target,
                        self.send_sem.at[0],
                        self.recv_sem.at[other, goal, piece, part],
                        (self.core, rank_of(self.plane, self.spot)),
                    ).wait_recv()
        for copy in self.sends:
            copy.wait_send()
        for copy in self.keeps:
            copy.wait()


KEYS_A, QUERIES, KEYS_B = range(3)


def plane_attend_back_kernel(*refs):
    table_ref, sorted_ref, qk_ref, shared_ref, near_grad_ref, far_grad_ref, lse_ref, hidden_ref = (
        refs[:8]
    )
    sources, half_up_ref, half_down_ref, refs = refs[8:11], refs[11], refs[12], refs[13:]
    sources = list(sources[:2]) + [sources[2].at[number] for number in range(LATE)]
    back_ref, far_back_ref, hidden_out_ref, t_out_ref, t_up_ref, t_down_ref = refs[:6]
    count = 2 + LATE
    refs = refs[6:]
    buffers, mines, refs = refs[: 3 * count], refs[3 * count : 4 * count], refs[4 * count :]
    part_out_ref, part_up_ref, part_down_ref, far_out_ref, far_up_ref, far_down_ref = refs[:6]
    grad_ref, packed_ref, out_ref, sums_ref, shares_ref, walked_ref, sibling_ref = refs[6:13]
    pack_ref, scores_refs, refs = refs[13], refs[14:18], refs[18:]
    reduce_send, reduce_recv, far_send, far_recv, load_sem = refs[:5]
    grad_sems, back_sems, move_sems, sibling_sems = refs[5:8], refs[8:11], refs[11:14], refs[14:16]
    pack_send, pack_recv = refs[16:18]

    local = qk_ref.shape[3]
    groups = PLANES * SPOTS
    blocks = groups * local
    core, plane, spot = place_here()
    low = low_lanes(BLOCK)
    masks = [half_mask(True), half_mask(False)]

    greet(both_partners(core, plane, spot))
    grads = Outward(near_grad_ref, far_grad_ref, grad_ref, packed_ref, *grad_sems)
    reduces = [
        SpotReduce(
            source,
            *buffers[3 * number : 3 * number + 3],
            reduce_send.at[number],
            reduce_recv.at[number],
            rows=FF // RANKS if number >= 2 else None,
            mine=mine,
        )
        for number, (source, mine) in enumerate(zip(sources, mines))
    ]
    ready = PER_STAGE * EARLY
    loads = [
        pltpu.make_async_copy(one.half(core), mine, load_sem.at[number])
        for number, (one, mine) in enumerate(zip(reduces, mines))
    ] + [
        pltpu.make_async_copy(half_up_ref, part_up_ref.at[0:ready], load_sem.at[count]),
        pltpu.make_async_copy(half_down_ref, part_down_ref.at[0:EARLY], load_sem.at[count + 1]),
    ]
    for one in reduces:
        one.start()
    for copy in loads:
        copy.start()

    def far(bits, number, source, target):
        return remote(
            source,
            target,
            far_send.at[number, bits - 1],
            far_recv.at[number, bits - 1],
            (core, rank_of(flip(plane, bits), spot)),
        )

    def far_down(bits, source):
        return far(bits, 3, source, far_down_ref.at[bits - 1])

    fars = []
    for bits in range(1, PLANES):
        goal = flip(plane, bits)
        copy = far(bits, 0, half_up_ref.at[:, goal], far_up_ref.at[bits - 1, 0:ready])
        copy.start()
        fars.append(copy)

        @pl.when(goal < EARLY)
        def _(bits=bits, goal=goal):
            far_down(bits, half_down_ref.at[jnp.minimum(goal, EARLY - 1)]).start()

    finish_hidden = from_planes(hidden_ref, hidden_out_ref, *move_sems)

    def load(component, block):
        rank, number = lax.div(block, local), lax.rem(block, local)
        if component == 2:
            return shared_ref[lax.div(rank, SPOTS), lax.rem(rank, SPOTS), number]
        return qk_ref[lax.div(rank, SPOTS), lax.rem(rank, SPOTS), component, number]

    def load_grad(block):
        rank = lax.div(block, local)
        return grad_ref[lax.div(rank, SPOTS), lax.rem(rank, SPOTS), lax.rem(block, local)]

    def store(component, block, value):
        rank = lax.div(block, local)
        out_ref[
            lax.div(rank, SPOTS), lax.rem(rank, SPOTS), component, lax.rem(block, local)
        ] = value.astype(BF16)

    def stored(component, block):
        rank = lax.div(block, local)
        return out_ref[
            lax.div(rank, SPOTS), lax.rem(rank, SPOTS), component, lax.rem(block, local)
        ].astype(F32)

    nothing = jnp.zeros((BLOCK, LANES), F32)

    def clear(block, carry):
        for slot in range(2):
            sums_ref[slot, block] = nothing
        return carry

    lax.fori_loop(0, blocks, clear, 0)

    def picked(block, number):
        return table_ref[0, block * RANDOM + number]

    def one_block(block, slot):
        ids, bias = inner_slots(picked, block, blocks)
        keys = jnp.concatenate([load(1 + slot, number) for number in ids], axis=0)
        both = jnp.concatenate(
            [load(0, block) * masks[slot], load_grad(block) * masks[1 - slot]], axis=0
        )
        products = dot_rt(both, keys)
        logs = lse_ref[block][:, slot * HEAD_DIM : slot * HEAD_DIM + 1]
        weights = jnp.exp(products[:BLOCK] + bias - logs)
        grad_weights = products[BLOCK:]
        delta = jnp.sum(weights * grad_weights, axis=1, keepdims=True)
        grad_scores = weights * (grad_weights - delta)
        stacked = jnp.concatenate([grad_scores, weights], axis=0).astype(BF16)
        return dot(stacked[:BLOCK], keys), dot_lt(stacked, both)

    fixed = 5

    def rank_blocks(rank, slot):
        first = rank * local
        results = [one_block(first + number, slot) for number in range(local)]

        def share(number, place):
            return results[number][1][place * BLOCK : (place + 1) * BLOCK]

        for shift in range(-1, local + 1):
            parts = [
                share(number, shift - number + 1)
                for number in range(local)
                if 0 <= shift - number + 1 <= 2
            ]
            target = jnp.minimum(jnp.maximum(first + shift, 0), blocks - 1)
            sums_ref[slot, target] += functools.reduce(jnp.add, parts)
        for place, target in ((3, 0), (4, blocks - 1)):
            sums_ref[slot, target] += functools.reduce(
                jnp.add, [share(number, place) for number in range(local)]
            )
        for number in range(local):
            for pick in range(RANDOM):
                shares_ref[slot, (first + number) * RANDOM + pick] = share(number, fixed + pick)
        return [result[0] for result in results]

    def head_a(side):
        def body(number, carry):
            rank = number * SPOTS + flip(spot, side)
            for place, query in enumerate(rank_blocks(rank, 0)):
                store(QUERIES, rank * local + place, query * SCALE)
            return carry

        lax.fori_loop(0, PLANES, body, 0)

    def head_b(number, carry):
        rank = core * (groups // 2) + number
        for place, query in enumerate(rank_blocks(rank, 1)):
            block = rank * local + place
            store(QUERIES, block, jnp.where(low, stored(QUERIES, block), query * SCALE))
        return carry

    spans = blocks // SPAN
    ends = (0, blocks - 1)

    def dense(slot, p_ref, d_ref, numbers):
        both = jnp.concatenate(
            [load(0, number) * masks[slot] for number in numbers]
            + [load_grad(number) * masks[1 - slot] for number in numbers],
            axis=0,
        )
        rows = len(numbers) * BLOCK
        column = slot * HEAD_DIM
        logs = jnp.concatenate(
            [lse_ref[number][:, column : column + 1] for number in numbers], axis=0
        )

        def keys_at(span):
            return jnp.concatenate(
                [load(1 + slot, span * SPAN + number) for number in range(SPAN)], axis=0
            )

        def first_pass(span, delta):
            products = dot_rt(both, keys_at(span))
            weights = jnp.exp(products[:rows] - logs)
            grad_weights = products[rows:]
            p_ref[span] = weights
            d_ref[span] = grad_weights
            return delta + jnp.sum(weights * grad_weights, axis=1, keepdims=True)

        delta = lax.fori_loop(0, spans, first_pass, jnp.zeros((rows, 1), F32), unroll=2)

        def second_pass(span, total):
            weights = p_ref[span]
            grad_scores = weights * (d_ref[span] - delta)
            stacked = jnp.concatenate([grad_scores, weights], axis=0).astype(BF16)
            shares = dot_lt(stacked, both)
            for number in range(SPAN):
                sums_ref[slot, span * SPAN + number] += shares[
                    number * BLOCK : (number + 1) * BLOCK
                ]
            return total + dot(stacked[:rows], keys_at(span))

        total = lax.fori_loop(0, spans, second_pass, jnp.zeros((rows, LANES), F32), unroll=2)
        for place, number in enumerate(numbers):
            query = total[place * BLOCK : (place + 1) * BLOCK] * SCALE
            if slot == 1:
                query = jnp.where(low, stored(QUERIES, number), query)
            store(QUERIES, number, query)

    def walk(slot, length):
        def body(number, total):
            entry = sorted_ref[2 * slot, number]
            earlier = sorted_ref[2 * slot, jnp.maximum(number - 1, 0)]
            keep = jnp.where(table_ref[0, entry] == table_ref[0, earlier], 1.0, 0.0).astype(F32)
            total = total * keep + shares_ref[slot, entry]
            walked_ref[slot, number] = total.astype(BF16)
            return total

        lax.fori_loop(0, length, body, nothing, unroll=4)

    def close(slot, rank, component):
        def body(number, carry):
            block = rank * local + number
            stop = sorted_ref[2 * slot + 1, block]
            start = jnp.where(block == 0, 0, sorted_ref[2 * slot + 1, jnp.maximum(block - 1, 0)])
            some = jnp.where(stop > start, 1.0, 0.0).astype(F32)
            share = walked_ref[slot, jnp.maximum(stop - 1, 0)].astype(F32)
            store(component, block, sums_ref[slot, block] + share * some)
            return carry

        lax.fori_loop(0, local, body, 0, unroll=True)

    back = Inward(out_ref, back_ref, *back_sems)
    own_parts = (slice(0, 1), slice(1, 2), slice(2, 3))
    far_parts = (slice(0, 1),)
    packs = []

    for side in range(SPOTS):
        grads.arrive(side)
        head_a(side)
        if side == 0:
            for copy in loads:
                copy.wait()
            for one in reduces:
                one.corners()
        if side == 1:
            for one in reduces:
                one.sides()
    reduces[0].close(part_out_ref)
    reduces[1].close(part_up_ref.at[ready : PER_STAGE * STAGES])
    for number in range(LATE):
        reduces[2 + number].close(part_down_ref.at[EARLY + number])
    for bits in range(1, PLANES):
        goal = flip(plane, bits)
        late = slice(ready, PER_STAGE * STAGES)
        for copy in (
            far(bits, 1, part_out_ref.at[:, goal], far_out_ref.at[bits - 1]),
            far(bits, 2, part_up_ref.at[late, goal], far_up_ref.at[bits - 1, late]),
        ):
            copy.start()
            fars.append(copy)

        @pl.when(goal >= EARLY)
        def _(bits=bits, goal=goal):
            far_down(bits, part_down_ref.at[goal]).start()

        fars.append(far_down(bits, part_down_ref.at[goal]))
    dense(0, scores_refs[0], scores_refs[1], ends)
    walk(0, blocks * RANDOM)
    for side, other, goal, stays in inward_targets(core, spot):
        for piece in range(PIECES):
            close(0, (2 * other + piece) * SPOTS + goal, KEYS_A)
            if other is core:
                back.send(other, goal, stays, piece, 0, own_parts[0])
            else:
                back.send(other, goal, stays, piece, 0, far_parts[0])
                pack_halves(
                    lambda number, other=other, goal=goal, piece=piece: out_ref[
                        2 * other + piece, goal, QUERIES, number
                    ],
                    pack_ref,
                    (piece, goal),
                    local,
                    low,
                    0,
                )
                copy = remote(
                    pack_ref.at[piece, goal],
                    far_back_ref.at[spot, piece],
                    pack_send.at[piece, side],
                    pack_recv.at[spot, piece],
                    (other, rank_of(plane, goal)),
                )
                copy.start()
                packs.append(copy)
    lax.fori_loop(0, groups // 2, head_b, 0)
    dense(1, scores_refs[2], scores_refs[3], (core * (blocks - 1),))
    for side, other, goal, stays in inward_targets(core, spot):
        if other is core:
            for piece in range(PIECES):
                back.send(other, goal, stays, piece, 1, own_parts[1])
    walk(1, blocks * RANDOM // 2)
    for number in range(PIECES):
        for goal in range(SPOTS):
            close(1, (2 * (1 - core) + number) * SPOTS + goal, KEYS_B)
    across = remote(
        out_ref.at[pl.ds(2 * (1 - core), PIECES), :, KEYS_B],
        sibling_ref,
        sibling_sems[0],
        sibling_sems[1],
        (1 - core, rank_of(plane, spot)),
    )
    across.start()
    for number in range(PIECES):
        for goal in range(SPOTS):
            close(1, (2 * core + number) * SPOTS + goal, KEYS_B)
    across.wait_recv()
    for side, other, goal, stays in inward_targets(core, spot):
        if other is core:
            for piece in range(PIECES):
                place = (2 * core + piece, goal, KEYS_B)
                out_ref[place] = (
                    out_ref[place].astype(F32) + sibling_ref[piece, goal].astype(F32)
                ).astype(BF16)
                back.send(other, goal, stays, piece, 2, own_parts[2])
    for copy in fars:
        copy.wait()

    def total(part, far, index):
        value = part.astype(F32)
        for bits in range(PLANES - 1):
            value = value + far[(bits,) + index].astype(F32)
        return value

    t_out_ref[...] = total(part_out_ref[0, plane], far_out_ref, (0,))

    def close_up(number, carry):
        t_up_ref[number] = total(part_up_ref[number, plane], far_up_ref, (number,))
        return carry

    lax.fori_loop(0, PER_STAGE * STAGES, close_up, 0)
    t_down_ref[...] = total(part_down_ref[plane], far_down_ref, ())
    finish_hidden()
    grads.finish()
    across.wait_send()
    back.finish((own_parts, far_parts))
    for copy in packs:
        copy.wait_send()
    for goal in range(SPOTS):
        for piece in range(PIECES):
            target = far_back_ref.at[goal, piece]
            remote(
                target,
                target,
                pack_send.at[0, 0],
                pack_recv.at[goal, piece],
                (core, rank_of(plane, spot)),
            ).wait_recv()


def plane_attention_back(
    table, sorted_table, qk, shared, near, far, lse, hidden, sources, half_up, half_down
):
    local = qk.shape[3]
    blocks = PLANES * SPOTS * local
    spans = blocks // SPAN
    shard, rows = D // RANKS, FF // RANKS
    up_count = PER_STAGE * STAGES
    up_tail, out_tail = (2 * shard, LANES), (2 * shard, D // 2)
    buffers = block_scratch(1, *out_tail) + block_scratch(PER_STAGE * LATE, *up_tail)
    for _ in range(LATE):
        buffers += row_scratch(rows, D)
    count = 2 + LATE
    mines = [
        VMEM((1, PLANES, SPOTS) + out_tail, BF16),
        VMEM((PER_STAGE * LATE, PLANES, SPOTS) + up_tail, BF16),
    ] + [VMEM((SPOTS * rows, D), BF16)] * LATE
    parts = [
        VMEM((1, PLANES) + out_tail, BF16),
        VMEM((up_count, PLANES) + up_tail, BF16),
        VMEM((STAGES, rows, D), BF16),
        VMEM((PLANES - 1, 1) + out_tail, BF16),
        VMEM((PLANES - 1, up_count) + up_tail, BF16),
        VMEM((PLANES - 1, rows, D), BF16),
    ]
    tile = (local, BLOCK, LANES)
    wide = VMEM((spans, 2 * BLOCK, SPAN * BLOCK), F32)
    thin = VMEM((spans, BLOCK, SPAN * BLOCK), F32)
    dma = pltpu.SemaphoreType.DMA
    return pl.pallas_call(
        plane_attend_back_kernel,
        out_shape=(
            jax.ShapeDtypeStruct((2, SPOTS, PIECES, 3) + tile, BF16),
            jax.ShapeDtypeStruct((SPOTS, PIECES, local // 2, BLOCK, LANES), BF16),
            jax.ShapeDtypeStruct(hidden.shape, BF16),
            jax.ShapeDtypeStruct(out_tail, F32),
            jax.ShapeDtypeStruct((up_count,) + up_tail, F32),
            jax.ShapeDtypeStruct((rows, D), F32),
        ),
        in_specs=[
            whole(pltpu.SMEM),
            whole(pltpu.SMEM),
            whole(),
            whole(),
            whole(ANY),
            whole(ANY),
            whole(),
            whole(ANY),
        ]
        + [whole(ANY)] * 5,
        out_specs=(whole(ANY),) * 3 + (whole(),) * 3,
        scratch_shapes=buffers
        + mines
        + parts
        + [
            VMEM((PLANES, SPOTS) + tile, BF16),
            VMEM((PLANES, SPOTS, local // 2, BLOCK, LANES), BF16),
            VMEM((PLANES, SPOTS, 3) + tile, BF16),
            VMEM((2, blocks, BLOCK, LANES), F32),
            VMEM((2, blocks * RANDOM, BLOCK, LANES), F32),
            VMEM((2, blocks * RANDOM, BLOCK, LANES), BF16),
            VMEM((PIECES, SPOTS) + tile, BF16),
            VMEM((PIECES, SPOTS, local // 2, BLOCK, LANES), BF16),
            wide,
            wide,
            thin,
            thin,
            dma((count, SpotReduce.SEMS)),
            dma((count, SpotReduce.SEMS)),
            dma((4, PLANES - 1)),
            dma((4, PLANES - 1)),
            dma((count + 2,)),
        ]
        + exchange_sems((PLANES, SPOTS))
        + [
            dma((36,)),
            dma((2, SPOTS, PIECES, 3)),
            dma((3, PIECES)),
            dma((2,)),
            dma((2,)),
            dma((2,)),
            dma,
            dma,
            dma((PIECES, SPOTS)),
            dma((SPOTS, PIECES)),
        ],
        compiler_params=pltpu.CompilerParams(
            vmem_limit_bytes=62 * 1024 * 1024, collective_id=5, has_side_effects=True
        ),
        name="plane_attention_back",
    )(table, sorted_table, qk, shared, near, far, lse, hidden, *sources, half_up, half_down)


class PlaneGather:
    SENDS = 3 + 3 + 4 + 2

    def __init__(self, source, target, send_sem, column_sem, recv_sem, local_sem):
        self.source, self.target = source, target
        self.send_sem, self.column_sem, self.recv_sem = send_sem, column_sem, recv_sem
        self.core, self.plane, self.spot = place_here()
        self.sends = []
        self.own = pltpu.make_async_copy(
            source, target.at[self.core, self.plane, self.spot], local_sem
        )
        self.own.start()
        for bits in range(1, PLANES):
            copy = remote(
                source,
                target.at[self.core, self.plane, self.spot],
                send_sem.at[len(self.sends)],
                column_sem.at[self.plane],
                (self.core, rank_of(flip(self.plane, bits), self.spot)),
            )
            copy.start()
            self.sends.append(copy)

    def neighbour(self, bits):
        return (self.core, rank_of(self.plane, flip(self.spot, bits)))

    def sibling(self):
        return (1 - self.core, rank_of(self.plane, self.spot))

    def piece(self, core, planes, spot):
        return self.target.at[core, planes, spot]

    def send(self, planes, spot, part, goal):
        piece = self.piece(self.core, planes, spot)
        copy = remote(
            piece,
            piece,
            self.send_sem.at[len(self.sends)],
            self.recv_sem.at[self.core, spot, part],
            goal,
        )
        copy.start()
        self.sends.append(copy)

    def arrive(self, core, planes, spot, part):
        piece = self.piece(core, planes, spot)
        remote(
            piece,
            piece,
            self.send_sem.at[0],
            self.recv_sem.at[core, spot, part],
            (self.core, rank_of(self.plane, self.spot)),
        ).wait_recv()

    def columns(self):
        self.own.wait()
        for bits in range(1, PLANES):
            other = flip(self.plane, bits)
            shard = self.target.at[self.core, other, self.spot]
            remote(
                shard,
                shard,
                self.send_sem.at[0],
                self.column_sem.at[other],
                (self.core, rank_of(self.plane, self.spot)),
            ).wait_recv()
        for goal in (self.neighbour(1), self.neighbour(2), self.sibling()):
            self.send(slice(0, PLANES), self.spot, 0, goal)

    def forward(self):
        everything = slice(0, PLANES)
        for side in (1, 2):
            spot = flip(self.spot, side)
            self.arrive(self.core, everything, spot, 0)
            half = slice(0, 2) if side == 1 else slice(2, 4)
            self.send(half, spot, side - 1, self.neighbour(3 - side))
            self.send(everything, spot, 0, self.sibling())

    def corner(self):
        spot = flip(self.spot, 3)
        for part, half in enumerate((slice(0, 2), slice(2, 4))):
            self.arrive(self.core, half, spot, part)
            self.send(half, spot, part, self.sibling())

    def finish(self):
        for side in range(3):
            self.arrive(1 - self.core, slice(0, PLANES), flip(self.spot, side), 0)
        for part, half in enumerate((slice(0, 2), slice(2, 4))):
            self.arrive(1 - self.core, half, flip(self.spot, 3), part)
        for copy in self.sends:
            copy.wait_send()


class CrossGather:
    SENDS = 2 + 1 + 3 + 3 * 4

    def __init__(self, source, target, send_sem, spot_sem, recv_sem, local_sem):
        self.target = target
        self.send_sem, self.spot_sem, self.recv_sem = send_sem, spot_sem, recv_sem
        self.core, self.plane, self.spot = place_here()
        self.sends = []
        self.own = pltpu.make_async_copy(
            source, target.at[self.core, self.plane, self.spot], local_sem
        )
        self.own.start()
        for side in (1, 2):
            self.pass_on(source, self.spot, flip(self.spot, side))

    def push(self, source, target, recv_sem, device):
        copy = remote(source, target, self.send_sem.at[len(self.sends)], recv_sem, device)
        copy.start()
        self.sends.append(copy)

    def pass_on(self, source, spot, goal):
        self.push(
            source,
            self.target.at[self.core, self.plane, spot],
            self.spot_sem.at[spot],
            (self.core, rank_of(self.plane, goal)),
        )

    def await_spot(self, spot):
        shard = self.target.at[self.core, self.plane, spot]
        remote(
            shard,
            shard,
            self.send_sem.at[0],
            self.spot_sem.at[spot],
            (self.core, rank_of(self.plane, self.spot)),
        ).wait_recv()

    def across(self):
        beside, beyond = flip(self.spot, 1), flip(self.spot, 2)
        for side in (1, 2):
            self.await_spot(flip(self.spot, side))
        spot = beside * (1 - self.core) + beyond * self.core
        goal = beyond * (1 - self.core) + beside * self.core
        self.pass_on(self.target.at[self.core, self.plane, spot], spot, goal)

    def blocks(self):
        self.own.wait()
        self.await_spot(flip(self.spot, 3))
        self.maybe = []
        self.along(self.plane, 1, self.plane < PLANES - 1)
        self.along(self.plane, -1, self.plane > 0)
        self.to_sibling(self.plane, self.plane >= 0)

    def along(self, plane, step, wanted):
        block = self.target.at[self.core, plane]
        copy = remote(
            block,
            block,
            self.send_sem.at[3 + len(self.maybe)],
            self.recv_sem.at[self.core, plane],
            (self.core, rank_of(self.plane + step, self.spot)),
        )
        self.begin(copy, wanted)

    def to_sibling(self, plane, wanted):
        block = self.target.at[self.core, plane]
        copy = remote(
            block,
            block,
            self.send_sem.at[3 + len(self.maybe)],
            self.recv_sem.at[self.core, plane],
            (1 - self.core, rank_of(self.plane, self.spot)),
        )
        self.begin(copy, wanted)

    def begin(self, copy, wanted):
        self.maybe.append((copy, wanted))

        @pl.when(wanted)
        def _():
            copy.start()

    def arrive(self, core, plane):
        block = self.target.at[core, plane]
        remote(
            block,
            block,
            self.send_sem.at[0],
            self.recv_sem.at[core, plane],
            (self.core, rank_of(self.plane, self.spot)),
        ).wait_recv()

    def hop(self, distance):
        for step in (1, -1):
            origin = self.plane - step * distance
            here = (origin >= 0) & (origin < PLANES)
            onward = self.plane + step
            more = here & (onward >= 0) & (onward < PLANES)

            @pl.when(here)
            def _(origin=origin):
                self.arrive(self.core, origin)

            self.along(origin, step, more)
            self.to_sibling(origin, here)

    def finish(self):
        for bits in range(PLANES):
            self.arrive(1 - self.core, flip(self.plane, bits))
        for copy in self.sends:
            copy.wait_send()
        for copy, wanted in self.maybe:

            @pl.when(wanted)
            def _(copy=copy):
                copy.wait_send()


def pair_of_blocks(read, first, second):
    low = low_lanes(1)
    tiles = []
    for block, wanted in ((first, 0), (second, 1)):
        tile = read(block // 2)
        tiles.append(tile if block % 2 == wanted else swap_halves(tile))
    return jnp.where(low, tiles[0], tiles[1])


def fold_tiles(target_ref, start, tiles, read):
    half = len(tiles) // 2
    for number in range(half):
        columns = slice((start + number) * LANES, (start + number + 1) * LANES)
        target_ref[:, columns] = jnp.concatenate(
            [read(tiles[number]), read(tiles[half + number])], axis=0
        ).astype(BF16)


VECTORS = 8


def lay_vectors(vecs_ref, vectors_ref, up_ref):
    rows = vecs_ref.shape[3]
    own, wide = D // RANKS, FF // RANKS
    values = vecs_ref[...].reshape(RANKS, rows, LANES).astype(F32)

    def spread_out(count, width):
        place = lax.broadcasted_iota(jnp.int32, (LANES, count), 1)
        lane = lax.broadcasted_iota(jnp.int32, (LANES, count), 0)
        start = lax.div(place, width) * width
        return jnp.where(place - start == lane, 1.0, 0.0).astype(BF16)

    laid = dot(vecs_ref[...].reshape(RANKS * rows, LANES), spread_out(D, own))
    owner = lax.broadcasted_iota(jnp.int32, (RANKS, 1, D), 0)
    column = lax.broadcasted_iota(jnp.int32, (RANKS, 1, D), 2)
    laid = jnp.where(lax.div(column, own) == owner, laid.reshape(RANKS, rows, D), 0.0)
    vectors_ref[...] = jnp.sum(laid, axis=0)[:VECTORS]
    row = lax.broadcasted_iota(jnp.int32, (1, rows, LANES), 1)
    last = jnp.sum(jnp.where(row == VECTORS, values, 0.0), axis=1)
    laid = dot(last.astype(BF16), spread_out(FF, wide))
    owner = lax.broadcasted_iota(jnp.int32, (RANKS, FF), 0)
    column = lax.broadcasted_iota(jnp.int32, (RANKS, FF), 1)
    laid = jnp.sum(jnp.where(lax.div(column, wide) == owner, laid, 0.0), axis=0, keepdims=True)
    for chunk in range(FF // CHUNK):
        for side in range(2):
            start = side * (FF // 2) + chunk * LANES
            up_ref[chunk, :, side * LANES : (side + 1) * LANES] = laid[:, start : start + LANES]


def lay_table(tables_ref, core, micro, entries):
    count = 2 * LANES
    ranks = PLANES * SPOTS
    values = tables_ref[core].reshape(ranks, tables_ref.shape[3], LANES).astype(F32)
    row = lax.broadcasted_iota(jnp.int32, (1, tables_ref.shape[3], LANES), 1)
    values = jnp.sum(jnp.where(row == micro, values, 0.0), axis=1)
    place = lax.broadcasted_iota(jnp.int32, (LANES, count), 1)
    lane = lax.broadcasted_iota(jnp.int32, (LANES, count), 0)
    start = lax.div(place, entries) * entries
    laid = dot(values.astype(BF16), jnp.where(place - start == lane, 1.0, 0.0).astype(BF16))
    owner = lax.broadcasted_iota(jnp.int32, (ranks, count), 0)
    column = lax.broadcasted_iota(jnp.int32, (ranks, count), 1)
    laid = jnp.sum(jnp.where(lax.div(column, entries) == owner, laid, 0.0), axis=0, keepdims=True)
    column = lax.broadcasted_iota(jnp.int32, (1, count), 1)
    return jnp.where(column < ranks * entries, laid, 2.0 * LANES)


def front_kernel(
    x_in_ref,
    dy_ref,
    vec_ref,
    tab_ref,
    w_qkv_in_ref,
    w_out_in_ref,
    w_up_in_ref,
    w_down_in_ref,
    back_ref,
    far_back_ref,
    x_ref,
    dys_ref,
    w_down_ref,
    w_qkv_hbm,
    w_out_hbm,
    w_up_hbm,
    qk_hbm,
    shared_hbm,
    normed_ref,
    lse_ref,
    vectors_ref,
    up_ref,
    table_ref,
    sorted_ref,
    s_qkv_ref,
    s_ou_ref,
    g_qkv_ref,
    g_ou_ref,
    w_qkv_ref,
    w_out_ref,
    w_up_ref,
    xs_ref,
    vecs_ref,
    tabs_ref,
    bias_ref,
    send_ref,
    qk_ref,
    shared_ref,
    out_ref,
    pack_ref,
    p_ref,
    q_ref,
    picks_ref,
    *sems,
):
    gather_send, gather_recv, gather_local = sems[:3]
    plane_sems, cross_sems = sems[3:7], sems[7:11]
    x_sems, dy_sems = sems[11:14], sems[14:17]
    qkv_send, qkv_recv, qkv_local, shared_send, shared_recv = sems[17:22]
    back_send, back_recv, back_local, far_send, far_recv, local_sem = sems[22:28]
    core, plane, spot = place_here()
    micro, rows, _ = x_in_ref.shape
    tokens = PIECES * rows
    local = rows // BLOCK
    blocks = PLANES * SPOTS * local

    barrier = pltpu.get_barrier_semaphore()
    partners = both_partners(core, plane, spot)
    for partner in partners:
        pl.semaphore_signal(barrier, inc=1, device_id=partner, device_id_type=MESH)

    def natural(ref):
        return lambda tile: ref[:, tile * LANES : (tile + 1) * LANES].astype(F32)

    order = [natural_block(entry) for entry in column_order()]
    read = natural(w_qkv_in_ref)
    fold_tiles(
        s_qkv_ref,
        0,
        list(range(TILES)),
        lambda tile: pair_of_blocks(read, order[2 * tile], order[2 * tile + 1]),
    )
    pl.semaphore_wait(barrier, len(partners))

    gathers = []
    for number, (source, target) in enumerate(
        ((tab_ref, tabs_ref), (vec_ref, vecs_ref), (s_qkv_ref, g_qkv_ref))
    ):
        one = Gather(
            source, target, gather_send.at[number], gather_recv.at[number], gather_local.at[number]
        )
        one.start()
        gathers.append(one)
    outs = D // LANES // 2
    fold_tiles(s_ou_ref, 0, list(range(D // LANES)), natural(w_out_in_ref))
    fold_tiles(s_ou_ref, outs, list(range(FF // LANES)), natural(w_up_in_ref))
    for one in gathers:
        one.column()
    finish_x = to_planes(x_in_ref, xs_ref, *x_sems)
    cross = CrossGather(w_down_in_ref, w_down_ref, *cross_sems)
    for one in gathers:
        one.across()
    for one in gathers:
        one.corner()
    cross.across()
    for one in gathers[:2]:
        one.finish()
    window_core, window_micro = lax.rem(plane, 2), lax.div(plane, 2)
    scalars = pltpu.make_async_copy(tabs_ref.at[window_core], picks_ref, local_sem.at[1])
    scalars.start()
    lay_vectors(vecs_ref, vectors_ref, up_ref)
    for tile in range(TILES):
        halves = []
        for entry in column_order()[2 * tile : 2 * tile + 2]:
            halves.append(entry)

        def bias_tile(number, halves=halves):
            if number < D // LANES:
                return vectors_ref[2:3, number * LANES : (number + 1) * LANES]
            if number < 2 * D // LANES:
                return jnp.zeros((1, LANES), F32)
            start = (number - 2 * D // LANES) * LANES
            return vectors_ref[3:4, start : start + LANES]

        chunk, side = tile % HALF_TILES, tile // HALF_TILES
        start = chunk * CHUNK + side * LANES
        bias_ref[:, start : start + LANES] = pair_of_blocks(
            bias_tile, order[2 * tile], order[2 * tile + 1]
        )
    spread = PlaneGather(s_ou_ref, g_ou_ref, *plane_sems)
    gathers[2].finish()
    settle(g_qkv_ref, [(tile, w_qkv_ref, alternate(tile)) for tile in range(HALF_TILES)])
    keep_w = pltpu.make_async_copy(w_qkv_ref, w_qkv_hbm, local_sem.at[2])
    keep_w.start()

    finish_x()
    keep_x = pltpu.make_async_copy(xs_ref, x_ref, local_sem.at[0])
    keep_x.start()
    normal, _ = norm_parts(xs_ref[...].reshape(tokens, D).astype(F32))
    normed_ref[...] = (normal * vectors_ref[0:1] + vectors_ref[1:2]).astype(BF16)

    def shaped(value):
        return value.astype(BF16).reshape(local, BLOCK, LANES)

    low = low_lanes(rows)
    queries = D // LANES
    for chunk in range(HALF_TILES):
        columns = slice(chunk * CHUNK, (chunk + 1) * CHUNK)
        packed = dot(normed_ref[...], w_qkv_ref[:, columns]) + bias_ref[:, columns]
        for side in range(2):
            tile = chunk + side * HALF_TILES
            whole_tile = packed[:, side * LANES : (side + 1) * LANES]
            if tile < queries:
                whole_tile = whole_tile.astype(BF16).astype(F32) * SCALE
            for piece in range(PIECES):
                part = whole_tile[piece * rows : (piece + 1) * rows]
                if tile < SPOTS:
                    send_ref[0, tile, piece, 0] = shaped(part)
                elif tile < queries:
                    first = 2 * (tile - SPOTS)
                    shared = send_ref[0, first, piece, 0].reshape(rows, LANES).astype(F32)
                    send_ref[1, first, piece, 0] = shaped(jnp.where(low, part, shared))
                    shared = send_ref[0, first + 1, piece, 0].reshape(rows, LANES).astype(F32)
                    send_ref[1, first + 1, piece, 0] = shaped(
                        jnp.where(low, swap_halves(part), shared)
                    )
                else:
                    goal, role = (tile - queries) // 3, (tile - queries) % 3
                    if role < 2:
                        send_ref[role, goal, piece, 1] = shaped(part)
                    else:
                        send_ref[0, goal, piece, 2] = shaped(part)
    sends, keeps = [], []
    for part, (parts, landing) in enumerate(((slice(0, 2), qk_ref), (2, shared_ref))):
        for side in (3, 1, 2, 0):
            for other in (core, 1 - core) if part == 0 else (core,):
                goal = flip(spot, side)
                for piece in range(PIECES):
                    source = send_ref.at[other if part == 0 else 0, goal, piece, parts]
                    target = landing.at[2 * core + piece, spot]
                    if side == 0 and other is core:
                        copy = pltpu.make_async_copy(source, target, qkv_local.at[part, piece])
                        keeps.append((part, copy))
                    else:
                        copy = remote(
                            source,
                            target,
                            qkv_send.at[len(sends)],
                            qkv_recv.at[2 * core + piece, spot, part],
                            (other, rank_of(plane, goal)),
                        )
                        sends.append(copy)
                    copy.start()
    spread.columns()
    cross.blocks()
    table = lay_table(tabs_ref, window_core, window_micro, local * RANDOM)
    table_ref[...] = table.astype(jnp.int32)
    sort_entries(table, sorted_ref, blocks * RANDOM)
    scalars.wait()

    def arrive(part, other, piece, goal):
        target = (qk_ref, shared_ref)[part].at[2 * other + piece, goal]
        remote(
            target,
            target,
            qkv_send.at[0],
            qkv_recv.at[2 * other + piece, goal, part],
            (core, rank_of(plane, spot)),
        ).wait_recv()

    for side in range(SPOTS):
        for other in (core, 1 - core):
            if side > 0 or other is not core:
                for piece in range(PIECES):
                    arrive(0, other, piece, flip(spot, side))
    for part, copy in keeps:
        copy.wait()
    cross.hop(1)

    low = low_lanes(BLOCK)
    masks = [half_mask(True), half_mask(False)]

    def tile_of(component, block):
        rank, number = lax.div(block, local), lax.rem(block, local)
        if component == 2:
            return shared_ref[lax.div(rank, SPOTS), lax.rem(rank, SPOTS), number]
        return qk_ref[lax.div(rank, SPOTS), lax.rem(rank, SPOTS), component, number]

    def picked(block, number):
        rank = lax.div(block, local)
        return picks_ref[
            lax.div(rank, SPOTS),
            lax.rem(rank, SPOTS),
            window_micro,
            lax.rem(block, local) * RANDOM + number,
        ]

    def place_of(block):
        rank = lax.div(block, local)
        return lax.div(rank, SPOTS), lax.rem(rank, SPOTS), lax.rem(block, local)

    def put(block, slot, mixed, log):
        place = place_of(block)
        if slot == 0:
            out_ref[place] = mixed.astype(BF16)
            lse_ref[block] = jnp.where(low, log, 0.0)
        else:
            out_ref[place] = jnp.where(low, mixed, out_ref[place].astype(F32)).astype(BF16)
            lse_ref[block] = jnp.where(low, lse_ref[block], log)

    def one_block(block, slot):
        ids, bias = inner_slots(picked, block, blocks)
        keys = jnp.concatenate([tile_of(1 + slot, number) for number in ids], axis=0)
        scores = dot_rt(tile_of(0, block) * masks[slot], keys) + bias
        top = jnp.max(scores, axis=1, keepdims=True)
        powered = jnp.exp(scores - top)
        total = jnp.sum(powered, axis=1, keepdims=True)
        mixed = dot(powered.astype(BF16), keys) * (1.0 / total)
        return mixed, top + jnp.log(total)

    def rank_blocks(rank, slot):
        results = [one_block(rank * local + number, slot) for number in range(local)]
        for number, (mixed, log) in enumerate(results):
            put(rank * local + number, slot, mixed, log)

    spans = blocks // SPAN
    ends = (0, blocks - 1)

    def dense(slot, scores_ref, numbers):
        size = len(numbers) * BLOCK
        query = jnp.concatenate([tile_of(0, number) * masks[slot] for number in numbers], axis=0)

        def keys_at(span):
            return jnp.concatenate(
                [tile_of(1 + slot, span * SPAN + number) for number in range(SPAN)], axis=0
            )

        def first_pass(span, top):
            scores = dot_rt(query, keys_at(span))
            scores_ref[span] = scores
            return jnp.maximum(top, jnp.max(scores, axis=1, keepdims=True))

        top = lax.fori_loop(
            0, spans, first_pass, jnp.full((size, 1), NEGATIVE, F32), unroll=2
        )

        def second_pass(span, carry):
            total, mixed = carry
            powered = jnp.exp(scores_ref[span] - top)
            return (
                total + jnp.sum(powered, axis=1, keepdims=True),
                mixed + dot(powered.astype(BF16), keys_at(span)),
            )

        total, mixed = lax.fori_loop(
            0,
            spans,
            second_pass,
            (jnp.zeros((size, 1), F32), jnp.zeros((size, LANES), F32)),
            unroll=2,
        )
        mixed = mixed * (1.0 / total)
        log = top + jnp.log(total)
        for place, number in enumerate(numbers):
            span = slice(place * BLOCK, (place + 1) * BLOCK)
            put(number, slot, mixed[span], log[span])

    def head_a(number, carry):
        rank_blocks(number, 0)
        return carry

    def head_b(number, carry):
        rank_blocks(core * (PLANES * SPOTS // 2) + number, 1)
        return carry

    shared = []
    half_way = PLANES * SPOTS // 2
    lax.fori_loop(0, half_way, head_a, 0)
    for side in range(SPOTS):
        goal = flip(spot, side)
        for piece in range(PIECES):
            if side > 0:
                arrive(1, core, piece, goal)
            source = shared_ref.at[2 * core + piece, goal]
            copy = remote(
                source,
                source,
                shared_send.at[2 * side + piece],
                shared_recv.at[2 * core + piece, goal],
                (1 - core, rank_of(plane, spot)),
            )
            copy.start()
            shared.append(copy)
    finish_dy = to_planes(dy_ref, dys_ref, *dy_sems)
    lax.fori_loop(half_way, PLANES * SPOTS, head_a, 0)
    dense(0, p_ref, ends)
    spread.forward()
    backs, stay = [], []
    for side in (3, 1, 2, 0):
        goal = flip(spot, side)
        for piece in range(PIECES):
            pack_halves(
                lambda number, piece=piece, goal=goal: out_ref[
                    2 * (1 - core) + piece, goal, number
                ],
                pack_ref,
                (piece, goal),
                local,
                low,
                1,
            )
            copy = remote(
                pack_ref.at[piece, goal],
                far_back_ref.at[spot, piece],
                far_send.at[piece, side],
                far_recv.at[spot, piece],
                (1 - core, rank_of(plane, goal)),
            )
            copy.start()
            backs.append(copy)
    for side in range(SPOTS):
        for piece in range(PIECES):
            target = shared_ref.at[2 * (1 - core) + piece, flip(spot, side)]
            remote(
                target,
                target,
                shared_send.at[0],
                shared_recv.at[2 * (1 - core) + piece, flip(spot, side)],
                (core, rank_of(plane, spot)),
            ).wait_recv()
    cross.hop(2)
    keep_qk = pltpu.make_async_copy(qk_ref, qk_hbm, local_sem.at[3])
    keep_qk.start()
    keep_shared = pltpu.make_async_copy(shared_ref, shared_hbm, local_sem.at[6])
    keep_shared.start()
    lax.fori_loop(0, half_way, head_b, 0)
    dense(1, q_ref, (core * (blocks - 1),))
    spread.corner()
    for side in (3, 1, 2, 0):
        goal = flip(spot, side)
        for piece in range(PIECES):
            source, target = out_ref.at[2 * core + piece, goal], back_ref.at[spot, piece]
            if side == 0:
                copy = pltpu.make_async_copy(source, target, back_local.at[piece])
                stay.append(copy)
            else:
                copy = remote(
                    source,
                    target,
                    back_send.at[piece, side],
                    back_recv.at[spot, piece],
                    (core, rank_of(plane, goal)),
                )
                backs.append(copy)
            copy.start()
    cross.hop(3)
    spread.finish()
    settle(
        g_ou_ref,
        [(tile, w_out_ref, (tile, outs + tile)) for tile in range(outs)]
        + [(outs + tile, w_up_ref, alternate(tile)) for tile in range(FF // CHUNK)],
    )
    keep_out = pltpu.make_async_copy(w_out_ref, w_out_hbm, local_sem.at[4])
    keep_out.start()
    keep_up = pltpu.make_async_copy(w_up_ref, w_up_hbm, local_sem.at[5])
    keep_up.start()
    cross.finish()
    finish_dy()
    for copy in sends:
        copy.wait_send()
    for copy in shared:
        copy.wait_send()
    for side in range(SPOTS):
        goal = flip(spot, side)
        for piece in range(PIECES):
            here = (core, rank_of(plane, spot))
            if side > 0:
                target = back_ref.at[goal, piece]
                remote(target, target, back_send.at[0, 0], back_recv.at[goal, piece], here).wait_recv()
            target = far_back_ref.at[goal, piece]
            remote(target, target, far_send.at[0, 0], far_recv.at[goal, piece], here).wait_recv()
    for copy in backs:
        copy.wait_send()
    for copy in stay:
        copy.wait()
    for copy in (keep_x, keep_w, keep_qk, keep_shared, keep_out, keep_up):
        copy.wait()


def front(x, dy, vec, tab, w_qkv, w_out, w_up, w_down):
    micro, rows, _ = x.shape
    tokens = PIECES * rows
    local = rows // BLOCK
    blocks = PLANES * SPOTS * local
    spans = blocks // SPAN
    grid = (2, PLANES, SPOTS)
    shard = D // RANKS
    tile = (local, BLOCK, LANES)
    dma = pltpu.SemaphoreType.DMA
    struct = jax.ShapeDtypeStruct
    ou = (2 * shard, (D + FF) // 2)
    return pl.pallas_call(
        front_kernel,
        out_shape=(
            struct((SPOTS, PIECES) + tile, BF16),
            struct((SPOTS, PIECES, local // 2, BLOCK, LANES), BF16),
            struct(x.shape, BF16),
            struct(dy.shape, BF16),
            struct(grid + w_down.shape, BF16),
            struct((D, 3 * D), BF16),
            struct((D, D), BF16),
            struct((D, FF), BF16),
            struct((PLANES, SPOTS, 2) + tile, BF16),
            struct((PLANES, SPOTS) + tile, BF16),
            struct((tokens, D), BF16),
            struct((blocks, BLOCK, LANES), F32),
            struct((VECTORS, D), F32),
            struct((FF // CHUNK, 1, CHUNK), F32),
            struct((1, 2 * LANES), jnp.int32),
            struct((4, 2 * LANES), jnp.int32),
        ),
        in_specs=[
            whole(ANY),
            whole(ANY),
            whole(ANY),
            whole(ANY),
            whole(),
            whole(),
            whole(),
            whole(ANY),
        ],
        out_specs=(whole(ANY),) * 10 + (whole(),) * 6,
        scratch_shapes=[
            VMEM((2 * shard, 3 * D // 2), BF16),
            VMEM(ou, BF16),
            VMEM(grid + (2 * shard, 3 * D // 2), BF16),
            VMEM(grid + ou, BF16),
            VMEM((D, 3 * D), BF16),
            VMEM((D, D), BF16),
            VMEM((D, FF), BF16),
            VMEM((PIECES, rows, D), BF16),
            VMEM(grid + vec.shape, BF16),
            VMEM(grid + tab.shape, jnp.int32),
            VMEM((1, 3 * D), F32),
            VMEM((2, SPOTS, PIECES, 3) + tile, BF16),
            VMEM((PLANES, SPOTS, 2) + tile, BF16),
            VMEM((PLANES, SPOTS) + tile, BF16),
            VMEM((PLANES, SPOTS) + tile, BF16),
            VMEM((PIECES, SPOTS, local // 2, BLOCK, LANES), BF16),
            VMEM((spans, 2 * BLOCK, SPAN * BLOCK), F32),
            VMEM((spans, BLOCK, SPAN * BLOCK), F32),
            pltpu.SMEM((PLANES, SPOTS) + tab.shape, jnp.int32),
            dma((3, Gather.SENDS)),
            dma((3,) + grid),
            dma((3,)),
            dma((PlaneGather.SENDS,)),
            dma((PLANES,)),
            dma((2, SPOTS, 2)),
            dma,
            dma((CrossGather.SENDS,)),
            dma((SPOTS,)),
            dma((2, PLANES)),
            dma,
        ]
        + [dma((2,))] * 6
        + [
            dma((20,)),
            dma((PLANES, SPOTS, 2)),
            dma((2, PIECES)),
            dma((2 * SPOTS,)),
            dma((PLANES, SPOTS)),
            dma((PIECES, SPOTS)),
            dma((SPOTS, PIECES)),
            dma((PIECES,)),
            dma((PIECES, SPOTS)),
            dma((SPOTS, PIECES)),
            dma((7,)),
        ],
        compiler_params=pltpu.CompilerParams(
            vmem_limit_bytes=60 * 1024 * 1024, collective_id=1, has_side_effects=True
        ),
        name="front",
    )(x, dy, vec, tab, w_qkv, w_out, w_up, w_down)


class SpotReduce:
    SEMS = 4

    def __init__(self, source, near, corner, sides, send_sem, recv_sem, rows=None, mine=None):
        self.source, self.near, self.corner, self.side = source, near, corner, sides
        self.send_sem, self.recv_sem, self.rows, self.mine = send_sem, recv_sem, rows, mine
        self.core, self.plane, self.spot = place_here()
        beside, beyond = flip(self.spot, 1), flip(self.spot, 2)
        self.via = beyond * (1 - self.core) + beside * self.core
        self.other = beside * (1 - self.core) + beyond * self.core

    def half(self, core):
        return self.source.at[core] if self.rows else self.source.at[:, core]

    def part(self, spot):
        if self.rows:
            start = pl.multiple_of(spot * self.rows, 16)
            return self.near.at[pl.ds(start, self.rows)]
        return self.near.at[:, :, spot]

    def copy(self, number):
        sibling = (1 - self.core, rank_of(self.plane, self.spot))
        if number == 0:
            source, target, device = self.half(1 - self.core), self.near, sibling
        elif number == 1:
            source, target = self.part(flip(self.spot, 3)), self.corner
            device = (self.core, rank_of(self.plane, self.via))
        else:
            spot = flip(self.spot, number - 1)
            source, target = self.part(spot), self.side.at[number - 2]
            device = (self.core, rank_of(self.plane, spot))
        return remote(source, target, self.send_sem.at[number], self.recv_sem.at[number], device)

    def start(self):
        self.copy(0).start()

    def add(self, spot, terms, target=None):
        if self.rows:
            rows = self.rows

            def slab(number, carry):
                size = rows // 3
                first = pl.multiple_of(spot * rows + number * size, 16)
                place = pl.ds(first, size)
                inner = pl.ds(pl.multiple_of(number * size, 16), size)
                total = self.near[place].astype(F32)
                for read in terms:
                    total = total + read(place, inner).astype(F32)
                if target is None:
                    self.near[place] = total.astype(BF16)
                else:
                    target[inner] = total.astype(BF16)
                return carry

            lax.fori_loop(0, 3, slab, 0, unroll=True)
            return
        count = self.near.shape[0]

        def block(number, carry):
            first, plane = lax.div(number, PLANES), lax.rem(number, PLANES)
            total = self.near[first, plane, spot].astype(F32)
            for read in terms:
                total = total + read(first, plane).astype(F32)
            if target is None:
                self.near[first, plane, spot] = total.astype(BF16)
            else:
                target[first, plane] = total.astype(BF16)
            return carry

        lax.fori_loop(0, count * PLANES, block, 0, unroll=4)

    def corners(self):
        self.copy(0).wait_recv()
        core = self.core
        for spot in range(SPOTS):
            if self.rows and self.mine is None:
                self.add(spot, [lambda place, inner: self.source[core, place]])
            elif self.rows:
                self.add(spot, [lambda place, inner: self.mine[place]])
            elif self.mine is None:
                self.add(spot, [lambda first, plane, spot=spot: self.source[first, core, plane, spot]])
            else:
                self.add(spot, [lambda first, plane, spot=spot: self.mine[first, plane, spot]])
        self.copy(1).start()

    def sides(self):
        self.copy(1).wait_recv()
        if self.rows:
            self.add(self.other, [lambda place, inner: self.corner[inner]])
        else:
            self.add(self.other, [lambda first, plane: self.corner[first, plane]])
        self.copy(2).start()
        self.copy(3).start()

    def close(self, target):
        self.copy(2).wait_recv()
        self.copy(3).wait_recv()
        if self.rows:
            terms = [lambda place, inner, n=n: self.side[n, inner] for n in range(2)]
        else:
            terms = [lambda first, plane, n=n: self.side[n, first, plane] for n in range(2)]
        self.add(self.spot, terms, target)
        for number in range(self.SEMS):
            self.copy(number).wait_send()


def block_scratch(count, rows, width):
    return [
        VMEM((count, PLANES, SPOTS, rows, width), BF16),
        VMEM((count, PLANES, rows, width), BF16),
        VMEM((2, count, PLANES, rows, width), BF16),
    ]


def row_scratch(rows, width):
    return [
        VMEM((SPOTS * rows, width), BF16),
        VMEM((rows, width), BF16),
        VMEM((2, rows, width), BF16),
    ]


STAGES = 4
PER_STAGE = FF // CHUNK // STAGES
EARLY = 2
LATE = STAGES - EARLY
WAITS = (2, 4, 6)


def by_owner(out_ref, values):
    rows = D // RANKS
    width = values.shape[1] // 2
    for owner in range(RANKS):
        part = values[owner * rows : (owner + 1) * rows]
        out_ref[owner] = jnp.concatenate([part[:, :width], part[:, width:]], axis=0).astype(BF16)


def plane_middle_kernel(
    mixed_in_ref,
    far_in_ref,
    x_ref,
    dy_ref,
    vec_ref,
    w_out_ref,
    up_shift_ref,
    w_up_ref,
    w_down_ref,
    hidden_ref,
    send_ref,
    far_ref,
    dres_ref,
    g_out_ref,
    half_up_ref,
    half_down_ref,
    last_up_ref,
    last_down_ref,
    g_up_bias_ref,
    g_small_ref,
    mixed_ref,
    residual_ref,
    second_ref,
    second_t_ref,
    total_ref,
    dsecond_ref,
    g_up_ref,
    g_down_ref,
    *scratch,
):
    send_sem, recv_sem, local_sem = scratch[-3:]
    stages = []
    for number in range(EARLY):
        buffers = scratch[6 * number : 6 * number + 6]
        stages.append(
            (
                SpotReduce(
                    g_up_ref.at[PER_STAGE * number : PER_STAGE * (number + 1)],
                    *buffers[:3],
                    send_sem.at[number, 0],
                    recv_sem.at[number, 0],
                ),
                SpotReduce(
                    g_down_ref.at[number],
                    *buffers[3:],
                    send_sem.at[number, 1],
                    recv_sem.at[number, 1],
                    rows=FF // RANKS,
                ),
            )
        )
    pieces, rows, _ = x_ref.shape
    tokens = pieces * rows
    step = pl.program_id(0)
    low = low_lanes(rows)
    out_shift, gain, shift, down_shift = (vec_ref[number : number + 1] for number in (4, 5, 6, 7))

    @pl.when(step == 0)
    def _():
        core, plane, spot = place_here()
        greet(
            [
                (1 - core, rank_of(plane, spot)),
                (core, rank_of(plane, flip(spot, 1))),
                (core, rank_of(plane, flip(spot, 2))),
            ]
        )
        def received(spot, piece):
            own = mixed_in_ref[spot, piece].astype(F32)
            halves = far_in_ref[spot, piece].astype(F32)
            parts = []
            for number in range(rows // BLOCK // 2):
                part = halves[number * BLOCK : (number + 1) * BLOCK]
                parts += [part, swap_halves(part)]
            other = jnp.concatenate(parts, axis=0)
            return (jnp.where(core == 0, own, other), jnp.where(core == 0, other, own)), own

        for piece in range(pieces):
            span = slice(piece * rows, (piece + 1) * rows)
            for spot in (0, 2):
                first, own_first = received(spot, piece)
                last_two, own_last = received(spot + 1, piece)
                tiles = (
                    jnp.where(low, swap_halves(first[0]), first[1]),
                    jnp.where(low, own_first, last_two[0]),
                    swap_halves(jnp.where(low, own_last, last_two[1])),
                )
                for number, tile in enumerate(tiles):
                    spread = 3 * (spot // 2) + number
                    mixed_ref[span, spread * LANES : (spread + 1) * LANES] = tile.astype(BF16)
        residual = x_ref[...].reshape(tokens, D).astype(F32) + (
            dot(mixed_ref[...], w_out_ref[...]) + out_shift
        )
        residual_ref[...] = residual
        normal, _ = norm_parts(residual)
        second = normal * gain + shift
        second_ref[...] = second.astype(BF16)
        second_t_ref[...] = second.T.astype(BF16)
        total_ref[...] = jnp.zeros_like(total_ref)
        dsecond_ref[...] = jnp.zeros_like(dsecond_ref)

    w_down = w_down_ref[...].reshape(CHUNK, D)
    upper = dot(second_ref[...], w_up_ref[...]) + up_shift_ref[0]
    factor = 0.7978845608028654
    square = upper * upper
    bent = jnp.tanh(factor * (upper + 0.044715 * (upper * square)))
    middle_half = 0.5 * (1.0 + bent)
    active = (upper * middle_half).astype(BF16)
    slope = middle_half + 0.5 * upper * (1.0 - bent * bent) * (
        factor + (3.0 * 0.044715 * factor) * square
    )
    dy = dy_ref[...]
    total_ref[...] += dot(active, w_down)
    stage, turn = lax.div(step, PER_STAGE), lax.rem(step, PER_STAGE)
    down_share = dot_lt(active, dy).astype(BF16)
    place = pl.ds(pl.multiple_of(turn * LANES, LANES), LANES)
    for side in range(2):
        g_down_ref[stage, side, place] = down_share[side * LANES : (side + 1) * LANES]
    dupper = (dot_rt(dy, w_down) * slope).astype(BF16)
    g_up_bias_ref[0] = jnp.sum(dupper.astype(F32), axis=0, keepdims=True)
    up_share = dot(second_t_ref[...], dupper)
    shard = D // RANKS
    for owner in range(RANKS):
        part = up_share[owner * shard : (owner + 1) * shard]
        g_up_ref[step, owner // (PLANES * SPOTS), owner // SPOTS % PLANES, owner % SPOTS] = (
            jnp.concatenate([part[:, :LANES], part[:, LANES:]], axis=0).astype(BF16)
        )
    dsecond_ref[...] += dot_rt(dupper, w_up_ref[...])

    last = FF // CHUNK - 1
    for number, pair in enumerate(stages):
        done = PER_STAGE * (number + 1) - 1

        @pl.when(step == done)
        def _(pair=pair):
            for one in pair:
                one.start()

        @pl.when(step == done + WAITS[0])
        def _(pair=pair):
            for one in pair:
                one.corners()

        @pl.when(step == done + WAITS[1])
        def _(pair=pair):
            for one in pair:
                one.sides()

        if done + WAITS[2] < last:

            @pl.when(step == done + WAITS[2])
            def _(pair=pair, number=number):
                pair[0].close(half_up_ref.at[PER_STAGE * number : PER_STAGE * (number + 1)])
                pair[1].close(half_down_ref.at[number])

    @pl.when(step == last)
    def _():
        keep_up = pltpu.make_async_copy(
            g_up_ref.at[PER_STAGE * EARLY : PER_STAGE * STAGES], last_up_ref, local_sem.at[0]
        )
        keep_up.start()
        keep_down = pltpu.make_async_copy(
            g_down_ref.at[EARLY:STAGES], last_down_ref, local_sem.at[1]
        )
        keep_down.start()
        residual = residual_ref[...]
        hidden_ref[...] = (
            (residual + (total_ref[...] + down_shift)).astype(BF16).reshape(x_ref.shape)
        )
        normal, inverse = norm_parts(residual)
        dsecond = dsecond_ref[...]
        grad_out = dy_ref[...].astype(F32)
        g_small_ref[0:1] = jnp.sum(dsecond * normal, axis=0, keepdims=True)
        g_small_ref[1:2] = jnp.sum(dsecond, axis=0, keepdims=True)
        g_small_ref[2:3] = jnp.sum(grad_out, axis=0, keepdims=True)
        dres = grad_out + norm_pull(dsecond, normal, inverse, gain)
        dres_ref[...] = dres
        branch = dres.astype(BF16)
        g_small_ref[3:4] = jnp.sum(branch.astype(F32), axis=0, keepdims=True)
        by_owner(g_out_ref, dot_lt(mixed_ref[...], branch))
        dmixed = dot_rt(branch, w_out_ref[...])
        core = lax.axis_index("gx")

        def hand_over(spot, piece, first, second):
            send_ref[spot, piece] = jnp.where(core == 0, first, second).astype(BF16)
            far = jnp.where(core == 0, second, first)
            for number in range(rows // BLOCK // 2):
                start = 2 * number * BLOCK
                far_ref[spot, piece, number * BLOCK : (number + 1) * BLOCK] = jnp.where(
                    low_lanes(BLOCK),
                    swap_halves(far[start + BLOCK : start + 2 * BLOCK]),
                    far[start : start + BLOCK],
                ).astype(BF16)

        for piece in range(pieces):
            span = slice(piece * rows, (piece + 1) * rows)
            for spot in (0, 2):
                tiles = [
                    dmixed[span, number * LANES : (number + 1) * LANES]
                    for number in range(3 * (spot // 2), 3 * (spot // 2) + 3)
                ]
                flipped = [swap_halves(tile) for tile in tiles]
                hand_over(
                    spot,
                    piece,
                    jnp.where(low, tiles[1], flipped[0]),
                    jnp.where(low, tiles[1], tiles[0]),
                )
                hand_over(
                    spot + 1, piece, jnp.where(low, flipped[2], tiles[1]), flipped[2]
                )
        for number, pair in enumerate(stages):
            if PER_STAGE * (number + 1) - 1 + WAITS[2] >= last:
                pair[0].close(half_up_ref.at[PER_STAGE * number : PER_STAGE * (number + 1)])
                pair[1].close(half_down_ref.at[number])
        keep_up.wait()
        keep_down.wait()


def plane_middle(mixed_in, far_in, x, dy, vec, w_out, up_shift, w_up, w_down):
    pieces, rows, _ = x.shape
    tokens = pieces * rows
    shard = D // RANKS

    def fixed(shape):
        return pl.BlockSpec(shape, lambda step: (0,) * len(shape))

    steps = FF // CHUNK
    grid = (2, PLANES, SPOTS)
    down_rows = FF // RANKS
    half_up = (PER_STAGE * EARLY, PLANES, 2 * shard, LANES)
    half_down = (EARLY, down_rows, D)
    buffers = []
    for _ in range(EARLY):
        buffers += block_scratch(PER_STAGE, 2 * shard, LANES) + row_scratch(down_rows, D)
    down = pl.BlockSpec((2, LANES, D), lambda step: (0, step, 0))
    return pl.pallas_call(
        plane_middle_kernel,
        grid=(steps,),
        out_shape=(
            jax.ShapeDtypeStruct(x.shape, BF16),
            jax.ShapeDtypeStruct(mixed_in.shape, BF16),
            jax.ShapeDtypeStruct(far_in.shape, BF16),
            jax.ShapeDtypeStruct((tokens, D), F32),
            jax.ShapeDtypeStruct((RANKS, 2 * shard, D // 2), BF16),
            jax.ShapeDtypeStruct(half_up, BF16),
            jax.ShapeDtypeStruct(half_down, BF16),
            jax.ShapeDtypeStruct((PER_STAGE * LATE,) + grid + (2 * shard, LANES), BF16),
            jax.ShapeDtypeStruct((LATE, 2, FF // 2 // STAGES, D), BF16),
            jax.ShapeDtypeStruct((steps, 1, CHUNK), F32),
            jax.ShapeDtypeStruct((4, D), F32),
        ),
        in_specs=[
            fixed(mixed_in.shape),
            fixed(far_in.shape),
            fixed(x.shape),
            fixed((tokens, D)),
            fixed(vec.shape),
            fixed((D, D)),
            pl.BlockSpec((1, 1, CHUNK), lambda step: (step, 0, 0)),
            pl.BlockSpec((D, CHUNK), lambda step: (0, step)),
            down,
        ],
        out_specs=(
            fixed(x.shape),
            fixed(mixed_in.shape),
            fixed(far_in.shape),
            fixed((tokens, D)),
            fixed((RANKS, 2 * shard, D // 2)),
            fixed(half_up),
            fixed(half_down),
            whole(ANY),
            whole(ANY),
            pl.BlockSpec((1, 1, CHUNK), lambda step: (step, 0, 0)),
            fixed((4, D)),
        ),
        scratch_shapes=[
            VMEM((tokens, D), BF16),
            VMEM((tokens, D), F32),
            VMEM((tokens, D), BF16),
            VMEM((D, tokens), BF16),
            VMEM((tokens, D), F32),
            VMEM((tokens, D), F32),
            VMEM((steps,) + grid + (2 * shard, LANES), BF16),
            VMEM((STAGES, 2, FF // 2 // STAGES, D), BF16),
        ]
        + buffers
        + [
            pltpu.SemaphoreType.DMA((EARLY, 2, SpotReduce.SEMS)),
            pltpu.SemaphoreType.DMA((EARLY, 2, SpotReduce.SEMS)),
            pltpu.SemaphoreType.DMA((2,)),
        ],
        compiler_params=pltpu.CompilerParams(
            vmem_limit_bytes=60 * 1024 * 1024, collective_id=3, has_side_effects=True
        ),
        name="plane_middle",
    )(mixed_in, far_in, x, dy, vec, w_out, up_shift, w_up, w_down)


class Reduce:
    SENDS = 4 + 2 + 2 + 3
    RECVS = SENDS

    def __init__(self, source, total, near, corner_x, corner_y, side_x, side_y, far, out, sems):
        self.source, self.total, self.near = source, total, near
        self.corner = {1: corner_x, 2: corner_y}
        self.side = {1: side_x, 2: side_y}
        self.far, self.out = far, out
        self.send_sem, self.recv_sem, self.local_sem = sems
        self.core, self.plane, self.spot = place_here()
        self.copies = []
        self.locals = []

    def start(self):
        sibling = (1 - self.core, rank_of(self.plane, self.spot))
        for number, side in enumerate((3, 1, 2, 0)):
            spot = flip(self.spot, side)
            copy = remote(
                self.source.at[1 - self.core, :, spot],
                self.near.at[:, spot],
                self.send_sem.at[number],
                self.recv_sem.at[number],
                sibling,
            )
            copy.start()
            self.copies.append(copy)
            keep = pltpu.make_async_copy(
                self.source.at[self.core, :, spot],
                self.total.at[:, spot],
                self.local_sem.at[number],
            )
            keep.start()
            self.locals.append(keep)

    def take(self, number, side):
        self.copies[number].wait_recv()
        self.locals[number].wait()
        spot = flip(self.spot, side)

        def add(plane, carry):
            self.total[plane, spot] = (
                self.total[plane, spot].astype(F32) + self.near[plane, spot].astype(F32)
            ).astype(self.total.dtype)
            return carry

        lax.fori_loop(0, PLANES, add, 0, unroll=True)

    def corners(self):
        self.take(0, 3)
        spot = flip(self.spot, 3)
        index = 4
        self.corner_copies = []
        for bits in range(PLANES):
            side = 2 if bits < 2 else 1
            self.corner_copies.append(None)
            plane = flip(self.plane, bits)
            copy = remote(
                self.total.at[plane, spot],
                self.corner[side].at[bits % 2],
                self.send_sem.at[index + bits],
                self.recv_sem.at[index + bits],
                (self.core, rank_of(self.plane, flip(self.spot, side))),
            )
            copy.start()
            self.corner_copies[bits] = copy

    def sides(self):
        self.take(1, 1)
        self.take(2, 2)
        self.side_copies = {}
        for side in (1, 2):
            spot = flip(self.spot, side)
            came = 3 - side
            for bits in (0, 1) if came == 2 else (2, 3):
                self.corner_copies[bits].wait_recv()
                plane = flip(self.plane, bits)
                self.total[plane, spot] = (
                    self.total[plane, spot].astype(F32)
                    + self.corner[came][bits % 2].astype(F32)
                ).astype(self.total.dtype)
            copy = remote(
                self.total.at[:, spot],
                self.side[side],
                self.send_sem.at[7 + side],
                self.recv_sem.at[7 + side],
                (self.core, rank_of(self.plane, spot)),
            )
            copy.start()
            self.side_copies[side] = copy

    def columns(self):
        self.take(3, 0)
        for side in (1, 2):
            self.side_copies[side].wait_recv()

        def add(plane, carry):
            self.total[plane, self.spot] = (
                self.total[plane, self.spot].astype(F32)
                + self.side[1][plane].astype(F32)
                + self.side[2][plane].astype(F32)
            ).astype(self.total.dtype)
            return carry

        lax.fori_loop(0, PLANES, add, 0, unroll=True)
        self.far_copies = []
        for bits in range(1, PLANES):
            plane = flip(self.plane, bits)
            copy = remote(
                self.total.at[plane, self.spot],
                self.far.at[bits - 1],
                self.send_sem.at[9 + bits],
                self.recv_sem.at[9 + bits],
                (self.core, rank_of(plane, self.spot)),
            )
            copy.start()
            self.far_copies.append(copy)

    def finish(self):
        value = self.total[self.plane, self.spot].astype(F32)
        for bits in range(1, PLANES):
            self.far_copies[bits - 1].wait_recv()
            value = value + self.far[bits - 1].astype(F32)
        self.out[...] = value
        for copy in self.copies + self.corner_copies + self.far_copies:
            copy.wait_send()
        for side in (1, 2):
            self.side_copies[side].wait_send()


REDUCE_SEMS = 13


def reduce_scratch(shape, kind):
    tail = shape[3:]
    return [
        VMEM((PLANES, SPOTS) + tail, kind),
        VMEM((PLANES, SPOTS) + tail, kind),
        VMEM((2,) + tail, kind),
        VMEM((2,) + tail, kind),
        VMEM((PLANES,) + tail, kind),
        VMEM((PLANES,) + tail, kind),
        VMEM((PLANES - 1,) + tail, kind),
    ]


class Doubling:
    STEPS = 5

    def __init__(self, totals, boxes, send_sem, recv_sem):
        self.totals, self.boxes = totals, boxes
        self.send_sem, self.recv_sem = send_sem, recv_sem
        core, plane, spot = place_here()
        self.partners = (
            (1 - core, rank_of(plane, spot)),
            (core, rank_of(plane, flip(spot, 1))),
            (core, rank_of(plane, flip(spot, 2))),
            (core, rank_of(flip(plane, 1), spot)),
            (core, rank_of(flip(plane, 2), spot)),
        )
        self.copies = []

    def start(self, step):
        self.copies = []
        for number, (total, box) in enumerate(zip(self.totals, self.boxes)):
            copy = remote(
                total,
                box.at[step],
                self.send_sem.at[step, number],
                self.recv_sem.at[step, number],
                self.partners[step],
            )
            copy.start()
            self.copies.append(copy)

    def finish(self, step):
        for copy, total, box in zip(self.copies, self.totals, self.boxes):
            copy.wait()
            total[...] += box[step]


PARTS = 3


def finish_kernel(
    recv_ref,
    far_ref,
    normed_ref,
    x_ref,
    dres_hbm,
    vec_ref,
    w_hbm,
    g_mid_ref,
    g_up_bias_ref,
    grad_ref,
    g_qkv_ref,
    rows_out_ref,
    tiles_out_ref,
    *scratch,
):
    sources, scratch = scratch[:PARTS], scratch[PARTS:]
    buffers, scratch = scratch[: 7 * PARTS], scratch[7 * PARTS :]
    packed_ref, dnormed_ref, gradient_ref, dres_ref, w_ref = scratch[:5]
    rows_ref, tiles_ref, rows_box, tiles_box = scratch[5:9]
    send_sem, recv_sem, local_sem, load_sem, sum_send, sum_recv = scratch[9:15]
    move_sems = scratch[15:18]
    pieces, rows, _ = x_ref.shape
    tokens = pieces * rows
    core, plane, spot = place_here()
    low = low_lanes(rows)

    load_w = pltpu.make_async_copy(w_hbm, w_ref, load_sem.at[0])
    load_dres = pltpu.make_async_copy(dres_hbm, dres_ref, load_sem.at[1])
    load_w.start()
    load_dres.start()
    greet(all_partners(core, plane, spot))

    def put(tile, piece, value):
        side, chunk = tile // HALF_TILES, tile % HALF_TILES
        packed_ref[
            piece * rows : (piece + 1) * rows,
            chunk * CHUNK + side * LANES : chunk * CHUNK + (side + 1) * LANES,
        ] = value.astype(BF16)

    start_piece, finish_grad = from_planes(gradient_ref, grad_ref, *move_sems, later=True)
    for piece in range(pieces):
        seconds = []
        for goal in range(SPOTS):
            own = recv_ref[core, goal, piece, QUERIES].astype(F32)
            halves = far_ref[goal, piece].astype(F32)
            parts = []
            for number in range(rows // BLOCK // 2):
                part = halves[number * BLOCK : (number + 1) * BLOCK]
                parts += [part, swap_halves(part)]
            other = jnp.concatenate(parts, axis=0)
            second = jnp.where(core == 0, other, own)
            put(goal, piece, jnp.where(low & (core == 1), other, own))
            seconds.append(second)
            base = D // LANES + 3 * goal
            put(base, piece, recv_ref[0, goal, piece, KEYS_A])
            put(base + 1, piece, recv_ref[1, goal, piece, KEYS_A])
            put(base + 2, piece, recv_ref[core, goal, piece, KEYS_B])
        for number in range(2):
            put(
                SPOTS + number,
                piece,
                jnp.where(low, seconds[2 * number], swap_halves(seconds[2 * number + 1])),
            )
        if piece == 0:
            load_w.wait()
            load_dres.wait()
        span = slice(piece * rows, (piece + 1) * rows)
        share = dot_rt(packed_ref[span], w_ref[...])
        dnormed_ref[span] = share
        normal, inverse = norm_parts(x_ref[piece].astype(F32))
        gradient = dres_ref[span] + norm_pull(share, normal, inverse, vec_ref[0:1])
        gradient_ref[piece] = gradient.astype(BF16)
        start_piece(piece)
        sums = [
            jnp.sum(share * normal, axis=0, keepdims=True),
            jnp.sum(share, axis=0, keepdims=True),
        ]
        for number in range(2):
            if piece == 0:
                rows_ref[number : number + 1] = sums[number]
            else:
                rows_ref[number : number + 1] += sums[number]

    rows_ref[2:6] = g_mid_ref[...]
    rows_ref[6:8] = jnp.zeros((2, D), F32)
    tiles_ref[...] = jnp.zeros_like(tiles_ref)
    for step in range(FF // CHUNK):
        tiles_ref[step : step + 1] = g_up_bias_ref[step]
    for chunk in range(HALF_TILES):
        number = FF // CHUNK + chunk
        tiles_ref[number : number + 1] = jnp.sum(
            packed_ref[:, chunk * CHUNK : (chunk + 1) * CHUNK].astype(F32), axis=0, keepdims=True
        )
    sums = Doubling((rows_ref, tiles_ref), (rows_box, tiles_box), sum_send, sum_recv)
    sums.start(0)

    width = HALF_TILES // PARTS * LANES
    reduces = [
        Reduce(
            sources[part],
            *buffers[7 * part : 7 * part + 7],
            g_qkv_ref.at[:, part * width : (part + 1) * width],
            (send_sem.at[part], recv_sem.at[part], local_sem.at[part]),
        )
        for part in range(PARTS)
    ]
    shard = D // RANKS
    normed_t = normed_ref[...].astype(F32).T.astype(BF16)
    for part in range(PARTS):
        for number in range(HALF_TILES // PARTS):
            chunk = part * (HALF_TILES // PARTS) + number
            values = dot(normed_t, packed_ref[:, chunk * CHUNK : (chunk + 1) * CHUNK])
            columns = slice(number * LANES, (number + 1) * LANES)
            for owner in range(RANKS):
                mine = values[owner * shard : (owner + 1) * shard]
                sources[part][
                    owner // (PLANES * SPOTS), owner // SPOTS % PLANES, owner % SPOTS, :, columns
                ] = jnp.concatenate([mine[:, :LANES], mine[:, LANES:]], axis=0).astype(BF16)
        reduces[part].start()
        if part > 0:
            reduces[part - 1].corners()
        if part > 1:
            reduces[part - 2].sides()
    sums.finish(0)
    sums.start(1)
    reduces[2].corners()
    reduces[1].sides()
    sums.finish(1)
    sums.start(2)
    reduces[0].columns()
    reduces[2].sides()
    sums.finish(2)
    sums.start(3)
    reduces[1].columns()
    sums.finish(3)
    sums.start(4)
    reduces[2].columns()
    sums.finish(4)
    for one in reduces:
        one.finish()
    rows_out_ref[...] = rows_ref[...]
    tiles_out_ref[...] = tiles_ref[...]
    finish_grad()


def finish_layer(recv, far, normed, x, dres, vec, w, g_mid, g_up_bias):
    pieces, rows, _ = x.shape
    tokens = pieces * rows
    shard = D // RANKS
    grid = (2, PLANES, SPOTS)
    part = grid + (2 * shard, HALF_TILES // PARTS * LANES)
    buffers = []
    for _ in range(PARTS):
        buffers += reduce_scratch(part, BF16)
    tiles = -(-(FF // CHUNK + HALF_TILES) // 8) * 8
    dma = pltpu.SemaphoreType.DMA
    return pl.pallas_call(
        finish_kernel,
        out_shape=(
            jax.ShapeDtypeStruct(x.shape, BF16),
            jax.ShapeDtypeStruct((2 * shard, 3 * D // 2), F32),
            jax.ShapeDtypeStruct((8, D), F32),
            jax.ShapeDtypeStruct((tiles, CHUNK), F32),
        ),
        in_specs=[
            whole(),
            whole(),
            whole(),
            whole(),
            whole(ANY),
            whole(),
            whole(ANY),
            whole(),
            whole(),
        ],
        out_specs=(whole(ANY), whole(), whole(), whole()),
        scratch_shapes=[VMEM(part, BF16)] * PARTS
        + buffers
        + [
            VMEM((tokens, 3 * D), BF16),
            VMEM((tokens, D), F32),
            VMEM(x.shape, BF16),
            VMEM((tokens, D), F32),
            VMEM(w.shape, BF16),
            VMEM((8, D), F32),
            VMEM((tiles, CHUNK), F32),
            VMEM((Doubling.STEPS, 8, D), F32),
            VMEM((Doubling.STEPS, tiles, CHUNK), F32),
            dma((PARTS, REDUCE_SEMS)),
            dma((PARTS, REDUCE_SEMS)),
            dma((PARTS, 4)),
            dma((2,)),
            dma((Doubling.STEPS, 2)),
            dma((Doubling.STEPS, 2)),
            dma((2,)),
            dma((2,)),
            dma((2,)),
        ],
        compiler_params=pltpu.CompilerParams(
            vmem_limit_bytes=60 * 1024 * 1024, collective_id=2, has_side_effects=True
        ),
        name="finish_layer",
    )(recv, far, normed, x, dres, vec, w, g_mid, g_up_bias)


def present_kernel(
    hidden_hbm,
    grad_hbm,
    t_qkv_hbm,
    t_out_hbm,
    t_up_hbm,
    t_down_hbm,
    rows_hbm,
    tiles_hbm,
    hidden_out_ref,
    grad_out_ref,
    g_qkv_ref,
    g_out_ref,
    g_up_ref,
    g_down_ref,
    *outs,
):
    singles, (grad_ref, t_qkv_ref, t_out_ref, t_up_ref, rows_ref, tiles_ref, copy_sem) = (
        outs[:-7],
        outs[-7:],
    )
    loads = [
        pltpu.make_async_copy(source, target, copy_sem.at[number])
        for number, (source, target) in enumerate(
            (
                (rows_hbm, rows_ref),
                (tiles_hbm, tiles_ref),
                (t_qkv_hbm, t_qkv_ref),
                (t_out_hbm, t_out_ref),
                (t_up_hbm, t_up_ref),
                (grad_hbm, grad_ref),
                (t_down_hbm, g_down_ref),
                (hidden_hbm, hidden_out_ref),
            )
        )
    ]
    for copy in loads:
        copy.start()
    core, plane, spot = place_here()
    mine = core * (PLANES * SPOTS) + rank_of(plane, spot)
    own, wide = D // RANKS, FF // RANKS
    order = [natural_block(entry) for entry in column_order()]
    inverse = [order.index(number) for number in range(len(order))]

    for copy in loads[:5]:
        copy.wait()
    half = D // 2
    for side in range(2):
        rows = slice(side * own, (side + 1) * own)
        g_out_ref[:, side * half : (side + 1) * half] = t_out_ref[rows]
        for chunk in range(FF // CHUNK):
            start = side * (FF // 2) + chunk * LANES
            g_up_ref[:, start : start + LANES] = t_up_ref[chunk, rows]

    def folded(tile):
        side, chunk = tile // HALF_TILES, tile % HALF_TILES
        return t_qkv_ref[
            side * own : (side + 1) * own, chunk * LANES : (chunk + 1) * LANES
        ]

    def bias_sum(tile):
        side, chunk = tile // HALF_TILES, tile % HALF_TILES
        row = FF // CHUNK + chunk
        return tiles_ref[row : row + 1, side * LANES : (side + 1) * LANES]

    biases = []
    for tile in range(TILES):
        blocks = inverse[2 * tile], inverse[2 * tile + 1]
        g_qkv_ref[:, tile * LANES : (tile + 1) * LANES] = pair_of_blocks(folded, *blocks)
        biases.append(pair_of_blocks(bias_sum, *blocks))
    third = TILES // 3
    query = jnp.concatenate(biases[:third], axis=1)
    value = jnp.concatenate(biases[2 * third :], axis=1)
    vectors = jnp.concatenate([rows_ref[0:6], query, value], axis=0)

    def pick(values, first, wanted):
        place = lax.broadcasted_iota(jnp.int32, (values.shape[1], LANES), 0) + first
        lane = lax.broadcasted_iota(jnp.int32, (values.shape[1], LANES), 1)
        one_hot = jnp.where(place == mine * wanted + lane, 1.0, 0.0)
        return lax.dot_general(
            values,
            one_hot,
            (((1,), (0,)), ((), ())),
            precision=lax.Precision.HIGHEST,
            preferred_element_type=F32,
        )

    picked = pick(vectors, 0, own)
    for number in range(VECTORS):
        singles[number][...] = picked[number : number + 1, :own]
    total = jnp.zeros((1, LANES), F32)
    for chunk in range(FF // CHUNK):
        for side in range(2):
            total = total + pick(
                tiles_ref[chunk : chunk + 1, side * LANES : (side + 1) * LANES],
                side * (FF // 2) + chunk * LANES,
                wide,
            )
    singles[VECTORS][...] = total[:, :wide]
    loads[5].wait()
    grad_out_ref[...] = grad_ref[...].astype(F32)
    for copy in loads[6:]:
        copy.wait()


def present(hidden, grad, t_qkv, t_out, t_up, t_down, rows, tiles):
    own, wide = D // RANKS, FF // RANKS
    struct = jax.ShapeDtypeStruct
    return pl.pallas_call(
        present_kernel,
        out_shape=(
            struct(hidden.shape, BF16),
            struct(grad.shape, F32),
            struct((own, 3 * D), F32),
            struct((own, D), F32),
            struct((own, FF), F32),
            struct((wide, D), F32),
        )
        + (struct((1, own), F32),) * VECTORS
        + (struct((1, wide), F32),),
        in_specs=[whole(ANY)] * 8,
        out_specs=(whole(),) * (7 + VECTORS),
        scratch_shapes=[
            VMEM(item.shape, item.dtype) for item in (grad, t_qkv, t_out, t_up, rows, tiles)
        ]
        + [pltpu.SemaphoreType.DMA((8,))],
        compiler_params=params_of(63),
        name="present",
    )(hidden, grad, t_qkv, t_out, t_up, t_down, rows, tiles)


def plane_shards(
    hidden_in,
    rand_table,
    norm1_gain,
    norm1_bias,
    w_qkv,
    query_bias,
    value_bias,
    w_out,
    out_bias,
    norm2_gain,
    norm2_bias,
    w_up,
    up_bias,
    w_down,
    down_bias,
    cotangent,
):
    micro, rows, _ = hidden_in.shape
    local = rows // BLOCK

    def in_row(vector, number):
        return jnp.pad(vector[None], ((number, 15 - number), (0, LANES - vector.shape[0])))

    vec = functools.reduce(
        jnp.add,
        [
            in_row(vector, number)
            for number, vector in enumerate(
                (
                    norm1_gain,
                    norm1_bias,
                    query_bias,
                    value_bias,
                    out_bias,
                    norm2_gain,
                    norm2_bias,
                    down_bias,
                    up_bias,
                )
            )
        ],
    )
    tab = jnp.pad(
        rand_table.reshape(micro, local * RANDOM), ((0, 8 - micro), (0, LANES - local * RANDOM))
    )
    (
        mixed,
        far_mixed,
        x,
        dy,
        w_down_all,
        w_qkv_all,
        w_out_all,
        w_up_all,
        qk,
        shared,
        normed,
        lse,
        vectors,
        up_shift,
        table,
        sorted_table,
    ) = front(hidden_in, cotangent, vec, tab, w_qkv, w_out, w_up, w_down)
    mixed = mixed.reshape(SPOTS, PIECES, rows, LANES)
    far_mixed = far_mixed.reshape(SPOTS, PIECES, rows // 2, LANES)
    (
        hidden,
        near_grad,
        far_grad,
        dres,
        g_out,
        half_up,
        half_down,
        last_up,
        last_down,
        g_up_bias,
        g_mid,
    ) = plane_middle(
        mixed,
        far_mixed,
        x,
        dy.reshape(micro * rows, D),
        vectors,
        w_out_all,
        up_shift,
        w_up_all,
        w_down_all.reshape(2, FF // 2, D),
    )
    grid = (2, PLANES, SPOTS)
    dqkv, far_dq, hidden_out, t_out, t_up, t_down = plane_attention_back(
        table,
        sorted_table,
        qk,
        shared,
        near_grad.reshape(SPOTS, PIECES, local, BLOCK, LANES),
        far_grad.reshape(SPOTS, PIECES, local // 2, BLOCK, LANES),
        lse,
        hidden,
        [
            g_out.reshape((1,) + grid + g_out.shape[1:]),
            last_up,
            last_down,
        ],
        half_up,
        half_down,
    )
    dqkv = dqkv.reshape(2, SPOTS, PIECES, 3, rows, LANES)
    far_dq = far_dq.reshape(SPOTS, PIECES, rows // 2, LANES)
    grad_hidden, t_qkv, sum_rows, sum_tiles = finish_layer(
        dqkv, far_dq, normed, x, dres, vectors, w_qkv_all, g_mid, g_up_bias
    )

    results = present(hidden_out, grad_hidden, t_qkv, t_out, t_up, t_down, sum_rows, sum_tiles)
    hidden_out, grad_hidden, g_qkv, g_out, g_up, g_down = results[:6]
    n1g, n1b, n2g, n2b, db, ob, qb, vb, ub = (item.reshape(item.size) for item in results[6:])
    return (
        hidden_out,
        grad_hidden,
        n1g,
        n1b,
        g_qkv,
        qb,
        vb,
        g_out,
        ob,
        n2g,
        n2b,
        g_up,
        ub,
        g_down,
        db,
    )


def shards(*arrays):
    micro, rows, _ = arrays[0].shape
    fits = lax.axis_size("gx") == 2 and lax.axis_size("gy") == PLANES * SPOTS
    fits = fits and micro == 2 and rows == 4 * BLOCK
    return (plane_shards if fits else general_shards)(*arrays)


def solution(mesh):
    tokens = P(None, AXES, None)
    vector = P(AXES)
    matrix = P(AXES, None)
    placed = (
        tokens,
        tokens,
        vector,
        vector,
        matrix,
        vector,
        vector,
        matrix,
        vector,
        vector,
        vector,
        matrix,
        vector,
        matrix,
        vector,
        tokens,
    )
    returned = (
        tokens,
        tokens,
        vector,
        vector,
        matrix,
        vector,
        vector,
        matrix,
        vector,
        vector,
        vector,
        matrix,
        vector,
        matrix,
        vector,
    )
    return jax.shard_map(
        shards, mesh=mesh, in_specs=placed, out_specs=returned, check_vma=False
    )
```
